32 devices in a mesh: fsdp: 2 (over x), ctx: 4 (over y, core), tp: 4 (over z).
Axes of the slice: x: 2, y: 2, z: 4, core: 2. Of those that a mesh axis runs over, the one named last changes fastest.
Arguments:
- inputs: bfloat16 [8192, 2048], P(('fsdp', 'ctx'), 'tp'), may hold values from -6 to 6
- cotangent: bfloat16 [8192, 2048], P(('fsdp', 'ctx'), 'tp'), may hold values from -6 to 6
- first_gain: float32 [2048], replicated, may hold values from 0.5 to 1.5
- first_bias: float32 [2048], replicated, may hold values from -4 to 4
- qkv_weight: bfloat16 [2048, 3, 2048], P(('fsdp', 'ctx'), None, 'tp'), may hold values from -0.125 to 0.125
- qkv_bias: float32 [3, 2048], P(None, 'tp'), may hold values from -6 to 6
- out_weight: bfloat16 [2048, 2048], P('tp', ('fsdp', 'ctx')), may hold values from -0.75 to 0.75
- second_gain: float32 [2048], replicated, may hold values from 0.5 to 1.5
- second_bias: float32 [2048], replicated, may hold values from -4 to 4
- gate_weight: bfloat16 [2048, 5632], P(('fsdp', 'ctx'), 'tp'), may hold values from -0.125 to 0.125
- up_weight: bfloat16 [2048, 5632], P(('fsdp', 'ctx'), 'tp'), may hold values from -0.125 to 0.125
- down_weight: bfloat16 [5632, 2048], P('tp', ('fsdp', 'ctx')), may hold values from -0.078125 to 0.078125
- lengths: int32 [2, 8], P('fsdp'), may hold values from 0 to 2048, as said below
- fill_counts: int32 [2, 4], P('fsdp'), may hold values from 614 to 1024, as said below
Outputs:
- layer_out: bfloat16 [8192, 2048], P(('fsdp', 'ctx'), 'tp')
- grad_inputs: bfloat16 [8192, 2048], P(('fsdp', 'ctx'), 'tp')
- grad_first_gain: float32 [2048], replicated
- grad_first_bias: float32 [2048], replicated
- grad_qkv_weight: float32 [2048, 3, 2048], P(('fsdp', 'ctx'), None, 'tp')
- grad_qkv_bias: float32 [3, 2048], P(None, 'tp')
- grad_out_weight: float32 [2048, 2048], P('tp', ('fsdp', 'ctx'))
- grad_second_gain: float32 [2048], replicated
- grad_second_bias: float32 [2048], replicated
- grad_gate_weight: float32 [2048, 5632], P(('fsdp', 'ctx'), 'tp')
- grad_up_weight: float32 [2048, 5632], P(('fsdp', 'ctx'), 'tp')
- grad_down_weight: float32 [5632, 2048], P('tp', ('fsdp', 'ctx'))
The draws below stay inside these ranges and needn't reach their ends.
Inputs may be any that keep to these rules, and one draw needn't show every extreme that they name: fill_counts[f, c] is the number of leading rows of block c of group f that hold tokens; the other rows of the block are padding; in every group some block is full. lengths[f, :] are the lengths of the 8 sequences packed in order into the token-holding rows of group f, block after block; they sum to the group's token-holding rows; a zero is an empty sequence; one sequence of every group is 2048 tokens long and has rows in the group's first and last block.
All inputs are finite; a program needn't handle non-finite values.
Results may differ from the reference program's by a relative error of at most 0.025.
Values may be sent and summed in bfloat16 or wider, within the bound.
No kernel may reach another device: no remote copies, remote signals or barrier semaphores. Data moves between devices by JAX's collectives and lax.ppermute only.
A program may use at most 256 MiB of HBM per device.

```python
import jax
import jax.numpy as jnp
from jax import lax

D = 2048
HEADS = 32
HEAD_DIM = 64
FF = 5632
TOK_DEV = 1024
SEQS = 8
ROT = 16
LONGEST = 2048
GROUPS = 2
BLOCKS = 4
TOKENS = 8192


def packing(key):
    fill_key, full_key, offset_key, head_key, tail_key = jax.random.split(key, 5)
    lowest = 3 * TOK_DEV // 5
    counts = jax.random.randint(fill_key, (GROUPS, BLOCKS), lowest, TOK_DEV)
    full_block = (BLOCKS - 1) * jax.random.randint(full_key, (GROUPS, 1), 0, 2)
    counts = jnp.where(jnp.arange(BLOCKS)[None, :] == full_block, TOK_DEV, counts).astype(jnp.int32)
    filled = jnp.sum(counts, axis=1).astype(jnp.int32)
    middle = jnp.sum(counts[:, 1:BLOCKS - 1], axis=1).astype(jnp.int32)
    bottom = jnp.maximum(0, counts[:, 0] + middle + 1 - LONGEST)
    ceiling = jnp.minimum(counts[:, 0] - 1, filled - LONGEST)
    offset = jax.random.randint(offset_key, (GROUPS,), bottom, ceiling + 1).astype(jnp.int32)
    remain = (filled - offset - LONGEST).astype(jnp.int32)
    head_cuts = jnp.sort(jax.random.randint(head_key, (GROUPS, 3), 0, offset[:, None] + 1), axis=1).astype(jnp.int32)
    tail_cuts = jnp.sort(jax.random.randint(tail_key, (GROUPS, SEQS - 6), 0, remain[:, None] + 1), axis=1).astype(jnp.int32)
    zero_column = jnp.zeros((GROUPS, 1), jnp.int32)
    head_edges = jnp.concatenate([zero_column, head_cuts, offset[:, None]], axis=1)
    tail_edges = jnp.concatenate([zero_column, tail_cuts, remain[:, None]], axis=1)
    longest_column = jnp.full((GROUPS, 1), LONGEST, jnp.int32)
    seq_lengths = jnp.concatenate([head_edges[:, 1:] - head_edges[:, :-1], longest_column, tail_edges[:, 1:] - tail_edges[:, :-1]], axis=1)
    return (seq_lengths.astype(jnp.int32), counts)


def draw_lengths(key, part):
    shared = packing(key)
    return shared[0]


def draw_fill_counts(key, part):
    shared = packing(key)
    return shared[1]


def levels(key, dims, cuts, smallest, largest):
    loudness, own = 1.0, jax.random.fold_in(key, 6)
    for axis_at, parts in cuts:
        steps = jnp.exp(jax.random.uniform(jax.random.fold_in(own, axis_at), (parts,), jnp.float32, smallest / len(cuts), largest / len(cuts)))
        loudness = loudness * jnp.repeat(steps, dims[axis_at] // parts).reshape([-1 if axis == axis_at else 1 for axis in range(len(dims))])
    return loudness


def gaussian(rng, dims, scale, bound, shards=(), kind=jnp.bfloat16):
    loudness = levels(rng, dims, shards, -0.22, 0.18) if shards else 1.0
    array = jax.random.normal(rng, dims, jnp.float32) * scale * loudness
    return jnp.minimum(jnp.maximum(array, -bound), bound).astype(kind)


def setup_inputs(seed: int = 0) -> dict:
    splits = jax.random.split(jax.random.key(seed), 15)
    inputs = gaussian(splits[0], (TOKENS, D), 1.0, 6.0, ((0, 8), (1, 4)))
    cotangent = gaussian(splits[1], (TOKENS, D), 1.0, 6.0, ((0, 8), (1, 4)))
    first_gain = jnp.clip(1.0 + 0.1 * jax.random.normal(splits[2], (D,), jnp.float32), 0.5, 1.5)
    first_bias = gaussian(splits[3], (D,), 0.3, 4.0, (), jnp.float32)
    qkv_weight = gaussian(splits[4], (D, 3, D), D ** -0.5, 0.125, ((0, 8), (2, 4)))
    qkv_bias = gaussian(splits[5], (3, D), 0.5, 6.0, ((1, 4),), jnp.float32)
    out_weight = gaussian(splits[6], (D, D), (D // 32) ** -0.5, 0.75, ((0, 4), (1, 8)))
    second_gain = jnp.clip(1.0 + 0.1 * jax.random.normal(splits[7], (D,), jnp.float32), 0.5, 1.5)
    second_bias = gaussian(splits[8], (D,), 0.3, 4.0, (), jnp.float32)
    gate_weight = gaussian(splits[9], (D, FF), D ** -0.5, 0.125, ((0, 8), (1, 4)))
    up_weight = gaussian(splits[10], (D, FF), D ** -0.5, 0.125, ((0, 8), (1, 4)))
    down_weight = gaussian(splits[11], (FF, D), FF ** -0.5, 0.078125, ((0, 4), (1, 8)))
    lengths = draw_lengths(jax.random.fold_in(splits[14], 71), 0)
    fill_counts = draw_fill_counts(jax.random.fold_in(splits[14], 71), 0)
    return dict(inputs=inputs, cotangent=cotangent, first_gain=first_gain, first_bias=first_bias, qkv_weight=qkv_weight, qkv_bias=qkv_bias, out_weight=out_weight, second_gain=second_gain, second_bias=second_bias, gate_weight=gate_weight, up_weight=up_weight, down_weight=down_weight, lengths=lengths, fill_counts=fill_counts)


HIGHEST = lax.Precision.HIGHEST
EPSILON = 1e-05
NEGATIVE = -1e+30

@jax.custom_vjp
def low(v):
    return lax.optimization_barrier(v.astype(jnp.bfloat16)).astype(jnp.float32)

@jax.custom_vjp
def low_back(v):
    return v

def low_keep(v):
    return (low(v), None)

def low_pass(kept, grad):
    return (grad,)

def back_keep(v):
    return (v, None)

def back_low(kept, grad):
    return (low(grad),)
low.defvjp(low_keep, low_pass)
low_back.defvjp(back_keep, back_low)

def layout(lengths, fill_counts, block_rows):
    blocks_count = fill_counts.shape[0]
    seq_count = lengths.shape[0]
    slot_index = jnp.arange(blocks_count * block_rows, dtype=jnp.int32)
    block_of = (slot_index // block_rows).astype(jnp.int32)
    within = (slot_index - block_of * block_rows).astype(jnp.int32)
    chooser = block_of[:, None] == jnp.arange(blocks_count, dtype=jnp.int32)[None, :]
    fill_here = lax.optimization_barrier(jnp.sum(jnp.where(chooser, fill_counts[None, :], 0), axis=1)).astype(jnp.int32)
    before = (jnp.cumsum(fill_counts) - fill_counts).astype(jnp.int32)
    before_here = lax.optimization_barrier(jnp.sum(jnp.where(chooser, before[None, :], 0), axis=1)).astype(jnp.int32)
    validity = within < fill_here
    used_index = (before_here + within).astype(jnp.int32)
    seq_ends = jnp.cumsum(lengths).astype(jnp.int32)
    sequence = lax.optimization_barrier(jnp.sum((used_index[:, None] >= seq_ends[None, :]).astype(jnp.int32), axis=1)).astype(jnp.int32)
    seq_starts = (seq_ends - lengths).astype(jnp.int32)
    picker = sequence[:, None] == jnp.arange(seq_count, dtype=jnp.int32)[None, :]
    start_here = lax.optimization_barrier(jnp.sum(jnp.where(picker, seq_starts[None, :], 0), axis=1)).astype(jnp.int32)
    return (validity, sequence, (used_index - start_here).astype(jnp.int32))

def rotary_tables(position, rotary_dims):
    half_dims = rotary_dims // 2
    frequency = 10000.0 ** (-(2.0 * jnp.arange(half_dims, dtype=jnp.float32)) / rotary_dims)
    angles = position.astype(jnp.float32)[:, None] * frequency[None, :]
    return (jnp.cos(angles), jnp.sin(angles))

def rotate(values, cosine, sine, rotary_dims):
    half_dims = rotary_dims // 2
    leading = values[..., :half_dims]
    trailing = values[..., half_dims:rotary_dims]
    cosine = cosine[:, None, :]
    sine = sine[:, None, :]
    return jnp.concatenate([leading * cosine - trailing * sine, trailing * cosine + leading * sine, values[..., rotary_dims:]], axis=-1)

def layer_norm(values, gain, norm_bias):
    centre = lax.optimization_barrier(jnp.mean(values, axis=-1, keepdims=True))
    centered = values - centre
    spread = lax.optimization_barrier(jnp.mean(centered * centered, axis=-1, keepdims=True))
    return centered * lax.rsqrt(spread + EPSILON) * gain + norm_bias

def group_attention(packed):
    grouped, validity, sequence, position = packed
    scale = HEAD_DIM ** (-0.5)
    allowed = validity[:, None] & validity[None, :] & (sequence[:, None] == sequence[None, :]) & (position[None, :] <= position[:, None])
    row_weight = validity.astype(jnp.float32)

    def one_head(triple):
        queries, keys_all, values_all = triple
        scores = low_back(jnp.dot(queries, keys_all.T, precision=HIGHEST) * scale)
        scores = jnp.where(allowed, scores, NEGATIVE)
        softmax_low = low(jax.nn.softmax(scores, axis=-1) * row_weight[:, None])
        return jnp.dot(softmax_low, values_all, precision=HIGHEST)
    triples = (jnp.transpose(grouped[:, 0], (1, 0, 2)), jnp.transpose(grouped[:, 1], (1, 0, 2)), jnp.transpose(grouped[:, 2], (1, 0, 2)))
    per_head = lax.map(jax.checkpoint(one_head), triples)
    return jnp.transpose(per_head, (1, 0, 2))

def layer_forward(source, gain_one, bias_one, weight_qkv, bias_qkv, weight_out, gain_two, bias_two, weight_gate, weight_up, weight_down, validity, sequence, position):
    token_count = source.shape[0]
    first_low = low(layer_norm(source, gain_one, bias_one))
    projected = low_back(jnp.einsum('td,dkh->tkh', first_low, weight_qkv, precision=HIGHEST)) + bias_qkv[None]
    shaped = projected.reshape(token_count, 3, HEADS, HEAD_DIM)
    cosine, sine = rotary_tables(position.reshape(-1), ROT)
    turned = jnp.stack([rotate(shaped[:, 0], cosine, sine, ROT), rotate(shaped[:, 1], cosine, sine, ROT), shaped[:, 2]], axis=1)
    turned = low_back(low(turned))
    group_count = validity.shape[0]
    grouped = turned.reshape(group_count, BLOCKS * TOK_DEV, 3, HEADS, HEAD_DIM)
    attended = lax.map(jax.checkpoint(group_attention), (grouped, validity, sequence, position))
    attended = low_back(low(attended.reshape(token_count, HEADS * HEAD_DIM)))
    attention_sum = low_back(jnp.dot(attended, weight_out, precision=HIGHEST))
    mixed = source + attention_sum
    second_low = low(layer_norm(mixed, gain_two, bias_two))
    gate_proj = low_back(jnp.dot(second_low, weight_gate, precision=HIGHEST))
    up_proj = low_back(jnp.dot(second_low, weight_up, precision=HIGHEST))
    hidden = low(jax.nn.silu(gate_proj) * up_proj)
    return mixed + jnp.dot(hidden, weight_down, precision=HIGHEST)

def reference(inputs, cotangent, first_gain, first_bias, qkv_weight, qkv_bias, out_weight, second_gain, second_bias, gate_weight, up_weight, down_weight, lengths, fill_counts):

    def group_layout(group_lengths, group_fills):
        return layout(group_lengths, group_fills, TOK_DEV)
    validity, sequence, position = jax.vmap(group_layout)(lengths, fill_counts)

    def forward(source, gain_one, bias_one, weight_qkv, bias_qkv, weight_out, gain_two, bias_two, weight_gate, weight_up, weight_down):
        return layer_forward(source, gain_one, bias_one, weight_qkv, bias_qkv, weight_out, gain_two, bias_two, weight_gate, weight_up, weight_down, validity, sequence, position)
    primals = (inputs.astype(jnp.float32), first_gain.astype(jnp.float32), first_bias.astype(jnp.float32), qkv_weight.astype(jnp.float32), qkv_bias.astype(jnp.float32), out_weight.astype(jnp.float32), second_gain.astype(jnp.float32), second_bias.astype(jnp.float32), gate_weight.astype(jnp.float32), up_weight.astype(jnp.float32), down_weight.astype(jnp.float32))
    result, pullback = jax.vjp(forward, *primals)
    grads = pullback(cotangent.astype(jnp.float32))
    return (result.astype(jnp.bfloat16), grads[0].astype(jnp.bfloat16), grads[1], grads[2], grads[3], grads[4], grads[5], grads[6], grads[7], grads[8], grads[9], grads[10])
```

```python
import functools

import jax
import jax.numpy as jnp
from jax import lax
from jax.experimental import pallas as pl
from jax.experimental.pallas import tpu as pltpu
from jax.sharding import PartitionSpec as P

HEAD_DIM = 64
ROT = 16
EPSILON = 1e-05
NEGATIVE = -1e30
FLOOR = -1e20
VMEM_LIMIT = 56 * 1024 * 1024
TILE_Q = 512
TILE_K = 512
CHUNKS = 2

F32 = jnp.float32
BF16 = jnp.bfloat16


def layout(lengths, fill_counts, block_rows):
    blocks_count = fill_counts.shape[0]
    seq_count = lengths.shape[0]
    slot_index = jnp.arange(blocks_count * block_rows, dtype=jnp.int32)
    block_of = slot_index // block_rows
    within = slot_index - block_of * block_rows
    chooser = block_of[:, None] == jnp.arange(blocks_count, dtype=jnp.int32)[None, :]
    fill_here = jnp.sum(jnp.where(chooser, fill_counts[None, :], 0), axis=1)
    before = jnp.cumsum(fill_counts) - fill_counts
    before_here = jnp.sum(jnp.where(chooser, before[None, :], 0), axis=1)
    validity = within < fill_here
    used_index = before_here + within
    seq_ends = jnp.cumsum(lengths)
    sequence = jnp.sum((used_index[:, None] >= seq_ends[None, :]).astype(jnp.int32), axis=1)
    seq_starts = seq_ends - lengths
    picker = sequence[:, None] == jnp.arange(seq_count, dtype=jnp.int32)[None, :]
    start_here = jnp.sum(jnp.where(picker, seq_starts[None, :], 0), axis=1)
    after = before + fill_counts
    start_block = jnp.sum((seq_starts[:, None] >= after[None, :]).astype(jnp.int32), axis=1)
    start_block = jnp.minimum(start_block, blocks_count - 1)
    block_pick = start_block[:, None] == jnp.arange(blocks_count, dtype=jnp.int32)[None, :]
    start_before = jnp.sum(jnp.where(block_pick, before[None, :], 0), axis=1)
    start_slot = start_block * block_rows + seq_starts - start_before
    slot_here = jnp.sum(jnp.where(picker, start_slot[None, :], 0), axis=1)
    first_key = jnp.where(validity, slot_here, 0).astype(jnp.int32)
    last_key = jnp.where(validity, slot_index, -1).astype(jnp.int32)
    return (validity, used_index - start_here, first_key, last_key)


def rotary_tables(position):
    half = ROT // 2
    lane = jnp.arange(2 * HEAD_DIM, dtype=jnp.int32) % HEAD_DIM
    frequency = 10000.0 ** (-(2.0 * (lane % half).astype(F32)) / ROT)
    angles = position.astype(F32)[:, None] * frequency[None, :]
    cosine, sine = jnp.cos(angles), jnp.sin(angles)
    lane = lane[None, :]
    return (
        jnp.where(lane < ROT, cosine, 1.0),
        jnp.where(lane < half, -sine, 0.0),
        jnp.where((lane >= half) & (lane < ROT), sine, 0.0),
    )


def params(**extra):
    return pltpu.CompilerParams(vmem_limit_bytes=VMEM_LIMIT, **extra)


def whole(shape):
    return pl.BlockSpec(shape, lambda *_: (0,) * len(shape))


def project_kernel(tp, nctx, per, place, *refs):
    blocks = refs[:tp]
    gain, bias, weight, weight_bias, cosine, sine_up, sine_down = refs[tp : tp + 7]
    low, full, out = refs[tp + 7 :]
    rows, width = blocks[0].shape
    depth = tp * width
    piece = out.shape[2] // 3
    strip = 64

    @pl.when(pl.program_id(0) == 0)
    def _():
        def one(index, _):
            at = pl.ds(pl.multiple_of(index * strip, strip), strip)
            parts = [block[at, :].astype(F32) for block in blocks]
            centre = sum(jnp.sum(part, axis=1, keepdims=True) for part in parts) / depth
            parts = [part - centre for part in parts]
            spread = sum(jnp.sum(part * part, axis=1, keepdims=True) for part in parts) / depth
            scaling = lax.rsqrt(spread + EPSILON)
            for step in range(tp):
                owner = lax.rem(place[0] - step + tp, tp)
                columns = pl.ds(pl.multiple_of(owner * width, width), width)
                normed = parts[step] * scaling
                low[at, columns] = (normed * gain[:, columns] + bias[:, columns]).astype(BF16)
                full[at, columns] = blocks[step][at, :]
            return 0

        lax.fori_loop(0, rows // strip, one, 0)

    product = jnp.dot(low[...], weight[...], preferred_element_type=F32) + weight_bias[...]
    for group in range(per):
        for part in range(3):
            first = (group * 3 + part) * piece
            values = product[:, first : first + piece]
            if part < 2:
                values = (
                    values * cosine[...]
                    + pltpu.roll(values, piece - ROT // 2, 1) * sine_up[...]
                    + pltpu.roll(values, ROT // 2, 1) * sine_down[...]
                )
            out[group, :, part * piece : (part + 1) * piece] = values.astype(BF16)


def project(blocks, place, gain, bias, weight, weight_bias, tables, nctx):
    tp = len(blocks)
    rows, width = blocks[0].shape
    depth = tp * width
    total = weight.shape[1]
    wide = total // nctx
    per = 2 if nctx % 2 == 0 else 1
    grid_spec = pltpu.PrefetchScalarGridSpec(
        num_scalar_prefetch=1,
        grid=(nctx // per,),
        in_specs=[whole((rows, width))] * tp
        + [whole((1, depth))] * 2
        + [
            pl.BlockSpec((depth, per * wide), lambda i, s: (0, i)),
            pl.BlockSpec((1, per * wide), lambda i, s: (0, i)),
        ]
        + [whole((rows, 2 * HEAD_DIM))] * 3,
        out_specs=[
            whole((rows, depth)),
            whole((rows, depth)),
            pl.BlockSpec((per, rows, wide), lambda i, s: (i, 0, 0)),
        ],
    )
    return pl.pallas_call(
        functools.partial(project_kernel, tp, nctx, per),
        grid_spec=grid_spec,
        out_shape=[
            jax.ShapeDtypeStruct((rows, depth), BF16),
            jax.ShapeDtypeStruct((rows, depth), BF16),
            jax.ShapeDtypeStruct((nctx, rows, wide), BF16),
        ],
        compiler_params=params(),
        cost_estimate=pl.CostEstimate(
            flops=2 * rows * depth * total, bytes_accessed=2 * depth * total, transcendentals=0
        ),
        name="project",
    )(place, *blocks, gain, bias, weight, weight_bias, *tables)


def stack_heads(tile, heads):
    lane = lax.broadcasted_iota(jnp.int32, tile.shape, 1) // HEAD_DIM
    return jnp.concatenate(
        [jnp.where(lane == head, tile, jnp.zeros_like(tile)) for head in range(heads)], axis=0
    )


def fold_heads(stacked, heads, columns):
    row = lax.broadcasted_iota(jnp.int32, (stacked.shape[0], columns), 0) // HEAD_DIM
    folded = jnp.zeros((stacked.shape[0], columns), F32)
    for head in range(heads):
        folded = folded + jnp.where(row == head, stacked[:, head * columns : (head + 1) * columns], 0.0)
    return jnp.transpose(folded)


def load_pieces(place, pieces, nctx, held, block_rows):
    chunk_rows = pieces[0].shape[0]
    chunks = len(pieces) // nctx
    for chunk in range(chunks):
        for step in range(nctx):
            source = jnp.bitwise_xor(place, step)
            first = source * block_rows + chunk * chunk_rows
            held[pl.ds(pl.multiple_of(first, chunk_rows), chunk_rows), :] = pieces[
                chunk * nctx + step
            ][...]


def attend_kernel(nctx, heads, count, block_rows, place, lows, ends, bounds, *refs):
    pieces = refs[:count]
    out, logs, held, turned, total, high, sums = refs[count:]
    tile_q, tile_k = out.shape[0], turned.shape[2]
    width = heads * HEAD_DIM
    index = pl.program_id(0)

    @pl.when(index == 0)
    def _():
        load_pieces(place[0], pieces, nctx, held, block_rows)
        for tile in range(turned.shape[0]):
            turned[tile] = jnp.transpose(held[tile * tile_k : (tile + 1) * tile_k, 2 * width :])

    query_rows = pl.ds(pl.multiple_of(index * tile_q, tile_q), tile_q)
    queries = stack_heads(held[query_rows, :width] * jnp.asarray(HEAD_DIM**-0.5, BF16), heads)
    first_key = jnp.concatenate([bounds[0:1, :]] * heads, axis=1)
    last_key = jnp.concatenate([bounds[1:2, :]] * heads, axis=1)
    total[...] = jnp.zeros_like(total)
    high[...] = jnp.full_like(high, FLOOR)
    sums[...] = jnp.zeros_like(sums)

    def one(tile, _):
        start = tile * tile_k
        keys = held[pl.ds(pl.multiple_of(start, tile_k), tile_k), width : 2 * width]
        scores = lax.dot_general(
            keys, queries, (((1,), (1,)), ((), ())), preferred_element_type=F32
        )
        row = lax.broadcasted_iota(jnp.int32, scores.shape, 0)
        last = jnp.minimum(last_key, ends[tile] - 1) - start
        allowed = (row <= last) & (row >= first_key - start)
        scores = jnp.where(allowed, scores, NEGATIVE)
        highest = jnp.maximum(high[...], jnp.max(scores, axis=0, keepdims=True))
        raised = jnp.exp(scores - highest)
        shrink = jnp.exp(high[...] - highest)
        sums[...] = sums[...] * shrink + jnp.sum(raised, axis=0, keepdims=True)
        total[...] = total[...] * shrink + jnp.dot(
            turned[tile], raised.astype(BF16), preferred_element_type=F32
        )
        high[...] = highest
        return 0

    upper = (index * tile_q + tile_q - 1) // tile_k + 1
    lax.fori_loop(lows[index], upper, one, 0)
    found = sums[...] > 0.0
    safe = jnp.where(found, sums[...], 1.0)
    out[...] = fold_heads(
        total[...] * jnp.where(found, 1.0 / safe, 0.0), heads, tile_q
    ).astype(BF16)
    log_total = jnp.where(found, high[...] + jnp.log(safe), 0.0)
    for head in range(heads):
        logs[head : head + 1, :] = log_total[:, head * tile_q : (head + 1) * tile_q]


def attend(pieces, place, lows, ends, bounds, nctx, block_rows):
    total_rows = nctx * block_rows
    width = pieces[0].shape[1] // 3
    heads = width // HEAD_DIM
    steps = total_rows // TILE_Q
    grid_spec = pltpu.PrefetchScalarGridSpec(
        num_scalar_prefetch=3,
        grid=(steps,),
        in_specs=[pl.BlockSpec((2, TILE_Q), lambda i, *_: (0, i))]
        + [whole(piece.shape) for piece in pieces],
        out_specs=[
            pl.BlockSpec((TILE_Q, width), lambda i, *_: (i, 0)),
            pl.BlockSpec((heads, TILE_Q), lambda i, *_: (0, i)),
        ],
        scratch_shapes=[
            pltpu.VMEM((total_rows, 3 * width), BF16),
            pltpu.VMEM((total_rows // TILE_K, width, TILE_K), BF16),
            pltpu.VMEM((width, heads * TILE_Q), F32),
            pltpu.VMEM((1, heads * TILE_Q), F32),
            pltpu.VMEM((1, heads * TILE_Q), F32),
        ],
    )
    return pl.pallas_call(
        functools.partial(attend_kernel, nctx, heads, len(pieces), block_rows),
        grid_spec=grid_spec,
        out_shape=[
            jax.ShapeDtypeStruct((total_rows, width), BF16),
            jax.ShapeDtypeStruct((heads, total_rows), F32),
        ],
        compiler_params=params(),
        cost_estimate=pl.CostEstimate(
            flops=8 * total_rows * total_rows * width // 4,
            bytes_accessed=8 * total_rows * width,
            transcendentals=heads * total_rows * total_rows // 4,
        ),
        name="attend",
    )(place, lows, ends, bounds, *pieces)


def attend_back_kernel(nctx, heads, count, block_rows, place, lows, ends, bounds, logs, *refs):
    pieces = refs[:count]
    grad, attended, out, held, turned, grad_keys, grad_values, grad_query = refs[count:]
    tile_q, tile_k = grad.shape[0], turned.shape[2]
    width = heads * HEAD_DIM
    index = pl.program_id(0)
    scale = jnp.asarray(HEAD_DIM**-0.5, BF16)

    @pl.when(index == 0)
    def _():
        load_pieces(place[0], pieces, nctx, held, block_rows)
        for tile in range(turned.shape[0]):
            turned[tile] = jnp.transpose(
                held[tile * tile_k : (tile + 1) * tile_k, width : 2 * width]
            )
        grad_keys[...] = jnp.zeros_like(grad_keys)
        grad_values[...] = jnp.zeros_like(grad_values)

    query_rows = pl.ds(pl.multiple_of(index * tile_q, tile_q), tile_q)
    queries = stack_heads(held[query_rows, :width] * scale, heads)
    incoming = stack_heads(grad[...], heads)
    product = jnp.transpose(grad[...].astype(F32) * attended[...].astype(F32))
    centre = jnp.concatenate(
        [
            jnp.sum(product[head * HEAD_DIM : (head + 1) * HEAD_DIM, :], axis=0, keepdims=True)
            for head in range(heads)
        ],
        axis=1,
    )
    first_key = jnp.concatenate([bounds[0:1, :]] * heads, axis=1)
    last_key = jnp.concatenate([bounds[1:2, :]] * heads, axis=1)
    log_total = jnp.concatenate([logs[head : head + 1, :] for head in range(heads)], axis=1)
    grad_query[...] = jnp.zeros_like(grad_query)

    def one(tile, _):
        start = tile * tile_k
        key_rows = pl.ds(pl.multiple_of(start, tile_k), tile_k)
        scores = lax.dot_general(
            held[key_rows, width : 2 * width],
            queries,
            (((1,), (1,)), ((), ())),
            preferred_element_type=F32,
        )
        row = lax.broadcasted_iota(jnp.int32, scores.shape, 0)
        last = jnp.minimum(last_key, ends[tile] - 1) - start
        allowed = (row <= last) & (row >= first_key - start)
        chance = jnp.exp(jnp.where(allowed, scores - log_total, NEGATIVE))
        grad_chance = lax.dot_general(
            held[key_rows, 2 * width :],
            incoming,
            (((1,), (1,)), ((), ())),
            preferred_element_type=F32,
        )
        grad_scores = (chance * (grad_chance - centre)).astype(BF16)
        grad_values[key_rows, :] += jnp.dot(
            chance.astype(BF16), incoming, preferred_element_type=F32
        )
        grad_keys[key_rows, :] += jnp.dot(grad_scores, queries, preferred_element_type=F32)
        grad_query[...] += jnp.dot(turned[tile], grad_scores, preferred_element_type=F32)
        return 0

    upper = (index * tile_q + tile_q - 1) // tile_k + 1
    lax.fori_loop(lows[index], upper, one, 0)
    out[query_rows, :width] = (
        fold_heads(grad_query[...], heads, tile_q) * HEAD_DIM**-0.5
    ).astype(BF16)

    @pl.when(index == pl.num_programs(0) - 1)
    def _():
        out[:, width : 2 * width] = grad_keys[...].astype(BF16)
        out[:, 2 * width :] = grad_values[...].astype(BF16)


def attend_back(pieces, place, lows, ends, bounds, logs, grad, attended, nctx, block_rows):
    total_rows, width = grad.shape
    heads = width // HEAD_DIM
    steps = total_rows // TILE_Q
    grid_spec = pltpu.PrefetchScalarGridSpec(
        num_scalar_prefetch=3,
        grid=(steps,),
        in_specs=[
            pl.BlockSpec((2, TILE_Q), lambda i, *_: (0, i)),
            pl.BlockSpec((heads, TILE_Q), lambda i, *_: (0, i)),
        ]
        + [whole(piece.shape) for piece in pieces]
        + [pl.BlockSpec((TILE_Q, width), lambda i, *_: (i, 0))] * 2,
        out_specs=whole((total_rows, 3 * width)),
        scratch_shapes=[
            pltpu.VMEM((total_rows, 3 * width), BF16),
            pltpu.VMEM((total_rows // TILE_K, width, TILE_K), BF16),
            pltpu.VMEM((total_rows, width), F32),
            pltpu.VMEM((total_rows, width), F32),
            pltpu.VMEM((width, heads * TILE_Q), F32),
        ],
    )
    return pl.pallas_call(
        functools.partial(attend_back_kernel, nctx, heads, len(pieces), block_rows),
        grid_spec=grid_spec,
        out_shape=jax.ShapeDtypeStruct((total_rows, 3 * width), BF16),
        compiler_params=params(),
        cost_estimate=pl.CostEstimate(
            flops=20 * total_rows * total_rows * width // 4,
            bytes_accessed=16 * total_rows * width,
            transcendentals=heads * total_rows * total_rows // 4,
        ),
        name="attend_back",
    )(place, lows, ends, bounds, logs, *pieces, grad, attended)


def finish_kernel(nctx, chunk, place, *refs):
    pieces = refs[:nctx]
    (cosine, sine_up, sine_down, full, extra, gain, weight) = refs[nctx : nctx + 7]
    out, low, bias_grad, gain_grad, shift_grad, spare = refs[nctx + 7 :]
    rows, wide = pieces[0].shape
    piece = wide // 3
    tp, width = out.shape[0], out.shape[2]
    depth = tp * width
    strip = spare.shape[0]
    extra_rows = extra.shape[0]

    @pl.when(pl.program_id(0) == 0)
    def _():
        bias_grad[...] = jnp.zeros_like(bias_grad)
        gain_grad[...] = jnp.zeros_like(gain_grad)
        shift_grad[...] = jnp.zeros_like(shift_grad)

    for step in range(nctx):
        source = jnp.bitwise_xor(place[0], step)
        for part in range(3):
            values = pieces[step][:, part * piece : (part + 1) * piece].astype(F32)
            if part < 2:
                values = (
                    values * cosine[...]
                    - pltpu.roll(values, piece - ROT // 2, 1) * sine_up[...]
                    - pltpu.roll(values, ROT // 2, 1) * sine_down[...]
                )
            columns = pl.ds(pl.multiple_of(source * wide + part * piece, piece), piece)
            bias_grad[:, columns] += jnp.sum(values, axis=0, keepdims=True)
            low[:, columns] = values.astype(BF16)

    incoming = lax.dot_general(
        low[...], weight[...], (((1,), (1,)), ((), ())), preferred_element_type=F32
    )
    source = full[...].astype(F32)
    centre = jnp.mean(source, axis=1, keepdims=True)
    source = source - centre
    scaling = lax.rsqrt(jnp.mean(source * source, axis=1, keepdims=True) + EPSILON)
    normed = source * scaling
    shift_grad[...] += jnp.sum(incoming, axis=0, keepdims=True)
    gain_grad[...] += jnp.sum(incoming * normed, axis=0, keepdims=True)
    scaled = incoming * gain[...]
    spare[...] = scaling * (
        scaled
        - jnp.mean(scaled, axis=1, keepdims=True)
        - normed * jnp.mean(scaled * normed, axis=1, keepdims=True)
    )
    first = chunk * pl.num_programs(0) * strip + pl.program_id(0) * strip
    wanted = place[1] * extra_rows

    if strip <= extra_rows:

        @pl.when((first >= wanted) & (first < wanted + extra_rows))
        def _():
            spare[...] += extra[pl.ds(pl.multiple_of(first - wanted, strip), strip), :]

    else:

        @pl.when((wanted >= first) & (wanted < first + strip))
        def _():
            spare[pl.ds(pl.multiple_of(wanted - first, extra_rows), extra_rows), :] += extra[...]

    for block in range(tp):
        out[block] = spare[:, block * width : (block + 1) * width].astype(BF16)


def finish(pieces, place, tables, full, extra, gain, weight, chunk, tp):
    rows, wide = pieces[0].shape
    depth = full.shape[1]
    total = weight.shape[1]
    strip = 256
    steps = rows // strip
    width = depth // tp
    nctx = len(pieces)
    by_rows = lambda columns: pl.BlockSpec((strip, columns), lambda i, s: (i, 0))
    grid_spec = pltpu.PrefetchScalarGridSpec(
        num_scalar_prefetch=1,
        grid=(steps,),
        in_specs=[by_rows(wide)] * nctx
        + [by_rows(2 * HEAD_DIM)] * 3
        + [by_rows(depth), whole(extra.shape), whole((1, depth)), whole(weight.shape)],
        out_specs=[
            pl.BlockSpec((tp, strip, width), lambda i, s: (0, i, 0)),
            by_rows(total),
            whole((1, total)),
            whole((1, depth)),
            whole((1, depth)),
        ],
        scratch_shapes=[pltpu.VMEM((strip, depth), F32)],
    )
    return pl.pallas_call(
        functools.partial(finish_kernel, nctx, chunk),
        grid_spec=grid_spec,
        out_shape=[
            jax.ShapeDtypeStruct((tp, rows, width), BF16),
            jax.ShapeDtypeStruct((rows, total), BF16),
            jax.ShapeDtypeStruct((1, total), F32),
            jax.ShapeDtypeStruct((1, depth), F32),
            jax.ShapeDtypeStruct((1, depth), F32),
        ],
        compiler_params=params(),
        cost_estimate=pl.CostEstimate(
            flops=2 * rows * depth * total, bytes_accessed=2 * depth * total, transcendentals=0
        ),
        name="finish",
    )(place, *pieces, *tables, full, extra, gain, weight)


def join_kernel(tp, place, *refs):
    blocks, out = refs[:tp], refs[tp]
    width = blocks[0].shape[1]
    for step in range(tp):
        owner = lax.rem(place[0] - step + tp, tp)
        out[:, pl.ds(pl.multiple_of(owner * width, width), width)] = blocks[step][...]


def join(blocks, place):
    tp = len(blocks)
    rows, width = blocks[0].shape
    strip = 256
    grid_spec = pltpu.PrefetchScalarGridSpec(
        num_scalar_prefetch=1,
        grid=(rows // strip,),
        in_specs=[pl.BlockSpec((strip, width), lambda i, s: (i, 0))] * tp,
        out_specs=pl.BlockSpec((strip, tp * width), lambda i, s: (i, 0)),
    )
    return pl.pallas_call(
        functools.partial(join_kernel, tp),
        grid_spec=grid_spec,
        out_shape=jax.ShapeDtypeStruct((rows, tp * width), BF16),
        compiler_params=params(),
        cost_estimate=pl.CostEstimate(
            flops=0, bytes_accessed=4 * rows * tp * width, transcendentals=0
        ),
        name="join",
    )(place, *blocks)


def norm_forward(values, gain, norm_bias):
    centre = jnp.mean(values, axis=-1, keepdims=True)
    centered = values - centre
    spread = jnp.mean(centered * centered, axis=-1, keepdims=True)
    scaling = lax.rsqrt(spread + EPSILON)
    normed = centered * scaling
    return (normed * gain + norm_bias, normed, scaling)


def norm_backward(incoming, normed, scaling, gain):
    scaled = incoming * gain
    return scaling * (
        scaled
        - jnp.mean(scaled, axis=-1, keepdims=True)
        - normed * jnp.mean(scaled * normed, axis=-1, keepdims=True)
    )


def contract_rows(left, right):
    return lax.dot_general(
        left, right, (((0,), (0,)), ((), ())), preferred_element_type=F32
    )


def contract_cols(left, right):
    return lax.dot_general(
        left, right, (((1,), (1,)), ((), ())), preferred_element_type=F32
    )


def pick(stack, index):
    return lax.dynamic_index_in_dim(stack, index, 0, keepdims=False)


def after(value, *others):
    return lax.optimization_barrier((value, *others))[0]


def shards(
    nctx,
    tp,
    inputs,
    cotangent,
    first_gain,
    first_bias,
    qkv_weight,
    qkv_bias,
    out_weight,
    second_gain,
    second_bias,
    gate_weight,
    up_weight,
    down_weight,
    lengths,
    fill_counts,
):
    data = ("fsdp", "ctx")
    block_rows, width = inputs.shape
    depth = tp * width
    tensor_index = lax.axis_index("tp")
    context_index = lax.axis_index("ctx")
    part_rows = block_rows // tp
    chunk_rows = block_rows // CHUNKS
    head_width = qkv_weight.shape[2]
    piece = head_width // nctx
    wide = 3 * piece
    place_tp = tensor_index.astype(jnp.int32)[None]
    place_ctx = context_index.astype(jnp.int32)[None]

    def ring(value):
        return lax.ppermute(value, "tp", [(i, (i + 1) % tp) for i in range(tp)])

    def swap(value, step):
        return lax.ppermute(value, "ctx", [(i, i ^ step) for i in range(nctx)])

    own_qkv = (
        qkv_weight.reshape(-1, 3, nctx, piece).transpose(0, 2, 1, 3).reshape(-1, 3 * head_width)
    )
    full_qkv = lax.all_gather(own_qkv, data, axis=0, tiled=True)
    full_out = lax.all_gather(
        lax.all_gather(out_weight, "tp", axis=0, tiled=True), data, axis=1, tiled=True
    )
    full_gate = lax.all_gather(gate_weight, data, axis=0, tiled=True)
    full_up = lax.all_gather(up_weight, data, axis=0, tiled=True)
    full_down = lax.all_gather(down_weight, data, axis=1, tiled=True)

    validity, position, first_key, last_key = layout(lengths[0], fill_counts[0], block_rows)
    own_position = lax.dynamic_slice_in_dim(position, context_index * block_rows, block_rows, 0)
    tables = rotary_tables(own_position)
    bounds = jnp.stack([first_key, last_key])
    tile_first = first_key[::TILE_Q]
    tile_count = tile_first.shape[0]
    lows = jnp.where(validity[::TILE_Q], tile_first // TILE_K, tile_count * TILE_Q).astype(jnp.int32)
    key_block = jnp.arange(0, nctx * block_rows, TILE_K, dtype=jnp.int32) // block_rows
    ends = (
        key_block * block_rows
        + jnp.sum(
            jnp.where(
                key_block[:, None] == jnp.arange(nctx, dtype=jnp.int32)[None, :],
                fill_counts[0][None, :],
                0,
            ),
            axis=1,
        )
    ).astype(jnp.int32)

    flat_bias = qkv_bias.reshape(3, nctx, piece).transpose(1, 0, 2).reshape(1, -1)
    gain_one, bias_one = first_gain[None], first_bias[None]

    rings = [[inputs[c * chunk_rows : (c + 1) * chunk_rows]] for c in range(CHUNKS)]
    for chunk in range(CHUNKS):
        for _ in range(tp - 1):
            rings[chunk].append(ring(rings[chunk][-1]))
    lows_one, fulls, pieces, chunk_tables = [], [], [], []
    for chunk in range(CHUNKS):
        at = slice(chunk * chunk_rows, (chunk + 1) * chunk_rows)
        chunk_tables.append([table[at] for table in tables])
        low, full, outgoing = project(
            rings[chunk],
            place_tp,
            gain_one,
            bias_one,
            full_qkv,
            flat_bias,
            chunk_tables[chunk],
            nctx,
        )
        lows_one.append(low)
        fulls.append(full)
        pieces.append(pick(outgoing, context_index))
        for step in range(1, nctx):
            pieces.append(swap(pick(outgoing, context_index ^ step), step))

    cot_ring = [after(cotangent, rings[-1][-1])]
    for _ in range(tp - 1):
        cot_ring.append(ring(cot_ring[-1]))
    full_cot = join(cot_ring, place_tp)

    attended, logs = attend(pieces, place_ctx, lows, ends, bounds, nctx, block_rows)
    returned = lax.all_to_all(
        attended.reshape(nctx * tp, part_rows, piece),
        ("ctx", "tp"),
        split_axis=0,
        concat_axis=0,
        tiled=True,
    )
    returned = (
        returned.reshape(nctx, tp, part_rows, piece)
        .transpose(2, 1, 0, 3)
        .reshape(part_rows, depth)
    )
    attention = jnp.dot(returned, full_out, preferred_element_type=F32)
    source_rows = pick(
        jnp.concatenate([full.reshape(-1, part_rows, depth) for full in fulls], axis=0),
        tensor_index,
    )
    mixed = source_rows.astype(F32) + attention
    second_norm, second_normed, second_scaling = norm_forward(mixed, second_gain, second_bias)
    second_low = second_norm.astype(BF16)

    cot_blocks = full_cot.reshape(tp, part_rows, depth)
    seconds, hiddens, gates, ups, partials = [second_low], [], [], [], []
    for _ in range(tp - 1):
        seconds.append(ring(seconds[-1]))
    owners = [(tensor_index - step + tp) % tp for step in range(tp)]
    for step in range(tp):
        low = seconds[step]
        cot_rows = pick(cot_blocks, owners[step])
        gate_proj = jnp.dot(low, full_gate, preferred_element_type=F32)
        up_proj = jnp.dot(low, full_up, preferred_element_type=F32)
        sigmoid_gate = jax.nn.sigmoid(gate_proj)
        activated = gate_proj * sigmoid_gate
        hiddens.append((activated * up_proj).astype(BF16))
        grad_hidden = contract_cols(cot_rows, full_down)
        gates.append(
            (grad_hidden * up_proj * sigmoid_gate * (1.0 + gate_proj * (1.0 - sigmoid_gate))).astype(
                BF16
            )
        )
        ups.append((grad_hidden * activated).astype(BF16))
        partials.append(
            contract_cols(gates[step], full_gate) + contract_cols(ups[step], full_up)
        )

    travelling = partials[1 % tp].astype(BF16)
    for step in range(1, tp):
        arrived = ring(travelling).astype(F32) + partials[(step + 1) % tp]
        travelling = arrived.astype(BF16)
    second_incoming = arrived if tp > 1 else partials[0]

    cot_own = pick(cot_blocks, tensor_index).astype(F32)
    grad_mixed = cot_own + norm_backward(
        second_incoming, second_normed, second_scaling, second_gain
    )
    grad_second_gain = jnp.sum(second_incoming * second_normed, axis=0)
    grad_second_bias = jnp.sum(second_incoming, axis=0)
    mixed_low = grad_mixed.astype(BF16)
    grad_returned = contract_cols(mixed_low, full_out).astype(BF16)
    grad_heads = lax.all_to_all(
        grad_returned.reshape(part_rows, tp, nctx, piece)
        .transpose(2, 1, 0, 3)
        .reshape(nctx * tp, part_rows, piece),
        ("ctx", "tp"),
        split_axis=0,
        concat_axis=0,
        tiled=True,
    ).reshape(nctx * block_rows, piece)

    def ordered(blocks):
        stack = jnp.zeros((tp,) + blocks[0].shape, blocks[0].dtype)
        for step in range(tp):
            stack = lax.dynamic_update_index_in_dim(stack, blocks[step], owners[step], 0)
        return stack.reshape(block_rows, -1)

    hidden = ordered(hiddens)
    all_gate, all_up, all_second = ordered(gates), ordered(ups), ordered(seconds)
    feedforward = jnp.dot(hidden, full_down, preferred_element_type=F32)
    mine = jnp.arange(tp, dtype=jnp.int32)[:, None, None] == tensor_index
    feedforward = (
        feedforward.reshape(tp, part_rows, depth) + jnp.where(mine, mixed[None], 0.0)
    ).astype(BF16)
    feedforward = feedforward.reshape(block_rows, tp, width).transpose(1, 0, 2)
    feedforward = after(feedforward, second_incoming)
    travelling = pick(feedforward, owners[1 % tp])
    for step in range(1, tp):
        arrived = ring(travelling).astype(F32) + pick(feedforward, owners[(step + 1) % tp]).astype(
            F32
        )
        travelling = arrived.astype(BF16)
    layer_out = travelling

    grad_gate = contract_rows(all_second, all_gate).astype(BF16)
    grad_up = contract_rows(all_second, all_up).astype(BF16)
    grad_down = contract_rows(hidden, full_cot).astype(BF16)
    grad_out = contract_rows(returned, mixed_low).astype(BF16)
    total_gate = lax.psum_scatter(grad_gate, data, scatter_dimension=0, tiled=True)
    total_up = lax.psum_scatter(grad_up, data, scatter_dimension=0, tiled=True)
    total_down = lax.psum_scatter(grad_down, data, scatter_dimension=1, tiled=True)
    total_out = lax.psum_scatter(
        lax.psum_scatter(grad_out, data, scatter_dimension=1, tiled=True),
        "tp",
        scatter_dimension=0,
        tiled=True,
    )

    grad_grouped = attend_back(
        pieces, place_ctx, lows, ends, bounds, logs, grad_heads, attended, nctx, block_rows
    )
    grad_grouped = grad_grouped.reshape(nctx, CHUNKS, chunk_rows, wide)
    place_both = jnp.stack([context_index, tensor_index]).astype(jnp.int32)
    grad_lows, bias_grads, gain_grads, shift_grads, grad_rows = [], [], [], [], []
    for chunk in range(CHUNKS):
        outgoing = grad_grouped[:, chunk]
        arrived = [pick(outgoing, context_index)]
        for step in range(1, nctx):
            arrived.append(swap(pick(outgoing, context_index ^ step), step))
        partial, low, bias_grad, gain_grad, shift_grad = finish(
            arrived,
            place_both,
            chunk_tables[chunk],
            fulls[chunk],
            grad_mixed,
            gain_one,
            full_qkv,
            chunk,
            tp,
        )
        grad_lows.append(low)
        bias_grads.append(bias_grad)
        gain_grads.append(gain_grad)
        shift_grads.append(shift_grad)
        travelling = pick(partial, owners[1 % tp])
        for step in range(1, tp):
            total = ring(travelling).astype(F32) + pick(partial, owners[(step + 1) % tp]).astype(
                F32
            )
            travelling = total.astype(BF16)
        grad_rows.append(travelling)
    grad_inputs = jnp.concatenate(grad_rows, axis=0)

    grad_qkv = contract_rows(
        jnp.concatenate(lows_one, axis=0), jnp.concatenate(grad_lows, axis=0)
    ).astype(BF16)
    total_qkv = lax.psum_scatter(grad_qkv, data, scatter_dimension=0, tiled=True)
    total_qkv = (
        total_qkv.astype(F32)
        .reshape(-1, nctx, 3, piece)
        .transpose(0, 2, 1, 3)
        .reshape(-1, 3, head_width)
    )

    bias_total = lax.psum(sum(bias_grads).astype(BF16), data).astype(F32)
    bias_total = bias_total.reshape(nctx, 3, piece).transpose(1, 0, 2).reshape(3, head_width)
    small = jnp.stack(
        [sum(gain_grads)[0], sum(shift_grads)[0], grad_second_gain, grad_second_bias]
    )
    small = lax.psum(small.astype(BF16), ("fsdp", "ctx", "tp")).astype(F32)
    return (
        layer_out,
        grad_inputs,
        small[0],
        small[1],
        total_qkv,
        bias_total,
        total_out.astype(F32),
        small[2],
        small[3],
        total_gate.astype(F32),
        total_up.astype(F32),
        total_down.astype(F32),
    )


def solution(mesh):
    data = ("fsdp", "ctx")
    by_rows = P(data, "tp")
    by_columns = P("tp", data)
    qkv = P(data, None, "tp")
    return jax.shard_map(
        functools.partial(shards, mesh.shape["ctx"], mesh.shape["tp"]),
        mesh=mesh,
        in_specs=(
            by_rows,
            by_rows,
            P(),
            P(),
            qkv,
            P(None, "tp"),
            by_columns,
            P(),
            P(),
            by_rows,
            by_rows,
            by_columns,
            P("fsdp", None),
            P("fsdp", None),
        ),
        out_specs=(
            by_rows,
            by_rows,
            P(),
            P(),
            qkv,
            P(None, "tp"),
            by_columns,
            P(),
            P(),
            by_rows,
            by_rows,
            by_columns,
        ),
        check_vma=False,
    )
```

```python
import functools

import jax
import jax.numpy as jnp
from jax import lax
from jax.experimental import pallas as pl
from jax.experimental.pallas import tpu as pltpu
from jax.sharding import PartitionSpec as P

HEAD_DIM = 64
ROT = 16
EPSILON = 1e-05
NEGATIVE = -1e30
FLOOR = -1e20
VMEM_LIMIT = 56 * 1024 * 1024
TILE_Q = 512
TILE_K = 512
CHUNKS = 2

F32 = jnp.float32
BF16 = jnp.bfloat16


def layout(lengths, fill_counts, block_rows):
    blocks_count = fill_counts.shape[0]
    seq_count = lengths.shape[0]
    slot_index = jnp.arange(blocks_count * block_rows, dtype=jnp.int32)
    block_of = slot_index // block_rows
    within = slot_index - block_of * block_rows
    chooser = block_of[:, None] == jnp.arange(blocks_count, dtype=jnp.int32)[None, :]
    fill_here = jnp.sum(jnp.where(chooser, fill_counts[None, :], 0), axis=1)
    before = jnp.cumsum(fill_counts) - fill_counts
    before_here = jnp.sum(jnp.where(chooser, before[None, :], 0), axis=1)
    validity = within < fill_here
    used_index = before_here + within
    seq_ends = jnp.cumsum(lengths)
    sequence = jnp.sum((used_index[:, None] >= seq_ends[None, :]).astype(jnp.int32), axis=1)
    seq_starts = seq_ends - lengths
    picker = sequence[:, None] == jnp.arange(seq_count, dtype=jnp.int32)[None, :]
    start_here = jnp.sum(jnp.where(picker, seq_starts[None, :], 0), axis=1)
    after = before + fill_counts
    start_block = jnp.sum((seq_starts[:, None] >= after[None, :]).astype(jnp.int32), axis=1)
    start_block = jnp.minimum(start_block, blocks_count - 1)
    block_pick = start_block[:, None] == jnp.arange(blocks_count, dtype=jnp.int32)[None, :]
    start_before = jnp.sum(jnp.where(block_pick, before[None, :], 0), axis=1)
    start_slot = start_block * block_rows + seq_starts - start_before
    slot_here = jnp.sum(jnp.where(picker, start_slot[None, :], 0), axis=1)
    first_key = jnp.where(validity, slot_here, 0).astype(jnp.int32)
    last_key = jnp.where(validity, slot_index, -1).astype(jnp.int32)
    return (validity, used_index - start_here, first_key, last_key)


def rotary_tables(position):
    half = ROT // 2
    lane = jnp.arange(2 * HEAD_DIM, dtype=jnp.int32) % HEAD_DIM
    frequency = 10000.0 ** (-(2.0 * (lane % half).astype(F32)) / ROT)
    angles = position.astype(F32)[:, None] * frequency[None, :]
    cosine, sine = jnp.cos(angles), jnp.sin(angles)
    lane = lane[None, :]
    return (
        jnp.where(lane < ROT, cosine, 1.0),
        jnp.where(lane < half, -sine, 0.0),
        jnp.where((lane >= half) & (lane < ROT), sine, 0.0),
    )


def params(**extra):
    return pltpu.CompilerParams(vmem_limit_bytes=VMEM_LIMIT, **extra)


def whole(shape):
    return pl.BlockSpec(shape, lambda *_: (0,) * len(shape))


def anywhere(count):
    return [pl.BlockSpec(memory_space=pl.ANY)] * count


def halves(place, half_depth):
    mine = pl.multiple_of(place[2] * half_depth, half_depth)
    theirs = pl.multiple_of((1 - place[2]) * half_depth, half_depth)
    return pl.ds(mine, half_depth), pl.ds(theirs, half_depth)


def dot(left, right):
    return jnp.dot(left, right, preferred_element_type=F32)


def dot_turned(left, right):
    return lax.dot_general(left, right, (((1,), (1,)), ((), ())), preferred_element_type=F32)


def tie(value, *needed):
    def kernel(*refs):
        del refs

    return pl.pallas_call(
        kernel,
        in_specs=anywhere(1 + len(needed)),
        out_specs=pl.BlockSpec(memory_space=pl.ANY),
        out_shape=jax.ShapeDtypeStruct(value.shape, value.dtype),
        input_output_aliases={0: 0},
        name="tie",
    )(value, *needed)


def add_kernel(left, right, *refs):
    refs[-1][...] = (left[...].astype(F32) + right[...].astype(F32)).astype(BF16)


def add(left, right, *needed):
    rows, columns = left.shape
    strip = min(rows, 128)
    block = pl.BlockSpec((strip, columns), lambda i: (i, 0))
    return pl.pallas_call(
        add_kernel,
        grid=(rows // strip,),
        in_specs=[block, block] + anywhere(len(needed)),
        out_specs=block,
        out_shape=jax.ShapeDtypeStruct(left.shape, BF16),
        compiler_params=params(),
        cost_estimate=pl.CostEstimate(
            flops=rows * columns, bytes_accessed=6 * rows * columns, transcendentals=0
        ),
        name="ring_add",
    )(left, right, *needed)


def project_kernel(tp, per, spans, place, *refs):
    blocks = refs[:tp]
    gain, bias, mine, theirs, weight_bias, cosine, sine_up, sine_down = refs[tp : tp + 8]
    low, full, out = refs[tp + 8 :]
    rows, width = blocks[0].shape
    depth = tp * width
    piece = out.shape[2] // 3
    strip = 64

    @pl.when(pl.program_id(0) == 0)
    def _():
        def one(index, _):
            at = pl.ds(pl.multiple_of(index * strip, strip), strip)
            parts = [block[at, :].astype(F32) for block in blocks]
            centre = sum(jnp.sum(part, axis=1, keepdims=True) for part in parts) / depth
            parts = [part - centre for part in parts]
            spread = sum(jnp.sum(part * part, axis=1, keepdims=True) for part in parts) / depth
            scaling = lax.rsqrt(spread + EPSILON)
            for step in range(tp):
                owner = lax.rem(place[0] - step + tp, tp)
                normed = parts[step] * scaling
                for first, size, base, stride in spans:
                    columns = pl.ds(pl.multiple_of(base + owner * stride, size), size)
                    low[at, columns] = (
                        normed[:, first : first + size] * gain[:, columns] + bias[:, columns]
                    ).astype(BF16)
                    full[at, columns] = blocks[step][at, first : first + size]
            return 0

        lax.fori_loop(0, rows // strip, one, 0)

    at_mine, at_theirs = halves(place, depth // 2)
    product = dot(low[:, at_mine], mine[...]) + dot(low[:, at_theirs], theirs[...])
    product = product + weight_bias[...]
    for group in range(per):
        for part in range(3):
            first = (group * 3 + part) * piece
            values = product[:, first : first + piece]
            if part < 2:
                values = (
                    values * cosine[...]
                    + pltpu.roll(values, piece - ROT // 2, 1) * sine_up[...]
                    + pltpu.roll(values, ROT // 2, 1) * sine_down[...]
                )
            out[group, :, part * piece : (part + 1) * piece] = values.astype(BF16)


def project(blocks, place, gain, bias, weights, weight_bias, tables, nctx, spans):
    tp = len(blocks)
    rows, width = blocks[0].shape
    depth = tp * width
    total = weights[0].shape[1]
    wide = total // nctx
    per = 2 if nctx % 2 == 0 else 1
    by_columns = lambda count: pl.BlockSpec((count, per * wide), lambda i, s: (0, i))
    grid_spec = pltpu.PrefetchScalarGridSpec(
        num_scalar_prefetch=1,
        grid=(nctx // per,),
        in_specs=[whole((rows, width))] * tp
        + [whole((1, depth))] * 2
        + [by_columns(depth // 2)] * 2
        + [by_columns(1)]
        + [whole((rows, 2 * HEAD_DIM))] * 3,
        out_specs=[
            whole((rows, depth)),
            whole((rows, depth)),
            pl.BlockSpec((per, rows, wide), lambda i, s: (i, 0, 0)),
        ],
    )
    return pl.pallas_call(
        functools.partial(project_kernel, tp, per, spans),
        grid_spec=grid_spec,
        out_shape=[
            jax.ShapeDtypeStruct((rows, depth), BF16),
            jax.ShapeDtypeStruct((rows, depth), BF16),
            jax.ShapeDtypeStruct((nctx, rows, wide), BF16),
        ],
        compiler_params=params(),
        cost_estimate=pl.CostEstimate(
            flops=2 * rows * depth * total, bytes_accessed=2 * depth * total, transcendentals=0
        ),
        name="project",
    )(place, *blocks, gain, bias, *weights, weight_bias, *tables)


def stack_heads(tile, heads):
    lane = lax.broadcasted_iota(jnp.int32, tile.shape, 1) // HEAD_DIM
    return jnp.concatenate(
        [jnp.where(lane == head, tile, jnp.zeros_like(tile)) for head in range(heads)], axis=0
    )


def fold_heads(stacked, heads, columns):
    row = lax.broadcasted_iota(jnp.int32, (stacked.shape[0], columns), 0) // HEAD_DIM
    folded = jnp.zeros((stacked.shape[0], columns), F32)
    for head in range(heads):
        folded = folded + jnp.where(row == head, stacked[:, head * columns : (head + 1) * columns], 0.0)
    return jnp.transpose(folded)


def load_pieces(place, pieces, nctx, held, block_rows):
    chunk_rows = pieces[0].shape[0]
    chunks = len(pieces) // nctx
    for chunk in range(chunks):
        for step in range(nctx):
            source = jnp.bitwise_xor(place, step)
            first = source * block_rows + chunk * chunk_rows
            held[pl.ds(pl.multiple_of(first, chunk_rows), chunk_rows), :] = pieces[
                chunk * nctx + step
            ][...]


def attend_kernel(nctx, heads, count, block_rows, place, lows, ends, bounds, *refs):
    pieces = refs[:count]
    out, logs, held, turned, total, high, sums = refs[count:]
    tile_q, tile_k = out.shape[0], turned.shape[2]
    width = heads * HEAD_DIM
    index = pl.program_id(0)

    @pl.when(index == 0)
    def _():
        load_pieces(place[0], pieces, nctx, held, block_rows)
        for tile in range(turned.shape[0]):
            turned[tile] = jnp.transpose(held[tile * tile_k : (tile + 1) * tile_k, 2 * width :])

    query_rows = pl.ds(pl.multiple_of(index * tile_q, tile_q), tile_q)
    queries = stack_heads(held[query_rows, :width] * jnp.asarray(HEAD_DIM**-0.5, BF16), heads)
    first_key = jnp.concatenate([bounds[0:1, :]] * heads, axis=1)
    last_key = jnp.concatenate([bounds[1:2, :]] * heads, axis=1)
    total[...] = jnp.zeros_like(total)
    high[...] = jnp.full_like(high, FLOOR)
    sums[...] = jnp.zeros_like(sums)

    def one(tile, _):
        start = tile * tile_k
        keys = held[pl.ds(pl.multiple_of(start, tile_k), tile_k), width : 2 * width]
        scores = lax.dot_general(
            keys, queries, (((1,), (1,)), ((), ())), preferred_element_type=F32
        )
        row = lax.broadcasted_iota(jnp.int32, scores.shape, 0)
        last = jnp.minimum(last_key, ends[tile] - 1) - start
        allowed = (row <= last) & (row >= first_key - start)
        scores = jnp.where(allowed, scores, NEGATIVE)
        highest = jnp.maximum(high[...], jnp.max(scores, axis=0, keepdims=True))
        raised = jnp.exp(scores - highest)
        shrink = jnp.exp(high[...] - highest)
        sums[...] = sums[...] * shrink + jnp.sum(raised, axis=0, keepdims=True)
        total[...] = total[...] * shrink + jnp.dot(
            turned[tile], raised.astype(BF16), preferred_element_type=F32
        )
        high[...] = highest
        return 0

    upper = (index * tile_q + tile_q - 1) // tile_k + 1
    lax.fori_loop(lows[index], upper, one, 0)
    found = sums[...] > 0.0
    safe = jnp.where(found, sums[...], 1.0)
    out[...] = fold_heads(
        total[...] * jnp.where(found, 1.0 / safe, 0.0), heads, tile_q
    ).astype(BF16)
    log_total = jnp.where(found, high[...] + jnp.log(safe), 0.0)
    for head in range(heads):
        logs[head : head + 1, :] = log_total[:, head * tile_q : (head + 1) * tile_q]


def attend(pieces, place, lows, ends, bounds, nctx, block_rows):
    total_rows = nctx * block_rows
    width = pieces[0].shape[1] // 3
    heads = width // HEAD_DIM
    steps = total_rows // TILE_Q
    grid_spec = pltpu.PrefetchScalarGridSpec(
        num_scalar_prefetch=3,
        grid=(steps,),
        in_specs=[pl.BlockSpec((2, TILE_Q), lambda i, *_: (0, i))]
        + [whole(piece.shape) for piece in pieces],
        out_specs=[
            pl.BlockSpec((TILE_Q, width), lambda i, *_: (i, 0)),
            pl.BlockSpec((heads, TILE_Q), lambda i, *_: (0, i)),
        ],
        scratch_shapes=[
            pltpu.VMEM((total_rows, 3 * width), BF16),
            pltpu.VMEM((total_rows // TILE_K, width, TILE_K), BF16),
            pltpu.VMEM((width, heads * TILE_Q), F32),
            pltpu.VMEM((1, heads * TILE_Q), F32),
            pltpu.VMEM((1, heads * TILE_Q), F32),
        ],
    )
    return pl.pallas_call(
        functools.partial(attend_kernel, nctx, heads, len(pieces), block_rows),
        grid_spec=grid_spec,
        out_shape=[
            jax.ShapeDtypeStruct((total_rows, width), BF16),
            jax.ShapeDtypeStruct((heads, total_rows), F32),
        ],
        compiler_params=params(),
        cost_estimate=pl.CostEstimate(
            flops=8 * total_rows * total_rows * width // 4,
            bytes_accessed=8 * total_rows * width,
            transcendentals=heads * total_rows * total_rows // 4,
        ),
        name="attend",
    )(place, lows, ends, bounds, *pieces)


def attend_back_kernel(nctx, heads, count, block_rows, place, lows, ends, bounds, logs, *refs):
    pieces = refs[:count]
    grad, attended, out, held, turned, grad_keys, grad_values, grad_query = refs[count:]
    tile_q, tile_k = grad.shape[0], turned.shape[2]
    width = heads * HEAD_DIM
    index = pl.program_id(0)
    scale = jnp.asarray(HEAD_DIM**-0.5, BF16)

    @pl.when(index == 0)
    def _():
        load_pieces(place[0], pieces, nctx, held, block_rows)
        for tile in range(turned.shape[0]):
            turned[tile] = jnp.transpose(
                held[tile * tile_k : (tile + 1) * tile_k, width : 2 * width]
            )
        grad_keys[...] = jnp.zeros_like(grad_keys)
        grad_values[...] = jnp.zeros_like(grad_values)

    query_rows = pl.ds(pl.multiple_of(index * tile_q, tile_q), tile_q)
    queries = stack_heads(held[query_rows, :width] * scale, heads)
    incoming = stack_heads(grad[...], heads)
    product = jnp.transpose(grad[...].astype(F32) * attended[...].astype(F32))
    centre = jnp.concatenate(
        [
            jnp.sum(product[head * HEAD_DIM : (head + 1) * HEAD_DIM, :], axis=0, keepdims=True)
            for head in range(heads)
        ],
        axis=1,
    )
    first_key = jnp.concatenate([bounds[0:1, :]] * heads, axis=1)
    last_key = jnp.concatenate([bounds[1:2, :]] * heads, axis=1)
    log_total = jnp.concatenate([logs[head : head + 1, :] for head in range(heads)], axis=1)
    grad_query[...] = jnp.zeros_like(grad_query)

    def one(tile, _):
        start = tile * tile_k
        key_rows = pl.ds(pl.multiple_of(start, tile_k), tile_k)
        scores = lax.dot_general(
            held[key_rows, width : 2 * width],
            queries,
            (((1,), (1,)), ((), ())),
            preferred_element_type=F32,
        )
        row = lax.broadcasted_iota(jnp.int32, scores.shape, 0)
        last = jnp.minimum(last_key, ends[tile] - 1) - start
        allowed = (row <= last) & (row >= first_key - start)
        chance = jnp.exp(jnp.where(allowed, scores - log_total, NEGATIVE))
        grad_chance = lax.dot_general(
            held[key_rows, 2 * width :],
            incoming,
            (((1,), (1,)), ((), ())),
            preferred_element_type=F32,
        )
        grad_scores = (chance * (grad_chance - centre)).astype(BF16)
        grad_values[key_rows, :] += jnp.dot(
            chance.astype(BF16), incoming, preferred_element_type=F32
        )
        grad_keys[key_rows, :] += jnp.dot(grad_scores, queries, preferred_element_type=F32)
        grad_query[...] += jnp.dot(turned[tile], grad_scores, preferred_element_type=F32)
        return 0

    upper = (index * tile_q + tile_q - 1) // tile_k + 1
    lax.fori_loop(lows[index], upper, one, 0)
    out[query_rows, :width] = (
        fold_heads(grad_query[...], heads, tile_q) * HEAD_DIM**-0.5
    ).astype(BF16)

    @pl.when(index == pl.num_programs(0) - 1)
    def _():
        out[:, width : 2 * width] = grad_keys[...].astype(BF16)
        out[:, 2 * width :] = grad_values[...].astype(BF16)


def attend_back(pieces, place, lows, ends, bounds, logs, grad, attended, nctx, block_rows):
    total_rows, width = grad.shape
    heads = width // HEAD_DIM
    steps = total_rows // TILE_Q
    grid_spec = pltpu.PrefetchScalarGridSpec(
        num_scalar_prefetch=3,
        grid=(steps,),
        in_specs=[
            pl.BlockSpec((2, TILE_Q), lambda i, *_: (0, i)),
            pl.BlockSpec((heads, TILE_Q), lambda i, *_: (0, i)),
        ]
        + [whole(piece.shape) for piece in pieces]
        + [pl.BlockSpec((TILE_Q, width), lambda i, *_: (i, 0))] * 2,
        out_specs=whole((total_rows, 3 * width)),
        scratch_shapes=[
            pltpu.VMEM((total_rows, 3 * width), BF16),
            pltpu.VMEM((total_rows // TILE_K, width, TILE_K), BF16),
            pltpu.VMEM((total_rows, width), F32),
            pltpu.VMEM((total_rows, width), F32),
            pltpu.VMEM((width, heads * TILE_Q), F32),
        ],
    )
    return pl.pallas_call(
        functools.partial(attend_back_kernel, nctx, heads, len(pieces), block_rows),
        grid_spec=grid_spec,
        out_shape=jax.ShapeDtypeStruct((total_rows, 3 * width), BF16),
        compiler_params=params(),
        cost_estimate=pl.CostEstimate(
            flops=20 * total_rows * total_rows * width // 4,
            bytes_accessed=16 * total_rows * width,
            transcendentals=heads * total_rows * total_rows // 4,
        ),
        name="attend_back",
    )(place, lows, ends, bounds, logs, *pieces, grad, attended)


def mix_kernel(nctx, place, heads_in, mine, theirs, source, gain, bias, returned, mixed, low):
    half_depth = mine.shape[1]
    step = pl.program_id(0)
    left = jnp.concatenate([heads_in[c, 0] for c in range(nctx)], axis=1)
    returned[...] = left
    at_mine, at_theirs = halves(place, half_depth)

    @pl.when(step == 0)
    def _():
        mixed[...] = source[...].astype(F32)

    mixed[:, at_mine] += dot(left, mine[...])
    mixed[:, at_theirs] += dot(left, theirs[...])

    @pl.when(step == pl.num_programs(0) - 1)
    def _():
        values = mixed[...]
        values = values - jnp.mean(values, axis=1, keepdims=True)
        scaling = lax.rsqrt(jnp.mean(values * values, axis=1, keepdims=True) + EPSILON)
        low[...] = (values * scaling * gain[...] + bias[...]).astype(BF16)


def mix(heads_in, weights, full, gain, bias, place):
    nctx, tp, rows, piece = heads_in.shape
    depth = full.shape[1]
    head_width = nctx * piece
    by_rows = pl.BlockSpec((head_width, depth // 2), lambda k, s: (k, 0))
    grid_spec = pltpu.PrefetchScalarGridSpec(
        num_scalar_prefetch=1,
        grid=(tp,),
        in_specs=[
            pl.BlockSpec((nctx, 1, rows, piece), lambda k, s: (0, k, 0, 0)),
            by_rows,
            by_rows,
            pl.BlockSpec((rows, depth), lambda k, s: (s[0], 0)),
            whole((1, depth)),
            whole((1, depth)),
        ],
        out_specs=[
            pl.BlockSpec((rows, head_width), lambda k, s: (0, k)),
            whole((rows, depth)),
            whole((rows, depth)),
        ],
    )
    return pl.pallas_call(
        functools.partial(mix_kernel, nctx),
        grid_spec=grid_spec,
        out_shape=[
            jax.ShapeDtypeStruct((rows, tp * head_width), BF16),
            jax.ShapeDtypeStruct((rows, depth), F32),
            jax.ShapeDtypeStruct((rows, depth), BF16),
        ],
        compiler_params=params(),
        cost_estimate=pl.CostEstimate(
            flops=2 * rows * depth * tp * head_width,
            bytes_accessed=2 * depth * tp * head_width,
            transcendentals=0,
        ),
        name="mix",
    )(place, heads_in, *weights, full, gain, bias)


def feed_kernel(cuts, place, low, cot, *refs):
    sources = refs[:6]
    hidden, grad_gate, grad_up, partial = refs[6:10]
    held, sems = refs[10:16], refs[16]
    half_depth = low.shape[1] // 2
    at_mine, at_theirs = halves(place, half_depth)

    def copies(index):
        first, size = cuts[index]
        found = []
        for which in range(6):
            if which < 4:
                at = (slice(None), pl.ds(first, size))
            else:
                at = (pl.ds(first, size), slice(None))
            found.append(
                pltpu.make_async_copy(
                    sources[which].at[at], held[which].at[at], sems.at[index * 6 + which]
                )
            )
        return found

    for index in range(len(cuts)):
        for copy in copies(index):
            copy.start()
    gate_mine, gate_theirs, up_mine, up_theirs, down_mine, down_theirs = held
    for index, (first, size) in enumerate(cuts):
        for copy in copies(index):
            copy.wait()
        at = slice(first, first + size)
        gate = dot(low[:, at_mine], gate_mine[:, at]) + dot(low[:, at_theirs], gate_theirs[:, at])
        up = dot(low[:, at_mine], up_mine[:, at]) + dot(low[:, at_theirs], up_theirs[:, at])
        sigma = 1.0 / (1.0 + jnp.exp(-gate))
        active = gate * sigma
        hidden[:, at] = (active * up).astype(BF16)
        grad = dot_turned(cot[:, at_mine], down_mine[at, :]) + dot_turned(
            cot[:, at_theirs], down_theirs[at, :]
        )
        grad_gate[:, at] = (grad * up * sigma * (1.0 + gate * (1.0 - sigma))).astype(BF16)
        grad_up[:, at] = (grad * active).astype(BF16)
    partial[:, at_mine] = (
        dot_turned(grad_gate[...], gate_mine[...]) + dot_turned(grad_up[...], up_mine[...])
    ).astype(BF16)
    partial[:, at_theirs] = (
        dot_turned(grad_gate[...], gate_theirs[...]) + dot_turned(grad_up[...], up_theirs[...])
    ).astype(BF16)


def feed(low, cot, block, gates, ups, downs, place):
    rows, depth = low.shape
    hidden = gates[0].shape[1]
    cuts = []
    while sum(size for _, size in cuts) < hidden:
        first = sum(size for _, size in cuts)
        cuts.append((first, min(512, hidden - first)))
    grid_spec = pltpu.PrefetchScalarGridSpec(
        num_scalar_prefetch=1,
        grid=(1,),
        in_specs=[whole((rows, depth)), pl.BlockSpec((rows, depth), lambda i, s: (block, 0))]
        + anywhere(6),
        out_specs=[whole((rows, hidden))] * 3 + [whole((rows, depth))],
        scratch_shapes=[pltpu.VMEM(w.shape, BF16) for w in (*gates, *ups, *downs)]
        + [pltpu.SemaphoreType.DMA((6 * len(cuts),))],
    )
    return pl.pallas_call(
        functools.partial(feed_kernel, tuple(cuts)),
        grid_spec=grid_spec,
        out_shape=[jax.ShapeDtypeStruct((rows, hidden), BF16)] * 3
        + [jax.ShapeDtypeStruct((rows, depth), BF16)],
        compiler_params=params(),
        cost_estimate=pl.CostEstimate(
            flops=10 * rows * depth * hidden,
            bytes_accessed=6 * depth * hidden,
            transcendentals=rows * hidden,
        ),
        name="feed",
    )(place, low, cot, *gates, *ups, *downs)


def down_kernel(tp, spans, place, *refs):
    hiddens = refs[:tp]
    mixed, mine, theirs, out, spare = refs[tp:]
    half_depth = mine.shape[1]
    at_mine, at_theirs = halves(place, half_depth)
    for step in range(tp):

        @pl.when(pl.program_id(0) == step)
        def _():
            spare[:, at_mine] = dot(hiddens[step][...], mine[...])
            spare[:, at_theirs] = dot(hiddens[step][...], theirs[...])
            if step == 0:
                spare[...] += mixed[...]

    for block in range(tp):
        for first, size, base, stride in spans:
            column = base + block * stride
            out[block, :, first : first + size] = spare[:, column : column + size].astype(BF16)


def down(hiddens, mixed, weights, place, spans, *needed):
    tp = len(hiddens)
    rows, hidden = hiddens[0].shape
    depth = mixed.shape[1]
    width = depth // tp
    count = len(needed)
    grid_spec = pltpu.PrefetchScalarGridSpec(
        num_scalar_prefetch=1,
        grid=(tp,),
        in_specs=[whole((rows, hidden))] * tp
        + [whole((rows, depth))]
        + [whole((hidden, depth // 2))] * 2
        + anywhere(count),
        out_specs=pl.BlockSpec((tp, rows, width), lambda k, s: (0, lax.rem(s[0] - k + tp, tp), 0)),
        scratch_shapes=[pltpu.VMEM((rows, depth), F32)],
    )

    def kernel(place, *refs):
        down_kernel(tp, spans, place, *refs[: tp + 3], *refs[tp + 3 + count :])

    return pl.pallas_call(
        kernel,
        grid_spec=grid_spec,
        out_shape=jax.ShapeDtypeStruct((tp, tp * rows, width), BF16),
        compiler_params=params(),
        cost_estimate=pl.CostEstimate(
            flops=2 * tp * rows * depth * hidden,
            bytes_accessed=2 * depth * hidden,
            transcendentals=0,
        ),
        name="down",
    )(place, *hiddens, mixed, *weights, *needed)


def turn_kernel(nctx, count, place, arrived, own, mixed, cot, gain, mine, theirs, *refs):
    out, grad_mixed, grad_low, gain_grad, shift_grad = refs[count:]
    half_depth = mine.shape[1]
    piece = out.shape[3]
    at_mine, at_theirs = halves(place, half_depth)

    @pl.when(pl.program_id(0) == 0)
    def _():
        incoming = arrived[...].astype(F32) + own[...].astype(F32)
        values = mixed[...]
        values = values - jnp.mean(values, axis=1, keepdims=True)
        scaling = lax.rsqrt(jnp.mean(values * values, axis=1, keepdims=True) + EPSILON)
        normed = values * scaling
        shift_grad[...] = jnp.sum(incoming, axis=0, keepdims=True)
        gain_grad[...] = jnp.sum(incoming * normed, axis=0, keepdims=True)
        scaled = incoming * gain[...]
        total = cot[...].astype(F32) + scaling * (
            scaled
            - jnp.mean(scaled, axis=1, keepdims=True)
            - normed * jnp.mean(scaled * normed, axis=1, keepdims=True)
        )
        grad_mixed[...] = total
        grad_low[...] = total.astype(BF16)

    product = dot_turned(grad_low[:, at_mine], mine[...]) + dot_turned(
        grad_low[:, at_theirs], theirs[...]
    )
    for c in range(nctx):
        out[c, 0] = product[:, c * piece : (c + 1) * piece].astype(BF16)


def turn(arrived, own, mixed, cot, gain, weights, place, nctx, tp, *needed):
    rows, depth = mixed.shape
    head_width = weights[0].shape[0] // tp
    piece = head_width // nctx
    by_rows = pl.BlockSpec((head_width, depth // 2), lambda k, s: (k, 0))
    grid_spec = pltpu.PrefetchScalarGridSpec(
        num_scalar_prefetch=1,
        grid=(tp,),
        in_specs=[whole((rows, depth))] * 4
        + [whole((1, depth)), by_rows, by_rows]
        + anywhere(len(needed)),
        out_specs=[
            pl.BlockSpec((nctx, 1, rows, piece), lambda k, s: (0, k, 0, 0)),
            whole((rows, depth)),
            whole((rows, depth)),
            whole((1, depth)),
            whole((1, depth)),
        ],
    )
    return pl.pallas_call(
        functools.partial(turn_kernel, nctx, len(needed)),
        grid_spec=grid_spec,
        out_shape=[
            jax.ShapeDtypeStruct((nctx, tp, rows, piece), BF16),
            jax.ShapeDtypeStruct((rows, depth), F32),
            jax.ShapeDtypeStruct((rows, depth), BF16),
            jax.ShapeDtypeStruct((1, depth), F32),
            jax.ShapeDtypeStruct((1, depth), F32),
        ],
        compiler_params=params(),
        cost_estimate=pl.CostEstimate(
            flops=2 * rows * depth * tp * head_width,
            bytes_accessed=2 * depth * tp * head_width,
            transcendentals=0,
        ),
        name="turn",
    )(place, arrived, own, mixed, cot, gain, *weights, *needed)


def finish_kernel(nctx, chunk, spans, place, *refs):
    pieces = refs[:nctx]
    (cosine, sine_up, sine_down, full, extra, gain, mine, theirs) = refs[nctx : nctx + 8]
    out, low, bias_grad, gain_grad, shift_grad, spare = refs[nctx + 8 :]
    rows, wide = pieces[0].shape
    piece = wide // 3
    tp, width = out.shape[0], out.shape[2]
    depth = tp * width
    strip = spare.shape[0]
    extra_rows = extra.shape[0]

    @pl.when(pl.program_id(0) == 0)
    def _():
        bias_grad[...] = jnp.zeros_like(bias_grad)
        gain_grad[...] = jnp.zeros_like(gain_grad)
        shift_grad[...] = jnp.zeros_like(shift_grad)

    for step in range(nctx):
        source = jnp.bitwise_xor(place[1], step)
        for part in range(3):
            values = pieces[step][:, part * piece : (part + 1) * piece].astype(F32)
            if part < 2:
                values = (
                    values * cosine[...]
                    - pltpu.roll(values, piece - ROT // 2, 1) * sine_up[...]
                    - pltpu.roll(values, ROT // 2, 1) * sine_down[...]
                )
            columns = pl.ds(pl.multiple_of(source * wide + part * piece, piece), piece)
            bias_grad[:, columns] += jnp.sum(values, axis=0, keepdims=True)
            low[:, columns] = values.astype(BF16)

    at_mine, at_theirs = halves(place, depth // 2)
    spare[:, at_mine] = dot_turned(low[...], mine[...])
    spare[:, at_theirs] = dot_turned(low[...], theirs[...])
    incoming = spare[...]
    source = full[...].astype(F32)
    centre = jnp.mean(source, axis=1, keepdims=True)
    source = source - centre
    scaling = lax.rsqrt(jnp.mean(source * source, axis=1, keepdims=True) + EPSILON)
    normed = source * scaling
    shift_grad[...] += jnp.sum(incoming, axis=0, keepdims=True)
    gain_grad[...] += jnp.sum(incoming * normed, axis=0, keepdims=True)
    scaled = incoming * gain[...]
    spare[...] = scaling * (
        scaled
        - jnp.mean(scaled, axis=1, keepdims=True)
        - normed * jnp.mean(scaled * normed, axis=1, keepdims=True)
    )
    first = chunk * pl.num_programs(0) * strip + pl.program_id(0) * strip
    wanted = place[0] * extra_rows

    if strip <= extra_rows:

        @pl.when((first >= wanted) & (first < wanted + extra_rows))
        def _():
            spare[...] += extra[pl.ds(pl.multiple_of(first - wanted, strip), strip), :]

    else:

        @pl.when((wanted >= first) & (wanted < first + strip))
        def _():
            spare[pl.ds(pl.multiple_of(wanted - first, extra_rows), extra_rows), :] += extra[...]

    for block in range(tp):
        for first_column, size, base, stride in spans:
            column = base + block * stride
            out[block, :, first_column : first_column + size] = spare[
                :, column : column + size
            ].astype(BF16)


def finish(pieces, place, tables, full, extra, gain, weights, chunk, tp, spans):
    rows, wide = pieces[0].shape
    depth = full.shape[1]
    total = weights[0].shape[1]
    strip = 256
    steps = rows // strip
    width = depth // tp
    nctx = len(pieces)
    by_rows = lambda columns: pl.BlockSpec((strip, columns), lambda i, s: (i, 0))
    grid_spec = pltpu.PrefetchScalarGridSpec(
        num_scalar_prefetch=1,
        grid=(steps,),
        in_specs=[by_rows(wide)] * nctx
        + [by_rows(2 * HEAD_DIM)] * 3
        + [
            pl.BlockSpec((strip, depth), lambda i, s: (i + chunk * steps, 0)),
            whole(extra.shape),
            whole((1, depth)),
        ]
        + [whole(weight.shape) for weight in weights],
        out_specs=[
            pl.BlockSpec((tp, strip, width), lambda i, s: (0, i, 0)),
            by_rows(total),
            whole((1, total)),
            whole((1, depth)),
            whole((1, depth)),
        ],
        scratch_shapes=[pltpu.VMEM((strip, depth), F32)],
    )
    return pl.pallas_call(
        functools.partial(finish_kernel, nctx, chunk, spans),
        grid_spec=grid_spec,
        out_shape=[
            jax.ShapeDtypeStruct((tp, rows, width), BF16),
            jax.ShapeDtypeStruct((rows, total), BF16),
            jax.ShapeDtypeStruct((1, total), F32),
            jax.ShapeDtypeStruct((1, depth), F32),
            jax.ShapeDtypeStruct((1, depth), F32),
        ],
        compiler_params=params(),
        cost_estimate=pl.CostEstimate(
            flops=2 * rows * depth * total, bytes_accessed=2 * depth * total, transcendentals=0
        ),
        name="finish",
    )(place, *pieces, *tables, full, extra, gain, *weights)


def join_kernel(tp, spans, place, *refs):
    blocks, out = refs[:tp], refs[tp]
    for step in range(tp):
        owner = lax.rem(place[0] - step + tp, tp)
        for first, size, base, stride in spans:
            columns = pl.ds(pl.multiple_of(base + owner * stride, size), size)
            out[:, columns] = blocks[step][:, first : first + size]


def join(blocks, place, spans):
    tp = len(blocks)
    rows, width = blocks[0].shape
    strip = rows // tp
    grid_spec = pltpu.PrefetchScalarGridSpec(
        num_scalar_prefetch=1,
        grid=(tp,),
        in_specs=[pl.BlockSpec((strip, width), lambda i, s: (lax.rem(s[0] - i + tp, tp), 0))] * tp,
        out_specs=pl.BlockSpec((strip, tp * width), lambda i, s: (i, 0)),
    )
    return pl.pallas_call(
        functools.partial(join_kernel, tp, spans),
        grid_spec=grid_spec,
        out_shape=jax.ShapeDtypeStruct((rows, tp * width), BF16),
        compiler_params=params(),
        cost_estimate=pl.CostEstimate(
            flops=0, bytes_accessed=4 * rows * tp * width, transcendentals=0
        ),
        name="join",
    )(place, *blocks)


def contract_rows(left, right):
    return lax.dot_general(left, right, (((0,), (0,)), ((), ())), preferred_element_type=F32)


def pick(stack, index):
    return lax.dynamic_index_in_dim(stack, index, 0, keepdims=False)


def shards(
    nfsdp,
    nctx,
    tp,
    inputs,
    cotangent,
    first_gain,
    first_bias,
    qkv_weight,
    qkv_bias,
    out_weight,
    second_gain,
    second_bias,
    gate_weight,
    up_weight,
    down_weight,
    lengths,
    fill_counts,
):
    data = ("fsdp", "ctx")
    ndata = nfsdp * nctx
    block_rows, width = inputs.shape
    depth = tp * width
    half_depth = depth // 2
    unit = depth // ndata
    tensor_index = lax.axis_index("tp").astype(jnp.int32)
    context_index = lax.axis_index("ctx").astype(jnp.int32)
    fsdp_index = lax.axis_index("fsdp").astype(jnp.int32)
    part_rows = block_rows // tp
    chunk_rows = block_rows // CHUNKS
    head_width = qkv_weight.shape[2]
    piece = head_width // nctx
    wide = 3 * piece

    paired = nctx % 2 == 0 and unit % 128 == 0 and (width // unit) % 2 == 0
    if paired:
        half_index = context_index % 2
        groups = [list(range(0, ndata, 2)), list(range(1, ndata, 2))]
        per = width // unit
        spans = tuple(
            (u * unit, unit, (u % 2) * half_depth + (u // 2) * unit, (per // 2) * unit)
            for u in range(per)
        )
    else:
        half_index = fsdp_index // (nfsdp // 2)
        groups = [list(range(ndata // 2)), list(range(ndata // 2, ndata))]
        spans = ((0, width, 0, width),)
    place = jnp.stack([tensor_index, context_index, half_index])

    def mate(value):
        if paired:
            return lax.ppermute(value, "ctx", [(i, i ^ 1) for i in range(nctx)])
        return lax.ppermute(value, "fsdp", [(i, i ^ (nfsdp // 2)) for i in range(nfsdp)])

    def to_halves(vector):
        if not paired:
            return vector
        return jnp.swapaxes(vector.reshape(-1, ndata // 2, 2, unit), 1, 2).reshape(vector.shape)

    def from_halves(vector):
        if not paired:
            return vector
        return jnp.swapaxes(vector.reshape(-1, 2, ndata // 2, unit), 1, 2).reshape(vector.shape)

    def shift(value, step):
        return lax.ppermute(value, "tp", [(i, (i + step) % tp) for i in range(tp)])

    def swap(value, step):
        return lax.ppermute(value, "ctx", [(i, i ^ step) for i in range(nctx)])

    def gather(value, axis):
        mine = lax.all_gather(value, data, axis=axis, tiled=True, axis_index_groups=groups)
        return (mine, mate(mine))

    def scatter(make, axis):
        arrived = mate(make(1 - half_index).astype(BF16))
        total = (make(half_index) + arrived.astype(F32)).astype(BF16)
        return lax.psum_scatter(
            total, data, scatter_dimension=axis, tiled=True, axis_index_groups=groups
        )

    def half_of(value, index):
        return lax.dynamic_slice_in_dim(value, index * half_depth, half_depth, 1)

    owners = [(tensor_index - step + tp) % tp for step in range(tp)]

    own_qkv = (
        qkv_weight.reshape(-1, 3, nctx, piece).transpose(0, 2, 1, 3).reshape(-1, 3 * head_width)
    )
    qkv_halves = gather(own_qkv, 0)
    stack = jnp.zeros((tp,) + out_weight.shape, BF16)
    stack = lax.dynamic_update_index_in_dim(stack, out_weight, tensor_index, 0)
    for step in range(1, tp):
        stack = lax.dynamic_update_index_in_dim(stack, shift(out_weight, step), owners[step], 0)
    out_halves = gather(stack.reshape(depth, -1), 1)
    gate_halves = gather(gate_weight, 0)
    up_halves = gather(up_weight, 0)
    down_halves = gather(down_weight, 1)

    validity, position, first_key, last_key = layout(lengths[0], fill_counts[0], block_rows)
    own_position = lax.dynamic_slice_in_dim(position, context_index * block_rows, block_rows, 0)
    tables = rotary_tables(own_position)
    bounds = jnp.stack([first_key, last_key])
    tile_first = first_key[::TILE_Q]
    tile_count = tile_first.shape[0]
    lows = jnp.where(validity[::TILE_Q], tile_first // TILE_K, tile_count * TILE_Q).astype(jnp.int32)
    key_block = jnp.arange(0, nctx * block_rows, TILE_K, dtype=jnp.int32) // block_rows
    ends = (
        key_block * block_rows
        + jnp.sum(
            jnp.where(
                key_block[:, None] == jnp.arange(nctx, dtype=jnp.int32)[None, :],
                fill_counts[0][None, :],
                0,
            ),
            axis=1,
        )
    ).astype(jnp.int32)

    flat_bias = qkv_bias.reshape(3, nctx, piece).transpose(1, 0, 2).reshape(1, -1)
    gain_one, bias_one = to_halves(first_gain[None]), to_halves(first_bias[None])
    gain_two, bias_two = to_halves(second_gain[None]), to_halves(second_bias[None])

    rings = [[inputs[c * chunk_rows : (c + 1) * chunk_rows]] for c in range(CHUNKS)]
    for chunk in range(CHUNKS):
        for _ in range(tp - 1):
            rings[chunk].append(shift(rings[chunk][-1], 1))
    lows_one, fulls, pieces, chunk_tables = [], [], [], []
    for chunk in range(CHUNKS):
        at = slice(chunk * chunk_rows, (chunk + 1) * chunk_rows)
        chunk_tables.append([table[at] for table in tables])
        low, full, outgoing = project(
            rings[chunk],
            place,
            gain_one,
            bias_one,
            qkv_halves,
            flat_bias,
            chunk_tables[chunk],
            nctx,
            spans,
        )
        lows_one.append(low)
        fulls.append(full)
        pieces.append(pick(outgoing, context_index))
        for step in range(1, nctx):
            pieces.append(swap(pick(outgoing, context_index ^ step), step))
    full = jnp.concatenate(fulls, axis=0)

    cot_own = tie(cotangent, rings[-1][-1])
    cot = join([cot_own] + [shift(cot_own, step) for step in range(1, tp)], place, spans)

    attended, logs = attend(pieces, place[1:2], lows, ends, bounds, nctx, block_rows)
    arrived = lax.all_to_all(
        attended.reshape(nctx * tp, part_rows, piece),
        ("ctx", "tp"),
        split_axis=0,
        concat_axis=0,
        tiled=True,
    )
    returned, mixed, second_low = mix(
        arrived.reshape(nctx, tp, part_rows, piece), out_halves, full, gain_two, bias_two, place
    )

    seconds, hiddens, gates, ups, partials = [second_low], [], [], [], []
    for _ in range(tp - 1):
        seconds.append(shift(seconds[-1], 1))
    for step in range(tp):
        hidden, gate, up, partial = feed(
            seconds[step], cot, step, gate_halves, up_halves, down_halves, place
        )
        hiddens.append(hidden)
        gates.append(gate)
        ups.append(up)
        partials.append(partial)

    all_second = jnp.concatenate(seconds, axis=0)
    all_hidden = jnp.concatenate(hiddens, axis=0)
    all_gate = jnp.concatenate(gates, axis=0)
    all_up = jnp.concatenate(ups, axis=0)

    travelling = partials[1 % tp]
    for step in range(2, tp):
        travelling = add(shift(travelling, 1), partials[step])
    feedforward = down(hiddens, mixed, down_halves, place, spans)
    total_gate = scatter(lambda half: contract_rows(half_of(all_second, half), all_gate), 0)
    total_up = scatter(lambda half: contract_rows(half_of(all_second, half), all_up), 0)
    total_down = scatter(lambda half: contract_rows(all_hidden, half_of(cot, half)), 1)

    grad_heads, grad_mixed, mixed_low, gain_grad_two, shift_grad_two = turn(
        shift(travelling, 1),
        partials[0],
        mixed,
        cot,
        gain_two,
        out_halves,
        place,
        nctx,
        tp,
        feedforward,
    )
    grad_heads = lax.all_to_all(
        grad_heads.reshape(nctx * tp, part_rows, piece),
        ("ctx", "tp"),
        split_axis=0,
        concat_axis=0,
        tiled=True,
    ).reshape(nctx * block_rows, piece)

    feedforward = tie(feedforward, grad_heads)
    layer_out = pick(feedforward, tensor_index).astype(F32)
    for step in range(1, tp):
        layer_out = layer_out + shift(
            pick(feedforward, (tensor_index + step) % tp), step
        ).astype(F32)
    layer_out = layer_out.astype(BF16)

    total_out = scatter(lambda half: contract_rows(returned, half_of(mixed_low, half)), 1)
    out_blocks = total_out.reshape(tp, head_width, -1)
    total_out = pick(out_blocks, tensor_index).astype(F32)
    for step in range(1, tp):
        total_out = total_out + shift(
            pick(out_blocks, (tensor_index + step) % tp), step
        ).astype(F32)

    grad_grouped = attend_back(
        pieces, place[1:2], lows, ends, bounds, logs, grad_heads, attended, nctx, block_rows
    )
    grad_grouped = grad_grouped.reshape(nctx, CHUNKS, chunk_rows, wide)
    grad_lows, bias_grads, gain_grads, shift_grads, grad_rows = [], [], [], [], []
    for chunk in range(CHUNKS):
        outgoing = grad_grouped[:, chunk]
        arrived = [pick(outgoing, context_index)]
        for step in range(1, nctx):
            arrived.append(swap(pick(outgoing, context_index ^ step), step))
        partial, low, bias_grad, gain_grad, shift_grad = finish(
            arrived,
            place,
            chunk_tables[chunk],
            full,
            grad_mixed,
            gain_one,
            qkv_halves,
            chunk,
            tp,
            spans,
        )
        grad_lows.append(low)
        bias_grads.append(bias_grad)
        gain_grads.append(gain_grad)
        shift_grads.append(shift_grad)
        travelling = pick(partial, owners[1 % tp])
        for step in range(1, tp):
            travelling = add(shift(travelling, 1), pick(partial, owners[(step + 1) % tp]))
        grad_rows.append(travelling)
    grad_inputs = jnp.concatenate(grad_rows, axis=0)

    all_low, all_grad = jnp.concatenate(lows_one, axis=0), jnp.concatenate(grad_lows, axis=0)
    total_qkv = scatter(lambda half: contract_rows(half_of(all_low, half), all_grad), 0)
    total_qkv = (
        total_qkv.astype(F32)
        .reshape(-1, nctx, 3, piece)
        .transpose(0, 2, 1, 3)
        .reshape(-1, 3, head_width)
    )

    small = jnp.concatenate(
        [sum(bias_grads), sum(gain_grads), sum(shift_grads), gain_grad_two, shift_grad_two], axis=1
    )
    for axis, size in (("ctx", nctx), ("fsdp", nfsdp), ("tp", tp)):
        if axis == "tp":
            bias_total, small = small[:, : 3 * head_width], small[:, 3 * head_width :]
        step = 1
        while step < size:
            small = small + lax.ppermute(small, axis, [(i, i ^ step) for i in range(size)])
            step *= 2
    bias_total = bias_total.reshape(nctx, 3, piece).transpose(1, 0, 2).reshape(3, head_width)
    small = from_halves(small.reshape(4, depth))
    return (
        layer_out,
        grad_inputs,
        small[0],
        small[1],
        total_qkv,
        bias_total,
        total_out,
        small[2],
        small[3],
        total_gate.astype(F32),
        total_up.astype(F32),
        total_down.astype(F32),
    )


def solution(mesh):
    data = ("fsdp", "ctx")
    by_rows = P(data, "tp")
    by_columns = P("tp", data)
    qkv = P(data, None, "tp")
    return jax.shard_map(
        functools.partial(shards, mesh.shape["fsdp"], mesh.shape["ctx"], mesh.shape["tp"]),
        mesh=mesh,
        in_specs=(
            by_rows,
            by_rows,
            P(),
            P(),
            qkv,
            P(None, "tp"),
            by_columns,
            P(),
            P(),
            by_rows,
            by_rows,
            by_columns,
            P("fsdp", None),
            P("fsdp", None),
        ),
        out_specs=(
            by_rows,
            by_rows,
            P(),
            P(),
            qkv,
            P(None, "tp"),
            by_columns,
            P(),
            P(),
            by_rows,
            by_rows,
            by_columns,
        ),
        check_vma=False,
    )
```

```python
import functools

import jax
import jax.numpy as jnp
from jax import lax
from jax.experimental import pallas as pl
from jax.experimental.pallas import tpu as pltpu
from jax.sharding import PartitionSpec as P

HEAD_DIM = 64
ROT = 16
EPSILON = 1e-05
NEGATIVE = -1e30
FLOOR = -1e20
VMEM_LIMIT = 56 * 1024 * 1024
TILE_Q = 512
TILE_K = 512
CHUNKS = 2
STRIP = 16
NOTHING = pl.CostEstimate(flops=0, bytes_accessed=0, transcendentals=0)

F32 = jnp.float32
BF16 = jnp.bfloat16


def layout(lengths, fill_counts, block_rows):
    blocks_count = fill_counts.shape[0]
    seq_count = lengths.shape[0]
    slot_index = jnp.arange(blocks_count * block_rows, dtype=jnp.int32)
    block_of = slot_index // block_rows
    within = slot_index - block_of * block_rows
    chooser = block_of[:, None] == jnp.arange(blocks_count, dtype=jnp.int32)[None, :]
    fill_here = jnp.sum(jnp.where(chooser, fill_counts[None, :], 0), axis=1)
    before = jnp.cumsum(fill_counts) - fill_counts
    before_here = jnp.sum(jnp.where(chooser, before[None, :], 0), axis=1)
    validity = within < fill_here
    used_index = before_here + within
    seq_ends = jnp.cumsum(lengths)
    sequence = jnp.sum((used_index[:, None] >= seq_ends[None, :]).astype(jnp.int32), axis=1)
    seq_starts = seq_ends - lengths
    picker = sequence[:, None] == jnp.arange(seq_count, dtype=jnp.int32)[None, :]
    start_here = jnp.sum(jnp.where(picker, seq_starts[None, :], 0), axis=1)
    after = before + fill_counts
    start_block = jnp.sum((seq_starts[:, None] >= after[None, :]).astype(jnp.int32), axis=1)
    start_block = jnp.minimum(start_block, blocks_count - 1)
    block_pick = start_block[:, None] == jnp.arange(blocks_count, dtype=jnp.int32)[None, :]
    start_before = jnp.sum(jnp.where(block_pick, before[None, :], 0), axis=1)
    start_slot = start_block * block_rows + seq_starts - start_before
    slot_here = jnp.sum(jnp.where(picker, start_slot[None, :], 0), axis=1)
    first_key = jnp.where(validity, slot_here, 0).astype(jnp.int32)
    last_key = jnp.where(validity, slot_index, -1).astype(jnp.int32)
    return (validity, used_index - start_here, first_key, last_key)


def rotary_tables(position):
    half = ROT // 2
    lane = jnp.arange(2 * HEAD_DIM, dtype=jnp.int32) % HEAD_DIM
    frequency = 10000.0 ** (-(2.0 * (lane % half).astype(F32)) / ROT)
    angles = position.astype(F32)[:, None] * frequency[None, :]
    cosine, sine = jnp.cos(angles), jnp.sin(angles)
    lane = lane[None, :]
    return (
        jnp.where(lane < ROT, cosine, 1.0),
        jnp.where(lane < half, -sine, 0.0),
        jnp.where((lane >= half) & (lane < ROT), sine, 0.0),
    )


def params(**extra):
    return pltpu.CompilerParams(vmem_limit_bytes=VMEM_LIMIT, **extra)


def whole(shape):
    return pl.BlockSpec(shape, lambda *_: (0,) * len(shape))


def anywhere(count):
    return [pl.BlockSpec(memory_space=pl.ANY)] * count


def natural(place, which, block, size):
    if size is None:
        return slice(None)
    f, c = place[2], place[1]
    c_high = lax.shift_right_logical(c, 1)
    high = jnp.bitwise_xor(f, block // 2) * 2 + jnp.bitwise_xor(c_high, block % 2)
    low = jnp.bitwise_xor(jnp.bitwise_and(c, 1), which)
    return pl.ds(pl.multiple_of((high * 2 + low) * size, size), size)


def every(place, weights, depth):
    size = None if len(weights) == 1 else depth // (len(weights) * weights[0].shape[0])
    return [
        (weight, block, natural(place, which, block, size))
        for which, weight in enumerate(weights)
        for block in range(weight.shape[0])
    ]


def strips(rows, body):
    def one(index, carry):
        body(pl.ds(pl.multiple_of(index * STRIP, STRIP), STRIP))
        return carry

    lax.fori_loop(0, rows // STRIP, one, 0)


def fold_rows(values):
    return sum(values[first : first + 8] for first in range(0, values.shape[0], 8))


def dot(left, right):
    return jnp.dot(left, right, preferred_element_type=F32)


def dot_turned(left, right):
    return lax.dot_general(left, right, (((1,), (1,)), ((), ())), preferred_element_type=F32)


def tie(value, *needed):
    def kernel(*refs):
        del refs

    return pl.pallas_call(
        kernel,
        in_specs=anywhere(1 + len(needed)),
        out_specs=pl.BlockSpec(memory_space=pl.ANY),
        out_shape=jax.ShapeDtypeStruct(value.shape, value.dtype),
        input_output_aliases={0: 0},
        name="tie",
    )(value, *needed)


def add_kernel(left, right, *refs):
    refs[-1][...] = (left[...].astype(F32) + right[...].astype(F32)).astype(BF16)


def add(left, right, *needed):
    rows, columns = left.shape
    strip = min(rows, 128)
    block = pl.BlockSpec((strip, columns), lambda i: (i, 0))
    return pl.pallas_call(
        add_kernel,
        grid=(rows // strip,),
        in_specs=[block, block] + anywhere(len(needed)),
        out_specs=block,
        out_shape=jax.ShapeDtypeStruct(left.shape, BF16),
        compiler_params=params(),
        cost_estimate=NOTHING,
        name="ring_add",
    )(left, right, *needed)


def project_kernel(tp, per, nweights, place, *refs):
    blocks = refs[:tp]
    gain, bias = refs[tp : tp + 2]
    weights = refs[tp + 2 : tp + 2 + nweights]
    weight_bias, cosine, sine_up, sine_down, low, full, out, moved = refs[tp + 2 + nweights :]
    rows, width = blocks[0].shape
    depth = tp * width
    piece = out.shape[2] // 3

    @pl.when(pl.program_id(0) == 0)
    def _():
        def one(at):
            parts = [block[at, :].astype(F32) for block in blocks]
            centre = sum(jnp.sum(part, axis=1, keepdims=True) for part in parts) / depth
            parts = [part - centre for part in parts]
            spread = sum(jnp.sum(part * part, axis=1, keepdims=True) for part in parts) / depth
            scaling = lax.rsqrt(spread + EPSILON)
            for step in range(tp):
                owner = lax.rem(place[0] - step + tp, tp)
                columns = pl.ds(pl.multiple_of(owner * width, width), width)
                low[at, columns] = (
                    parts[step] * scaling * gain[:, columns] + bias[:, columns]
                ).astype(BF16)
                full[at, columns] = blocks[step][at, :]

        strips(rows, one)
        first = 0
        for weight, block, columns in every(place, weights, depth):
            size = weight.shape[1]
            moved[:, first : first + size] = low[:, columns]
            first += size

    product = weight_bias[...]
    first = 0
    for weight in weights:
        size = weight.shape[0] * weight.shape[1]
        product = product + dot(
            moved[:, first : first + size], weight[...].reshape(size, weight.shape[2])
        )
        first += size
    for group in range(per):
        for part in range(3):
            first = (group * 3 + part) * piece
            values = product[:, first : first + piece]
            if part < 2:
                values = (
                    values * cosine[...]
                    + pltpu.roll(values, piece - ROT // 2, 1) * sine_up[...]
                    + pltpu.roll(values, ROT // 2, 1) * sine_down[...]
                )
            out[group, :, part * piece : (part + 1) * piece] = values.astype(BF16)


def project(blocks, place, gain, bias, weights, weight_bias, tables, nctx):
    tp = len(blocks)
    rows, width = blocks[0].shape
    depth = tp * width
    total = weights[0].shape[2]
    wide = total // nctx
    per = 2 if nctx % 2 == 0 else 1
    grid_spec = pltpu.PrefetchScalarGridSpec(
        num_scalar_prefetch=1,
        grid=(nctx // per,),
        in_specs=[whole((rows, width))] * tp
        + [whole((1, depth))] * 2
        + [pl.BlockSpec((*w.shape[:2], per * wide), lambda i, s: (0, 0, i)) for w in weights]
        + [pl.BlockSpec((1, per * wide), lambda i, s: (0, i))]
        + [whole((rows, 2 * HEAD_DIM))] * 3,
        out_specs=[
            whole((rows, depth)),
            whole((rows, depth)),
            pl.BlockSpec((per, rows, wide), lambda i, s: (i, 0, 0)),
        ],
        scratch_shapes=[pltpu.VMEM((rows, depth), BF16)],
    )
    return pl.pallas_call(
        functools.partial(project_kernel, tp, per, len(weights)),
        grid_spec=grid_spec,
        out_shape=[
            jax.ShapeDtypeStruct((rows, depth), BF16),
            jax.ShapeDtypeStruct((rows, depth), BF16),
            jax.ShapeDtypeStruct((nctx, rows, wide), BF16),
        ],
        compiler_params=params(),
        cost_estimate=NOTHING,
        name="project",
    )(place, *blocks, gain, bias, *weights, weight_bias, *tables)


def stack_heads(tile, heads):
    lane = lax.broadcasted_iota(jnp.int32, tile.shape, 1) // HEAD_DIM
    return jnp.concatenate(
        [jnp.where(lane == head, tile, jnp.zeros_like(tile)) for head in range(heads)], axis=0
    )


def fold_heads(stacked, heads, columns):
    row = lax.broadcasted_iota(jnp.int32, (stacked.shape[0], columns), 0) // HEAD_DIM
    folded = jnp.zeros((stacked.shape[0], columns), F32)
    for head in range(heads):
        folded = folded + jnp.where(row == head, stacked[:, head * columns : (head + 1) * columns], 0.0)
    return jnp.transpose(folded)


def load_pieces(place, pieces, nctx, held, block_rows):
    chunk_rows = pieces[0].shape[0]
    chunks = len(pieces) // nctx
    for chunk in range(chunks):
        for step in range(nctx):
            source = jnp.bitwise_xor(place, step)
            first = source * block_rows + chunk * chunk_rows
            held[pl.ds(pl.multiple_of(first, chunk_rows), chunk_rows), :] = pieces[
                chunk * nctx + step
            ][...]


def attend_kernel(nctx, heads, count, block_rows, place, lows, ends, bounds, *refs):
    pieces = refs[:count]
    out, logs, held, turned, total, high, sums = refs[count:]
    tile_q, tile_k = out.shape[0], turned.shape[2]
    width = heads * HEAD_DIM
    index = pl.program_id(0)

    @pl.when(index == 0)
    def _():
        load_pieces(place[0], pieces, nctx, held, block_rows)
        for tile in range(turned.shape[0]):
            turned[tile] = jnp.transpose(held[tile * tile_k : (tile + 1) * tile_k, 2 * width :])

    query_rows = pl.ds(pl.multiple_of(index * tile_q, tile_q), tile_q)
    queries = stack_heads(held[query_rows, :width] * jnp.asarray(HEAD_DIM**-0.5, BF16), heads)
    first_key = jnp.concatenate([bounds[0:1, :]] * heads, axis=1)
    last_key = jnp.concatenate([bounds[1:2, :]] * heads, axis=1)
    total[...] = jnp.zeros_like(total)
    high[...] = jnp.full_like(high, FLOOR)
    sums[...] = jnp.zeros_like(sums)

    def one(tile, _):
        start = tile * tile_k
        keys = held[pl.ds(pl.multiple_of(start, tile_k), tile_k), width : 2 * width]
        scores = lax.dot_general(
            keys, queries, (((1,), (1,)), ((), ())), preferred_element_type=F32
        )
        row = lax.broadcasted_iota(jnp.int32, scores.shape, 0)
        last = jnp.minimum(last_key, ends[tile] - 1) - start
        allowed = (row <= last) & (row >= first_key - start)
        scores = jnp.where(allowed, scores, NEGATIVE)
        highest = jnp.maximum(high[...], jnp.max(scores, axis=0, keepdims=True))
        raised = jnp.exp(scores - highest)
        shrink = jnp.exp(high[...] - highest)
        sums[...] = sums[...] * shrink + jnp.sum(raised, axis=0, keepdims=True)
        total[...] = total[...] * shrink + jnp.dot(
            turned[tile], raised.astype(BF16), preferred_element_type=F32
        )
        high[...] = highest
        return 0

    upper = (index * tile_q + tile_q - 1) // tile_k + 1
    lax.fori_loop(lows[index], upper, one, 0)
    found = sums[...] > 0.0
    safe = jnp.where(found, sums[...], 1.0)
    out[...] = fold_heads(
        total[...] * jnp.where(found, 1.0 / safe, 0.0), heads, tile_q
    ).astype(BF16)
    log_total = jnp.where(found, high[...] + jnp.log(safe), 0.0)
    for head in range(heads):
        logs[head : head + 1, :] = log_total[:, head * tile_q : (head + 1) * tile_q]


def attend(pieces, place, lows, ends, bounds, nctx, block_rows):
    total_rows = nctx * block_rows
    width = pieces[0].shape[1] // 3
    heads = width // HEAD_DIM
    steps = total_rows // TILE_Q
    grid_spec = pltpu.PrefetchScalarGridSpec(
        num_scalar_prefetch=3,
        grid=(steps,),
        in_specs=[pl.BlockSpec((2, TILE_Q), lambda i, *_: (0, i))]
        + [whole(piece.shape) for piece in pieces],
        out_specs=[
            pl.BlockSpec((TILE_Q, width), lambda i, *_: (i, 0)),
            pl.BlockSpec((heads, TILE_Q), lambda i, *_: (0, i)),
        ],
        scratch_shapes=[
            pltpu.VMEM((total_rows, 3 * width), BF16),
            pltpu.VMEM((total_rows // TILE_K, width, TILE_K), BF16),
            pltpu.VMEM((width, heads * TILE_Q), F32),
            pltpu.VMEM((1, heads * TILE_Q), F32),
            pltpu.VMEM((1, heads * TILE_Q), F32),
        ],
    )
    return pl.pallas_call(
        functools.partial(attend_kernel, nctx, heads, len(pieces), block_rows),
        grid_spec=grid_spec,
        out_shape=[
            jax.ShapeDtypeStruct((total_rows, width), BF16),
            jax.ShapeDtypeStruct((heads, total_rows), F32),
        ],
        compiler_params=params(),
        cost_estimate=NOTHING,
        name="attend",
    )(place, lows, ends, bounds, *pieces)


def attend_back_kernel(
    nctx, heads, count, extra, block_rows, place, lows, ends, bounds, logs, *refs
):
    pieces = refs[:count]
    grad, attended = refs[count : count + 2]
    out, held, turned, grad_keys, grad_values, grad_query = refs[count + 2 + extra :]
    tile_q, tile_k = grad.shape[0], turned.shape[2]
    width = heads * HEAD_DIM
    index = pl.program_id(0)
    scale = jnp.asarray(HEAD_DIM**-0.5, BF16)

    @pl.when(index == 0)
    def _():
        load_pieces(place[0], pieces, nctx, held, block_rows)
        for tile in range(turned.shape[0]):
            turned[tile] = jnp.transpose(
                held[tile * tile_k : (tile + 1) * tile_k, width : 2 * width]
            )
        grad_keys[...] = jnp.zeros_like(grad_keys)
        grad_values[...] = jnp.zeros_like(grad_values)

    query_rows = pl.ds(pl.multiple_of(index * tile_q, tile_q), tile_q)
    queries = stack_heads(held[query_rows, :width] * scale, heads)
    incoming = stack_heads(grad[...], heads)
    product = jnp.transpose(grad[...].astype(F32) * attended[...].astype(F32))
    centre = jnp.concatenate(
        [
            jnp.sum(product[head * HEAD_DIM : (head + 1) * HEAD_DIM, :], axis=0, keepdims=True)
            for head in range(heads)
        ],
        axis=1,
    )
    first_key = jnp.concatenate([bounds[0:1, :]] * heads, axis=1)
    last_key = jnp.concatenate([bounds[1:2, :]] * heads, axis=1)
    log_total = jnp.concatenate([logs[head : head + 1, :] for head in range(heads)], axis=1)
    grad_query[...] = jnp.zeros_like(grad_query)

    def one(tile, _):
        start = tile * tile_k
        key_rows = pl.ds(pl.multiple_of(start, tile_k), tile_k)
        scores = lax.dot_general(
            held[key_rows, width : 2 * width],
            queries,
            (((1,), (1,)), ((), ())),
            preferred_element_type=F32,
        )
        row = lax.broadcasted_iota(jnp.int32, scores.shape, 0)
        last = jnp.minimum(last_key, ends[tile] - 1) - start
        allowed = (row <= last) & (row >= first_key - start)
        chance = jnp.exp(jnp.where(allowed, scores - log_total, NEGATIVE))
        grad_chance = lax.dot_general(
            held[key_rows, 2 * width :],
            incoming,
            (((1,), (1,)), ((), ())),
            preferred_element_type=F32,
        )
        grad_scores = (chance * (grad_chance - centre)).astype(BF16)
        grad_values[key_rows, :] += jnp.dot(
            chance.astype(BF16), incoming, preferred_element_type=F32
        )
        grad_keys[key_rows, :] += jnp.dot(grad_scores, queries, preferred_element_type=F32)
        grad_query[...] += jnp.dot(turned[tile], grad_scores, preferred_element_type=F32)
        return 0

    upper = (index * tile_q + tile_q - 1) // tile_k + 1
    lax.fori_loop(lows[index], upper, one, 0)
    out[query_rows, :width] = (
        fold_heads(grad_query[...], heads, tile_q) * HEAD_DIM**-0.5
    ).astype(BF16)

    @pl.when(index == pl.num_programs(0) - 1)
    def _():
        out[:, width : 2 * width] = grad_keys[...].astype(BF16)
        out[:, 2 * width :] = grad_values[...].astype(BF16)


def attend_back(
    pieces, place, lows, ends, bounds, logs, grad, attended, nctx, block_rows, *needed
):
    total_rows, width = grad.shape
    heads = width // HEAD_DIM
    steps = total_rows // TILE_Q
    grid_spec = pltpu.PrefetchScalarGridSpec(
        num_scalar_prefetch=3,
        grid=(steps,),
        in_specs=[
            pl.BlockSpec((2, TILE_Q), lambda i, *_: (0, i)),
            pl.BlockSpec((heads, TILE_Q), lambda i, *_: (0, i)),
        ]
        + [whole(piece.shape) for piece in pieces]
        + [pl.BlockSpec((TILE_Q, width), lambda i, *_: (i, 0))] * 2
        + anywhere(len(needed)),
        out_specs=whole((total_rows, 3 * width)),
        scratch_shapes=[
            pltpu.VMEM((total_rows, 3 * width), BF16),
            pltpu.VMEM((total_rows // TILE_K, width, TILE_K), BF16),
            pltpu.VMEM((total_rows, width), F32),
            pltpu.VMEM((total_rows, width), F32),
            pltpu.VMEM((width, heads * TILE_Q), F32),
        ],
    )
    return pl.pallas_call(
        functools.partial(attend_back_kernel, nctx, heads, len(pieces), len(needed), block_rows),
        grid_spec=grid_spec,
        out_shape=jax.ShapeDtypeStruct((total_rows, 3 * width), BF16),
        compiler_params=params(),
        cost_estimate=NOTHING,
        name="attend_back",
    )(place, lows, ends, bounds, logs, *pieces, grad, attended, *needed)


def mix_kernel(nctx, nweights, place, heads_in, *refs):
    weights = refs[:nweights]
    source, gain, bias, returned, mixed, low = refs[nweights:]
    rows, depth = mixed.shape
    step = pl.program_id(0)
    left = jnp.concatenate([heads_in[c, 0] for c in range(nctx)], axis=1)
    returned[...] = left

    @pl.when(step == 0)
    def _():
        mixed[...] = source[...].astype(F32)

    for weight, block, columns in every(place, weights, depth):
        mixed[:, columns] += dot(left, weight[block])

    @pl.when(step == pl.num_programs(0) - 1)
    def _():
        def one(at):
            values = mixed[at, :]
            values = values - jnp.mean(values, axis=1, keepdims=True)
            scaling = lax.rsqrt(jnp.mean(values * values, axis=1, keepdims=True) + EPSILON)
            low[at, :] = (values * scaling * gain[...] + bias[...]).astype(BF16)

        strips(rows, one)


def mix(heads_in, weights, full, gain, bias, place):
    nctx, tp, rows, piece = heads_in.shape
    depth = full.shape[1]
    head_width = nctx * piece
    grid_spec = pltpu.PrefetchScalarGridSpec(
        num_scalar_prefetch=1,
        grid=(tp,),
        in_specs=[pl.BlockSpec((nctx, 1, rows, piece), lambda k, s: (0, k, 0, 0))]
        + [
            pl.BlockSpec((w.shape[0], head_width, w.shape[2]), lambda k, s: (0, k, 0))
            for w in weights
        ]
        + [
            pl.BlockSpec((rows, depth), lambda k, s: (s[0], 0)),
            whole((1, depth)),
            whole((1, depth)),
        ],
        out_specs=[
            pl.BlockSpec((rows, head_width), lambda k, s: (0, k)),
            whole((rows, depth)),
            whole((rows, depth)),
        ],
    )
    return pl.pallas_call(
        functools.partial(mix_kernel, nctx, len(weights)),
        grid_spec=grid_spec,
        out_shape=[
            jax.ShapeDtypeStruct((rows, tp * head_width), BF16),
            jax.ShapeDtypeStruct((rows, depth), F32),
            jax.ShapeDtypeStruct((rows, depth), BF16),
        ],
        compiler_params=params(),
        cost_estimate=NOTHING,
        name="mix",
    )(place, heads_in, *weights, full, gain, bias)


def feed_kernel(cuts, low, cot, *refs):
    sources = refs[:3]
    hidden, grad_gate, grad_up, partial = refs[3:7]
    held, sems = refs[7:10], refs[10]

    def copies(index):
        first, size = cuts[index]
        found = []
        for which in range(3):
            if which < 2:
                at = (slice(None), pl.ds(first, size))
            else:
                at = (pl.ds(first, size), slice(None))
            found.append(
                pltpu.make_async_copy(
                    sources[which].at[at], held[which].at[at], sems.at[index * 3 + which]
                )
            )
        return found

    for index in range(len(cuts)):
        for copy in copies(index):
            copy.start()
    gate_weight, up_weight, down_weight = held
    for index, (first, size) in enumerate(cuts):
        for copy in copies(index):
            copy.wait()
        at = slice(first, first + size)
        gate = dot(low[...], gate_weight[:, at])
        up = dot(low[...], up_weight[:, at])
        sigma = 1.0 / (1.0 + jnp.exp(-gate))
        active = gate * sigma
        hidden[:, at] = (active * up).astype(BF16)
        grad = dot_turned(cot[...], down_weight[at, :])
        grad_gate[:, at] = (grad * up * sigma * (1.0 + gate * (1.0 - sigma))).astype(BF16)
        grad_up[:, at] = (grad * active).astype(BF16)
    partial[...] = (
        dot_turned(grad_gate[...], gate_weight[...]) + dot_turned(grad_up[...], up_weight[...])
    ).astype(BF16)


def feed(low, cot, block, gate, up, down_weight):
    rows, depth = low.shape
    hidden = gate.shape[1]
    cuts = []
    while sum(size for _, size in cuts) < hidden:
        first = sum(size for _, size in cuts)
        cuts.append((first, min(512, hidden - first)))
    return pl.pallas_call(
        functools.partial(feed_kernel, tuple(cuts)),
        grid=(1,),
        in_specs=[whole((rows, depth)), pl.BlockSpec((rows, depth), lambda i: (block, 0))]
        + anywhere(3),
        out_specs=[whole((rows, hidden))] * 3 + [whole((rows, depth))],
        scratch_shapes=[pltpu.VMEM(w.shape, BF16) for w in (gate, up, down_weight)]
        + [pltpu.SemaphoreType.DMA((3 * len(cuts),))],
        out_shape=[jax.ShapeDtypeStruct((rows, hidden), BF16)] * 3
        + [jax.ShapeDtypeStruct((rows, depth), BF16)],
        compiler_params=params(),
        cost_estimate=NOTHING,
        name="feed",
    )(low, cot, gate, up, down_weight)


def down(hiddens, mixed, weight, place):
    tp = len(hiddens)
    rows, hidden = hiddens[0].shape
    depth = mixed.shape[1]
    width = depth // tp

    def kernel(place, *refs):
        lefts, (mixed, weight, out, spare) = refs[:tp], refs[tp:]
        for step in range(tp):

            @pl.when(pl.program_id(0) == step)
            def _():
                spare[...] = dot(lefts[step][...], weight[...])
                if step == 0:
                    spare[...] += mixed[...]

        for block in range(tp):
            out[block] = spare[:, block * width : (block + 1) * width].astype(BF16)

    grid_spec = pltpu.PrefetchScalarGridSpec(
        num_scalar_prefetch=1,
        grid=(tp,),
        in_specs=[whole((rows, hidden))] * tp + [whole((rows, depth)), whole((hidden, depth))],
        out_specs=pl.BlockSpec((tp, rows, width), lambda k, s: (0, lax.rem(s[0] - k + tp, tp), 0)),
        scratch_shapes=[pltpu.VMEM((rows, depth), F32)],
    )
    return pl.pallas_call(
        kernel,
        grid_spec=grid_spec,
        out_shape=jax.ShapeDtypeStruct((tp, tp * rows, width), BF16),
        compiler_params=params(),
        cost_estimate=NOTHING,
        name="down",
    )(place, *hiddens, mixed, weight)


def turn_kernel(nctx, nweights, count, place, arrived, own, mixed, cot, gain, *refs):
    weights = refs[:nweights]
    out, grad_mixed, grad_low, gain_grad, shift_grad, moved, sums = refs[nweights + count :]
    rows, depth = mixed.shape
    piece = out.shape[3]

    @pl.when(pl.program_id(0) == 0)
    def _():
        sums[...] = jnp.zeros_like(sums)

        def one(at):
            incoming = arrived[at, :].astype(F32) + own[at, :].astype(F32)
            values = mixed[at, :]
            values = values - jnp.mean(values, axis=1, keepdims=True)
            scaling = lax.rsqrt(jnp.mean(values * values, axis=1, keepdims=True) + EPSILON)
            normed = values * scaling
            sums[0] += fold_rows(incoming)
            sums[1] += fold_rows(incoming * normed)
            scaled = incoming * gain[...]
            total = cot[at, :].astype(F32) + scaling * (
                scaled
                - jnp.mean(scaled, axis=1, keepdims=True)
                - normed * jnp.mean(scaled * normed, axis=1, keepdims=True)
            )
            grad_mixed[at, :] = total
            grad_low[at, :] = total.astype(BF16)

        strips(rows, one)
        shift_grad[...] = jnp.sum(sums[0], axis=0, keepdims=True)
        gain_grad[...] = jnp.sum(sums[1], axis=0, keepdims=True)
        first = 0
        for weight, block, columns in every(place, weights, depth):
            size = weight.shape[2]
            moved[:, first : first + size] = grad_low[:, columns]
            first += size

    product, first = 0.0, 0
    for weight in weights:
        for block in range(weight.shape[0]):
            size = weight.shape[2]
            product = product + dot_turned(moved[:, first : first + size], weight[block])
            first += size
    for c in range(nctx):
        out[c, 0] = product[:, c * piece : (c + 1) * piece].astype(BF16)


def turn(arrived, own, mixed, cot, gain, weights, place, nctx, tp, *needed):
    rows, depth = mixed.shape
    head_width = weights[0].shape[1] // tp
    piece = head_width // nctx
    grid_spec = pltpu.PrefetchScalarGridSpec(
        num_scalar_prefetch=1,
        grid=(tp,),
        in_specs=[whole((rows, depth))] * 4
        + [whole((1, depth))]
        + [
            pl.BlockSpec((w.shape[0], head_width, w.shape[2]), lambda k, s: (0, k, 0))
            for w in weights
        ]
        + anywhere(len(needed)),
        out_specs=[
            pl.BlockSpec((nctx, 1, rows, piece), lambda k, s: (0, k, 0, 0)),
            whole((rows, depth)),
            whole((rows, depth)),
            whole((1, depth)),
            whole((1, depth)),
        ],
        scratch_shapes=[pltpu.VMEM((rows, depth), BF16), pltpu.VMEM((2, 8, depth), F32)],
    )
    return pl.pallas_call(
        functools.partial(turn_kernel, nctx, len(weights), len(needed)),
        grid_spec=grid_spec,
        out_shape=[
            jax.ShapeDtypeStruct((nctx, tp, rows, piece), BF16),
            jax.ShapeDtypeStruct((rows, depth), F32),
            jax.ShapeDtypeStruct((rows, depth), BF16),
            jax.ShapeDtypeStruct((1, depth), F32),
            jax.ShapeDtypeStruct((1, depth), F32),
        ],
        compiler_params=params(),
        cost_estimate=NOTHING,
        name="turn",
    )(place, arrived, own, mixed, cot, gain, *weights, *needed)


def finish_kernel(nctx, nweights, chunk, place, *refs):
    pieces = refs[:nctx]
    cosine, sine_up, sine_down, full, extra, gain = refs[nctx : nctx + 6]
    weights = refs[nctx + 6 : nctx + 6 + nweights]
    out, low, bias_grad, gain_grad, shift_grad, spare, sums = refs[nctx + 6 + nweights :]
    rows, wide = pieces[0].shape
    piece = wide // 3
    tp, width = out.shape[0], out.shape[2]
    depth = tp * width
    strip = spare.shape[0]
    extra_rows = extra.shape[0]

    @pl.when(pl.program_id(0) == 0)
    def _():
        bias_grad[...] = jnp.zeros_like(bias_grad)
        sums[...] = jnp.zeros_like(sums)

    for step in range(nctx):
        source = jnp.bitwise_xor(place[1], step)
        for part in range(3):
            values = pieces[step][:, part * piece : (part + 1) * piece].astype(F32)
            if part < 2:
                values = (
                    values * cosine[...]
                    - pltpu.roll(values, piece - ROT // 2, 1) * sine_up[...]
                    - pltpu.roll(values, ROT // 2, 1) * sine_down[...]
                )
            columns = pl.ds(pl.multiple_of(source * wide + part * piece, piece), piece)
            bias_grad[:, columns] += jnp.sum(values, axis=0, keepdims=True)
            low[:, columns] = values.astype(BF16)

    for weight, block, columns in every(place, weights, depth):
        spare[:, columns] = dot_turned(low[...], weight[block])

    def one(at):
        source = full[at, :].astype(F32)
        source = source - jnp.mean(source, axis=1, keepdims=True)
        scaling = lax.rsqrt(jnp.mean(source * source, axis=1, keepdims=True) + EPSILON)
        normed = source * scaling
        incoming = spare[at, :]
        sums[0] += fold_rows(incoming)
        sums[1] += fold_rows(incoming * normed)
        scaled = incoming * gain[...]
        spare[at, :] = scaling * (
            scaled
            - jnp.mean(scaled, axis=1, keepdims=True)
            - normed * jnp.mean(scaled * normed, axis=1, keepdims=True)
        )

    strips(strip, one)
    first = chunk * pl.num_programs(0) * strip + pl.program_id(0) * strip
    wanted = place[0] * extra_rows

    if strip <= extra_rows:

        @pl.when((first >= wanted) & (first < wanted + extra_rows))
        def _():
            spare[...] += extra[pl.ds(pl.multiple_of(first - wanted, strip), strip), :]

    else:

        @pl.when((wanted >= first) & (wanted < first + strip))
        def _():
            spare[pl.ds(pl.multiple_of(wanted - first, extra_rows), extra_rows), :] += extra[...]

    for block in range(tp):
        out[block] = spare[:, block * width : (block + 1) * width].astype(BF16)

    @pl.when(pl.program_id(0) == pl.num_programs(0) - 1)
    def _():
        shift_grad[...] = jnp.sum(sums[0], axis=0, keepdims=True)
        gain_grad[...] = jnp.sum(sums[1], axis=0, keepdims=True)


def finish(pieces, place, tables, full, extra, gain, weights, chunk, tp):
    rows, wide = pieces[0].shape
    depth = full.shape[1]
    total = weights[0].shape[2]
    strip = 256
    steps = rows // strip
    width = depth // tp
    nctx = len(pieces)
    by_rows = lambda columns: pl.BlockSpec((strip, columns), lambda i, s: (i, 0))
    grid_spec = pltpu.PrefetchScalarGridSpec(
        num_scalar_prefetch=1,
        grid=(steps,),
        in_specs=[by_rows(wide)] * nctx
        + [by_rows(2 * HEAD_DIM)] * 3
        + [
            pl.BlockSpec((strip, depth), lambda i, s: (i + chunk * steps, 0)),
            whole(extra.shape),
            whole((1, depth)),
        ]
        + [whole(weight.shape) for weight in weights],
        out_specs=[
            pl.BlockSpec((tp, strip, width), lambda i, s: (0, i, 0)),
            by_rows(total),
            whole((1, total)),
            whole((1, depth)),
            whole((1, depth)),
        ],
        scratch_shapes=[pltpu.VMEM((strip, depth), F32), pltpu.VMEM((2, 8, depth), F32)],
    )
    return pl.pallas_call(
        functools.partial(finish_kernel, nctx, len(weights), chunk),
        grid_spec=grid_spec,
        out_shape=[
            jax.ShapeDtypeStruct((tp, rows, width), BF16),
            jax.ShapeDtypeStruct((rows, total), BF16),
            jax.ShapeDtypeStruct((1, total), F32),
            jax.ShapeDtypeStruct((1, depth), F32),
            jax.ShapeDtypeStruct((1, depth), F32),
        ],
        compiler_params=params(),
        cost_estimate=NOTHING,
        name="finish",
    )(place, *pieces, *tables, full, extra, gain, *weights)


def join_kernel(tp, place, *refs):
    blocks, out = refs[:tp], refs[tp]
    width = blocks[0].shape[1]
    for step in range(tp):
        owner = lax.rem(place[0] - step + tp, tp)
        out[:, pl.ds(pl.multiple_of(owner * width, width), width)] = blocks[step][...]


def join(blocks, place):
    tp = len(blocks)
    rows, width = blocks[0].shape
    strip = rows // tp
    grid_spec = pltpu.PrefetchScalarGridSpec(
        num_scalar_prefetch=1,
        grid=(tp,),
        in_specs=[pl.BlockSpec((strip, width), lambda i, s: (lax.rem(s[0] - i + tp, tp), 0))] * tp,
        out_specs=pl.BlockSpec((strip, tp * width), lambda i, s: (i, 0)),
    )
    return pl.pallas_call(
        functools.partial(join_kernel, tp),
        grid_spec=grid_spec,
        out_shape=jax.ShapeDtypeStruct((rows, tp * width), BF16),
        compiler_params=params(),
        cost_estimate=NOTHING,
        name="join",
    )(place, *blocks)


def contract_rows(left, right):
    return lax.dot_general(left, right, (((0,), (0,)), ((), ())), preferred_element_type=F32)


def pick(stack, index):
    return lax.dynamic_index_in_dim(stack, index, 0, keepdims=False)


def shards(
    nfsdp,
    nctx,
    tp,
    inputs,
    cotangent,
    first_gain,
    first_bias,
    qkv_weight,
    qkv_bias,
    out_weight,
    second_gain,
    second_bias,
    gate_weight,
    up_weight,
    down_weight,
    lengths,
    fill_counts,
):
    data = ("fsdp", "ctx")
    ndata = nfsdp * nctx
    block_rows, width = inputs.shape
    depth = tp * width
    half_depth = depth // 2
    unit = depth // ndata
    tensor_index = lax.axis_index("tp").astype(jnp.int32)
    context_index = lax.axis_index("ctx").astype(jnp.int32)
    fsdp_index = lax.axis_index("fsdp").astype(jnp.int32)
    part_rows = block_rows // tp
    chunk_rows = block_rows // CHUNKS
    head_width = qkv_weight.shape[2]
    piece = head_width // nctx
    wide = 3 * piece

    square = nfsdp == 2 and nctx == 4 and unit % 128 == 0
    place = jnp.stack([tensor_index, context_index, fsdp_index])

    def shift(value, step):
        return lax.ppermute(value, "tp", [(i, (i + step) % tp) for i in range(tp)])

    def swap(value, step):
        return lax.ppermute(value, "ctx", [(i, i ^ step) for i in range(nctx)])

    def cross(value):
        return lax.ppermute(value, "fsdp", [(0, 1), (1, 0)])

    def gather(value):
        rows = value.shape[0] // 2
        first, second = value[:rows], value[rows:]
        first_x, second_y = cross(first), swap(second, 2)
        first_y = swap(jnp.stack([first, first_x]), 2)
        second_x = cross(jnp.stack([second, second_y]))
        mine = jnp.stack(
            [
                jnp.concatenate([first, second]),
                jnp.concatenate([first_y[0], second_y]),
                jnp.concatenate([first_x, second_x[0]]),
                jnp.concatenate([first_y[1], second_x[1]]),
            ]
        )
        return (mine, swap(mine, 1))

    core_index = context_index % 2
    groups = [list(range(0, ndata, 2)), list(range(1, ndata, 2))]

    def half_of(value, index):
        rows = value.shape[0]
        blocks = value.reshape(rows, ndata // 2, 2, unit)
        return lax.dynamic_index_in_dim(blocks, index, 2, keepdims=False).reshape(rows, half_depth)

    def presum(make, value):
        arrived = swap(make(half_of(value, 1 - core_index)).astype(BF16), 1)
        return (make(half_of(value, core_index)) + arrived.astype(F32)).astype(BF16)

    def scatter(make, value, axis):
        if not square:
            return lax.psum_scatter(
                make(value).astype(BF16), data, scatter_dimension=axis, tiled=True
            )
        return lax.psum_scatter(
            presum(make, value), data, scatter_dimension=axis, tiled=True, axis_index_groups=groups
        )

    def total(left, right):
        return (left.astype(F32) + right.astype(F32)).astype(BF16)

    def scatter_rows(make, value):
        if not square:
            return lax.psum_scatter(make(value).astype(BF16), data, scatter_dimension=0, tiled=True)
        half = presum(make, value)
        half = half.reshape(2, 2, unit, half.shape[1])
        first, second = half[:, :, : unit // 2], half[:, :, unit // 2 :]
        far, near = 1 - fsdp_index, fsdp_index
        up, here = 1 - context_index // 2, context_index // 2
        first = total(pick(first, near), cross(pick(first, far)))
        second = jnp.swapaxes(second, 0, 1)
        second = total(pick(second, here), swap(pick(second, up), 2))
        first = total(pick(first, here), swap(pick(first, up), 2))
        second = total(pick(second, near), cross(pick(second, far)))
        return jnp.concatenate([first, second])

    owners = [(tensor_index - step + tp) % tp for step in range(tp)]

    own_qkv = (
        qkv_weight.reshape(-1, 3, nctx, piece).transpose(0, 2, 1, 3).reshape(-1, 3 * head_width)
    )
    if square:
        qkv_blocks = gather(own_qkv)
    else:
        qkv_blocks = (lax.all_gather(own_qkv, data, axis=0, tiled=True)[None],)
    full_gate = lax.all_gather(gate_weight, data, axis=0, tiled=True)
    full_up = lax.all_gather(up_weight, data, axis=0, tiled=True)
    full_down = lax.all_gather(down_weight, data, axis=1, tiled=True)

    validity, position, first_key, last_key = layout(lengths[0], fill_counts[0], block_rows)
    own_position = lax.dynamic_slice_in_dim(position, context_index * block_rows, block_rows, 0)
    tables = rotary_tables(own_position)
    bounds = jnp.stack([first_key, last_key])
    tile_first = first_key[::TILE_Q]
    tile_count = tile_first.shape[0]
    lows = jnp.where(validity[::TILE_Q], tile_first // TILE_K, tile_count * TILE_Q).astype(jnp.int32)
    key_block = jnp.arange(0, nctx * block_rows, TILE_K, dtype=jnp.int32) // block_rows
    ends = (
        key_block * block_rows
        + jnp.sum(
            jnp.where(
                key_block[:, None] == jnp.arange(nctx, dtype=jnp.int32)[None, :],
                fill_counts[0][None, :],
                0,
            ),
            axis=1,
        )
    ).astype(jnp.int32)

    flat_bias = qkv_bias.reshape(3, nctx, piece).transpose(1, 0, 2).reshape(1, -1)
    gain_one, bias_one = first_gain[None], first_bias[None]
    gain_two, bias_two = second_gain[None], second_bias[None]

    rings = [[inputs[c * chunk_rows : (c + 1) * chunk_rows]] for c in range(CHUNKS)]
    for chunk in range(CHUNKS):
        for _ in range(tp - 1):
            rings[chunk].append(shift(rings[chunk][-1], 1))
    lows_one, fulls, pieces, chunk_tables = [], [], [], []
    for chunk in range(CHUNKS):
        at = slice(chunk * chunk_rows, (chunk + 1) * chunk_rows)
        chunk_tables.append([table[at] for table in tables])
        low, full, outgoing = project(
            rings[chunk],
            place,
            gain_one,
            bias_one,
            qkv_blocks,
            flat_bias,
            chunk_tables[chunk],
            nctx,
        )
        lows_one.append(low)
        fulls.append(full)
        pieces.append(pick(outgoing, context_index))
        for step in range(1, nctx):
            pieces.append(swap(pick(outgoing, context_index ^ step), step))
    full = jnp.concatenate(fulls, axis=0)

    own_out = tie(out_weight, rings[-1][-1])
    stack = jnp.zeros((tp,) + out_weight.shape, BF16)
    stack = lax.dynamic_update_index_in_dim(stack, own_out, tensor_index, 0)
    for step in range(1, tp):
        moved_out = shift(own_out, step)
        stack = lax.dynamic_update_index_in_dim(stack, moved_out, owners[step], 0)
    own_out = stack.reshape(depth, -1)
    if square:
        out_blocks = gather(own_out)
    else:
        out_blocks = (lax.all_gather(own_out, data, axis=1, tiled=True)[None],)

    cot_own = tie(cotangent, moved_out)
    cot = join([cot_own] + [shift(cot_own, step) for step in range(1, tp)], place)

    attended, logs = attend(pieces, place[1:2], lows, ends, bounds, nctx, block_rows)
    arrived = lax.all_to_all(
        attended.reshape(nctx * tp, part_rows, piece),
        ("ctx", "tp"),
        split_axis=0,
        concat_axis=0,
        tiled=True,
    )
    returned, mixed, second_low = mix(
        arrived.reshape(nctx, tp, part_rows, piece), out_blocks, full, gain_two, bias_two, place
    )

    seconds, hiddens, gates, ups, partials = [second_low], [], [], [], []
    for _ in range(tp - 1):
        seconds.append(shift(seconds[-1], 1))
    for step in range(tp):
        hidden, gate, up, partial = feed(
            seconds[step], cot, step, full_gate, full_up, full_down
        )
        hiddens.append(hidden)
        gates.append(gate)
        ups.append(up)
        partials.append(partial)

    all_second = jnp.concatenate(seconds, axis=0)
    all_hidden = jnp.concatenate(hiddens, axis=0)
    all_gate = jnp.concatenate(gates, axis=0)
    all_up = jnp.concatenate(ups, axis=0)

    feedforward = down(hiddens, mixed, full_down, place)
    travelling = partials[1 % tp]
    for step in range(2, tp):
        needed = [feedforward] if step == tp - 1 else []
        travelling = add(shift(travelling, 1), partials[step], *needed)
    by_gate = lambda value: contract_rows(value, all_gate)
    by_up = lambda value: contract_rows(value, all_up)
    by_hidden = lambda value: contract_rows(all_hidden, value)
    needed = []
    if square:
        half_gate = presum(by_gate, all_second)
        half_up = presum(by_up, all_second)
        needed = [half_gate, half_up]
        scatter_half = lambda value, axis: lax.psum_scatter(
            value, data, scatter_dimension=axis, tiled=True, axis_index_groups=groups
        )
        total_gate, total_up = scatter_half(half_gate, 0), scatter_half(half_up, 0)
    else:
        total_gate, total_up = scatter(by_gate, all_second, 0), scatter(by_up, all_second, 0)

    grad_heads, grad_mixed, mixed_low, gain_grad_two, shift_grad_two = turn(
        shift(travelling, 1),
        partials[0],
        mixed,
        cot,
        gain_two,
        out_blocks,
        place,
        nctx,
        tp,
        *needed,
    )
    grad_heads = lax.all_to_all(
        grad_heads.reshape(nctx * tp, part_rows, piece),
        ("ctx", "tp"),
        split_axis=0,
        concat_axis=0,
        tiled=True,
    ).reshape(nctx * block_rows, piece)

    feedforward = tie(feedforward, grad_heads)
    layer_out = pick(feedforward, tensor_index).astype(F32)
    for step in range(1, tp):
        layer_out = layer_out + shift(
            pick(feedforward, (tensor_index + step) % tp), step
        ).astype(F32)
    layer_out = layer_out.astype(BF16)

    by_returned = lambda value: contract_rows(value, returned)
    needed = []
    if square:
        half_down = presum(by_hidden, cot)
        needed = [half_down]
        total_down = scatter_half(half_down, 1)
    else:
        total_down = scatter(by_hidden, cot, 1)
    total_out = scatter_rows(by_returned, mixed_low)
    out_parts = jnp.swapaxes(total_out.reshape(-1, tp, head_width), 0, 1)
    total_out = pick(out_parts, tensor_index).astype(F32)
    for step in range(1, tp):
        total_out = total_out + shift(pick(out_parts, (tensor_index + step) % tp), step).astype(F32)
    total_out = total_out.T

    grad_grouped = attend_back(
        pieces, place[1:2], lows, ends, bounds, logs, grad_heads, attended, nctx, block_rows, *needed
    )
    grad_grouped = grad_grouped.reshape(nctx, CHUNKS, chunk_rows, wide)
    grad_lows, bias_grads, gain_grads, shift_grads, grad_rows = [], [], [], [], []
    for chunk in range(CHUNKS):
        outgoing = grad_grouped[:, chunk]
        arrived = [pick(outgoing, context_index)]
        for step in range(1, nctx):
            arrived.append(swap(pick(outgoing, context_index ^ step), step))
        partial, low, bias_grad, gain_grad, shift_grad = finish(
            arrived,
            place,
            chunk_tables[chunk],
            full,
            grad_mixed,
            gain_one,
            qkv_blocks,
            chunk,
            tp,
        )
        grad_lows.append(low)
        bias_grads.append(bias_grad)
        gain_grads.append(gain_grad)
        shift_grads.append(shift_grad)
        travelling = pick(partial, owners[1 % tp])
        for step in range(1, tp):
            needed = [layer_out] if (chunk, step) == (0, 1) else []
            travelling = add(shift(travelling, 1), pick(partial, owners[(step + 1) % tp]), *needed)
        grad_rows.append(travelling)
    grad_inputs = jnp.concatenate(grad_rows, axis=0)

    all_low, all_grad = jnp.concatenate(lows_one, axis=0), jnp.concatenate(grad_lows, axis=0)
    total_qkv = scatter_rows(lambda value: contract_rows(value, all_grad), all_low)
    total_qkv = (
        total_qkv.astype(F32)
        .reshape(-1, nctx, 3, piece)
        .transpose(0, 2, 1, 3)
        .reshape(-1, 3, head_width)
    )

    def exchange(value, axis, size):
        step = 1
        while step < size:
            value = value + lax.ppermute(value, axis, [(i, i ^ step) for i in range(size)])
            step *= 2
        return value

    small = jnp.concatenate([sum(gain_grads), sum(shift_grads), gain_grad_two, shift_grad_two], axis=1)
    small = exchange(small, "tp", tp)
    small = jnp.concatenate([sum(bias_grads), small], axis=1)
    small = exchange(exchange(small, "ctx", nctx), "fsdp", nfsdp)
    bias_total, small = small[:, : 3 * head_width], small[:, 3 * head_width :]
    bias_total = bias_total.reshape(nctx, 3, piece).transpose(1, 0, 2).reshape(3, head_width)
    small = small.reshape(4, depth)
    return (
        layer_out,
        grad_inputs,
        small[0],
        small[1],
        total_qkv,
        bias_total,
        total_out,
        small[2],
        small[3],
        total_gate.astype(F32),
        total_up.astype(F32),
        total_down.astype(F32),
    )


def solution(mesh):
    data = ("fsdp", "ctx")
    by_rows = P(data, "tp")
    by_columns = P("tp", data)
    qkv = P(data, None, "tp")
    return jax.shard_map(
        functools.partial(shards, mesh.shape["fsdp"], mesh.shape["ctx"], mesh.shape["tp"]),
        mesh=mesh,
        in_specs=(
            by_rows,
            by_rows,
            P(),
            P(),
            qkv,
            P(None, "tp"),
            by_columns,
            P(),
            P(),
            by_rows,
            by_rows,
            by_columns,
            P("fsdp", None),
            P("fsdp", None),
        ),
        out_specs=(
            by_rows,
            by_rows,
            P(),
            P(),
            qkv,
            P(None, "tp"),
            by_columns,
            P(),
            P(),
            by_rows,
            by_rows,
            by_columns,
        ),
        check_vma=False,
    )
```

```python
import functools

import jax
import jax.numpy as jnp
from jax import lax
from jax.experimental import pallas as pl
from jax.experimental.pallas import tpu as pltpu
from jax.sharding import PartitionSpec as P

HEAD_DIM = 64
ROT = 16
EPSILON = 1e-05
NEGATIVE = -1e30
FLOOR = -1e20
VMEM_LIMIT = 56 * 1024 * 1024
TILE_Q = 512
TILE_K = 512
CHUNKS = 2

F32 = jnp.float32
BF16 = jnp.bfloat16


def layout(lengths, fill_counts, block_rows):
    blocks_count = fill_counts.shape[0]
    seq_count = lengths.shape[0]
    slot_index = jnp.arange(blocks_count * block_rows, dtype=jnp.int32)
    block_of = slot_index // block_rows
    within = slot_index - block_of * block_rows
    chooser = block_of[:, None] == jnp.arange(blocks_count, dtype=jnp.int32)[None, :]
    fill_here = jnp.sum(jnp.where(chooser, fill_counts[None, :], 0), axis=1)
    before = jnp.cumsum(fill_counts) - fill_counts
    before_here = jnp.sum(jnp.where(chooser, before[None, :], 0), axis=1)
    validity = within < fill_here
    used_index = before_here + within
    seq_ends = jnp.cumsum(lengths)
    sequence = jnp.sum((used_index[:, None] >= seq_ends[None, :]).astype(jnp.int32), axis=1)
    seq_starts = seq_ends - lengths
    picker = sequence[:, None] == jnp.arange(seq_count, dtype=jnp.int32)[None, :]
    start_here = jnp.sum(jnp.where(picker, seq_starts[None, :], 0), axis=1)
    after = before + fill_counts
    start_block = jnp.sum((seq_starts[:, None] >= after[None, :]).astype(jnp.int32), axis=1)
    start_block = jnp.minimum(start_block, blocks_count - 1)
    block_pick = start_block[:, None] == jnp.arange(blocks_count, dtype=jnp.int32)[None, :]
    start_before = jnp.sum(jnp.where(block_pick, before[None, :], 0), axis=1)
    start_slot = start_block * block_rows + seq_starts - start_before
    slot_here = jnp.sum(jnp.where(picker, start_slot[None, :], 0), axis=1)
    first_key = jnp.where(validity, slot_here, 0).astype(jnp.int32)
    last_key = jnp.where(validity, slot_index, -1).astype(jnp.int32)
    return (validity, used_index - start_here, first_key, last_key)


def rotary_tables(position):
    half = ROT // 2
    lane = jnp.arange(2 * HEAD_DIM, dtype=jnp.int32) % HEAD_DIM
    frequency = 10000.0 ** (-(2.0 * (lane % half).astype(F32)) / ROT)
    angles = position.astype(F32)[:, None] * frequency[None, :]
    cosine, sine = jnp.cos(angles), jnp.sin(angles)
    lane = lane[None, :]
    return (
        jnp.where(lane < ROT, cosine, 1.0),
        jnp.where(lane < half, -sine, 0.0),
        jnp.where((lane >= half) & (lane < ROT), sine, 0.0),
    )


def params(**extra):
    return pltpu.CompilerParams(vmem_limit_bytes=VMEM_LIMIT, **extra)


def takes(microseconds):
    return pl.CostEstimate(
        flops=int(microseconds * 1e9), bytes_accessed=0, transcendentals=0
    )


def whole(shape):
    return pl.BlockSpec(shape, lambda *_: (0,) * len(shape))


def anywhere(count):
    return [pl.BlockSpec(memory_space=pl.ANY)] * count


def natural(place, which, block, size):
    if size is None:
        return slice(None)
    f, c = place[2], place[1]
    c_high = lax.shift_right_logical(c, 1)
    high = jnp.bitwise_xor(f, block // 2) * 2 + jnp.bitwise_xor(c_high, block % 2)
    low = jnp.bitwise_xor(jnp.bitwise_and(c, 1), which)
    return pl.ds(pl.multiple_of((high * 2 + low) * size, size), size)


def every(place, weights, depth):
    size = None if len(weights) == 1 else depth // (len(weights) * weights[0].shape[0])
    return [
        (weight, block, natural(place, which, block, size))
        for which, weight in enumerate(weights)
        for block in range(weight.shape[0])
    ]


def dot(left, right):
    return jnp.dot(left, right, preferred_element_type=F32)


def dot_turned(left, right):
    return lax.dot_general(left, right, (((1,), (1,)), ((), ())), preferred_element_type=F32)


def tie(value, *needed):
    def kernel(*refs):
        del refs

    return pl.pallas_call(
        kernel,
        in_specs=anywhere(1 + len(needed)),
        out_specs=pl.BlockSpec(memory_space=pl.ANY),
        out_shape=jax.ShapeDtypeStruct(value.shape, value.dtype),
        input_output_aliases={0: 0},
        name="tie",
    )(value, *needed)


def add_kernel(left, right, *refs):
    refs[-1][...] = (left[...].astype(F32) + right[...].astype(F32)).astype(BF16)


def add(left, right, *needed):
    rows, columns = left.shape
    strip = min(rows, 128)
    block = pl.BlockSpec((strip, columns), lambda i: (i, 0))
    return pl.pallas_call(
        add_kernel,
        grid=(rows // strip,),
        in_specs=[block, block] + anywhere(len(needed)),
        out_specs=block,
        out_shape=jax.ShapeDtypeStruct(left.shape, BF16),
        compiler_params=params(),
        cost_estimate=takes(1),
        name="ring_add",
    )(left, right, *needed)


def project_kernel(tp, per, place, *refs):
    blocks = refs[:tp]
    gain, bias, weight, weight_bias, cosine, sine_up, sine_down = refs[tp : tp + 7]
    low, full, out = refs[tp + 7 :]
    rows, width = blocks[0].shape
    depth = tp * width
    piece = out.shape[2] // 3

    @pl.when(pl.program_id(0) == 0)
    def _():
        strip = 128
        for start in range(0, rows, strip):
            at = slice(start, start + strip)
            parts = [block[at, :].astype(F32) for block in blocks]
            centre = sum(jnp.sum(part, axis=1, keepdims=True) for part in parts) / depth
            parts = [part - centre for part in parts]
            spread = sum(jnp.sum(part * part, axis=1, keepdims=True) for part in parts) / depth
            scaling = lax.rsqrt(spread + EPSILON)
            for step in range(tp):
                owner = lax.rem(place[0] - step + tp, tp)
                columns = pl.ds(pl.multiple_of(owner * width, width), width)
                low[at, columns] = (
                    parts[step] * scaling * gain[:, columns] + bias[:, columns]
                ).astype(BF16)
                full[at, columns] = blocks[step][at, :]

    product = dot(low[...], weight[...]) + weight_bias[...]
    for group in range(per):
        for part in range(3):
            first = (group * 3 + part) * piece
            values = product[:, first : first + piece]
            if part < 2:
                values = (
                    values * cosine[...]
                    + pltpu.roll(values, piece - ROT // 2, 1) * sine_up[...]
                    + pltpu.roll(values, ROT // 2, 1) * sine_down[...]
                )
            out[group, :, part * piece : (part + 1) * piece] = values.astype(BF16)


def project(blocks, place, gain, bias, weight, weight_bias, tables, nctx):
    tp = len(blocks)
    rows, width = blocks[0].shape
    depth = tp * width
    total = weight.shape[1]
    wide = total // nctx
    per = 2 if nctx % 2 == 0 else 1
    grid_spec = pltpu.PrefetchScalarGridSpec(
        num_scalar_prefetch=1,
        grid=(nctx // per,),
        in_specs=[whole((rows, width))] * tp
        + [whole((1, depth))] * 2
        + [
            pl.BlockSpec((depth, per * wide), lambda i, s: (0, i)),
            pl.BlockSpec((1, per * wide), lambda i, s: (0, i)),
        ]
        + [whole((rows, 2 * HEAD_DIM))] * 3,
        out_specs=[
            whole((rows, depth)),
            whole((rows, depth)),
            pl.BlockSpec((per, rows, wide), lambda i, s: (i, 0, 0)),
        ],
    )
    return pl.pallas_call(
        functools.partial(project_kernel, tp, per),
        grid_spec=grid_spec,
        out_shape=[
            jax.ShapeDtypeStruct((rows, depth), BF16),
            jax.ShapeDtypeStruct((rows, depth), BF16),
            jax.ShapeDtypeStruct((nctx, rows, wide), BF16),
        ],
        compiler_params=params(),
        cost_estimate=takes(6),
        name="project",
    )(place, *blocks, gain, bias, weight, weight_bias, *tables)


def stack_heads(tile, heads):
    lane = lax.broadcasted_iota(jnp.int32, tile.shape, 1) // HEAD_DIM
    return jnp.concatenate(
        [jnp.where(lane == head, tile, jnp.zeros_like(tile)) for head in range(heads)], axis=0
    )


def fold_heads(stacked, heads, columns):
    row = lax.broadcasted_iota(jnp.int32, (stacked.shape[0], columns), 0) // HEAD_DIM
    folded = jnp.zeros((stacked.shape[0], columns), F32)
    for head in range(heads):
        folded = folded + jnp.where(row == head, stacked[:, head * columns : (head + 1) * columns], 0.0)
    return jnp.transpose(folded)


def load_pieces(place, pieces, nctx, held, block_rows):
    chunk_rows = pieces[0].shape[0]
    chunks = len(pieces) // nctx
    for chunk in range(chunks):
        for step in range(nctx):
            source = jnp.bitwise_xor(place, step)
            first = source * block_rows + chunk * chunk_rows
            held[pl.ds(pl.multiple_of(first, chunk_rows), chunk_rows), :] = pieces[
                chunk * nctx + step
            ][...]


def attend_kernel(nctx, heads, count, block_rows, place, lows, ends, bounds, *refs):
    pieces = refs[:count]
    out, logs, held, turned, total, high, sums = refs[count:]
    tile_q, tile_k = out.shape[0], turned.shape[2]
    width = heads * HEAD_DIM
    index = pl.program_id(0)

    @pl.when(index == 0)
    def _():
        load_pieces(place[0], pieces, nctx, held, block_rows)
        for tile in range(turned.shape[0]):
            turned[tile] = jnp.transpose(held[tile * tile_k : (tile + 1) * tile_k, 2 * width :])

    query_rows = pl.ds(pl.multiple_of(index * tile_q, tile_q), tile_q)
    queries = stack_heads(held[query_rows, :width] * jnp.asarray(HEAD_DIM**-0.5, BF16), heads)
    first_key = jnp.concatenate([bounds[0:1, :]] * heads, axis=1)
    last_key = jnp.concatenate([bounds[1:2, :]] * heads, axis=1)
    total[...] = jnp.zeros_like(total)
    high[...] = jnp.full_like(high, FLOOR)
    sums[...] = jnp.zeros_like(sums)

    def one(tile, _):
        start = tile * tile_k
        keys = held[pl.ds(pl.multiple_of(start, tile_k), tile_k), width : 2 * width]
        scores = lax.dot_general(
            keys, queries, (((1,), (1,)), ((), ())), preferred_element_type=F32
        )
        row = lax.broadcasted_iota(jnp.int32, scores.shape, 0)
        last = jnp.minimum(last_key, ends[tile] - 1) - start
        allowed = (row <= last) & (row >= first_key - start)
        scores = jnp.where(allowed, scores, NEGATIVE)
        highest = jnp.maximum(high[...], jnp.max(scores, axis=0, keepdims=True))
        raised = jnp.exp(scores - highest)
        shrink = jnp.exp(high[...] - highest)
        sums[...] = sums[...] * shrink + jnp.sum(raised, axis=0, keepdims=True)
        total[...] = total[...] * shrink + jnp.dot(
            turned[tile], raised.astype(BF16), preferred_element_type=F32
        )
        high[...] = highest
        return 0

    upper = (index * tile_q + tile_q - 1) // tile_k + 1
    lax.fori_loop(lows[index], upper, one, 0)
    found = sums[...] > 0.0
    safe = jnp.where(found, sums[...], 1.0)
    out[...] = fold_heads(
        total[...] * jnp.where(found, 1.0 / safe, 0.0), heads, tile_q
    ).astype(BF16)
    log_total = jnp.where(found, high[...] + jnp.log(safe), 0.0)
    for head in range(heads):
        logs[head : head + 1, :] = log_total[:, head * tile_q : (head + 1) * tile_q]


def attend(pieces, place, lows, ends, bounds, nctx, block_rows):
    total_rows = nctx * block_rows
    width = pieces[0].shape[1] // 3
    heads = width // HEAD_DIM
    steps = total_rows // TILE_Q
    grid_spec = pltpu.PrefetchScalarGridSpec(
        num_scalar_prefetch=3,
        grid=(steps,),
        in_specs=[pl.BlockSpec((2, TILE_Q), lambda i, *_: (0, i))]
        + [whole(piece.shape) for piece in pieces],
        out_specs=[
            pl.BlockSpec((TILE_Q, width), lambda i, *_: (i, 0)),
            pl.BlockSpec((heads, TILE_Q), lambda i, *_: (0, i)),
        ],
        scratch_shapes=[
            pltpu.VMEM((total_rows, 3 * width), BF16),
            pltpu.VMEM((total_rows // TILE_K, width, TILE_K), BF16),
            pltpu.VMEM((width, heads * TILE_Q), F32),
            pltpu.VMEM((1, heads * TILE_Q), F32),
            pltpu.VMEM((1, heads * TILE_Q), F32),
        ],
    )
    return pl.pallas_call(
        functools.partial(attend_kernel, nctx, heads, len(pieces), block_rows),
        grid_spec=grid_spec,
        out_shape=[
            jax.ShapeDtypeStruct((total_rows, width), BF16),
            jax.ShapeDtypeStruct((heads, total_rows), F32),
        ],
        compiler_params=params(),
        cost_estimate=takes(20),
        name="attend",
    )(place, lows, ends, bounds, *pieces)


def attend_back_kernel(
    nctx, heads, count, extra, block_rows, place, lows, ends, bounds, logs, *refs
):
    pieces = refs[:count]
    grad, attended = refs[count : count + 2]
    out, held, turned, grad_keys, grad_values, grad_query = refs[count + 2 + extra :]
    tile_q, tile_k = grad.shape[0], turned.shape[2]
    width = heads * HEAD_DIM
    index = pl.program_id(0)
    scale = jnp.asarray(HEAD_DIM**-0.5, BF16)

    @pl.when(index == 0)
    def _():
        load_pieces(place[0], pieces, nctx, held, block_rows)
        for tile in range(turned.shape[0]):
            turned[tile] = jnp.transpose(
                held[tile * tile_k : (tile + 1) * tile_k, width : 2 * width]
            )
        grad_keys[...] = jnp.zeros_like(grad_keys)
        grad_values[...] = jnp.zeros_like(grad_values)

    query_rows = pl.ds(pl.multiple_of(index * tile_q, tile_q), tile_q)
    queries = stack_heads(held[query_rows, :width] * scale, heads)
    incoming = stack_heads(grad[...], heads)
    product = jnp.transpose(grad[...].astype(F32) * attended[...].astype(F32))
    centre = jnp.concatenate(
        [
            jnp.sum(product[head * HEAD_DIM : (head + 1) * HEAD_DIM, :], axis=0, keepdims=True)
            for head in range(heads)
        ],
        axis=1,
    )
    first_key = jnp.concatenate([bounds[0:1, :]] * heads, axis=1)
    last_key = jnp.concatenate([bounds[1:2, :]] * heads, axis=1)
    log_total = jnp.concatenate([logs[head : head + 1, :] for head in range(heads)], axis=1)
    grad_query[...] = jnp.zeros_like(grad_query)

    def one(tile, _):
        start = tile * tile_k
        key_rows = pl.ds(pl.multiple_of(start, tile_k), tile_k)
        scores = lax.dot_general(
            held[key_rows, width : 2 * width],
            queries,
            (((1,), (1,)), ((), ())),
            preferred_element_type=F32,
        )
        row = lax.broadcasted_iota(jnp.int32, scores.shape, 0)
        last = jnp.minimum(last_key, ends[tile] - 1) - start
        allowed = (row <= last) & (row >= first_key - start)
        chance = jnp.exp(jnp.where(allowed, scores - log_total, NEGATIVE))
        grad_chance = lax.dot_general(
            held[key_rows, 2 * width :],
            incoming,
            (((1,), (1,)), ((), ())),
            preferred_element_type=F32,
        )
        grad_scores = (chance * (grad_chance - centre)).astype(BF16)
        grad_values[key_rows, :] += jnp.dot(
            chance.astype(BF16), incoming, preferred_element_type=F32
        )
        grad_keys[key_rows, :] += jnp.dot(grad_scores, queries, preferred_element_type=F32)
        grad_query[...] += jnp.dot(turned[tile], grad_scores, preferred_element_type=F32)
        return 0

    upper = (index * tile_q + tile_q - 1) // tile_k + 1
    lax.fori_loop(lows[index], upper, one, 0)
    out[query_rows, :width] = (
        fold_heads(grad_query[...], heads, tile_q) * HEAD_DIM**-0.5
    ).astype(BF16)

    @pl.when(index == pl.num_programs(0) - 1)
    def _():
        out[:, width : 2 * width] = grad_keys[...].astype(BF16)
        out[:, 2 * width :] = grad_values[...].astype(BF16)


def attend_back(
    pieces, place, lows, ends, bounds, logs, grad, attended, nctx, block_rows, *needed
):
    total_rows, width = grad.shape
    heads = width // HEAD_DIM
    steps = total_rows // TILE_Q
    grid_spec = pltpu.PrefetchScalarGridSpec(
        num_scalar_prefetch=3,
        grid=(steps,),
        in_specs=[
            pl.BlockSpec((2, TILE_Q), lambda i, *_: (0, i)),
            pl.BlockSpec((heads, TILE_Q), lambda i, *_: (0, i)),
        ]
        + [whole(piece.shape) for piece in pieces]
        + [pl.BlockSpec((TILE_Q, width), lambda i, *_: (i, 0))] * 2
        + anywhere(len(needed)),
        out_specs=whole((total_rows, 3 * width)),
        scratch_shapes=[
            pltpu.VMEM((total_rows, 3 * width), BF16),
            pltpu.VMEM((total_rows // TILE_K, width, TILE_K), BF16),
            pltpu.VMEM((total_rows, width), F32),
            pltpu.VMEM((total_rows, width), F32),
            pltpu.VMEM((width, heads * TILE_Q), F32),
        ],
    )
    return pl.pallas_call(
        functools.partial(attend_back_kernel, nctx, heads, len(pieces), len(needed), block_rows),
        grid_spec=grid_spec,
        out_shape=jax.ShapeDtypeStruct((total_rows, 3 * width), BF16),
        compiler_params=params(),
        cost_estimate=takes(25),
        name="attend_back",
    )(place, lows, ends, bounds, logs, *pieces, grad, attended, *needed)


def mix_kernel(nctx, nweights, place, heads_in, *refs):
    weights = refs[:nweights]
    source, gain, bias, returned, mixed, low = refs[nweights:]
    rows, depth = mixed.shape
    step = pl.program_id(0)
    left = jnp.concatenate([heads_in[c, 0] for c in range(nctx)], axis=1)
    returned[...] = left

    @pl.when(step == 0)
    def _():
        mixed[...] = source[...].astype(F32)

    for weight, block, columns in every(place, weights, depth):
        mixed[:, columns] += dot(left, weight[block])

    @pl.when(step == pl.num_programs(0) - 1)
    def _():
        values = mixed[...]
        values = values - jnp.mean(values, axis=1, keepdims=True)
        scaling = lax.rsqrt(jnp.mean(values * values, axis=1, keepdims=True) + EPSILON)
        low[...] = (values * scaling * gain[...] + bias[...]).astype(BF16)


def mix(heads_in, weights, full, gain, bias, place):
    nctx, tp, rows, piece = heads_in.shape
    depth = full.shape[1]
    head_width = nctx * piece
    grid_spec = pltpu.PrefetchScalarGridSpec(
        num_scalar_prefetch=1,
        grid=(tp,),
        in_specs=[pl.BlockSpec((nctx, 1, rows, piece), lambda k, s: (0, k, 0, 0))]
        + [
            pl.BlockSpec((w.shape[0], head_width, w.shape[2]), lambda k, s: (0, k, 0))
            for w in weights
        ]
        + [
            pl.BlockSpec((rows, depth), lambda k, s: (s[0], 0)),
            whole((1, depth)),
            whole((1, depth)),
        ],
        out_specs=[
            pl.BlockSpec((rows, head_width), lambda k, s: (0, k)),
            whole((rows, depth)),
            whole((rows, depth)),
        ],
    )
    return pl.pallas_call(
        functools.partial(mix_kernel, nctx, len(weights)),
        grid_spec=grid_spec,
        out_shape=[
            jax.ShapeDtypeStruct((rows, tp * head_width), BF16),
            jax.ShapeDtypeStruct((rows, depth), F32),
            jax.ShapeDtypeStruct((rows, depth), BF16),
        ],
        compiler_params=params(),
        cost_estimate=takes(5),
        name="mix",
    )(place, heads_in, *weights, full, gain, bias)


def feed_kernel(cuts, place, low, cot, *refs):
    sources = refs[:3]
    kept, hidden, grad_gate, grad_up, partial = refs[-9:-4]
    held, sems = refs[-4:-1], refs[-1]

    def copies(index):
        first, size = cuts[index]
        found = []
        for which in range(3):
            if which < 2:
                at = (slice(None), pl.ds(first, size))
            else:
                at = (pl.ds(first, size), slice(None))
            found.append(
                pltpu.make_async_copy(
                    sources[which].at[at], held[which].at[at], sems.at[index * 3 + which]
                )
            )
        return found

    for index in range(len(cuts)):
        for copy in copies(index):
            copy.start()
    kept[...] = low[...]
    gate_weight, up_weight, down_weight = held
    for index, (first, size) in enumerate(cuts):
        for copy in copies(index):
            copy.wait()
        at = slice(first, first + size)
        gate = dot(low[...], gate_weight[:, at])
        up = dot(low[...], up_weight[:, at])
        sigma = 1.0 / (1.0 + jnp.exp(-gate))
        active = gate * sigma
        hidden[:, at] = (active * up).astype(BF16)
        grad = dot_turned(cot[...], down_weight[at, :])
        grad_gate[:, at] = (grad * up * sigma * (1.0 + gate * (1.0 - sigma))).astype(BF16)
        grad_up[:, at] = (grad * active).astype(BF16)
    partial[...] = (
        dot_turned(grad_gate[...], gate_weight[...]) + dot_turned(grad_up[...], up_weight[...])
    ).astype(BF16)


def feed(low, cot, step, tp, gate, up, down_weight, place, held):
    rows, depth = low.shape
    hidden = gate.shape[1]
    cuts = []
    while sum(size for _, size in cuts) < hidden:
        first = sum(size for _, size in cuts)
        cuts.append((first, min(512, hidden - first)))
    by_owner = lambda columns: pl.BlockSpec(
        (rows, columns), lambda i, s: (lax.rem(s[0] - step + tp, tp), 0)
    )
    grid_spec = pltpu.PrefetchScalarGridSpec(
        num_scalar_prefetch=1,
        grid=(1,),
        in_specs=[whole((rows, depth)), by_owner(depth)] + anywhere(3 + len(held)),
        out_specs=[by_owner(depth)] + [by_owner(hidden)] * 3 + [whole((rows, depth))],
        scratch_shapes=[pltpu.VMEM(w.shape, BF16) for w in (gate, up, down_weight)]
        + [pltpu.SemaphoreType.DMA((3 * len(cuts),))],
    )
    return pl.pallas_call(
        functools.partial(feed_kernel, tuple(cuts)),
        grid_spec=grid_spec,
        out_shape=[jax.ShapeDtypeStruct((tp * rows, depth), BF16)]
        + [jax.ShapeDtypeStruct((tp * rows, hidden), BF16)] * 3
        + [jax.ShapeDtypeStruct((rows, depth), BF16)],
        input_output_aliases={6 + index: index for index in range(len(held))},
        compiler_params=params(),
        cost_estimate=takes(8),
        name="feed",
    )(place, low, cot, gate, up, down_weight, *held)


def down(hidden, mixed, weight, place):
    rows, depth = mixed.shape
    tp = hidden.shape[0] // rows
    inner = hidden.shape[1]

    def kernel(place, left, mixed, weight, out, spare):
        spare[...] = dot(left[...], weight[...])

        @pl.when(pl.program_id(0) == place[0])
        def _():
            spare[...] += mixed[...]

        out[...] = spare[...].astype(BF16)

    grid_spec = pltpu.PrefetchScalarGridSpec(
        num_scalar_prefetch=1,
        grid=(tp,),
        in_specs=[
            pl.BlockSpec((rows, inner), lambda k, s: (k, 0)),
            whole((rows, depth)),
            whole((inner, depth)),
        ],
        out_specs=pl.BlockSpec((rows, depth), lambda k, s: (k, 0)),
        scratch_shapes=[pltpu.VMEM((rows, depth), F32)],
    )
    return pl.pallas_call(
        kernel,
        grid_spec=grid_spec,
        out_shape=jax.ShapeDtypeStruct((tp * rows, depth), BF16),
        compiler_params=params(),
        cost_estimate=takes(7),
        name="down",
    )(place, hidden, mixed, weight)


def blame(left, right, which, pick_left, unit, arrived=None, *needed):
    rows = left.shape[0]
    picked = (left if pick_left else right).shape[1] // unit // 2
    other = (right if pick_left else left).shape[1]
    chosen = pl.BlockSpec((rows, unit), lambda j, s: (0, 2 * j + s[0]))
    kept = whole((rows, other))
    if pick_left:
        shape = (picked * unit, other)
        target = pl.BlockSpec((unit, other), lambda j, s: (j, 0))
    else:
        shape = (other, picked * unit)
        target = pl.BlockSpec((other, unit), lambda j, s: (0, j))
    extra = [] if arrived is None else [arrived]

    def kernel(which, left, right, *refs):
        product = lax.dot_general(
            left[...], right[...], (((0,), (0,)), ((), ())), preferred_element_type=F32
        )
        if extra:
            product = product + refs[0][...].astype(F32)
        refs[-1][...] = product.astype(BF16)

    grid_spec = pltpu.PrefetchScalarGridSpec(
        num_scalar_prefetch=1,
        grid=(picked,),
        in_specs=([chosen, kept] if pick_left else [kept, chosen])
        + [target] * len(extra)
        + anywhere(len(needed)),
        out_specs=target,
    )
    return pl.pallas_call(
        kernel,
        grid_spec=grid_spec,
        out_shape=jax.ShapeDtypeStruct(shape, BF16),
        compiler_params=params(),
        cost_estimate=takes(3),
        name="blame",
    )(which, left, right, *extra, *needed)


def turn_kernel(nctx, nweights, count, place, arrived, own, mixed, cot, gain, *refs):
    weights = refs[:nweights]
    out, grad_mixed, grad_low, gain_grad, shift_grad, moved = refs[nweights + count :]
    rows, depth = mixed.shape
    piece = out.shape[3]

    @pl.when(pl.program_id(0) == 0)
    def _():
        incoming = arrived[...].astype(F32) + own[...].astype(F32)
        values = mixed[...]
        values = values - jnp.mean(values, axis=1, keepdims=True)
        scaling = lax.rsqrt(jnp.mean(values * values, axis=1, keepdims=True) + EPSILON)
        normed = values * scaling
        shift_grad[...] = jnp.sum(incoming, axis=0, keepdims=True)
        gain_grad[...] = jnp.sum(incoming * normed, axis=0, keepdims=True)
        scaled = incoming * gain[...]
        total = cot[...].astype(F32) + scaling * (
            scaled
            - jnp.mean(scaled, axis=1, keepdims=True)
            - normed * jnp.mean(scaled * normed, axis=1, keepdims=True)
        )
        grad_mixed[...] = total
        grad_low[...] = total.astype(BF16)
        first = 0
        for weight, block, columns in every(place, weights, depth):
            size = weight.shape[2]
            moved[:, first : first + size] = grad_low[:, columns]
            first += size

    product, first = 0.0, 0
    for weight in weights:
        for block in range(weight.shape[0]):
            size = weight.shape[2]
            product = product + dot_turned(moved[:, first : first + size], weight[block])
            first += size
    for c in range(nctx):
        out[c, 0] = product[:, c * piece : (c + 1) * piece].astype(BF16)


def turn(arrived, own, mixed, cot, gain, weights, place, nctx, tp, *needed):
    rows, depth = mixed.shape
    head_width = weights[0].shape[1] // tp
    piece = head_width // nctx
    grid_spec = pltpu.PrefetchScalarGridSpec(
        num_scalar_prefetch=1,
        grid=(tp,),
        in_specs=[whole((rows, depth))] * 3
        + [pl.BlockSpec((rows, depth), lambda k, s: (s[0], 0)), whole((1, depth))]
        + [
            pl.BlockSpec((w.shape[0], head_width, w.shape[2]), lambda k, s: (0, k, 0))
            for w in weights
        ]
        + anywhere(len(needed)),
        out_specs=[
            pl.BlockSpec((nctx, 1, rows, piece), lambda k, s: (0, k, 0, 0)),
            whole((rows, depth)),
            whole((rows, depth)),
            whole((1, depth)),
            whole((1, depth)),
        ],
        scratch_shapes=[pltpu.VMEM((rows, depth), BF16)],
    )
    return pl.pallas_call(
        functools.partial(turn_kernel, nctx, len(weights), len(needed)),
        grid_spec=grid_spec,
        out_shape=[
            jax.ShapeDtypeStruct((nctx, tp, rows, piece), BF16),
            jax.ShapeDtypeStruct((rows, depth), F32),
            jax.ShapeDtypeStruct((rows, depth), BF16),
            jax.ShapeDtypeStruct((1, depth), F32),
            jax.ShapeDtypeStruct((1, depth), F32),
        ],
        compiler_params=params(),
        cost_estimate=takes(6),
        name="turn",
    )(place, arrived, own, mixed, cot, gain, *weights, *needed)


def finish_kernel(nctx, chunk, place, *refs):
    pieces = refs[:nctx]
    cosine, sine_up, sine_down, full, extra, gain = refs[nctx : nctx + 6]
    weight, out, low, bias_grad, gain_grad, shift_grad, spare = refs[nctx + 6 :]
    rows, wide = pieces[0].shape
    piece = wide // 3
    tp, width = out.shape[0], out.shape[2]
    depth = tp * width
    strip = spare.shape[0]
    extra_rows = extra.shape[0]

    @pl.when(pl.program_id(0) == 0)
    def _():
        bias_grad[...] = jnp.zeros_like(bias_grad)
        gain_grad[...] = jnp.zeros_like(gain_grad)
        shift_grad[...] = jnp.zeros_like(shift_grad)

    for step in range(nctx):
        source = jnp.bitwise_xor(place[1], step)
        for part in range(3):
            values = pieces[step][:, part * piece : (part + 1) * piece].astype(F32)
            if part < 2:
                values = (
                    values * cosine[...]
                    - pltpu.roll(values, piece - ROT // 2, 1) * sine_up[...]
                    - pltpu.roll(values, ROT // 2, 1) * sine_down[...]
                )
            columns = pl.ds(pl.multiple_of(source * wide + part * piece, piece), piece)
            bias_grad[:, columns] += jnp.sum(values, axis=0, keepdims=True)
            low[:, columns] = values.astype(BF16)

    incoming = dot_turned(low[...], weight[...])
    source = full[...].astype(F32)
    source = source - jnp.mean(source, axis=1, keepdims=True)
    scaling = lax.rsqrt(jnp.mean(source * source, axis=1, keepdims=True) + EPSILON)
    normed = source * scaling
    shift_grad[...] += jnp.sum(incoming, axis=0, keepdims=True)
    gain_grad[...] += jnp.sum(incoming * normed, axis=0, keepdims=True)
    scaled = incoming * gain[...]
    spare[...] = scaling * (
        scaled
        - jnp.mean(scaled, axis=1, keepdims=True)
        - normed * jnp.mean(scaled * normed, axis=1, keepdims=True)
    )
    first = chunk * pl.num_programs(0) * strip + pl.program_id(0) * strip
    wanted = place[0] * extra_rows

    if strip <= extra_rows:

        @pl.when((first >= wanted) & (first < wanted + extra_rows))
        def _():
            spare[...] += extra[pl.ds(pl.multiple_of(first - wanted, strip), strip), :]

    else:

        @pl.when((wanted >= first) & (wanted < first + strip))
        def _():
            spare[pl.ds(pl.multiple_of(wanted - first, extra_rows), extra_rows), :] += extra[...]

    for block in range(tp):
        out[block] = spare[:, block * width : (block + 1) * width].astype(BF16)


def finish(pieces, place, tables, full, extra, gain, weight, chunk, tp):
    rows, wide = pieces[0].shape
    depth = full.shape[1]
    total = weight.shape[1]
    strip = 256
    steps = rows // strip
    width = depth // tp
    nctx = len(pieces)
    by_rows = lambda columns: pl.BlockSpec((strip, columns), lambda i, s: (i, 0))
    grid_spec = pltpu.PrefetchScalarGridSpec(
        num_scalar_prefetch=1,
        grid=(steps,),
        in_specs=[by_rows(wide)] * nctx
        + [by_rows(2 * HEAD_DIM)] * 3
        + [
            pl.BlockSpec((strip, depth), lambda i, s: (i + chunk * steps, 0)),
            whole(extra.shape),
            whole((1, depth)),
        ]
        + [whole(weight.shape)],
        out_specs=[
            pl.BlockSpec((tp, strip, width), lambda i, s: (0, i, 0)),
            by_rows(total),
            whole((1, total)),
            whole((1, depth)),
            whole((1, depth)),
        ],
        scratch_shapes=[pltpu.VMEM((strip, depth), F32)],
    )
    return pl.pallas_call(
        functools.partial(finish_kernel, nctx, chunk),
        grid_spec=grid_spec,
        out_shape=[
            jax.ShapeDtypeStruct((tp, rows, width), BF16),
            jax.ShapeDtypeStruct((rows, total), BF16),
            jax.ShapeDtypeStruct((1, total), F32),
            jax.ShapeDtypeStruct((1, depth), F32),
            jax.ShapeDtypeStruct((1, depth), F32),
        ],
        compiler_params=params(),
        cost_estimate=takes(7),
        name="finish",
    )(place, *pieces, *tables, full, extra, gain, weight)


def contract_rows(left, right):
    return lax.dot_general(left, right, (((0,), (0,)), ((), ())), preferred_element_type=F32)


def pick(stack, index):
    return lax.dynamic_index_in_dim(stack, index, 0, keepdims=False)


def shards(
    nfsdp,
    nctx,
    tp,
    inputs,
    cotangent,
    first_gain,
    first_bias,
    qkv_weight,
    qkv_bias,
    out_weight,
    second_gain,
    second_bias,
    gate_weight,
    up_weight,
    down_weight,
    lengths,
    fill_counts,
):
    data = ("fsdp", "ctx")
    ndata = nfsdp * nctx
    block_rows, width = inputs.shape
    depth = tp * width
    half_depth = depth // 2
    unit = depth // ndata
    tensor_index = lax.axis_index("tp").astype(jnp.int32)
    context_index = lax.axis_index("ctx").astype(jnp.int32)
    fsdp_index = lax.axis_index("fsdp").astype(jnp.int32)
    part_rows = block_rows // tp
    chunk_rows = block_rows // CHUNKS
    head_width = qkv_weight.shape[2]
    piece = head_width // nctx
    wide = 3 * piece

    square = nfsdp == 2 and nctx == 4 and unit % 128 == 0
    place = jnp.stack([tensor_index, context_index, fsdp_index])

    def shift(value, step):
        return lax.ppermute(value, "tp", [(i, (i + step) % tp) for i in range(tp)])

    def swap(value, step):
        return lax.ppermute(value, "ctx", [(i, i ^ step) for i in range(nctx)])

    def cross(value):
        return lax.ppermute(value, "fsdp", [(0, 1), (1, 0)])

    def gather(value):
        rows = value.shape[0] // 2
        first, second = value[:rows], value[rows:]
        first_x, second_y = cross(first), swap(second, 2)
        first_y = swap(jnp.stack([first, first_x]), 2)
        second_x = cross(jnp.stack([second, second_y]))
        mine = jnp.stack(
            [
                jnp.concatenate([first, second]),
                jnp.concatenate([first_y[0], second_y]),
                jnp.concatenate([first_x, second_x[0]]),
                jnp.concatenate([first_y[1], second_x[1]]),
            ]
        )
        return (mine, swap(mine, 1))

    core_index = context_index % 2
    groups = [list(range(0, ndata, 2)), list(range(1, ndata, 2))]
    own_half, other_half = core_index[None], (1 - core_index)[None]

    def presum(left, right, pick_left, *needed):
        first = blame(left, right, other_half, pick_left, unit, None, *needed)
        return blame(left, right, own_half, pick_left, unit, swap(first, 1))

    def scatter_half(value, axis):
        return lax.psum_scatter(
            value, data, scatter_dimension=axis, tiled=True, axis_index_groups=groups
        )

    def scatter_whole(left, right, axis):
        return lax.psum_scatter(
            contract_rows(left, right).astype(BF16), data, scatter_dimension=axis, tiled=True
        )

    def total(left, right):
        return (left.astype(F32) + right.astype(F32)).astype(BF16)

    def scatter_rows(half):
        half = half.reshape(2, 2, unit, half.shape[1])
        first, second = half[:, :, : unit // 2], half[:, :, unit // 2 :]
        far, near = 1 - fsdp_index, fsdp_index
        up, here = 1 - context_index // 2, context_index // 2
        first = total(pick(first, near), cross(pick(first, far)))
        second = jnp.swapaxes(second, 0, 1)
        second = total(pick(second, here), swap(pick(second, up), 2))
        first = total(pick(first, here), swap(pick(first, up), 2))
        second = total(pick(second, near), cross(pick(second, far)))
        return jnp.concatenate([first, second])

    owners = [(tensor_index - step + tp) % tp for step in range(tp)]

    own_qkv = (
        qkv_weight.reshape(-1, 3, nctx, piece).transpose(0, 2, 1, 3).reshape(-1, 3 * head_width)
    )
    full_qkv = lax.all_gather(own_qkv, data, axis=0, tiled=True)
    full_cot = lax.all_gather(cotangent, "tp", axis=1, tiled=True)
    full_gate = lax.all_gather(gate_weight, data, axis=0, tiled=True)
    full_up = lax.all_gather(up_weight, data, axis=0, tiled=True)
    full_down = lax.all_gather(down_weight, data, axis=1, tiled=True)

    validity, position, first_key, last_key = layout(lengths[0], fill_counts[0], block_rows)
    own_position = lax.dynamic_slice_in_dim(position, context_index * block_rows, block_rows, 0)
    tables = rotary_tables(own_position)
    bounds = jnp.stack([first_key, last_key])
    tile_first = first_key[::TILE_Q]
    tile_count = tile_first.shape[0]
    lows = jnp.where(validity[::TILE_Q], tile_first // TILE_K, tile_count * TILE_Q).astype(jnp.int32)
    key_block = jnp.arange(0, nctx * block_rows, TILE_K, dtype=jnp.int32) // block_rows
    ends = (
        key_block * block_rows
        + jnp.sum(
            jnp.where(
                key_block[:, None] == jnp.arange(nctx, dtype=jnp.int32)[None, :],
                fill_counts[0][None, :],
                0,
            ),
            axis=1,
        )
    ).astype(jnp.int32)

    flat_bias = qkv_bias.reshape(3, nctx, piece).transpose(1, 0, 2).reshape(1, -1)
    gain_one, bias_one = first_gain[None], first_bias[None]
    gain_two, bias_two = second_gain[None], second_bias[None]

    rings = [[inputs[c * chunk_rows : (c + 1) * chunk_rows]] for c in range(CHUNKS)]
    for chunk in range(CHUNKS):
        for _ in range(tp - 1):
            rings[chunk].append(shift(rings[chunk][-1], 1))
    lows_one, fulls, pieces, chunk_tables = [], [], [], []
    for chunk in range(CHUNKS):
        at = slice(chunk * chunk_rows, (chunk + 1) * chunk_rows)
        chunk_tables.append([table[at] for table in tables])
        low, full, outgoing = project(
            rings[chunk],
            place,
            gain_one,
            bias_one,
            full_qkv,
            flat_bias,
            chunk_tables[chunk],
            nctx,
        )
        lows_one.append(low)
        fulls.append(full)
        pieces.append(pick(outgoing, context_index))
        for step in range(1, nctx):
            pieces.append(swap(pick(outgoing, context_index ^ step), step))
    full = jnp.concatenate(fulls, axis=0)

    own_out = tie(out_weight, *[blocks[-1] for blocks in rings])
    stack = jnp.zeros((tp,) + out_weight.shape, BF16)
    stack = lax.dynamic_update_index_in_dim(stack, own_out, tensor_index, 0)
    for step in range(1, tp):
        moved_out = shift(own_out, step)
        stack = lax.dynamic_update_index_in_dim(stack, moved_out, owners[step], 0)
    own_out = stack.reshape(depth, -1)
    if square:
        out_blocks = gather(own_out)
    else:
        out_blocks = (lax.all_gather(own_out, data, axis=1, tiled=True)[None],)

    attended, logs = attend(pieces, place[1:2], lows, ends, bounds, nctx, block_rows)
    arrived = lax.all_to_all(
        attended.reshape(nctx * tp, part_rows, piece),
        ("ctx", "tp"),
        split_axis=0,
        concat_axis=0,
        tiled=True,
    )
    returned, mixed, second_low = mix(
        arrived.reshape(nctx, tp, part_rows, piece), out_blocks, full, gain_two, bias_two, place
    )

    arrived, held, partials = second_low, [], []
    for step in range(tp):
        *held, partial = feed(
            arrived, full_cot, step, tp, full_gate, full_up, full_down, place, held
        )
        partials.append(partial)
        if step < tp - 1:
            arrived = shift(arrived, 1)
    all_second, hidden, all_gate, all_up = held

    feedforward = down(hidden, mixed, full_down, place)
    travelling = partials[1 % tp]
    for step in range(2, tp):
        needed = [feedforward] if step == tp - 1 else []
        travelling = add(shift(travelling, 1), partials[step], *needed)
    needed = []
    if square:
        needed = [presum(all_second, all_gate, True), presum(all_second, all_up, True)]
        total_gate, total_up = scatter_half(needed[0], 0), scatter_half(needed[1], 0)
    else:
        total_gate = scatter_whole(all_second, all_gate, 0)
        total_up = scatter_whole(all_second, all_up, 0)

    grad_heads, grad_mixed, mixed_low, gain_grad_two, shift_grad_two = turn(
        shift(travelling, 1),
        partials[0],
        mixed,
        full_cot,
        gain_two,
        out_blocks,
        place,
        nctx,
        tp,
        *needed,
    )
    grad_heads = lax.all_to_all(
        grad_heads.reshape(nctx * tp, part_rows, piece),
        ("ctx", "tp"),
        split_axis=0,
        concat_axis=0,
        tiled=True,
    ).reshape(nctx * block_rows, piece)

    layer_out = lax.psum_scatter(feedforward, "tp", scatter_dimension=1, tiled=True)

    needed = []
    if square:
        needed = [presum(hidden, full_cot, False)]
        total_down = scatter_half(needed[0], 1)
        total_out = scatter_rows(presum(mixed_low, returned, True))
    else:
        total_down = scatter_whole(hidden, full_cot, 1)
        total_out = scatter_whole(mixed_low, returned, 0)
    out_parts = jnp.swapaxes(total_out.reshape(-1, tp, head_width), 0, 1)
    total_out = pick(out_parts, tensor_index).astype(F32)
    for step in range(1, tp):
        total_out = total_out + shift(pick(out_parts, (tensor_index + step) % tp), step).astype(F32)
    total_out = total_out.T

    grad_grouped = attend_back(
        pieces, place[1:2], lows, ends, bounds, logs, grad_heads, attended, nctx, block_rows, *needed
    )
    grad_grouped = grad_grouped.reshape(nctx, CHUNKS, chunk_rows, wide)
    grad_lows, bias_grads, gain_grads, shift_grads, grad_rows = [], [], [], [], []
    for chunk in range(CHUNKS):
        outgoing = grad_grouped[:, chunk]
        arrived = [pick(outgoing, context_index)]
        for step in range(1, nctx):
            arrived.append(swap(pick(outgoing, context_index ^ step), step))
        partial, low, bias_grad, gain_grad, shift_grad = finish(
            arrived,
            place,
            chunk_tables[chunk],
            full,
            grad_mixed,
            gain_one,
            full_qkv,
            chunk,
            tp,
        )
        grad_lows.append(low)
        bias_grads.append(bias_grad)
        gain_grads.append(gain_grad)
        shift_grads.append(shift_grad)
        travelling = pick(partial, owners[1 % tp])
        for step in range(1, tp):
            travelling = add(shift(travelling, 1), pick(partial, owners[(step + 1) % tp]))
        grad_rows.append(travelling)
    grad_inputs = jnp.concatenate(grad_rows, axis=0)

    all_low, all_grad = jnp.concatenate(lows_one, axis=0), jnp.concatenate(grad_lows, axis=0)
    if square:
        total_qkv = scatter_half(presum(all_low, all_grad, True), 0)
    else:
        total_qkv = scatter_whole(all_low, all_grad, 0)
    total_qkv = (
        total_qkv.astype(F32)
        .reshape(-1, nctx, 3, piece)
        .transpose(0, 2, 1, 3)
        .reshape(-1, 3, head_width)
    )

    def exchange(value, axis, size):
        step = 1
        while step < size:
            value = value + lax.ppermute(value, axis, [(i, i ^ step) for i in range(size)])
            step *= 2
        return value

    small = jnp.concatenate([sum(gain_grads), sum(shift_grads), gain_grad_two, shift_grad_two], axis=1)
    small = exchange(small, "tp", tp)
    small = jnp.concatenate([sum(bias_grads), small], axis=1)
    small = exchange(exchange(small, "ctx", nctx), "fsdp", nfsdp)
    bias_total, small = small[:, : 3 * head_width], small[:, 3 * head_width :]
    bias_total = bias_total.reshape(nctx, 3, piece).transpose(1, 0, 2).reshape(3, head_width)
    small = small.reshape(4, depth)
    return (
        layer_out,
        grad_inputs,
        small[0],
        small[1],
        total_qkv,
        bias_total,
        total_out,
        small[2],
        small[3],
        total_gate.astype(F32),
        total_up.astype(F32),
        total_down.astype(F32),
    )


def solution(mesh):
    data = ("fsdp", "ctx")
    by_rows = P(data, "tp")
    by_columns = P("tp", data)
    qkv = P(data, None, "tp")
    return jax.shard_map(
        functools.partial(shards, mesh.shape["fsdp"], mesh.shape["ctx"], mesh.shape["tp"]),
        mesh=mesh,
        in_specs=(
            by_rows,
            by_rows,
            P(),
            P(),
            qkv,
            P(None, "tp"),
            by_columns,
            P(),
            P(),
            by_rows,
            by_rows,
            by_columns,
            P("fsdp", None),
            P("fsdp", None),
        ),
        out_specs=(
            by_rows,
            by_rows,
            P(),
            P(),
            qkv,
            P(None, "tp"),
            by_columns,
            P(),
            P(),
            by_rows,
            by_rows,
            by_columns,
        ),
        check_vma=False,
    )
```

```python
import functools

import jax
import jax.numpy as jnp
from jax import lax
from jax.experimental import pallas as pl
from jax.experimental.pallas import tpu as pltpu
from jax.sharding import PartitionSpec as P

HEAD_DIM = 64
ROT = 16
EPSILON = 1e-05
NEGATIVE = -1e30
FLOOR = -1e20
VMEM_LIMIT = 56 * 1024 * 1024
TILE_Q = 512
TILE_K = 512
CHUNKS = 2
HALVES = 2

F32 = jnp.float32
BF16 = jnp.bfloat16


def layout(lengths, fill_counts, block_rows):
    blocks_count = fill_counts.shape[0]
    seq_count = lengths.shape[0]
    slot_index = jnp.arange(blocks_count * block_rows, dtype=jnp.int32)
    block_of = slot_index // block_rows
    within = slot_index - block_of * block_rows
    chooser = block_of[:, None] == jnp.arange(blocks_count, dtype=jnp.int32)[None, :]
    fill_here = jnp.sum(jnp.where(chooser, fill_counts[None, :], 0), axis=1)
    before = jnp.cumsum(fill_counts) - fill_counts
    before_here = jnp.sum(jnp.where(chooser, before[None, :], 0), axis=1)
    validity = within < fill_here
    used_index = before_here + within
    seq_ends = jnp.cumsum(lengths)
    sequence = jnp.sum((used_index[:, None] >= seq_ends[None, :]).astype(jnp.int32), axis=1)
    seq_starts = seq_ends - lengths
    picker = sequence[:, None] == jnp.arange(seq_count, dtype=jnp.int32)[None, :]
    start_here = jnp.sum(jnp.where(picker, seq_starts[None, :], 0), axis=1)
    after = before + fill_counts
    start_block = jnp.sum((seq_starts[:, None] >= after[None, :]).astype(jnp.int32), axis=1)
    start_block = jnp.minimum(start_block, blocks_count - 1)
    block_pick = start_block[:, None] == jnp.arange(blocks_count, dtype=jnp.int32)[None, :]
    start_before = jnp.sum(jnp.where(block_pick, before[None, :], 0), axis=1)
    start_slot = start_block * block_rows + seq_starts - start_before
    slot_here = jnp.sum(jnp.where(picker, start_slot[None, :], 0), axis=1)
    first_key = jnp.where(validity, slot_here, 0).astype(jnp.int32)
    last_key = jnp.where(validity, slot_index, -1).astype(jnp.int32)
    return (validity, used_index - start_here, first_key, last_key)


def rotary_tables(position):
    half = ROT // 2
    lane = jnp.arange(2 * HEAD_DIM, dtype=jnp.int32) % HEAD_DIM
    frequency = 10000.0 ** (-(2.0 * (lane % half).astype(F32)) / ROT)
    angles = position.astype(F32)[:, None] * frequency[None, :]
    cosine, sine = jnp.cos(angles), jnp.sin(angles)
    lane = lane[None, :]
    return (
        jnp.where(lane < ROT, cosine, 1.0),
        jnp.where(lane < half, -sine, 0.0),
        jnp.where((lane >= half) & (lane < ROT), sine, 0.0),
    )


def params(**extra):
    return pltpu.CompilerParams(vmem_limit_bytes=VMEM_LIMIT, **extra)


def takes(microseconds):
    return pl.CostEstimate(
        flops=int(microseconds * 1e9), bytes_accessed=0, transcendentals=0
    )


def whole(shape):
    return pl.BlockSpec(shape, lambda *_: (0,) * len(shape))


def anywhere(count):
    return [pl.BlockSpec(memory_space=pl.ANY)] * count


def natural(place, which, block, size):
    if size is None:
        return slice(None)
    f, c = place[2], place[1]
    c_high = lax.shift_right_logical(c, 1)
    high = jnp.bitwise_xor(f, block // 2) * 2 + jnp.bitwise_xor(c_high, block % 2)
    low = jnp.bitwise_xor(jnp.bitwise_and(c, 1), which)
    return pl.ds(pl.multiple_of((high * 2 + low) * size, size), size)


def every(place, weights, depth):
    size = None if len(weights) == 1 else depth // (len(weights) * weights[0].shape[0])
    return [
        (weight, block, natural(place, which, block, size))
        for which, weight in enumerate(weights)
        for block in range(weight.shape[0])
    ]


def dot(left, right):
    return jnp.dot(left, right, preferred_element_type=F32)


def dot_turned(left, right):
    return lax.dot_general(left, right, (((1,), (1,)), ((), ())), preferred_element_type=F32)


def tie(value, *needed):
    def kernel(*refs):
        del refs

    return pl.pallas_call(
        kernel,
        in_specs=anywhere(1 + len(needed)),
        out_specs=pl.BlockSpec(memory_space=pl.ANY),
        out_shape=jax.ShapeDtypeStruct(value.shape, value.dtype),
        input_output_aliases={0: 0},
        name="tie",
    )(value, *needed)


def add_kernel(left, right, *refs):
    refs[-1][...] = (left[...].astype(F32) + right[...].astype(F32)).astype(BF16)


def add(left, right, *needed):
    rows, columns = left.shape
    strip = min(rows, 128)
    block = pl.BlockSpec((strip, columns), lambda i: (i, 0))
    return pl.pallas_call(
        add_kernel,
        grid=(rows // strip,),
        in_specs=[block, block] + anywhere(len(needed)),
        out_specs=block,
        out_shape=jax.ShapeDtypeStruct(left.shape, BF16),
        compiler_params=params(),
        cost_estimate=takes(1),
        name="ring_add",
    )(left, right, *needed)


def project_kernel(tp, per, place, *refs):
    blocks = refs[:tp]
    gain, bias, weight, weight_bias, cosine, sine_up, sine_down = refs[tp : tp + 7]
    low, full, out = refs[tp + 7 :]
    rows, width = blocks[0].shape
    depth = tp * width
    piece = out.shape[2] // 3

    @pl.when(pl.program_id(0) == 0)
    def _():
        strip = 128
        for start in range(0, rows, strip):
            at = slice(start, start + strip)
            parts = [block[at, :].astype(F32) for block in blocks]
            centre = sum(jnp.sum(part, axis=1, keepdims=True) for part in parts) / depth
            parts = [part - centre for part in parts]
            spread = sum(jnp.sum(part * part, axis=1, keepdims=True) for part in parts) / depth
            scaling = lax.rsqrt(spread + EPSILON)
            for step in range(tp):
                owner = lax.rem(place[0] - step + tp, tp)
                columns = pl.ds(pl.multiple_of(owner * width, width), width)
                low[at, columns] = (
                    parts[step] * scaling * gain[:, columns] + bias[:, columns]
                ).astype(BF16)
                full[at, columns] = blocks[step][at, :]

    product = dot(low[...], weight[...]) + weight_bias[...]
    for group in range(per):
        for part in range(3):
            first = (group * 3 + part) * piece
            values = product[:, first : first + piece]
            if part < 2:
                values = (
                    values * cosine[...]
                    + pltpu.roll(values, piece - ROT // 2, 1) * sine_up[...]
                    + pltpu.roll(values, ROT // 2, 1) * sine_down[...]
                )
            out[group, :, part * piece : (part + 1) * piece] = values.astype(BF16)


def project(blocks, place, gain, bias, weight, weight_bias, tables, nctx):
    tp = len(blocks)
    rows, width = blocks[0].shape
    depth = tp * width
    total = weight.shape[1]
    wide = total // nctx
    per = 2 if nctx % 2 == 0 else 1
    grid_spec = pltpu.PrefetchScalarGridSpec(
        num_scalar_prefetch=1,
        grid=(nctx // per,),
        in_specs=[whole((rows, width))] * tp
        + [whole((1, depth))] * 2
        + [
            pl.BlockSpec((depth, per * wide), lambda i, s: (0, i)),
            pl.BlockSpec((1, per * wide), lambda i, s: (0, i)),
        ]
        + [whole((rows, 2 * HEAD_DIM))] * 3,
        out_specs=[
            whole((rows, depth)),
            whole((rows, depth)),
            pl.BlockSpec((per, rows, wide), lambda i, s: (i, 0, 0)),
        ],
    )
    return pl.pallas_call(
        functools.partial(project_kernel, tp, per),
        grid_spec=grid_spec,
        out_shape=[
            jax.ShapeDtypeStruct((rows, depth), BF16),
            jax.ShapeDtypeStruct((rows, depth), BF16),
            jax.ShapeDtypeStruct((nctx, rows, wide), BF16),
        ],
        compiler_params=params(),
        cost_estimate=takes(6),
        name="project",
    )(place, *blocks, gain, bias, weight, weight_bias, *tables)


def stack_heads(tile, heads):
    lane = lax.broadcasted_iota(jnp.int32, tile.shape, 1) // HEAD_DIM
    return jnp.concatenate(
        [jnp.where(lane == head, tile, jnp.zeros_like(tile)) for head in range(heads)], axis=0
    )


def fold_heads(stacked, heads, columns):
    row = lax.broadcasted_iota(jnp.int32, (stacked.shape[0], columns), 0) // HEAD_DIM
    folded = jnp.zeros((stacked.shape[0], columns), F32)
    for head in range(heads):
        folded = folded + jnp.where(row == head, stacked[:, head * columns : (head + 1) * columns], 0.0)
    return jnp.transpose(folded)


def load_pieces(place, pieces, nctx, held, block_rows):
    chunk_rows = pieces[0].shape[0]
    chunks = len(pieces) // nctx
    for chunk in range(chunks):
        for step in range(nctx):
            source = jnp.bitwise_xor(place, step)
            first = source * block_rows + chunk * chunk_rows
            held[pl.ds(pl.multiple_of(first, chunk_rows), chunk_rows), :] = pieces[
                chunk * nctx + step
            ][...]


def attend_kernel(nctx, heads, count, extra, block_rows, place, lows, ends, bounds, *refs):
    pieces = refs[:count]
    out, logs, held, turned, total, high, sums = refs[count + extra :]
    tile_q, tile_k = out.shape[0], turned.shape[2]
    width = heads * HEAD_DIM
    index = pl.program_id(0)

    @pl.when(index == 0)
    def _():
        load_pieces(place[0], pieces, nctx, held, block_rows)
        for tile in range(turned.shape[0]):
            turned[tile] = jnp.transpose(held[tile * tile_k : (tile + 1) * tile_k, 2 * width :])

    query_rows = pl.ds(pl.multiple_of(index * tile_q, tile_q), tile_q)
    queries = stack_heads(held[query_rows, :width] * jnp.asarray(HEAD_DIM**-0.5, BF16), heads)
    first_key = jnp.concatenate([bounds[0:1, :]] * heads, axis=1)
    last_key = jnp.concatenate([bounds[1:2, :]] * heads, axis=1)
    total[...] = jnp.zeros_like(total)
    high[...] = jnp.full_like(high, FLOOR)
    sums[...] = jnp.zeros_like(sums)

    def one(tile, _):
        start = tile * tile_k
        keys = held[pl.ds(pl.multiple_of(start, tile_k), tile_k), width : 2 * width]
        scores = lax.dot_general(
            keys, queries, (((1,), (1,)), ((), ())), preferred_element_type=F32
        )
        row = lax.broadcasted_iota(jnp.int32, scores.shape, 0)
        last = jnp.minimum(last_key, ends[tile] - 1) - start
        allowed = (row <= last) & (row >= first_key - start)
        scores = jnp.where(allowed, scores, NEGATIVE)
        highest = jnp.maximum(high[...], jnp.max(scores, axis=0, keepdims=True))
        raised = jnp.exp(scores - highest)
        shrink = jnp.exp(high[...] - highest)
        sums[...] = sums[...] * shrink + jnp.sum(raised, axis=0, keepdims=True)
        total[...] = total[...] * shrink + jnp.dot(
            turned[tile], raised.astype(BF16), preferred_element_type=F32
        )
        high[...] = highest
        return 0

    upper = (index * tile_q + tile_q - 1) // tile_k + 1
    lax.fori_loop(lows[index], upper, one, 0)
    found = sums[...] > 0.0
    safe = jnp.where(found, sums[...], 1.0)
    out[...] = fold_heads(
        total[...] * jnp.where(found, 1.0 / safe, 0.0), heads, tile_q
    ).astype(BF16)
    log_total = jnp.where(found, high[...] + jnp.log(safe), 0.0)
    for head in range(heads):
        logs[head : head + 1, :] = log_total[:, head * tile_q : (head + 1) * tile_q]


def attend(pieces, place, lows, ends, bounds, nctx, block_rows, *needed):
    total_rows = nctx * block_rows
    width = pieces[0].shape[1] // 3
    heads = width // HEAD_DIM
    steps = total_rows // TILE_Q
    grid_spec = pltpu.PrefetchScalarGridSpec(
        num_scalar_prefetch=3,
        grid=(steps,),
        in_specs=[pl.BlockSpec((2, TILE_Q), lambda i, *_: (0, i))]
        + [whole(piece.shape) for piece in pieces]
        + anywhere(len(needed)),
        out_specs=[
            pl.BlockSpec((TILE_Q, width), lambda i, *_: (i, 0)),
            pl.BlockSpec((heads, TILE_Q), lambda i, *_: (0, i)),
        ],
        scratch_shapes=[
            pltpu.VMEM((total_rows, 3 * width), BF16),
            pltpu.VMEM((total_rows // TILE_K, width, TILE_K), BF16),
            pltpu.VMEM((width, heads * TILE_Q), F32),
            pltpu.VMEM((1, heads * TILE_Q), F32),
            pltpu.VMEM((1, heads * TILE_Q), F32),
        ],
    )
    return pl.pallas_call(
        functools.partial(attend_kernel, nctx, heads, len(pieces), len(needed), block_rows),
        grid_spec=grid_spec,
        out_shape=[
            jax.ShapeDtypeStruct((total_rows, width), BF16),
            jax.ShapeDtypeStruct((heads, total_rows), F32),
        ],
        compiler_params=params(),
        cost_estimate=takes(2),
        name="attend",
    )(place, lows, ends, bounds, *pieces, *needed)


def attend_back_kernel(
    nctx, heads, count, extra, block_rows, place, lows, ends, bounds, logs, *refs
):
    pieces = refs[:count]
    grad, attended = refs[count : count + 2]
    out, held, turned, grad_keys, grad_values, grad_query = refs[count + 2 + extra :]
    tile_q, tile_k = grad.shape[0], turned.shape[2]
    width = heads * HEAD_DIM
    index = pl.program_id(0)
    scale = jnp.asarray(HEAD_DIM**-0.5, BF16)

    @pl.when(index == 0)
    def _():
        load_pieces(place[0], pieces, nctx, held, block_rows)
        for tile in range(turned.shape[0]):
            turned[tile] = jnp.transpose(
                held[tile * tile_k : (tile + 1) * tile_k, width : 2 * width]
            )
        grad_keys[...] = jnp.zeros_like(grad_keys)
        grad_values[...] = jnp.zeros_like(grad_values)

    query_rows = pl.ds(pl.multiple_of(index * tile_q, tile_q), tile_q)
    queries = stack_heads(held[query_rows, :width] * scale, heads)
    incoming = stack_heads(grad[...], heads)
    product = jnp.transpose(grad[...].astype(F32) * attended[...].astype(F32))
    centre = jnp.concatenate(
        [
            jnp.sum(product[head * HEAD_DIM : (head + 1) * HEAD_DIM, :], axis=0, keepdims=True)
            for head in range(heads)
        ],
        axis=1,
    )
    first_key = jnp.concatenate([bounds[0:1, :]] * heads, axis=1)
    last_key = jnp.concatenate([bounds[1:2, :]] * heads, axis=1)
    log_total = jnp.concatenate([logs[head : head + 1, :] for head in range(heads)], axis=1)
    grad_query[...] = jnp.zeros_like(grad_query)

    def one(tile, _):
        start = tile * tile_k
        key_rows = pl.ds(pl.multiple_of(start, tile_k), tile_k)
        scores = lax.dot_general(
            held[key_rows, width : 2 * width],
            queries,
            (((1,), (1,)), ((), ())),
            preferred_element_type=F32,
        )
        row = lax.broadcasted_iota(jnp.int32, scores.shape, 0)
        last = jnp.minimum(last_key, ends[tile] - 1) - start
        allowed = (row <= last) & (row >= first_key - start)
        chance = jnp.exp(jnp.where(allowed, scores - log_total, NEGATIVE))
        grad_chance = lax.dot_general(
            held[key_rows, 2 * width :],
            incoming,
            (((1,), (1,)), ((), ())),
            preferred_element_type=F32,
        )
        grad_scores = (chance * (grad_chance - centre)).astype(BF16)
        grad_values[key_rows, :] += jnp.dot(
            chance.astype(BF16), incoming, preferred_element_type=F32
        )
        grad_keys[key_rows, :] += jnp.dot(grad_scores, queries, preferred_element_type=F32)
        grad_query[...] += jnp.dot(turned[tile], grad_scores, preferred_element_type=F32)
        return 0

    upper = (index * tile_q + tile_q - 1) // tile_k + 1
    lax.fori_loop(lows[index], upper, one, 0)
    out[query_rows, :width] = (
        fold_heads(grad_query[...], heads, tile_q) * HEAD_DIM**-0.5
    ).astype(BF16)

    @pl.when(index == pl.num_programs(0) - 1)
    def _():
        out[:, width : 2 * width] = grad_keys[...].astype(BF16)
        out[:, 2 * width :] = grad_values[...].astype(BF16)


def attend_back(
    pieces, place, lows, ends, bounds, logs, grad, attended, nctx, block_rows, *needed
):
    total_rows, width = grad.shape
    heads = width // HEAD_DIM
    steps = total_rows // TILE_Q
    grid_spec = pltpu.PrefetchScalarGridSpec(
        num_scalar_prefetch=3,
        grid=(steps,),
        in_specs=[
            pl.BlockSpec((2, TILE_Q), lambda i, *_: (0, i)),
            pl.BlockSpec((heads, TILE_Q), lambda i, *_: (0, i)),
        ]
        + [whole(piece.shape) for piece in pieces]
        + [pl.BlockSpec((TILE_Q, width), lambda i, *_: (i, 0))] * 2
        + anywhere(len(needed)),
        out_specs=whole((total_rows, 3 * width)),
        scratch_shapes=[
            pltpu.VMEM((total_rows, 3 * width), BF16),
            pltpu.VMEM((total_rows // TILE_K, width, TILE_K), BF16),
            pltpu.VMEM((total_rows, width), F32),
            pltpu.VMEM((total_rows, width), F32),
            pltpu.VMEM((width, heads * TILE_Q), F32),
        ],
    )
    return pl.pallas_call(
        functools.partial(attend_back_kernel, nctx, heads, len(pieces), len(needed), block_rows),
        grid_spec=grid_spec,
        out_shape=jax.ShapeDtypeStruct((total_rows, 3 * width), BF16),
        compiler_params=params(),
        cost_estimate=takes(4),
        name="attend_back",
    )(place, lows, ends, bounds, logs, *pieces, grad, attended, *needed)


def mix_kernel(nctx, nweights, place, heads_in, *refs):
    weights = refs[:nweights]
    source, gain, bias, returned, mixed, *lows = refs[nweights:]
    rows, depth = mixed.shape
    step = pl.program_id(0)
    left = jnp.concatenate([heads_in[c, 0] for c in range(nctx)], axis=1)
    returned[...] = left

    @pl.when(step == 0)
    def _():
        mixed[...] = source[...].astype(F32)

    for weight, block, columns in every(place, weights, depth):
        mixed[:, columns] += dot(left, weight[block])

    @pl.when(step == pl.num_programs(0) - 1)
    def _():
        values = mixed[...]
        values = values - jnp.mean(values, axis=1, keepdims=True)
        scaling = lax.rsqrt(jnp.mean(values * values, axis=1, keepdims=True) + EPSILON)
        values = (values * scaling * gain[...] + bias[...]).astype(BF16)
        part_rows = lows[0].shape[0]
        for part, low in enumerate(lows):
            low[...] = values[part * part_rows : (part + 1) * part_rows]


def mix(heads_in, weights, full, gain, bias, place, parts):
    nctx, tp, rows, piece = heads_in.shape
    depth = full.shape[1]
    head_width = nctx * piece
    grid_spec = pltpu.PrefetchScalarGridSpec(
        num_scalar_prefetch=1,
        grid=(tp,),
        in_specs=[pl.BlockSpec((nctx, 1, rows, piece), lambda k, s: (0, k, 0, 0))]
        + [
            pl.BlockSpec((w.shape[0], head_width, w.shape[2]), lambda k, s: (0, k, 0))
            for w in weights
        ]
        + [
            pl.BlockSpec((rows, depth), lambda k, s: (s[0], 0)),
            whole((1, depth)),
            whole((1, depth)),
        ],
        out_specs=[
            pl.BlockSpec((rows, head_width), lambda k, s: (0, k)),
            whole((rows, depth)),
        ]
        + [whole((rows // parts, depth))] * parts,
    )
    return pl.pallas_call(
        functools.partial(mix_kernel, nctx, len(weights)),
        grid_spec=grid_spec,
        out_shape=[
            jax.ShapeDtypeStruct((rows, tp * head_width), BF16),
            jax.ShapeDtypeStruct((rows, depth), F32),
        ]
        + [jax.ShapeDtypeStruct((rows // parts, depth), BF16)] * parts,
        compiler_params=params(),
        cost_estimate=takes(5),
        name="mix",
    )(place, heads_in, *weights, full, gain, bias)


def feed_kernel(cuts, parts, place, *refs):
    lows, cot, sources = refs[:parts], refs[parts], refs[parts + 1 : parts + 4]
    kept, hidden, grad_gate, grad_up = refs[-8 - parts : -4 - parts]
    partials = refs[-4 - parts : -4]
    held, sems = refs[-4:-1], refs[-1]

    def copies(index):
        first, size = cuts[index]
        found = []
        for which in range(3):
            if which < 2:
                at = (slice(None), pl.ds(first, size))
            else:
                at = (pl.ds(first, size), slice(None))
            found.append(
                pltpu.make_async_copy(
                    sources[which].at[at], held[which].at[at], sems.at[index * 3 + which]
                )
            )
        return found

    for index in range(len(cuts)):
        for copy in copies(index):
            copy.start()
    low = kept
    rows = lows[0].shape[0]
    for part in range(parts):
        kept[part * rows : (part + 1) * rows] = lows[part][...]
    gate_weight, up_weight, down_weight = held
    for index, (first, size) in enumerate(cuts):
        for copy in copies(index):
            copy.wait()
        at = slice(first, first + size)
        gate = dot(low[...], gate_weight[:, at])
        up = dot(low[...], up_weight[:, at])
        sigma = 1.0 / (1.0 + jnp.exp(-gate))
        active = gate * sigma
        hidden[:, at] = (active * up).astype(BF16)
        grad = dot_turned(cot[...], down_weight[at, :])
        grad_gate[:, at] = (grad * up * sigma * (1.0 + gate * (1.0 - sigma))).astype(BF16)
        grad_up[:, at] = (grad * active).astype(BF16)
    product = dot_turned(grad_gate[...], gate_weight[...])
    product = product + dot_turned(grad_up[...], up_weight[...])
    for part in range(parts):
        partials[part][...] = product[part * rows : (part + 1) * rows].astype(BF16)


def feed(lows, cot, step, tp, gate, up, down_weight, place, held, *needed):
    parts = len(lows)
    part_rows, depth = lows[0].shape
    rows = parts * part_rows
    hidden = gate.shape[1]
    cuts = []
    while sum(size for _, size in cuts) < hidden:
        first = sum(size for _, size in cuts)
        cuts.append((first, min(512, hidden - first)))
    by_owner = lambda columns: pl.BlockSpec(
        (rows, columns), lambda i, s: (lax.rem(s[0] - step + tp, tp), 0)
    )
    grid_spec = pltpu.PrefetchScalarGridSpec(
        num_scalar_prefetch=1,
        grid=(1,),
        in_specs=[whole((part_rows, depth))] * parts
        + [by_owner(depth)]
        + anywhere(3 + len(held) + len(needed)),
        out_specs=[by_owner(depth)] + [by_owner(hidden)] * 3 + [whole((part_rows, depth))] * parts,
        scratch_shapes=[pltpu.VMEM(w.shape, BF16) for w in (gate, up, down_weight)]
        + [pltpu.SemaphoreType.DMA((3 * len(cuts),))],
    )
    return pl.pallas_call(
        functools.partial(feed_kernel, tuple(cuts), parts),
        grid_spec=grid_spec,
        out_shape=[jax.ShapeDtypeStruct((tp * rows, depth), BF16)]
        + [jax.ShapeDtypeStruct((tp * rows, hidden), BF16)] * 3
        + [jax.ShapeDtypeStruct((part_rows, depth), BF16)] * parts,
        input_output_aliases={5 + parts + index: index for index in range(len(held))},
        compiler_params=params(),
        cost_estimate=takes(8),
        name="feed",
    )(place, *lows, cot, gate, up, down_weight, *held, *needed)


def down(hidden, mixed, weight, place, *needed):
    rows, depth = mixed.shape
    tp = hidden.shape[0] // rows
    inner = hidden.shape[1]

    def kernel(place, left, mixed, weight, *refs):
        out, spare = refs[-2:]
        spare[...] = dot(left[...], weight[...])

        @pl.when(pl.program_id(0) == place[0])
        def _():
            spare[...] += mixed[...]

        out[...] = spare[...].astype(BF16)

    grid_spec = pltpu.PrefetchScalarGridSpec(
        num_scalar_prefetch=1,
        grid=(tp,),
        in_specs=[
            pl.BlockSpec((rows, inner), lambda k, s: (k, 0)),
            whole((rows, depth)),
            whole((inner, depth)),
        ]
        + anywhere(len(needed)),
        out_specs=pl.BlockSpec((rows, depth), lambda k, s: (k, 0)),
        scratch_shapes=[pltpu.VMEM((rows, depth), F32)],
    )
    return pl.pallas_call(
        kernel,
        grid_spec=grid_spec,
        out_shape=jax.ShapeDtypeStruct((tp * rows, depth), BF16),
        compiler_params=params(),
        cost_estimate=takes(7),
        name="down",
    )(place, hidden, mixed, weight, *needed)


def blame(left, right, which, pick_left, unit, arrived=None, *needed):
    rows = left.shape[0]
    picked = (left if pick_left else right).shape[1] // unit // 2
    other = (right if pick_left else left).shape[1]
    chosen = pl.BlockSpec((rows, unit), lambda j, s: (0, 2 * j + s[0]))
    kept = whole((rows, other))
    if pick_left:
        shape = (picked * unit, other)
        target = pl.BlockSpec((unit, other), lambda j, s: (j, 0))
    else:
        shape = (other, picked * unit)
        target = pl.BlockSpec((other, unit), lambda j, s: (0, j))
    extra = [] if arrived is None else [arrived]

    def kernel(which, left, right, *refs):
        product = lax.dot_general(
            left[...], right[...], (((0,), (0,)), ((), ())), preferred_element_type=F32
        )
        if extra:
            product = product + refs[0][...].astype(F32)
        refs[-1][...] = product.astype(BF16)

    grid_spec = pltpu.PrefetchScalarGridSpec(
        num_scalar_prefetch=1,
        grid=(picked,),
        in_specs=([chosen, kept] if pick_left else [kept, chosen])
        + [target] * len(extra)
        + anywhere(len(needed)),
        out_specs=target,
    )
    return pl.pallas_call(
        kernel,
        grid_spec=grid_spec,
        out_shape=jax.ShapeDtypeStruct(shape, BF16),
        compiler_params=params(),
        cost_estimate=takes(3),
        name="blame",
    )(which, left, right, *extra, *needed)


def turn_kernel(nctx, nweights, count, parts, place, *refs):
    arrived, own = refs[:parts], refs[parts : 2 * parts]
    mixed, cot, gain = refs[2 * parts : 2 * parts + 3]
    refs = refs[2 * parts + 3 :]
    weights = refs[:nweights]
    out, grad_mixed, grad_low, gain_grad, shift_grad, moved = refs[nweights + count :]
    rows, depth = mixed.shape
    piece = out.shape[3]

    @pl.when(pl.program_id(0) == 0)
    def _():
        incoming = jnp.concatenate(
            [there[...].astype(F32) + here[...].astype(F32) for there, here in zip(arrived, own)]
        )
        values = mixed[...]
        values = values - jnp.mean(values, axis=1, keepdims=True)
        scaling = lax.rsqrt(jnp.mean(values * values, axis=1, keepdims=True) + EPSILON)
        normed = values * scaling
        shift_grad[...] = jnp.sum(incoming, axis=0, keepdims=True)
        gain_grad[...] = jnp.sum(incoming * normed, axis=0, keepdims=True)
        scaled = incoming * gain[...]
        total = cot[...].astype(F32) + scaling * (
            scaled
            - jnp.mean(scaled, axis=1, keepdims=True)
            - normed * jnp.mean(scaled * normed, axis=1, keepdims=True)
        )
        grad_mixed[...] = total
        grad_low[...] = total.astype(BF16)
        first = 0
        for weight, block, columns in every(place, weights, depth):
            size = weight.shape[2]
            moved[:, first : first + size] = grad_low[:, columns]
            first += size

    product, first = 0.0, 0
    for weight in weights:
        for block in range(weight.shape[0]):
            size = weight.shape[2]
            product = product + dot_turned(moved[:, first : first + size], weight[block])
            first += size
    for c in range(nctx):
        out[c, 0] = product[:, c * piece : (c + 1) * piece].astype(BF16)


def turn(arrived, own, mixed, cot, gain, weights, place, nctx, tp, *needed):
    rows, depth = mixed.shape
    parts = len(arrived)
    head_width = weights[0].shape[1] // tp
    piece = head_width // nctx
    grid_spec = pltpu.PrefetchScalarGridSpec(
        num_scalar_prefetch=1,
        grid=(tp,),
        in_specs=[whole((rows // parts, depth))] * (2 * parts)
        + [whole((rows, depth))]
        + [pl.BlockSpec((rows, depth), lambda k, s: (s[0], 0)), whole((1, depth))]
        + [
            pl.BlockSpec((w.shape[0], head_width, w.shape[2]), lambda k, s: (0, k, 0))
            for w in weights
        ]
        + anywhere(len(needed)),
        out_specs=[
            pl.BlockSpec((nctx, 1, rows, piece), lambda k, s: (0, k, 0, 0)),
            whole((rows, depth)),
            whole((rows, depth)),
            whole((1, depth)),
            whole((1, depth)),
        ],
        scratch_shapes=[pltpu.VMEM((rows, depth), BF16)],
    )
    return pl.pallas_call(
        functools.partial(turn_kernel, nctx, len(weights), len(needed), parts),
        grid_spec=grid_spec,
        out_shape=[
            jax.ShapeDtypeStruct((nctx, tp, rows, piece), BF16),
            jax.ShapeDtypeStruct((rows, depth), F32),
            jax.ShapeDtypeStruct((rows, depth), BF16),
            jax.ShapeDtypeStruct((1, depth), F32),
            jax.ShapeDtypeStruct((1, depth), F32),
        ],
        compiler_params=params(),
        cost_estimate=takes(6),
        name="turn",
    )(place, *arrived, *own, mixed, cot, gain, *weights, *needed)


def finish_kernel(nctx, chunk, place, *refs):
    pieces = refs[:nctx]
    cosine, sine_up, sine_down, full, extra, gain = refs[nctx : nctx + 6]
    weight, out, low, bias_grad, gain_grad, shift_grad, spare = refs[nctx + 6 :]
    rows, wide = pieces[0].shape
    piece = wide // 3
    tp, width = out.shape[0], out.shape[2]
    depth = tp * width
    strip = spare.shape[0]
    extra_rows = extra.shape[0]

    @pl.when(pl.program_id(0) == 0)
    def _():
        bias_grad[...] = jnp.zeros_like(bias_grad)
        gain_grad[...] = jnp.zeros_like(gain_grad)
        shift_grad[...] = jnp.zeros_like(shift_grad)

    for step in range(nctx):
        source = jnp.bitwise_xor(place[1], step)
        for part in range(3):
            values = pieces[step][:, part * piece : (part + 1) * piece].astype(F32)
            if part < 2:
                values = (
                    values * cosine[...]
                    - pltpu.roll(values, piece - ROT // 2, 1) * sine_up[...]
                    - pltpu.roll(values, ROT // 2, 1) * sine_down[...]
                )
            columns = pl.ds(pl.multiple_of(source * wide + part * piece, piece), piece)
            bias_grad[:, columns] += jnp.sum(values, axis=0, keepdims=True)
            low[:, columns] = values.astype(BF16)

    incoming = dot_turned(low[...], weight[...])
    source = full[...].astype(F32)
    source = source - jnp.mean(source, axis=1, keepdims=True)
    scaling = lax.rsqrt(jnp.mean(source * source, axis=1, keepdims=True) + EPSILON)
    normed = source * scaling
    shift_grad[...] += jnp.sum(incoming, axis=0, keepdims=True)
    gain_grad[...] += jnp.sum(incoming * normed, axis=0, keepdims=True)
    scaled = incoming * gain[...]
    spare[...] = scaling * (
        scaled
        - jnp.mean(scaled, axis=1, keepdims=True)
        - normed * jnp.mean(scaled * normed, axis=1, keepdims=True)
    )
    first = chunk * pl.num_programs(0) * strip + pl.program_id(0) * strip
    wanted = place[0] * extra_rows

    if strip <= extra_rows:

        @pl.when((first >= wanted) & (first < wanted + extra_rows))
        def _():
            spare[...] += extra[pl.ds(pl.multiple_of(first - wanted, strip), strip), :]

    else:

        @pl.when((wanted >= first) & (wanted < first + strip))
        def _():
            spare[pl.ds(pl.multiple_of(wanted - first, extra_rows), extra_rows), :] += extra[...]

    for block in range(tp):
        out[block] = spare[:, block * width : (block + 1) * width].astype(BF16)


def finish(pieces, place, tables, full, extra, gain, weight, chunk, tp):
    rows, wide = pieces[0].shape
    depth = full.shape[1]
    total = weight.shape[1]
    strip = 256
    steps = rows // strip
    width = depth // tp
    nctx = len(pieces)
    by_rows = lambda columns: pl.BlockSpec((strip, columns), lambda i, s: (i, 0))
    grid_spec = pltpu.PrefetchScalarGridSpec(
        num_scalar_prefetch=1,
        grid=(steps,),
        in_specs=[by_rows(wide)] * nctx
        + [by_rows(2 * HEAD_DIM)] * 3
        + [
            pl.BlockSpec((strip, depth), lambda i, s: (i + chunk * steps, 0)),
            whole(extra.shape),
            whole((1, depth)),
        ]
        + [whole(weight.shape)],
        out_specs=[
            pl.BlockSpec((tp, strip, width), lambda i, s: (0, i, 0)),
            by_rows(total),
            whole((1, total)),
            whole((1, depth)),
            whole((1, depth)),
        ],
        scratch_shapes=[pltpu.VMEM((strip, depth), F32)],
    )
    return pl.pallas_call(
        functools.partial(finish_kernel, nctx, chunk),
        grid_spec=grid_spec,
        out_shape=[
            jax.ShapeDtypeStruct((tp, rows, width), BF16),
            jax.ShapeDtypeStruct((rows, total), BF16),
            jax.ShapeDtypeStruct((1, total), F32),
            jax.ShapeDtypeStruct((1, depth), F32),
            jax.ShapeDtypeStruct((1, depth), F32),
        ],
        compiler_params=params(),
        cost_estimate=takes(7),
        name="finish",
    )(place, *pieces, *tables, full, extra, gain, weight)


def join(blocks, place, *needed):
    tp = len(blocks)
    rows, width = blocks[0].shape
    strip = rows // tp
    count = len(needed)

    def kernel(place, *refs):
        for step in range(tp):
            owner = lax.rem(place[0] - step + tp, tp)
            refs[-1][:, pl.ds(pl.multiple_of(owner * width, width), width)] = refs[step][...]

    grid_spec = pltpu.PrefetchScalarGridSpec(
        num_scalar_prefetch=1,
        grid=(tp,),
        in_specs=[pl.BlockSpec((strip, width), lambda i, s: (i, 0))] * tp + anywhere(count),
        out_specs=pl.BlockSpec((strip, tp * width), lambda i, s: (i, 0)),
    )
    return pl.pallas_call(
        kernel,
        grid_spec=grid_spec,
        out_shape=jax.ShapeDtypeStruct((rows, tp * width), BF16),
        compiler_params=params(),
        cost_estimate=takes(3),
        name="join",
    )(place, *blocks, *needed)


def contract_rows(left, right):
    return lax.dot_general(left, right, (((0,), (0,)), ((), ())), preferred_element_type=F32)


def pick(stack, index):
    return lax.dynamic_index_in_dim(stack, index, 0, keepdims=False)


def shards(
    nfsdp,
    nctx,
    tp,
    inputs,
    cotangent,
    first_gain,
    first_bias,
    qkv_weight,
    qkv_bias,
    out_weight,
    second_gain,
    second_bias,
    gate_weight,
    up_weight,
    down_weight,
    lengths,
    fill_counts,
):
    data = ("fsdp", "ctx")
    ndata = nfsdp * nctx
    block_rows, width = inputs.shape
    depth = tp * width
    half_depth = depth // 2
    unit = depth // ndata
    tensor_index = lax.axis_index("tp").astype(jnp.int32)
    context_index = lax.axis_index("ctx").astype(jnp.int32)
    fsdp_index = lax.axis_index("fsdp").astype(jnp.int32)
    part_rows = block_rows // tp
    chunk_rows = block_rows // CHUNKS
    head_width = qkv_weight.shape[2]
    piece = head_width // nctx
    wide = 3 * piece

    square = nfsdp == 2 and nctx == 4 and unit % 128 == 0
    place = jnp.stack([tensor_index, context_index, fsdp_index])

    def shift(value, step):
        return lax.ppermute(value, "tp", [(i, (i + step) % tp) for i in range(tp)])

    def swap(value, step):
        return lax.ppermute(value, "ctx", [(i, i ^ step) for i in range(nctx)])

    def cross(value):
        return lax.ppermute(value, "fsdp", [(0, 1), (1, 0)])

    def gather(value):
        rows = value.shape[0] // 2
        first, second = value[:rows], value[rows:]
        first_x, second_y = cross(first), swap(second, 2)
        first_y = swap(jnp.stack([first, first_x]), 2)
        second_x = cross(jnp.stack([second, second_y]))
        mine = jnp.stack(
            [
                jnp.concatenate([first, second]),
                jnp.concatenate([first_y[0], second_y]),
                jnp.concatenate([first_x, second_x[0]]),
                jnp.concatenate([first_y[1], second_x[1]]),
            ]
        )
        return (mine, swap(mine, 1))

    core_index = context_index % 2
    groups = [list(range(0, ndata, 2)), list(range(1, ndata, 2))]
    own_half, other_half = core_index[None], (1 - core_index)[None]

    def presum(left, right, pick_left, first_needs=(), second_needs=()):
        first = blame(left, right, other_half, pick_left, unit, None, *first_needs)
        return first, blame(
            left, right, own_half, pick_left, unit, swap(first, 1), *second_needs
        )

    def scatter_half(value, axis):
        return lax.psum_scatter(
            value, data, scatter_dimension=axis, tiled=True, axis_index_groups=groups
        )

    def scatter_whole(left, right, axis):
        return lax.psum_scatter(
            contract_rows(left, right).astype(BF16), data, scatter_dimension=axis, tiled=True
        )

    def total(left, right):
        return (left.astype(F32) + right.astype(F32)).astype(BF16)

    def scatter_rows(half):
        half = half.reshape(2, 2, unit, half.shape[1])
        first, second = half[:, :, : unit // 2], half[:, :, unit // 2 :]
        far, near = 1 - fsdp_index, fsdp_index
        up, here = 1 - context_index // 2, context_index // 2
        first = total(pick(first, near), cross(pick(first, far)))
        second = jnp.swapaxes(second, 0, 1)
        second = total(pick(second, here), swap(pick(second, up), 2))
        first = total(pick(first, here), swap(pick(first, up), 2))
        second = total(pick(second, near), cross(pick(second, far)))
        return jnp.concatenate([first, second])

    owners = [(tensor_index - step + tp) % tp for step in range(tp)]

    own_qkv = (
        qkv_weight.reshape(-1, 3, nctx, piece).transpose(0, 2, 1, 3).reshape(-1, 3 * head_width)
    )
    full_qkv = lax.all_gather(own_qkv, data, axis=0, tiled=True)
    full_gate = lax.all_gather(gate_weight, data, axis=0, tiled=True)
    full_up = lax.all_gather(up_weight, data, axis=0, tiled=True)
    full_down = lax.all_gather(down_weight, data, axis=1, tiled=True)

    validity, position, first_key, last_key = layout(lengths[0], fill_counts[0], block_rows)
    own_position = lax.dynamic_slice_in_dim(position, context_index * block_rows, block_rows, 0)
    tables = rotary_tables(own_position)
    bounds = jnp.stack([first_key, last_key])
    tile_first = first_key[::TILE_Q]
    tile_count = tile_first.shape[0]
    lows = jnp.where(validity[::TILE_Q], tile_first // TILE_K, tile_count * TILE_Q).astype(jnp.int32)
    key_block = jnp.arange(0, nctx * block_rows, TILE_K, dtype=jnp.int32) // block_rows
    ends = (
        key_block * block_rows
        + jnp.sum(
            jnp.where(
                key_block[:, None] == jnp.arange(nctx, dtype=jnp.int32)[None, :],
                fill_counts[0][None, :],
                0,
            ),
            axis=1,
        )
    ).astype(jnp.int32)

    flat_bias = qkv_bias.reshape(3, nctx, piece).transpose(1, 0, 2).reshape(1, -1)
    gain_one, bias_one = first_gain[None], first_bias[None]
    gain_two, bias_two = second_gain[None], second_bias[None]

    rings = [[inputs[c * chunk_rows : (c + 1) * chunk_rows]] for c in range(CHUNKS)]
    for chunk in range(CHUNKS):
        for _ in range(tp - 1):
            rings[chunk].append(shift(rings[chunk][-1], 1))
    own_out = tie(out_weight, rings[0][1 % tp])
    stack = jnp.zeros((tp,) + out_weight.shape, BF16)
    stack = lax.dynamic_update_index_in_dim(stack, own_out, tensor_index, 0)
    for step in range(1, tp):
        stack = lax.dynamic_update_index_in_dim(stack, shift(own_out, step), owners[step], 0)
    out_blocks = (lax.all_gather(stack.reshape(depth, -1), data, axis=1, tiled=True)[None],)
    lows_one, fulls, pieces, chunk_tables = [], [], [], []
    for chunk in range(CHUNKS):
        at = slice(chunk * chunk_rows, (chunk + 1) * chunk_rows)
        chunk_tables.append([table[at] for table in tables])
        low, full, outgoing = project(
            rings[chunk],
            place,
            gain_one,
            bias_one,
            full_qkv,
            flat_bias,
            chunk_tables[chunk],
            nctx,
        )
        lows_one.append(low)
        fulls.append(full)
        pieces.append(pick(outgoing, context_index))
        for step in range(1, nctx):
            pieces.append(swap(pick(outgoing, context_index ^ step), step))
    full = jnp.concatenate(fulls, axis=0)

    cot_blocks = [tie(cotangent, *[blocks[-1] for blocks in rings])]
    for step in range(1, tp):
        cot_blocks.append(shift(cot_blocks[0], step))

    attended, logs = attend(
        pieces, place[1:2], lows, ends, bounds, nctx, block_rows, *cot_blocks[1:2]
    )
    outgoing = tie(attended, *cot_blocks[2:])
    full_cot = join(cot_blocks, place, outgoing)
    arrived = lax.all_to_all(
        outgoing.reshape(nctx * tp, part_rows, piece),
        ("ctx", "tp"),
        split_axis=0,
        concat_axis=0,
        tiled=True,
    )
    returned, mixed, *second_low = mix(
        arrived.reshape(nctx, tp, part_rows, piece),
        out_blocks,
        full,
        gain_two,
        bias_two,
        place,
        HALVES,
    )

    arrived, held, partials, travelling = second_low, [], [], None
    for step in range(tp):
        coming = [shift(value, 1) for value in arrived] if step < tp - 1 else None
        needed = travelling if step == tp - 1 and step > 2 else []
        *held, first, second = feed(
            arrived, full_cot, step, tp, full_gate, full_up, full_down, place, held, *needed
        )
        partials.append([first, second])
        if step == 1 % tp:
            travelling = partials[step]
        elif 1 < step < tp - 1:
            travelling = [
                total(shift(value, 1), own) for value, own in zip(travelling, partials[step])
            ]
        if step == 0 and coming is not None:
            coming = [tie(value, partials[0][0]) for value in coming]
        arrived = coming
    all_second, hidden, all_gate, all_up = held

    if square:
        first, half_gate = presum(all_second, all_gate, True)
        total_gate = scatter_half(half_gate, 0)
    else:
        first, total_gate = all_gate, scatter_whole(all_second, all_gate, 0)
    if tp > 2:
        travelling = [
            add(shift(value, 1), own, first) for value, own in zip(travelling, partials[-1])
        ]
    needed = []
    if square:
        first, half_up = presum(all_second, all_up, True, travelling)
        total_up = scatter_half(half_up, 0)
        needed = [half_gate, half_up]
    else:
        total_up = scatter_whole(all_second, all_up, 0)

    grad_heads, grad_mixed, mixed_low, gain_grad_two, shift_grad_two = turn(
        [shift(value, 1) for value in travelling],
        partials[0],
        mixed,
        full_cot,
        gain_two,
        out_blocks,
        place,
        nctx,
        tp,
        *needed,
    )
    grad_heads = lax.all_to_all(
        grad_heads.reshape(nctx * tp, part_rows, piece),
        ("ctx", "tp"),
        split_axis=0,
        concat_axis=0,
        tiled=True,
    ).reshape(nctx * block_rows, piece)

    feedforward = down(hidden, mixed, full_down, place, grad_mixed)
    layer_out = lax.psum_scatter(feedforward, "tp", scatter_dimension=1, tiled=True)

    if square:
        first, half_out = presum(mixed_low, returned, True)
        needed = [feedforward, half_out]
        total_out = scatter_rows(half_out)
    else:
        needed = [feedforward]
        total_out = scatter_whole(mixed_low, returned, 0)
    out_parts = jnp.swapaxes(total_out.reshape(-1, tp, head_width), 0, 1)
    total_out = pick(out_parts, tensor_index).astype(F32)
    for step in range(1, tp):
        total_out = total_out + shift(pick(out_parts, (tensor_index + step) % tp), step).astype(F32)
    total_out = total_out.T

    grad_grouped = attend_back(
        pieces, place[1:2], lows, ends, bounds, logs, grad_heads, attended, nctx, block_rows, *needed
    )
    if square:
        first, half_down = presum(hidden, full_cot, False, [grad_grouped])
        total_down = scatter_half(half_down, 1)
    else:
        total_down = scatter_whole(hidden, full_cot, 1)
    grad_grouped = grad_grouped.reshape(nctx, CHUNKS, chunk_rows, wide)
    grad_lows, bias_grads, gain_grads, shift_grads, grad_rows = [], [], [], [], []
    ring_steps = []
    for chunk in range(CHUNKS):
        outgoing = grad_grouped[:, chunk]
        arrived = [pick(outgoing, context_index)]
        for step in range(1, nctx):
            arrived.append(swap(pick(outgoing, context_index ^ step), step))
        partial, low, bias_grad, gain_grad, shift_grad = finish(
            arrived,
            place,
            chunk_tables[chunk],
            full,
            grad_mixed,
            gain_one,
            full_qkv,
            chunk,
            tp,
        )
        grad_lows.append(low)
        bias_grads.append(bias_grad)
        gain_grads.append(gain_grad)
        shift_grads.append(shift_grad)
        travelling = pick(partial, owners[1 % tp])
        for step in range(1, tp):
            travelling = total(shift(travelling, 1), pick(partial, owners[(step + 1) % tp]))
            if step == 1:
                ring_steps.append(travelling)
        grad_rows.append(travelling)
    grad_inputs = jnp.concatenate(grad_rows, axis=0)

    all_low, all_grad = jnp.concatenate(lows_one, axis=0), jnp.concatenate(grad_lows, axis=0)
    if square:
        first, half_qkv = presum(all_low, all_grad, True, ring_steps[:1], ring_steps[1:2])
        total_qkv = scatter_half(half_qkv, 0)
    else:
        total_qkv = scatter_whole(all_low, all_grad, 0)
    total_qkv = (
        total_qkv.astype(F32)
        .reshape(-1, nctx, 3, piece)
        .transpose(0, 2, 1, 3)
        .reshape(-1, 3, head_width)
    )

    def exchange(value, axis, size):
        step = 1
        while step < size:
            value = value + lax.ppermute(value, axis, [(i, i ^ step) for i in range(size)])
            step *= 2
        return value

    small = jnp.concatenate([sum(gain_grads), sum(shift_grads), gain_grad_two, shift_grad_two], axis=1)
    small = exchange(tie(small, *ring_steps), "tp", tp)
    small = jnp.concatenate([sum(bias_grads), small], axis=1)
    small = exchange(exchange(small, "ctx", nctx), "fsdp", nfsdp)
    bias_total, small = small[:, : 3 * head_width], small[:, 3 * head_width :]
    bias_total = bias_total.reshape(nctx, 3, piece).transpose(1, 0, 2).reshape(3, head_width)
    small = small.reshape(4, depth)
    return (
        layer_out,
        grad_inputs,
        small[0],
        small[1],
        total_qkv,
        bias_total,
        total_out,
        small[2],
        small[3],
        total_gate.astype(F32),
        total_up.astype(F32),
        total_down.astype(F32),
    )


def solution(mesh):
    data = ("fsdp", "ctx")
    by_rows = P(data, "tp")
    by_columns = P("tp", data)
    qkv = P(data, None, "tp")
    return jax.shard_map(
        functools.partial(shards, mesh.shape["fsdp"], mesh.shape["ctx"], mesh.shape["tp"]),
        mesh=mesh,
        in_specs=(
            by_rows,
            by_rows,
            P(),
            P(),
            qkv,
            P(None, "tp"),
            by_columns,
            P(),
            P(),
            by_rows,
            by_rows,
            by_columns,
            P("fsdp", None),
            P("fsdp", None),
        ),
        out_specs=(
            by_rows,
            by_rows,
            P(),
            P(),
            qkv,
            P(None, "tp"),
            by_columns,
            P(),
            P(),
            by_rows,
            by_rows,
            by_columns,
        ),
        check_vma=False,
    )
```

```python
import functools

import jax
import jax.numpy as jnp
from jax import lax
from jax.experimental import pallas as pl
from jax.experimental.pallas import tpu as pltpu
from jax.sharding import PartitionSpec as P

HEAD_DIM = 64
ROT = 16
EPSILON = 1e-05
NEGATIVE = -1e30
FLOOR = -1e20
VMEM_LIMIT = 56 * 1024 * 1024
TILE_Q = 512
TILE_K = 512
STRIP = 32
CHUNKS = 2
HALVES = 2

F32 = jnp.float32
BF16 = jnp.bfloat16


def layout(lengths, fill_counts, block_rows):
    blocks_count = fill_counts.shape[0]
    seq_count = lengths.shape[0]
    slot_index = jnp.arange(blocks_count * block_rows, dtype=jnp.int32)
    block_of = slot_index // block_rows
    within = slot_index - block_of * block_rows
    chooser = block_of[:, None] == jnp.arange(blocks_count, dtype=jnp.int32)[None, :]
    fill_here = jnp.sum(jnp.where(chooser, fill_counts[None, :], 0), axis=1)
    before = jnp.cumsum(fill_counts) - fill_counts
    before_here = jnp.sum(jnp.where(chooser, before[None, :], 0), axis=1)
    validity = within < fill_here
    used_index = before_here + within
    seq_ends = jnp.cumsum(lengths)
    sequence = jnp.sum((used_index[:, None] >= seq_ends[None, :]).astype(jnp.int32), axis=1)
    seq_starts = seq_ends - lengths
    picker = sequence[:, None] == jnp.arange(seq_count, dtype=jnp.int32)[None, :]
    start_here = jnp.sum(jnp.where(picker, seq_starts[None, :], 0), axis=1)
    after = before + fill_counts
    start_block = jnp.sum((seq_starts[:, None] >= after[None, :]).astype(jnp.int32), axis=1)
    start_block = jnp.minimum(start_block, blocks_count - 1)
    block_pick = start_block[:, None] == jnp.arange(blocks_count, dtype=jnp.int32)[None, :]
    start_before = jnp.sum(jnp.where(block_pick, before[None, :], 0), axis=1)
    start_slot = start_block * block_rows + seq_starts - start_before
    slot_here = jnp.sum(jnp.where(picker, start_slot[None, :], 0), axis=1)
    first_key = jnp.where(validity, slot_here, 0).astype(jnp.int32)
    last_key = jnp.where(validity, slot_index, -1).astype(jnp.int32)
    return (validity, used_index - start_here, first_key, last_key)


def rotary_tables(position):
    half = ROT // 2
    lane = jnp.arange(2 * HEAD_DIM, dtype=jnp.int32) % HEAD_DIM
    frequency = 10000.0 ** (-(2.0 * (lane % half).astype(F32)) / ROT)
    angles = position.astype(F32)[:, None] * frequency[None, :]
    cosine, sine = jnp.cos(angles), jnp.sin(angles)
    lane = lane[None, :]
    return (
        jnp.where(lane < ROT, cosine, 1.0),
        jnp.where(lane < half, -sine, 0.0),
        jnp.where((lane >= half) & (lane < ROT), sine, 0.0),
    )


def params(**extra):
    return pltpu.CompilerParams(vmem_limit_bytes=VMEM_LIMIT, **extra)


def takes(microseconds):
    return pl.CostEstimate(
        flops=int(microseconds * 1e8), bytes_accessed=0, transcendentals=0
    )


def whole(shape):
    return pl.BlockSpec(shape, lambda *_: (0,) * len(shape))


def anywhere(count):
    return [pl.BlockSpec(memory_space=pl.ANY)] * count


def dot(left, right):
    return jnp.dot(left, right, preferred_element_type=F32)


def dot_turned(left, right):
    return lax.dot_general(left, right, (((1,), (1,)), ((), ())), preferred_element_type=F32)


def tie(value, *needed):
    def kernel(*refs):
        del refs

    return pl.pallas_call(
        kernel,
        in_specs=anywhere(1 + len(needed)),
        out_specs=pl.BlockSpec(memory_space=pl.ANY),
        out_shape=jax.ShapeDtypeStruct(value.shape, value.dtype),
        input_output_aliases={0: 0},
        name="tie",
    )(value, *needed)


def add_kernel(left, right, *refs):
    refs[-1][...] = (left[...].astype(F32) + right[...].astype(F32)).astype(BF16)


def add(left, right, *needed):
    rows, columns = left.shape
    strip = min(rows, 128)
    block = pl.BlockSpec((strip, columns), lambda i: (i, 0))
    return pl.pallas_call(
        add_kernel,
        grid=(rows // strip,),
        in_specs=[block, block] + anywhere(len(needed)),
        out_specs=block,
        out_shape=jax.ShapeDtypeStruct(left.shape, BF16),
        compiler_params=params(),
        cost_estimate=takes(1),
        name="ring_add",
    )(left, right, *needed)


def project_kernel(tp, per, place, *refs):
    blocks = refs[:tp]
    gain, bias, weight, weight_bias, cosine, sine_up, sine_down = refs[tp : tp + 7]
    low, full, *outs = refs[tp + 7 :]
    rows, width = low.shape[0], blocks[0].shape[1]
    depth = tp * width
    wide = outs[0].shape[1]
    piece = wide // 3
    step = pl.program_id(0)

    @pl.when(pl.program_id(0) == 0)
    def _():
        strip = 128
        for start in range(0, rows, strip):
            at = slice(start, start + strip)
            parts = [block[at, :].astype(F32) for block in blocks]
            centre = sum(jnp.sum(part, axis=1, keepdims=True) for part in parts) / depth
            parts = [part - centre for part in parts]
            spread = sum(jnp.sum(part * part, axis=1, keepdims=True) for part in parts) / depth
            scaling = lax.rsqrt(spread + EPSILON)
            for step in range(tp):
                owner = lax.rem(place[0] - step + tp, tp)
                columns = pl.ds(pl.multiple_of(owner * width, width), width)
                low[at, columns] = (
                    parts[step] * scaling * gain[:, columns] + bias[:, columns]
                ).astype(BF16)
                full[at, columns] = blocks[step][at, :]

    product = dot(low[...], weight[...]) + weight_bias[...]
    groups = []
    for group in range(per):
        parts = []
        for part in range(3):
            first = (group * 3 + part) * piece
            values = product[:, first : first + piece]
            if part < 2:
                values = (
                    values * cosine[...]
                    + pltpu.roll(values, piece - ROT // 2, 1) * sine_up[...]
                    + pltpu.roll(values, ROT // 2, 1) * sine_down[...]
                )
            parts.append(values.astype(BF16))
        groups.append(parts)
    flip = lax.rem(place[1], per)
    for way, out in enumerate(outs):
        for group in range(per):

            @pl.when((step == way // per) & (jnp.bitwise_xor(group, flip) == way % per))
            def _():
                for part in range(3):
                    out[:, part * piece : (part + 1) * piece] = groups[group][part]


def project(blocks, place, gain, bias, weight, weight_bias, tables, nctx):
    tp = len(blocks)
    rows, width = tables[0].shape[0], blocks[0].shape[1]
    depth = tp * width
    total = weight.shape[1]
    wide = total // nctx
    per = 2 if nctx % 2 == 0 else 1
    grid_spec = pltpu.PrefetchScalarGridSpec(
        num_scalar_prefetch=1,
        grid=(nctx // per,),
        in_specs=[whole((rows, width))] * tp
        + [whole((1, depth))] * 2
        + [
            pl.BlockSpec((depth, per * wide), lambda i, s: (0, jnp.bitwise_xor(i, s[1] // per))),
            pl.BlockSpec((1, per * wide), lambda i, s: (0, jnp.bitwise_xor(i, s[1] // per))),
        ]
        + [whole((rows, 2 * HEAD_DIM))] * 3,
        out_specs=[whole((rows, depth))] * 2 + [whole((rows, wide))] * nctx,
    )
    return pl.pallas_call(
        functools.partial(project_kernel, tp, per),
        grid_spec=grid_spec,
        out_shape=[
            jax.ShapeDtypeStruct((rows, depth), BF16),
            jax.ShapeDtypeStruct((rows, depth), BF16),
        ]
        + [jax.ShapeDtypeStruct((rows, wide), BF16)] * nctx,
        compiler_params=params(),
        cost_estimate=takes(20),
        name="project",
    )(place, *blocks, gain, bias, weight, weight_bias, *tables)


def stack_heads(tile, heads):
    lane = lax.broadcasted_iota(jnp.int32, tile.shape, 1) // HEAD_DIM
    return jnp.concatenate(
        [jnp.where(lane == head, tile, jnp.zeros_like(tile)) for head in range(heads)], axis=0
    )


def fold_heads(stacked, heads, columns):
    row = lax.broadcasted_iota(jnp.int32, (stacked.shape[0], columns), 0) // HEAD_DIM
    folded = jnp.zeros((stacked.shape[0], columns), F32)
    for head in range(heads):
        folded = folded + jnp.where(row == head, stacked[:, head * columns : (head + 1) * columns], 0.0)
    return jnp.transpose(folded)


def load_pieces(place, pieces, nctx, held, block_rows):
    chunk_rows = pieces[0].shape[0]
    chunks = len(pieces) // nctx
    for chunk in range(chunks):
        for step in range(nctx):
            source = jnp.bitwise_xor(place, step)
            first = source * block_rows + chunk * chunk_rows
            held[pl.ds(pl.multiple_of(first, chunk_rows), chunk_rows), :] = pieces[
                chunk * nctx + step
            ][...]


def attend_kernel(nctx, heads, count, extra, block_rows, place, lows, ends, bounds, *refs):
    pieces = refs[:count]
    out, logs, held, turned, total, high, sums, raw, chances = refs[count + extra :]
    tile_q, tile_k = out.shape[0], turned.shape[2]
    width = heads * HEAD_DIM
    index = pl.program_id(0)

    @pl.when(index == 0)
    def _():
        load_pieces(place[0], pieces, nctx, held, block_rows)
        for tile in range(turned.shape[0]):
            turned[tile] = jnp.transpose(held[tile * tile_k : (tile + 1) * tile_k, 2 * width :])

    query_rows = pl.ds(pl.multiple_of(index * tile_q, tile_q), tile_q)
    queries = stack_heads(held[query_rows, :width] * jnp.asarray(HEAD_DIM**-0.5, BF16), heads)
    first_key = jnp.concatenate([bounds[0:1, :]] * heads, axis=1)
    last_key = jnp.concatenate([bounds[1:2, :]] * heads, axis=1)
    total[...] = jnp.zeros_like(total)
    high[...] = jnp.full_like(high, FLOOR)
    sums[...] = jnp.zeros_like(sums)

    def one(tile, _):
        start = tile * tile_k
        keys = held[pl.ds(pl.multiple_of(start, tile_k), tile_k), width : 2 * width]
        raw[...] = dot_turned(keys, queries)
        last = jnp.minimum(last_key, ends[tile] - 1) - start
        first = first_key - start
        peaks = jnp.broadcast_to(high[...], (8, raw.shape[1]))
        for begin in range(0, tile_k, STRIP):
            scores = raw[begin : begin + STRIP, :]
            row = lax.broadcasted_iota(jnp.int32, scores.shape, 0) + begin
            scores = jnp.where((row <= last) & (row >= first), scores, NEGATIVE)
            raw[begin : begin + STRIP, :] = scores
            for group in range(0, STRIP, 8):
                peaks = jnp.maximum(peaks, scores[group : group + 8])
        highest = jnp.max(peaks, axis=0, keepdims=True)
        partial = jnp.zeros((8, raw.shape[1]), F32)
        for begin in range(0, tile_k, STRIP):
            raised = jnp.exp(raw[begin : begin + STRIP, :] - highest)
            chances[begin : begin + STRIP, :] = raised.astype(BF16)
            for group in range(0, STRIP, 8):
                partial = partial + raised[group : group + 8]
        shrink = jnp.exp(high[...] - highest)
        sums[...] = sums[...] * shrink + jnp.sum(partial, axis=0, keepdims=True)
        total[...] = total[...] * shrink + dot(turned[tile], chances[...])
        high[...] = highest
        return 0

    upper = (index * tile_q + tile_q - 1) // tile_k + 1
    lax.fori_loop(lows[index], upper, one, 0)
    found = sums[...] > 0.0
    safe = jnp.where(found, sums[...], 1.0)
    out[...] = fold_heads(
        total[...] * jnp.where(found, 1.0 / safe, 0.0), heads, tile_q
    ).astype(BF16)
    log_total = jnp.where(found, high[...] + jnp.log(safe), 0.0)
    for head in range(heads):
        logs[head : head + 1, :] = log_total[:, head * tile_q : (head + 1) * tile_q]


def attend(pieces, place, lows, ends, bounds, nctx, block_rows, *needed):
    total_rows = nctx * block_rows
    width = pieces[0].shape[1] // 3
    heads = width // HEAD_DIM
    steps = total_rows // TILE_Q
    grid_spec = pltpu.PrefetchScalarGridSpec(
        num_scalar_prefetch=3,
        grid=(steps,),
        in_specs=[pl.BlockSpec((2, TILE_Q), lambda i, *_: (0, i))]
        + [whole(piece.shape) for piece in pieces]
        + anywhere(len(needed)),
        out_specs=[
            pl.BlockSpec((TILE_Q, width), lambda i, *_: (i, 0)),
            pl.BlockSpec((heads, TILE_Q), lambda i, *_: (0, i)),
        ],
        scratch_shapes=[
            pltpu.VMEM((total_rows, 3 * width), BF16),
            pltpu.VMEM((total_rows // TILE_K, width, TILE_K), BF16),
            pltpu.VMEM((width, heads * TILE_Q), F32),
            pltpu.VMEM((1, heads * TILE_Q), F32),
            pltpu.VMEM((1, heads * TILE_Q), F32),
            pltpu.VMEM((TILE_K, heads * TILE_Q), F32),
            pltpu.VMEM((TILE_K, heads * TILE_Q), BF16),
        ],
    )
    return pl.pallas_call(
        functools.partial(attend_kernel, nctx, heads, len(pieces), len(needed), block_rows),
        grid_spec=grid_spec,
        out_shape=[
            jax.ShapeDtypeStruct((total_rows, width), BF16),
            jax.ShapeDtypeStruct((heads, total_rows), F32),
        ],
        compiler_params=params(),
        cost_estimate=takes(10),
        name="attend",
    )(place, lows, ends, bounds, *pieces, *needed)


def attend_back_kernel(
    nctx, head, last_one, count, extra, block_rows, place, lows, ends, bounds, logs, *refs
):
    pieces, refs = refs[:count], refs[count:]
    grad, attended, refs = refs[0], refs[1], refs[2:]
    prior = refs[0] if head else None
    refs = refs[extra + (1 if head else 0) :]
    outs, refs = refs[: count if last_one else 1], refs[count if last_one else 1 :]
    held, turned, grad_keys, grad_values, grad_query, raw, raw_grad, chances, steps, merged = refs
    tile_q, tile_k = grad.shape[0], turned.shape[2]
    width = grad.shape[1]
    index = pl.program_id(0)
    scale = jnp.asarray(HEAD_DIM**-0.5, BF16)

    @pl.when(index == 0)
    def _():
        load_pieces(place[0], pieces, nctx, held, block_rows)
        for tile in range(turned.shape[0]):
            turned[tile] = jnp.transpose(
                held[tile * tile_k : (tile + 1) * tile_k, width : 2 * width]
            )
        grad_keys[...] = jnp.zeros_like(grad_keys)
        grad_values[...] = jnp.zeros_like(grad_values)

    mine = lax.broadcasted_iota(jnp.int32, (tile_q, width), 1) // HEAD_DIM == head
    query_rows = pl.ds(pl.multiple_of(index * tile_q, tile_q), tile_q)
    queries = jnp.where(mine, held[query_rows, :width], jnp.zeros((), BF16)) * scale
    incoming = jnp.where(mine, grad[...], jnp.zeros((), BF16))
    product = jnp.transpose(incoming.astype(F32) * attended[...].astype(F32))
    centre = jnp.sum(product, axis=0, keepdims=True)
    first_key, last_key = bounds[0:1, :], bounds[1:2, :]
    log_total = logs[head : head + 1, :]
    grad_query[...] = jnp.zeros_like(grad_query)

    def one(tile, _):
        start = tile * tile_k
        key_rows = pl.ds(pl.multiple_of(start, tile_k), tile_k)
        raw[...] = dot_turned(held[key_rows, width : 2 * width], queries)
        raw_grad[...] = dot_turned(held[key_rows, 2 * width :], incoming)
        last = jnp.minimum(last_key, ends[tile] - 1) - start
        first = first_key - start
        for begin in range(0, tile_k, STRIP):
            at = slice(begin, begin + STRIP)
            row = lax.broadcasted_iota(jnp.int32, (STRIP, tile_q), 0) + begin
            allowed = (row <= last) & (row >= first)
            chance = jnp.exp(jnp.where(allowed, raw[at, :] - log_total, NEGATIVE))
            chances[at, :] = chance.astype(BF16)
            steps[at, :] = (chance * (raw_grad[at, :] - centre)).astype(BF16)
        grad_values[key_rows, :] += dot(chances[...], incoming)
        grad_keys[key_rows, :] += dot(steps[...], queries)
        grad_query[...] += dot(turned[tile], steps[...])
        return 0

    upper = (index * tile_q + tile_q - 1) // tile_k + 1
    lax.fori_loop(lows[index], upper, one, 0)
    merged[query_rows, :width] = (jnp.transpose(grad_query[...]) * HEAD_DIM**-0.5).astype(BF16)

    @pl.when(index == pl.num_programs(0) - 1)
    def _():
        merged[:, width : 2 * width] = grad_keys[...].astype(BF16)
        merged[:, 2 * width :] = grad_values[...].astype(BF16)
        own = lax.broadcasted_iota(jnp.int32, (tile_q, 3 * width), 1) % width // HEAD_DIM >= head
        if head:
            for begin in range(0, merged.shape[0], tile_q):
                at = slice(begin, begin + tile_q)
                merged[at, :] = jnp.where(own, merged[at, :], prior[at, :])
        if not last_one:
            outs[0][...] = merged[...]
        else:
            chunk_rows = outs[0].shape[0]
            for chunk in range(count // nctx):
                for way in range(nctx):
                    first = jnp.bitwise_xor(place[0], way) * block_rows + chunk * chunk_rows
                    outs[chunk * nctx + way][...] = merged[
                        pl.ds(pl.multiple_of(first, chunk_rows), chunk_rows), :
                    ]


def attend_back(
    pieces, place, lows, ends, bounds, logs, grad, attended, nctx, block_rows, head, prior, *needed
):
    total_rows, width = grad.shape
    heads = width // HEAD_DIM
    steps = total_rows // TILE_Q
    last_one = head == heads - 1
    by_tile = pl.BlockSpec((TILE_Q, width), lambda i, *_: (i, 0))
    everything = jax.ShapeDtypeStruct((total_rows, 3 * width), BF16)
    shapes = [jax.ShapeDtypeStruct(p.shape, BF16) for p in pieces] if last_one else [everything]
    grid_spec = pltpu.PrefetchScalarGridSpec(
        num_scalar_prefetch=3,
        grid=(steps,),
        in_specs=[
            pl.BlockSpec((2, TILE_Q), lambda i, *_: (0, i)),
            pl.BlockSpec((heads, TILE_Q), lambda i, *_: (0, i)),
        ]
        + [whole(piece.shape) for piece in pieces]
        + [by_tile] * 2
        + [whole(value.shape) for value in prior]
        + anywhere(len(needed)),
        out_specs=[whole(shape.shape) for shape in shapes],
        scratch_shapes=[
            pltpu.VMEM((total_rows, 3 * width), BF16),
            pltpu.VMEM((total_rows // TILE_K, width, TILE_K), BF16),
            pltpu.VMEM((total_rows, width), F32),
            pltpu.VMEM((total_rows, width), F32),
            pltpu.VMEM((width, TILE_Q), F32),
            pltpu.VMEM((TILE_K, TILE_Q), F32),
            pltpu.VMEM((TILE_K, TILE_Q), F32),
            pltpu.VMEM((TILE_K, TILE_Q), BF16),
            pltpu.VMEM((TILE_K, TILE_Q), BF16),
            pltpu.VMEM((total_rows, 3 * width), BF16),
        ],
    )
    return pl.pallas_call(
        functools.partial(
            attend_back_kernel, nctx, head, last_one, len(pieces), len(needed), block_rows
        ),
        grid_spec=grid_spec,
        out_shape=shapes,
        compiler_params=params(),
        cost_estimate=takes(10),
        name="attend_back",
    )(place, lows, ends, bounds, logs, *pieces, grad, attended, *prior, *needed)


def mix_kernel(nctx, place, heads_in, weight, source, gain, bias, returned, mixed, *lows):
    rows, depth = mixed.shape
    step = pl.program_id(0)
    left = jnp.concatenate([heads_in[c, 0] for c in range(nctx)], axis=1)
    returned[...] = left

    @pl.when(step == 0)
    def _():
        mixed[...] = source[...].astype(F32)

    mixed[...] += dot_turned(left, weight[0])

    @pl.when(step == pl.num_programs(0) - 1)
    def _():
        values = mixed[...]
        values = values - jnp.mean(values, axis=1, keepdims=True)
        scaling = lax.rsqrt(jnp.mean(values * values, axis=1, keepdims=True) + EPSILON)
        values = (values * scaling * gain[...] + bias[...]).astype(BF16)
        part_rows = lows[0].shape[0]
        for part, low in enumerate(lows):
            low[...] = values[part * part_rows : (part + 1) * part_rows]


def mix(heads_in, weight, full, gain, bias, place, parts):
    nctx, tp, rows, piece = heads_in.shape
    depth = full.shape[1]
    head_width = nctx * piece
    grid_spec = pltpu.PrefetchScalarGridSpec(
        num_scalar_prefetch=1,
        grid=(tp,),
        in_specs=[
            pl.BlockSpec((nctx, 1, rows, piece), lambda k, s: (0, k, 0, 0)),
            pl.BlockSpec((1, depth, head_width), lambda k, s: (k, 0, 0)),
            pl.BlockSpec((rows, depth), lambda k, s: (s[0], 0)),
            whole((1, depth)),
            whole((1, depth)),
        ],
        out_specs=[
            pl.BlockSpec((rows, head_width), lambda k, s: (0, k)),
            whole((rows, depth)),
        ]
        + [whole((rows // parts, depth))] * parts,
    )
    return pl.pallas_call(
        functools.partial(mix_kernel, nctx),
        grid_spec=grid_spec,
        out_shape=[
            jax.ShapeDtypeStruct((rows, tp * head_width), BF16),
            jax.ShapeDtypeStruct((rows, depth), F32),
        ]
        + [jax.ShapeDtypeStruct((rows // parts, depth), BF16)] * parts,
        compiler_params=params(),
        cost_estimate=takes(20),
        name="mix",
    )(place, heads_in, weight, full, gain, bias)


def feed_kernel(cuts, parts, tp, first_one, place, *refs):
    lows, cot, mixed, source = refs[:parts], refs[parts], refs[parts + 1], refs[parts + 2]
    refs = refs[-(4 + tp + 1 + 4) :]
    kept, hidden, grad_gate, grad_up, *outs = refs[: 4 + tp]
    partial, held, sems = refs[4 + tp], refs[-4:-1], refs[-1]
    unit = source.shape[1] // 3
    width = outs[0].shape[1]

    def copies(index):
        first, size = cuts[index]
        at = pl.ds(first, size)
        return [
            pltpu.make_async_copy(
                source.at[:, pl.ds(which * unit, unit), at],
                held[which].at[:, :, at],
                sems.at[index * 3 + which],
            )
            for which in range(3)
        ]

    for index in range(len(cuts)):
        for copy in copies(index):
            copy.start()
    rows = lows[0].shape[0]
    for part in range(parts):
        kept[part * rows : (part + 1) * rows] = lows[part][...]
    depth = kept.shape[1]
    for index, (first, size) in enumerate(cuts):
        for copy in copies(index):
            copy.wait()
        at = slice(first, first + size)
        gate_weight, up_weight, down_weight = [w[:, :, at].reshape(depth, size) for w in held]
        gate = dot(kept[...], gate_weight)
        up = dot(kept[...], up_weight)
        sigma = 1.0 / (1.0 + jnp.exp(-gate))
        active = gate * sigma
        hidden[:, at] = (active * up).astype(BF16)
        grad = dot(cot[...], down_weight)
        grad_gate[:, at] = (grad * up * sigma * (1.0 + gate * (1.0 - sigma))).astype(BF16)
        grad_up[:, at] = (grad * active).astype(BF16)
    gate_weight, up_weight, down_weight = [w[...].reshape(depth, w.shape[2]) for w in held]
    product = dot_turned(grad_gate[...], gate_weight) + dot_turned(grad_up[...], up_weight)
    partial[...] = product.astype(BF16)
    per = width // unit if width % unit == 0 else 1
    for step, out in enumerate(outs):
        owner = lax.rem(place[0] - step + tp, tp)
        right = held[2][pl.ds(owner * per, per)].reshape(width, hidden.shape[1])
        values = dot_turned(hidden[...], right)
        if first_one:
            values = values + mixed[:, pl.ds(pl.multiple_of(owner * width, width), width)]
        out[...] = values.astype(BF16)


def feed(lows, cot, mixed, weights, step, tp, place, held, *needed):
    parts = len(lows)
    part_rows, depth = lows[0].shape
    rows = parts * part_rows
    blocks, triple, hidden = weights.shape
    cuts = []
    while sum(size for _, size in cuts) < hidden:
        first = sum(size for _, size in cuts)
        cuts.append((first, min(512, hidden - first)))
    by_owner = lambda columns: pl.BlockSpec(
        (rows, columns), lambda i, s: (lax.rem(s[0] - step + tp, tp), 0)
    )
    width = depth // tp
    grid_spec = pltpu.PrefetchScalarGridSpec(
        num_scalar_prefetch=1,
        grid=(1,),
        in_specs=[whole((part_rows, depth))] * parts
        + [by_owner(depth), whole(mixed.shape)]
        + anywhere(1 + len(held) + len(needed)),
        out_specs=[by_owner(depth)]
        + [by_owner(hidden)] * 3
        + [by_owner(width)] * tp
        + [whole((rows, depth))],
        scratch_shapes=[pltpu.VMEM((blocks, triple // 3, hidden), BF16)] * 3
        + [pltpu.SemaphoreType.DMA((3 * len(cuts),))],
    )
    return pl.pallas_call(
        functools.partial(feed_kernel, tuple(cuts), parts, tp, step == 0),
        grid_spec=grid_spec,
        out_shape=[jax.ShapeDtypeStruct((tp * rows, depth), BF16)]
        + [jax.ShapeDtypeStruct((tp * rows, hidden), BF16)] * 3
        + [jax.ShapeDtypeStruct((tp * rows, width), BF16)] * tp
        + [jax.ShapeDtypeStruct((rows, depth), BF16)],
        input_output_aliases={4 + parts + index: index for index in range(len(held))},
        compiler_params=params(),
        cost_estimate=takes(150),
        name="feed",
    )(place, *lows, cot, mixed, weights, *held, *needed)


def blame(left, right, which, pick_left, unit, arrived, needed, buffer=None, slot=0, slots=1):
    rows = left.shape[0]
    picked = (left if pick_left else right).shape[1] // unit // 2
    other = (right if pick_left else left).shape[1]
    chosen = pl.BlockSpec((rows, unit), lambda j, s: (0, 2 * j + s[0]))
    kept = whole((rows, other))
    if pick_left:
        shape = (slots * picked * unit, other)
        target = pl.BlockSpec((unit, other), lambda j, s: (slots * j + slot, 0))
        source = pl.BlockSpec((unit, other), lambda j, s: (j, 0))
    else:
        shape = (other, picked * unit)
        target = source = pl.BlockSpec((other, unit), lambda j, s: (0, j))
    extra = [] if arrived is None else [arrived]
    held = [] if buffer is None else [buffer]

    def kernel(which, left, right, *refs):
        product = lax.dot_general(
            left[...], right[...], (((0,), (0,)), ((), ())), preferred_element_type=F32
        )
        if extra:
            product = product + refs[0][...].astype(F32)
        refs[-1][...] = product.astype(BF16)

    grid_spec = pltpu.PrefetchScalarGridSpec(
        num_scalar_prefetch=1,
        grid=(picked,),
        in_specs=([chosen, kept] if pick_left else [kept, chosen])
        + [source] * len(extra)
        + anywhere(len(held) + len(needed)),
        out_specs=target,
    )
    return pl.pallas_call(
        kernel,
        grid_spec=grid_spec,
        out_shape=jax.ShapeDtypeStruct(shape, BF16),
        input_output_aliases={3 + len(extra): 0} if held else {},
        compiler_params=params(),
        cost_estimate=takes(70),
        name="blame",
    )(which, left, right, *extra, *held, *needed)


def turn_kernel(nctx, count, parts, place, *refs):
    arrived, own = refs[:parts], refs[parts : 2 * parts]
    mixed, cot, gain = refs[2 * parts : 2 * parts + 3]
    weight, refs = refs[2 * parts + 3], refs[2 * parts + 4 + count :]
    out, grad_mixed, grad_low, gain_grad, shift_grad = refs
    rows, depth = mixed.shape
    piece = out.shape[3]

    @pl.when(pl.program_id(0) == 0)
    def _():
        incoming = jnp.concatenate(
            [there[...].astype(F32) + here[...].astype(F32) for there, here in zip(arrived, own)]
        )
        values = mixed[...]
        values = values - jnp.mean(values, axis=1, keepdims=True)
        scaling = lax.rsqrt(jnp.mean(values * values, axis=1, keepdims=True) + EPSILON)
        normed = values * scaling
        shift_grad[...] = jnp.sum(incoming, axis=0, keepdims=True)
        gain_grad[...] = jnp.sum(incoming * normed, axis=0, keepdims=True)
        scaled = incoming * gain[...]
        total = cot[...].astype(F32) + scaling * (
            scaled
            - jnp.mean(scaled, axis=1, keepdims=True)
            - normed * jnp.mean(scaled * normed, axis=1, keepdims=True)
        )
        grad_mixed[...] = total
        grad_low[...] = total.astype(BF16)

    product = dot(grad_low[...], weight[0])
    for c in range(nctx):
        out[c, 0] = product[:, c * piece : (c + 1) * piece].astype(BF16)


def turn(arrived, own, mixed, cot, gain, weight, place, nctx, tp, *needed):
    rows, depth = mixed.shape
    parts = len(arrived)
    head_width = weight.shape[2]
    piece = head_width // nctx
    grid_spec = pltpu.PrefetchScalarGridSpec(
        num_scalar_prefetch=1,
        grid=(tp,),
        in_specs=[whole((rows // parts, depth))] * (2 * parts)
        + [whole((rows, depth))]
        + [
            pl.BlockSpec((rows, depth), lambda k, s: (s[0], 0)),
            whole((1, depth)),
            pl.BlockSpec((1, depth, head_width), lambda k, s: (k, 0, 0)),
        ]
        + anywhere(len(needed)),
        out_specs=[
            pl.BlockSpec((nctx, 1, rows, piece), lambda k, s: (0, k, 0, 0)),
            whole((rows, depth)),
            whole((rows, depth)),
            whole((1, depth)),
            whole((1, depth)),
        ],
    )
    return pl.pallas_call(
        functools.partial(turn_kernel, nctx, len(needed), parts),
        grid_spec=grid_spec,
        out_shape=[
            jax.ShapeDtypeStruct((nctx, tp, rows, piece), BF16),
            jax.ShapeDtypeStruct((rows, depth), F32),
            jax.ShapeDtypeStruct((rows, depth), BF16),
            jax.ShapeDtypeStruct((1, depth), F32),
            jax.ShapeDtypeStruct((1, depth), F32),
        ],
        compiler_params=params(),
        cost_estimate=takes(20),
        name="turn",
    )(place, *arrived, *own, mixed, cot, gain, weight, *needed)


def finish_kernel(nctx, tp, extra_count, chunk, place, *refs):
    pieces = refs[:nctx]
    cosine, sine_up, sine_down, full, extra, gain = refs[nctx : nctx + 6]
    weight, refs = refs[nctx + 6], refs[nctx + 7 + extra_count :]
    outs = refs[:tp]
    low, bias_grad, gain_grad, shift_grad, spare = refs[tp:]
    rows, wide = pieces[0].shape
    piece = wide // 3
    width = outs[0].shape[1]
    strip = spare.shape[0]
    extra_rows = extra.shape[0]

    @pl.when(pl.program_id(0) == 0)
    def _():
        bias_grad[...] = jnp.zeros_like(bias_grad)
        gain_grad[...] = jnp.zeros_like(gain_grad)
        shift_grad[...] = jnp.zeros_like(shift_grad)

    for step in range(nctx):
        source = jnp.bitwise_xor(place[1], step)
        for part in range(3):
            values = pieces[step][:, part * piece : (part + 1) * piece].astype(F32)
            if part < 2:
                values = (
                    values * cosine[...]
                    - pltpu.roll(values, piece - ROT // 2, 1) * sine_up[...]
                    - pltpu.roll(values, ROT // 2, 1) * sine_down[...]
                )
            columns = pl.ds(pl.multiple_of(source * wide + part * piece, piece), piece)
            bias_grad[:, columns] += jnp.sum(values, axis=0, keepdims=True)
            low[:, columns] = values.astype(BF16)

    incoming = dot_turned(low[...], weight[...])
    source = full[...].astype(F32)
    source = source - jnp.mean(source, axis=1, keepdims=True)
    scaling = lax.rsqrt(jnp.mean(source * source, axis=1, keepdims=True) + EPSILON)
    normed = source * scaling
    shift_grad[...] += jnp.sum(incoming, axis=0, keepdims=True)
    gain_grad[...] += jnp.sum(incoming * normed, axis=0, keepdims=True)
    scaled = incoming * gain[...]
    spare[...] = scaling * (
        scaled
        - jnp.mean(scaled, axis=1, keepdims=True)
        - normed * jnp.mean(scaled * normed, axis=1, keepdims=True)
    )
    first = chunk * pl.num_programs(0) * strip + pl.program_id(0) * strip
    wanted = place[0] * extra_rows

    if strip <= extra_rows:

        @pl.when((first >= wanted) & (first < wanted + extra_rows))
        def _():
            spare[...] += extra[pl.ds(pl.multiple_of(first - wanted, strip), strip), :]

    else:

        @pl.when((wanted >= first) & (wanted < first + strip))
        def _():
            spare[pl.ds(pl.multiple_of(wanted - first, extra_rows), extra_rows), :] += extra[...]

    for step, out in enumerate(outs):
        owner = lax.rem(place[0] - step + tp, tp)
        out[...] = spare[:, pl.ds(pl.multiple_of(owner * width, width), width)].astype(BF16)


def finish(pieces, place, tables, full, extra, gain, weight, chunk, tp, *needed):
    rows, wide = pieces[0].shape
    depth = full.shape[1]
    total = weight.shape[1]
    strip = 256
    steps = rows // strip
    width = depth // tp
    nctx = len(pieces)
    by_rows = lambda columns: pl.BlockSpec((strip, columns), lambda i, s: (i, 0))
    grid_spec = pltpu.PrefetchScalarGridSpec(
        num_scalar_prefetch=1,
        grid=(steps,),
        in_specs=[by_rows(wide)] * nctx
        + [by_rows(2 * HEAD_DIM)] * 3
        + [
            pl.BlockSpec((strip, depth), lambda i, s: (i + chunk * steps, 0)),
            whole(extra.shape),
            whole((1, depth)),
        ]
        + [whole(weight.shape)]
        + anywhere(len(needed)),
        out_specs=[by_rows(width)] * tp
        + [
            by_rows(total),
            whole((1, total)),
            whole((1, depth)),
            whole((1, depth)),
        ],
        scratch_shapes=[pltpu.VMEM((strip, depth), F32)],
    )
    return pl.pallas_call(
        functools.partial(finish_kernel, nctx, tp, len(needed), chunk),
        grid_spec=grid_spec,
        out_shape=[jax.ShapeDtypeStruct((rows, width), BF16)] * tp
        + [
            jax.ShapeDtypeStruct((rows, total), BF16),
            jax.ShapeDtypeStruct((1, total), F32),
            jax.ShapeDtypeStruct((1, depth), F32),
            jax.ShapeDtypeStruct((1, depth), F32),
        ],
        compiler_params=params(),
        cost_estimate=takes(20),
        name="finish",
    )(place, *pieces, *tables, full, extra, gain, weight, *needed)


def join(rings, place, *needed):
    chunks, tp = len(rings), len(rings[0])
    rows, width = rings[0][0].shape

    def kernel(place, *refs):
        for chunk in range(chunks):

            @pl.when(pl.program_id(0) == chunk)
            def _():
                for step in range(tp):
                    owner = lax.rem(place[0] - step + tp, tp)
                    refs[-1][:, pl.ds(pl.multiple_of(owner * width, width), width)] = refs[
                        chunk * tp + step
                    ][...]

    grid_spec = pltpu.PrefetchScalarGridSpec(
        num_scalar_prefetch=1,
        grid=(chunks,),
        in_specs=[whole((rows, width))] * (chunks * tp) + anywhere(len(needed)),
        out_specs=pl.BlockSpec((rows, tp * width), lambda i, s: (i, 0)),
    )
    return pl.pallas_call(
        kernel,
        grid_spec=grid_spec,
        out_shape=jax.ShapeDtypeStruct((chunks * rows, tp * width), BF16),
        compiler_params=params(),
        cost_estimate=takes(1),
        name="join",
    )(place, *[block for blocks in rings for block in blocks], *needed)


def contract_rows(left, right):
    return lax.dot_general(left, right, (((0,), (0,)), ((), ())), preferred_element_type=F32)


def pick(stack, index):
    return lax.dynamic_index_in_dim(stack, index, 0, keepdims=False)


def shards(
    nfsdp,
    nctx,
    tp,
    inputs,
    cotangent,
    first_gain,
    first_bias,
    qkv_weight,
    qkv_bias,
    out_weight,
    second_gain,
    second_bias,
    gate_weight,
    up_weight,
    down_weight,
    lengths,
    fill_counts,
):
    data = ("fsdp", "ctx")
    ndata = nfsdp * nctx
    block_rows, width = inputs.shape
    depth = tp * width
    half_depth = depth // 2
    unit = depth // ndata
    tensor_index = lax.axis_index("tp").astype(jnp.int32)
    context_index = lax.axis_index("ctx").astype(jnp.int32)
    fsdp_index = lax.axis_index("fsdp").astype(jnp.int32)
    part_rows = block_rows // tp
    chunk_rows = block_rows // CHUNKS
    head_width = qkv_weight.shape[2]
    piece = head_width // nctx
    wide = 3 * piece

    square = nfsdp == 2 and nctx == 4 and unit % 128 == 0
    place = jnp.stack([tensor_index, context_index, fsdp_index])

    def shift(value, step):
        return lax.ppermute(value, "tp", [(i, (i + step) % tp) for i in range(tp)])

    def swap(value, step):
        return lax.ppermute(value, "ctx", [(i, i ^ step) for i in range(nctx)])

    core_index = context_index % 2
    groups = [list(range(0, ndata, 2)), list(range(1, ndata, 2))]
    own_half, other_half = core_index[None], (1 - core_index)[None]

    def partner(left, right, pick_left, *needed):
        first = blame(left, right, other_half, pick_left, unit, None, needed)
        return first, swap(first, 1)

    def own(left, right, pick_left, arrived, *needed, **buffer):
        return blame(left, right, own_half, pick_left, unit, arrived, needed, **buffer)

    def scatter_half(value, axis):
        return lax.psum_scatter(
            value, data, scatter_dimension=axis, tiled=True, axis_index_groups=groups
        )

    def scatter_whole(left, right, axis):
        return lax.psum_scatter(
            contract_rows(left, right).astype(BF16), data, scatter_dimension=axis, tiled=True
        )

    def total(left, right):
        return (left.astype(F32) + right.astype(F32)).astype(BF16)

    owners = [(tensor_index - step + tp) % tp for step in range(tp)]

    own_qkv = (
        qkv_weight.reshape(-1, 3, nctx, piece).transpose(0, 2, 1, 3).reshape(-1, 3 * head_width)
    )
    full_qkv = lax.all_gather(own_qkv, data, axis=0, tiled=True)
    own_feed = jnp.concatenate([gate_weight, up_weight, down_weight.T], axis=0)
    feed_weights = lax.all_gather(own_feed, data, axis=0, tiled=True).reshape(ndata, 3 * unit, -1)

    validity, position, first_key, last_key = layout(lengths[0], fill_counts[0], block_rows)
    own_position = lax.dynamic_slice_in_dim(position, context_index * block_rows, block_rows, 0)
    tables = rotary_tables(own_position)
    bounds = jnp.stack([first_key, last_key])
    tile_first = first_key[::TILE_Q]
    tile_count = tile_first.shape[0]
    lows = jnp.where(validity[::TILE_Q], tile_first // TILE_K, tile_count * TILE_Q).astype(jnp.int32)
    key_block = jnp.arange(0, nctx * block_rows, TILE_K, dtype=jnp.int32) // block_rows
    ends = (
        key_block * block_rows
        + jnp.sum(
            jnp.where(
                key_block[:, None] == jnp.arange(nctx, dtype=jnp.int32)[None, :],
                fill_counts[0][None, :],
                0,
            ),
            axis=1,
        )
    ).astype(jnp.int32)

    flat_bias = qkv_bias.reshape(3, nctx, piece).transpose(1, 0, 2).reshape(1, -1)
    gain_one, bias_one = first_gain[None], first_bias[None]
    gain_two, bias_two = second_gain[None], second_bias[None]

    rings = [[inputs[c * chunk_rows : (c + 1) * chunk_rows]] for c in range(CHUNKS)]
    share = unit // CHUNKS
    for chunk in range(CHUNKS):
        carried = out_weight.T[chunk * share : (chunk + 1) * share]
        rings[chunk][0] = jnp.concatenate([rings[chunk][0], carried], axis=0)
    for chunk in range(CHUNKS):
        for _ in range(tp - 1):
            rings[chunk].append(shift(rings[chunk][-1], 1))
    stack = jnp.zeros((tp, unit, head_width), BF16)
    for step in range(tp):
        carried = jnp.concatenate([blocks[step][chunk_rows:] for blocks in rings], axis=0)
        stack = lax.dynamic_update_index_in_dim(stack, carried, owners[step], 0)
    full_out = lax.all_gather(stack, data, axis=1, tiled=True)
    lows_one, fulls, pieces, chunk_tables = [], [], [], []
    for chunk in range(CHUNKS):
        at = slice(chunk * chunk_rows, (chunk + 1) * chunk_rows)
        chunk_tables.append([table[at] for table in tables])
        low, full, *outgoing = project(
            rings[chunk],
            place,
            gain_one,
            bias_one,
            full_qkv,
            flat_bias,
            chunk_tables[chunk],
            nctx,
        )
        lows_one.append(low)
        fulls.append(full)
        pieces.append(outgoing[0])
        for way in range(1, nctx):
            pieces.append(swap(outgoing[way], way))
    full = jnp.concatenate(fulls, axis=0)

    cot_start = tie(cotangent, *[blocks[-1] for blocks in rings])
    cot_rings = [[cot_start[c * chunk_rows : (c + 1) * chunk_rows]] for c in range(CHUNKS)]
    for _ in range(tp - 1):
        for blocks in cot_rings:
            blocks.append(shift(blocks[-1], 1))

    attended, logs = attend(
        pieces,
        place[1:2],
        lows,
        ends,
        bounds,
        nctx,
        block_rows,
    )
    full_cot = join(cot_rings, place, attended)
    arrived = lax.all_to_all(
        attended.reshape(nctx * tp, part_rows, piece),
        ("ctx", "tp"),
        split_axis=0,
        concat_axis=0,
        tiled=True,
    )
    returned, mixed, *second_low = mix(
        arrived.reshape(nctx, tp, part_rows, piece),
        full_out,
        full,
        gain_two,
        bias_two,
        place,
        HALVES,
    )

    arrived, held, partials, travelling = second_low, [], [], None
    for step in range(tp):
        coming = [shift(value, 1) for value in arrived] if step < tp - 1 else None
        needed = [travelling] if step == tp - 1 and step > 2 else []
        results = feed(
            arrived, full_cot, mixed, feed_weights, step, tp, place, held, *needed
        )
        held, partial = results[: 4 + tp], results[4 + tp]
        partials.append(partial)
        if step == 1 % tp:
            travelling = partials[step]
        elif 1 < step < tp - 1:
            travelling = total(shift(travelling, 1), partials[step])
        if step == 0 and coming is not None:
            coming = [tie(value, partials[0]) for value in coming]
        arrived = coming
    all_second, hidden, all_gate, all_up, *feedforward = held

    needed = []
    if square:
        first, gate_arrived = partner(all_second, all_gate, True)
        second, up_arrived = partner(all_second, all_up, True)
        needed = [first, second]
    if tp > 2:
        travelling = add(shift(travelling, 1), partials[-1], *needed)
    needed = []
    if square:
        last = shift(travelling, 1)
        pair = own(all_second, all_gate, True, gate_arrived, travelling, slot=0, slots=2)
        pair = own(all_second, all_up, True, up_arrived, buffer=pair, slot=1, slots=2)
        needed = [pair]
        pair = scatter_half(pair, 0)
        total_gate, total_up = pair[:unit], pair[unit:]
    else:
        last = shift(travelling, 1)
        total_gate = scatter_whole(all_second, all_gate, 0)
        total_up = scatter_whole(all_second, all_up, 0)

    grad_heads, grad_mixed, mixed_low, gain_grad_two, shift_grad_two = turn(
        [last],
        [partials[0]],
        mixed,
        full_cot,
        gain_two,
        full_out,
        place,
        nctx,
        tp,
        *needed,
    )
    grad_heads = lax.all_to_all(
        grad_heads.reshape(nctx * tp, part_rows, piece),
        ("ctx", "tp"),
        split_axis=0,
        concat_axis=0,
        tiled=True,
    ).reshape(nctx * block_rows, piece)

    by_row = (pieces, place[1:2], lows, ends, bounds, logs, grad_heads, attended, nctx, block_rows)
    needed = []
    if square:
        first, out_arrived = partner(mixed_low, returned, True)
        half_out = own(mixed_low, returned, True, out_arrived)
        needed = [half_out]
        total_out = scatter_half(half_out, 0)
    else:
        total_out = scatter_whole(mixed_low, returned, 0)

    heads = piece // HEAD_DIM
    layer_out, grad_pieces, hop = tie(feedforward[1 % tp], grad_heads), [], 2
    for head in range(heads):
        grad_pieces = attend_back(*by_row, head, grad_pieces, *needed)
        if hop < tp:
            layer_out = add(shift(layer_out, 1), feedforward[hop], grad_pieces[0])
            needed, hop = [layer_out], hop + 1
    while hop < tp:
        layer_out = add(shift(layer_out, 1), feedforward[hop])
        hop += 1
    needed = [layer_out]
    if tp > 1:
        layer_out = total(shift(layer_out, 1), feedforward[0])
    if square:
        first, down_arrived = partner(hidden, full_cot, False, grad_pieces[0])
    else:
        total_down = scatter_whole(hidden, full_cot, 1)
    out_parts = jnp.swapaxes(total_out.reshape(-1, tp, head_width), 0, 1)
    total_out = pick(out_parts, tensor_index).astype(F32)
    for step in range(1, tp):
        total_out = total_out + shift(pick(out_parts, (tensor_index + step) % tp), step).astype(F32)
    total_out = total_out.T
    grad_lows, bias_grads, gain_grads, shift_grads, grad_rows = [], [], [], [], []
    ring_steps = []
    for chunk in range(CHUNKS):
        outgoing = grad_pieces[chunk * nctx : (chunk + 1) * nctx]
        arrived = [outgoing[0]] + [swap(outgoing[way], way) for way in range(1, nctx)]
        *partial, low, bias_grad, gain_grad, shift_grad = finish(
            arrived,
            place,
            chunk_tables[chunk],
            full,
            grad_mixed,
            gain_one,
            full_qkv,
            chunk,
            tp,
            *needed,
        )
        grad_lows.append(low)
        bias_grads.append(bias_grad)
        gain_grads.append(gain_grad)
        shift_grads.append(shift_grad)
        travelling = partial[1 % tp]
        for step in range(1, tp):
            travelling = total(shift(travelling, 1), partial[(step + 1) % tp])
            ring_steps.append(travelling)
        grad_rows.append(travelling)
    grad_inputs = jnp.concatenate(grad_rows, axis=0)

    all_low, all_grad = jnp.concatenate(lows_one, axis=0), jnp.concatenate(grad_lows, axis=0)
    if square:
        first, qkv_arrived = partner(all_low, all_grad, True, *ring_steps[:1])
        half_qkv = own(all_low, all_grad, True, qkv_arrived, *ring_steps[tp - 1 : tp])
        total_qkv = scatter_half(half_qkv, 0)
        half_down = own(hidden, full_cot, False, down_arrived, *ring_steps[1:2])
        total_down = scatter_half(half_down, 1)
    else:
        total_qkv = scatter_whole(all_low, all_grad, 0)
    total_qkv = (
        total_qkv.astype(F32)
        .reshape(-1, nctx, 3, piece)
        .transpose(0, 2, 1, 3)
        .reshape(-1, 3, head_width)
    )

    def exchange(value, axis, size):
        moved = [
            lax.ppermute(value, axis, [(i, i ^ step) for i in range(size)])
            for step in range(1, size)
        ]
        return sum(moved, value)

    small = jnp.concatenate([sum(gain_grads), sum(shift_grads), gain_grad_two, shift_grad_two], axis=1)
    small = jnp.concatenate([sum(bias_grads), small], axis=1)
    small = tie(small, *ring_steps[1:2], *ring_steps[tp - 1 : tp])
    small = exchange(exchange(small, "ctx", nctx), "fsdp", nfsdp)
    bias_total, small = small[:, : 3 * head_width], small[:, 3 * head_width :]
    small = exchange(small, "tp", tp)
    bias_total = bias_total.reshape(nctx, 3, piece).transpose(1, 0, 2).reshape(3, head_width)
    small = small.reshape(4, depth)
    return (
        layer_out,
        grad_inputs,
        small[0],
        small[1],
        total_qkv,
        bias_total,
        total_out,
        small[2],
        small[3],
        total_gate.astype(F32),
        total_up.astype(F32),
        total_down.astype(F32),
    )


def solution(mesh):
    data = ("fsdp", "ctx")
    by_rows = P(data, "tp")
    by_columns = P("tp", data)
    qkv = P(data, None, "tp")
    return jax.shard_map(
        functools.partial(shards, mesh.shape["fsdp"], mesh.shape["ctx"], mesh.shape["tp"]),
        mesh=mesh,
        in_specs=(
            by_rows,
            by_rows,
            P(),
            P(),
            qkv,
            P(None, "tp"),
            by_columns,
            P(),
            P(),
            by_rows,
            by_rows,
            by_columns,
            P("fsdp", None),
            P("fsdp", None),
        ),
        out_specs=(
            by_rows,
            by_rows,
            P(),
            P(),
            qkv,
            P(None, "tp"),
            by_columns,
            P(),
            P(),
            by_rows,
            by_rows,
            by_columns,
        ),
        check_vma=False,
    )
```

```python
import functools

import jax
import jax.numpy as jnp
from jax import lax
from jax.experimental import pallas as pl
from jax.experimental.pallas import tpu as pltpu
from jax.sharding import PartitionSpec as P

HEAD_DIM = 64
ROT = 16
EPSILON = 1e-05
NEGATIVE = -1e30
FLOOR = -1e20
VMEM_LIMIT = 56 * 1024 * 1024
TILE_Q = 512
TILE_K = 512
STRIP = 32
CHUNKS = 2
HALVES = 2

F32 = jnp.float32
BF16 = jnp.bfloat16


def layout(lengths, fill_counts, block_rows):
    blocks_count = fill_counts.shape[0]
    seq_count = lengths.shape[0]
    slot_index = jnp.arange(blocks_count * block_rows, dtype=jnp.int32)
    block_of = slot_index // block_rows
    within = slot_index - block_of * block_rows
    chooser = block_of[:, None] == jnp.arange(blocks_count, dtype=jnp.int32)[None, :]
    fill_here = jnp.sum(jnp.where(chooser, fill_counts[None, :], 0), axis=1)
    before = jnp.cumsum(fill_counts) - fill_counts
    before_here = jnp.sum(jnp.where(chooser, before[None, :], 0), axis=1)
    validity = within < fill_here
    used_index = before_here + within
    seq_ends = jnp.cumsum(lengths)
    sequence = jnp.sum((used_index[:, None] >= seq_ends[None, :]).astype(jnp.int32), axis=1)
    seq_starts = seq_ends - lengths
    picker = sequence[:, None] == jnp.arange(seq_count, dtype=jnp.int32)[None, :]
    start_here = jnp.sum(jnp.where(picker, seq_starts[None, :], 0), axis=1)
    after = before + fill_counts
    start_block = jnp.sum((seq_starts[:, None] >= after[None, :]).astype(jnp.int32), axis=1)
    start_block = jnp.minimum(start_block, blocks_count - 1)
    block_pick = start_block[:, None] == jnp.arange(blocks_count, dtype=jnp.int32)[None, :]
    start_before = jnp.sum(jnp.where(block_pick, before[None, :], 0), axis=1)
    start_slot = start_block * block_rows + seq_starts - start_before
    slot_here = jnp.sum(jnp.where(picker, start_slot[None, :], 0), axis=1)
    first_key = jnp.where(validity, slot_here, 0).astype(jnp.int32)
    last_key = jnp.where(validity, slot_index, -1).astype(jnp.int32)
    return (validity, used_index - start_here, first_key, last_key)


def rotary_tables(position):
    half = ROT // 2
    lane = jnp.arange(2 * HEAD_DIM, dtype=jnp.int32) % HEAD_DIM
    frequency = 10000.0 ** (-(2.0 * (lane % half).astype(F32)) / ROT)
    angles = position.astype(F32)[:, None] * frequency[None, :]
    cosine, sine = jnp.cos(angles), jnp.sin(angles)
    lane = lane[None, :]
    return (
        jnp.where(lane < ROT, cosine, 1.0),
        jnp.where(lane < half, -sine, 0.0),
        jnp.where((lane >= half) & (lane < ROT), sine, 0.0),
    )


def params(**extra):
    return pltpu.CompilerParams(vmem_limit_bytes=VMEM_LIMIT, **extra)


def takes(microseconds):
    return pl.CostEstimate(
        flops=int(microseconds * 1e8), bytes_accessed=0, transcendentals=0
    )


def whole(shape):
    return pl.BlockSpec(shape, lambda *_: (0,) * len(shape))


def anywhere(count):
    return [pl.BlockSpec(memory_space=pl.ANY)] * count


def dot(left, right):
    return jnp.dot(left, right, preferred_element_type=F32)


def dot_turned(left, right):
    return lax.dot_general(left, right, (((1,), (1,)), ((), ())), preferred_element_type=F32)


def tie(value, *needed):
    def kernel(*refs):
        del refs

    return pl.pallas_call(
        kernel,
        in_specs=anywhere(1 + len(needed)),
        out_specs=pl.BlockSpec(memory_space=pl.ANY),
        out_shape=jax.ShapeDtypeStruct(value.shape, value.dtype),
        input_output_aliases={0: 0},
        name="tie",
    )(value, *needed)


def add_kernel(left, right, *refs):
    refs[-1][...] = (left[...].astype(F32) + right[...].astype(F32)).astype(BF16)


def add(left, right, *needed):
    rows, columns = left.shape
    strip = min(rows, 128)
    block = pl.BlockSpec((strip, columns), lambda i: (i, 0))
    return pl.pallas_call(
        add_kernel,
        grid=(rows // strip,),
        in_specs=[block, block] + anywhere(len(needed)),
        out_specs=block,
        out_shape=jax.ShapeDtypeStruct(left.shape, BF16),
        compiler_params=params(),
        cost_estimate=takes(10),
        name="ring_add",
    )(left, right, *needed)


def project_kernel(tp, per, place, *refs):
    blocks = refs[:tp]
    gain, bias, weight, weight_bias, cosine, sine_up, sine_down = refs[tp : tp + 7]
    low, full, *outs = refs[tp + 7 :]
    rows, width = low.shape[0], blocks[0].shape[1]
    depth = tp * width
    wide = outs[0].shape[1]
    piece = wide // 3
    step = pl.program_id(0)

    @pl.when(pl.program_id(0) == 0)
    def _():
        strip = 128
        for start in range(0, rows, strip):
            at = slice(start, start + strip)
            parts = [block[at, :].astype(F32) for block in blocks]
            centre = sum(jnp.sum(part, axis=1, keepdims=True) for part in parts) / depth
            parts = [part - centre for part in parts]
            spread = sum(jnp.sum(part * part, axis=1, keepdims=True) for part in parts) / depth
            scaling = lax.rsqrt(spread + EPSILON)
            for step in range(tp):
                owner = lax.rem(place[0] - step + tp, tp)
                columns = pl.ds(pl.multiple_of(owner * width, width), width)
                low[at, columns] = (
                    parts[step] * scaling * gain[:, columns] + bias[:, columns]
                ).astype(BF16)
                full[at, columns] = blocks[step][at, :]

    product = dot(low[...], weight[...]) + weight_bias[...]
    groups = []
    for group in range(per):
        parts = []
        for part in range(3):
            first = (group * 3 + part) * piece
            values = product[:, first : first + piece]
            if part < 2:
                values = (
                    values * cosine[...]
                    + pltpu.roll(values, piece - ROT // 2, 1) * sine_up[...]
                    + pltpu.roll(values, ROT // 2, 1) * sine_down[...]
                )
            parts.append(values.astype(BF16))
        groups.append(parts)
    flip = lax.rem(place[1], per)
    for way, out in enumerate(outs):
        for group in range(per):

            @pl.when((step == way // per) & (jnp.bitwise_xor(group, flip) == way % per))
            def _():
                for part in range(3):
                    out[:, part * piece : (part + 1) * piece] = groups[group][part]


def project(blocks, place, gain, bias, weight, weight_bias, tables, nctx):
    tp = len(blocks)
    rows, width = tables[0].shape[0], blocks[0].shape[1]
    depth = tp * width
    total = weight.shape[1]
    wide = total // nctx
    per = 2 if nctx % 2 == 0 else 1
    grid_spec = pltpu.PrefetchScalarGridSpec(
        num_scalar_prefetch=1,
        grid=(nctx // per,),
        in_specs=[whole((rows, width))] * tp
        + [whole((1, depth))] * 2
        + [
            pl.BlockSpec((depth, per * wide), lambda i, s: (0, jnp.bitwise_xor(i, s[1] // per))),
            pl.BlockSpec((1, per * wide), lambda i, s: (0, jnp.bitwise_xor(i, s[1] // per))),
        ]
        + [whole((rows, 2 * HEAD_DIM))] * 3,
        out_specs=[whole((rows, depth))] * 2 + [whole((rows, wide))] * nctx,
    )
    return pl.pallas_call(
        functools.partial(project_kernel, tp, per),
        grid_spec=grid_spec,
        out_shape=[
            jax.ShapeDtypeStruct((rows, depth), BF16),
            jax.ShapeDtypeStruct((rows, depth), BF16),
        ]
        + [jax.ShapeDtypeStruct((rows, wide), BF16)] * nctx,
        compiler_params=params(),
        cost_estimate=takes(60),
        name="project",
    )(place, *blocks, gain, bias, weight, weight_bias, *tables)


def stack_heads(tile, heads):
    lane = lax.broadcasted_iota(jnp.int32, tile.shape, 1) // HEAD_DIM
    return jnp.concatenate(
        [jnp.where(lane == head, tile, jnp.zeros_like(tile)) for head in range(heads)], axis=0
    )


def fold_heads(stacked, heads, columns):
    row = lax.broadcasted_iota(jnp.int32, (stacked.shape[0], columns), 0) // HEAD_DIM
    folded = jnp.zeros((stacked.shape[0], columns), F32)
    for head in range(heads):
        folded = folded + jnp.where(row == head, stacked[:, head * columns : (head + 1) * columns], 0.0)
    return jnp.transpose(folded)


def load_pieces(place, pieces, nctx, held, block_rows):
    chunk_rows = pieces[0].shape[0]
    chunks = len(pieces) // nctx
    for chunk in range(chunks):
        for step in range(nctx):
            source = jnp.bitwise_xor(place, step)
            first = source * block_rows + chunk * chunk_rows
            held[pl.ds(pl.multiple_of(first, chunk_rows), chunk_rows), :] = pieces[
                chunk * nctx + step
            ][...]


def attend_kernel(nctx, heads, count, extra, block_rows, place, lows, ends, bounds, *refs):
    pieces = refs[:count]
    out, logs, held, turned, total, high, sums, raw, chances = refs[count + extra :]
    tile_q, tile_k = out.shape[0], turned.shape[2]
    width = heads * HEAD_DIM
    index = pl.program_id(0)

    @pl.when(index == 0)
    def _():
        load_pieces(place[0], pieces, nctx, held, block_rows)
        for tile in range(turned.shape[0]):
            turned[tile] = jnp.transpose(held[tile * tile_k : (tile + 1) * tile_k, 2 * width :])

    query_rows = pl.ds(pl.multiple_of(index * tile_q, tile_q), tile_q)
    queries = stack_heads(held[query_rows, :width] * jnp.asarray(HEAD_DIM**-0.5, BF16), heads)
    first_key = jnp.concatenate([bounds[0:1, :]] * heads, axis=1)
    last_key = jnp.concatenate([bounds[1:2, :]] * heads, axis=1)
    total[...] = jnp.zeros_like(total)
    high[...] = jnp.full_like(high, FLOOR)
    sums[...] = jnp.zeros_like(sums)

    def one(tile, _):
        start = tile * tile_k
        keys = held[pl.ds(pl.multiple_of(start, tile_k), tile_k), width : 2 * width]
        raw[...] = dot_turned(keys, queries)
        last = jnp.minimum(last_key, ends[tile] - 1) - start
        first = first_key - start
        peaks = jnp.broadcast_to(high[...], (8, raw.shape[1]))
        for begin in range(0, tile_k, STRIP):
            scores = raw[begin : begin + STRIP, :]
            row = lax.broadcasted_iota(jnp.int32, scores.shape, 0) + begin
            scores = jnp.where((row <= last) & (row >= first), scores, NEGATIVE)
            raw[begin : begin + STRIP, :] = scores
            for group in range(0, STRIP, 8):
                peaks = jnp.maximum(peaks, scores[group : group + 8])
        highest = jnp.max(peaks, axis=0, keepdims=True)
        partial = jnp.zeros((8, raw.shape[1]), F32)
        for begin in range(0, tile_k, STRIP):
            raised = jnp.exp(raw[begin : begin + STRIP, :] - highest)
            chances[begin : begin + STRIP, :] = raised.astype(BF16)
            for group in range(0, STRIP, 8):
                partial = partial + raised[group : group + 8]
        shrink = jnp.exp(high[...] - highest)
        sums[...] = sums[...] * shrink + jnp.sum(partial, axis=0, keepdims=True)
        total[...] = total[...] * shrink + dot(turned[tile], chances[...])
        high[...] = highest
        return 0

    upper = (index * tile_q + tile_q - 1) // tile_k + 1
    lax.fori_loop(lows[index], upper, one, 0)
    found = sums[...] > 0.0
    safe = jnp.where(found, sums[...], 1.0)
    out[...] = fold_heads(
        total[...] * jnp.where(found, 1.0 / safe, 0.0), heads, tile_q
    ).astype(BF16)
    log_total = jnp.where(found, high[...] + jnp.log(safe), 0.0)
    for head in range(heads):
        logs[head : head + 1, :] = log_total[:, head * tile_q : (head + 1) * tile_q]


def attend(pieces, place, lows, ends, bounds, nctx, block_rows, *needed):
    total_rows = nctx * block_rows
    width = pieces[0].shape[1] // 3
    heads = width // HEAD_DIM
    steps = total_rows // TILE_Q
    grid_spec = pltpu.PrefetchScalarGridSpec(
        num_scalar_prefetch=3,
        grid=(steps,),
        in_specs=[pl.BlockSpec((2, TILE_Q), lambda i, *_: (0, i))]
        + [whole(piece.shape) for piece in pieces]
        + anywhere(len(needed)),
        out_specs=[
            pl.BlockSpec((TILE_Q, width), lambda i, *_: (i, 0)),
            pl.BlockSpec((heads, TILE_Q), lambda i, *_: (0, i)),
        ],
        scratch_shapes=[
            pltpu.VMEM((total_rows, 3 * width), BF16),
            pltpu.VMEM((total_rows // TILE_K, width, TILE_K), BF16),
            pltpu.VMEM((width, heads * TILE_Q), F32),
            pltpu.VMEM((1, heads * TILE_Q), F32),
            pltpu.VMEM((1, heads * TILE_Q), F32),
            pltpu.VMEM((TILE_K, heads * TILE_Q), F32),
            pltpu.VMEM((TILE_K, heads * TILE_Q), BF16),
        ],
    )
    return pl.pallas_call(
        functools.partial(attend_kernel, nctx, heads, len(pieces), len(needed), block_rows),
        grid_spec=grid_spec,
        out_shape=[
            jax.ShapeDtypeStruct((total_rows, width), BF16),
            jax.ShapeDtypeStruct((heads, total_rows), F32),
        ],
        compiler_params=params(),
        cost_estimate=takes(200),
        name="attend",
    )(place, lows, ends, bounds, *pieces, *needed)


def attend_back_kernel(
    nctx, heads, count, extra, block_rows, place, lows, ends, bounds, logs, *refs
):
    pieces, refs = refs[:count], refs[count:]
    grad, attended, refs = refs[0], refs[1], refs[2 + extra :]
    outs, refs = refs[:count], refs[count:]
    held, turned, grad_keys, grad_values, grad_query, raw, raw_grad, chances, steps, merged = refs
    tile_q, tile_k = grad.shape[0], turned.shape[2]
    width = grad.shape[1]
    index = pl.program_id(0)
    scale = jnp.asarray(HEAD_DIM**-0.5, BF16)

    @pl.when(index == 0)
    def _():
        load_pieces(place[0], pieces, nctx, held, block_rows)
        for tile in range(turned.shape[0]):
            turned[tile] = jnp.transpose(
                held[tile * tile_k : (tile + 1) * tile_k, width : 2 * width]
            )
        grad_keys[...] = jnp.zeros_like(grad_keys)
        grad_values[...] = jnp.zeros_like(grad_values)

    query_rows = pl.ds(pl.multiple_of(index * tile_q, tile_q), tile_q)
    queries = stack_heads(held[query_rows, :width] * scale, heads)
    incoming = stack_heads(grad[...], heads)
    product = jnp.transpose(grad[...].astype(F32) * attended[...].astype(F32))
    centre = jnp.concatenate(
        [
            jnp.sum(product[head * HEAD_DIM : (head + 1) * HEAD_DIM, :], axis=0, keepdims=True)
            for head in range(heads)
        ],
        axis=1,
    )
    first_key = jnp.concatenate([bounds[0:1, :]] * heads, axis=1)
    last_key = jnp.concatenate([bounds[1:2, :]] * heads, axis=1)
    log_total = jnp.concatenate([logs[head : head + 1, :] for head in range(heads)], axis=1)
    grad_query[...] = jnp.zeros_like(grad_query)

    def one(tile, _):
        start = tile * tile_k
        key_rows = pl.ds(pl.multiple_of(start, tile_k), tile_k)
        raw[...] = dot_turned(held[key_rows, width : 2 * width], queries)
        raw_grad[...] = dot_turned(held[key_rows, 2 * width :], incoming)
        last = jnp.minimum(last_key, ends[tile] - 1) - start
        first = first_key - start
        for begin in range(0, tile_k, STRIP):
            at = slice(begin, begin + STRIP)
            row = lax.broadcasted_iota(jnp.int32, (STRIP, raw.shape[1]), 0) + begin
            allowed = (row <= last) & (row >= first)
            chance = jnp.exp(jnp.where(allowed, raw[at, :] - log_total, NEGATIVE))
            chances[at, :] = chance.astype(BF16)
            steps[at, :] = (chance * (raw_grad[at, :] - centre)).astype(BF16)
        grad_values[key_rows, :] += dot(chances[...], incoming)
        grad_keys[key_rows, :] += dot(steps[...], queries)
        grad_query[...] += dot(turned[tile], steps[...])
        return 0

    upper = (index * tile_q + tile_q - 1) // tile_k + 1
    lax.fori_loop(lows[index], upper, one, 0)
    merged[query_rows, :width] = (
        fold_heads(grad_query[...], heads, tile_q) * HEAD_DIM**-0.5
    ).astype(BF16)

    @pl.when(index == pl.num_programs(0) - 1)
    def _():
        merged[:, width : 2 * width] = grad_keys[...].astype(BF16)
        merged[:, 2 * width :] = grad_values[...].astype(BF16)
        chunk_rows = outs[0].shape[0]
        for chunk in range(count // nctx):
            for way in range(nctx):
                first = jnp.bitwise_xor(place[0], way) * block_rows + chunk * chunk_rows
                outs[chunk * nctx + way][...] = merged[
                    pl.ds(pl.multiple_of(first, chunk_rows), chunk_rows), :
                ]


def attend_back(pieces, place, lows, ends, bounds, logs, grad, attended, nctx, block_rows, *needed):
    total_rows, width = grad.shape
    heads = width // HEAD_DIM
    by_tile = pl.BlockSpec((TILE_Q, width), lambda i, *_: (i, 0))
    grid_spec = pltpu.PrefetchScalarGridSpec(
        num_scalar_prefetch=3,
        grid=(total_rows // TILE_Q,),
        in_specs=[
            pl.BlockSpec((2, TILE_Q), lambda i, *_: (0, i)),
            pl.BlockSpec((heads, TILE_Q), lambda i, *_: (0, i)),
        ]
        + [whole(piece.shape) for piece in pieces]
        + [by_tile] * 2
        + anywhere(len(needed)),
        out_specs=[whole(piece.shape) for piece in pieces],
        scratch_shapes=[
            pltpu.VMEM((total_rows, 3 * width), BF16),
            pltpu.VMEM((total_rows // TILE_K, width, TILE_K), BF16),
            pltpu.VMEM((total_rows, width), F32),
            pltpu.VMEM((total_rows, width), F32),
            pltpu.VMEM((width, heads * TILE_Q), F32),
            pltpu.VMEM((TILE_K, heads * TILE_Q), F32),
            pltpu.VMEM((TILE_K, heads * TILE_Q), F32),
            pltpu.VMEM((TILE_K, heads * TILE_Q), BF16),
            pltpu.VMEM((TILE_K, heads * TILE_Q), BF16),
            pltpu.VMEM((total_rows, 3 * width), BF16),
        ],
    )
    return pl.pallas_call(
        functools.partial(
            attend_back_kernel, nctx, heads, len(pieces), len(needed), block_rows
        ),
        grid_spec=grid_spec,
        out_shape=[jax.ShapeDtypeStruct(p.shape, BF16) for p in pieces],
        compiler_params=params(),
        cost_estimate=takes(250),
        name="attend_back",
    )(place, lows, ends, bounds, logs, *pieces, grad, attended, *needed)


def mix_kernel(nctx, count, place, heads_in, weight, source, gain, bias, *refs):
    returned, mixed, *lows = refs[count:]
    rows, depth = mixed.shape
    step = pl.program_id(0)
    left = jnp.concatenate([heads_in[c, 0] for c in range(nctx)], axis=1)
    returned[...] = left

    @pl.when(step == 0)
    def _():
        mixed[...] = source[...].astype(F32)

    mixed[...] += dot_turned(left, weight[0])

    @pl.when(step == pl.num_programs(0) - 1)
    def _():
        values = mixed[...]
        values = values - jnp.mean(values, axis=1, keepdims=True)
        scaling = lax.rsqrt(jnp.mean(values * values, axis=1, keepdims=True) + EPSILON)
        values = (values * scaling * gain[...] + bias[...]).astype(BF16)
        part_rows = lows[0].shape[0]
        for part, low in enumerate(lows):
            low[...] = values[part * part_rows : (part + 1) * part_rows]


def mix(heads_in, weight, full, gain, bias, place, parts, *needed):
    nctx, tp, rows, piece = heads_in.shape
    depth = full.shape[1]
    head_width = nctx * piece
    grid_spec = pltpu.PrefetchScalarGridSpec(
        num_scalar_prefetch=1,
        grid=(tp,),
        in_specs=[
            pl.BlockSpec((nctx, 1, rows, piece), lambda k, s: (0, k, 0, 0)),
            pl.BlockSpec((1, depth, head_width), lambda k, s: (k, 0, 0)),
            pl.BlockSpec((rows, depth), lambda k, s: (s[0], 0)),
            whole((1, depth)),
            whole((1, depth)),
        ]
        + anywhere(len(needed)),
        out_specs=[
            pl.BlockSpec((rows, head_width), lambda k, s: (0, k)),
            whole((rows, depth)),
        ]
        + [whole((rows // parts, depth))] * parts,
    )
    return pl.pallas_call(
        functools.partial(mix_kernel, nctx, len(needed)),
        grid_spec=grid_spec,
        out_shape=[
            jax.ShapeDtypeStruct((rows, tp * head_width), BF16),
            jax.ShapeDtypeStruct((rows, depth), F32),
        ]
        + [jax.ShapeDtypeStruct((rows // parts, depth), BF16)] * parts,
        compiler_params=params(),
        cost_estimate=takes(50),
        name="mix",
    )(place, heads_in, weight, full, gain, bias, *needed)


def feed_kernel(cuts, parts, tp, first_one, place, *refs):
    lows, cot, mixed, source = refs[:parts], refs[parts], refs[parts + 1], refs[parts + 2]
    refs = refs[-(5 + parts + 4) :]
    kept, hidden, grad_gate, grad_up, out = refs[:5]
    partials, held, sems = refs[5 : 5 + parts], refs[-4:-1], refs[-1]
    unit = source.shape[1] // 3
    width = out.shape[2]

    def copies(index):
        first, size = cuts[index]
        at = pl.ds(first, size)
        return [
            pltpu.make_async_copy(
                source.at[:, pl.ds(which * unit, unit), at],
                held[which].at[:, :, at],
                sems.at[index * 3 + which],
            )
            for which in range(3)
        ]

    for index in range(len(cuts)):
        for copy in copies(index):
            copy.start()
    rows = lows[0].shape[0]
    for part in range(parts):
        kept[part * rows : (part + 1) * rows] = lows[part][...]
    depth = kept.shape[1]
    grads = jnp.concatenate([cot[block] for block in range(tp)], axis=1)
    for index, (first, size) in enumerate(cuts):
        for copy in copies(index):
            copy.wait()
        at = slice(first, first + size)
        gate_weight, up_weight, down_weight = [w[:, :, at].reshape(depth, size) for w in held]
        gate = dot(kept[...], gate_weight)
        up = dot(kept[...], up_weight)
        sigma = 1.0 / (1.0 + jnp.exp(-gate))
        active = gate * sigma
        hidden[:, at] = (active * up).astype(BF16)
        grad = dot(grads, down_weight)
        grad_gate[:, at] = (grad * up * sigma * (1.0 + gate * (1.0 - sigma))).astype(BF16)
        grad_up[:, at] = (grad * active).astype(BF16)
    gate_weight, up_weight, down_weight = [w[...].reshape(depth, w.shape[2]) for w in held]
    product = dot_turned(grad_gate[...], gate_weight) + dot_turned(grad_up[...], up_weight)
    for part in range(parts):
        partials[part][...] = product[part * rows : (part + 1) * rows].astype(BF16)
    values = dot_turned(hidden[...], down_weight)
    if first_one:
        values = values + mixed[...]
    for block in range(tp):
        out[block] = values[:, block * width : (block + 1) * width].astype(BF16)


def feed(lows, cot, mixed, weights, step, tp, place, held, *needed):
    parts = len(lows)
    part_rows, depth = lows[0].shape
    rows = parts * part_rows
    blocks, triple, hidden = weights.shape
    cuts = []
    while sum(size for _, size in cuts) < hidden:
        first = sum(size for _, size in cuts)
        cuts.append((first, min(512, hidden - first)))
    by_owner = lambda columns: pl.BlockSpec(
        (rows, columns), lambda i, s: (lax.rem(s[0] - step + tp, tp), 0)
    )
    width = depth // tp
    blocks_of_owner = pl.BlockSpec(
        (tp, rows, width), lambda i, s: (0, lax.rem(s[0] - step + tp, tp), 0)
    )
    grid_spec = pltpu.PrefetchScalarGridSpec(
        num_scalar_prefetch=1,
        grid=(1,),
        in_specs=[whole((part_rows, depth))] * parts
        + [blocks_of_owner, whole(mixed.shape)]
        + anywhere(1 + len(held) + len(needed)),
        out_specs=[by_owner(depth)]
        + [by_owner(hidden)] * 3
        + [blocks_of_owner]
        + [whole((part_rows, depth))] * parts,
        scratch_shapes=[pltpu.VMEM((blocks, triple // 3, hidden), BF16)] * 3
        + [pltpu.SemaphoreType.DMA((3 * len(cuts),))],
    )
    return pl.pallas_call(
        functools.partial(feed_kernel, tuple(cuts), parts, tp, step == 0),
        grid_spec=grid_spec,
        out_shape=[jax.ShapeDtypeStruct((tp * rows, depth), BF16)]
        + [jax.ShapeDtypeStruct((tp * rows, hidden), BF16)] * 3
        + [jax.ShapeDtypeStruct((tp, tp * rows, width), BF16)]
        + [jax.ShapeDtypeStruct((part_rows, depth), BF16)] * parts,
        input_output_aliases={4 + parts + index: index for index in range(len(held))},
        compiler_params=params(),
        cost_estimate=takes(100),
        name="feed",
    )(place, *lows, cot, mixed, weights, *held, *needed)


def blame(left, right, which, pick_left, unit, arrived, needed, buffer=None, slot=0, slots=1):
    rows = left.shape[0]
    side = left if pick_left else right
    picked = side.size // side.shape[-2] // unit // 2
    other = (right if pick_left else left).shape[1]
    if side.ndim == 3:
        per = side.shape[2] // unit
        chosen = pl.BlockSpec(
            (1, rows, unit), lambda j, s: ((2 * j + s[0]) // per, 0, lax.rem(2 * j + s[0], per))
        )
    else:
        chosen = pl.BlockSpec((rows, unit), lambda j, s: (0, 2 * j + s[0]))
    kept = whole((rows, other))
    if pick_left:
        shape = (slots * picked * unit, other)
        target = pl.BlockSpec((unit, other), lambda j, s: (slots * j + slot, 0))
        source = pl.BlockSpec((unit, other), lambda j, s: (j, 0))
    else:
        shape = (other, picked * unit)
        target = source = pl.BlockSpec((other, unit), lambda j, s: (0, j))
    extra = [] if arrived is None else [arrived]
    held = [] if buffer is None else [buffer]

    def kernel(which, left, right, *refs):
        ours, theirs = left[...], right[...]
        if side.ndim == 3:
            theirs = theirs[0]
        product = lax.dot_general(
            ours, theirs, (((0,), (0,)), ((), ())), preferred_element_type=F32
        )
        if extra:
            product = product + refs[0][...].astype(F32)
        refs[-1][...] = product.astype(BF16)

    grid_spec = pltpu.PrefetchScalarGridSpec(
        num_scalar_prefetch=1,
        grid=(picked,),
        in_specs=([chosen, kept] if pick_left else [kept, chosen])
        + [source] * len(extra)
        + anywhere(len(held) + len(needed)),
        out_specs=target,
    )
    return pl.pallas_call(
        kernel,
        grid_spec=grid_spec,
        out_shape=jax.ShapeDtypeStruct(shape, BF16),
        input_output_aliases={3 + len(extra): 0} if held else {},
        compiler_params=params(),
        cost_estimate=takes(30),
        name="blame",
    )(which, left, right, *extra, *held, *needed)


def turn_kernel(nctx, count, parts, place, *refs):
    arrived, own = refs[:parts], refs[parts : 2 * parts]
    mixed, cot, gain = refs[2 * parts : 2 * parts + 3]
    weight, refs = refs[2 * parts + 3], refs[2 * parts + 4 + count :]
    out, grad_mixed, grad_low, gain_grad, shift_grad = refs
    rows, depth = mixed.shape
    piece = out.shape[3]

    @pl.when(pl.program_id(0) == 0)
    def _():
        incoming = jnp.concatenate(
            [there[...].astype(F32) + here[...].astype(F32) for there, here in zip(arrived, own)]
        )
        values = mixed[...]
        values = values - jnp.mean(values, axis=1, keepdims=True)
        scaling = lax.rsqrt(jnp.mean(values * values, axis=1, keepdims=True) + EPSILON)
        normed = values * scaling
        shift_grad[...] = jnp.sum(incoming, axis=0, keepdims=True)
        gain_grad[...] = jnp.sum(incoming * normed, axis=0, keepdims=True)
        scaled = incoming * gain[...]
        grads = jnp.concatenate([cot[block] for block in range(cot.shape[0])], axis=1)
        total = grads.astype(F32) + scaling * (
            scaled
            - jnp.mean(scaled, axis=1, keepdims=True)
            - normed * jnp.mean(scaled * normed, axis=1, keepdims=True)
        )
        grad_mixed[...] = total
        grad_low[...] = total.astype(BF16)

    product = dot(grad_low[...], weight[0])
    for c in range(nctx):
        out[c, 0] = product[:, c * piece : (c + 1) * piece].astype(BF16)


def turn(arrived, own, mixed, cot, gain, weight, place, nctx, tp, *needed):
    rows, depth = mixed.shape
    parts = len(arrived)
    head_width = weight.shape[2]
    piece = head_width // nctx
    grid_spec = pltpu.PrefetchScalarGridSpec(
        num_scalar_prefetch=1,
        grid=(tp,),
        in_specs=[whole((rows // parts, depth))] * (2 * parts)
        + [whole((rows, depth))]
        + [
            pl.BlockSpec((tp, rows, depth // tp), lambda k, s: (0, s[0], 0)),
            whole((1, depth)),
            pl.BlockSpec((1, depth, head_width), lambda k, s: (k, 0, 0)),
        ]
        + anywhere(len(needed)),
        out_specs=[
            pl.BlockSpec((nctx, 1, rows, piece), lambda k, s: (0, k, 0, 0)),
            whole((rows, depth)),
            whole((rows, depth)),
            whole((1, depth)),
            whole((1, depth)),
        ],
    )
    return pl.pallas_call(
        functools.partial(turn_kernel, nctx, len(needed), parts),
        grid_spec=grid_spec,
        out_shape=[
            jax.ShapeDtypeStruct((nctx, tp, rows, piece), BF16),
            jax.ShapeDtypeStruct((rows, depth), F32),
            jax.ShapeDtypeStruct((rows, depth), BF16),
            jax.ShapeDtypeStruct((1, depth), F32),
            jax.ShapeDtypeStruct((1, depth), F32),
        ],
        compiler_params=params(),
        cost_estimate=takes(60),
        name="turn",
    )(place, *arrived, *own, mixed, cot, gain, weight, *needed)


def finish_kernel(nctx, tp, extra_count, chunk, place, *refs):
    pieces = refs[:nctx]
    cosine, sine_up, sine_down, full, extra, gain = refs[nctx : nctx + 6]
    weight, refs = refs[nctx + 6], refs[nctx + 7 + extra_count :]
    outs = refs[:tp]
    low, bias_grad, gain_grad, shift_grad, spare = refs[tp:]
    rows, wide = pieces[0].shape
    piece = wide // 3
    width = outs[0].shape[1]
    strip = spare.shape[0]
    extra_rows = extra.shape[0]

    @pl.when(pl.program_id(0) == 0)
    def _():
        bias_grad[...] = jnp.zeros_like(bias_grad)
        gain_grad[...] = jnp.zeros_like(gain_grad)
        shift_grad[...] = jnp.zeros_like(shift_grad)

    for step in range(nctx):
        source = jnp.bitwise_xor(place[1], step)
        for part in range(3):
            values = pieces[step][:, part * piece : (part + 1) * piece].astype(F32)
            if part < 2:
                values = (
                    values * cosine[...]
                    - pltpu.roll(values, piece - ROT // 2, 1) * sine_up[...]
                    - pltpu.roll(values, ROT // 2, 1) * sine_down[...]
                )
            columns = pl.ds(pl.multiple_of(source * wide + part * piece, piece), piece)
            bias_grad[:, columns] += jnp.sum(values, axis=0, keepdims=True)
            low[:, columns] = values.astype(BF16)

    incoming = dot_turned(low[...], weight[...])
    source = full[...].astype(F32)
    source = source - jnp.mean(source, axis=1, keepdims=True)
    scaling = lax.rsqrt(jnp.mean(source * source, axis=1, keepdims=True) + EPSILON)
    normed = source * scaling
    shift_grad[...] += jnp.sum(incoming, axis=0, keepdims=True)
    gain_grad[...] += jnp.sum(incoming * normed, axis=0, keepdims=True)
    scaled = incoming * gain[...]
    spare[...] = scaling * (
        scaled
        - jnp.mean(scaled, axis=1, keepdims=True)
        - normed * jnp.mean(scaled * normed, axis=1, keepdims=True)
    )
    first = chunk * pl.num_programs(0) * strip + pl.program_id(0) * strip
    wanted = place[0] * extra_rows

    if strip <= extra_rows:

        @pl.when((first >= wanted) & (first < wanted + extra_rows))
        def _():
            spare[...] += extra[pl.ds(pl.multiple_of(first - wanted, strip), strip), :]

    else:

        @pl.when((wanted >= first) & (wanted < first + strip))
        def _():
            spare[pl.ds(pl.multiple_of(wanted - first, extra_rows), extra_rows), :] += extra[...]

    for step, out in enumerate(outs):
        owner = lax.rem(place[0] - step + tp, tp)
        out[...] = spare[:, pl.ds(pl.multiple_of(owner * width, width), width)].astype(BF16)


def finish(pieces, place, tables, full, extra, gain, weight, chunk, tp, *needed):
    rows, wide = pieces[0].shape
    depth = full.shape[1]
    total = weight.shape[1]
    strip = 256
    steps = rows // strip
    width = depth // tp
    nctx = len(pieces)
    by_rows = lambda columns: pl.BlockSpec((strip, columns), lambda i, s: (i, 0))
    grid_spec = pltpu.PrefetchScalarGridSpec(
        num_scalar_prefetch=1,
        grid=(steps,),
        in_specs=[by_rows(wide)] * nctx
        + [by_rows(2 * HEAD_DIM)] * 3
        + [
            pl.BlockSpec((strip, depth), lambda i, s: (i + chunk * steps, 0)),
            whole(extra.shape),
            whole((1, depth)),
        ]
        + [whole(weight.shape)]
        + anywhere(len(needed)),
        out_specs=[by_rows(width)] * tp
        + [
            by_rows(total),
            whole((1, total)),
            whole((1, depth)),
            whole((1, depth)),
        ],
        scratch_shapes=[pltpu.VMEM((strip, depth), F32)],
    )
    return pl.pallas_call(
        functools.partial(finish_kernel, nctx, tp, len(needed), chunk),
        grid_spec=grid_spec,
        out_shape=[jax.ShapeDtypeStruct((rows, width), BF16)] * tp
        + [
            jax.ShapeDtypeStruct((rows, total), BF16),
            jax.ShapeDtypeStruct((1, total), F32),
            jax.ShapeDtypeStruct((1, depth), F32),
            jax.ShapeDtypeStruct((1, depth), F32),
        ],
        compiler_params=params(),
        cost_estimate=takes(70),
        name="finish",
    )(place, *pieces, *tables, full, extra, gain, weight, *needed)


def pack_kernel(gate, up, down, out):
    rows = gate.shape[0]
    out[:rows] = gate[...]
    out[rows : 2 * rows] = up[...]
    out[2 * rows :] = jnp.transpose(down[...])


def pack(gate, up, down):
    rows, columns = gate.shape
    return pl.pallas_call(
        pack_kernel,
        out_shape=jax.ShapeDtypeStruct((3 * rows, columns), BF16),
        compiler_params=params(),
        cost_estimate=takes(10),
        name="pack",
    )(gate, up, down)


def contract_rows(left, right):
    return lax.dot_general(left, right, (((0,), (0,)), ((), ())), preferred_element_type=F32)


def pick(stack, index):
    return lax.dynamic_index_in_dim(stack, index, 0, keepdims=False)


def shards(
    nfsdp,
    nctx,
    tp,
    inputs,
    cotangent,
    first_gain,
    first_bias,
    qkv_weight,
    qkv_bias,
    out_weight,
    second_gain,
    second_bias,
    gate_weight,
    up_weight,
    down_weight,
    lengths,
    fill_counts,
):
    data = ("fsdp", "ctx")
    ndata = nfsdp * nctx
    block_rows, width = inputs.shape
    depth = tp * width
    half_depth = depth // 2
    unit = depth // ndata
    tensor_index = lax.axis_index("tp").astype(jnp.int32)
    context_index = lax.axis_index("ctx").astype(jnp.int32)
    fsdp_index = lax.axis_index("fsdp").astype(jnp.int32)
    part_rows = block_rows // tp
    chunk_rows = block_rows // CHUNKS
    head_width = qkv_weight.shape[2]
    piece = head_width // nctx
    wide = 3 * piece

    square = nfsdp == 2 and nctx == 4 and unit % 128 == 0
    place = jnp.stack([tensor_index, context_index, fsdp_index])

    def shift(value, step):
        return lax.ppermute(value, "tp", [(i, (i + step) % tp) for i in range(tp)])

    def swap(value, step):
        return lax.ppermute(value, "ctx", [(i, i ^ step) for i in range(nctx)])

    core_index = context_index % 2
    groups = [list(range(0, ndata, 2)), list(range(1, ndata, 2))]
    own_half, other_half = core_index[None], (1 - core_index)[None]

    def partner(left, right, pick_left, *needed):
        first = blame(left, right, other_half, pick_left, unit, None, needed)
        return first, swap(first, 1)

    def own(left, right, pick_left, arrived, *needed, **buffer):
        return blame(left, right, own_half, pick_left, unit, arrived, needed, **buffer)

    def scatter_half(value, axis):
        return lax.psum_scatter(
            value, data, scatter_dimension=axis, tiled=True, axis_index_groups=groups
        )

    def exchange_sum(half):
        blocks = half.reshape(ndata // 2, unit, half.shape[1])
        blocks = lax.all_to_all(
            blocks, data, split_axis=0, concat_axis=0, tiled=True, axis_index_groups=groups
        )
        return jnp.sum(blocks.astype(F32), axis=0)

    def scatter_whole(left, right, axis):
        return lax.psum_scatter(
            contract_rows(left, right).astype(BF16), data, scatter_dimension=axis, tiled=True
        )

    def total(left, right):
        return (left.astype(F32) + right.astype(F32)).astype(BF16)

    owners = [(tensor_index - step + tp) % tp for step in range(tp)]

    own_qkv = (
        qkv_weight.reshape(-1, 3, nctx, piece).transpose(0, 2, 1, 3).reshape(-1, 3 * head_width)
    )
    full_qkv = lax.all_gather(own_qkv, data, axis=0, tiled=True)
    own_feed = pack(gate_weight, up_weight, down_weight)
    feed_weights = lax.all_gather(own_feed, data, axis=0, tiled=True).reshape(ndata, 3 * unit, -1)

    validity, position, first_key, last_key = layout(lengths[0], fill_counts[0], block_rows)
    own_position = lax.dynamic_slice_in_dim(position, context_index * block_rows, block_rows, 0)
    tables = rotary_tables(own_position)
    bounds = jnp.stack([first_key, last_key])
    tile_first = first_key[::TILE_Q]
    tile_count = tile_first.shape[0]
    lows = jnp.where(validity[::TILE_Q], tile_first // TILE_K, tile_count * TILE_Q).astype(jnp.int32)
    key_block = jnp.arange(0, nctx * block_rows, TILE_K, dtype=jnp.int32) // block_rows
    ends = (
        key_block * block_rows
        + jnp.sum(
            jnp.where(
                key_block[:, None] == jnp.arange(nctx, dtype=jnp.int32)[None, :],
                fill_counts[0][None, :],
                0,
            ),
            axis=1,
        )
    ).astype(jnp.int32)

    flat_bias = qkv_bias.reshape(3, nctx, piece).transpose(1, 0, 2).reshape(1, -1)
    gain_one, bias_one = first_gain[None], first_bias[None]
    gain_two, bias_two = second_gain[None], second_bias[None]

    rings = [[inputs[c * chunk_rows : (c + 1) * chunk_rows]] for c in range(CHUNKS)]
    share = unit // CHUNKS
    for chunk in range(CHUNKS):
        carried = out_weight.T[chunk * share : (chunk + 1) * share]
        rings[chunk][0] = tie(jnp.concatenate([rings[chunk][0], carried], axis=0), own_feed)
    for chunk in range(CHUNKS):
        for _ in range(tp - 1):
            rings[chunk].append(shift(rings[chunk][-1], 1))
    stack = jnp.zeros((tp, unit, head_width), BF16)
    for step in range(tp):
        carried = jnp.concatenate([blocks[step][chunk_rows:] for blocks in rings], axis=0)
        stack = lax.dynamic_update_index_in_dim(stack, carried, owners[step], 0)
    lows_one, fulls, pieces, chunk_tables = [], [], [], []
    for chunk in range(CHUNKS):
        at = slice(chunk * chunk_rows, (chunk + 1) * chunk_rows)
        chunk_tables.append([table[at] for table in tables])
        low, full, *outgoing = project(
            rings[chunk],
            place,
            gain_one,
            bias_one,
            full_qkv,
            flat_bias,
            chunk_tables[chunk],
            nctx,
        )
        lows_one.append(low)
        fulls.append(full)
        pieces.append(outgoing[0])
        for way in range(1, nctx):
            pieces.append(swap(outgoing[way], way))
    full = jnp.concatenate(fulls, axis=0)

    full_out = lax.all_gather(tie(stack, outgoing[0]), data, axis=1, tiled=True)
    cot = tie(cotangent, *[blocks[-1] for blocks in rings])
    cot = lax.all_to_all(
        jnp.broadcast_to(cot[None], (tp, block_rows, width)),
        "tp",
        split_axis=0,
        concat_axis=0,
        tiled=True,
    )

    attended, logs = attend(
        pieces,
        place[1:2],
        lows,
        ends,
        bounds,
        nctx,
        block_rows,
    )
    arrived = lax.all_to_all(
        attended.reshape(nctx * tp, part_rows, piece),
        ("ctx", "tp"),
        split_axis=0,
        concat_axis=0,
        tiled=True,
    )
    returned, mixed, *second_low = mix(
        arrived.reshape(nctx, tp, part_rows, piece),
        full_out,
        full,
        gain_two,
        bias_two,
        place,
        HALVES,
        feed_weights,
    )

    arrived, held, partials, travelling = second_low, [], [], None
    for step in range(tp):
        coming = [shift(value, 1) for value in arrived] if step < tp - 1 else None
        needed = travelling if step == tp - 1 and step > 2 else []
        *held, first, second = feed(
            arrived, cot, mixed, feed_weights, step, tp, place, held, *needed
        )
        partials.append([first, second])
        if step == 1 % tp:
            travelling = partials[step]
        elif step > 1:
            travelling = [
                total(shift(value, 1), kept) for value, kept in zip(travelling, partials[step])
            ]
        if step == 0 and coming is not None:
            coming = [tie(value, partials[0][0]) for value in coming]
        arrived = coming
    all_second, hidden, all_gate, all_up, feedforward = held

    needed = []
    if square:
        gate_first, gate_arrived = partner(all_second, all_gate, True, *travelling)
        up_first, up_arrived = partner(all_second, all_up, True, *travelling)
        needed = [gate_first, up_first]
    else:
        total_gate = scatter_whole(all_second, all_gate, 0)
        total_up = scatter_whole(all_second, all_up, 0)

    grad_heads, grad_mixed, mixed_low, gain_grad_two, shift_grad_two = turn(
        [shift(value, 1) for value in travelling],
        partials[0],
        mixed,
        cot,
        gain_two,
        full_out,
        place,
        nctx,
        tp,
        *needed,
    )
    grad_heads = lax.all_to_all(
        grad_heads.reshape(nctx * tp, part_rows, piece),
        ("ctx", "tp"),
        split_axis=0,
        concat_axis=0,
        tiled=True,
    ).reshape(nctx * block_rows, piece)

    needed = []
    flat_cot = jnp.swapaxes(cot, 0, 1).reshape(block_rows, depth)
    if square:
        pair = own(all_second, all_gate, True, gate_arrived, mixed_low, slot=0, slots=2)
        pair = own(all_second, all_up, True, up_arrived, buffer=pair, slot=1, slots=2)
        out_first, out_arrived = partner(mixed_low, returned, True)
        down_first, down_arrived = partner(hidden, cot, False, mixed_low)
        needed = [pair, out_first, down_first]
        pair = scatter_half(pair, 0)
        total_gate, total_up = pair[:unit], pair[unit:]
    else:
        total_out = scatter_whole(mixed_low, returned, 0)
        total_down = scatter_whole(hidden, flat_cot, 1)

    layer_out = lax.all_to_all(
        tie(feedforward, grad_heads), "tp", split_axis=0, concat_axis=0, tiled=True
    )
    layer_out = jnp.sum(layer_out.astype(F32), axis=0).astype(BF16)

    grad_pieces = attend_back(
        pieces, place[1:2], lows, ends, bounds, logs, grad_heads, attended, nctx, block_rows, *needed
    )
    needed = []
    if square:
        half_out = own(mixed_low, returned, True, out_arrived, grad_pieces[0])
        half_down = own(hidden, cot, False, down_arrived, grad_pieces[0])
        needed = [half_out, half_down]
        total_down = scatter_half(half_down, 1)
    grad_lows, bias_grads, gain_grads, shift_grads, grad_rows = [], [], [], [], []
    ring_steps = []
    for chunk in range(CHUNKS):
        outgoing = grad_pieces[chunk * nctx : (chunk + 1) * nctx]
        arrived = [outgoing[0]] + [swap(outgoing[way], way) for way in range(1, nctx)]
        *partial, low, bias_grad, gain_grad, shift_grad = finish(
            arrived,
            place,
            chunk_tables[chunk],
            full,
            grad_mixed,
            gain_one,
            full_qkv,
            chunk,
            tp,
            *(needed if chunk == CHUNKS - 1 else []),
        )
        grad_lows.append(low)
        bias_grads.append(bias_grad)
        gain_grads.append(gain_grad)
        shift_grads.append(shift_grad)
        travelling = partial[1 % tp]
        for step in range(1, tp):
            travelling = total(shift(travelling, 1), partial[(step + 1) % tp])
            ring_steps.append(travelling)
        grad_rows.append(travelling)
    grad_inputs = jnp.concatenate(grad_rows, axis=0)

    all_low, all_grad = jnp.concatenate(lows_one, axis=0), jnp.concatenate(grad_lows, axis=0)
    if square:
        first, qkv_arrived = partner(all_low, all_grad, True, *ring_steps[:1])
        half_qkv = own(all_low, all_grad, True, qkv_arrived, *ring_steps[tp - 1 : tp])
        total_qkv = exchange_sum(half_qkv)
        total_out = exchange_sum(tie(half_out, arrived[-1]))
    else:
        total_qkv = scatter_whole(all_low, all_grad, 0).astype(F32)
    total_qkv = (
        total_qkv
        .reshape(-1, nctx, 3, piece)
        .transpose(0, 2, 1, 3)
        .reshape(-1, 3, head_width)
    )

    def exchange(value, axis, size):
        moved = [
            lax.ppermute(value, axis, [(i, i ^ step) for i in range(size)])
            for step in range(1, size)
        ]
        return sum(moved, value)

    out_parts = jnp.swapaxes(total_out.astype(BF16).reshape(-1, tp, head_width), 0, 1)
    total_out = pick(out_parts, tensor_index).astype(F32)
    for step in range(1, tp):
        total_out = total_out + shift(pick(out_parts, (tensor_index + step) % tp), step).astype(F32)
    total_out = total_out.T

    small = jnp.concatenate([sum(gain_grads), sum(shift_grads), gain_grad_two, shift_grad_two], axis=1)
    small = jnp.concatenate([sum(bias_grads), small], axis=1)
    small = tie(small, *ring_steps[1:2], *ring_steps[tp - 1 : tp])
    small = exchange(exchange(small, "ctx", nctx), "fsdp", nfsdp)
    bias_total, small = small[:, : 3 * head_width], small[:, 3 * head_width :]
    small = exchange(small, "tp", tp)
    bias_total = bias_total.reshape(nctx, 3, piece).transpose(1, 0, 2).reshape(3, head_width)
    small = small.reshape(4, depth)
    return (
        layer_out,
        grad_inputs,
        small[0],
        small[1],
        total_qkv,
        bias_total,
        total_out,
        small[2],
        small[3],
        total_gate.astype(F32),
        total_up.astype(F32),
        total_down.astype(F32),
    )


def solution(mesh):
    data = ("fsdp", "ctx")
    by_rows = P(data, "tp")
    by_columns = P("tp", data)
    qkv = P(data, None, "tp")
    return jax.shard_map(
        functools.partial(shards, mesh.shape["fsdp"], mesh.shape["ctx"], mesh.shape["tp"]),
        mesh=mesh,
        in_specs=(
            by_rows,
            by_rows,
            P(),
            P(),
            qkv,
            P(None, "tp"),
            by_columns,
            P(),
            P(),
            by_rows,
            by_rows,
            by_columns,
            P("fsdp", None),
            P("fsdp", None),
        ),
        out_specs=(
            by_rows,
            by_rows,
            P(),
            P(),
            qkv,
            P(None, "tp"),
            by_columns,
            P(),
            P(),
            by_rows,
            by_rows,
            by_columns,
        ),
        check_vma=False,
    )
```

```python
import functools

import jax
import jax.numpy as jnp
from jax import lax
from jax.experimental import pallas as pl
from jax.experimental.pallas import tpu as pltpu
from jax.sharding import PartitionSpec as P

HEAD_DIM = 64
ROT = 16
EPSILON = 1e-05
NEGATIVE = -1e30
FLOOR = -1e20
VMEM_LIMIT = 56 * 1024 * 1024
TILE_Q = 512
TILE_K = 512
STRIP = 32
CHUNKS = 2
HALVES = 2

F32 = jnp.float32
BF16 = jnp.bfloat16


def layout(lengths, fill_counts, block_rows):
    blocks_count = fill_counts.shape[0]
    seq_count = lengths.shape[0]
    slot_index = jnp.arange(blocks_count * block_rows, dtype=jnp.int32)
    block_of = slot_index // block_rows
    within = slot_index - block_of * block_rows
    chooser = block_of[:, None] == jnp.arange(blocks_count, dtype=jnp.int32)[None, :]
    fill_here = jnp.sum(jnp.where(chooser, fill_counts[None, :], 0), axis=1)
    before = jnp.cumsum(fill_counts) - fill_counts
    before_here = jnp.sum(jnp.where(chooser, before[None, :], 0), axis=1)
    validity = within < fill_here
    used_index = before_here + within
    seq_ends = jnp.cumsum(lengths)
    sequence = jnp.sum((used_index[:, None] >= seq_ends[None, :]).astype(jnp.int32), axis=1)
    seq_starts = seq_ends - lengths
    picker = sequence[:, None] == jnp.arange(seq_count, dtype=jnp.int32)[None, :]
    start_here = jnp.sum(jnp.where(picker, seq_starts[None, :], 0), axis=1)
    after = before + fill_counts
    start_block = jnp.sum((seq_starts[:, None] >= after[None, :]).astype(jnp.int32), axis=1)
    start_block = jnp.minimum(start_block, blocks_count - 1)
    block_pick = start_block[:, None] == jnp.arange(blocks_count, dtype=jnp.int32)[None, :]
    start_before = jnp.sum(jnp.where(block_pick, before[None, :], 0), axis=1)
    start_slot = start_block * block_rows + seq_starts - start_before
    slot_here = jnp.sum(jnp.where(picker, start_slot[None, :], 0), axis=1)
    first_key = jnp.where(validity, slot_here, 0).astype(jnp.int32)
    last_key = jnp.where(validity, slot_index, -1).astype(jnp.int32)
    return (validity, used_index - start_here, first_key, last_key)


def rotary_tables(position):
    half = ROT // 2
    lane = jnp.arange(2 * HEAD_DIM, dtype=jnp.int32) % HEAD_DIM
    frequency = 10000.0 ** (-(2.0 * (lane % half).astype(F32)) / ROT)
    angles = position.astype(F32)[:, None] * frequency[None, :]
    cosine, sine = jnp.cos(angles), jnp.sin(angles)
    lane = lane[None, :]
    return (
        jnp.where(lane < ROT, cosine, 1.0),
        jnp.where(lane < half, -sine, 0.0),
        jnp.where((lane >= half) & (lane < ROT), sine, 0.0),
    )


def params(**extra):
    return pltpu.CompilerParams(vmem_limit_bytes=VMEM_LIMIT, **extra)


def takes(microseconds):
    return pl.CostEstimate(
        flops=int(microseconds * 1e8), bytes_accessed=0, transcendentals=0
    )


def whole(shape):
    return pl.BlockSpec(shape, lambda *_: (0,) * len(shape))


def anywhere(count):
    return [pl.BlockSpec(memory_space=pl.ANY)] * count


def dot(left, right):
    return jnp.dot(left, right, preferred_element_type=F32)


def dot_turned(left, right):
    return lax.dot_general(left, right, (((1,), (1,)), ((), ())), preferred_element_type=F32)


def tie(value, *needed):
    def kernel(*refs):
        del refs

    return pl.pallas_call(
        kernel,
        in_specs=anywhere(1 + len(needed)),
        out_specs=pl.BlockSpec(memory_space=pl.ANY),
        out_shape=jax.ShapeDtypeStruct(value.shape, value.dtype),
        input_output_aliases={0: 0},
        name="tie",
    )(value, *needed)


def add_kernel(left, right, *refs):
    refs[-1][...] = (left[...].astype(F32) + right[...].astype(F32)).astype(BF16)


def add(left, right, *needed):
    rows, columns = left.shape
    strip = min(rows, 128)
    block = pl.BlockSpec((strip, columns), lambda i: (i, 0))
    return pl.pallas_call(
        add_kernel,
        grid=(rows // strip,),
        in_specs=[block, block] + anywhere(len(needed)),
        out_specs=block,
        out_shape=jax.ShapeDtypeStruct(left.shape, BF16),
        compiler_params=params(),
        cost_estimate=takes(10),
        name="ring_add",
    )(left, right, *needed)


def project_kernel(tp, chunks, per, place, *refs):
    rings, refs = refs[: tp * chunks], refs[tp * chunks :]
    gain, bias, weight, weight_bias, cosine, sine_up, sine_down, low, full, *outs = refs
    rows, width = low.shape[0] // chunks, rings[0].shape[1]
    depth = tp * width
    wide = outs[0].shape[1]
    piece = wide // 3
    step = pl.program_id(0)

    @pl.when(pl.program_id(0) == 0)
    def _():
        strip = 128
        for start in range(0, rows * chunks, strip):
            chunk, first = start // rows, start % rows
            blocks = rings[chunk * tp : (chunk + 1) * tp]
            at = slice(start, start + strip)
            inner = slice(first, first + strip)
            parts = [block[inner, :].astype(F32) for block in blocks]
            centre = sum(jnp.sum(part, axis=1, keepdims=True) for part in parts) / depth
            parts = [part - centre for part in parts]
            spread = sum(jnp.sum(part * part, axis=1, keepdims=True) for part in parts) / depth
            scaling = lax.rsqrt(spread + EPSILON)
            for step in range(tp):
                owner = lax.rem(place[0] - step + tp, tp)
                columns = pl.ds(pl.multiple_of(owner * width, width), width)
                low[at, columns] = (
                    parts[step] * scaling * gain[:, columns] + bias[:, columns]
                ).astype(BF16)
                full[at, columns] = blocks[step][inner, :]

    product = dot(low[...], weight[...]) + weight_bias[...]
    groups = []
    for group in range(per):
        parts = []
        for part in range(3):
            first = (group * 3 + part) * piece
            values = product[:, first : first + piece]
            if part < 2:
                values = (
                    values * cosine[...]
                    + pltpu.roll(values, piece - ROT // 2, 1) * sine_up[...]
                    + pltpu.roll(values, ROT // 2, 1) * sine_down[...]
                )
            parts.append(values.astype(BF16))
        groups.append(parts)
    flip = lax.rem(place[1], per)
    for way, out in enumerate(outs):
        for group in range(per):

            @pl.when((step == way // per) & (jnp.bitwise_xor(group, flip) == way % per))
            def _():
                for part in range(3):
                    out[:, part * piece : (part + 1) * piece] = groups[group][part]


def project(rings, place, gain, bias, weight, weight_bias, tables, nctx):
    chunks, tp = len(rings), len(rings[0])
    rows, width = tables[0].shape[0], rings[0][0].shape[1]
    depth = tp * width
    total = weight.shape[1]
    wide = total // nctx
    per = 2 if nctx % 2 == 0 else 1
    grid_spec = pltpu.PrefetchScalarGridSpec(
        num_scalar_prefetch=1,
        grid=(nctx // per,),
        in_specs=[whole((rows // chunks, width))] * (tp * chunks)
        + [whole((1, depth))] * 2
        + [
            pl.BlockSpec((depth, per * wide), lambda i, s: (0, jnp.bitwise_xor(i, s[1] // per))),
            pl.BlockSpec((1, per * wide), lambda i, s: (0, jnp.bitwise_xor(i, s[1] // per))),
        ]
        + [whole((rows, 2 * HEAD_DIM))] * 3,
        out_specs=[whole((rows, depth))] * 2 + [whole((rows, wide))] * nctx,
    )
    return pl.pallas_call(
        functools.partial(project_kernel, tp, chunks, per),
        grid_spec=grid_spec,
        out_shape=[
            jax.ShapeDtypeStruct((rows, depth), BF16),
            jax.ShapeDtypeStruct((rows, depth), BF16),
        ]
        + [jax.ShapeDtypeStruct((rows, wide), BF16)] * nctx,
        compiler_params=params(),
        cost_estimate=takes(60),
        name="project",
    )(
        place,
        *[block for blocks in rings for block in blocks],
        gain,
        bias,
        weight,
        weight_bias,
        *tables,
    )


def stack_heads(tile, heads):
    lane = lax.broadcasted_iota(jnp.int32, tile.shape, 1) // HEAD_DIM
    return jnp.concatenate(
        [jnp.where(lane == head, tile, jnp.zeros_like(tile)) for head in range(heads)], axis=0
    )


def fold_heads(stacked, heads, columns):
    row = lax.broadcasted_iota(jnp.int32, (stacked.shape[0], columns), 0) // HEAD_DIM
    folded = jnp.zeros((stacked.shape[0], columns), F32)
    for head in range(heads):
        folded = folded + jnp.where(row == head, stacked[:, head * columns : (head + 1) * columns], 0.0)
    return jnp.transpose(folded)


def load_pieces(place, pieces, nctx, held, block_rows):
    chunk_rows = pieces[0].shape[0]
    chunks = len(pieces) // nctx
    for chunk in range(chunks):
        for step in range(nctx):
            source = jnp.bitwise_xor(place, step)
            first = source * block_rows + chunk * chunk_rows
            held[pl.ds(pl.multiple_of(first, chunk_rows), chunk_rows), :] = pieces[
                chunk * nctx + step
            ][...]


def attend_kernel(nctx, heads, count, extra, block_rows, place, lows, ends, bounds, *refs):
    pieces = refs[:count]
    out, logs, held, turned, total, high, sums, raw, chances = refs[count + extra :]
    tile_q, tile_k = out.shape[0], turned.shape[2]
    width = heads * HEAD_DIM
    index = pl.program_id(0)

    @pl.when(index == 0)
    def _():
        load_pieces(place[0], pieces, nctx, held, block_rows)
        for tile in range(turned.shape[0]):
            turned[tile] = jnp.transpose(held[tile * tile_k : (tile + 1) * tile_k, 2 * width :])

    query_rows = pl.ds(pl.multiple_of(index * tile_q, tile_q), tile_q)
    queries = stack_heads(held[query_rows, :width] * jnp.asarray(HEAD_DIM**-0.5, BF16), heads)
    first_key = jnp.concatenate([bounds[0:1, :]] * heads, axis=1)
    last_key = jnp.concatenate([bounds[1:2, :]] * heads, axis=1)
    total[...] = jnp.zeros_like(total)
    high[...] = jnp.full_like(high, FLOOR)
    sums[...] = jnp.zeros_like(sums)

    def one(tile, _):
        start = tile * tile_k
        keys = held[pl.ds(pl.multiple_of(start, tile_k), tile_k), width : 2 * width]
        raw[...] = dot_turned(keys, queries)
        last = jnp.minimum(last_key, ends[tile] - 1) - start
        first = first_key - start
        peaks = jnp.broadcast_to(high[...], (8, raw.shape[1]))
        for begin in range(0, tile_k, STRIP):
            scores = raw[begin : begin + STRIP, :]
            row = lax.broadcasted_iota(jnp.int32, scores.shape, 0) + begin
            scores = jnp.where((row <= last) & (row >= first), scores, NEGATIVE)
            raw[begin : begin + STRIP, :] = scores
            for group in range(0, STRIP, 8):
                peaks = jnp.maximum(peaks, scores[group : group + 8])
        highest = jnp.max(peaks, axis=0, keepdims=True)
        partial = jnp.zeros((8, raw.shape[1]), F32)
        for begin in range(0, tile_k, STRIP):
            raised = jnp.exp(raw[begin : begin + STRIP, :] - highest)
            chances[begin : begin + STRIP, :] = raised.astype(BF16)
            for group in range(0, STRIP, 8):
                partial = partial + raised[group : group + 8]
        shrink = jnp.exp(high[...] - highest)
        sums[...] = sums[...] * shrink + jnp.sum(partial, axis=0, keepdims=True)
        total[...] = total[...] * shrink + dot(turned[tile], chances[...])
        high[...] = highest
        return 0

    upper = (index * tile_q + tile_q - 1) // tile_k + 1
    lax.fori_loop(lows[index], upper, one, 0)
    found = sums[...] > 0.0
    safe = jnp.where(found, sums[...], 1.0)
    out[...] = fold_heads(
        total[...] * jnp.where(found, 1.0 / safe, 0.0), heads, tile_q
    ).astype(BF16)
    log_total = jnp.where(found, high[...] + jnp.log(safe), 0.0)
    for head in range(heads):
        logs[head : head + 1, :] = log_total[:, head * tile_q : (head + 1) * tile_q]


def attend(pieces, place, lows, ends, bounds, nctx, block_rows, *needed):
    total_rows = nctx * block_rows
    width = pieces[0].shape[1] // 3
    heads = width // HEAD_DIM
    steps = total_rows // TILE_Q
    grid_spec = pltpu.PrefetchScalarGridSpec(
        num_scalar_prefetch=3,
        grid=(steps,),
        in_specs=[pl.BlockSpec((2, TILE_Q), lambda i, *_: (0, i))]
        + [whole(piece.shape) for piece in pieces]
        + anywhere(len(needed)),
        out_specs=[
            pl.BlockSpec((TILE_Q, width), lambda i, *_: (i, 0)),
            pl.BlockSpec((heads, TILE_Q), lambda i, *_: (0, i)),
        ],
        scratch_shapes=[
            pltpu.VMEM((total_rows, 3 * width), BF16),
            pltpu.VMEM((total_rows // TILE_K, width, TILE_K), BF16),
            pltpu.VMEM((width, heads * TILE_Q), F32),
            pltpu.VMEM((1, heads * TILE_Q), F32),
            pltpu.VMEM((1, heads * TILE_Q), F32),
            pltpu.VMEM((TILE_K, heads * TILE_Q), F32),
            pltpu.VMEM((TILE_K, heads * TILE_Q), BF16),
        ],
    )
    return pl.pallas_call(
        functools.partial(attend_kernel, nctx, heads, len(pieces), len(needed), block_rows),
        grid_spec=grid_spec,
        out_shape=[
            jax.ShapeDtypeStruct((total_rows, width), BF16),
            jax.ShapeDtypeStruct((heads, total_rows), F32),
        ],
        compiler_params=params(),
        cost_estimate=takes(200),
        name="attend",
    )(place, lows, ends, bounds, *pieces, *needed)


def attend_back_kernel(
    nctx, heads, count, extra, block_rows, place, lows, ends, bounds, logs, *refs
):
    pieces, refs = refs[:count], refs[count:]
    grad, attended, refs = refs[0], refs[1], refs[2 + extra :]
    outs, refs = refs[: nctx * CHUNKS], refs[nctx * CHUNKS :]
    held, turned, grad_keys, grad_values, grad_query, raw, raw_grad, chances, steps, merged = refs
    tile_q, tile_k = grad.shape[0], turned.shape[2]
    width = grad.shape[1]
    index = pl.program_id(0)
    scale = jnp.asarray(HEAD_DIM**-0.5, BF16)

    @pl.when(index == 0)
    def _():
        load_pieces(place[0], pieces, nctx, held, block_rows)
        for tile in range(turned.shape[0]):
            turned[tile] = jnp.transpose(
                held[tile * tile_k : (tile + 1) * tile_k, width : 2 * width]
            )
        grad_keys[...] = jnp.zeros_like(grad_keys)
        grad_values[...] = jnp.zeros_like(grad_values)

    query_rows = pl.ds(pl.multiple_of(index * tile_q, tile_q), tile_q)
    queries = stack_heads(held[query_rows, :width] * scale, heads)
    incoming = stack_heads(grad[...], heads)
    product = jnp.transpose(grad[...].astype(F32) * attended[...].astype(F32))
    centre = jnp.concatenate(
        [
            jnp.sum(product[head * HEAD_DIM : (head + 1) * HEAD_DIM, :], axis=0, keepdims=True)
            for head in range(heads)
        ],
        axis=1,
    )
    first_key = jnp.concatenate([bounds[0:1, :]] * heads, axis=1)
    last_key = jnp.concatenate([bounds[1:2, :]] * heads, axis=1)
    log_total = jnp.concatenate([logs[head : head + 1, :] for head in range(heads)], axis=1)
    grad_query[...] = jnp.zeros_like(grad_query)

    def one(tile, _):
        start = tile * tile_k
        key_rows = pl.ds(pl.multiple_of(start, tile_k), tile_k)
        raw[...] = dot_turned(held[key_rows, width : 2 * width], queries)
        raw_grad[...] = dot_turned(held[key_rows, 2 * width :], incoming)
        last = jnp.minimum(last_key, ends[tile] - 1) - start
        first = first_key - start
        for begin in range(0, tile_k, STRIP):
            at = slice(begin, begin + STRIP)
            row = lax.broadcasted_iota(jnp.int32, (STRIP, raw.shape[1]), 0) + begin
            allowed = (row <= last) & (row >= first)
            chance = jnp.exp(jnp.where(allowed, raw[at, :] - log_total, NEGATIVE))
            chances[at, :] = chance.astype(BF16)
            steps[at, :] = (chance * (raw_grad[at, :] - centre)).astype(BF16)
        grad_values[key_rows, :] += dot(chances[...], incoming)
        grad_keys[key_rows, :] += dot(steps[...], queries)
        grad_query[...] += dot(turned[tile], steps[...])
        return 0

    upper = (index * tile_q + tile_q - 1) // tile_k + 1
    lax.fori_loop(lows[index], upper, one, 0)
    merged[query_rows, :width] = (
        fold_heads(grad_query[...], heads, tile_q) * HEAD_DIM**-0.5
    ).astype(BF16)

    @pl.when(index == pl.num_programs(0) - 1)
    def _():
        merged[:, width : 2 * width] = grad_keys[...].astype(BF16)
        merged[:, 2 * width :] = grad_values[...].astype(BF16)
        chunk_rows = outs[0].shape[0]
        for chunk in range(CHUNKS):
            for way in range(nctx):
                first = jnp.bitwise_xor(place[0], way) * block_rows + chunk * chunk_rows
                outs[chunk * nctx + way][...] = merged[
                    pl.ds(pl.multiple_of(first, chunk_rows), chunk_rows), :
                ]


def attend_back(pieces, place, lows, ends, bounds, logs, grad, attended, nctx, block_rows, *needed):
    total_rows, width = grad.shape
    heads = width // HEAD_DIM
    by_tile = pl.BlockSpec((TILE_Q, width), lambda i, *_: (i, 0))
    sent = jax.ShapeDtypeStruct((block_rows // CHUNKS, 3 * width), BF16)
    grid_spec = pltpu.PrefetchScalarGridSpec(
        num_scalar_prefetch=3,
        grid=(total_rows // TILE_Q,),
        in_specs=[
            pl.BlockSpec((2, TILE_Q), lambda i, *_: (0, i)),
            pl.BlockSpec((heads, TILE_Q), lambda i, *_: (0, i)),
        ]
        + [whole(piece.shape) for piece in pieces]
        + [by_tile] * 2
        + anywhere(len(needed)),
        out_specs=[whole(sent.shape)] * (nctx * CHUNKS),
        scratch_shapes=[
            pltpu.VMEM((total_rows, 3 * width), BF16),
            pltpu.VMEM((total_rows // TILE_K, width, TILE_K), BF16),
            pltpu.VMEM((total_rows, width), F32),
            pltpu.VMEM((total_rows, width), F32),
            pltpu.VMEM((width, heads * TILE_Q), F32),
            pltpu.VMEM((TILE_K, heads * TILE_Q), F32),
            pltpu.VMEM((TILE_K, heads * TILE_Q), F32),
            pltpu.VMEM((TILE_K, heads * TILE_Q), BF16),
            pltpu.VMEM((TILE_K, heads * TILE_Q), BF16),
            pltpu.VMEM((total_rows, 3 * width), BF16),
        ],
    )
    return pl.pallas_call(
        functools.partial(
            attend_back_kernel, nctx, heads, len(pieces), len(needed), block_rows
        ),
        grid_spec=grid_spec,
        out_shape=[sent] * (nctx * CHUNKS),
        compiler_params=params(),
        cost_estimate=takes(250),
        name="attend_back",
    )(place, lows, ends, bounds, logs, *pieces, grad, attended, *needed)


def mix_kernel(nctx, count, place, heads_in, weight, source, gain, bias, *refs):
    returned, mixed, *lows = refs[count:]
    rows, depth = mixed.shape
    step = pl.program_id(0)
    left = jnp.concatenate([heads_in[c, 0] for c in range(nctx)], axis=1)
    returned[...] = left

    @pl.when(step == 0)
    def _():
        mixed[...] = source[...].astype(F32)

    mixed[...] += dot_turned(left, weight[0])

    @pl.when(step == pl.num_programs(0) - 1)
    def _():
        values = mixed[...]
        values = values - jnp.mean(values, axis=1, keepdims=True)
        scaling = lax.rsqrt(jnp.mean(values * values, axis=1, keepdims=True) + EPSILON)
        values = (values * scaling * gain[...] + bias[...]).astype(BF16)
        part_rows = lows[0].shape[0]
        for part, low in enumerate(lows):
            low[...] = values[part * part_rows : (part + 1) * part_rows]


def mix(heads_in, weight, full, gain, bias, place, parts, *needed):
    nctx, tp, rows, piece = heads_in.shape
    depth = full.shape[1]
    head_width = nctx * piece
    grid_spec = pltpu.PrefetchScalarGridSpec(
        num_scalar_prefetch=1,
        grid=(tp,),
        in_specs=[
            pl.BlockSpec((nctx, 1, rows, piece), lambda k, s: (0, k, 0, 0)),
            pl.BlockSpec((1, depth, head_width), lambda k, s: (k, 0, 0)),
            pl.BlockSpec((rows, depth), lambda k, s: (s[0], 0)),
            whole((1, depth)),
            whole((1, depth)),
        ]
        + anywhere(len(needed)),
        out_specs=[
            pl.BlockSpec((rows, head_width), lambda k, s: (0, k)),
            whole((rows, depth)),
        ]
        + [whole((rows // parts, depth))] * parts,
    )
    return pl.pallas_call(
        functools.partial(mix_kernel, nctx, len(needed)),
        grid_spec=grid_spec,
        out_shape=[
            jax.ShapeDtypeStruct((rows, tp * head_width), BF16),
            jax.ShapeDtypeStruct((rows, depth), F32),
        ]
        + [jax.ShapeDtypeStruct((rows // parts, depth), BF16)] * parts,
        compiler_params=params(),
        cost_estimate=takes(50),
        name="mix",
    )(place, heads_in, weight, full, gain, bias, *needed)


def feed_kernel(cuts, parts, tp, first_one, place, low, cot, mixed, source, *refs):
    refs = refs[-(5 + parts + 4) :]
    kept, hidden, grad_gate, grad_up, out = refs[:5]
    partials, held, sems = refs[5 : 5 + parts], refs[-4:-1], refs[-1]
    unit = source.shape[1] // 3
    width = out.shape[2]

    def copies(index):
        first, size = cuts[index]
        at = pl.ds(first, size)
        return [
            pltpu.make_async_copy(
                source.at[:, pl.ds(which * unit, unit), at],
                held[which].at[:, :, at],
                sems.at[index * 3 + which],
            )
            for which in range(3)
        ]

    for index in range(len(cuts)):
        for copy in copies(index):
            copy.start()
    kept[...] = low[...]
    rows, depth = kept.shape[0] // parts, kept.shape[1]
    grads = jnp.concatenate([cot[block] for block in range(tp)], axis=1)
    for index, (first, size) in enumerate(cuts):
        for copy in copies(index):
            copy.wait()
        at = slice(first, first + size)
        gate_weight, up_weight, down_weight = [w[:, :, at].reshape(depth, size) for w in held]
        gate = dot(kept[...], gate_weight)
        up = dot(kept[...], up_weight)
        sigma = 1.0 / (1.0 + jnp.exp(-gate))
        active = gate * sigma
        hidden[:, at] = (active * up).astype(BF16)
        grad = dot(grads, down_weight)
        grad_gate[:, at] = (grad * up * sigma * (1.0 + gate * (1.0 - sigma))).astype(BF16)
        grad_up[:, at] = (grad * active).astype(BF16)
    gate_weight, up_weight, down_weight = [w[...].reshape(depth, w.shape[2]) for w in held]
    product = dot_turned(grad_gate[...], gate_weight) + dot_turned(grad_up[...], up_weight)
    for part in range(parts):
        partials[part][...] = product[part * rows : (part + 1) * rows].astype(BF16)
    values = dot_turned(hidden[...], down_weight)
    if first_one:
        values = values + mixed[...]
    for block in range(tp):
        out[block] = values[:, block * width : (block + 1) * width].astype(BF16)


def feed(low, cot, mixed, weights, step, tp, place, held, parts, *needed):
    rows, depth = low.shape
    part_rows = rows // parts
    blocks, triple, hidden = weights.shape
    cuts = []
    while sum(size for _, size in cuts) < hidden:
        first = sum(size for _, size in cuts)
        cuts.append((first, min(512, hidden - first)))
    by_owner = lambda columns: pl.BlockSpec(
        (rows, columns), lambda i, s: (lax.rem(s[0] - step + tp, tp), 0)
    )
    width = depth // tp
    blocks_of_owner = pl.BlockSpec(
        (tp, rows, width), lambda i, s: (0, lax.rem(s[0] - step + tp, tp), 0)
    )
    grid_spec = pltpu.PrefetchScalarGridSpec(
        num_scalar_prefetch=1,
        grid=(1,),
        in_specs=[whole((rows, depth)), blocks_of_owner, whole(mixed.shape)]
        + anywhere(1 + len(held) + len(needed)),
        out_specs=[by_owner(depth)]
        + [by_owner(hidden)] * 3
        + [blocks_of_owner]
        + [whole((part_rows, depth))] * parts,
        scratch_shapes=[pltpu.VMEM((blocks, triple // 3, hidden), BF16)] * 3
        + [pltpu.SemaphoreType.DMA((3 * len(cuts),))],
    )
    return pl.pallas_call(
        functools.partial(feed_kernel, tuple(cuts), parts, tp, step == 0),
        grid_spec=grid_spec,
        out_shape=[jax.ShapeDtypeStruct((tp * rows, depth), BF16)]
        + [jax.ShapeDtypeStruct((tp * rows, hidden), BF16)] * 3
        + [jax.ShapeDtypeStruct((tp, tp * rows, width), BF16)]
        + [jax.ShapeDtypeStruct((part_rows, depth), BF16)] * parts,
        input_output_aliases={5 + index: index for index in range(len(held))},
        compiler_params=params(),
        cost_estimate=takes(100),
        name="feed",
    )(place, low, cot, mixed, weights, *held, *needed)


def blame(left, right, which, pick_left, unit, arrived, needed, split=False):
    rows = left.shape[0]
    side = left if pick_left else right
    picked = side.size // side.shape[-2] // unit // 2
    other = (right if pick_left else left).shape[1]
    if side.ndim == 3:
        per = side.shape[2] // unit
        chosen = pl.BlockSpec(
            (1, rows, unit), lambda j, s: ((2 * (j ^ s[1]) + s[0]) // per, 0, lax.rem(2 * (j ^ s[1]) + s[0], per))
        )
    else:
        chosen = pl.BlockSpec((rows, unit), lambda j, s: (0, 2 * (j ^ s[1]) + s[0]))
    kept = whole((rows, other))
    small = (unit, other) if pick_left else (other, unit)
    split = split or arrived is None
    if split:
        target, shape = [whole(small)] * picked, [small] * picked
    elif pick_left:
        target, shape = [pl.BlockSpec(small, lambda j, s: (j, 0))], [(picked * unit, other)]
    else:
        target, shape = [pl.BlockSpec(small, lambda j, s: (0, j))], [(other, picked * unit)]
    extra = [] if arrived is None else list(arrived)

    def kernel(which, left, right, *refs):
        ours, theirs = left[...], right[...]
        if side.ndim == 3:
            theirs = theirs[0]
        product = lax.dot_general(
            ours, theirs, (((0,), (0,)), ((), ())), preferred_element_type=F32
        )
        for j in range(picked):

            @pl.when(pl.program_id(0) == j)
            def _():
                total = product + refs[j][...].astype(F32) if extra else product
                refs[j - picked if split else -1][...] = total.astype(BF16)

    grid_spec = pltpu.PrefetchScalarGridSpec(
        num_scalar_prefetch=1,
        grid=(picked,),
        in_specs=([chosen, kept] if pick_left else [kept, chosen])
        + [whole(small)] * len(extra)
        + anywhere(len(needed)),
        out_specs=target,
    )
    return pl.pallas_call(
        kernel,
        grid_spec=grid_spec,
        out_shape=[jax.ShapeDtypeStruct(one, BF16) for one in shape],
        compiler_params=params(),
        cost_estimate=takes(30),
        name="blame",
    )(which, left, right, *extra, *needed)


def turn_kernel(nctx, count, parts, place, *refs):
    arrived, own = refs[:parts], refs[parts : 2 * parts]
    mixed, cot, gain = refs[2 * parts : 2 * parts + 3]
    weight, refs = refs[2 * parts + 3], refs[2 * parts + 4 + count :]
    out, grad_mixed, grad_low, gain_grad, shift_grad = refs
    rows, depth = mixed.shape
    piece = out.shape[3]

    @pl.when(pl.program_id(0) == 0)
    def _():
        incoming = jnp.concatenate(
            [there[...].astype(F32) + here[...].astype(F32) for there, here in zip(arrived, own)]
        )
        values = mixed[...]
        values = values - jnp.mean(values, axis=1, keepdims=True)
        scaling = lax.rsqrt(jnp.mean(values * values, axis=1, keepdims=True) + EPSILON)
        normed = values * scaling
        shift_grad[...] = jnp.sum(incoming, axis=0, keepdims=True)
        gain_grad[...] = jnp.sum(incoming * normed, axis=0, keepdims=True)
        scaled = incoming * gain[...]
        grads = jnp.concatenate([cot[block] for block in range(cot.shape[0])], axis=1)
        total = grads.astype(F32) + scaling * (
            scaled
            - jnp.mean(scaled, axis=1, keepdims=True)
            - normed * jnp.mean(scaled * normed, axis=1, keepdims=True)
        )
        grad_mixed[...] = total
        grad_low[...] = total.astype(BF16)

    product = dot(grad_low[...], weight[0])
    for c in range(nctx):
        out[c, 0] = product[:, c * piece : (c + 1) * piece].astype(BF16)


def turn(arrived, own, mixed, cot, gain, weight, place, nctx, tp, *needed):
    rows, depth = mixed.shape
    parts = len(arrived)
    head_width = weight.shape[2]
    piece = head_width // nctx
    grid_spec = pltpu.PrefetchScalarGridSpec(
        num_scalar_prefetch=1,
        grid=(tp,),
        in_specs=[whole((rows // parts, depth))] * (2 * parts)
        + [whole((rows, depth))]
        + [
            pl.BlockSpec((tp, rows, depth // tp), lambda k, s: (0, s[0], 0)),
            whole((1, depth)),
            pl.BlockSpec((1, depth, head_width), lambda k, s: (k, 0, 0)),
        ]
        + anywhere(len(needed)),
        out_specs=[
            pl.BlockSpec((nctx, 1, rows, piece), lambda k, s: (0, k, 0, 0)),
            whole((rows, depth)),
            whole((rows, depth)),
            whole((1, depth)),
            whole((1, depth)),
        ],
    )
    return pl.pallas_call(
        functools.partial(turn_kernel, nctx, len(needed), parts),
        grid_spec=grid_spec,
        out_shape=[
            jax.ShapeDtypeStruct((nctx, tp, rows, piece), BF16),
            jax.ShapeDtypeStruct((rows, depth), F32),
            jax.ShapeDtypeStruct((rows, depth), BF16),
            jax.ShapeDtypeStruct((1, depth), F32),
            jax.ShapeDtypeStruct((1, depth), F32),
        ],
        compiler_params=params(),
        cost_estimate=takes(60),
        name="turn",
    )(place, *arrived, *own, mixed, cot, gain, weight, *needed)


def finish_kernel(nctx, tp, parts, extra_count, chunk, place, *refs):
    pieces = refs[:nctx]
    cosine, sine_up, sine_down, full, extra, gain = refs[nctx : nctx + 6]
    weight, refs = refs[nctx + 6], refs[nctx + 7 + extra_count :]
    outs = refs[: tp * parts]
    low, bias_grad, gain_grad, shift_grad, spare = refs[tp * parts :]
    rows, wide = pieces[0].shape
    piece = wide // 3
    width = outs[0].shape[1]
    strip = spare.shape[0]
    extra_rows = extra.shape[0]

    @pl.when(pl.program_id(0) == 0)
    def _():
        bias_grad[...] = jnp.zeros_like(bias_grad)
        gain_grad[...] = jnp.zeros_like(gain_grad)
        shift_grad[...] = jnp.zeros_like(shift_grad)

    for step in range(nctx):
        source = jnp.bitwise_xor(place[1], step)
        for part in range(3):
            values = pieces[step][:, part * piece : (part + 1) * piece].astype(F32)
            if part < 2:
                values = (
                    values * cosine[...]
                    - pltpu.roll(values, piece - ROT // 2, 1) * sine_up[...]
                    - pltpu.roll(values, ROT // 2, 1) * sine_down[...]
                )
            columns = pl.ds(pl.multiple_of(source * wide + part * piece, piece), piece)
            bias_grad[:, columns] += jnp.sum(values, axis=0, keepdims=True)
            low[:, columns] = values.astype(BF16)

    incoming = dot_turned(low[...], weight[...])
    source = full[...].astype(F32)
    source = source - jnp.mean(source, axis=1, keepdims=True)
    scaling = lax.rsqrt(jnp.mean(source * source, axis=1, keepdims=True) + EPSILON)
    normed = source * scaling
    shift_grad[...] += jnp.sum(incoming, axis=0, keepdims=True)
    gain_grad[...] += jnp.sum(incoming * normed, axis=0, keepdims=True)
    scaled = incoming * gain[...]
    spare[...] = scaling * (
        scaled
        - jnp.mean(scaled, axis=1, keepdims=True)
        - normed * jnp.mean(scaled * normed, axis=1, keepdims=True)
    )
    first = chunk * pl.num_programs(0) * strip + pl.program_id(0) * strip
    wanted = place[0] * extra_rows

    if strip <= extra_rows:

        @pl.when((first >= wanted) & (first < wanted + extra_rows))
        def _():
            spare[...] += extra[pl.ds(pl.multiple_of(first - wanted, strip), strip), :]

    else:

        @pl.when((wanted >= first) & (wanted < first + strip))
        def _():
            spare[pl.ds(pl.multiple_of(wanted - first, extra_rows), extra_rows), :] += extra[...]

    for part in range(parts):

        @pl.when((pl.program_id(0) == part) | (parts == 1))
        def _():
            for step in range(tp):
                owner = lax.rem(place[0] - step + tp, tp)
                outs[step * parts + part][...] = spare[
                    :, pl.ds(pl.multiple_of(owner * width, width), width)
                ].astype(BF16)


def finish(pieces, place, tables, full, extra, gain, weight, chunk, tp, split, *needed):
    rows, wide = pieces[0].shape
    depth = full.shape[1]
    total = weight.shape[1]
    strip = 256
    steps = rows // strip
    parts = steps if split else 1
    width = depth // tp
    nctx = len(pieces)
    by_rows = lambda columns: pl.BlockSpec((strip, columns), lambda i, s: (i, 0))
    grid_spec = pltpu.PrefetchScalarGridSpec(
        num_scalar_prefetch=1,
        grid=(steps,),
        in_specs=[by_rows(wide)] * nctx
        + [by_rows(2 * HEAD_DIM)] * 3
        + [
            pl.BlockSpec((strip, depth), lambda i, s: (i + chunk * steps, 0)),
            whole(extra.shape),
            whole((1, depth)),
        ]
        + [whole(weight.shape)]
        + anywhere(len(needed)),
        out_specs=([whole((strip, width))] * (tp * parts) if split else [by_rows(width)] * tp)
        + [
            by_rows(total),
            whole((1, total)),
            whole((1, depth)),
            whole((1, depth)),
        ],
        scratch_shapes=[pltpu.VMEM((strip, depth), F32)],
    )
    return pl.pallas_call(
        functools.partial(finish_kernel, nctx, tp, parts, len(needed), chunk),
        grid_spec=grid_spec,
        out_shape=[jax.ShapeDtypeStruct((rows // parts, width), BF16)] * (tp * parts)
        + [
            jax.ShapeDtypeStruct((rows, total), BF16),
            jax.ShapeDtypeStruct((1, total), F32),
            jax.ShapeDtypeStruct((1, depth), F32),
            jax.ShapeDtypeStruct((1, depth), F32),
        ],
        compiler_params=params(),
        cost_estimate=takes(70),
        name="finish",
    )(place, *pieces, *tables, full, extra, gain, weight, *needed)


def join(rings, place):
    parts, tp = len(rings), len(rings[0])
    rows, width = rings[0][0].shape

    def kernel(place, *refs):
        for part in range(parts):
            for step in range(tp):
                owner = lax.rem(place[0] - step + tp, tp)
                refs[-1][owner, part * rows : (part + 1) * rows, :] = refs[part * tp + step][...]

    grid_spec = pltpu.PrefetchScalarGridSpec(
        num_scalar_prefetch=1,
        grid=(1,),
        in_specs=[whole((rows, width))] * (parts * tp),
        out_specs=whole((tp, parts * rows, width)),
    )
    return pl.pallas_call(
        kernel,
        grid_spec=grid_spec,
        out_shape=jax.ShapeDtypeStruct((tp, parts * rows, width), BF16),
        compiler_params=params(),
        cost_estimate=takes(10),
        name="join",
    )(place, *[block for blocks in rings for block in blocks])


def pack_kernel(gate, up, down, out):
    rows = gate.shape[0]
    out[:rows] = gate[...]
    out[rows : 2 * rows] = up[...]
    out[2 * rows :] = jnp.transpose(down[...])


def pack(gate, up, down):
    rows, columns = gate.shape
    return pl.pallas_call(
        pack_kernel,
        out_shape=jax.ShapeDtypeStruct((3 * rows, columns), BF16),
        compiler_params=params(),
        cost_estimate=takes(10),
        name="pack",
    )(gate, up, down)


def contract_rows(left, right):
    return lax.dot_general(left, right, (((0,), (0,)), ((), ())), preferred_element_type=F32)


def pick(stack, index):
    return lax.dynamic_index_in_dim(stack, index, 0, keepdims=False)


def shards(
    nfsdp,
    nctx,
    tp,
    inputs,
    cotangent,
    first_gain,
    first_bias,
    qkv_weight,
    qkv_bias,
    out_weight,
    second_gain,
    second_bias,
    gate_weight,
    up_weight,
    down_weight,
    lengths,
    fill_counts,
):
    data = ("fsdp", "ctx")
    ndata = nfsdp * nctx
    block_rows, width = inputs.shape
    depth = tp * width
    half_depth = depth // 2
    unit = depth // ndata
    tensor_index = lax.axis_index("tp").astype(jnp.int32)
    context_index = lax.axis_index("ctx").astype(jnp.int32)
    fsdp_index = lax.axis_index("fsdp").astype(jnp.int32)
    part_rows = block_rows // tp
    chunk_rows = block_rows // CHUNKS
    head_width = qkv_weight.shape[2]
    piece = head_width // nctx
    wide = 3 * piece

    square = nfsdp == 2 and nctx == 4 and unit % 128 == 0
    place = jnp.stack([tensor_index, context_index, fsdp_index])

    def shift(value, step):
        return lax.ppermute(value, "tp", [(i, (i + step) % tp) for i in range(tp)])

    def swap(value, step):
        return lax.ppermute(value, "ctx", [(i, i ^ step) for i in range(nctx)])

    core_index = context_index % 2
    groups = [list(range(0, ndata, 2)), list(range(1, ndata, 2))]
    place_xy = fsdp_index * 2 + context_index // 2

    def partner(left, right, pick_left, *needed, split=False):
        which = jnp.stack([1 - core_index, place_xy if split else 0 * place_xy])
        first = blame(left, right, which, pick_left, unit, None, needed)
        return first, [swap(part, 1) for part in first]

    def own(left, right, pick_left, arrived, *needed, split=False):
        which = jnp.stack([core_index, place_xy if split else 0 * place_xy])
        parts = blame(left, right, which, pick_left, unit, arrived, needed, split)
        return parts if split else parts[0]

    def cross(value):
        return lax.ppermute(value, "fsdp", [(i, i ^ 1) for i in range(nfsdp)])

    def scatter_half(value, axis):
        return lax.psum_scatter(
            value, data, scatter_dimension=axis, tiled=True, axis_index_groups=groups
        )

    def scatter_whole(left, right, axis):
        return lax.psum_scatter(
            contract_rows(left, right).astype(BF16), data, scatter_dimension=axis, tiled=True
        )

    def total(left, right):
        return (left.astype(F32) + right.astype(F32)).astype(BF16)

    owners = [(tensor_index - step + tp) % tp for step in range(tp)]

    own_qkv = (
        qkv_weight.reshape(-1, 3, nctx, piece).transpose(0, 2, 1, 3).reshape(-1, 3 * head_width)
    )
    full_qkv = lax.all_gather(own_qkv, data, axis=0, tiled=True)
    own_feed = pack(gate_weight, up_weight, down_weight)
    feed_weights = lax.all_gather(own_feed, data, axis=0, tiled=True).reshape(ndata, 3 * unit, -1)

    validity, position, first_key, last_key = layout(lengths[0], fill_counts[0], block_rows)
    own_position = lax.dynamic_slice_in_dim(position, context_index * block_rows, block_rows, 0)
    tables = rotary_tables(own_position)
    bounds = jnp.stack([first_key, last_key])
    tile_first = first_key[::TILE_Q]
    tile_count = tile_first.shape[0]
    lows = jnp.where(validity[::TILE_Q], tile_first // TILE_K, tile_count * TILE_Q).astype(jnp.int32)
    key_block = jnp.arange(0, nctx * block_rows, TILE_K, dtype=jnp.int32) // block_rows
    ends = (
        key_block * block_rows
        + jnp.sum(
            jnp.where(
                key_block[:, None] == jnp.arange(nctx, dtype=jnp.int32)[None, :],
                fill_counts[0][None, :],
                0,
            ),
            axis=1,
        )
    ).astype(jnp.int32)

    flat_bias = qkv_bias.reshape(3, nctx, piece).transpose(1, 0, 2).reshape(1, -1)
    gain_one, bias_one = first_gain[None], first_bias[None]
    gain_two, bias_two = second_gain[None], second_bias[None]

    rings = [[inputs[c * chunk_rows : (c + 1) * chunk_rows]] for c in range(CHUNKS)]
    share = unit // CHUNKS
    for chunk in range(CHUNKS):
        carried = out_weight.T[chunk * share : (chunk + 1) * share]
        rings[chunk][0] = tie(jnp.concatenate([rings[chunk][0], carried], axis=0), own_feed)
    for chunk in range(CHUNKS):
        for _ in range(tp - 1):
            rings[chunk].append(shift(rings[chunk][-1], 1))
    all_low, full, *outgoing = project(
        rings, place, gain_one, bias_one, full_qkv, flat_bias, tables, nctx
    )
    pieces = [outgoing[0]] + [swap(outgoing[way], way) for way in range(1, nctx)]
    chunk_tables = [
        [table[c * chunk_rows : (c + 1) * chunk_rows] for table in tables] for c in range(CHUNKS)
    ]
    stack = jnp.zeros((tp, unit, head_width), BF16)
    for step in range(tp):
        carried = jnp.concatenate([blocks[step][chunk_rows:] for blocks in rings], axis=0)
        stack = lax.dynamic_update_index_in_dim(stack, carried, owners[step], 0)
    full_out = lax.all_gather(stack, data, axis=1, tiled=True)

    cot = tie(cotangent, *[blocks[-1] for blocks in rings])
    cot_rings = [[cot[c * chunk_rows : (c + 1) * chunk_rows]] for c in range(CHUNKS)]
    for blocks in cot_rings:
        for _ in range(tp - 1):
            blocks.append(shift(blocks[-1], 1))

    attended, logs = attend(
        pieces,
        place[1:2],
        lows,
        ends,
        bounds,
        nctx,
        block_rows,
        feed_weights,
    )
    cot = join(cot_rings, place)
    arrived = lax.all_to_all(
        tie(attended, *[blocks[max(tp - 2, 0)] for blocks in cot_rings]).reshape(nctx * tp, part_rows, piece),
        ("ctx", "tp"),
        split_axis=0,
        concat_axis=0,
        tiled=True,
    )
    returned, mixed, second_low = mix(
        arrived.reshape(nctx, tp, part_rows, piece),
        full_out,
        full,
        gain_two,
        bias_two,
        place,
        1,
    )

    arrived, held, partials, travelling = second_low, [], [], None
    for step in range(tp):
        coming = shift(arrived, 1) if step < tp - 1 else None
        needed = travelling if step == tp - 1 and step > 2 else []
        *held, first, second = feed(
            arrived, cot, mixed, feed_weights, step, tp, place, held, HALVES, *needed
        )
        partials.append([first, second])
        if step == 1 % tp:
            travelling = partials[step]
        elif step > 1:
            travelling = [
                total(shift(value, 1), kept) for value, kept in zip(travelling, partials[step])
            ]
        if step == 0 and coming is not None:
            coming = tie(coming, partials[0][0])
        arrived = coming
    all_second, hidden, all_gate, all_up, feedforward = held

    needed = []
    if square:
        gate_first, gate_arrived = partner(all_second, all_gate, True, *travelling, split=True)
        up_first, up_arrived = partner(all_second, all_up, True, *travelling, split=True)
        down_first, down_arrived = partner(hidden, cot, False, *travelling)
        needed = [gate_first[0], up_first[0], down_first[0]]
    else:
        total_gate = scatter_whole(all_second, all_gate, 0)
        total_up = scatter_whole(all_second, all_up, 0)

    grad_heads, grad_mixed, mixed_low, gain_grad_two, shift_grad_two = turn(
        [shift(value, 1) for value in travelling],
        partials[0],
        mixed,
        cot,
        gain_two,
        full_out,
        place,
        nctx,
        tp,
        *needed,
    )
    grad_heads = lax.all_to_all(
        grad_heads.reshape(nctx * tp, part_rows, piece),
        ("ctx", "tp"),
        split_axis=0,
        concat_axis=0,
        tiled=True,
    ).reshape(nctx * block_rows, piece)

    needed, first_adds = [], []
    flat_cot = jnp.swapaxes(cot, 0, 1).reshape(block_rows, depth)
    if square:
        gates = own(all_second, all_gate, True, gate_arrived, mixed_low, split=True)
        ups = own(all_second, all_up, True, up_arrived, mixed_low, split=True)
        out_first, out_arrived = partner(mixed_low, returned, True)
        half_down = own(hidden, cot, False, down_arrived, mixed_low)
        needed = [gates[0], ups[0], out_first[0], half_down]
        total_down = scatter_half(half_down, 1).astype(F32)
        gates = [total(gates[way], cross(gates[way + 2])) for way in (0, 1)]
        ups = [total(ups[way], swap(ups[way + 1], 2)) for way in (0, 2)]
        first_adds = [*gates, *ups]
        total_gate = gates[0].astype(F32) + swap(gates[1], 2).astype(F32)
        total_up = ups[0].astype(F32) + cross(ups[1]).astype(F32)
    else:
        total_out = scatter_whole(mixed_low, returned, 0)
        total_down = scatter_whole(hidden, flat_cot, 1)

    layer_out = lax.all_to_all(
        tie(feedforward, grad_heads), "tp", split_axis=0, concat_axis=0, tiled=True
    )
    layer_out = jnp.sum(layer_out.astype(F32), axis=0).astype(BF16)

    grad_pieces = attend_back(
        pieces, place[1:2], lows, ends, bounds, logs, grad_heads, attended, nctx, block_rows, *needed
    )
    grad_lows, bias_grads, gain_grads, shift_grads, grad_rows = [], [], [], [], []
    ring_steps = []
    for chunk in range(CHUNKS):
        outgoing = grad_pieces[chunk * nctx : (chunk + 1) * nctx]
        arrived = [outgoing[0]] + [swap(outgoing[way], way) for way in range(1, nctx)]
        *partial, low, bias_grad, gain_grad, shift_grad = finish(
            arrived,
            place,
            chunk_tables[chunk],
            full,
            grad_mixed,
            gain_one,
            full_qkv,
            chunk,
            tp,
            chunk > 0,
            *(ring_steps[:1] if chunk > 0 else [layer_out, *first_adds]),
        )
        grad_lows.append(low)
        bias_grads.append(bias_grad)
        gain_grads.append(gain_grad)
        shift_grads.append(shift_grad)
        parts = len(partial) // tp
        rows = []
        for part in range(parts):
            travelling = partial[(1 % tp) * parts + part]
            for step in range(1, tp):
                kept = partial[((step + 1) % tp) * parts + part]
                if chunk > 0 and step == 2:
                    travelling = add(shift(travelling, 1), kept, grad_rows[0])
                else:
                    travelling = total(shift(travelling, 1), kept)
                ring_steps.append(travelling)
            rows.append(travelling)
        grad_rows += rows
    grad_inputs = jnp.concatenate(grad_rows, axis=0)

    all_grad = jnp.concatenate(grad_lows, axis=0)
    if square:
        half_out = own(mixed_low, returned, True, out_arrived, ring_steps[0])
        total_out = scatter_half(half_out, 0)
        first, qkv_arrived = partner(all_low, all_grad, True, *ring_steps[1:2], ring_steps[tp - 1])
        half_qkv = own(all_low, all_grad, True, qkv_arrived, total_gate, total_up, total_down)
        total_qkv = scatter_half(half_qkv, 0).astype(F32)
    else:
        total_qkv = scatter_whole(all_low, all_grad, 0).astype(F32)
    total_qkv = (
        total_qkv
        .reshape(-1, nctx, 3, piece)
        .transpose(0, 2, 1, 3)
        .reshape(-1, 3, head_width)
    )

    def exchange(value, axis, size):
        step = 1
        while step < size:
            value = value + lax.ppermute(value, axis, [(i, i ^ step) for i in range(size)])
            step *= 2
        return value

    out_parts = jnp.swapaxes(total_out.astype(BF16).reshape(-1, tp, head_width), 0, 1)
    total_out = pick(out_parts, tensor_index).astype(F32)
    for step in range(1, tp):
        total_out = total_out + shift(pick(out_parts, (tensor_index + step) % tp), step).astype(F32)
    total_out = total_out.T

    small = jnp.concatenate([sum(gain_grads), sum(shift_grads), gain_grad_two, shift_grad_two], axis=1)
    small = jnp.concatenate([sum(bias_grads), small], axis=1)
    small = exchange(exchange(small, "ctx", nctx), "fsdp", nfsdp)
    bias_total, small = small[:, : 3 * head_width], small[:, 3 * head_width :]
    small = exchange(small, "tp", tp)
    bias_total = bias_total.reshape(nctx, 3, piece).transpose(1, 0, 2).reshape(3, head_width)
    small = small.reshape(4, depth)
    return (
        layer_out,
        grad_inputs,
        small[0],
        small[1],
        total_qkv,
        bias_total,
        total_out,
        small[2],
        small[3],
        total_gate.astype(F32),
        total_up.astype(F32),
        total_down.astype(F32),
    )


def solution(mesh):
    data = ("fsdp", "ctx")
    by_rows = P(data, "tp")
    by_columns = P("tp", data)
    qkv = P(data, None, "tp")
    return jax.shard_map(
        functools.partial(shards, mesh.shape["fsdp"], mesh.shape["ctx"], mesh.shape["tp"]),
        mesh=mesh,
        in_specs=(
            by_rows,
            by_rows,
            P(),
            P(),
            qkv,
            P(None, "tp"),
            by_columns,
            P(),
            P(),
            by_rows,
            by_rows,
            by_columns,
            P("fsdp", None),
            P("fsdp", None),
        ),
        out_specs=(
            by_rows,
            by_rows,
            P(),
            P(),
            qkv,
            P(None, "tp"),
            by_columns,
            P(),
            P(),
            by_rows,
            by_rows,
            by_columns,
        ),
        check_vma=False,
    )
```

```python
import functools

import jax
import jax.numpy as jnp
from jax import lax
from jax.experimental import pallas as pl
from jax.experimental.pallas import tpu as pltpu
from jax.sharding import PartitionSpec as P

HEAD_DIM = 64
ROT = 16
EPSILON = 1e-05
NEGATIVE = -1e30
FLOOR = -1e20
VMEM_LIMIT = 56 * 1024 * 1024
TILE_Q = 512
TILE_K = 512
STRIP = 32
CHUNKS = 2
HALVES = 2

F32 = jnp.float32
BF16 = jnp.bfloat16


def layout(lengths, fill_counts, block_rows):
    blocks_count = fill_counts.shape[0]
    seq_count = lengths.shape[0]
    slot_index = jnp.arange(blocks_count * block_rows, dtype=jnp.int32)
    block_of = slot_index // block_rows
    within = slot_index - block_of * block_rows
    chooser = block_of[:, None] == jnp.arange(blocks_count, dtype=jnp.int32)[None, :]
    fill_here = jnp.sum(jnp.where(chooser, fill_counts[None, :], 0), axis=1)
    before = jnp.cumsum(fill_counts) - fill_counts
    before_here = jnp.sum(jnp.where(chooser, before[None, :], 0), axis=1)
    validity = within < fill_here
    used_index = before_here + within
    seq_ends = jnp.cumsum(lengths)
    sequence = jnp.sum((used_index[:, None] >= seq_ends[None, :]).astype(jnp.int32), axis=1)
    seq_starts = seq_ends - lengths
    picker = sequence[:, None] == jnp.arange(seq_count, dtype=jnp.int32)[None, :]
    start_here = jnp.sum(jnp.where(picker, seq_starts[None, :], 0), axis=1)
    after = before + fill_counts
    start_block = jnp.sum((seq_starts[:, None] >= after[None, :]).astype(jnp.int32), axis=1)
    start_block = jnp.minimum(start_block, blocks_count - 1)
    block_pick = start_block[:, None] == jnp.arange(blocks_count, dtype=jnp.int32)[None, :]
    start_before = jnp.sum(jnp.where(block_pick, before[None, :], 0), axis=1)
    start_slot = start_block * block_rows + seq_starts - start_before
    slot_here = jnp.sum(jnp.where(picker, start_slot[None, :], 0), axis=1)
    first_key = jnp.where(validity, slot_here, 0).astype(jnp.int32)
    last_key = jnp.where(validity, slot_index, -1).astype(jnp.int32)
    return (validity, used_index - start_here, first_key, last_key)


def rotary_tables(position):
    half = ROT // 2
    lane = jnp.arange(2 * HEAD_DIM, dtype=jnp.int32) % HEAD_DIM
    frequency = 10000.0 ** (-(2.0 * (lane % half).astype(F32)) / ROT)
    angles = position.astype(F32)[:, None] * frequency[None, :]
    cosine, sine = jnp.cos(angles), jnp.sin(angles)
    lane = lane[None, :]
    return (
        jnp.where(lane < ROT, cosine, 1.0),
        jnp.where(lane < half, -sine, 0.0),
        jnp.where((lane >= half) & (lane < ROT), sine, 0.0),
    )


def params(**extra):
    return pltpu.CompilerParams(vmem_limit_bytes=VMEM_LIMIT, **extra)


def takes(microseconds):
    return pl.CostEstimate(
        flops=int(microseconds * 1e8), bytes_accessed=0, transcendentals=0
    )


def whole(shape):
    return pl.BlockSpec(shape, lambda *_: (0,) * len(shape))


def anywhere(count):
    return [pl.BlockSpec(memory_space=pl.ANY)] * count


def write_half(out, values, half, unit):
    if unit % 128:
        out[...] = values[:, : out.shape[1]]
        return
    for block in range(out.shape[1] // unit):
        first = pl.multiple_of((2 * block + half) * unit, unit)
        out[:, block * unit : (block + 1) * unit] = values[:, pl.ds(first, unit)]


def dot(left, right):
    return jnp.dot(left, right, preferred_element_type=F32)


def dot_turned(left, right):
    return lax.dot_general(left, right, (((1,), (1,)), ((), ())), preferred_element_type=F32)


def tie(value, *needed):
    def kernel(*refs):
        del refs

    return pl.pallas_call(
        kernel,
        in_specs=anywhere(1 + len(needed)),
        out_specs=pl.BlockSpec(memory_space=pl.ANY),
        out_shape=jax.ShapeDtypeStruct(value.shape, value.dtype),
        input_output_aliases={0: 0},
        name="tie",
    )(value, *needed)


def add_kernel(left, right, *refs):
    refs[-1][...] = (left[...].astype(F32) + right[...].astype(F32)).astype(BF16)


def add(left, right, *needed):
    rows, columns = left.shape
    strip = min(rows, 128)
    block = pl.BlockSpec((strip, columns), lambda i: (i, 0))
    return pl.pallas_call(
        add_kernel,
        grid=(rows // strip,),
        in_specs=[block, block] + anywhere(len(needed)),
        out_specs=block,
        out_shape=jax.ShapeDtypeStruct(left.shape, BF16),
        compiler_params=params(),
        cost_estimate=takes(10),
        name="ring_add",
    )(left, right, *needed)


def project_kernel(tp, chunks, per, unit, place, *refs):
    rings, refs = refs[: tp * chunks], refs[tp * chunks :]
    gain, bias, weight, weight_bias, cosine, sine_up, sine_down = refs[:7]
    low, full, half, here, near, far = refs[7:]
    outs = [here, near] + [far.at[way] for way in range(far.shape[0])]
    rows, width = low.shape[0] // chunks, rings[0].shape[1]
    depth = tp * width
    wide = here.shape[1]
    piece = wide // 3
    step = pl.program_id(0)

    @pl.when(pl.program_id(0) == 0)
    def _():
        strip = 128
        for start in range(0, rows * chunks, strip):
            chunk, first = start // rows, start % rows
            blocks = rings[chunk * tp : (chunk + 1) * tp]
            at = slice(start, start + strip)
            inner = slice(first, first + strip)
            parts = [block[inner, :].astype(F32) for block in blocks]
            centre = sum(jnp.sum(part, axis=1, keepdims=True) for part in parts) / depth
            parts = [part - centre for part in parts]
            spread = sum(jnp.sum(part * part, axis=1, keepdims=True) for part in parts) / depth
            scaling = lax.rsqrt(spread + EPSILON)
            for step in range(tp):
                owner = lax.rem(place[0] - step + tp, tp)
                columns = pl.ds(pl.multiple_of(owner * width, width), width)
                low[at, columns] = (
                    parts[step] * scaling * gain[:, columns] + bias[:, columns]
                ).astype(BF16)
                full[at, columns] = blocks[step][inner, :]
        write_half(half, low, 1 - lax.rem(place[1], 2), unit)

    product = dot(low[...], weight[...]) + weight_bias[...]
    groups = []
    for group in range(per):
        parts = []
        for part in range(3):
            first = (group * 3 + part) * piece
            values = product[:, first : first + piece]
            if part < 2:
                values = (
                    values * cosine[...]
                    + pltpu.roll(values, piece - ROT // 2, 1) * sine_up[...]
                    + pltpu.roll(values, ROT // 2, 1) * sine_down[...]
                )
            parts.append(values.astype(BF16))
        groups.append(parts)
    flip = lax.rem(place[1], per)
    for way, out in enumerate(outs):
        for group in range(per):

            @pl.when((step == way // per) & (jnp.bitwise_xor(group, flip) == way % per))
            def _():
                for part in range(3):
                    out[:, part * piece : (part + 1) * piece] = groups[group][part]


def project(rings, place, gain, bias, weight, weight_bias, tables, nctx, unit):
    chunks, tp = len(rings), len(rings[0])
    rows, width = tables[0].shape[0], rings[0][0].shape[1]
    depth = tp * width
    total = weight.shape[1]
    wide = total // nctx
    per = 2 if nctx % 2 == 0 else 1
    grid_spec = pltpu.PrefetchScalarGridSpec(
        num_scalar_prefetch=1,
        grid=(nctx // per,),
        in_specs=[whole((rows // chunks, width))] * (tp * chunks)
        + [whole((1, depth))] * 2
        + [
            pl.BlockSpec((depth, per * wide), lambda i, s: (0, jnp.bitwise_xor(i, s[1] // per))),
            pl.BlockSpec((1, per * wide), lambda i, s: (0, jnp.bitwise_xor(i, s[1] // per))),
        ]
        + [whole((rows, 2 * HEAD_DIM))] * 3,
        out_specs=[whole((rows, depth))] * 2
        + [whole((rows, depth // 2))]
        + [whole((rows, wide))] * 2
        + [whole((nctx - 2, rows, wide))],
    )
    return pl.pallas_call(
        functools.partial(project_kernel, tp, chunks, per, unit),
        grid_spec=grid_spec,
        out_shape=[
            jax.ShapeDtypeStruct((rows, depth), BF16),
            jax.ShapeDtypeStruct((rows, depth), BF16),
            jax.ShapeDtypeStruct((rows, depth // 2), BF16),
        ]
        + [jax.ShapeDtypeStruct((rows, wide), BF16)] * 2
        + [jax.ShapeDtypeStruct((nctx - 2, rows, wide), BF16)],
        compiler_params=params(),
        cost_estimate=takes(60),
        name="project",
    )(
        place,
        *[block for blocks in rings for block in blocks],
        gain,
        bias,
        weight,
        weight_bias,
        *tables,
    )


def stack_heads(tile, heads):
    lane = lax.broadcasted_iota(jnp.int32, tile.shape, 1) // HEAD_DIM
    return jnp.concatenate(
        [jnp.where(lane == head, tile, jnp.zeros_like(tile)) for head in range(heads)], axis=0
    )


def fold_heads(stacked, heads, columns):
    row = lax.broadcasted_iota(jnp.int32, (stacked.shape[0], columns), 0) // HEAD_DIM
    folded = jnp.zeros((stacked.shape[0], columns), F32)
    for head in range(heads):
        folded = folded + jnp.where(row == head, stacked[:, head * columns : (head + 1) * columns], 0.0)
    return jnp.transpose(folded)


def load_pieces(place, pieces, nctx, held, block_rows):
    chunk_rows = pieces[0].shape[0]
    chunks = len(pieces) // nctx
    for chunk in range(chunks):
        for step in range(nctx):
            source = jnp.bitwise_xor(place, step)
            first = source * block_rows + chunk * chunk_rows
            held[pl.ds(pl.multiple_of(first, chunk_rows), chunk_rows), :] = pieces[
                chunk * nctx + step
            ][...]


def attend_kernel(nctx, heads, count, extra, block_rows, place, lows, ends, bounds, *refs):
    pieces = refs[:count]
    out, logs, held, turned, total, high, sums, raw, chances = refs[count + extra :]
    tile_q, tile_k = out.shape[0], turned.shape[2]
    width = heads * HEAD_DIM
    index = pl.program_id(0)

    @pl.when(index == 0)
    def _():
        load_pieces(place[0], pieces, nctx, held, block_rows)
        for tile in range(turned.shape[0]):
            turned[tile] = jnp.transpose(held[tile * tile_k : (tile + 1) * tile_k, 2 * width :])

    query_rows = pl.ds(pl.multiple_of(index * tile_q, tile_q), tile_q)
    queries = stack_heads(held[query_rows, :width] * jnp.asarray(HEAD_DIM**-0.5, BF16), heads)
    first_key = jnp.concatenate([bounds[0:1, :]] * heads, axis=1)
    last_key = jnp.concatenate([bounds[1:2, :]] * heads, axis=1)
    total[...] = jnp.zeros_like(total)
    high[...] = jnp.full_like(high, FLOOR)
    sums[...] = jnp.zeros_like(sums)

    def one(tile, _):
        start = tile * tile_k
        keys = held[pl.ds(pl.multiple_of(start, tile_k), tile_k), width : 2 * width]
        raw[...] = dot_turned(keys, queries)
        last = jnp.minimum(last_key, ends[tile] - 1) - start
        first = first_key - start
        peaks = jnp.broadcast_to(high[...], (8, raw.shape[1]))
        for begin in range(0, tile_k, STRIP):
            scores = raw[begin : begin + STRIP, :]
            row = lax.broadcasted_iota(jnp.int32, scores.shape, 0) + begin
            scores = jnp.where((row <= last) & (row >= first), scores, NEGATIVE)
            raw[begin : begin + STRIP, :] = scores
            for group in range(0, STRIP, 8):
                peaks = jnp.maximum(peaks, scores[group : group + 8])
        highest = jnp.max(peaks, axis=0, keepdims=True)
        partial = jnp.zeros((8, raw.shape[1]), F32)
        for begin in range(0, tile_k, STRIP):
            raised = jnp.exp(raw[begin : begin + STRIP, :] - highest)
            chances[begin : begin + STRIP, :] = raised.astype(BF16)
            for group in range(0, STRIP, 8):
                partial = partial + raised[group : group + 8]
        shrink = jnp.exp(high[...] - highest)
        sums[...] = sums[...] * shrink + jnp.sum(partial, axis=0, keepdims=True)
        total[...] = total[...] * shrink + dot(turned[tile], chances[...])
        high[...] = highest
        return 0

    upper = (index * tile_q + tile_q - 1) // tile_k + 1
    lax.fori_loop(lows[index], upper, one, 0)
    found = sums[...] > 0.0
    safe = jnp.where(found, sums[...], 1.0)
    out[...] = fold_heads(
        total[...] * jnp.where(found, 1.0 / safe, 0.0), heads, tile_q
    ).astype(BF16)
    log_total = jnp.where(found, high[...] + jnp.log(safe), 0.0)
    for head in range(heads):
        logs[head : head + 1, :] = log_total[:, head * tile_q : (head + 1) * tile_q]


def attend(pieces, place, lows, ends, bounds, nctx, block_rows, *needed):
    total_rows = nctx * block_rows
    width = pieces[0].shape[1] // 3
    heads = width // HEAD_DIM
    steps = total_rows // TILE_Q
    grid_spec = pltpu.PrefetchScalarGridSpec(
        num_scalar_prefetch=3,
        grid=(steps,),
        in_specs=[pl.BlockSpec((2, TILE_Q), lambda i, *_: (0, i))]
        + [whole(piece.shape) for piece in pieces]
        + anywhere(len(needed)),
        out_specs=[
            pl.BlockSpec((TILE_Q, width), lambda i, *_: (i, 0)),
            pl.BlockSpec((heads, TILE_Q), lambda i, *_: (0, i)),
        ],
        scratch_shapes=[
            pltpu.VMEM((total_rows, 3 * width), BF16),
            pltpu.VMEM((total_rows // TILE_K, width, TILE_K), BF16),
            pltpu.VMEM((width, heads * TILE_Q), F32),
            pltpu.VMEM((1, heads * TILE_Q), F32),
            pltpu.VMEM((1, heads * TILE_Q), F32),
            pltpu.VMEM((TILE_K, heads * TILE_Q), F32),
            pltpu.VMEM((TILE_K, heads * TILE_Q), BF16),
        ],
    )
    return pl.pallas_call(
        functools.partial(attend_kernel, nctx, heads, len(pieces), len(needed), block_rows),
        grid_spec=grid_spec,
        out_shape=[
            jax.ShapeDtypeStruct((total_rows, width), BF16),
            jax.ShapeDtypeStruct((heads, total_rows), F32),
        ],
        compiler_params=params(),
        cost_estimate=takes(200),
        name="attend",
    )(place, lows, ends, bounds, *pieces, *needed)


def attend_back_kernel(
    nctx, heads, count, extra, block_rows, place, lows, ends, bounds, logs, *refs
):
    pieces, refs = refs[:count], refs[count:]
    grad, attended, refs = refs[0], refs[1], refs[2 + extra :]
    here, near, far, refs = *refs[:3], refs[3:]
    held, turned, grad_keys, grad_values, grad_query, raw, raw_grad, chances, steps, merged = refs
    tile_q, tile_k = grad.shape[0], turned.shape[2]
    width = grad.shape[1]
    index = pl.program_id(0)
    scale = jnp.asarray(HEAD_DIM**-0.5, BF16)

    @pl.when(index == 0)
    def _():
        load_pieces(place[0], pieces, nctx, held, block_rows)
        for tile in range(turned.shape[0]):
            turned[tile] = jnp.transpose(
                held[tile * tile_k : (tile + 1) * tile_k, width : 2 * width]
            )
        grad_keys[...] = jnp.zeros_like(grad_keys)
        grad_values[...] = jnp.zeros_like(grad_values)

    query_rows = pl.ds(pl.multiple_of(index * tile_q, tile_q), tile_q)
    queries = stack_heads(held[query_rows, :width] * scale, heads)
    incoming = stack_heads(grad[...], heads)
    product = jnp.transpose(grad[...].astype(F32) * attended[...].astype(F32))
    centre = jnp.concatenate(
        [
            jnp.sum(product[head * HEAD_DIM : (head + 1) * HEAD_DIM, :], axis=0, keepdims=True)
            for head in range(heads)
        ],
        axis=1,
    )
    first_key = jnp.concatenate([bounds[0:1, :]] * heads, axis=1)
    last_key = jnp.concatenate([bounds[1:2, :]] * heads, axis=1)
    log_total = jnp.concatenate([logs[head : head + 1, :] for head in range(heads)], axis=1)
    grad_query[...] = jnp.zeros_like(grad_query)

    def one(tile, _):
        start = tile * tile_k
        key_rows = pl.ds(pl.multiple_of(start, tile_k), tile_k)
        raw[...] = dot_turned(held[key_rows, width : 2 * width], queries)
        raw_grad[...] = dot_turned(held[key_rows, 2 * width :], incoming)
        last = jnp.minimum(last_key, ends[tile] - 1) - start
        first = first_key - start
        for begin in range(0, tile_k, STRIP):
            at = slice(begin, begin + STRIP)
            row = lax.broadcasted_iota(jnp.int32, (STRIP, raw.shape[1]), 0) + begin
            allowed = (row <= last) & (row >= first)
            chance = jnp.exp(jnp.where(allowed, raw[at, :] - log_total, NEGATIVE))
            chances[at, :] = chance.astype(BF16)
            steps[at, :] = (chance * (raw_grad[at, :] - centre)).astype(BF16)
        grad_values[key_rows, :] += dot(chances[...], incoming)
        grad_keys[key_rows, :] += dot(steps[...], queries)
        grad_query[...] += dot(turned[tile], steps[...])
        return 0

    upper = (index * tile_q + tile_q - 1) // tile_k + 1
    lax.fori_loop(lows[index], upper, one, 0)
    merged[query_rows, :width] = (
        fold_heads(grad_query[...], heads, tile_q) * HEAD_DIM**-0.5
    ).astype(BF16)

    @pl.when(index == pl.num_programs(0) - 1)
    def _():
        merged[:, width : 2 * width] = grad_keys[...].astype(BF16)
        merged[:, 2 * width :] = grad_values[...].astype(BF16)
        outs = [here, near] + [far.at[way] for way in range(nctx - 2)]
        for way, out in enumerate(outs):
            first = jnp.bitwise_xor(place[0], way) * block_rows
            out[...] = merged[pl.ds(pl.multiple_of(first, block_rows), block_rows), :]


def attend_back(pieces, place, lows, ends, bounds, logs, grad, attended, nctx, block_rows, *needed):
    total_rows, width = grad.shape
    heads = width // HEAD_DIM
    by_tile = pl.BlockSpec((TILE_Q, width), lambda i, *_: (i, 0))
    sent = (block_rows, 3 * width)
    sent = [sent, sent, (nctx - 2, *sent)]
    grid_spec = pltpu.PrefetchScalarGridSpec(
        num_scalar_prefetch=3,
        grid=(total_rows // TILE_Q,),
        in_specs=[
            pl.BlockSpec((2, TILE_Q), lambda i, *_: (0, i)),
            pl.BlockSpec((heads, TILE_Q), lambda i, *_: (0, i)),
        ]
        + [whole(piece.shape) for piece in pieces]
        + [by_tile] * 2
        + anywhere(len(needed)),
        out_specs=[whole(shape) for shape in sent],
        scratch_shapes=[
            pltpu.VMEM((total_rows, 3 * width), BF16),
            pltpu.VMEM((total_rows // TILE_K, width, TILE_K), BF16),
            pltpu.VMEM((total_rows, width), F32),
            pltpu.VMEM((total_rows, width), F32),
            pltpu.VMEM((width, heads * TILE_Q), F32),
            pltpu.VMEM((TILE_K, heads * TILE_Q), F32),
            pltpu.VMEM((TILE_K, heads * TILE_Q), F32),
            pltpu.VMEM((TILE_K, heads * TILE_Q), BF16),
            pltpu.VMEM((TILE_K, heads * TILE_Q), BF16),
            pltpu.VMEM((total_rows, 3 * width), BF16),
        ],
    )
    return pl.pallas_call(
        functools.partial(
            attend_back_kernel, nctx, heads, len(pieces), len(needed), block_rows
        ),
        grid_spec=grid_spec,
        out_shape=[jax.ShapeDtypeStruct(shape, BF16) for shape in sent],
        compiler_params=params(),
        cost_estimate=takes(250),
        name="attend_back",
    )(place, lows, ends, bounds, logs, *pieces, grad, attended, *needed)


def mix_kernel(nctx, count, place, heads_in, weight, source, gain, bias, *refs):
    returned, mixed, *lows = refs[count:]
    rows, depth = mixed.shape
    step = pl.program_id(0)
    left = jnp.concatenate([heads_in[c, 0] for c in range(nctx)], axis=1)
    returned[...] = left

    @pl.when(step == 0)
    def _():
        mixed[...] = source[...].astype(F32)

    mixed[...] += dot_turned(left, weight[0])

    @pl.when(step == pl.num_programs(0) - 1)
    def _():
        values = mixed[...]
        values = values - jnp.mean(values, axis=1, keepdims=True)
        scaling = lax.rsqrt(jnp.mean(values * values, axis=1, keepdims=True) + EPSILON)
        values = (values * scaling * gain[...] + bias[...]).astype(BF16)
        part_rows = lows[0].shape[0]
        for part, low in enumerate(lows):
            low[...] = values[part * part_rows : (part + 1) * part_rows]


def mix(heads_in, weight, full, gain, bias, place, parts, *needed):
    nctx, tp, rows, piece = heads_in.shape
    depth = full.shape[1]
    head_width = nctx * piece
    grid_spec = pltpu.PrefetchScalarGridSpec(
        num_scalar_prefetch=1,
        grid=(tp,),
        in_specs=[
            pl.BlockSpec((nctx, 1, rows, piece), lambda k, s: (0, k, 0, 0)),
            pl.BlockSpec((1, depth, head_width), lambda k, s: (k, 0, 0)),
            pl.BlockSpec((rows, depth), lambda k, s: (s[0], 0)),
            whole((1, depth)),
            whole((1, depth)),
        ]
        + anywhere(len(needed)),
        out_specs=[
            pl.BlockSpec((rows, head_width), lambda k, s: (0, k)),
            whole((rows, depth)),
        ]
        + [whole((rows // parts, depth))] * parts,
    )
    return pl.pallas_call(
        functools.partial(mix_kernel, nctx, len(needed)),
        grid_spec=grid_spec,
        out_shape=[
            jax.ShapeDtypeStruct((rows, tp * head_width), BF16),
            jax.ShapeDtypeStruct((rows, depth), F32),
        ]
        + [jax.ShapeDtypeStruct((rows // parts, depth), BF16)] * parts,
        compiler_params=params(),
        cost_estimate=takes(50),
        name="mix",
    )(place, heads_in, weight, full, gain, bias, *needed)


def feed_kernel(cuts, parts, tp, first_one, place, low, cot, mixed, source, *refs):
    refs = refs[-(5 + parts + 4) :]
    kept, grad_gate, grad_up, hidden, out = refs[:5]
    partials, held, sems = refs[5 : 5 + parts], refs[-4:-1], refs[-1]
    unit = source.shape[1] // 3
    width = out.shape[2]

    def copies(index):
        first, size = cuts[index]
        at = pl.ds(first, size)
        return [
            pltpu.make_async_copy(
                source.at[:, pl.ds(which * unit, unit), at],
                held[which].at[:, :, at],
                sems.at[index * 3 + which],
            )
            for which in range(3)
        ]

    for index in range(len(cuts)):
        for copy in copies(index):
            copy.start()
    kept[...] = low[...]
    rows, depth = kept.shape[0] // parts, kept.shape[1]
    grads = jnp.concatenate([cot[block] for block in range(tp)], axis=1)
    for index, (first, size) in enumerate(cuts):
        for copy in copies(index):
            copy.wait()
        at = slice(first, first + size)
        gate_weight, up_weight, down_weight = [w[:, :, at].reshape(depth, size) for w in held]
        gate = dot(kept[...], gate_weight)
        up = dot(kept[...], up_weight)
        sigma = 1.0 / (1.0 + jnp.exp(-gate))
        active = gate * sigma
        hidden[:, at] = (active * up).astype(BF16)
        grad = dot(grads, down_weight)
        grad_gate[:, at] = (grad * up * sigma * (1.0 + gate * (1.0 - sigma))).astype(BF16)
        grad_up[:, at] = (grad * active).astype(BF16)
    gate_weight, up_weight, down_weight = [w[...].reshape(depth, w.shape[2]) for w in held]
    product = dot_turned(grad_gate[...], gate_weight) + dot_turned(grad_up[...], up_weight)
    for part in range(parts):
        partials[part][...] = product[part * rows : (part + 1) * rows].astype(BF16)
    values = dot_turned(hidden[...], down_weight)
    if first_one:
        values = values + mixed[...]
    for block in range(tp):
        out[block] = values[:, block * width : (block + 1) * width].astype(BF16)


def feed(low, cot, mixed, weights, step, tp, place, held, parts, *needed):
    rows, depth = low.shape
    part_rows = rows // parts
    blocks, triple, hidden = weights.shape
    cuts = []
    while sum(size for _, size in cuts) < hidden:
        first = sum(size for _, size in cuts)
        cuts.append((first, min(512, hidden - first)))
    by_owner = lambda columns: pl.BlockSpec(
        (rows, columns), lambda i, s: (lax.rem(s[0] - step + tp, tp), 0)
    )
    width = depth // tp
    blocks_of_owner = pl.BlockSpec(
        (tp, rows, width), lambda i, s: (0, lax.rem(s[0] - step + tp, tp), 0)
    )
    grid_spec = pltpu.PrefetchScalarGridSpec(
        num_scalar_prefetch=1,
        grid=(1,),
        in_specs=[whole((rows, depth)), blocks_of_owner, whole(mixed.shape)]
        + anywhere(1 + len(held) + len(needed)),
        out_specs=[by_owner(depth)]
        + [by_owner(hidden)] * 3
        + [blocks_of_owner]
        + [whole((part_rows, depth))] * parts,
        scratch_shapes=[pltpu.VMEM((blocks, triple // 3, hidden), BF16)] * 3
        + [pltpu.SemaphoreType.DMA((3 * len(cuts),))],
    )
    return pl.pallas_call(
        functools.partial(feed_kernel, tuple(cuts), parts, tp, step == 0),
        grid_spec=grid_spec,
        out_shape=[
            jax.ShapeDtypeStruct((tp * rows, columns), BF16)
            for columns in (depth, hidden, hidden, hidden)
        ]
        + [jax.ShapeDtypeStruct((tp, tp * rows, width), BF16)]
        + [jax.ShapeDtypeStruct((part_rows, depth), BF16)] * parts,
        input_output_aliases={5 + index: index for index in range(len(held))},
        compiler_params=params(),
        cost_estimate=takes(100),
        name="feed",
    )(place, low, cot, mixed, weights, *held, *needed)


def blame_halves(lefts, rights, place, unit, *needed, parts=0):
    rows = lefts[0].shape[0]
    other = rights[0].shape[1]
    picked = lefts[1].shape[1] // unit
    chosen = pl.BlockSpec((rows, unit), lambda j, s: (0, 2 * (j ^ s[3]) + s[1] % 2))
    cut = pl.BlockSpec((rows, unit), lambda j, s: (0, j ^ s[3]))
    if parts:
        shapes = [(unit // parts, other)] * (picked * parts)
        targets = [whole(shape) for shape in shapes]
    else:
        shapes = [(picked * unit, other)]
        targets = [pl.BlockSpec((unit, other), lambda j, s: (j, 0))]

    def kernel(place, left_here, left_there, right_here, right_there, *refs):
        outs = refs[len(needed) :]
        product = 0.0
        for left, right in ((left_here, right_here), (left_there, right_there)):
            product = product + lax.dot_general(
                left[...], right[...], (((0,), (0,)), ((), ())), preferred_element_type=F32
            )
        product = product.astype(BF16)
        if not parts:
            outs[0][...] = product
        for j in range(picked if parts else 0):

            @pl.when(pl.program_id(0) == j)
            def _():
                for part in range(parts):
                    first = part * unit // parts
                    outs[j * parts + part][...] = product[first : first + unit // parts]

    grid_spec = pltpu.PrefetchScalarGridSpec(
        num_scalar_prefetch=1,
        grid=(picked,),
        in_specs=[chosen, cut] + [whole((rows, other))] * 2 + anywhere(len(needed)),
        out_specs=targets,
    )
    place = jnp.concatenate([place, place[2:3] * 2 + place[1:2] // 2 if parts else 0 * place[:1]])
    outs = pl.pallas_call(
        kernel,
        grid_spec=grid_spec,
        out_shape=[jax.ShapeDtypeStruct(shape, BF16) for shape in shapes],
        compiler_params=params(),
        cost_estimate=takes(60),
        name="blame_halves",
    )(place, *lefts, *rights, *needed)
    return outs if parts else outs[0]


def blame(left, right, *needed):
    rows, columns = left.shape
    if right.ndim == 3:
        steps, other = right.shape[0], right.shape[2]
        in_specs = [whole((rows, columns)), pl.BlockSpec((1, rows, other), lambda j: (j, 0, 0))]
        target, shape = pl.BlockSpec((columns, other), lambda j: (0, j)), (columns, steps * other)
    else:
        steps, other = 4, right.shape[1]
        in_specs = [pl.BlockSpec((rows, columns // steps), lambda j: (0, j)), whole((rows, other))]
        target, shape = pl.BlockSpec((columns // steps, other), lambda j: (j, 0)), (columns, other)

    def kernel(left, right, *refs):
        theirs = right[0] if len(right.shape) == 3 else right[...]
        refs[-1][...] = lax.dot_general(
            left[...], theirs, (((0,), (0,)), ((), ())), preferred_element_type=F32
        ).astype(BF16)

    return pl.pallas_call(
        kernel,
        grid=(steps,),
        in_specs=in_specs + anywhere(len(needed)),
        out_specs=target,
        out_shape=jax.ShapeDtypeStruct(shape, BF16),
        compiler_params=params(),
        cost_estimate=takes(60),
        name="blame",
    )(left, right, *needed)


def turn_kernel(nctx, count, parts, unit, place, *refs):
    arrived, own = refs[:parts], refs[parts : 2 * parts]
    mixed, cot, gain = refs[2 * parts : 2 * parts + 3]
    weight, refs = refs[2 * parts + 3], refs[2 * parts + 4 + count :]
    out, grad_mixed, grad_low, gain_grad, shift_grad, half = refs
    rows, depth = mixed.shape
    piece = out.shape[3]

    @pl.when(pl.program_id(0) == 0)
    def _():
        incoming = jnp.concatenate(
            [there[...].astype(F32) + here[...].astype(F32) for there, here in zip(arrived, own)]
        )
        values = mixed[...]
        values = values - jnp.mean(values, axis=1, keepdims=True)
        scaling = lax.rsqrt(jnp.mean(values * values, axis=1, keepdims=True) + EPSILON)
        normed = values * scaling
        shift_grad[...] = jnp.sum(incoming, axis=0, keepdims=True)
        gain_grad[...] = jnp.sum(incoming * normed, axis=0, keepdims=True)
        scaled = incoming * gain[...]
        grads = jnp.concatenate([cot[block] for block in range(cot.shape[0])], axis=1)
        total = grads.astype(F32) + scaling * (
            scaled
            - jnp.mean(scaled, axis=1, keepdims=True)
            - normed * jnp.mean(scaled * normed, axis=1, keepdims=True)
        )
        grad_mixed[...] = total
        grad_low[...] = total.astype(BF16)
        write_half(half, grad_low, 1 - lax.rem(place[1], 2), unit)

    product = dot(grad_low[...], weight[0])
    for c in range(nctx):
        out[c, 0] = product[:, c * piece : (c + 1) * piece].astype(BF16)


def turn(arrived, own, mixed, cot, gain, weight, place, nctx, tp, unit, *needed):
    rows, depth = mixed.shape
    parts = len(arrived)
    head_width = weight.shape[2]
    piece = head_width // nctx
    grid_spec = pltpu.PrefetchScalarGridSpec(
        num_scalar_prefetch=1,
        grid=(tp,),
        in_specs=[whole((rows // parts, depth))] * (2 * parts)
        + [whole((rows, depth))]
        + [
            pl.BlockSpec((tp, rows, depth // tp), lambda k, s: (0, s[0], 0)),
            whole((1, depth)),
            pl.BlockSpec((1, depth, head_width), lambda k, s: (k, 0, 0)),
        ]
        + anywhere(len(needed)),
        out_specs=[
            pl.BlockSpec((nctx, 1, rows, piece), lambda k, s: (0, k, 0, 0)),
            whole((rows, depth)),
            whole((rows, depth)),
            whole((1, depth)),
            whole((1, depth)),
            whole((rows, depth // 2)),
        ],
    )
    return pl.pallas_call(
        functools.partial(turn_kernel, nctx, len(needed), parts, unit),
        grid_spec=grid_spec,
        out_shape=[
            jax.ShapeDtypeStruct((nctx, tp, rows, piece), BF16),
            jax.ShapeDtypeStruct((rows, depth), F32),
            jax.ShapeDtypeStruct((rows, depth), BF16),
            jax.ShapeDtypeStruct((1, depth), F32),
            jax.ShapeDtypeStruct((1, depth), F32),
            jax.ShapeDtypeStruct((rows, depth // 2), BF16),
        ],
        compiler_params=params(),
        cost_estimate=takes(60),
        name="turn",
    )(place, *arrived, *own, mixed, cot, gain, weight, *needed)


def finish_kernel(nctx, tp, extra_count, place, *refs):
    pieces = refs[:nctx]
    cosine, sine_up, sine_down, full, extra, gain = refs[nctx : nctx + 6]
    weight, refs = refs[nctx + 6], refs[nctx + 7 + extra_count :]
    outs = refs[:tp]
    low, bias_grad, gain_grad, shift_grad, spare = refs[tp:]
    rows, wide = pieces[0].shape
    piece = wide // 3
    width = outs[0].shape[1]
    strip = spare.shape[0]
    extra_rows = extra.shape[0]

    @pl.when(pl.program_id(0) == 0)
    def _():
        bias_grad[...] = jnp.zeros_like(bias_grad)
        gain_grad[...] = jnp.zeros_like(gain_grad)
        shift_grad[...] = jnp.zeros_like(shift_grad)

    for step in range(nctx):
        source = jnp.bitwise_xor(place[1], step)
        for part in range(3):
            values = pieces[step][:, part * piece : (part + 1) * piece].astype(F32)
            if part < 2:
                values = (
                    values * cosine[...]
                    - pltpu.roll(values, piece - ROT // 2, 1) * sine_up[...]
                    - pltpu.roll(values, ROT // 2, 1) * sine_down[...]
                )
            columns = pl.ds(pl.multiple_of(source * wide + part * piece, piece), piece)
            bias_grad[:, columns] += jnp.sum(values, axis=0, keepdims=True)
            low[:, columns] = values.astype(BF16)

    incoming = dot_turned(low[...], weight[...])
    source = full[...].astype(F32)
    source = source - jnp.mean(source, axis=1, keepdims=True)
    scaling = lax.rsqrt(jnp.mean(source * source, axis=1, keepdims=True) + EPSILON)
    normed = source * scaling
    shift_grad[...] += jnp.sum(incoming, axis=0, keepdims=True)
    gain_grad[...] += jnp.sum(incoming * normed, axis=0, keepdims=True)
    scaled = incoming * gain[...]
    spare[...] = scaling * (
        scaled
        - jnp.mean(scaled, axis=1, keepdims=True)
        - normed * jnp.mean(scaled * normed, axis=1, keepdims=True)
    )
    first = pl.program_id(0) * strip
    wanted = place[0] * extra_rows

    if strip <= extra_rows:

        @pl.when((first >= wanted) & (first < wanted + extra_rows))
        def _():
            spare[...] += extra[pl.ds(pl.multiple_of(first - wanted, strip), strip), :]

    else:

        @pl.when((wanted >= first) & (wanted < first + strip))
        def _():
            spare[pl.ds(pl.multiple_of(wanted - first, extra_rows), extra_rows), :] += extra[...]

    for step, out in enumerate(outs):
        owner = lax.rem(place[0] - step + tp, tp)
        out[...] = spare[:, pl.ds(pl.multiple_of(owner * width, width), width)].astype(BF16)


def finish(pieces, place, tables, full, extra, gain, weight, tp, *needed):
    rows, wide = pieces[0].shape
    depth = full.shape[1]
    total = weight.shape[1]
    strip = 256
    steps = rows // strip
    width = depth // tp
    nctx = len(pieces)
    by_rows = lambda columns: pl.BlockSpec((strip, columns), lambda i, s: (i, 0))
    grid_spec = pltpu.PrefetchScalarGridSpec(
        num_scalar_prefetch=1,
        grid=(steps,),
        in_specs=[by_rows(wide)] * nctx
        + [by_rows(2 * HEAD_DIM)] * 3
        + [
            by_rows(depth),
            whole(extra.shape),
            whole((1, depth)),
        ]
        + [whole(weight.shape)]
        + anywhere(len(needed)),
        out_specs=[by_rows(width)] * tp
        + [
            by_rows(total),
            whole((1, total)),
            whole((1, depth)),
            whole((1, depth)),
        ],
        scratch_shapes=[pltpu.VMEM((strip, depth), F32)],
    )
    return pl.pallas_call(
        functools.partial(finish_kernel, nctx, tp, len(needed)),
        grid_spec=grid_spec,
        out_shape=[jax.ShapeDtypeStruct((rows, width), BF16)] * tp
        + [
            jax.ShapeDtypeStruct((rows, total), BF16),
            jax.ShapeDtypeStruct((1, total), F32),
            jax.ShapeDtypeStruct((1, depth), F32),
            jax.ShapeDtypeStruct((1, depth), F32),
        ],
        compiler_params=params(),
        cost_estimate=takes(70),
        name="finish",
    )(place, *pieces, *tables, full, extra, gain, weight, *needed)


def join(rings, place):
    parts, tp = len(rings), len(rings[0])
    rows, width = rings[0][0].shape

    def kernel(place, *refs):
        for part in range(parts):
            for step in range(tp):
                owner = lax.rem(place[0] - step + tp, tp)
                refs[-1][owner, part * rows : (part + 1) * rows, :] = refs[part * tp + step][...]

    grid_spec = pltpu.PrefetchScalarGridSpec(
        num_scalar_prefetch=1,
        grid=(1,),
        in_specs=[whole((rows, width))] * (parts * tp),
        out_specs=whole((tp, parts * rows, width)),
    )
    return pl.pallas_call(
        kernel,
        grid_spec=grid_spec,
        out_shape=jax.ShapeDtypeStruct((tp, parts * rows, width), BF16),
        compiler_params=params(),
        cost_estimate=takes(10),
        name="join",
    )(place, *[block for blocks in rings for block in blocks])


def pack_kernel(gate, up, down, out):
    rows = gate.shape[0]
    out[:rows] = gate[...]
    out[rows : 2 * rows] = up[...]
    out[2 * rows :] = jnp.transpose(down[...])


def pack(gate, up, down):
    rows, columns = gate.shape
    return pl.pallas_call(
        pack_kernel,
        out_shape=jax.ShapeDtypeStruct((3 * rows, columns), BF16),
        compiler_params=params(),
        cost_estimate=takes(10),
        name="pack",
    )(gate, up, down)


def contract_rows(left, right):
    return lax.dot_general(left, right, (((0,), (0,)), ((), ())), preferred_element_type=F32)


def pick(stack, index):
    return lax.dynamic_index_in_dim(stack, index, 0, keepdims=False)


def shards(
    nfsdp,
    nctx,
    tp,
    inputs,
    cotangent,
    first_gain,
    first_bias,
    qkv_weight,
    qkv_bias,
    out_weight,
    second_gain,
    second_bias,
    gate_weight,
    up_weight,
    down_weight,
    lengths,
    fill_counts,
):
    data = ("fsdp", "ctx")
    ndata = nfsdp * nctx
    block_rows, width = inputs.shape
    depth = tp * width
    half_depth = depth // 2
    unit = depth // ndata
    tensor_index = lax.axis_index("tp").astype(jnp.int32)
    context_index = lax.axis_index("ctx").astype(jnp.int32)
    fsdp_index = lax.axis_index("fsdp").astype(jnp.int32)
    part_rows = block_rows // tp
    chunk_rows = block_rows // CHUNKS
    head_width = qkv_weight.shape[2]
    piece = head_width // nctx
    wide = 3 * piece

    square = nfsdp == 2 and nctx == 4 and unit % 128 == 0
    place = jnp.stack([tensor_index, context_index, fsdp_index])

    def shift(value, step):
        return lax.ppermute(value, "tp", [(i, (i + step) % tp) for i in range(tp)])

    def swap(value, step):
        return lax.ppermute(value, "ctx", [(i, i ^ step) for i in range(nctx)])

    core_index = context_index % 2
    groups = [list(range(0, ndata, 2)), list(range(1, ndata, 2))]
    def mate(value):
        return swap(value, 1)

    def send(here, near, far):
        far = swap(far, 2)
        return [here, swap(near, 1), far[0], swap(far[1], 1)]

    def scatter_half(value, axis):
        return lax.psum_scatter(
            value, data, scatter_dimension=axis, tiled=True, axis_index_groups=groups
        )

    def scatter(value, axis):
        return lax.psum_scatter(value, data, scatter_dimension=axis, tiled=True)

    def cross(value):
        return lax.ppermute(value, "fsdp", [(i, i ^ 1) for i in range(nfsdp)])

    def total(left, right):
        return (left.astype(F32) + right.astype(F32)).astype(BF16)

    owners = [(tensor_index - step + tp) % tp for step in range(tp)]

    own_qkv = (
        qkv_weight.reshape(-1, 3, nctx, piece).transpose(0, 2, 1, 3).reshape(-1, 3 * head_width)
    )
    full_qkv = lax.all_gather(own_qkv, data, axis=0, tiled=True)
    own_feed = pack(gate_weight, up_weight, down_weight)
    feed_weights = lax.all_gather(own_feed, data, axis=0, tiled=True).reshape(ndata, 3 * unit, -1)

    validity, position, first_key, last_key = layout(lengths[0], fill_counts[0], block_rows)
    own_position = lax.dynamic_slice_in_dim(position, context_index * block_rows, block_rows, 0)
    tables = rotary_tables(own_position)
    bounds = jnp.stack([first_key, last_key])
    tile_first = first_key[::TILE_Q]
    tile_count = tile_first.shape[0]
    lows = jnp.where(validity[::TILE_Q], tile_first // TILE_K, tile_count * TILE_Q).astype(jnp.int32)
    key_block = jnp.arange(0, nctx * block_rows, TILE_K, dtype=jnp.int32) // block_rows
    ends = (
        key_block * block_rows
        + jnp.sum(
            jnp.where(
                key_block[:, None] == jnp.arange(nctx, dtype=jnp.int32)[None, :],
                fill_counts[0][None, :],
                0,
            ),
            axis=1,
        )
    ).astype(jnp.int32)

    flat_bias = qkv_bias.reshape(3, nctx, piece).transpose(1, 0, 2).reshape(1, -1)
    gain_one, bias_one = first_gain[None], first_bias[None]
    gain_two, bias_two = second_gain[None], second_bias[None]

    rings = [[inputs[c * chunk_rows : (c + 1) * chunk_rows]] for c in range(CHUNKS)]
    share = unit // CHUNKS
    for chunk in range(CHUNKS):
        carried = out_weight.T[chunk * share : (chunk + 1) * share]
        rings[chunk][0] = tie(jnp.concatenate([rings[chunk][0], carried], axis=0), own_feed)
    for chunk in range(CHUNKS):
        for _ in range(tp - 1):
            rings[chunk].append(shift(rings[chunk][-1], 1))
    all_low, full, low_half, *outgoing = project(
        rings, place, gain_one, bias_one, full_qkv, flat_bias, tables, nctx, unit
    )
    pieces = send(*outgoing)
    stack = jnp.zeros((tp, unit, head_width), BF16)
    for step in range(tp):
        carried = jnp.concatenate([blocks[step][chunk_rows:] for blocks in rings], axis=0)
        stack = lax.dynamic_update_index_in_dim(stack, carried, owners[step], 0)
    full_out = lax.all_gather(stack, data, axis=1, tiled=True)

    cot = tie(cotangent, *[blocks[-1] for blocks in rings])
    cot_rings = [[cot[c * chunk_rows : (c + 1) * chunk_rows]] for c in range(CHUNKS)]
    for blocks in cot_rings:
        for _ in range(tp - 1):
            blocks.append(shift(blocks[-1], 1))

    attended, logs = attend(
        pieces,
        place[1:2],
        lows,
        ends,
        bounds,
        nctx,
        block_rows,
        feed_weights,
    )
    cot = join(cot_rings, place)
    arrived = lax.all_to_all(
        tie(attended, *[blocks[-1] for blocks in cot_rings]).reshape(nctx * tp, part_rows, piece),
        ("ctx", "tp"),
        split_axis=0,
        concat_axis=0,
        tiled=True,
    )
    returned, mixed, second_low = mix(
        arrived.reshape(nctx, tp, part_rows, piece),
        full_out,
        full,
        gain_two,
        bias_two,
        place,
        1,
    )

    arrived, held, partials, travelling = second_low, [], [], None
    for step in range(tp):
        coming = shift(arrived, 1) if step < tp - 1 else None
        needed = travelling if step == tp - 1 and step > 2 else []
        *held, first, second = feed(
            arrived, cot, mixed, feed_weights, step, tp, place, held, HALVES, *needed
        )
        partials.append([first, second])
        if step == 1 % tp:
            travelling = partials[step]
        elif step > 1:
            travelling = [
                total(shift(value, 1), kept) for value, kept in zip(travelling, partials[step])
            ]
        if step == 0 and coming is not None:
            coming = tie(coming, partials[0][0])
        arrived = coming
    all_second, all_gate, all_up, hidden, feedforward = held

    last = [shift(value, 1) for value in travelling]
    half_gate = blame(all_second, all_gate, *travelling)
    half_up = blame(all_second, all_up, *travelling)
    half_down = blame(hidden, cot, *travelling)
    grad_heads, grad_mixed, mixed_low, gain_grad_two, shift_grad_two, mixed_half = turn(
        last,
        partials[0],
        mixed,
        cot,
        gain_two,
        full_out,
        place,
        nctx,
        tp,
        unit,
        half_gate,
        half_up,
        half_down,
    )
    grad_heads = lax.all_to_all(
        grad_heads.reshape(nctx * tp, part_rows, piece),
        ("ctx", "tp"),
        split_axis=0,
        concat_axis=0,
        tiled=True,
    ).reshape(nctx * block_rows, piece)

    total_gate = scatter(tie(half_gate, mixed_low), 0).astype(F32)
    total_up = scatter(tie(half_up, mixed_low), 0).astype(F32)
    total_down = scatter(tie(half_down, mixed_low), 1).astype(F32)

    feedforward = tie(feedforward, grad_heads)
    layer_out = pick(feedforward, owners[1 % tp])
    for step in range(1, tp):
        layer_out = total(shift(layer_out, 1), pick(feedforward, owners[(step + 1) % tp]))

    grad_pieces = attend_back(
        pieces, place[1:2], lows, ends, bounds, logs, grad_heads, attended, nctx, block_rows
    )
    arrived = send(*grad_pieces)
    if square:
        half_out = blame_halves(
            (mixed_low, mate(mixed_half)), (returned, mate(returned)), place, unit, arrived[2]
        )
        total_out = scatter_half(half_out, 0)
    else:
        half_out = blame(mixed_low, returned)
        total_out = scatter(half_out, 0)
    low_halves = mate(low_half) if square else low_half
    needed = [layer_out, total_gate, total_up, low_halves, half_out]
    *partial, all_grad, bias_grad, gain_grad, shift_grad = finish(
        arrived, place, tables, full, grad_mixed, gain_one, full_qkv, tp, *needed
    )
    parts = []
    if square:
        parts = blame_halves((all_low, low_halves), (all_grad, mate(all_grad)), place, unit, parts=2)
    travelling, needed = partial[1 % tp], [total_down, *parts[:1]]
    ring_steps = []
    for step in range(1, tp):
        travelling = add(
            shift(travelling, 1), partial[(step + 1) % tp], *(needed if step == 1 else [])
        )
        ring_steps.append(travelling)
    grad_inputs = travelling
    if square:
        first, second = parts[0::2], parts[1::2]
        first = [total(first[way], cross(first[way + 2])) for way in (0, 1)]
        second = [total(second[way], swap(second[way + 1], 2)) for way in (0, 2)]
        first = first[0].astype(F32) + swap(first[1], 2).astype(F32)
        second = second[0].astype(F32) + cross(second[1]).astype(F32)
        total_qkv = jnp.concatenate([first, second], axis=0)
    else:
        total_qkv = scatter(blame(all_low, all_grad), 0).astype(F32)

    total_qkv = (
        total_qkv
        .reshape(-1, nctx, 3, piece)
        .transpose(0, 2, 1, 3)
        .reshape(-1, 3, head_width)
    )

    def exchange(value, axis, size):
        step = 1
        while step < size:
            value = value + lax.ppermute(value, axis, [(i, i ^ step) for i in range(size)])
            step *= 2
        return value

    total_out = tie(total_out, *ring_steps[1:2])
    out_parts = jnp.swapaxes(total_out.reshape(-1, tp, head_width), 0, 1)
    total_out = pick(out_parts, tensor_index).astype(F32)
    for step in range(1, tp):
        total_out = total_out + shift(pick(out_parts, (tensor_index + step) % tp), step).astype(F32)
    total_out = total_out.T

    small = jnp.concatenate([gain_grad, shift_grad, gain_grad_two, shift_grad_two], axis=1)
    small = tie(jnp.concatenate([bias_grad, small], axis=1), *ring_steps[1:2])
    small = exchange(exchange(small, "ctx", nctx), "fsdp", nfsdp)
    bias_total, small = small[:, : 3 * head_width], small[:, 3 * head_width :]
    small = exchange(small, "tp", tp)
    bias_total = bias_total.reshape(nctx, 3, piece).transpose(1, 0, 2).reshape(3, head_width)
    small = small.reshape(4, depth)
    return (
        layer_out,
        grad_inputs,
        small[0],
        small[1],
        total_qkv,
        bias_total,
        total_out,
        small[2],
        small[3],
        total_gate,
        total_up,
        total_down,
    )


def solution(mesh):
    data = ("fsdp", "ctx")
    by_rows = P(data, "tp")
    by_columns = P("tp", data)
    qkv = P(data, None, "tp")
    return jax.shard_map(
        functools.partial(shards, mesh.shape["fsdp"], mesh.shape["ctx"], mesh.shape["tp"]),
        mesh=mesh,
        in_specs=(
            by_rows,
            by_rows,
            P(),
            P(),
            qkv,
            P(None, "tp"),
            by_columns,
            P(),
            P(),
            by_rows,
            by_rows,
            by_columns,
            P("fsdp", None),
            P("fsdp", None),
        ),
        out_specs=(
            by_rows,
            by_rows,
            P(),
            P(),
            qkv,
            P(None, "tp"),
            by_columns,
            P(),
            P(),
            by_rows,
            by_rows,
            by_columns,
        ),
        check_vma=False,
    )
```

```python
import functools

import jax
import jax.numpy as jnp
from jax import lax
from jax.experimental import pallas as pl
from jax.experimental.pallas import tpu as pltpu
from jax.sharding import PartitionSpec as P

HEAD_DIM = 64
ROT = 16
EPSILON = 1e-05
NEGATIVE = -1e30
FLOOR = -1e20
VMEM_LIMIT = 56 * 1024 * 1024
TILE_Q = 512
TILE_K = 512
STRIP = 32
CHUNKS = 2
HALVES = 2

F32 = jnp.float32
BF16 = jnp.bfloat16


def layout(lengths, fill_counts, block_rows):
    blocks_count = fill_counts.shape[0]
    seq_count = lengths.shape[0]
    slot_index = jnp.arange(blocks_count * block_rows, dtype=jnp.int32)
    block_of = slot_index // block_rows
    within = slot_index - block_of * block_rows
    chooser = block_of[:, None] == jnp.arange(blocks_count, dtype=jnp.int32)[None, :]
    fill_here = jnp.sum(jnp.where(chooser, fill_counts[None, :], 0), axis=1)
    before = jnp.cumsum(fill_counts) - fill_counts
    before_here = jnp.sum(jnp.where(chooser, before[None, :], 0), axis=1)
    validity = within < fill_here
    used_index = before_here + within
    seq_ends = jnp.cumsum(lengths)
    sequence = jnp.sum((used_index[:, None] >= seq_ends[None, :]).astype(jnp.int32), axis=1)
    seq_starts = seq_ends - lengths
    picker = sequence[:, None] == jnp.arange(seq_count, dtype=jnp.int32)[None, :]
    start_here = jnp.sum(jnp.where(picker, seq_starts[None, :], 0), axis=1)
    after = before + fill_counts
    start_block = jnp.sum((seq_starts[:, None] >= after[None, :]).astype(jnp.int32), axis=1)
    start_block = jnp.minimum(start_block, blocks_count - 1)
    block_pick = start_block[:, None] == jnp.arange(blocks_count, dtype=jnp.int32)[None, :]
    start_before = jnp.sum(jnp.where(block_pick, before[None, :], 0), axis=1)
    start_slot = start_block * block_rows + seq_starts - start_before
    slot_here = jnp.sum(jnp.where(picker, start_slot[None, :], 0), axis=1)
    first_key = jnp.where(validity, slot_here, 0).astype(jnp.int32)
    last_key = jnp.where(validity, slot_index, -1).astype(jnp.int32)
    return (validity, used_index - start_here, first_key, last_key)


def rotary_tables(position):
    half = ROT // 2
    lane = jnp.arange(2 * HEAD_DIM, dtype=jnp.int32) % HEAD_DIM
    frequency = 10000.0 ** (-(2.0 * (lane % half).astype(F32)) / ROT)
    angles = position.astype(F32)[:, None] * frequency[None, :]
    cosine, sine = jnp.cos(angles), jnp.sin(angles)
    lane = lane[None, :]
    return (
        jnp.where(lane < ROT, cosine, 1.0),
        jnp.where(lane < half, -sine, 0.0),
        jnp.where((lane >= half) & (lane < ROT), sine, 0.0),
    )


def params(**extra):
    return pltpu.CompilerParams(vmem_limit_bytes=VMEM_LIMIT, **extra)


def takes(microseconds):
    return pl.CostEstimate(
        flops=int(microseconds * 1e8), bytes_accessed=0, transcendentals=0
    )


def whole(shape):
    return pl.BlockSpec(shape, lambda *_: (0,) * len(shape))


def anywhere(count):
    return [pl.BlockSpec(memory_space=pl.ANY)] * count


def write_half(out, values, half, unit):
    if unit % 128:
        out[...] = values[:, : out.shape[1]]
        return
    for block in range(out.shape[1] // unit):
        first = pl.multiple_of((2 * block + half) * unit, unit)
        out[:, block * unit : (block + 1) * unit] = values[:, pl.ds(first, unit)]


def dot(left, right):
    return jnp.dot(left, right, preferred_element_type=F32)


def dot_turned(left, right):
    return lax.dot_general(left, right, (((1,), (1,)), ((), ())), preferred_element_type=F32)


def tie(value, *needed):
    def kernel(*refs):
        del refs

    return pl.pallas_call(
        kernel,
        in_specs=anywhere(1 + len(needed)),
        out_specs=pl.BlockSpec(memory_space=pl.ANY),
        out_shape=jax.ShapeDtypeStruct(value.shape, value.dtype),
        input_output_aliases={0: 0},
        name="tie",
    )(value, *needed)


def add_kernel(left, right, *refs):
    refs[-1][...] = (left[...].astype(F32) + right[...].astype(F32)).astype(BF16)


def add(left, right, *needed):
    rows, columns = left.shape
    strip = min(rows, 512)
    block = pl.BlockSpec((strip, columns), lambda i: (i, 0))
    return pl.pallas_call(
        add_kernel,
        grid=(rows // strip,),
        in_specs=[block, block] + anywhere(len(needed)),
        out_specs=block,
        out_shape=jax.ShapeDtypeStruct(left.shape, BF16),
        compiler_params=params(),
        cost_estimate=takes(10),
        name="ring_add",
    )(left, right, *needed)


def project_kernel(tp, chunks, per, unit, place, *refs):
    rings, refs = refs[: tp * chunks], refs[tp * chunks :]
    gain, bias, weight, weight_bias, cosine, sine_up, sine_down = refs[:7]
    low, full, half, here, near, far, stack = refs[7:]
    outs = [here, near] + [far.at[way] for way in range(far.shape[0])]
    rows, width = low.shape[0] // chunks, rings[0].shape[1]
    depth = tp * width
    wide = here.shape[1]
    piece = wide // 3
    step = pl.program_id(0)

    @pl.when(pl.program_id(0) == 0)
    def _():
        strip = 128
        for start in range(0, rows * chunks, strip):
            chunk, first = start // rows, start % rows
            blocks = rings[chunk * tp : (chunk + 1) * tp]
            at = slice(start, start + strip)
            inner = slice(first, first + strip)
            parts = [block[inner, :].astype(F32) for block in blocks]
            centre = sum(jnp.sum(part, axis=1, keepdims=True) for part in parts) / depth
            parts = [part - centre for part in parts]
            spread = sum(jnp.sum(part * part, axis=1, keepdims=True) for part in parts) / depth
            scaling = lax.rsqrt(spread + EPSILON)
            for step in range(tp):
                owner = lax.rem(place[0] - step + tp, tp)
                columns = pl.ds(pl.multiple_of(owner * width, width), width)
                low[at, columns] = (
                    parts[step] * scaling * gain[:, columns] + bias[:, columns]
                ).astype(BF16)
                full[at, columns] = blocks[step][inner, :]
        write_half(half, low, 1 - lax.rem(place[1], 2), unit)
        share = rings[0].shape[0] - rows
        for chunk in range(chunks):
            for step in range(tp):
                owner = lax.rem(place[0] - step + tp, tp)
                stack[owner, chunk * share : (chunk + 1) * share, :] = rings[chunk * tp + step][
                    rows:, :
                ]

    product = dot(low[...], weight[...]) + weight_bias[...]
    groups = []
    for group in range(per):
        parts = []
        for part in range(3):
            first = (group * 3 + part) * piece
            values = product[:, first : first + piece]
            if part < 2:
                values = (
                    values * cosine[...]
                    + pltpu.roll(values, piece - ROT // 2, 1) * sine_up[...]
                    + pltpu.roll(values, ROT // 2, 1) * sine_down[...]
                )
            parts.append(values.astype(BF16))
        groups.append(parts)
    flip = lax.rem(place[1], per)
    for way, out in enumerate(outs):
        for group in range(per):

            @pl.when((step == way // per) & (jnp.bitwise_xor(group, flip) == way % per))
            def _():
                for part in range(3):
                    out[:, part * piece : (part + 1) * piece] = groups[group][part]


def project(rings, place, gain, bias, weight, weight_bias, tables, nctx, unit):
    chunks, tp = len(rings), len(rings[0])
    rows, width = tables[0].shape[0], rings[0][0].shape[1]
    depth = tp * width
    total = weight.shape[1]
    wide = total // nctx
    per = 2 if nctx % 2 == 0 else 1
    grid_spec = pltpu.PrefetchScalarGridSpec(
        num_scalar_prefetch=1,
        grid=(nctx // per,),
        in_specs=[whole(rings[0][0].shape)] * (tp * chunks)
        + [whole((1, depth))] * 2
        + [
            pl.BlockSpec((depth, per * wide), lambda i, s: (0, jnp.bitwise_xor(i, s[1] // per))),
            pl.BlockSpec((1, per * wide), lambda i, s: (0, jnp.bitwise_xor(i, s[1] // per))),
        ]
        + [whole((rows, 2 * HEAD_DIM))] * 3,
        out_specs=[whole((rows, depth))] * 2
        + [whole((rows, depth // 2))]
        + [whole((rows, wide))] * 2
        + [whole((nctx - 2, rows, wide)), whole((tp, unit, width))],
    )
    return pl.pallas_call(
        functools.partial(project_kernel, tp, chunks, per, unit),
        grid_spec=grid_spec,
        out_shape=[
            jax.ShapeDtypeStruct((rows, depth), BF16),
            jax.ShapeDtypeStruct((rows, depth), BF16),
            jax.ShapeDtypeStruct((rows, depth // 2), BF16),
        ]
        + [jax.ShapeDtypeStruct((rows, wide), BF16)] * 2
        + [
            jax.ShapeDtypeStruct((nctx - 2, rows, wide), BF16),
            jax.ShapeDtypeStruct((tp, unit, width), BF16),
        ],
        compiler_params=params(),
        cost_estimate=takes(60),
        name="project",
    )(
        place,
        *[block for blocks in rings for block in blocks],
        gain,
        bias,
        weight,
        weight_bias,
        *tables,
    )


def stack_heads(tile, heads):
    lane = lax.broadcasted_iota(jnp.int32, tile.shape, 1) // HEAD_DIM
    return jnp.concatenate(
        [jnp.where(lane == head, tile, jnp.zeros_like(tile)) for head in range(heads)], axis=0
    )


def fold_heads(stacked, heads, columns):
    row = lax.broadcasted_iota(jnp.int32, (stacked.shape[0], columns), 0) // HEAD_DIM
    folded = jnp.zeros((stacked.shape[0], columns), F32)
    for head in range(heads):
        folded = folded + jnp.where(row == head, stacked[:, head * columns : (head + 1) * columns], 0.0)
    return jnp.transpose(folded)


def load_pieces(place, pieces, nctx, held, block_rows):
    chunk_rows = pieces[0].shape[0]
    chunks = len(pieces) // nctx
    for chunk in range(chunks):
        for step in range(nctx):
            source = jnp.bitwise_xor(place, step)
            first = source * block_rows + chunk * chunk_rows
            held[pl.ds(pl.multiple_of(first, chunk_rows), chunk_rows), :] = pieces[
                chunk * nctx + step
            ][...]


def attend_kernel(nctx, heads, count, extra, block_rows, place, lows, ends, bounds, *refs):
    pieces = refs[:count]
    out, sent, logs, held, turned, total, high, sums, raw, chances = refs[count + extra :]
    tile_q, tile_k = out.shape[0], turned.shape[2]
    width = heads * HEAD_DIM
    index = pl.program_id(0)

    @pl.when(index == 0)
    def _():
        load_pieces(place[0], pieces, nctx, held, block_rows)
        for tile in range(turned.shape[0]):
            turned[tile] = jnp.transpose(held[tile * tile_k : (tile + 1) * tile_k, 2 * width :])

    query_rows = pl.ds(pl.multiple_of(index * tile_q, tile_q), tile_q)
    queries = stack_heads(held[query_rows, :width] * jnp.asarray(HEAD_DIM**-0.5, BF16), heads)
    first_key = jnp.concatenate([bounds[0:1, :]] * heads, axis=1)
    last_key = jnp.concatenate([bounds[1:2, :]] * heads, axis=1)
    total[...] = jnp.zeros_like(total)
    high[...] = jnp.full_like(high, FLOOR)
    sums[...] = jnp.zeros_like(sums)

    def one(tile, _):
        start = tile * tile_k
        keys = held[pl.ds(pl.multiple_of(start, tile_k), tile_k), width : 2 * width]
        raw[...] = dot_turned(keys, queries)
        last = jnp.minimum(last_key, ends[tile] - 1) - start
        first = first_key - start
        peaks = jnp.broadcast_to(high[...], (8, raw.shape[1]))
        for begin in range(0, tile_k, STRIP):
            scores = raw[begin : begin + STRIP, :]
            row = lax.broadcasted_iota(jnp.int32, scores.shape, 0) + begin
            scores = jnp.where((row <= last) & (row >= first), scores, NEGATIVE)
            raw[begin : begin + STRIP, :] = scores
            for group in range(0, STRIP, 8):
                peaks = jnp.maximum(peaks, scores[group : group + 8])
        highest = jnp.max(peaks, axis=0, keepdims=True)
        partial = jnp.zeros((8, raw.shape[1]), F32)
        for begin in range(0, tile_k, STRIP):
            raised = jnp.exp(raw[begin : begin + STRIP, :] - highest)
            chances[begin : begin + STRIP, :] = raised.astype(BF16)
            for group in range(0, STRIP, 8):
                partial = partial + raised[group : group + 8]
        shrink = jnp.exp(high[...] - highest)
        sums[...] = sums[...] * shrink + jnp.sum(partial, axis=0, keepdims=True)
        total[...] = total[...] * shrink + dot(turned[tile], chances[...])
        high[...] = highest
        return 0

    upper = (index * tile_q + tile_q - 1) // tile_k + 1
    lax.fori_loop(lows[index], upper, one, 0)
    found = sums[...] > 0.0
    safe = jnp.where(found, sums[...], 1.0)
    result = fold_heads(total[...] * jnp.where(found, 1.0 / safe, 0.0), heads, tile_q)
    out[...] = result.astype(BF16)
    sent[...] = result.astype(BF16)
    log_total = jnp.where(found, high[...] + jnp.log(safe), 0.0)
    for head in range(heads):
        logs[head : head + 1, :] = log_total[:, head * tile_q : (head + 1) * tile_q]


def attend(pieces, place, lows, ends, bounds, nctx, block_rows, *needed):
    total_rows = nctx * block_rows
    width = pieces[0].shape[1] // 3
    heads = width // HEAD_DIM
    steps = total_rows // TILE_Q
    grid_spec = pltpu.PrefetchScalarGridSpec(
        num_scalar_prefetch=3,
        grid=(steps,),
        in_specs=[pl.BlockSpec((2, TILE_Q), lambda i, *_: (0, i))]
        + [whole(piece.shape) for piece in pieces]
        + anywhere(len(needed)),
        out_specs=[
            pl.BlockSpec((TILE_Q, width), lambda i, *_: (i, 0)),
            pl.BlockSpec((TILE_Q, width), lambda i, *_: (i, 0)),
            pl.BlockSpec((heads, TILE_Q), lambda i, *_: (0, i)),
        ],
        scratch_shapes=[
            pltpu.VMEM((total_rows, 3 * width), BF16),
            pltpu.VMEM((total_rows // TILE_K, width, TILE_K), BF16),
            pltpu.VMEM((width, heads * TILE_Q), F32),
            pltpu.VMEM((1, heads * TILE_Q), F32),
            pltpu.VMEM((1, heads * TILE_Q), F32),
            pltpu.VMEM((TILE_K, heads * TILE_Q), F32),
            pltpu.VMEM((TILE_K, heads * TILE_Q), BF16),
        ],
    )
    return pl.pallas_call(
        functools.partial(attend_kernel, nctx, heads, len(pieces), len(needed), block_rows),
        grid_spec=grid_spec,
        out_shape=[
            jax.ShapeDtypeStruct((total_rows, width), BF16),
            jax.ShapeDtypeStruct((total_rows, width), BF16),
            jax.ShapeDtypeStruct((heads, total_rows), F32),
        ],
        compiler_params=params(),
        cost_estimate=takes(200),
        name="attend",
    )(place, lows, ends, bounds, *pieces, *needed)


def attend_back_kernel(
    nctx, heads, count, extra, block_rows, place, lows, ends, bounds, logs, *refs
):
    pieces, refs = refs[:count], refs[count:]
    grad, attended, refs = refs[0], refs[1], refs[2 + extra :]
    here, near, far, refs = *refs[:3], refs[3:]
    held, turned, grad_keys, grad_values, grad_query, raw, raw_grad, chances, steps, merged = refs
    tile_q, tile_k = grad.shape[0], turned.shape[2]
    width = grad.shape[1]
    index = pl.program_id(0)
    scale = jnp.asarray(HEAD_DIM**-0.5, BF16)

    @pl.when(index == 0)
    def _():
        load_pieces(place[0], pieces, nctx, held, block_rows)
        for tile in range(turned.shape[0]):
            turned[tile] = jnp.transpose(
                held[tile * tile_k : (tile + 1) * tile_k, width : 2 * width]
            )
        grad_keys[...] = jnp.zeros_like(grad_keys)
        grad_values[...] = jnp.zeros_like(grad_values)

    query_rows = pl.ds(pl.multiple_of(index * tile_q, tile_q), tile_q)
    queries = stack_heads(held[query_rows, :width] * scale, heads)
    incoming = stack_heads(grad[...], heads)
    product = jnp.transpose(grad[...].astype(F32) * attended[...].astype(F32))
    centre = jnp.concatenate(
        [
            jnp.sum(product[head * HEAD_DIM : (head + 1) * HEAD_DIM, :], axis=0, keepdims=True)
            for head in range(heads)
        ],
        axis=1,
    )
    first_key = jnp.concatenate([bounds[0:1, :]] * heads, axis=1)
    last_key = jnp.concatenate([bounds[1:2, :]] * heads, axis=1)
    log_total = jnp.concatenate([logs[head : head + 1, :] for head in range(heads)], axis=1)
    grad_query[...] = jnp.zeros_like(grad_query)

    def one(tile, _):
        start = tile * tile_k
        key_rows = pl.ds(pl.multiple_of(start, tile_k), tile_k)
        raw[...] = dot_turned(held[key_rows, width : 2 * width], queries)
        raw_grad[...] = dot_turned(held[key_rows, 2 * width :], incoming)
        last = jnp.minimum(last_key, ends[tile] - 1) - start
        first = first_key - start
        for begin in range(0, tile_k, STRIP):
            at = slice(begin, begin + STRIP)
            row = lax.broadcasted_iota(jnp.int32, (STRIP, raw.shape[1]), 0) + begin
            allowed = (row <= last) & (row >= first)
            chance = jnp.exp(jnp.where(allowed, raw[at, :] - log_total, NEGATIVE))
            chances[at, :] = chance.astype(BF16)
            steps[at, :] = (chance * (raw_grad[at, :] - centre)).astype(BF16)
        grad_values[key_rows, :] += dot(chances[...], incoming)
        grad_keys[key_rows, :] += dot(steps[...], queries)
        grad_query[...] += dot(turned[tile], steps[...])
        return 0

    upper = (index * tile_q + tile_q - 1) // tile_k + 1
    lax.fori_loop(lows[index], upper, one, 0)
    merged[query_rows, :width] = (
        fold_heads(grad_query[...], heads, tile_q) * HEAD_DIM**-0.5
    ).astype(BF16)

    @pl.when(index == pl.num_programs(0) - 1)
    def _():
        merged[:, width : 2 * width] = grad_keys[...].astype(BF16)
        merged[:, 2 * width :] = grad_values[...].astype(BF16)
        outs = [here, near] + [far.at[way] for way in range(nctx - 2)]
        for way, out in enumerate(outs):
            first = jnp.bitwise_xor(place[0], way) * block_rows
            out[...] = merged[pl.ds(pl.multiple_of(first, block_rows), block_rows), :]


def attend_back(pieces, place, lows, ends, bounds, logs, grad, attended, nctx, block_rows, *needed):
    total_rows, width = grad.shape
    heads = width // HEAD_DIM
    by_tile = pl.BlockSpec((TILE_Q, width), lambda i, *_: (i, 0))
    sent = (block_rows, 3 * width)
    sent = [sent, sent, (nctx - 2, *sent)]
    grid_spec = pltpu.PrefetchScalarGridSpec(
        num_scalar_prefetch=3,
        grid=(total_rows // TILE_Q,),
        in_specs=[
            pl.BlockSpec((2, TILE_Q), lambda i, *_: (0, i)),
            pl.BlockSpec((heads, TILE_Q), lambda i, *_: (0, i)),
        ]
        + [whole(piece.shape) for piece in pieces]
        + [by_tile] * 2
        + anywhere(len(needed)),
        out_specs=[whole(shape) for shape in sent],
        scratch_shapes=[
            pltpu.VMEM((total_rows, 3 * width), BF16),
            pltpu.VMEM((total_rows // TILE_K, width, TILE_K), BF16),
            pltpu.VMEM((total_rows, width), F32),
            pltpu.VMEM((total_rows, width), F32),
            pltpu.VMEM((width, heads * TILE_Q), F32),
            pltpu.VMEM((TILE_K, heads * TILE_Q), F32),
            pltpu.VMEM((TILE_K, heads * TILE_Q), F32),
            pltpu.VMEM((TILE_K, heads * TILE_Q), BF16),
            pltpu.VMEM((TILE_K, heads * TILE_Q), BF16),
            pltpu.VMEM((total_rows, 3 * width), BF16),
        ],
    )
    return pl.pallas_call(
        functools.partial(
            attend_back_kernel, nctx, heads, len(pieces), len(needed), block_rows
        ),
        grid_spec=grid_spec,
        out_shape=[jax.ShapeDtypeStruct(shape, BF16) for shape in sent],
        compiler_params=params(),
        cost_estimate=takes(250),
        name="attend_back",
    )(place, lows, ends, bounds, logs, *pieces, grad, attended, *needed)


def mix_kernel(nctx, count, place, heads_in, weight, source, gain, bias, *refs):
    returned, mixed, *lows = refs[count:]
    rows, depth = mixed.shape
    step = pl.program_id(0)
    left = jnp.concatenate([heads_in[c, 0] for c in range(nctx)], axis=1)
    returned[...] = left

    @pl.when(step == 0)
    def _():
        mixed[...] = source[...].astype(F32)

    mixed[...] += dot_turned(left, weight[0])

    @pl.when(step == pl.num_programs(0) - 1)
    def _():
        values = mixed[...]
        values = values - jnp.mean(values, axis=1, keepdims=True)
        scaling = lax.rsqrt(jnp.mean(values * values, axis=1, keepdims=True) + EPSILON)
        values = (values * scaling * gain[...] + bias[...]).astype(BF16)
        part_rows = lows[0].shape[0]
        for part, low in enumerate(lows):
            low[...] = values[part * part_rows : (part + 1) * part_rows]


def mix(heads_in, weight, full, gain, bias, place, parts, *needed):
    nctx, tp, rows, piece = heads_in.shape
    depth = full.shape[1]
    head_width = nctx * piece
    grid_spec = pltpu.PrefetchScalarGridSpec(
        num_scalar_prefetch=1,
        grid=(tp,),
        in_specs=[
            pl.BlockSpec((nctx, 1, rows, piece), lambda k, s: (0, k, 0, 0)),
            pl.BlockSpec((1, depth, head_width), lambda k, s: (k, 0, 0)),
            pl.BlockSpec((rows, depth), lambda k, s: (s[0], 0)),
            whole((1, depth)),
            whole((1, depth)),
        ]
        + anywhere(len(needed)),
        out_specs=[
            pl.BlockSpec((rows, head_width), lambda k, s: (0, k)),
            whole((rows, depth)),
        ]
        + [whole((rows // parts, depth))] * parts,
    )
    return pl.pallas_call(
        functools.partial(mix_kernel, nctx, len(needed)),
        grid_spec=grid_spec,
        out_shape=[
            jax.ShapeDtypeStruct((rows, tp * head_width), BF16),
            jax.ShapeDtypeStruct((rows, depth), F32),
        ]
        + [jax.ShapeDtypeStruct((rows // parts, depth), BF16)] * parts,
        compiler_params=params(),
        cost_estimate=takes(50),
        name="mix",
    )(place, heads_in, weight, full, gain, bias, *needed)


def feed_kernel(cuts, parts, tp, first_one, place, low, cot, mixed, source, *refs):
    refs = refs[-(5 + parts + 4) :]
    kept, grad_gate, grad_up, hidden, out = refs[:5]
    partials, held, sems = refs[5 : 5 + parts], refs[-4:-1], refs[-1]
    unit = source.shape[1] // 3
    width = out.shape[2]

    def copies(index):
        first, size = cuts[index]
        at = pl.ds(first, size)
        return [
            pltpu.make_async_copy(
                source.at[:, pl.ds(which * unit, unit), at],
                held[which].at[:, :, at],
                sems.at[index * 3 + which],
            )
            for which in range(3)
        ]

    for index in range(len(cuts)):
        for copy in copies(index):
            copy.start()
    kept[...] = low[...]
    rows, depth = kept.shape[0] // parts, kept.shape[1]
    grads = jnp.concatenate([cot[block] for block in range(tp)], axis=1)
    for index, (first, size) in enumerate(cuts):
        for copy in copies(index):
            copy.wait()
        at = slice(first, first + size)
        gate_weight, up_weight, down_weight = [w[:, :, at].reshape(depth, size) for w in held]
        gate = dot(kept[...], gate_weight)
        up = dot(kept[...], up_weight)
        sigma = 1.0 / (1.0 + jnp.exp(-gate))
        active = gate * sigma
        hidden[:, at] = (active * up).astype(BF16)
        grad = dot(grads, down_weight)
        grad_gate[:, at] = (grad * up * sigma * (1.0 + gate * (1.0 - sigma))).astype(BF16)
        grad_up[:, at] = (grad * active).astype(BF16)
    gate_weight, up_weight, down_weight = [w[...].reshape(depth, w.shape[2]) for w in held]
    product = dot_turned(grad_gate[...], gate_weight) + dot_turned(grad_up[...], up_weight)
    for part in range(parts):
        partials[part][...] = product[part * rows : (part + 1) * rows].astype(BF16)
    values = dot_turned(hidden[...], down_weight)
    if first_one:
        values = values + mixed[...]
    for block in range(tp):
        out[block] = values[:, block * width : (block + 1) * width].astype(BF16)


def feed(low, cot, mixed, weights, step, tp, place, held, parts, *needed):
    rows, depth = low.shape
    part_rows = rows // parts
    blocks, triple, hidden = weights.shape
    cuts = []
    while sum(size for _, size in cuts) < hidden:
        first = sum(size for _, size in cuts)
        cuts.append((first, min(512, hidden - first)))
    by_owner = lambda columns: pl.BlockSpec(
        (rows, columns), lambda i, s: (lax.rem(s[0] - step + tp, tp), 0)
    )
    width = depth // tp
    blocks_of_owner = pl.BlockSpec(
        (tp, rows, width), lambda i, s: (0, lax.rem(s[0] - step + tp, tp), 0)
    )
    grid_spec = pltpu.PrefetchScalarGridSpec(
        num_scalar_prefetch=1,
        grid=(1,),
        in_specs=[whole((rows, depth)), blocks_of_owner, whole(mixed.shape)]
        + anywhere(1 + len(held) + len(needed)),
        out_specs=[by_owner(depth)]
        + [by_owner(hidden)] * 3
        + [blocks_of_owner]
        + [whole((part_rows, depth))] * parts,
        scratch_shapes=[pltpu.VMEM((blocks, triple // 3, hidden), BF16)] * 3
        + [pltpu.SemaphoreType.DMA((3 * len(cuts),))],
    )
    return pl.pallas_call(
        functools.partial(feed_kernel, tuple(cuts), parts, tp, step == 0),
        grid_spec=grid_spec,
        out_shape=[
            jax.ShapeDtypeStruct((tp * rows, columns), BF16)
            for columns in (depth, hidden, hidden, hidden)
        ]
        + [jax.ShapeDtypeStruct((tp, tp * rows, width), BF16)]
        + [jax.ShapeDtypeStruct((part_rows, depth), BF16)] * parts,
        input_output_aliases={5 + index: index for index in range(len(held))},
        compiler_params=params(),
        cost_estimate=takes(100),
        name="feed",
    )(place, low, cot, mixed, weights, *held, *needed)


def blame_halves(lefts, rights, place, unit, *needed, split=False):
    rows = lefts[0].shape[0]
    other = rights[0].shape[1]
    picked = lefts[1].shape[1] // unit
    chosen = pl.BlockSpec((rows, unit), lambda j, s: (0, 2 * (j ^ s[3]) + s[1] % 2))
    cut = pl.BlockSpec((rows, unit), lambda j, s: (0, j ^ s[3]))
    if split:
        shapes = [(2, unit // 2, other)] * 4
        targets = [whole(shape) for shape in shapes]
    else:
        shapes = [(picked * unit, other)]
        targets = [pl.BlockSpec((unit, other), lambda j, s: (j, 0))]

    def kernel(place, left_here, left_there, right_here, right_there, *refs):
        outs = refs[len(needed) :]
        product = 0.0
        for left, right in ((left_here, right_here), (left_there, right_there)):
            product = product + lax.dot_general(
                left[...], right[...], (((0,), (0,)), ((), ())), preferred_element_type=F32
            )
        product = product.astype(BF16)
        if not split:
            outs[0][...] = product
        for j in range(picked if split else 0):

            @pl.when(pl.program_id(0) == j)
            def _():
                outs[j // 2][j % 2] = product[: unit // 2]
                outs[2 + j % 2][j // 2] = product[unit // 2 :]

    grid_spec = pltpu.PrefetchScalarGridSpec(
        num_scalar_prefetch=1,
        grid=(picked,),
        in_specs=[chosen, cut] + [whole((rows, other))] * 2 + anywhere(len(needed)),
        out_specs=targets,
    )
    place = jnp.concatenate([place, place[2:3] * 2 + place[1:2] // 2 if split else 0 * place[:1]])
    outs = pl.pallas_call(
        kernel,
        grid_spec=grid_spec,
        out_shape=[jax.ShapeDtypeStruct(shape, BF16) for shape in shapes],
        compiler_params=params(),
        cost_estimate=takes(60),
        name="blame_halves",
    )(place, *lefts, *rights, *needed)
    return outs if split else outs[0]


def blame(left, right, *needed):
    rows, columns = left.shape
    if right.ndim == 3:
        steps, other = right.shape[0], right.shape[2]
        in_specs = [whole((rows, columns)), pl.BlockSpec((1, rows, other), lambda j: (j, 0, 0))]
        target, shape = pl.BlockSpec((columns, other), lambda j: (0, j)), (columns, steps * other)
    else:
        steps, other = 4, right.shape[1]
        in_specs = [pl.BlockSpec((rows, columns // steps), lambda j: (0, j)), whole((rows, other))]
        target, shape = pl.BlockSpec((columns // steps, other), lambda j: (j, 0)), (columns, other)

    def kernel(left, right, *refs):
        theirs = right[0] if len(right.shape) == 3 else right[...]
        refs[-1][...] = lax.dot_general(
            left[...], theirs, (((0,), (0,)), ((), ())), preferred_element_type=F32
        ).astype(BF16)

    return pl.pallas_call(
        kernel,
        grid=(steps,),
        in_specs=in_specs + anywhere(len(needed)),
        out_specs=target,
        out_shape=jax.ShapeDtypeStruct(shape, BF16),
        compiler_params=params(),
        cost_estimate=takes(60),
        name="blame",
    )(left, right, *needed)


def turn_kernel(nctx, count, parts, unit, place, *refs):
    arrived, own = refs[:parts], refs[parts : 2 * parts]
    mixed, cot, gain = refs[2 * parts : 2 * parts + 3]
    weight, refs = refs[2 * parts + 3], refs[2 * parts + 4 + count :]
    out, grad_mixed, grad_low, gain_grad, shift_grad, half = refs
    rows, depth = mixed.shape
    piece = out.shape[3]

    @pl.when(pl.program_id(0) == 0)
    def _():
        incoming = jnp.concatenate(
            [there[...].astype(F32) + here[...].astype(F32) for there, here in zip(arrived, own)]
        )
        values = mixed[...]
        values = values - jnp.mean(values, axis=1, keepdims=True)
        scaling = lax.rsqrt(jnp.mean(values * values, axis=1, keepdims=True) + EPSILON)
        normed = values * scaling
        shift_grad[...] = jnp.sum(incoming, axis=0, keepdims=True)
        gain_grad[...] = jnp.sum(incoming * normed, axis=0, keepdims=True)
        scaled = incoming * gain[...]
        grads = jnp.concatenate([cot[block] for block in range(cot.shape[0])], axis=1)
        total = grads.astype(F32) + scaling * (
            scaled
            - jnp.mean(scaled, axis=1, keepdims=True)
            - normed * jnp.mean(scaled * normed, axis=1, keepdims=True)
        )
        grad_mixed[...] = total
        grad_low[...] = total.astype(BF16)
        write_half(half, grad_low, 1 - lax.rem(place[1], 2), unit)

    product = dot(grad_low[...], weight[0])
    for c in range(nctx):
        out[c, 0] = product[:, c * piece : (c + 1) * piece].astype(BF16)


def turn(arrived, own, mixed, cot, gain, weight, place, nctx, tp, unit, *needed):
    rows, depth = mixed.shape
    parts = len(arrived)
    head_width = weight.shape[2]
    piece = head_width // nctx
    grid_spec = pltpu.PrefetchScalarGridSpec(
        num_scalar_prefetch=1,
        grid=(tp,),
        in_specs=[whole((rows // parts, depth))] * (2 * parts)
        + [whole((rows, depth))]
        + [
            pl.BlockSpec((tp, rows, depth // tp), lambda k, s: (0, s[0], 0)),
            whole((1, depth)),
            pl.BlockSpec((1, depth, head_width), lambda k, s: (k, 0, 0)),
        ]
        + anywhere(len(needed)),
        out_specs=[
            pl.BlockSpec((nctx, 1, rows, piece), lambda k, s: (0, k, 0, 0)),
            whole((rows, depth)),
            whole((rows, depth)),
            whole((1, depth)),
            whole((1, depth)),
            whole((rows, depth // 2)),
        ],
    )
    return pl.pallas_call(
        functools.partial(turn_kernel, nctx, len(needed), parts, unit),
        grid_spec=grid_spec,
        out_shape=[
            jax.ShapeDtypeStruct((nctx, tp, rows, piece), BF16),
            jax.ShapeDtypeStruct((rows, depth), F32),
            jax.ShapeDtypeStruct((rows, depth), BF16),
            jax.ShapeDtypeStruct((1, depth), F32),
            jax.ShapeDtypeStruct((1, depth), F32),
            jax.ShapeDtypeStruct((rows, depth // 2), BF16),
        ],
        compiler_params=params(),
        cost_estimate=takes(60),
        name="turn",
    )(place, *arrived, *own, mixed, cot, gain, weight, *needed)


def finish_kernel(nctx, tp, extra_count, place, *refs):
    pieces = refs[:nctx]
    cosine, sine_up, sine_down, full, extra, gain = refs[nctx : nctx + 6]
    weight, refs = refs[nctx + 6], refs[nctx + 7 + extra_count :]
    outs = refs[:tp]
    low, bias_grad, gain_grad, shift_grad, spare = refs[tp:]
    rows, wide = pieces[0].shape
    piece = wide // 3
    width = outs[0].shape[1]
    strip = spare.shape[0]
    extra_rows = extra.shape[0]

    @pl.when(pl.program_id(0) == 0)
    def _():
        bias_grad[...] = jnp.zeros_like(bias_grad)
        gain_grad[...] = jnp.zeros_like(gain_grad)
        shift_grad[...] = jnp.zeros_like(shift_grad)

    for step in range(nctx):
        source = jnp.bitwise_xor(place[1], step)
        for part in range(3):
            values = pieces[step][:, part * piece : (part + 1) * piece].astype(F32)
            if part < 2:
                values = (
                    values * cosine[...]
                    - pltpu.roll(values, piece - ROT // 2, 1) * sine_up[...]
                    - pltpu.roll(values, ROT // 2, 1) * sine_down[...]
                )
            columns = pl.ds(pl.multiple_of(source * wide + part * piece, piece), piece)
            bias_grad[:, columns] += jnp.sum(values, axis=0, keepdims=True)
            low[:, columns] = values.astype(BF16)

    incoming = dot_turned(low[...], weight[...])
    source = full[...].astype(F32)
    source = source - jnp.mean(source, axis=1, keepdims=True)
    scaling = lax.rsqrt(jnp.mean(source * source, axis=1, keepdims=True) + EPSILON)
    normed = source * scaling
    shift_grad[...] += jnp.sum(incoming, axis=0, keepdims=True)
    gain_grad[...] += jnp.sum(incoming * normed, axis=0, keepdims=True)
    scaled = incoming * gain[...]
    spare[...] = scaling * (
        scaled
        - jnp.mean(scaled, axis=1, keepdims=True)
        - normed * jnp.mean(scaled * normed, axis=1, keepdims=True)
    )
    first = pl.program_id(0) * strip
    wanted = place[0] * extra_rows

    if strip <= extra_rows:

        @pl.when((first >= wanted) & (first < wanted + extra_rows))
        def _():
            spare[...] += extra[pl.ds(pl.multiple_of(first - wanted, strip), strip), :]

    else:

        @pl.when((wanted >= first) & (wanted < first + strip))
        def _():
            spare[pl.ds(pl.multiple_of(wanted - first, extra_rows), extra_rows), :] += extra[...]

    for step, out in enumerate(outs):
        owner = lax.rem(place[0] - step + tp, tp)
        out[...] = spare[:, pl.ds(pl.multiple_of(owner * width, width), width)].astype(BF16)


def finish(pieces, place, tables, full, extra, gain, weight, tp, *needed):
    rows, wide = pieces[0].shape
    depth = full.shape[1]
    total = weight.shape[1]
    strip = 256
    steps = rows // strip
    width = depth // tp
    nctx = len(pieces)
    by_rows = lambda columns: pl.BlockSpec((strip, columns), lambda i, s: (i, 0))
    grid_spec = pltpu.PrefetchScalarGridSpec(
        num_scalar_prefetch=1,
        grid=(steps,),
        in_specs=[by_rows(wide)] * nctx
        + [by_rows(2 * HEAD_DIM)] * 3
        + [
            by_rows(depth),
            whole(extra.shape),
            whole((1, depth)),
        ]
        + [whole(weight.shape)]
        + anywhere(len(needed)),
        out_specs=[by_rows(width)] * tp
        + [
            by_rows(total),
            whole((1, total)),
            whole((1, depth)),
            whole((1, depth)),
        ],
        scratch_shapes=[pltpu.VMEM((strip, depth), F32)],
    )
    return pl.pallas_call(
        functools.partial(finish_kernel, nctx, tp, len(needed)),
        grid_spec=grid_spec,
        out_shape=[jax.ShapeDtypeStruct((rows, width), BF16)] * tp
        + [
            jax.ShapeDtypeStruct((rows, total), BF16),
            jax.ShapeDtypeStruct((1, total), F32),
            jax.ShapeDtypeStruct((1, depth), F32),
            jax.ShapeDtypeStruct((1, depth), F32),
        ],
        compiler_params=params(),
        cost_estimate=takes(70),
        name="finish",
    )(place, *pieces, *tables, full, extra, gain, weight, *needed)


def join(rings, place):
    parts, tp = len(rings), len(rings[0])
    rows, width = rings[0][0].shape

    def kernel(place, *refs):
        for part in range(parts):
            for step in range(tp):
                owner = lax.rem(place[0] - step + tp, tp)
                refs[-1][owner, part * rows : (part + 1) * rows, :] = refs[part * tp + step][...]

    grid_spec = pltpu.PrefetchScalarGridSpec(
        num_scalar_prefetch=1,
        grid=(1,),
        in_specs=[whole((rows, width))] * (parts * tp),
        out_specs=whole((tp, parts * rows, width)),
    )
    return pl.pallas_call(
        kernel,
        grid_spec=grid_spec,
        out_shape=jax.ShapeDtypeStruct((tp, parts * rows, width), BF16),
        compiler_params=params(),
        cost_estimate=takes(10),
        name="join",
    )(place, *[block for blocks in rings for block in blocks])


def pack_kernel(gate, up, down, out):
    rows = gate.shape[0]
    out[:rows] = gate[...]
    out[rows : 2 * rows] = up[...]
    out[2 * rows :] = jnp.transpose(down[...])


def pack(gate, up, down):
    rows, columns = gate.shape
    return pl.pallas_call(
        pack_kernel,
        out_shape=jax.ShapeDtypeStruct((3 * rows, columns), BF16),
        compiler_params=params(),
        cost_estimate=takes(10),
        name="pack",
    )(gate, up, down)


def contract_rows(left, right):
    return lax.dot_general(left, right, (((0,), (0,)), ((), ())), preferred_element_type=F32)


def pick(stack, index):
    return lax.dynamic_index_in_dim(stack, index, 0, keepdims=False)


def shards(
    nfsdp,
    nctx,
    tp,
    inputs,
    cotangent,
    first_gain,
    first_bias,
    qkv_weight,
    qkv_bias,
    out_weight,
    second_gain,
    second_bias,
    gate_weight,
    up_weight,
    down_weight,
    lengths,
    fill_counts,
):
    data = ("fsdp", "ctx")
    ndata = nfsdp * nctx
    block_rows, width = inputs.shape
    depth = tp * width
    half_depth = depth // 2
    unit = depth // ndata
    tensor_index = lax.axis_index("tp").astype(jnp.int32)
    context_index = lax.axis_index("ctx").astype(jnp.int32)
    fsdp_index = lax.axis_index("fsdp").astype(jnp.int32)
    part_rows = block_rows // tp
    chunk_rows = block_rows // CHUNKS
    head_width = qkv_weight.shape[2]
    piece = head_width // nctx
    wide = 3 * piece

    square = nfsdp == 2 and nctx == 4 and unit % 128 == 0
    place = jnp.stack([tensor_index, context_index, fsdp_index])

    def shift(value, step):
        return lax.ppermute(value, "tp", [(i, (i + step) % tp) for i in range(tp)])

    def swap(value, step):
        return lax.ppermute(value, "ctx", [(i, i ^ step) for i in range(nctx)])

    core_index = context_index % 2
    groups = [list(range(0, ndata, 2)), list(range(1, ndata, 2))]
    def mate(value):
        return swap(value, 1)

    def send(here, near, far, *needed):
        far = swap(far, 2)
        return [here, swap(near, 1), far[0], swap(tie(far[1], *needed), 1)]

    def scatter_half(value, axis):
        return lax.psum_scatter(
            value, data, scatter_dimension=axis, tiled=True, axis_index_groups=groups
        )

    def scatter(value, axis):
        return lax.psum_scatter(value, data, scatter_dimension=axis, tiled=True)

    def cross(value):
        return lax.ppermute(value, "fsdp", [(i, i ^ 1) for i in range(nfsdp)])

    def square_sum(parts):
        near, far, low, high = parts
        first = total(near, cross(far))
        second = total(low, swap(high, 2))
        first = first[0].astype(F32) + swap(first[1], 2).astype(F32)
        second = second[0].astype(F32) + cross(second[1]).astype(F32)
        return jnp.concatenate([first, second], axis=0)

    def total(left, right):
        return (left.astype(F32) + right.astype(F32)).astype(BF16)

    owners = [(tensor_index - step + tp) % tp for step in range(tp)]

    own_qkv = (
        qkv_weight.reshape(-1, 3, nctx, piece).transpose(0, 2, 1, 3).reshape(-1, 3 * head_width)
    )
    full_qkv = lax.all_gather(own_qkv, data, axis=0, tiled=True)
    own_feed = pack(gate_weight, up_weight, down_weight)
    feed_weights = lax.all_gather(own_feed, data, axis=0, tiled=True).reshape(ndata, 3 * unit, -1)

    validity, position, first_key, last_key = layout(lengths[0], fill_counts[0], block_rows)
    own_position = lax.dynamic_slice_in_dim(position, context_index * block_rows, block_rows, 0)
    tables = rotary_tables(own_position)
    bounds = jnp.stack([first_key, last_key])
    tile_first = first_key[::TILE_Q]
    tile_count = tile_first.shape[0]
    lows = jnp.where(validity[::TILE_Q], tile_first // TILE_K, tile_count * TILE_Q).astype(jnp.int32)
    key_block = jnp.arange(0, nctx * block_rows, TILE_K, dtype=jnp.int32) // block_rows
    ends = (
        key_block * block_rows
        + jnp.sum(
            jnp.where(
                key_block[:, None] == jnp.arange(nctx, dtype=jnp.int32)[None, :],
                fill_counts[0][None, :],
                0,
            ),
            axis=1,
        )
    ).astype(jnp.int32)

    flat_bias = qkv_bias.reshape(3, nctx, piece).transpose(1, 0, 2).reshape(1, -1)
    gain_one, bias_one = first_gain[None], first_bias[None]
    gain_two, bias_two = second_gain[None], second_bias[None]

    rings = [[inputs[c * chunk_rows : (c + 1) * chunk_rows]] for c in range(CHUNKS)]
    share = unit // CHUNKS
    for chunk in range(CHUNKS):
        carried = out_weight.T[chunk * share : (chunk + 1) * share]
        rings[chunk][0] = jnp.concatenate([rings[chunk][0], carried], axis=0)
    for chunk in range(CHUNKS):
        for _ in range(tp - 1):
            rings[chunk].append(shift(rings[chunk][-1], 1))
            if len(rings[chunk]) == 2:
                rings[chunk][-1] = tie(rings[chunk][-1], own_feed)
    all_low, full, low_half, *outgoing, stack = project(
        rings, place, gain_one, bias_one, full_qkv, flat_bias, tables, nctx, unit
    )
    full_out = lax.all_gather(stack, data, axis=1, tiled=True)

    cot = tie(cotangent, *[blocks[-1] for blocks in rings])
    cot_rings = [[cot[c * chunk_rows : (c + 1) * chunk_rows]] for c in range(CHUNKS)]
    for blocks in cot_rings:
        for _ in range(tp - 1):
            blocks.append(shift(blocks[-1], 1))
    pieces = send(*outgoing, *[blocks[max(tp - 2, 0)] for blocks in cot_rings])

    attended, outgoing, logs = attend(
        pieces,
        place[1:2],
        lows,
        ends,
        bounds,
        nctx,
        block_rows,
        feed_weights,
    )
    cot = join(cot_rings, place)
    arrived = lax.all_to_all(
        tie(outgoing, *[blocks[-1] for blocks in cot_rings]).reshape(nctx * tp, part_rows, piece),
        ("ctx", "tp"),
        split_axis=0,
        concat_axis=0,
        tiled=True,
    )
    returned, mixed, second_low = mix(
        arrived.reshape(nctx, tp, part_rows, piece),
        full_out,
        full,
        gain_two,
        bias_two,
        place,
        1,
    )

    arrived, held, partials, travelling = second_low, [], [], None
    for step in range(tp):
        coming = shift(arrived, 1) if step < tp - 1 else None
        needed = travelling if step == tp - 1 and step > 2 else []
        *held, first, second = feed(
            arrived, cot, mixed, feed_weights, step, tp, place, held, HALVES, *needed
        )
        partials.append([first, second])
        if step == 1 % tp:
            travelling = partials[step]
        elif step > 1:
            travelling = [
                total(shift(value, 1), kept) for value, kept in zip(travelling, partials[step])
            ]
        if step == 0 and coming is not None:
            coming = tie(coming, partials[0][0])
        arrived = coming
    all_second, all_gate, all_up, hidden, feedforward = held

    last = [shift(value, 1) for value in travelling]
    half_gate = blame(all_second, all_gate, *travelling)
    half_up = blame(all_second, all_up, *travelling)
    half_down = blame(hidden, cot, *travelling)
    grad_heads, grad_mixed, mixed_low, gain_grad_two, shift_grad_two, mixed_half = turn(
        last,
        partials[0],
        mixed,
        cot,
        gain_two,
        full_out,
        place,
        nctx,
        tp,
        unit,
        half_gate,
        half_up,
        half_down,
    )
    grad_heads = lax.all_to_all(
        grad_heads.reshape(nctx * tp, part_rows, piece),
        ("ctx", "tp"),
        split_axis=0,
        concat_axis=0,
        tiled=True,
    ).reshape(nctx * block_rows, piece)

    total_gate = scatter(tie(half_gate, mixed_low), 0).astype(F32)
    total_up = scatter(tie(half_up, mixed_low), 0).astype(F32)
    total_down = scatter(tie(half_down, mixed_low), 1).astype(F32)

    feedforward = tie(feedforward, grad_heads)
    layer_out = [pick(feedforward, owners[1 % tp])]
    for step in range(1, tp):
        kept = pick(feedforward, owners[(step + 1) % tp])
        layer_out.append(total(shift(layer_out[-1], 1), kept))

    grad_pieces = attend_back(
        pieces, place[1:2], lows, ends, bounds, logs, grad_heads, attended, nctx, block_rows
    )
    arrived = send(*grad_pieces, *layer_out[max(tp - 2, 0) : tp - 1])
    layer_out = layer_out[-1]
    if square:
        out_parts = blame_halves(
            (mixed_low, mate(mixed_half)),
            (returned, mate(returned)),
            place,
            unit,
            arrived[2],
            split=True,
        )
        half_out = out_parts[0]
    else:
        half_out = blame(mixed_low, returned)
        total_out = scatter(half_out, 0).astype(F32)
    low_halves = mate(low_half) if square else low_half
    needed = [layer_out, low_halves, half_out]
    *partial, all_grad, bias_grad, gain_grad, shift_grad = finish(
        arrived, place, tables, full, grad_mixed, gain_one, full_qkv, tp, *needed
    )
    parts = []
    if square:
        parts = blame_halves((all_low, low_halves), (all_grad, mate(all_grad)), place, unit, split=True)
    if square:
        total_out = square_sum(out_parts)
    travelling, ring_steps = partial[1 % tp], []
    needed = [[total_gate, total_up, total_out, *parts[:1]], [], [total_down]]
    for step in range(1, tp):
        travelling = add(
            shift(travelling, 1), partial[(step + 1) % tp], *(needed[step - 1] if step < 4 else [])
        )
        ring_steps.append(travelling)
    grad_inputs = travelling
    if square:
        total_qkv = square_sum(parts)
    else:
        total_qkv = scatter(blame(all_low, all_grad), 0).astype(F32)

    total_qkv = (
        total_qkv
        .reshape(-1, nctx, 3, piece)
        .transpose(0, 2, 1, 3)
        .reshape(-1, 3, head_width)
    )

    def exchange(value, axis, size):
        step = 1
        while step < size:
            value = value + lax.ppermute(value, axis, [(i, i ^ step) for i in range(size)])
            step *= 2
        return value

    out_parts = jnp.swapaxes(
        tie(total_out.astype(BF16), *ring_steps[1:2]).reshape(-1, tp, head_width), 0, 1
    )
    total_out = pick(out_parts, tensor_index).astype(F32)
    for step in range(1, tp):
        total_out = total_out + shift(pick(out_parts, (tensor_index + step) % tp), step).astype(F32)
    total_out = total_out.T

    small = jnp.concatenate(
        [bias_grad, gain_grad, shift_grad, gain_grad_two, shift_grad_two], axis=1
    )
    small = exchange(exchange(small, "ctx", nctx), "fsdp", nfsdp)
    bias_total, small = small[:, : 3 * head_width], small[:, 3 * head_width :]
    small, step = tie(small, *ring_steps[:1]), 1
    while step < tp:
        small = small + lax.ppermute(small, "tp", [(i, i ^ step) for i in range(tp)])
        step *= 2
        if step < tp:
            small = tie(small, *ring_steps[1:2])
    bias_total = bias_total.reshape(nctx, 3, piece).transpose(1, 0, 2).reshape(3, head_width)
    small = small.reshape(4, depth)
    return (
        layer_out,
        grad_inputs,
        small[0],
        small[1],
        total_qkv,
        bias_total,
        total_out,
        small[2],
        small[3],
        total_gate,
        total_up,
        total_down,
    )


def solution(mesh):
    data = ("fsdp", "ctx")
    by_rows = P(data, "tp")
    by_columns = P("tp", data)
    qkv = P(data, None, "tp")
    return jax.shard_map(
        functools.partial(shards, mesh.shape["fsdp"], mesh.shape["ctx"], mesh.shape["tp"]),
        mesh=mesh,
        in_specs=(
            by_rows,
            by_rows,
            P(),
            P(),
            qkv,
            P(None, "tp"),
            by_columns,
            P(),
            P(),
            by_rows,
            by_rows,
            by_columns,
            P("fsdp", None),
            P("fsdp", None),
        ),
        out_specs=(
            by_rows,
            by_rows,
            P(),
            P(),
            qkv,
            P(None, "tp"),
            by_columns,
            P(),
            P(),
            by_rows,
            by_rows,
            by_columns,
        ),
        check_vma=False,
    )
```

```python
import functools

import jax
import jax.numpy as jnp
from jax import lax
from jax.experimental import pallas as pl
from jax.experimental.pallas import tpu as pltpu
from jax.sharding import PartitionSpec as P

HEAD_DIM = 64
ROT = 16
EPSILON = 1e-05
NEGATIVE = -1e30
FLOOR = -1e20
VMEM_LIMIT = 56 * 1024 * 1024
TILE_Q = 512
TILE_K = 512
STRIP = 32
CHUNKS = 2
HALVES = 2

F32 = jnp.float32
BF16 = jnp.bfloat16


def layout(lengths, fill_counts, block_rows):
    blocks_count = fill_counts.shape[0]
    seq_count = lengths.shape[0]
    slot_index = jnp.arange(blocks_count * block_rows, dtype=jnp.int32)
    block_of = slot_index // block_rows
    within = slot_index - block_of * block_rows
    chooser = block_of[:, None] == jnp.arange(blocks_count, dtype=jnp.int32)[None, :]
    fill_here = jnp.sum(jnp.where(chooser, fill_counts[None, :], 0), axis=1)
    before = jnp.cumsum(fill_counts) - fill_counts
    before_here = jnp.sum(jnp.where(chooser, before[None, :], 0), axis=1)
    validity = within < fill_here
    used_index = before_here + within
    seq_ends = jnp.cumsum(lengths)
    sequence = jnp.sum((used_index[:, None] >= seq_ends[None, :]).astype(jnp.int32), axis=1)
    seq_starts = seq_ends - lengths
    picker = sequence[:, None] == jnp.arange(seq_count, dtype=jnp.int32)[None, :]
    start_here = jnp.sum(jnp.where(picker, seq_starts[None, :], 0), axis=1)
    after = before + fill_counts
    start_block = jnp.sum((seq_starts[:, None] >= after[None, :]).astype(jnp.int32), axis=1)
    start_block = jnp.minimum(start_block, blocks_count - 1)
    block_pick = start_block[:, None] == jnp.arange(blocks_count, dtype=jnp.int32)[None, :]
    start_before = jnp.sum(jnp.where(block_pick, before[None, :], 0), axis=1)
    start_slot = start_block * block_rows + seq_starts - start_before
    slot_here = jnp.sum(jnp.where(picker, start_slot[None, :], 0), axis=1)
    first_key = jnp.where(validity, slot_here, 0).astype(jnp.int32)
    last_key = jnp.where(validity, slot_index, -1).astype(jnp.int32)
    return (validity, used_index - start_here, first_key, last_key)


def rotary_tables(position):
    half = ROT // 2
    lane = jnp.arange(2 * HEAD_DIM, dtype=jnp.int32) % HEAD_DIM
    frequency = 10000.0 ** (-(2.0 * (lane % half).astype(F32)) / ROT)
    angles = position.astype(F32)[:, None] * frequency[None, :]
    cosine, sine = jnp.cos(angles), jnp.sin(angles)
    lane = lane[None, :]
    return (
        jnp.where(lane < ROT, cosine, 1.0),
        jnp.where(lane < half, -sine, 0.0),
        jnp.where((lane >= half) & (lane < ROT), sine, 0.0),
    )


def params(**extra):
    return pltpu.CompilerParams(vmem_limit_bytes=VMEM_LIMIT, **extra)


def takes(microseconds):
    return pl.CostEstimate(
        flops=int(microseconds * 1e8), bytes_accessed=0, transcendentals=0
    )


def whole(shape):
    return pl.BlockSpec(shape, lambda *_: (0,) * len(shape))


def anywhere(count):
    return [pl.BlockSpec(memory_space=pl.ANY)] * count


def write_half(out, values, half, unit):
    if unit % 128:
        out[...] = values[:, : out.shape[1]]
        return
    for block in range(out.shape[1] // unit):
        first = pl.multiple_of((2 * block + half) * unit, unit)
        out[:, block * unit : (block + 1) * unit] = values[:, pl.ds(first, unit)]


def dot(left, right):
    return jnp.dot(left, right, preferred_element_type=F32)


def dot_turned(left, right):
    return lax.dot_general(left, right, (((1,), (1,)), ((), ())), preferred_element_type=F32)


def tie(value, *needed):
    def kernel(*refs):
        del refs

    return pl.pallas_call(
        kernel,
        in_specs=anywhere(1 + len(needed)),
        out_specs=pl.BlockSpec(memory_space=pl.ANY),
        out_shape=jax.ShapeDtypeStruct(value.shape, value.dtype),
        input_output_aliases={0: 0},
        name="tie",
    )(value, *needed)


def add_kernel(left, right, *refs):
    refs[-1][...] = (left[...].astype(F32) + right[...].astype(F32)).astype(BF16)


def add(left, right, *needed):
    rows, columns = left.shape
    strip = min(rows, 512)
    block = pl.BlockSpec((strip, columns), lambda i: (i, 0))
    return pl.pallas_call(
        add_kernel,
        grid=(rows // strip,),
        in_specs=[block, block] + anywhere(len(needed)),
        out_specs=block,
        out_shape=jax.ShapeDtypeStruct(left.shape, BF16),
        compiler_params=params(),
        cost_estimate=takes(10),
        name="ring_add",
    )(left, right, *needed)


def project_kernel(tp, chunks, per, unit, place, *refs):
    rings, refs = refs[: tp * chunks], refs[tp * chunks :]
    gain, bias, weight, weight_bias, cosine, sine_up, sine_down = refs[:7]
    low, full, half, here, near, far, stack = refs[7:]
    outs = [here, near] + [far.at[way] for way in range(far.shape[0])]
    rows, width = low.shape[0] // chunks, rings[0].shape[1]
    depth = tp * width
    wide = here.shape[1]
    piece = wide // 3
    step = pl.program_id(0)

    @pl.when(pl.program_id(0) == 0)
    def _():
        strip = 128
        for start in range(0, rows * chunks, strip):
            chunk, first = start // rows, start % rows
            blocks = rings[chunk * tp : (chunk + 1) * tp]
            at = slice(start, start + strip)
            inner = slice(first, first + strip)
            parts = [block[inner, :].astype(F32) for block in blocks]
            centre = sum(jnp.sum(part, axis=1, keepdims=True) for part in parts) / depth
            parts = [part - centre for part in parts]
            spread = sum(jnp.sum(part * part, axis=1, keepdims=True) for part in parts) / depth
            scaling = lax.rsqrt(spread + EPSILON)
            for step in range(tp):
                owner = lax.rem(place[0] - step + tp, tp)
                columns = pl.ds(pl.multiple_of(owner * width, width), width)
                low[at, columns] = (
                    parts[step] * scaling * gain[:, columns] + bias[:, columns]
                ).astype(BF16)
                full[at, columns] = blocks[step][inner, :]
        write_half(half, low, 1 - lax.rem(place[1], 2), unit)
        share = rings[0].shape[0] - rows
        for chunk in range(chunks):
            for step in range(tp):
                owner = lax.rem(place[0] - step + tp, tp)
                stack[owner, chunk * share : (chunk + 1) * share, :] = rings[chunk * tp + step][
                    rows:, :
                ]

    product = dot(low[...], weight[...]) + weight_bias[...]
    groups = []
    for group in range(per):
        parts = []
        for part in range(3):
            first = (group * 3 + part) * piece
            values = product[:, first : first + piece]
            if part < 2:
                values = (
                    values * cosine[...]
                    + pltpu.roll(values, piece - ROT // 2, 1) * sine_up[...]
                    + pltpu.roll(values, ROT // 2, 1) * sine_down[...]
                )
            parts.append(values.astype(BF16))
        groups.append(parts)
    flip = lax.rem(place[1], per)
    for way, out in enumerate(outs):
        for group in range(per):

            @pl.when((step == way // per) & (jnp.bitwise_xor(group, flip) == way % per))
            def _():
                for part in range(3):
                    out[:, part * piece : (part + 1) * piece] = groups[group][part]


def project(rings, place, gain, bias, weight, weight_bias, tables, nctx, unit):
    chunks, tp = len(rings), len(rings[0])
    rows, width = tables[0].shape[0], rings[0][0].shape[1]
    depth = tp * width
    total = weight.shape[1]
    wide = total // nctx
    per = 2 if nctx % 2 == 0 else 1
    grid_spec = pltpu.PrefetchScalarGridSpec(
        num_scalar_prefetch=1,
        grid=(nctx // per,),
        in_specs=[whole(rings[0][0].shape)] * (tp * chunks)
        + [whole((1, depth))] * 2
        + [
            pl.BlockSpec((depth, per * wide), lambda i, s: (0, jnp.bitwise_xor(i, s[1] // per))),
            pl.BlockSpec((1, per * wide), lambda i, s: (0, jnp.bitwise_xor(i, s[1] // per))),
        ]
        + [whole((rows, 2 * HEAD_DIM))] * 3,
        out_specs=[whole((rows, depth))] * 2
        + [whole((rows, depth // 2))]
        + [whole((rows, wide))] * 2
        + [whole((nctx - 2, rows, wide)), whole((tp, unit, width))],
    )
    return pl.pallas_call(
        functools.partial(project_kernel, tp, chunks, per, unit),
        grid_spec=grid_spec,
        out_shape=[
            jax.ShapeDtypeStruct((rows, depth), BF16),
            jax.ShapeDtypeStruct((rows, depth), BF16),
            jax.ShapeDtypeStruct((rows, depth // 2), BF16),
        ]
        + [jax.ShapeDtypeStruct((rows, wide), BF16)] * 2
        + [
            jax.ShapeDtypeStruct((nctx - 2, rows, wide), BF16),
            jax.ShapeDtypeStruct((tp, unit, width), BF16),
        ],
        compiler_params=params(),
        cost_estimate=takes(60),
        name="project",
    )(
        place,
        *[block for blocks in rings for block in blocks],
        gain,
        bias,
        weight,
        weight_bias,
        *tables,
    )


def stack_heads(tile, heads):
    lane = lax.broadcasted_iota(jnp.int32, tile.shape, 1) // HEAD_DIM
    return jnp.concatenate(
        [jnp.where(lane == head, tile, jnp.zeros_like(tile)) for head in range(heads)], axis=0
    )


def fold_heads(stacked, heads, columns):
    row = lax.broadcasted_iota(jnp.int32, (stacked.shape[0], columns), 0) // HEAD_DIM
    folded = jnp.zeros((stacked.shape[0], columns), F32)
    for head in range(heads):
        folded = folded + jnp.where(row == head, stacked[:, head * columns : (head + 1) * columns], 0.0)
    return jnp.transpose(folded)


def load_pieces(place, pieces, nctx, held, block_rows):
    chunk_rows = pieces[0].shape[0]
    chunks = len(pieces) // nctx
    for chunk in range(chunks):
        for step in range(nctx):
            source = jnp.bitwise_xor(place, step)
            first = source * block_rows + chunk * chunk_rows
            held[pl.ds(pl.multiple_of(first, chunk_rows), chunk_rows), :] = pieces[
                chunk * nctx + step
            ][...]


def attend_kernel(nctx, heads, count, extra, block_rows, place, lows, ends, bounds, *refs):
    pieces = refs[:count]
    out, sent, logs, held, turned, total, high, sums, raw, chances = refs[count + extra :]
    tile_q, tile_k = out.shape[0], turned.shape[2]
    width = heads * HEAD_DIM
    index = pl.program_id(0)

    @pl.when(index == 0)
    def _():
        load_pieces(place[0], pieces, nctx, held, block_rows)
        for tile in range(turned.shape[0]):
            turned[tile] = jnp.transpose(held[tile * tile_k : (tile + 1) * tile_k, 2 * width :])

    query_rows = pl.ds(pl.multiple_of(index * tile_q, tile_q), tile_q)
    queries = stack_heads(held[query_rows, :width] * jnp.asarray(HEAD_DIM**-0.5, BF16), heads)
    first_key = jnp.concatenate([bounds[0:1, :]] * heads, axis=1)
    last_key = jnp.concatenate([bounds[1:2, :]] * heads, axis=1)
    total[...] = jnp.zeros_like(total)
    high[...] = jnp.full_like(high, FLOOR)
    sums[...] = jnp.zeros_like(sums)

    def one(tile, _):
        start = tile * tile_k
        keys = held[pl.ds(pl.multiple_of(start, tile_k), tile_k), width : 2 * width]
        raw[...] = dot_turned(keys, queries)
        last = jnp.minimum(last_key, ends[tile] - 1) - start
        first = first_key - start
        peaks = jnp.broadcast_to(high[...], (8, raw.shape[1]))
        for begin in range(0, tile_k, STRIP):
            scores = raw[begin : begin + STRIP, :]
            row = lax.broadcasted_iota(jnp.int32, scores.shape, 0) + begin
            scores = jnp.where((row <= last) & (row >= first), scores, NEGATIVE)
            raw[begin : begin + STRIP, :] = scores
            for group in range(0, STRIP, 8):
                peaks = jnp.maximum(peaks, scores[group : group + 8])
        highest = jnp.max(peaks, axis=0, keepdims=True)
        partial = jnp.zeros((8, raw.shape[1]), F32)
        for begin in range(0, tile_k, STRIP):
            raised = jnp.exp(raw[begin : begin + STRIP, :] - highest)
            chances[begin : begin + STRIP, :] = raised.astype(BF16)
            for group in range(0, STRIP, 8):
                partial = partial + raised[group : group + 8]
        shrink = jnp.exp(high[...] - highest)
        sums[...] = sums[...] * shrink + jnp.sum(partial, axis=0, keepdims=True)
        total[...] = total[...] * shrink + dot(turned[tile], chances[...])
        high[...] = highest
        return 0

    upper = (index * tile_q + tile_q - 1) // tile_k + 1
    lax.fori_loop(lows[index], upper, one, 0)
    found = sums[...] > 0.0
    safe = jnp.where(found, sums[...], 1.0)
    result = fold_heads(total[...] * jnp.where(found, 1.0 / safe, 0.0), heads, tile_q)
    out[...] = result.astype(BF16)
    sent[...] = result.astype(BF16)
    log_total = jnp.where(found, high[...] + jnp.log(safe), 0.0)
    for head in range(heads):
        logs[head : head + 1, :] = log_total[:, head * tile_q : (head + 1) * tile_q]


def attend(pieces, place, lows, ends, bounds, nctx, block_rows, *needed):
    total_rows = nctx * block_rows
    width = pieces[0].shape[1] // 3
    heads = width // HEAD_DIM
    steps = total_rows // TILE_Q
    grid_spec = pltpu.PrefetchScalarGridSpec(
        num_scalar_prefetch=3,
        grid=(steps,),
        in_specs=[pl.BlockSpec((2, TILE_Q), lambda i, *_: (0, i))]
        + [whole(piece.shape) for piece in pieces]
        + anywhere(len(needed)),
        out_specs=[
            pl.BlockSpec((TILE_Q, width), lambda i, *_: (i, 0)),
            pl.BlockSpec((TILE_Q, width), lambda i, *_: (i, 0)),
            pl.BlockSpec((heads, TILE_Q), lambda i, *_: (0, i)),
        ],
        scratch_shapes=[
            pltpu.VMEM((total_rows, 3 * width), BF16),
            pltpu.VMEM((total_rows // TILE_K, width, TILE_K), BF16),
            pltpu.VMEM((width, heads * TILE_Q), F32),
            pltpu.VMEM((1, heads * TILE_Q), F32),
            pltpu.VMEM((1, heads * TILE_Q), F32),
            pltpu.VMEM((TILE_K, heads * TILE_Q), F32),
            pltpu.VMEM((TILE_K, heads * TILE_Q), BF16),
        ],
    )
    return pl.pallas_call(
        functools.partial(attend_kernel, nctx, heads, len(pieces), len(needed), block_rows),
        grid_spec=grid_spec,
        out_shape=[
            jax.ShapeDtypeStruct((total_rows, width), BF16),
            jax.ShapeDtypeStruct((total_rows, width), BF16),
            jax.ShapeDtypeStruct((heads, total_rows), F32),
        ],
        compiler_params=params(),
        cost_estimate=takes(200),
        name="attend",
    )(place, lows, ends, bounds, *pieces, *needed)


def attend_back_kernel(
    nctx, heads, count, extra, block_rows, place, lows, ends, bounds, logs, *refs
):
    pieces, refs = refs[:count], refs[count:]
    grad, attended, refs = refs[0], refs[1], refs[2 + extra :]
    here, near, far, refs = *refs[:3], refs[3:]
    held, turned, grad_keys, grad_values, grad_query, raw, raw_grad, chances, steps, merged = refs
    tile_q, tile_k = grad.shape[0], turned.shape[2]
    width = grad.shape[1]
    index = pl.program_id(0)
    scale = jnp.asarray(HEAD_DIM**-0.5, BF16)

    @pl.when(index == 0)
    def _():
        load_pieces(place[0], pieces, nctx, held, block_rows)
        for tile in range(turned.shape[0]):
            turned[tile] = jnp.transpose(
                held[tile * tile_k : (tile + 1) * tile_k, width : 2 * width]
            )
        grad_keys[...] = jnp.zeros_like(grad_keys)
        grad_values[...] = jnp.zeros_like(grad_values)

    query_rows = pl.ds(pl.multiple_of(index * tile_q, tile_q), tile_q)
    queries = stack_heads(held[query_rows, :width] * scale, heads)
    incoming = stack_heads(grad[...], heads)
    product = jnp.transpose(grad[...].astype(F32) * attended[...].astype(F32))
    centre = jnp.concatenate(
        [
            jnp.sum(product[head * HEAD_DIM : (head + 1) * HEAD_DIM, :], axis=0, keepdims=True)
            for head in range(heads)
        ],
        axis=1,
    )
    first_key = jnp.concatenate([bounds[0:1, :]] * heads, axis=1)
    last_key = jnp.concatenate([bounds[1:2, :]] * heads, axis=1)
    log_total = jnp.concatenate([logs[head : head + 1, :] for head in range(heads)], axis=1)
    grad_query[...] = jnp.zeros_like(grad_query)

    def one(tile, _):
        start = tile * tile_k
        key_rows = pl.ds(pl.multiple_of(start, tile_k), tile_k)
        raw[...] = dot_turned(held[key_rows, width : 2 * width], queries)
        raw_grad[...] = dot_turned(held[key_rows, 2 * width :], incoming)
        last = jnp.minimum(last_key, ends[tile] - 1) - start
        first = first_key - start
        for begin in range(0, tile_k, STRIP):
            at = slice(begin, begin + STRIP)
            row = lax.broadcasted_iota(jnp.int32, (STRIP, raw.shape[1]), 0) + begin
            allowed = (row <= last) & (row >= first)
            chance = jnp.exp(jnp.where(allowed, raw[at, :] - log_total, NEGATIVE))
            chances[at, :] = chance.astype(BF16)
            steps[at, :] = (chance * (raw_grad[at, :] - centre)).astype(BF16)
        grad_values[key_rows, :] += dot(chances[...], incoming)
        grad_keys[key_rows, :] += dot(steps[...], queries)
        grad_query[...] += dot(turned[tile], steps[...])
        return 0

    upper = (index * tile_q + tile_q - 1) // tile_k + 1
    lax.fori_loop(lows[index], upper, one, 0)
    merged[query_rows, :width] = (
        fold_heads(grad_query[...], heads, tile_q) * HEAD_DIM**-0.5
    ).astype(BF16)

    @pl.when(index == pl.num_programs(0) - 1)
    def _():
        merged[:, width : 2 * width] = grad_keys[...].astype(BF16)
        merged[:, 2 * width :] = grad_values[...].astype(BF16)
        outs = [here, near] + [far.at[way] for way in range(nctx - 2)]
        for way, out in enumerate(outs):
            first = jnp.bitwise_xor(place[0], way) * block_rows
            out[...] = merged[pl.ds(pl.multiple_of(first, block_rows), block_rows), :]


def attend_back(pieces, place, lows, ends, bounds, logs, grad, attended, nctx, block_rows, *needed):
    total_rows, width = grad.shape
    heads = width // HEAD_DIM
    by_tile = pl.BlockSpec((TILE_Q, width), lambda i, *_: (i, 0))
    sent = (block_rows, 3 * width)
    sent = [sent, sent, (nctx - 2, *sent)]
    grid_spec = pltpu.PrefetchScalarGridSpec(
        num_scalar_prefetch=3,
        grid=(total_rows // TILE_Q,),
        in_specs=[
            pl.BlockSpec((2, TILE_Q), lambda i, *_: (0, i)),
            pl.BlockSpec((heads, TILE_Q), lambda i, *_: (0, i)),
        ]
        + [whole(piece.shape) for piece in pieces]
        + [by_tile] * 2
        + anywhere(len(needed)),
        out_specs=[whole(shape) for shape in sent],
        scratch_shapes=[
            pltpu.VMEM((total_rows, 3 * width), BF16),
            pltpu.VMEM((total_rows // TILE_K, width, TILE_K), BF16),
            pltpu.VMEM((total_rows, width), F32),
            pltpu.VMEM((total_rows, width), F32),
            pltpu.VMEM((width, heads * TILE_Q), F32),
            pltpu.VMEM((TILE_K, heads * TILE_Q), F32),
            pltpu.VMEM((TILE_K, heads * TILE_Q), F32),
            pltpu.VMEM((TILE_K, heads * TILE_Q), BF16),
            pltpu.VMEM((TILE_K, heads * TILE_Q), BF16),
            pltpu.VMEM((total_rows, 3 * width), BF16),
        ],
    )
    return pl.pallas_call(
        functools.partial(
            attend_back_kernel, nctx, heads, len(pieces), len(needed), block_rows
        ),
        grid_spec=grid_spec,
        out_shape=[jax.ShapeDtypeStruct(shape, BF16) for shape in sent],
        compiler_params=params(),
        cost_estimate=takes(250),
        name="attend_back",
    )(place, lows, ends, bounds, logs, *pieces, grad, attended, *needed)


def mix_kernel(nctx, count, place, heads_in, weight, source, gain, bias, *refs):
    returned, mixed, *lows = refs[count:]
    rows, depth = mixed.shape
    step = pl.program_id(0)
    left = jnp.concatenate([heads_in[c, 0] for c in range(nctx)], axis=1)
    returned[...] = left

    @pl.when(step == 0)
    def _():
        mixed[...] = source[...].astype(F32)

    mixed[...] += dot_turned(left, weight[0])

    @pl.when(step == pl.num_programs(0) - 1)
    def _():
        values = mixed[...]
        values = values - jnp.mean(values, axis=1, keepdims=True)
        scaling = lax.rsqrt(jnp.mean(values * values, axis=1, keepdims=True) + EPSILON)
        values = (values * scaling * gain[...] + bias[...]).astype(BF16)
        part_rows = lows[0].shape[0]
        for part, low in enumerate(lows):
            low[...] = values[part * part_rows : (part + 1) * part_rows]


def mix(heads_in, weight, full, gain, bias, place, parts, *needed):
    nctx, tp, rows, piece = heads_in.shape
    depth = full.shape[1]
    head_width = nctx * piece
    grid_spec = pltpu.PrefetchScalarGridSpec(
        num_scalar_prefetch=1,
        grid=(tp,),
        in_specs=[
            pl.BlockSpec((nctx, 1, rows, piece), lambda k, s: (0, k, 0, 0)),
            pl.BlockSpec((1, depth, head_width), lambda k, s: (k, 0, 0)),
            pl.BlockSpec((rows, depth), lambda k, s: (s[0], 0)),
            whole((1, depth)),
            whole((1, depth)),
        ]
        + anywhere(len(needed)),
        out_specs=[
            pl.BlockSpec((rows, head_width), lambda k, s: (0, k)),
            whole((rows, depth)),
        ]
        + [whole((rows // parts, depth))] * parts,
    )
    return pl.pallas_call(
        functools.partial(mix_kernel, nctx, len(needed)),
        grid_spec=grid_spec,
        out_shape=[
            jax.ShapeDtypeStruct((rows, tp * head_width), BF16),
            jax.ShapeDtypeStruct((rows, depth), F32),
        ]
        + [jax.ShapeDtypeStruct((rows // parts, depth), BF16)] * parts,
        compiler_params=params(),
        cost_estimate=takes(50),
        name="mix",
    )(place, heads_in, weight, full, gain, bias, *needed)


def feed_kernel(cuts, parts, tp, first_one, place, low, cot, mixed, source, *refs):
    refs = refs[-(5 + parts + 4) :]
    kept, grad_gate, grad_up, hidden, out = refs[:5]
    partials, held, sems = refs[5 : 5 + parts], refs[-4:-1], refs[-1]
    unit = source.shape[1] // 3
    width = out.shape[2]

    def copies(index):
        first, size = cuts[index]
        at = pl.ds(first, size)
        return [
            pltpu.make_async_copy(
                source.at[:, pl.ds(which * unit, unit), at],
                held[which].at[:, :, at],
                sems.at[index * 3 + which],
            )
            for which in range(3)
        ]

    for index in range(len(cuts)):
        for copy in copies(index):
            copy.start()
    kept[...] = low[...]
    rows, depth = kept.shape[0] // parts, kept.shape[1]
    grads = jnp.concatenate([cot[block] for block in range(tp)], axis=1)
    for index, (first, size) in enumerate(cuts):
        for copy in copies(index):
            copy.wait()
        at = slice(first, first + size)
        gate_weight, up_weight, down_weight = [w[:, :, at].reshape(depth, size) for w in held]
        gate = dot(kept[...], gate_weight)
        up = dot(kept[...], up_weight)
        sigma = 1.0 / (1.0 + jnp.exp(-gate))
        active = gate * sigma
        hidden[:, at] = (active * up).astype(BF16)
        grad = dot(grads, down_weight)
        grad_gate[:, at] = (grad * up * sigma * (1.0 + gate * (1.0 - sigma))).astype(BF16)
        grad_up[:, at] = (grad * active).astype(BF16)
    gate_weight, up_weight, down_weight = [w[...].reshape(depth, w.shape[2]) for w in held]
    product = dot_turned(grad_gate[...], gate_weight) + dot_turned(grad_up[...], up_weight)
    for part in range(parts):
        partials[part][...] = product[part * rows : (part + 1) * rows].astype(BF16)
    values = dot_turned(hidden[...], down_weight)
    if first_one:
        values = values + mixed[...]
    for block in range(tp):
        out[block] = values[:, block * width : (block + 1) * width].astype(BF16)


def feed(low, cot, mixed, weights, step, tp, place, held, parts, *needed):
    rows, depth = low.shape
    part_rows = rows // parts
    blocks, triple, hidden = weights.shape
    cuts = []
    while sum(size for _, size in cuts) < hidden:
        first = sum(size for _, size in cuts)
        cuts.append((first, min(512, hidden - first)))
    by_owner = lambda columns: pl.BlockSpec(
        (rows, columns), lambda i, s: (lax.rem(s[0] - step + tp, tp), 0)
    )
    width = depth // tp
    blocks_of_owner = pl.BlockSpec(
        (tp, rows, width), lambda i, s: (0, lax.rem(s[0] - step + tp, tp), 0)
    )
    grid_spec = pltpu.PrefetchScalarGridSpec(
        num_scalar_prefetch=1,
        grid=(1,),
        in_specs=[whole((rows, depth)), blocks_of_owner, whole(mixed.shape)]
        + anywhere(1 + len(held) + len(needed)),
        out_specs=[by_owner(depth)]
        + [by_owner(hidden)] * 3
        + [blocks_of_owner]
        + [whole((part_rows, depth))] * parts,
        scratch_shapes=[pltpu.VMEM((blocks, triple // 3, hidden), BF16)] * 3
        + [pltpu.SemaphoreType.DMA((3 * len(cuts),))],
    )
    return pl.pallas_call(
        functools.partial(feed_kernel, tuple(cuts), parts, tp, step == 0),
        grid_spec=grid_spec,
        out_shape=[
            jax.ShapeDtypeStruct((tp * rows, columns), BF16)
            for columns in (depth, hidden, hidden, hidden)
        ]
        + [jax.ShapeDtypeStruct((tp, tp * rows, width), BF16)]
        + [jax.ShapeDtypeStruct((part_rows, depth), BF16)] * parts,
        input_output_aliases={5 + index: index for index in range(len(held))},
        compiler_params=params(),
        cost_estimate=takes(100),
        name="feed",
    )(place, low, cot, mixed, weights, *held, *needed)


def blame_halves(lefts, rights, place, unit, *needed, split=False):
    rows = lefts[0].shape[0]
    other = rights[0].shape[1]
    picked = lefts[1].shape[1] // unit
    chosen = pl.BlockSpec((rows, unit), lambda j, s: (0, 2 * (j ^ s[3]) + s[1] % 2))
    cut = pl.BlockSpec((rows, unit), lambda j, s: (0, j ^ s[3]))
    if split:
        shapes = [(2, unit // 2, other)] * 4
        targets = [whole(shape) for shape in shapes]
    else:
        shapes = [(picked * unit, other)]
        targets = [pl.BlockSpec((unit, other), lambda j, s: (j, 0))]

    def kernel(place, left_here, left_there, right_here, right_there, *refs):
        outs = refs[len(needed) :]
        product = 0.0
        for left, right in ((left_here, right_here), (left_there, right_there)):
            product = product + lax.dot_general(
                left[...], right[...], (((0,), (0,)), ((), ())), preferred_element_type=F32
            )
        product = product.astype(BF16)
        if not split:
            outs[0][...] = product
        for j in range(picked if split else 0):

            @pl.when(pl.program_id(0) == j)
            def _():
                outs[j // 2][j % 2] = product[: unit // 2]
                outs[2 + j % 2][j // 2] = product[unit // 2 :]

    grid_spec = pltpu.PrefetchScalarGridSpec(
        num_scalar_prefetch=1,
        grid=(picked,),
        in_specs=[chosen, cut] + [whole((rows, other))] * 2 + anywhere(len(needed)),
        out_specs=targets,
    )
    place = jnp.concatenate([place, place[2:3] * 2 + place[1:2] // 2 if split else 0 * place[:1]])
    outs = pl.pallas_call(
        kernel,
        grid_spec=grid_spec,
        out_shape=[jax.ShapeDtypeStruct(shape, BF16) for shape in shapes],
        compiler_params=params(),
        cost_estimate=takes(60),
        name="blame_halves",
    )(place, *lefts, *rights, *needed)
    return outs if split else outs[0]


def blame(left, right, *needed):
    rows, columns = left.shape
    if right.ndim == 3:
        steps, other = right.shape[0], right.shape[2]
        in_specs = [whole((rows, columns)), pl.BlockSpec((1, rows, other), lambda j: (j, 0, 0))]
        target, shape = pl.BlockSpec((columns, other), lambda j: (0, j)), (columns, steps * other)
    else:
        steps, other = 4, right.shape[1]
        in_specs = [pl.BlockSpec((rows, columns // steps), lambda j: (0, j)), whole((rows, other))]
        target, shape = pl.BlockSpec((columns // steps, other), lambda j: (j, 0)), (columns, other)

    def kernel(left, right, *refs):
        theirs = right[0] if len(right.shape) == 3 else right[...]
        refs[-1][...] = lax.dot_general(
            left[...], theirs, (((0,), (0,)), ((), ())), preferred_element_type=F32
        ).astype(BF16)

    return pl.pallas_call(
        kernel,
        grid=(steps,),
        in_specs=in_specs + anywhere(len(needed)),
        out_specs=target,
        out_shape=jax.ShapeDtypeStruct(shape, BF16),
        compiler_params=params(),
        cost_estimate=takes(60),
        name="blame",
    )(left, right, *needed)


def turn_kernel(nctx, count, parts, unit, place, *refs):
    arrived, own = refs[:parts], refs[parts : 2 * parts]
    mixed, cot, gain = refs[2 * parts : 2 * parts + 3]
    weight, refs = refs[2 * parts + 3], refs[2 * parts + 4 + count :]
    out, grad_mixed, grad_low, gain_grad, shift_grad, half = refs
    rows, depth = mixed.shape
    piece = out.shape[3]

    @pl.when(pl.program_id(0) == 0)
    def _():
        incoming = jnp.concatenate(
            [there[...].astype(F32) + here[...].astype(F32) for there, here in zip(arrived, own)]
        )
        values = mixed[...]
        values = values - jnp.mean(values, axis=1, keepdims=True)
        scaling = lax.rsqrt(jnp.mean(values * values, axis=1, keepdims=True) + EPSILON)
        normed = values * scaling
        shift_grad[...] = jnp.sum(incoming, axis=0, keepdims=True)
        gain_grad[...] = jnp.sum(incoming * normed, axis=0, keepdims=True)
        scaled = incoming * gain[...]
        grads = jnp.concatenate([cot[block] for block in range(cot.shape[0])], axis=1)
        total = grads.astype(F32) + scaling * (
            scaled
            - jnp.mean(scaled, axis=1, keepdims=True)
            - normed * jnp.mean(scaled * normed, axis=1, keepdims=True)
        )
        grad_mixed[...] = total
        grad_low[...] = total.astype(BF16)
        write_half(half, grad_low, 1 - lax.rem(place[1], 2), unit)

    product = dot(grad_low[...], weight[0])
    for c in range(nctx):
        out[c, 0] = product[:, c * piece : (c + 1) * piece].astype(BF16)


def turn(arrived, own, mixed, cot, gain, weight, place, nctx, tp, unit, *needed):
    rows, depth = mixed.shape
    parts = len(arrived)
    head_width = weight.shape[2]
    piece = head_width // nctx
    grid_spec = pltpu.PrefetchScalarGridSpec(
        num_scalar_prefetch=1,
        grid=(tp,),
        in_specs=[whole((rows // parts, depth))] * (2 * parts)
        + [whole((rows, depth))]
        + [
            pl.BlockSpec((tp, rows, depth // tp), lambda k, s: (0, s[0], 0)),
            whole((1, depth)),
            pl.BlockSpec((1, depth, head_width), lambda k, s: (k, 0, 0)),
        ]
        + anywhere(len(needed)),
        out_specs=[
            pl.BlockSpec((nctx, 1, rows, piece), lambda k, s: (0, k, 0, 0)),
            whole((rows, depth)),
            whole((rows, depth)),
            whole((1, depth)),
            whole((1, depth)),
            whole((rows, depth // 2)),
        ],
    )
    return pl.pallas_call(
        functools.partial(turn_kernel, nctx, len(needed), parts, unit),
        grid_spec=grid_spec,
        out_shape=[
            jax.ShapeDtypeStruct((nctx, tp, rows, piece), BF16),
            jax.ShapeDtypeStruct((rows, depth), F32),
            jax.ShapeDtypeStruct((rows, depth), BF16),
            jax.ShapeDtypeStruct((1, depth), F32),
            jax.ShapeDtypeStruct((1, depth), F32),
            jax.ShapeDtypeStruct((rows, depth // 2), BF16),
        ],
        compiler_params=params(),
        cost_estimate=takes(60),
        name="turn",
    )(place, *arrived, *own, mixed, cot, gain, weight, *needed)


def finish_kernel(nctx, tp, extra_count, place, *refs):
    pieces = refs[:nctx]
    cosine, sine_up, sine_down, full, extra, gain = refs[nctx : nctx + 6]
    weight, refs = refs[nctx + 6], refs[nctx + 7 + extra_count :]
    outs = refs[:tp]
    low, bias_grad, gain_grad, shift_grad, spare = refs[tp:]
    rows, wide = pieces[0].shape
    piece = wide // 3
    width = outs[0].shape[1]
    strip = spare.shape[0]
    extra_rows = extra.shape[0]

    @pl.when(pl.program_id(0) == 0)
    def _():
        bias_grad[...] = jnp.zeros_like(bias_grad)
        gain_grad[...] = jnp.zeros_like(gain_grad)
        shift_grad[...] = jnp.zeros_like(shift_grad)

    for step in range(nctx):
        source = jnp.bitwise_xor(place[1], step)
        for part in range(3):
            values = pieces[step][:, part * piece : (part + 1) * piece].astype(F32)
            if part < 2:
                values = (
                    values * cosine[...]
                    - pltpu.roll(values, piece - ROT // 2, 1) * sine_up[...]
                    - pltpu.roll(values, ROT // 2, 1) * sine_down[...]
                )
            columns = pl.ds(pl.multiple_of(source * wide + part * piece, piece), piece)
            bias_grad[:, columns] += jnp.sum(values, axis=0, keepdims=True)
            low[:, columns] = values.astype(BF16)

    incoming = dot_turned(low[...], weight[...])
    source = full[...].astype(F32)
    source = source - jnp.mean(source, axis=1, keepdims=True)
    scaling = lax.rsqrt(jnp.mean(source * source, axis=1, keepdims=True) + EPSILON)
    normed = source * scaling
    shift_grad[...] += jnp.sum(incoming, axis=0, keepdims=True)
    gain_grad[...] += jnp.sum(incoming * normed, axis=0, keepdims=True)
    scaled = incoming * gain[...]
    spare[...] = scaling * (
        scaled
        - jnp.mean(scaled, axis=1, keepdims=True)
        - normed * jnp.mean(scaled * normed, axis=1, keepdims=True)
    )
    first = pl.program_id(0) * strip
    wanted = place[0] * extra_rows

    if strip <= extra_rows:

        @pl.when((first >= wanted) & (first < wanted + extra_rows))
        def _():
            spare[...] += extra[pl.ds(pl.multiple_of(first - wanted, strip), strip), :]

    else:

        @pl.when((wanted >= first) & (wanted < first + strip))
        def _():
            spare[pl.ds(pl.multiple_of(wanted - first, extra_rows), extra_rows), :] += extra[...]

    for step, out in enumerate(outs):
        owner = lax.rem(place[0] - step + tp, tp)
        out[...] = spare[:, pl.ds(pl.multiple_of(owner * width, width), width)].astype(BF16)


def finish(pieces, place, tables, full, extra, gain, weight, tp, *needed):
    rows, wide = pieces[0].shape
    depth = full.shape[1]
    total = weight.shape[1]
    strip = 256
    steps = rows // strip
    width = depth // tp
    nctx = len(pieces)
    by_rows = lambda columns: pl.BlockSpec((strip, columns), lambda i, s: (i, 0))
    grid_spec = pltpu.PrefetchScalarGridSpec(
        num_scalar_prefetch=1,
        grid=(steps,),
        in_specs=[by_rows(wide)] * nctx
        + [by_rows(2 * HEAD_DIM)] * 3
        + [
            by_rows(depth),
            whole(extra.shape),
            whole((1, depth)),
        ]
        + [whole(weight.shape)]
        + anywhere(len(needed)),
        out_specs=[by_rows(width)] * tp
        + [
            by_rows(total),
            whole((1, total)),
            whole((1, depth)),
            whole((1, depth)),
        ],
        scratch_shapes=[pltpu.VMEM((strip, depth), F32)],
    )
    return pl.pallas_call(
        functools.partial(finish_kernel, nctx, tp, len(needed)),
        grid_spec=grid_spec,
        out_shape=[jax.ShapeDtypeStruct((rows, width), BF16)] * tp
        + [
            jax.ShapeDtypeStruct((rows, total), BF16),
            jax.ShapeDtypeStruct((1, total), F32),
            jax.ShapeDtypeStruct((1, depth), F32),
            jax.ShapeDtypeStruct((1, depth), F32),
        ],
        compiler_params=params(),
        cost_estimate=takes(70),
        name="finish",
    )(place, *pieces, *tables, full, extra, gain, weight, *needed)


def join(rings, place):
    parts, tp = len(rings), len(rings[0])
    rows, width = rings[0][0].shape

    def kernel(place, *refs):
        for part in range(parts):
            for step in range(tp):
                owner = lax.rem(place[0] - step + tp, tp)
                refs[-1][owner, part * rows : (part + 1) * rows, :] = refs[part * tp + step][...]

    grid_spec = pltpu.PrefetchScalarGridSpec(
        num_scalar_prefetch=1,
        grid=(1,),
        in_specs=[whole((rows, width))] * (parts * tp),
        out_specs=whole((tp, parts * rows, width)),
    )
    return pl.pallas_call(
        kernel,
        grid_spec=grid_spec,
        out_shape=jax.ShapeDtypeStruct((tp, parts * rows, width), BF16),
        compiler_params=params(),
        cost_estimate=takes(10),
        name="join",
    )(place, *[block for blocks in rings for block in blocks])


def pack_kernel(gate, up, down, out):
    rows = gate.shape[0]
    out[:rows] = gate[...]
    out[rows : 2 * rows] = up[...]
    out[2 * rows :] = jnp.transpose(down[...])


def pack(gate, up, down):
    rows, columns = gate.shape
    return pl.pallas_call(
        pack_kernel,
        out_shape=jax.ShapeDtypeStruct((3 * rows, columns), BF16),
        compiler_params=params(),
        cost_estimate=takes(10),
        name="pack",
    )(gate, up, down)


def contract_rows(left, right):
    return lax.dot_general(left, right, (((0,), (0,)), ((), ())), preferred_element_type=F32)


def pick(stack, index):
    return lax.dynamic_index_in_dim(stack, index, 0, keepdims=False)


def shards(
    nfsdp,
    nctx,
    tp,
    inputs,
    cotangent,
    first_gain,
    first_bias,
    qkv_weight,
    qkv_bias,
    out_weight,
    second_gain,
    second_bias,
    gate_weight,
    up_weight,
    down_weight,
    lengths,
    fill_counts,
):
    data = ("fsdp", "ctx")
    ndata = nfsdp * nctx
    block_rows, width = inputs.shape
    depth = tp * width
    half_depth = depth // 2
    unit = depth // ndata
    tensor_index = lax.axis_index("tp").astype(jnp.int32)
    context_index = lax.axis_index("ctx").astype(jnp.int32)
    fsdp_index = lax.axis_index("fsdp").astype(jnp.int32)
    part_rows = block_rows // tp
    chunk_rows = block_rows // CHUNKS
    head_width = qkv_weight.shape[2]
    piece = head_width // nctx
    wide = 3 * piece

    square = nfsdp == 2 and nctx == 4 and unit % 128 == 0
    place = jnp.stack([tensor_index, context_index, fsdp_index])

    def shift(value, step):
        return lax.ppermute(value, "tp", [(i, (i + step) % tp) for i in range(tp)])

    def swap(value, step):
        return lax.ppermute(value, "ctx", [(i, i ^ step) for i in range(nctx)])

    core_index = context_index % 2
    groups = [list(range(0, ndata, 2)), list(range(1, ndata, 2))]
    def mate(value):
        return swap(value, 1)

    def send(here, near, far, *needed):
        far = swap(far, 2)
        return [here, swap(near, 1), far[0], swap(tie(far[1], *needed), 1)]

    def scatter_half(value, axis):
        return lax.psum_scatter(
            value, data, scatter_dimension=axis, tiled=True, axis_index_groups=groups
        )

    def scatter(value, axis):
        return lax.psum_scatter(value, data, scatter_dimension=axis, tiled=True)

    def cross(value):
        return lax.ppermute(value, "fsdp", [(i, i ^ 1) for i in range(nfsdp)])

    def square_sum(parts):
        near, far, low, high = parts
        first = total(near, cross(far))
        second = total(low, swap(high, 2))
        first = first[0].astype(F32) + swap(first[1], 2).astype(F32)
        second = second[0].astype(F32) + cross(second[1]).astype(F32)
        return jnp.concatenate([first, second], axis=0)

    def total(left, right):
        return (left.astype(F32) + right.astype(F32)).astype(BF16)

    owners = [(tensor_index - step + tp) % tp for step in range(tp)]

    own_qkv = (
        qkv_weight.reshape(-1, 3, nctx, piece).transpose(0, 2, 1, 3).reshape(-1, 3 * head_width)
    )
    full_qkv = lax.all_gather(own_qkv, data, axis=0, tiled=True)
    own_feed = pack(gate_weight, up_weight, down_weight)
    feed_weights = lax.all_gather(own_feed, data, axis=0, tiled=True).reshape(ndata, 3 * unit, -1)

    validity, position, first_key, last_key = layout(lengths[0], fill_counts[0], block_rows)
    own_position = lax.dynamic_slice_in_dim(position, context_index * block_rows, block_rows, 0)
    tables = rotary_tables(own_position)
    bounds = jnp.stack([first_key, last_key])
    tile_first = first_key[::TILE_Q]
    tile_count = tile_first.shape[0]
    lows = jnp.where(validity[::TILE_Q], tile_first // TILE_K, tile_count * TILE_Q).astype(jnp.int32)
    key_block = jnp.arange(0, nctx * block_rows, TILE_K, dtype=jnp.int32) // block_rows
    ends = (
        key_block * block_rows
        + jnp.sum(
            jnp.where(
                key_block[:, None] == jnp.arange(nctx, dtype=jnp.int32)[None, :],
                fill_counts[0][None, :],
                0,
            ),
            axis=1,
        )
    ).astype(jnp.int32)

    flat_bias = qkv_bias.reshape(3, nctx, piece).transpose(1, 0, 2).reshape(1, -1)
    gain_one, bias_one = first_gain[None], first_bias[None]
    gain_two, bias_two = second_gain[None], second_bias[None]

    rings = [[inputs[c * chunk_rows : (c + 1) * chunk_rows]] for c in range(CHUNKS)]
    share = unit // CHUNKS
    for chunk in range(CHUNKS):
        carried = out_weight.T[chunk * share : (chunk + 1) * share]
        rings[chunk][0] = jnp.concatenate([rings[chunk][0], carried], axis=0)
    for chunk in range(CHUNKS):
        for _ in range(tp - 1):
            rings[chunk].append(shift(rings[chunk][-1], 1))
            if len(rings[chunk]) == 2:
                rings[chunk][-1] = tie(rings[chunk][-1], own_feed)
    all_low, full, low_half, *outgoing, stack = project(
        rings, place, gain_one, bias_one, full_qkv, flat_bias, tables, nctx, unit
    )
    full_out = lax.all_gather(stack, data, axis=1, tiled=True)

    cot = tie(cotangent, *[blocks[-1] for blocks in rings])
    cot_rings = [[cot[c * chunk_rows : (c + 1) * chunk_rows]] for c in range(CHUNKS)]
    for blocks in cot_rings:
        for _ in range(tp - 1):
            blocks.append(shift(blocks[-1], 1))
    pieces = send(*outgoing, *[blocks[max(tp - 2, 0)] for blocks in cot_rings])

    attended, outgoing, logs = attend(
        pieces,
        place[1:2],
        lows,
        ends,
        bounds,
        nctx,
        block_rows,
        feed_weights,
    )
    cot = join(cot_rings, place)
    arrived = lax.all_to_all(
        tie(outgoing, *[blocks[-1] for blocks in cot_rings]).reshape(nctx * tp, part_rows, piece),
        ("ctx", "tp"),
        split_axis=0,
        concat_axis=0,
        tiled=True,
    )
    returned, mixed, second_low = mix(
        arrived.reshape(nctx, tp, part_rows, piece),
        full_out,
        full,
        gain_two,
        bias_two,
        place,
        1,
    )

    arrived, held, partials, travelling = second_low, [], [], None
    for step in range(tp):
        coming = shift(arrived, 1) if step < tp - 1 else None
        needed = travelling if step == tp - 1 and step > 2 else []
        *held, first, second = feed(
            arrived, cot, mixed, feed_weights, step, tp, place, held, HALVES, *needed
        )
        partials.append([first, second])
        if step == 1 % tp:
            travelling = partials[step]
        elif step > 1:
            travelling = [
                total(shift(value, 1), kept) for value, kept in zip(travelling, partials[step])
            ]
        if step == 0 and coming is not None:
            coming = tie(coming, partials[0][0])
        arrived = coming
    all_second, all_gate, all_up, hidden, feedforward = held

    last = [shift(value, 1) for value in travelling]
    half_gate = blame(all_second, all_gate, *travelling)
    half_up = blame(all_second, all_up, *travelling)
    half_down = blame(hidden, cot, *travelling)
    grad_heads, grad_mixed, mixed_low, gain_grad_two, shift_grad_two, mixed_half = turn(
        last,
        partials[0],
        mixed,
        cot,
        gain_two,
        full_out,
        place,
        nctx,
        tp,
        unit,
        half_gate,
        half_up,
        half_down,
    )
    grad_heads = lax.all_to_all(
        grad_heads.reshape(nctx * tp, part_rows, piece),
        ("ctx", "tp"),
        split_axis=0,
        concat_axis=0,
        tiled=True,
    ).reshape(nctx * block_rows, piece)

    total_gate = scatter(tie(half_gate, mixed_low), 0).astype(F32)
    total_up = scatter(tie(half_up, mixed_low), 0).astype(F32)
    total_down = scatter(tie(half_down, mixed_low), 1).astype(F32)

    if square:
        out_parts = blame_halves(
            (mixed_low, mate(mixed_half)), (returned, mate(returned)), place, unit, split=True
        )
        half_out = out_parts[0]
        total_out = square_sum(out_parts)
    else:
        half_out = blame(mixed_low, returned)
        total_out = scatter(half_out, 0).astype(F32)

    feedforward = tie(feedforward, grad_heads)
    layer_out = [pick(feedforward, owners[1 % tp])]
    for step in range(1, tp):
        kept = pick(feedforward, owners[(step + 1) % tp])
        layer_out.append(total(shift(layer_out[-1], 1), kept))

    grad_pieces = attend_back(
        pieces, place[1:2], lows, ends, bounds, logs, grad_heads, attended, nctx, block_rows, half_out
    )
    total_out = total_out.astype(BF16)
    arrived = send(*grad_pieces, *layer_out[max(tp - 2, 0) : tp - 1], total_out)
    out_after, layer_out = layer_out[max(tp - 2, 0)], layer_out[-1]
    out_blocks = jnp.swapaxes(tie(total_out, out_after).reshape(-1, tp, head_width), 0, 1)
    total_out = pick(out_blocks, tensor_index).astype(F32)
    for step in range(1, tp):
        moved = shift(pick(out_blocks, (tensor_index + step) % tp), step)
        total_out = total_out + moved.astype(F32)
    total_out = total_out.T

    low_halves = mate(low_half) if square else low_half
    needed = [layer_out, low_halves, total_out]
    *partial, all_grad, bias_grad, gain_grad, shift_grad = finish(
        arrived, place, tables, full, grad_mixed, gain_one, full_qkv, tp, *needed
    )
    parts = []
    if square:
        parts = blame_halves((all_low, low_halves), (all_grad, mate(all_grad)), place, unit, split=True)
    def exchange(value, axis, size):
        step = 1
        while step < size:
            value = value + lax.ppermute(value, axis, [(i, i ^ step) for i in range(size)])
            step *= 2
        return value

    small = jnp.concatenate([gain_grad, shift_grad, gain_grad_two, shift_grad_two], axis=1)
    small = sum([shift(small, step) for step in range(1, tp)], small)
    travelling = tie(partial[1 % tp], small)
    small = jnp.concatenate([bias_grad, small], axis=1)
    small = exchange(exchange(small, "ctx", nctx), "fsdp", nfsdp)
    needed = {1: [small, *parts[:1]], tp - 1: [total_gate, total_up, total_down]}
    for step in range(1, tp):
        travelling = add(
            shift(travelling, 1), partial[(step + 1) % tp], *needed.get(step, [])
        )
    grad_inputs = travelling
    if square:
        total_qkv = square_sum(parts)
    else:
        total_qkv = scatter(blame(all_low, all_grad), 0).astype(F32)

    total_qkv = (
        total_qkv
        .reshape(-1, nctx, 3, piece)
        .transpose(0, 2, 1, 3)
        .reshape(-1, 3, head_width)
    )


    bias_total, small = small[:, : 3 * head_width], small[:, 3 * head_width :]
    bias_total = bias_total.reshape(nctx, 3, piece).transpose(1, 0, 2).reshape(3, head_width)
    small = small.reshape(4, depth)
    return (
        layer_out,
        grad_inputs,
        small[0],
        small[1],
        total_qkv,
        bias_total,
        total_out,
        small[2],
        small[3],
        total_gate,
        total_up,
        total_down,
    )


def solution(mesh):
    data = ("fsdp", "ctx")
    by_rows = P(data, "tp")
    by_columns = P("tp", data)
    qkv = P(data, None, "tp")
    return jax.shard_map(
        functools.partial(shards, mesh.shape["fsdp"], mesh.shape["ctx"], mesh.shape["tp"]),
        mesh=mesh,
        in_specs=(
            by_rows,
            by_rows,
            P(),
            P(),
            qkv,
            P(None, "tp"),
            by_columns,
            P(),
            P(),
            by_rows,
            by_rows,
            by_columns,
            P("fsdp", None),
            P("fsdp", None),
        ),
        out_specs=(
            by_rows,
            by_rows,
            P(),
            P(),
            qkv,
            P(None, "tp"),
            by_columns,
            P(),
            P(),
            by_rows,
            by_rows,
            by_columns,
        ),
        check_vma=False,
    )
```

```python
import functools

import jax
import jax.numpy as jnp
from jax import lax
from jax.experimental import pallas as pl
from jax.experimental.pallas import tpu as pltpu
from jax.sharding import PartitionSpec as P

HEAD_DIM = 64
ROT = 16
EPSILON = 1e-05
NEGATIVE = -1e30
FLOOR = -1e20
VMEM_LIMIT = 56 * 1024 * 1024
TILE_Q = 512
TILE_K = 512
STRIP = 32
CHUNKS = 2
HALVES = 2

F32 = jnp.float32
BF16 = jnp.bfloat16


def layout(lengths, fill_counts, block_rows):
    blocks_count = fill_counts.shape[0]
    seq_count = lengths.shape[0]
    slot_index = jnp.arange(blocks_count * block_rows, dtype=jnp.int32)
    block_of = slot_index // block_rows
    within = slot_index - block_of * block_rows
    chooser = block_of[:, None] == jnp.arange(blocks_count, dtype=jnp.int32)[None, :]
    fill_here = jnp.sum(jnp.where(chooser, fill_counts[None, :], 0), axis=1)
    before = jnp.cumsum(fill_counts) - fill_counts
    before_here = jnp.sum(jnp.where(chooser, before[None, :], 0), axis=1)
    validity = within < fill_here
    used_index = before_here + within
    seq_ends = jnp.cumsum(lengths)
    sequence = jnp.sum((used_index[:, None] >= seq_ends[None, :]).astype(jnp.int32), axis=1)
    seq_starts = seq_ends - lengths
    picker = sequence[:, None] == jnp.arange(seq_count, dtype=jnp.int32)[None, :]
    start_here = jnp.sum(jnp.where(picker, seq_starts[None, :], 0), axis=1)
    after = before + fill_counts
    start_block = jnp.sum((seq_starts[:, None] >= after[None, :]).astype(jnp.int32), axis=1)
    start_block = jnp.minimum(start_block, blocks_count - 1)
    block_pick = start_block[:, None] == jnp.arange(blocks_count, dtype=jnp.int32)[None, :]
    start_before = jnp.sum(jnp.where(block_pick, before[None, :], 0), axis=1)
    start_slot = start_block * block_rows + seq_starts - start_before
    slot_here = jnp.sum(jnp.where(picker, start_slot[None, :], 0), axis=1)
    first_key = jnp.where(validity, slot_here, 0).astype(jnp.int32)
    last_key = jnp.where(validity, slot_index, -1).astype(jnp.int32)
    return (validity, used_index - start_here, first_key, last_key)


def rotary_tables(position):
    half = ROT // 2
    lane = jnp.arange(2 * HEAD_DIM, dtype=jnp.int32) % HEAD_DIM
    frequency = 10000.0 ** (-(2.0 * (lane % half).astype(F32)) / ROT)
    angles = position.astype(F32)[:, None] * frequency[None, :]
    cosine, sine = jnp.cos(angles), jnp.sin(angles)
    lane = lane[None, :]
    return (
        jnp.where(lane < ROT, cosine, 1.0),
        jnp.where(lane < half, -sine, 0.0),
        jnp.where((lane >= half) & (lane < ROT), sine, 0.0),
    )


def params(**extra):
    return pltpu.CompilerParams(vmem_limit_bytes=VMEM_LIMIT, **extra)


def takes(microseconds):
    return pl.CostEstimate(
        flops=int(microseconds * 1e8), bytes_accessed=0, transcendentals=0
    )


def whole(shape):
    return pl.BlockSpec(shape, lambda *_: (0,) * len(shape))


def anywhere(count):
    return [pl.BlockSpec(memory_space=pl.ANY)] * count


def write_half(out, values, half, unit):
    if unit % 128:
        out[...] = values[:, : out.shape[1]]
        return
    for block in range(out.shape[1] // unit):
        first = pl.multiple_of((2 * block + half) * unit, unit)
        out[:, block * unit : (block + 1) * unit] = values[:, pl.ds(first, unit)]


def dot(left, right):
    return jnp.dot(left, right, preferred_element_type=F32)


def dot_turned(left, right):
    return lax.dot_general(left, right, (((1,), (1,)), ((), ())), preferred_element_type=F32)


def tie(value, *needed):
    def kernel(*refs):
        del refs

    return pl.pallas_call(
        kernel,
        in_specs=anywhere(1 + len(needed)),
        out_specs=pl.BlockSpec(memory_space=pl.ANY),
        out_shape=jax.ShapeDtypeStruct(value.shape, value.dtype),
        input_output_aliases={0: 0},
        name="tie",
    )(value, *needed)


def add_kernel(left, right, *refs):
    refs[-1][...] = (left[...].astype(F32) + right[...].astype(F32)).astype(BF16)


def add(left, right, *needed):
    rows, columns = left.shape
    strip = min(rows, 512)
    block = pl.BlockSpec((strip, columns), lambda i: (i, 0))
    return pl.pallas_call(
        add_kernel,
        grid=(rows // strip,),
        in_specs=[block, block] + anywhere(len(needed)),
        out_specs=block,
        out_shape=jax.ShapeDtypeStruct(left.shape, BF16),
        compiler_params=params(),
        cost_estimate=takes(10),
        name="ring_add",
    )(left, right, *needed)


def project_kernel(tp, chunks, per, unit, place, *refs):
    rings, refs = refs[: tp * chunks], refs[tp * chunks :]
    gain, bias, weight, weight_bias, cosine, sine_up, sine_down = refs[:7]
    low, full, half, here, near, far, stack = refs[7:]
    outs = [here, near] + [far.at[way] for way in range(far.shape[0])]
    rows, width = low.shape[0] // chunks, rings[0].shape[1]
    depth = tp * width
    wide = here.shape[1]
    piece = wide // 3
    step = pl.program_id(0)

    @pl.when(pl.program_id(0) == 0)
    def _():
        strip = 128
        for start in range(0, rows * chunks, strip):
            chunk, first = start // rows, start % rows
            blocks = rings[chunk * tp : (chunk + 1) * tp]
            at = slice(start, start + strip)
            inner = slice(first, first + strip)
            parts = [block[inner, :].astype(F32) for block in blocks]
            centre = sum(jnp.sum(part, axis=1, keepdims=True) for part in parts) / depth
            parts = [part - centre for part in parts]
            spread = sum(jnp.sum(part * part, axis=1, keepdims=True) for part in parts) / depth
            scaling = lax.rsqrt(spread + EPSILON)
            for step in range(tp):
                owner = lax.rem(place[0] - step + tp, tp)
                columns = pl.ds(pl.multiple_of(owner * width, width), width)
                low[at, columns] = (
                    parts[step] * scaling * gain[:, columns] + bias[:, columns]
                ).astype(BF16)
                full[at, columns] = blocks[step][inner, :]
        write_half(half, low, 1 - lax.rem(place[1], 2), unit)
        share = rings[0].shape[0] - rows
        for chunk in range(chunks):
            for step in range(tp):
                owner = lax.rem(place[0] - step + tp, tp)
                stack[owner, chunk * share : (chunk + 1) * share, :] = rings[chunk * tp + step][
                    rows:, :
                ]

    product = dot(low[...], weight[...]) + weight_bias[...]
    groups = []
    for group in range(per):
        parts = []
        for part in range(3):
            first = (group * 3 + part) * piece
            values = product[:, first : first + piece]
            if part < 2:
                values = (
                    values * cosine[...]
                    + pltpu.roll(values, piece - ROT // 2, 1) * sine_up[...]
                    + pltpu.roll(values, ROT // 2, 1) * sine_down[...]
                )
            parts.append(values.astype(BF16))
        groups.append(parts)
    flip = lax.rem(place[1], per)
    for way, out in enumerate(outs):
        for group in range(per):

            @pl.when((step == way // per) & (jnp.bitwise_xor(group, flip) == way % per))
            def _():
                for part in range(3):
                    out[:, part * piece : (part + 1) * piece] = groups[group][part]


def project(rings, place, gain, bias, weight, weight_bias, tables, nctx, unit):
    chunks, tp = len(rings), len(rings[0])
    rows, width = tables[0].shape[0], rings[0][0].shape[1]
    depth = tp * width
    total = weight.shape[1]
    wide = total // nctx
    per = 2 if nctx % 2 == 0 else 1
    grid_spec = pltpu.PrefetchScalarGridSpec(
        num_scalar_prefetch=1,
        grid=(nctx // per,),
        in_specs=[whole(rings[0][0].shape)] * (tp * chunks)
        + [whole((1, depth))] * 2
        + [
            pl.BlockSpec((depth, per * wide), lambda i, s: (0, jnp.bitwise_xor(i, s[1] // per))),
            pl.BlockSpec((1, per * wide), lambda i, s: (0, jnp.bitwise_xor(i, s[1] // per))),
        ]
        + [whole((rows, 2 * HEAD_DIM))] * 3,
        out_specs=[whole((rows, depth))] * 2
        + [whole((rows, depth // 2))]
        + [whole((rows, wide))] * 2
        + [whole((nctx - 2, rows, wide)), whole((tp, unit, width))],
    )
    return pl.pallas_call(
        functools.partial(project_kernel, tp, chunks, per, unit),
        grid_spec=grid_spec,
        out_shape=[
            jax.ShapeDtypeStruct((rows, depth), BF16),
            jax.ShapeDtypeStruct((rows, depth), BF16),
            jax.ShapeDtypeStruct((rows, depth // 2), BF16),
        ]
        + [jax.ShapeDtypeStruct((rows, wide), BF16)] * 2
        + [
            jax.ShapeDtypeStruct((nctx - 2, rows, wide), BF16),
            jax.ShapeDtypeStruct((tp, unit, width), BF16),
        ],
        compiler_params=params(),
        cost_estimate=takes(60),
        name="project",
    )(
        place,
        *[block for blocks in rings for block in blocks],
        gain,
        bias,
        weight,
        weight_bias,
        *tables,
    )


def stack_heads(tile, heads):
    lane = lax.broadcasted_iota(jnp.int32, tile.shape, 1) // HEAD_DIM
    return jnp.concatenate(
        [jnp.where(lane == head, tile, jnp.zeros_like(tile)) for head in range(heads)], axis=0
    )


def fold_heads(stacked, heads, columns):
    row = lax.broadcasted_iota(jnp.int32, (stacked.shape[0], columns), 0) // HEAD_DIM
    folded = jnp.zeros((stacked.shape[0], columns), F32)
    for head in range(heads):
        folded = folded + jnp.where(row == head, stacked[:, head * columns : (head + 1) * columns], 0.0)
    return jnp.transpose(folded)


def load_pieces(place, pieces, nctx, held, block_rows):
    chunk_rows = pieces[0].shape[0]
    chunks = len(pieces) // nctx
    for chunk in range(chunks):
        for step in range(nctx):
            source = jnp.bitwise_xor(place, step)
            first = source * block_rows + chunk * chunk_rows
            held[pl.ds(pl.multiple_of(first, chunk_rows), chunk_rows), :] = pieces[
                chunk * nctx + step
            ][...]


def attend_kernel(nctx, heads, count, extra, block_rows, place, lows, ends, bounds, *refs):
    pieces = refs[:count]
    out, sent, logs, held, turned, total, high, sums, raw, chances = refs[count + extra :]
    tile_q, tile_k = out.shape[0], turned.shape[2]
    width = heads * HEAD_DIM
    index = pl.program_id(0)

    @pl.when(index == 0)
    def _():
        load_pieces(place[0], pieces, nctx, held, block_rows)
        for tile in range(turned.shape[0]):
            turned[tile] = jnp.transpose(held[tile * tile_k : (tile + 1) * tile_k, 2 * width :])

    query_rows = pl.ds(pl.multiple_of(index * tile_q, tile_q), tile_q)
    queries = stack_heads(held[query_rows, :width] * jnp.asarray(HEAD_DIM**-0.5, BF16), heads)
    first_key = jnp.concatenate([bounds[0:1, :]] * heads, axis=1)
    last_key = jnp.concatenate([bounds[1:2, :]] * heads, axis=1)
    total[...] = jnp.zeros_like(total)
    high[...] = jnp.full_like(high, FLOOR)
    sums[...] = jnp.zeros_like(sums)

    def one(tile, _):
        start = tile * tile_k
        keys = held[pl.ds(pl.multiple_of(start, tile_k), tile_k), width : 2 * width]
        raw[...] = dot_turned(keys, queries)
        last = jnp.minimum(last_key, ends[tile] - 1) - start
        first = first_key - start
        peaks = jnp.broadcast_to(high[...], (8, raw.shape[1]))
        for begin in range(0, tile_k, STRIP):
            scores = raw[begin : begin + STRIP, :]
            row = lax.broadcasted_iota(jnp.int32, scores.shape, 0) + begin
            scores = jnp.where((row <= last) & (row >= first), scores, NEGATIVE)
            raw[begin : begin + STRIP, :] = scores
            for group in range(0, STRIP, 8):
                peaks = jnp.maximum(peaks, scores[group : group + 8])
        highest = jnp.max(peaks, axis=0, keepdims=True)
        partial = jnp.zeros((8, raw.shape[1]), F32)
        for begin in range(0, tile_k, STRIP):
            raised = jnp.exp(raw[begin : begin + STRIP, :] - highest)
            chances[begin : begin + STRIP, :] = raised.astype(BF16)
            for group in range(0, STRIP, 8):
                partial = partial + raised[group : group + 8]
        shrink = jnp.exp(high[...] - highest)
        sums[...] = sums[...] * shrink + jnp.sum(partial, axis=0, keepdims=True)
        total[...] = total[...] * shrink + dot(turned[tile], chances[...])
        high[...] = highest
        return 0

    upper = (index * tile_q + tile_q - 1) // tile_k + 1
    lax.fori_loop(lows[index], upper, one, 0)
    found = sums[...] > 0.0
    safe = jnp.where(found, sums[...], 1.0)
    result = fold_heads(total[...] * jnp.where(found, 1.0 / safe, 0.0), heads, tile_q)
    out[...] = result.astype(BF16)
    sent[...] = result.astype(BF16)
    log_total = jnp.where(found, high[...] + jnp.log(safe), 0.0)
    for head in range(heads):
        logs[head : head + 1, :] = log_total[:, head * tile_q : (head + 1) * tile_q]


def attend(pieces, place, lows, ends, bounds, nctx, block_rows, *needed):
    total_rows = nctx * block_rows
    width = pieces[0].shape[1] // 3
    heads = width // HEAD_DIM
    steps = total_rows // TILE_Q
    grid_spec = pltpu.PrefetchScalarGridSpec(
        num_scalar_prefetch=3,
        grid=(steps,),
        in_specs=[pl.BlockSpec((2, TILE_Q), lambda i, *_: (0, i))]
        + [whole(piece.shape) for piece in pieces]
        + anywhere(len(needed)),
        out_specs=[
            pl.BlockSpec((TILE_Q, width), lambda i, *_: (i, 0)),
            pl.BlockSpec((TILE_Q, width), lambda i, *_: (i, 0)),
            pl.BlockSpec((heads, TILE_Q), lambda i, *_: (0, i)),
        ],
        scratch_shapes=[
            pltpu.VMEM((total_rows, 3 * width), BF16),
            pltpu.VMEM((total_rows // TILE_K, width, TILE_K), BF16),
            pltpu.VMEM((width, heads * TILE_Q), F32),
            pltpu.VMEM((1, heads * TILE_Q), F32),
            pltpu.VMEM((1, heads * TILE_Q), F32),
            pltpu.VMEM((TILE_K, heads * TILE_Q), F32),
            pltpu.VMEM((TILE_K, heads * TILE_Q), BF16),
        ],
    )
    return pl.pallas_call(
        functools.partial(attend_kernel, nctx, heads, len(pieces), len(needed), block_rows),
        grid_spec=grid_spec,
        out_shape=[
            jax.ShapeDtypeStruct((total_rows, width), BF16),
            jax.ShapeDtypeStruct((total_rows, width), BF16),
            jax.ShapeDtypeStruct((heads, total_rows), F32),
        ],
        compiler_params=params(),
        cost_estimate=takes(200),
        name="attend",
    )(place, lows, ends, bounds, *pieces, *needed)


def attend_back_kernel(
    nctx, heads, count, extra, block_rows, place, lows, ends, bounds, logs, *refs
):
    pieces, refs = refs[:count], refs[count:]
    grad, attended, refs = refs[0], refs[1], refs[2 + extra :]
    here, near, far, refs = *refs[:3], refs[3:]
    held, turned, grad_keys, grad_values, grad_query, raw, raw_grad, chances, steps, merged = refs
    tile_q, tile_k = grad.shape[0], turned.shape[2]
    width = grad.shape[1]
    index = pl.program_id(0)
    scale = jnp.asarray(HEAD_DIM**-0.5, BF16)

    @pl.when(index == 0)
    def _():
        load_pieces(place[0], pieces, nctx, held, block_rows)
        for tile in range(turned.shape[0]):
            turned[tile] = jnp.transpose(
                held[tile * tile_k : (tile + 1) * tile_k, width : 2 * width]
            )
        grad_keys[...] = jnp.zeros_like(grad_keys)
        grad_values[...] = jnp.zeros_like(grad_values)

    query_rows = pl.ds(pl.multiple_of(index * tile_q, tile_q), tile_q)
    queries = stack_heads(held[query_rows, :width] * scale, heads)
    incoming = stack_heads(grad[...], heads)
    product = jnp.transpose(grad[...].astype(F32) * attended[...].astype(F32))
    centre = jnp.concatenate(
        [
            jnp.sum(product[head * HEAD_DIM : (head + 1) * HEAD_DIM, :], axis=0, keepdims=True)
            for head in range(heads)
        ],
        axis=1,
    )
    first_key = jnp.concatenate([bounds[0:1, :]] * heads, axis=1)
    last_key = jnp.concatenate([bounds[1:2, :]] * heads, axis=1)
    log_total = jnp.concatenate([logs[head : head + 1, :] for head in range(heads)], axis=1)
    grad_query[...] = jnp.zeros_like(grad_query)

    def one(tile, _):
        start = tile * tile_k
        key_rows = pl.ds(pl.multiple_of(start, tile_k), tile_k)
        raw[...] = dot_turned(held[key_rows, width : 2 * width], queries)
        raw_grad[...] = dot_turned(held[key_rows, 2 * width :], incoming)
        last = jnp.minimum(last_key, ends[tile] - 1) - start
        first = first_key - start
        for begin in range(0, tile_k, STRIP):
            at = slice(begin, begin + STRIP)
            row = lax.broadcasted_iota(jnp.int32, (STRIP, raw.shape[1]), 0) + begin
            allowed = (row <= last) & (row >= first)
            chance = jnp.exp(jnp.where(allowed, raw[at, :] - log_total, NEGATIVE))
            chances[at, :] = chance.astype(BF16)
            steps[at, :] = (chance * (raw_grad[at, :] - centre)).astype(BF16)
        grad_values[key_rows, :] += dot(chances[...], incoming)
        grad_keys[key_rows, :] += dot(steps[...], queries)
        grad_query[...] += dot(turned[tile], steps[...])
        return 0

    upper = (index * tile_q + tile_q - 1) // tile_k + 1
    lax.fori_loop(lows[index], upper, one, 0)
    merged[query_rows, :width] = (
        fold_heads(grad_query[...], heads, tile_q) * HEAD_DIM**-0.5
    ).astype(BF16)

    @pl.when(index == pl.num_programs(0) - 1)
    def _():
        merged[:, width : 2 * width] = grad_keys[...].astype(BF16)
        merged[:, 2 * width :] = grad_values[...].astype(BF16)
        outs = [here, near] + [far.at[way] for way in range(nctx - 2)]
        for way, out in enumerate(outs):
            first = jnp.bitwise_xor(place[0], way) * block_rows
            out[...] = merged[pl.ds(pl.multiple_of(first, block_rows), block_rows), :]


def attend_back(pieces, place, lows, ends, bounds, logs, grad, attended, nctx, block_rows, *needed):
    total_rows, width = grad.shape
    heads = width // HEAD_DIM
    by_tile = pl.BlockSpec((TILE_Q, width), lambda i, *_: (i, 0))
    sent = (block_rows, 3 * width)
    sent = [sent, sent, (nctx - 2, *sent)]
    grid_spec = pltpu.PrefetchScalarGridSpec(
        num_scalar_prefetch=3,
        grid=(total_rows // TILE_Q,),
        in_specs=[
            pl.BlockSpec((2, TILE_Q), lambda i, *_: (0, i)),
            pl.BlockSpec((heads, TILE_Q), lambda i, *_: (0, i)),
        ]
        + [whole(piece.shape) for piece in pieces]
        + [by_tile] * 2
        + anywhere(len(needed)),
        out_specs=[whole(shape) for shape in sent],
        scratch_shapes=[
            pltpu.VMEM((total_rows, 3 * width), BF16),
            pltpu.VMEM((total_rows // TILE_K, width, TILE_K), BF16),
            pltpu.VMEM((total_rows, width), F32),
            pltpu.VMEM((total_rows, width), F32),
            pltpu.VMEM((width, heads * TILE_Q), F32),
            pltpu.VMEM((TILE_K, heads * TILE_Q), F32),
            pltpu.VMEM((TILE_K, heads * TILE_Q), F32),
            pltpu.VMEM((TILE_K, heads * TILE_Q), BF16),
            pltpu.VMEM((TILE_K, heads * TILE_Q), BF16),
            pltpu.VMEM((total_rows, 3 * width), BF16),
        ],
    )
    return pl.pallas_call(
        functools.partial(
            attend_back_kernel, nctx, heads, len(pieces), len(needed), block_rows
        ),
        grid_spec=grid_spec,
        out_shape=[jax.ShapeDtypeStruct(shape, BF16) for shape in sent],
        compiler_params=params(),
        cost_estimate=takes(250),
        name="attend_back",
    )(place, lows, ends, bounds, logs, *pieces, grad, attended, *needed)


def mix_kernel(nctx, count, place, heads_in, weight, source, gain, bias, *refs):
    returned, mixed, *lows = refs[count:]
    rows, depth = mixed.shape
    step = pl.program_id(0)
    left = jnp.concatenate([heads_in[c, 0] for c in range(nctx)], axis=1)
    returned[...] = left

    @pl.when(step == 0)
    def _():
        mixed[...] = source[...].astype(F32)

    mixed[...] += dot_turned(left, weight[0])

    @pl.when(step == pl.num_programs(0) - 1)
    def _():
        values = mixed[...]
        values = values - jnp.mean(values, axis=1, keepdims=True)
        scaling = lax.rsqrt(jnp.mean(values * values, axis=1, keepdims=True) + EPSILON)
        values = (values * scaling * gain[...] + bias[...]).astype(BF16)
        part_rows = lows[0].shape[0]
        for part, low in enumerate(lows):
            low[...] = values[part * part_rows : (part + 1) * part_rows]


def mix(heads_in, weight, full, gain, bias, place, parts, *needed):
    nctx, tp, rows, piece = heads_in.shape
    depth = full.shape[1]
    head_width = nctx * piece
    grid_spec = pltpu.PrefetchScalarGridSpec(
        num_scalar_prefetch=1,
        grid=(tp,),
        in_specs=[
            pl.BlockSpec((nctx, 1, rows, piece), lambda k, s: (0, k, 0, 0)),
            pl.BlockSpec((1, depth, head_width), lambda k, s: (k, 0, 0)),
            pl.BlockSpec((rows, depth), lambda k, s: (s[0], 0)),
            whole((1, depth)),
            whole((1, depth)),
        ]
        + anywhere(len(needed)),
        out_specs=[
            pl.BlockSpec((rows, head_width), lambda k, s: (0, k)),
            whole((rows, depth)),
        ]
        + [whole((rows // parts, depth))] * parts,
    )
    return pl.pallas_call(
        functools.partial(mix_kernel, nctx, len(needed)),
        grid_spec=grid_spec,
        out_shape=[
            jax.ShapeDtypeStruct((rows, tp * head_width), BF16),
            jax.ShapeDtypeStruct((rows, depth), F32),
        ]
        + [jax.ShapeDtypeStruct((rows // parts, depth), BF16)] * parts,
        compiler_params=params(),
        cost_estimate=takes(50),
        name="mix",
    )(place, heads_in, weight, full, gain, bias, *needed)


def feed_kernel(cuts, parts, tp, first_one, place, low, cot, mixed, source, *refs):
    refs = refs[-(5 + parts + 4) :]
    kept, grad_gate, grad_up, hidden, out = refs[:5]
    partials, held, sems = refs[5 : 5 + parts], refs[-4:-1], refs[-1]
    unit = source.shape[1] // 3
    width = out.shape[2]

    def copies(index):
        first, size = cuts[index]
        at = pl.ds(first, size)
        return [
            pltpu.make_async_copy(
                source.at[:, pl.ds(which * unit, unit), at],
                held[which].at[:, :, at],
                sems.at[index * 3 + which],
            )
            for which in range(3)
        ]

    for index in range(len(cuts)):
        for copy in copies(index):
            copy.start()
    kept[...] = low[...]
    rows, depth = kept.shape[0] // parts, kept.shape[1]
    grads = jnp.concatenate([cot[block] for block in range(tp)], axis=1)
    for index, (first, size) in enumerate(cuts):
        for copy in copies(index):
            copy.wait()
        at = slice(first, first + size)
        gate_weight, up_weight, down_weight = [w[:, :, at].reshape(depth, size) for w in held]
        gate = dot(kept[...], gate_weight)
        up = dot(kept[...], up_weight)
        sigma = 1.0 / (1.0 + jnp.exp(-gate))
        active = gate * sigma
        hidden[:, at] = (active * up).astype(BF16)
        grad = dot(grads, down_weight)
        grad_gate[:, at] = (grad * up * sigma * (1.0 + gate * (1.0 - sigma))).astype(BF16)
        grad_up[:, at] = (grad * active).astype(BF16)
    gate_weight, up_weight, down_weight = [w[...].reshape(depth, w.shape[2]) for w in held]
    product = dot_turned(grad_gate[...], gate_weight) + dot_turned(grad_up[...], up_weight)
    for part in range(parts):
        partials[part][...] = product[part * rows : (part + 1) * rows].astype(BF16)
    values = dot_turned(hidden[...], down_weight)
    if first_one:
        values = values + mixed[...]
    for block in range(tp):
        out[block] = values[:, block * width : (block + 1) * width].astype(BF16)


def feed(low, cot, mixed, weights, step, tp, place, held, parts, *needed):
    rows, depth = low.shape
    part_rows = rows // parts
    blocks, triple, hidden = weights.shape
    cuts = []
    while sum(size for _, size in cuts) < hidden:
        first = sum(size for _, size in cuts)
        cuts.append((first, min(512, hidden - first)))
    by_owner = lambda columns: pl.BlockSpec(
        (rows, columns), lambda i, s: (lax.rem(s[0] - step + tp, tp), 0)
    )
    width = depth // tp
    blocks_of_owner = pl.BlockSpec(
        (tp, rows, width), lambda i, s: (0, lax.rem(s[0] - step + tp, tp), 0)
    )
    grid_spec = pltpu.PrefetchScalarGridSpec(
        num_scalar_prefetch=1,
        grid=(1,),
        in_specs=[whole((rows, depth)), blocks_of_owner, whole(mixed.shape)]
        + anywhere(1 + len(held) + len(needed)),
        out_specs=[by_owner(depth)]
        + [by_owner(hidden)] * 3
        + [blocks_of_owner]
        + [whole((part_rows, depth))] * parts,
        scratch_shapes=[pltpu.VMEM((blocks, triple // 3, hidden), BF16)] * 3
        + [pltpu.SemaphoreType.DMA((3 * len(cuts),))],
    )
    return pl.pallas_call(
        functools.partial(feed_kernel, tuple(cuts), parts, tp, step == 0),
        grid_spec=grid_spec,
        out_shape=[
            jax.ShapeDtypeStruct((tp * rows, columns), BF16)
            for columns in (depth, hidden, hidden, hidden)
        ]
        + [jax.ShapeDtypeStruct((tp, tp * rows, width), BF16)]
        + [jax.ShapeDtypeStruct((part_rows, depth), BF16)] * parts,
        input_output_aliases={5 + index: index for index in range(len(held))},
        compiler_params=params(),
        cost_estimate=takes(100),
        name="feed",
    )(place, low, cot, mixed, weights, *held, *needed)


def blame_halves(lefts, rights, place, unit, *needed, held=(), offset=0, total=None):
    rows = lefts[0].shape[0]
    other = rights[0].shape[1]
    picked = lefts[1].shape[1] // unit
    chosen = pl.BlockSpec((rows, unit), lambda j, s: (0, 2 * (j ^ s[3]) + s[1] % 2))
    cut = pl.BlockSpec((rows, unit), lambda j, s: (0, j ^ s[3]))
    shapes = [(2, unit // 2, total or other)] * 4

    def kernel(place, left_here, left_there, right_here, right_there, *refs):
        outs, spare, sems = refs[len(held) + len(needed) : -2], refs[-2], refs[-1]
        product = 0.0
        for left, right in ((left_here, right_here), (left_there, right_there)):
            product = product + lax.dot_general(
                left[...], right[...], (((0,), (0,)), ((), ())), preferred_element_type=F32
            )
        product = product.astype(BF16)
        for j in range(picked):

            @pl.when(pl.program_id(0) == j)
            def _():
                first, second = spare.at[j // 2, j % 2], spare.at[2 + j % 2, j // 2]
                first[...], second[...] = product[: unit // 2], product[unit // 2 :]

        @pl.when(pl.program_id(0) == picked - 1)
        def _():
            moves = [
                pltpu.make_async_copy(
                    spare.at[index], out.at[:, :, pl.ds(offset, other)], sems.at[index]
                )
                for index, out in enumerate(outs)
            ]
            for move in moves:
                move.start()
            for move in moves:
                move.wait()

    grid_spec = pltpu.PrefetchScalarGridSpec(
        num_scalar_prefetch=1,
        grid=(picked,),
        in_specs=[chosen, cut]
        + [whole((rows, other))] * 2
        + anywhere(len(held) + len(needed)),
        out_specs=anywhere(4),
        scratch_shapes=[
            pltpu.VMEM((4, 2, unit // 2, other), BF16),
            pltpu.SemaphoreType.DMA((4,)),
        ],
    )
    place = jnp.concatenate([place, place[2:3] * 2 + place[1:2] // 2])
    return pl.pallas_call(
        kernel,
        grid_spec=grid_spec,
        out_shape=[jax.ShapeDtypeStruct(shape, BF16) for shape in shapes],
        input_output_aliases={5 + index: index for index in range(len(held))},
        compiler_params=params(),
        cost_estimate=takes(60),
        name="blame_halves",
    )(place, *lefts, *rights, *held, *needed)


def blame(left, right, *needed):
    rows, columns = left.shape
    if right.ndim == 3:
        steps, other = right.shape[0], right.shape[2]
        in_specs = [whole((rows, columns)), pl.BlockSpec((1, rows, other), lambda j: (j, 0, 0))]
        target, shape = pl.BlockSpec((columns, other), lambda j: (0, j)), (columns, steps * other)
    else:
        steps, other = 4, right.shape[1]
        in_specs = [pl.BlockSpec((rows, columns // steps), lambda j: (0, j)), whole((rows, other))]
        target, shape = pl.BlockSpec((columns // steps, other), lambda j: (j, 0)), (columns, other)

    def kernel(left, right, *refs):
        theirs = right[0] if len(right.shape) == 3 else right[...]
        refs[-1][...] = lax.dot_general(
            left[...], theirs, (((0,), (0,)), ((), ())), preferred_element_type=F32
        ).astype(BF16)

    return pl.pallas_call(
        kernel,
        grid=(steps,),
        in_specs=in_specs + anywhere(len(needed)),
        out_specs=target,
        out_shape=jax.ShapeDtypeStruct(shape, BF16),
        compiler_params=params(),
        cost_estimate=takes(60),
        name="blame",
    )(left, right, *needed)


def turn_kernel(nctx, count, parts, unit, place, *refs):
    arrived, own = refs[:parts], refs[parts : 2 * parts]
    mixed, cot, gain = refs[2 * parts : 2 * parts + 3]
    weight, refs = refs[2 * parts + 3], refs[2 * parts + 4 + count :]
    out, grad_mixed, grad_low, gain_grad, shift_grad, half = refs
    rows, depth = mixed.shape
    piece = out.shape[3]

    @pl.when(pl.program_id(0) == 0)
    def _():
        incoming = jnp.concatenate(
            [there[...].astype(F32) + here[...].astype(F32) for there, here in zip(arrived, own)]
        )
        values = mixed[...]
        values = values - jnp.mean(values, axis=1, keepdims=True)
        scaling = lax.rsqrt(jnp.mean(values * values, axis=1, keepdims=True) + EPSILON)
        normed = values * scaling
        shift_grad[...] = jnp.sum(incoming, axis=0, keepdims=True)
        gain_grad[...] = jnp.sum(incoming * normed, axis=0, keepdims=True)
        scaled = incoming * gain[...]
        grads = jnp.concatenate([cot[block] for block in range(cot.shape[0])], axis=1)
        total = grads.astype(F32) + scaling * (
            scaled
            - jnp.mean(scaled, axis=1, keepdims=True)
            - normed * jnp.mean(scaled * normed, axis=1, keepdims=True)
        )
        grad_mixed[...] = total
        grad_low[...] = total.astype(BF16)
        write_half(half, grad_low, 1 - lax.rem(place[1], 2), unit)

    product = dot(grad_low[...], weight[0])
    for c in range(nctx):
        out[c, 0] = product[:, c * piece : (c + 1) * piece].astype(BF16)


def turn(arrived, own, mixed, cot, gain, weight, place, nctx, tp, unit, *needed):
    rows, depth = mixed.shape
    parts = len(arrived)
    head_width = weight.shape[2]
    piece = head_width // nctx
    grid_spec = pltpu.PrefetchScalarGridSpec(
        num_scalar_prefetch=1,
        grid=(tp,),
        in_specs=[whole((rows // parts, depth))] * (2 * parts)
        + [whole((rows, depth))]
        + [
            pl.BlockSpec((tp, rows, depth // tp), lambda k, s: (0, s[0], 0)),
            whole((1, depth)),
            pl.BlockSpec((1, depth, head_width), lambda k, s: (k, 0, 0)),
        ]
        + anywhere(len(needed)),
        out_specs=[
            pl.BlockSpec((nctx, 1, rows, piece), lambda k, s: (0, k, 0, 0)),
            whole((rows, depth)),
            whole((rows, depth)),
            whole((1, depth)),
            whole((1, depth)),
            whole((rows, depth // 2)),
        ],
    )
    return pl.pallas_call(
        functools.partial(turn_kernel, nctx, len(needed), parts, unit),
        grid_spec=grid_spec,
        out_shape=[
            jax.ShapeDtypeStruct((nctx, tp, rows, piece), BF16),
            jax.ShapeDtypeStruct((rows, depth), F32),
            jax.ShapeDtypeStruct((rows, depth), BF16),
            jax.ShapeDtypeStruct((1, depth), F32),
            jax.ShapeDtypeStruct((1, depth), F32),
            jax.ShapeDtypeStruct((rows, depth // 2), BF16),
        ],
        compiler_params=params(),
        cost_estimate=takes(60),
        name="turn",
    )(place, *arrived, *own, mixed, cot, gain, weight, *needed)


def finish_kernel(nctx, tp, extra_count, place, *refs):
    pieces = refs[:nctx]
    cosine, sine_up, sine_down, full, extra, gain = refs[nctx : nctx + 6]
    weight, refs = refs[nctx + 6], refs[nctx + 7 + extra_count :]
    outs = refs[:tp]
    low, bias_grad, gain_grad, shift_grad, spare = refs[tp:]
    rows, wide = pieces[0].shape
    piece = wide // 3
    width = outs[0].shape[1]
    strip = spare.shape[0]
    extra_rows = extra.shape[0]

    @pl.when(pl.program_id(0) == 0)
    def _():
        bias_grad[...] = jnp.zeros_like(bias_grad)
        gain_grad[...] = jnp.zeros_like(gain_grad)
        shift_grad[...] = jnp.zeros_like(shift_grad)

    for step in range(nctx):
        source = jnp.bitwise_xor(place[1], step)
        for part in range(3):
            values = pieces[step][:, part * piece : (part + 1) * piece].astype(F32)
            if part < 2:
                values = (
                    values * cosine[...]
                    - pltpu.roll(values, piece - ROT // 2, 1) * sine_up[...]
                    - pltpu.roll(values, ROT // 2, 1) * sine_down[...]
                )
            columns = pl.ds(pl.multiple_of(source * wide + part * piece, piece), piece)
            bias_grad[:, columns] += jnp.sum(values, axis=0, keepdims=True)
            low[:, columns] = values.astype(BF16)

    incoming = dot_turned(low[...], weight[...])
    source = full[...].astype(F32)
    source = source - jnp.mean(source, axis=1, keepdims=True)
    scaling = lax.rsqrt(jnp.mean(source * source, axis=1, keepdims=True) + EPSILON)
    normed = source * scaling
    shift_grad[...] += jnp.sum(incoming, axis=0, keepdims=True)
    gain_grad[...] += jnp.sum(incoming * normed, axis=0, keepdims=True)
    scaled = incoming * gain[...]
    spare[...] = scaling * (
        scaled
        - jnp.mean(scaled, axis=1, keepdims=True)
        - normed * jnp.mean(scaled * normed, axis=1, keepdims=True)
    )
    first = pl.program_id(0) * strip
    wanted = place[0] * extra_rows

    if strip <= extra_rows:

        @pl.when((first >= wanted) & (first < wanted + extra_rows))
        def _():
            spare[...] += extra[pl.ds(pl.multiple_of(first - wanted, strip), strip), :]

    else:

        @pl.when((wanted >= first) & (wanted < first + strip))
        def _():
            spare[pl.ds(pl.multiple_of(wanted - first, extra_rows), extra_rows), :] += extra[...]

    for step, out in enumerate(outs):
        owner = lax.rem(place[0] - step + tp, tp)
        out[...] = spare[:, pl.ds(pl.multiple_of(owner * width, width), width)].astype(BF16)


def finish(pieces, place, tables, full, extra, gain, weight, tp, *needed):
    rows, wide = pieces[0].shape
    depth = full.shape[1]
    total = weight.shape[1]
    strip = 256
    steps = rows // strip
    width = depth // tp
    nctx = len(pieces)
    by_rows = lambda columns: pl.BlockSpec((strip, columns), lambda i, s: (i, 0))
    grid_spec = pltpu.PrefetchScalarGridSpec(
        num_scalar_prefetch=1,
        grid=(steps,),
        in_specs=[by_rows(wide)] * nctx
        + [by_rows(2 * HEAD_DIM)] * 3
        + [
            by_rows(depth),
            whole(extra.shape),
            whole((1, depth)),
        ]
        + [whole(weight.shape)]
        + anywhere(len(needed)),
        out_specs=[by_rows(width)] * tp
        + [
            by_rows(total),
            whole((1, total)),
            whole((1, depth)),
            whole((1, depth)),
        ],
        scratch_shapes=[pltpu.VMEM((strip, depth), F32)],
    )
    return pl.pallas_call(
        functools.partial(finish_kernel, nctx, tp, len(needed)),
        grid_spec=grid_spec,
        out_shape=[jax.ShapeDtypeStruct((rows, width), BF16)] * tp
        + [
            jax.ShapeDtypeStruct((rows, total), BF16),
            jax.ShapeDtypeStruct((1, total), F32),
            jax.ShapeDtypeStruct((1, depth), F32),
            jax.ShapeDtypeStruct((1, depth), F32),
        ],
        compiler_params=params(),
        cost_estimate=takes(70),
        name="finish",
    )(place, *pieces, *tables, full, extra, gain, weight, *needed)


def join(rings, place):
    parts, tp = len(rings), len(rings[0])
    rows, width = rings[0][0].shape

    def kernel(place, *refs):
        for part in range(parts):
            for step in range(tp):
                owner = lax.rem(place[0] - step + tp, tp)
                refs[-1][owner, part * rows : (part + 1) * rows, :] = refs[part * tp + step][...]

    grid_spec = pltpu.PrefetchScalarGridSpec(
        num_scalar_prefetch=1,
        grid=(1,),
        in_specs=[whole((rows, width))] * (parts * tp),
        out_specs=whole((tp, parts * rows, width)),
    )
    return pl.pallas_call(
        kernel,
        grid_spec=grid_spec,
        out_shape=jax.ShapeDtypeStruct((tp, parts * rows, width), BF16),
        compiler_params=params(),
        cost_estimate=takes(10),
        name="join",
    )(place, *[block for blocks in rings for block in blocks])


def pack_kernel(gate, up, down, out):
    rows = gate.shape[0]
    out[:rows] = gate[...]
    out[rows : 2 * rows] = up[...]
    out[2 * rows :] = jnp.transpose(down[...])


def pack(gate, up, down):
    rows, columns = gate.shape
    return pl.pallas_call(
        pack_kernel,
        out_shape=jax.ShapeDtypeStruct((3 * rows, columns), BF16),
        compiler_params=params(),
        cost_estimate=takes(10),
        name="pack",
    )(gate, up, down)


def contract_rows(left, right):
    return lax.dot_general(left, right, (((0,), (0,)), ((), ())), preferred_element_type=F32)


def pick(stack, index):
    return lax.dynamic_index_in_dim(stack, index, 0, keepdims=False)


def shards(
    nfsdp,
    nctx,
    tp,
    inputs,
    cotangent,
    first_gain,
    first_bias,
    qkv_weight,
    qkv_bias,
    out_weight,
    second_gain,
    second_bias,
    gate_weight,
    up_weight,
    down_weight,
    lengths,
    fill_counts,
):
    data = ("fsdp", "ctx")
    ndata = nfsdp * nctx
    block_rows, width = inputs.shape
    depth = tp * width
    half_depth = depth // 2
    unit = depth // ndata
    tensor_index = lax.axis_index("tp").astype(jnp.int32)
    context_index = lax.axis_index("ctx").astype(jnp.int32)
    fsdp_index = lax.axis_index("fsdp").astype(jnp.int32)
    part_rows = block_rows // tp
    chunk_rows = block_rows // CHUNKS
    head_width = qkv_weight.shape[2]
    piece = head_width // nctx
    wide = 3 * piece

    square = nfsdp == 2 and nctx == 4 and unit % 128 == 0
    place = jnp.stack([tensor_index, context_index, fsdp_index])

    def shift(value, step):
        return lax.ppermute(value, "tp", [(i, (i + step) % tp) for i in range(tp)])

    def swap(value, step):
        return lax.ppermute(value, "ctx", [(i, i ^ step) for i in range(nctx)])

    core_index = context_index % 2
    groups = [list(range(0, ndata, 2)), list(range(1, ndata, 2))]
    def mate(value):
        return swap(value, 1)

    def send(here, near, far, *needed):
        far = swap(far, 2)
        return [here, swap(near, 1), far[0], swap(tie(far[1], *needed), 1)]

    def scatter_half(value, axis):
        return lax.psum_scatter(
            value, data, scatter_dimension=axis, tiled=True, axis_index_groups=groups
        )

    def scatter(value, axis):
        return lax.psum_scatter(value, data, scatter_dimension=axis, tiled=True)

    def cross(value):
        return lax.ppermute(value, "fsdp", [(i, i ^ 1) for i in range(nfsdp)])

    def square_once(parts):
        near, far, low, high = parts
        return total(near, cross(far)), total(low, swap(high, 2))

    def square_twice(first, second):
        first = first[0].astype(F32) + swap(first[1], 2).astype(F32)
        second = second[0].astype(F32) + cross(second[1]).astype(F32)
        return jnp.concatenate([first, second], axis=0)

    def total(left, right):
        return (left.astype(F32) + right.astype(F32)).astype(BF16)

    owners = [(tensor_index - step + tp) % tp for step in range(tp)]

    own_qkv = (
        qkv_weight.reshape(-1, 3, nctx, piece).transpose(0, 2, 1, 3).reshape(-1, 3 * head_width)
    )
    full_qkv = lax.all_gather(own_qkv, data, axis=0, tiled=True)
    own_feed = pack(gate_weight, up_weight, down_weight)
    feed_weights = lax.all_gather(own_feed, data, axis=0, tiled=True).reshape(ndata, 3 * unit, -1)

    validity, position, first_key, last_key = layout(lengths[0], fill_counts[0], block_rows)
    own_position = lax.dynamic_slice_in_dim(position, context_index * block_rows, block_rows, 0)
    tables = rotary_tables(own_position)
    bounds = jnp.stack([first_key, last_key])
    tile_first = first_key[::TILE_Q]
    tile_count = tile_first.shape[0]
    lows = jnp.where(validity[::TILE_Q], tile_first // TILE_K, tile_count * TILE_Q).astype(jnp.int32)
    key_block = jnp.arange(0, nctx * block_rows, TILE_K, dtype=jnp.int32) // block_rows
    ends = (
        key_block * block_rows
        + jnp.sum(
            jnp.where(
                key_block[:, None] == jnp.arange(nctx, dtype=jnp.int32)[None, :],
                fill_counts[0][None, :],
                0,
            ),
            axis=1,
        )
    ).astype(jnp.int32)

    flat_bias = qkv_bias.reshape(3, nctx, piece).transpose(1, 0, 2).reshape(1, -1)
    gain_one, bias_one = first_gain[None], first_bias[None]
    gain_two, bias_two = second_gain[None], second_bias[None]

    rings = [[inputs[c * chunk_rows : (c + 1) * chunk_rows]] for c in range(CHUNKS)]
    share = unit // CHUNKS
    for chunk in range(CHUNKS):
        carried = out_weight.T[chunk * share : (chunk + 1) * share]
        rings[chunk][0] = jnp.concatenate([rings[chunk][0], carried], axis=0)
    for chunk in range(CHUNKS):
        for _ in range(tp - 1):
            rings[chunk].append(shift(rings[chunk][-1], 1))
            if len(rings[chunk]) == 2:
                rings[chunk][-1] = tie(rings[chunk][-1], own_feed)
    all_low, full, low_half, *outgoing, stack = project(
        rings, place, gain_one, bias_one, full_qkv, flat_bias, tables, nctx, unit
    )
    full_out = lax.all_gather(stack, data, axis=1, tiled=True)

    cot = tie(cotangent, *[blocks[-1] for blocks in rings])
    cot_rings = [[cot[c * chunk_rows : (c + 1) * chunk_rows]] for c in range(CHUNKS)]
    for blocks in cot_rings:
        for _ in range(tp - 1):
            blocks.append(shift(blocks[-1], 1))
    pieces = send(*outgoing, *[blocks[max(tp - 2, 0)] for blocks in cot_rings])

    attended, outgoing, logs = attend(
        pieces,
        place[1:2],
        lows,
        ends,
        bounds,
        nctx,
        block_rows,
        feed_weights,
    )
    cot = join(cot_rings, place)
    arrived = lax.all_to_all(
        tie(outgoing, *[blocks[-1] for blocks in cot_rings]).reshape(nctx * tp, part_rows, piece),
        ("ctx", "tp"),
        split_axis=0,
        concat_axis=0,
        tiled=True,
    )
    returned, mixed, second_low = mix(
        arrived.reshape(nctx, tp, part_rows, piece),
        full_out,
        full,
        gain_two,
        bias_two,
        place,
        1,
    )

    arrived, held, partials, travelling = second_low, [], [], None
    for step in range(tp):
        coming = shift(arrived, 1) if step < tp - 1 else None
        needed = travelling if step == tp - 1 and step > 2 else []
        *held, first, second = feed(
            arrived, cot, mixed, feed_weights, step, tp, place, held, HALVES, *needed
        )
        partials.append([first, second])
        if step == 1 % tp:
            travelling = partials[step]
        elif step > 1:
            travelling = [
                total(shift(value, 1), kept) for value, kept in zip(travelling, partials[step])
            ]
        if step == 0 and coming is not None:
            coming = tie(coming, partials[0][0])
        arrived = coming
    all_second, all_gate, all_up, hidden, feedforward = held

    last = [shift(value, 1) for value in travelling]
    half_gate = blame(all_second, all_gate, *travelling)
    half_up = blame(all_second, all_up, *travelling)
    half_down = blame(hidden, cot, *travelling)
    grad_heads, grad_mixed, mixed_low, gain_grad_two, shift_grad_two, mixed_half = turn(
        last,
        partials[0],
        mixed,
        cot,
        gain_two,
        full_out,
        place,
        nctx,
        tp,
        unit,
        half_gate,
        half_up,
        half_down,
    )
    grad_heads = lax.all_to_all(
        grad_heads.reshape(nctx * tp, part_rows, piece),
        ("ctx", "tp"),
        split_axis=0,
        concat_axis=0,
        tiled=True,
    ).reshape(nctx * block_rows, piece)

    total_gate = scatter(tie(half_gate, mixed_low), 0).astype(F32)
    total_up = scatter(tie(half_up, mixed_low), 0).astype(F32)
    total_down = scatter(tie(half_down, mixed_low), 1).astype(F32)

    feedforward = tie(feedforward, grad_heads)
    layer_out = [pick(feedforward, owners[1 % tp])]
    for step in range(1, tp):
        kept = pick(feedforward, owners[(step + 1) % tp])
        layer_out.append(total(shift(layer_out[-1], 1), kept))

    grad_pieces = attend_back(
        pieces, place[1:2], lows, ends, bounds, logs, grad_heads, attended, nctx, block_rows
    )
    arrived = send(*grad_pieces, *layer_out[max(tp - 2, 0) : tp - 1])
    layer_out = layer_out[-1]
    both = depth + 3 * head_width
    if square:
        parts = blame_halves(
            (mixed_low, mate(mixed_half)),
            (returned, mate(returned)),
            place,
            unit,
            arrived[2],
            total=both,
        )
        half_out = parts[0]
    else:
        half_out = blame(mixed_low, returned)
        total_out = scatter(half_out, 0).astype(F32)
    low_halves = mate(low_half) if square else low_half
    needed = [layer_out, low_halves, half_out]
    *partial, all_grad, bias_grad, gain_grad, shift_grad = finish(
        arrived, place, tables, full, grad_mixed, gain_one, full_qkv, tp, *needed
    )
    if square:
        parts = blame_halves(
            (all_low, low_halves),
            (all_grad, mate(all_grad)),
            place,
            unit,
            held=parts,
            offset=depth,
            total=both,
        )
    else:
        parts = []
    def exchange(value, axis, steps, size):
        for step in steps:
            value = value + lax.ppermute(value, axis, [(i, i ^ step) for i in range(size)])
        return value

    def powers(first, size):
        return [1 << bit for bit in range(first, size.bit_length() - 1)]

    small = jnp.concatenate([gain_grad, shift_grad, gain_grad_two, shift_grad_two], axis=1)
    small = sum([shift(small, step) for step in range(1, tp)], small)
    small = jnp.concatenate([bias_grad, small], axis=1)
    travelling, ring_steps = partial[1 % tp], []
    once = square_once(parts) if square else ()
    needed = [[total_gate, total_up, small, *parts], [*once], [total_down]]
    for step in range(1, tp):
        travelling = add(
            shift(travelling, 1), partial[(step + 1) % tp], *(needed[step - 1] if step < 4 else [])
        )
        ring_steps.append(travelling)
        if step < 3:
            bits = powers(0, min(nctx, 2)) if step == 1 else powers(1, nctx)
            small = exchange(tie(small, travelling), "ctx", bits, nctx)
            needed[step].append(small)
    small = exchange(tie(small, travelling), "fsdp", powers(0, nfsdp), nfsdp)
    grad_inputs = travelling
    if square:
        totals = square_twice(*once)
        total_out, total_qkv = totals[:, :depth], totals[:, depth:]
    else:
        total_qkv = scatter(blame(all_low, all_grad), 0).astype(F32)

    total_qkv = (
        total_qkv
        .reshape(-1, nctx, 3, piece)
        .transpose(0, 2, 1, 3)
        .reshape(-1, 3, head_width)
    )

    out_parts = jnp.swapaxes(
        total_out.astype(BF16).reshape(-1, tp, head_width), 0, 1
    )
    total_out = pick(out_parts, tensor_index).astype(F32)
    for step in range(1, tp):
        total_out = total_out + shift(pick(out_parts, (tensor_index + step) % tp), step).astype(F32)
    total_out = total_out.T

    bias_total, small = small[:, : 3 * head_width], small[:, 3 * head_width :]
    bias_total = bias_total.reshape(nctx, 3, piece).transpose(1, 0, 2).reshape(3, head_width)
    small = small.reshape(4, depth)
    return (
        layer_out,
        grad_inputs,
        small[0],
        small[1],
        total_qkv,
        bias_total,
        total_out,
        small[2],
        small[3],
        total_gate,
        total_up,
        total_down,
    )


def solution(mesh):
    data = ("fsdp", "ctx")
    by_rows = P(data, "tp")
    by_columns = P("tp", data)
    qkv = P(data, None, "tp")
    return jax.shard_map(
        functools.partial(shards, mesh.shape["fsdp"], mesh.shape["ctx"], mesh.shape["tp"]),
        mesh=mesh,
        in_specs=(
            by_rows,
            by_rows,
            P(),
            P(),
            qkv,
            P(None, "tp"),
            by_columns,
            P(),
            P(),
            by_rows,
            by_rows,
            by_columns,
            P("fsdp", None),
            P("fsdp", None),
        ),
        out_specs=(
            by_rows,
            by_rows,
            P(),
            P(),
            qkv,
            P(None, "tp"),
            by_columns,
            P(),
            P(),
            by_rows,
            by_rows,
            by_columns,
        ),
        check_vma=False,
    )
```

```python
import functools

import jax
import jax.numpy as jnp
from jax import lax
from jax.experimental import pallas as pl
from jax.experimental.pallas import tpu as pltpu
from jax.sharding import PartitionSpec as P

HEAD_DIM = 64
ROT = 16
EPSILON = 1e-05
NEGATIVE = -1e30
FLOOR = -1e20
VMEM_LIMIT = 56 * 1024 * 1024
TILE_Q = 512
TILE_K = 512
STRIP = 32
CHUNKS = 2
HALVES = 2

F32 = jnp.float32
BF16 = jnp.bfloat16


def layout(lengths, fill_counts, block_rows):
    blocks_count = fill_counts.shape[0]
    seq_count = lengths.shape[0]
    slot_index = jnp.arange(blocks_count * block_rows, dtype=jnp.int32)
    block_of = slot_index // block_rows
    within = slot_index - block_of * block_rows
    chooser = block_of[:, None] == jnp.arange(blocks_count, dtype=jnp.int32)[None, :]
    fill_here = jnp.sum(jnp.where(chooser, fill_counts[None, :], 0), axis=1)
    before = jnp.cumsum(fill_counts) - fill_counts
    before_here = jnp.sum(jnp.where(chooser, before[None, :], 0), axis=1)
    validity = within < fill_here
    used_index = before_here + within
    seq_ends = jnp.cumsum(lengths)
    sequence = jnp.sum((used_index[:, None] >= seq_ends[None, :]).astype(jnp.int32), axis=1)
    seq_starts = seq_ends - lengths
    picker = sequence[:, None] == jnp.arange(seq_count, dtype=jnp.int32)[None, :]
    start_here = jnp.sum(jnp.where(picker, seq_starts[None, :], 0), axis=1)
    after = before + fill_counts
    start_block = jnp.sum((seq_starts[:, None] >= after[None, :]).astype(jnp.int32), axis=1)
    start_block = jnp.minimum(start_block, blocks_count - 1)
    block_pick = start_block[:, None] == jnp.arange(blocks_count, dtype=jnp.int32)[None, :]
    start_before = jnp.sum(jnp.where(block_pick, before[None, :], 0), axis=1)
    start_slot = start_block * block_rows + seq_starts - start_before
    slot_here = jnp.sum(jnp.where(picker, start_slot[None, :], 0), axis=1)
    first_key = jnp.where(validity, slot_here, 0).astype(jnp.int32)
    last_key = jnp.where(validity, slot_index, -1).astype(jnp.int32)
    return (validity, used_index - start_here, first_key, last_key)


def rotary_tables(position):
    half = ROT // 2
    lane = jnp.arange(2 * HEAD_DIM, dtype=jnp.int32) % HEAD_DIM
    frequency = 10000.0 ** (-(2.0 * (lane % half).astype(F32)) / ROT)
    angles = position.astype(F32)[:, None] * frequency[None, :]
    cosine, sine = jnp.cos(angles), jnp.sin(angles)
    lane = lane[None, :]
    return (
        jnp.where(lane < ROT, cosine, 1.0),
        jnp.where(lane < half, -sine, 0.0),
        jnp.where((lane >= half) & (lane < ROT), sine, 0.0),
    )


def params(**extra):
    return pltpu.CompilerParams(vmem_limit_bytes=VMEM_LIMIT, **extra)


def takes(microseconds):
    return pl.CostEstimate(
        flops=int(microseconds * 1e8), bytes_accessed=0, transcendentals=0
    )


def whole(shape):
    return pl.BlockSpec(shape, lambda *_: (0,) * len(shape))


def anywhere(count):
    return [pl.BlockSpec(memory_space=pl.ANY)] * count


def write_half(out, values, half, unit):
    if unit % 128:
        out[...] = values[:, : out.shape[1]]
        return
    for block in range(out.shape[1] // unit):
        first = pl.multiple_of((2 * block + half) * unit, unit)
        out[:, block * unit : (block + 1) * unit] = values[:, pl.ds(first, unit)]


def dot(left, right):
    return jnp.dot(left, right, preferred_element_type=F32)


def dot_turned(left, right):
    return lax.dot_general(left, right, (((1,), (1,)), ((), ())), preferred_element_type=F32)


def tie(value, *needed):
    def kernel(*refs):
        del refs

    return pl.pallas_call(
        kernel,
        in_specs=anywhere(1 + len(needed)),
        out_specs=pl.BlockSpec(memory_space=pl.ANY),
        out_shape=jax.ShapeDtypeStruct(value.shape, value.dtype),
        input_output_aliases={0: 0},
        name="tie",
    )(value, *needed)


def add_kernel(left, right, *refs):
    refs[-1][...] = (left[...].astype(F32) + right[...].astype(F32)).astype(BF16)


def add(left, right, *needed):
    rows, columns = left.shape
    strip = min(rows, 512)
    block = pl.BlockSpec((strip, columns), lambda i: (i, 0))
    return pl.pallas_call(
        add_kernel,
        grid=(rows // strip,),
        in_specs=[block, block] + anywhere(len(needed)),
        out_specs=block,
        out_shape=jax.ShapeDtypeStruct(left.shape, BF16),
        compiler_params=params(),
        cost_estimate=takes(10),
        name="ring_add",
    )(left, right, *needed)


def project_kernel(tp, chunks, per, unit, place, *refs):
    rings, refs = refs[: tp * chunks], refs[tp * chunks :]
    gain, bias, weight, weight_bias, cosine, sine_up, sine_down = refs[:7]
    low, full, half, here, near, far, stack = refs[7:]
    outs = [here, near] + [far.at[way] for way in range(far.shape[0])]
    rows, width = low.shape[0] // chunks, rings[0].shape[1]
    depth = tp * width
    wide = here.shape[1]
    piece = wide // 3
    step = pl.program_id(0)

    @pl.when(pl.program_id(0) == 0)
    def _():
        strip = 128
        for start in range(0, rows * chunks, strip):
            chunk, first = start // rows, start % rows
            blocks = rings[chunk * tp : (chunk + 1) * tp]
            at = slice(start, start + strip)
            inner = slice(first, first + strip)
            parts = [block[inner, :].astype(F32) for block in blocks]
            centre = sum(jnp.sum(part, axis=1, keepdims=True) for part in parts) / depth
            parts = [part - centre for part in parts]
            spread = sum(jnp.sum(part * part, axis=1, keepdims=True) for part in parts) / depth
            scaling = lax.rsqrt(spread + EPSILON)
            for step in range(tp):
                owner = lax.rem(place[0] - step + tp, tp)
                columns = pl.ds(pl.multiple_of(owner * width, width), width)
                low[at, columns] = (
                    parts[step] * scaling * gain[:, columns] + bias[:, columns]
                ).astype(BF16)
                full[at, columns] = blocks[step][inner, :]
        write_half(half, low, 1 - lax.rem(place[1], 2), unit)
        share = rings[0].shape[0] - rows
        for chunk in range(chunks):
            for step in range(tp):
                owner = lax.rem(place[0] - step + tp, tp)
                stack[owner, chunk * share : (chunk + 1) * share, :] = rings[chunk * tp + step][
                    rows:, :
                ]

    product = dot(low[...], weight[...]) + weight_bias[...]
    groups = []
    for group in range(per):
        parts = []
        for part in range(3):
            first = (group * 3 + part) * piece
            values = product[:, first : first + piece]
            if part < 2:
                values = (
                    values * cosine[...]
                    + pltpu.roll(values, piece - ROT // 2, 1) * sine_up[...]
                    + pltpu.roll(values, ROT // 2, 1) * sine_down[...]
                )
            parts.append(values.astype(BF16))
        groups.append(parts)
    flip = lax.rem(place[1], per)
    for way, out in enumerate(outs):
        for group in range(per):

            @pl.when((step == way // per) & (jnp.bitwise_xor(group, flip) == way % per))
            def _():
                for part in range(3):
                    out[:, part * piece : (part + 1) * piece] = groups[group][part]


def project(rings, place, gain, bias, weight, weight_bias, tables, nctx, unit):
    chunks, tp = len(rings), len(rings[0])
    rows, width = tables[0].shape[0], rings[0][0].shape[1]
    depth = tp * width
    total = weight.shape[1]
    wide = total // nctx
    per = 2 if nctx % 2 == 0 else 1
    grid_spec = pltpu.PrefetchScalarGridSpec(
        num_scalar_prefetch=1,
        grid=(nctx // per,),
        in_specs=[whole(rings[0][0].shape)] * (tp * chunks)
        + [whole((1, depth))] * 2
        + [
            pl.BlockSpec((depth, per * wide), lambda i, s: (0, jnp.bitwise_xor(i, s[1] // per))),
            pl.BlockSpec((1, per * wide), lambda i, s: (0, jnp.bitwise_xor(i, s[1] // per))),
        ]
        + [whole((rows, 2 * HEAD_DIM))] * 3,
        out_specs=[whole((rows, depth))] * 2
        + [whole((rows, depth // 2))]
        + [whole((rows, wide))] * 2
        + [whole((nctx - 2, rows, wide)), whole((tp, unit, width))],
    )
    return pl.pallas_call(
        functools.partial(project_kernel, tp, chunks, per, unit),
        grid_spec=grid_spec,
        out_shape=[
            jax.ShapeDtypeStruct((rows, depth), BF16),
            jax.ShapeDtypeStruct((rows, depth), BF16),
            jax.ShapeDtypeStruct((rows, depth // 2), BF16),
        ]
        + [jax.ShapeDtypeStruct((rows, wide), BF16)] * 2
        + [
            jax.ShapeDtypeStruct((nctx - 2, rows, wide), BF16),
            jax.ShapeDtypeStruct((tp, unit, width), BF16),
        ],
        compiler_params=params(),
        cost_estimate=takes(60),
        name="project",
    )(
        place,
        *[block for blocks in rings for block in blocks],
        gain,
        bias,
        weight,
        weight_bias,
        *tables,
    )


def stack_heads(tile, heads):
    lane = lax.broadcasted_iota(jnp.int32, tile.shape, 1) // HEAD_DIM
    return jnp.concatenate(
        [jnp.where(lane == head, tile, jnp.zeros_like(tile)) for head in range(heads)], axis=0
    )


def fold_heads(stacked, heads, columns):
    row = lax.broadcasted_iota(jnp.int32, (stacked.shape[0], columns), 0) // HEAD_DIM
    folded = jnp.zeros((stacked.shape[0], columns), F32)
    for head in range(heads):
        folded = folded + jnp.where(row == head, stacked[:, head * columns : (head + 1) * columns], 0.0)
    return jnp.transpose(folded)


def load_pieces(place, pieces, nctx, held, block_rows):
    chunk_rows = pieces[0].shape[0]
    chunks = len(pieces) // nctx
    for chunk in range(chunks):
        for step in range(nctx):
            source = jnp.bitwise_xor(place, step)
            first = source * block_rows + chunk * chunk_rows
            held[pl.ds(pl.multiple_of(first, chunk_rows), chunk_rows), :] = pieces[
                chunk * nctx + step
            ][...]


def attend_kernel(nctx, heads, count, extra, block_rows, place, lows, ends, bounds, *refs):
    pieces = refs[:count]
    out, sent, logs, held, turned, total, high, sums, raw, chances = refs[count + extra :]
    tile_q, tile_k = out.shape[0], turned.shape[2]
    width = heads * HEAD_DIM
    index = pl.program_id(0)

    @pl.when(index == 0)
    def _():
        load_pieces(place[0], pieces, nctx, held, block_rows)
        for tile in range(turned.shape[0]):
            turned[tile] = jnp.transpose(held[tile * tile_k : (tile + 1) * tile_k, 2 * width :])

    query_rows = pl.ds(pl.multiple_of(index * tile_q, tile_q), tile_q)
    queries = stack_heads(held[query_rows, :width] * jnp.asarray(HEAD_DIM**-0.5, BF16), heads)
    first_key = jnp.concatenate([bounds[0:1, :]] * heads, axis=1)
    last_key = jnp.concatenate([bounds[1:2, :]] * heads, axis=1)
    total[...] = jnp.zeros_like(total)
    high[...] = jnp.full_like(high, FLOOR)
    sums[...] = jnp.zeros_like(sums)

    def one(tile, _):
        start = tile * tile_k
        keys = held[pl.ds(pl.multiple_of(start, tile_k), tile_k), width : 2 * width]
        raw[...] = dot_turned(keys, queries)
        last = jnp.minimum(last_key, ends[tile] - 1) - start
        first = first_key - start
        peaks = jnp.broadcast_to(high[...], (8, raw.shape[1]))
        for begin in range(0, tile_k, STRIP):
            scores = raw[begin : begin + STRIP, :]
            row = lax.broadcasted_iota(jnp.int32, scores.shape, 0) + begin
            scores = jnp.where((row <= last) & (row >= first), scores, NEGATIVE)
            raw[begin : begin + STRIP, :] = scores
            for group in range(0, STRIP, 8):
                peaks = jnp.maximum(peaks, scores[group : group + 8])
        highest = jnp.max(peaks, axis=0, keepdims=True)
        partial = jnp.zeros((8, raw.shape[1]), F32)
        for begin in range(0, tile_k, STRIP):
            raised = jnp.exp(raw[begin : begin + STRIP, :] - highest)
            chances[begin : begin + STRIP, :] = raised.astype(BF16)
            for group in range(0, STRIP, 8):
                partial = partial + raised[group : group + 8]
        shrink = jnp.exp(high[...] - highest)
        sums[...] = sums[...] * shrink + jnp.sum(partial, axis=0, keepdims=True)
        total[...] = total[...] * shrink + dot(turned[tile], chances[...])
        high[...] = highest
        return 0

    upper = (index * tile_q + tile_q - 1) // tile_k + 1
    lax.fori_loop(lows[index], upper, one, 0)
    found = sums[...] > 0.0
    safe = jnp.where(found, sums[...], 1.0)
    result = fold_heads(total[...] * jnp.where(found, 1.0 / safe, 0.0), heads, tile_q)
    out[...] = result.astype(BF16)
    sent[...] = result.astype(BF16)
    log_total = jnp.where(found, high[...] + jnp.log(safe), 0.0)
    for head in range(heads):
        logs[head : head + 1, :] = log_total[:, head * tile_q : (head + 1) * tile_q]


def attend(pieces, place, lows, ends, bounds, nctx, block_rows, *needed):
    total_rows = nctx * block_rows
    width = pieces[0].shape[1] // 3
    heads = width // HEAD_DIM
    steps = total_rows // TILE_Q
    grid_spec = pltpu.PrefetchScalarGridSpec(
        num_scalar_prefetch=3,
        grid=(steps,),
        in_specs=[pl.BlockSpec((2, TILE_Q), lambda i, *_: (0, i))]
        + [whole(piece.shape) for piece in pieces]
        + anywhere(len(needed)),
        out_specs=[
            pl.BlockSpec((TILE_Q, width), lambda i, *_: (i, 0)),
            pl.BlockSpec((TILE_Q, width), lambda i, *_: (i, 0)),
            pl.BlockSpec((heads, TILE_Q), lambda i, *_: (0, i)),
        ],
        scratch_shapes=[
            pltpu.VMEM((total_rows, 3 * width), BF16),
            pltpu.VMEM((total_rows // TILE_K, width, TILE_K), BF16),
            pltpu.VMEM((width, heads * TILE_Q), F32),
            pltpu.VMEM((1, heads * TILE_Q), F32),
            pltpu.VMEM((1, heads * TILE_Q), F32),
            pltpu.VMEM((TILE_K, heads * TILE_Q), F32),
            pltpu.VMEM((TILE_K, heads * TILE_Q), BF16),
        ],
    )
    return pl.pallas_call(
        functools.partial(attend_kernel, nctx, heads, len(pieces), len(needed), block_rows),
        grid_spec=grid_spec,
        out_shape=[
            jax.ShapeDtypeStruct((total_rows, width), BF16),
            jax.ShapeDtypeStruct((total_rows, width), BF16),
            jax.ShapeDtypeStruct((heads, total_rows), F32),
        ],
        compiler_params=params(),
        cost_estimate=takes(200),
        name="attend",
    )(place, lows, ends, bounds, *pieces, *needed)


def attend_back_kernel(
    nctx, heads, count, extra, block_rows, place, lows, ends, bounds, logs, *refs
):
    pieces, refs = refs[:count], refs[count:]
    grad, attended, refs = refs[0], refs[1], refs[2 + extra :]
    here, near, far, refs = *refs[:3], refs[3:]
    held, turned, grad_keys, grad_values, grad_query, raw, raw_grad, chances, steps, merged = refs
    tile_q, tile_k = grad.shape[0], turned.shape[2]
    width = grad.shape[1]
    index = pl.program_id(0)
    scale = jnp.asarray(HEAD_DIM**-0.5, BF16)

    @pl.when(index == 0)
    def _():
        load_pieces(place[0], pieces, nctx, held, block_rows)
        for tile in range(turned.shape[0]):
            turned[tile] = jnp.transpose(
                held[tile * tile_k : (tile + 1) * tile_k, width : 2 * width]
            )
        grad_keys[...] = jnp.zeros_like(grad_keys)
        grad_values[...] = jnp.zeros_like(grad_values)

    query_rows = pl.ds(pl.multiple_of(index * tile_q, tile_q), tile_q)
    queries = stack_heads(held[query_rows, :width] * scale, heads)
    incoming = stack_heads(grad[...], heads)
    product = jnp.transpose(grad[...].astype(F32) * attended[...].astype(F32))
    centre = jnp.concatenate(
        [
            jnp.sum(product[head * HEAD_DIM : (head + 1) * HEAD_DIM, :], axis=0, keepdims=True)
            for head in range(heads)
        ],
        axis=1,
    )
    first_key = jnp.concatenate([bounds[0:1, :]] * heads, axis=1)
    last_key = jnp.concatenate([bounds[1:2, :]] * heads, axis=1)
    log_total = jnp.concatenate([logs[head : head + 1, :] for head in range(heads)], axis=1)
    grad_query[...] = jnp.zeros_like(grad_query)

    def one(tile, _):
        start = tile * tile_k
        key_rows = pl.ds(pl.multiple_of(start, tile_k), tile_k)
        raw[...] = dot_turned(held[key_rows, width : 2 * width], queries)
        raw_grad[...] = dot_turned(held[key_rows, 2 * width :], incoming)
        last = jnp.minimum(last_key, ends[tile] - 1) - start
        first = first_key - start
        for begin in range(0, tile_k, STRIP):
            at = slice(begin, begin + STRIP)
            row = lax.broadcasted_iota(jnp.int32, (STRIP, raw.shape[1]), 0) + begin
            allowed = (row <= last) & (row >= first)
            chance = jnp.exp(jnp.where(allowed, raw[at, :] - log_total, NEGATIVE))
            chances[at, :] = chance.astype(BF16)
            steps[at, :] = (chance * (raw_grad[at, :] - centre)).astype(BF16)
        grad_values[key_rows, :] += dot(chances[...], incoming)
        grad_keys[key_rows, :] += dot(steps[...], queries)
        grad_query[...] += dot(turned[tile], steps[...])
        return 0

    upper = (index * tile_q + tile_q - 1) // tile_k + 1
    lax.fori_loop(lows[index], upper, one, 0)
    merged[query_rows, :width] = (
        fold_heads(grad_query[...], heads, tile_q) * HEAD_DIM**-0.5
    ).astype(BF16)

    @pl.when(index == pl.num_programs(0) - 1)
    def _():
        merged[:, width : 2 * width] = grad_keys[...].astype(BF16)
        merged[:, 2 * width :] = grad_values[...].astype(BF16)
        outs = [here, near] + [far.at[way] for way in range(nctx - 2)]
        for way, out in enumerate(outs):
            first = jnp.bitwise_xor(place[0], way) * block_rows
            out[...] = merged[pl.ds(pl.multiple_of(first, block_rows), block_rows), :]


def attend_back(pieces, place, lows, ends, bounds, logs, grad, attended, nctx, block_rows, *needed):
    total_rows, width = grad.shape
    heads = width // HEAD_DIM
    by_tile = pl.BlockSpec((TILE_Q, width), lambda i, *_: (i, 0))
    sent = (block_rows, 3 * width)
    sent = [sent, sent, (nctx - 2, *sent)]
    grid_spec = pltpu.PrefetchScalarGridSpec(
        num_scalar_prefetch=3,
        grid=(total_rows // TILE_Q,),
        in_specs=[
            pl.BlockSpec((2, TILE_Q), lambda i, *_: (0, i)),
            pl.BlockSpec((heads, TILE_Q), lambda i, *_: (0, i)),
        ]
        + [whole(piece.shape) for piece in pieces]
        + [by_tile] * 2
        + anywhere(len(needed)),
        out_specs=[whole(shape) for shape in sent],
        scratch_shapes=[
            pltpu.VMEM((total_rows, 3 * width), BF16),
            pltpu.VMEM((total_rows // TILE_K, width, TILE_K), BF16),
            pltpu.VMEM((total_rows, width), F32),
            pltpu.VMEM((total_rows, width), F32),
            pltpu.VMEM((width, heads * TILE_Q), F32),
            pltpu.VMEM((TILE_K, heads * TILE_Q), F32),
            pltpu.VMEM((TILE_K, heads * TILE_Q), F32),
            pltpu.VMEM((TILE_K, heads * TILE_Q), BF16),
            pltpu.VMEM((TILE_K, heads * TILE_Q), BF16),
            pltpu.VMEM((total_rows, 3 * width), BF16),
        ],
    )
    return pl.pallas_call(
        functools.partial(
            attend_back_kernel, nctx, heads, len(pieces), len(needed), block_rows
        ),
        grid_spec=grid_spec,
        out_shape=[jax.ShapeDtypeStruct(shape, BF16) for shape in sent],
        compiler_params=params(),
        cost_estimate=takes(250),
        name="attend_back",
    )(place, lows, ends, bounds, logs, *pieces, grad, attended, *needed)


def mix_kernel(nctx, count, place, heads_in, weight, source, gain, bias, *refs):
    returned, mixed, *lows = refs[count:]
    rows, depth = mixed.shape
    step = pl.program_id(0)
    left = jnp.concatenate([heads_in[c, 0] for c in range(nctx)], axis=1)
    returned[...] = left

    @pl.when(step == 0)
    def _():
        mixed[...] = source[...].astype(F32)

    mixed[...] += dot_turned(left, weight[0])

    @pl.when(step == pl.num_programs(0) - 1)
    def _():
        values = mixed[...]
        values = values - jnp.mean(values, axis=1, keepdims=True)
        scaling = lax.rsqrt(jnp.mean(values * values, axis=1, keepdims=True) + EPSILON)
        values = (values * scaling * gain[...] + bias[...]).astype(BF16)
        part_rows = lows[0].shape[0]
        for part, low in enumerate(lows):
            low[...] = values[part * part_rows : (part + 1) * part_rows]


def mix(heads_in, weight, full, gain, bias, place, parts, *needed):
    nctx, tp, rows, piece = heads_in.shape
    depth = full.shape[1]
    head_width = nctx * piece
    grid_spec = pltpu.PrefetchScalarGridSpec(
        num_scalar_prefetch=1,
        grid=(tp,),
        in_specs=[
            pl.BlockSpec((nctx, 1, rows, piece), lambda k, s: (0, k, 0, 0)),
            pl.BlockSpec((1, depth, head_width), lambda k, s: (k, 0, 0)),
            pl.BlockSpec((rows, depth), lambda k, s: (s[0], 0)),
            whole((1, depth)),
            whole((1, depth)),
        ]
        + anywhere(len(needed)),
        out_specs=[
            pl.BlockSpec((rows, head_width), lambda k, s: (0, k)),
            whole((rows, depth)),
        ]
        + [whole((rows // parts, depth))] * parts,
    )
    return pl.pallas_call(
        functools.partial(mix_kernel, nctx, len(needed)),
        grid_spec=grid_spec,
        out_shape=[
            jax.ShapeDtypeStruct((rows, tp * head_width), BF16),
            jax.ShapeDtypeStruct((rows, depth), F32),
        ]
        + [jax.ShapeDtypeStruct((rows // parts, depth), BF16)] * parts,
        compiler_params=params(),
        cost_estimate=takes(50),
        name="mix",
    )(place, heads_in, weight, full, gain, bias, *needed)


def feed_kernel(cuts, parts, tp, first_one, place, low, cot, mixed, source, *refs):
    refs = refs[-(5 + parts + 4) :]
    kept, grad_gate, grad_up, hidden, out = refs[:5]
    partials, held, sems = refs[5 : 5 + parts], refs[-4:-1], refs[-1]
    unit = source.shape[1] // 3
    width = out.shape[2]

    def copies(index):
        first, size = cuts[index]
        at = pl.ds(first, size)
        return [
            pltpu.make_async_copy(
                source.at[:, pl.ds(which * unit, unit), at],
                held[which].at[:, :, at],
                sems.at[index * 3 + which],
            )
            for which in range(3)
        ]

    for index in range(len(cuts)):
        for copy in copies(index):
            copy.start()
    kept[...] = low[...]
    rows, depth = kept.shape[0] // parts, kept.shape[1]
    grads = jnp.concatenate([cot[block] for block in range(tp)], axis=1)
    for index, (first, size) in enumerate(cuts):
        for copy in copies(index):
            copy.wait()
        at = slice(first, first + size)
        gate_weight, up_weight, down_weight = [w[:, :, at].reshape(depth, size) for w in held]
        gate = dot(kept[...], gate_weight)
        up = dot(kept[...], up_weight)
        sigma = 1.0 / (1.0 + jnp.exp(-gate))
        active = gate * sigma
        hidden[:, at] = (active * up).astype(BF16)
        grad = dot(grads, down_weight)
        grad_gate[:, at] = (grad * up * sigma * (1.0 + gate * (1.0 - sigma))).astype(BF16)
        grad_up[:, at] = (grad * active).astype(BF16)
    gate_weight, up_weight, down_weight = [w[...].reshape(depth, w.shape[2]) for w in held]
    product = dot_turned(grad_gate[...], gate_weight) + dot_turned(grad_up[...], up_weight)
    for part in range(parts):
        partials[part][...] = product[part * rows : (part + 1) * rows].astype(BF16)
    values = dot_turned(hidden[...], down_weight)
    if first_one:
        values = values + mixed[...]
    for block in range(tp):
        out[block] = values[:, block * width : (block + 1) * width].astype(BF16)


def feed(low, cot, mixed, weights, step, tp, place, held, parts, *needed):
    rows, depth = low.shape
    part_rows = rows // parts
    blocks, triple, hidden = weights.shape
    cuts = []
    while sum(size for _, size in cuts) < hidden:
        first = sum(size for _, size in cuts)
        cuts.append((first, min(512, hidden - first)))
    by_owner = lambda columns: pl.BlockSpec(
        (rows, columns), lambda i, s: (lax.rem(s[0] - step + tp, tp), 0)
    )
    width = depth // tp
    blocks_of_owner = pl.BlockSpec(
        (tp, rows, width), lambda i, s: (0, lax.rem(s[0] - step + tp, tp), 0)
    )
    grid_spec = pltpu.PrefetchScalarGridSpec(
        num_scalar_prefetch=1,
        grid=(1,),
        in_specs=[whole((rows, depth)), blocks_of_owner, whole(mixed.shape)]
        + anywhere(1 + len(held) + len(needed)),
        out_specs=[by_owner(depth)]
        + [by_owner(hidden)] * 3
        + [blocks_of_owner]
        + [whole((part_rows, depth))] * parts,
        scratch_shapes=[pltpu.VMEM((blocks, triple // 3, hidden), BF16)] * 3
        + [pltpu.SemaphoreType.DMA((3 * len(cuts),))],
    )
    return pl.pallas_call(
        functools.partial(feed_kernel, tuple(cuts), parts, tp, step == 0),
        grid_spec=grid_spec,
        out_shape=[
            jax.ShapeDtypeStruct((tp * rows, columns), BF16)
            for columns in (depth, hidden, hidden, hidden)
        ]
        + [jax.ShapeDtypeStruct((tp, tp * rows, width), BF16)]
        + [jax.ShapeDtypeStruct((part_rows, depth), BF16)] * parts,
        input_output_aliases={5 + index: index for index in range(len(held))},
        compiler_params=params(),
        cost_estimate=takes(100),
        name="feed",
    )(place, low, cot, mixed, weights, *held, *needed)


def blame_halves(lefts, rights, place, unit, *needed, held=(), offset=0, total=None):
    rows, other = rights[0].shape
    picked = lefts[1].shape[1] // unit
    chosen = pl.BlockSpec((rows, unit), lambda j, s: (0, 2 * (j ^ s[3]) + s[1] % 2))
    if lefts[0].ndim == 3:
        per = lefts[0].shape[2] // unit
        chosen = pl.BlockSpec(
            (1, rows, unit),
            lambda j, s: (
                (2 * (j ^ s[3]) + s[1] % 2) // per,
                0,
                lax.rem(2 * (j ^ s[3]) + s[1] % 2, per),
            ),
        )
    cut = pl.BlockSpec((rows, unit), lambda j, s: (0, j ^ s[3]))
    shapes = [(2, unit // 2, total or other)] * 4

    def kernel(place, left_here, left_there, right_here, right_there, *refs):
        outs, spare, sems = refs[len(held) + len(needed) : -2], refs[-2], refs[-1]
        product = 0.0
        for left, right in ((left_here, right_here), (left_there, right_there)):
            ours = left[0] if len(left.shape) == 3 else left[...]
            product = product + lax.dot_general(
                ours, right[...], (((0,), (0,)), ((), ())), preferred_element_type=F32
            )
        product = product.astype(BF16)
        for j in range(picked):

            @pl.when(pl.program_id(0) == j)
            def _():
                first, second = spare.at[j // 2, j % 2], spare.at[2 + j % 2, j // 2]
                first[...], second[...] = product[: unit // 2], product[unit // 2 :]

        @pl.when(pl.program_id(0) == picked - 1)
        def _():
            moves = [
                pltpu.make_async_copy(
                    spare.at[index], out.at[:, :, pl.ds(offset, other)], sems.at[index]
                )
                for index, out in enumerate(outs)
            ]
            for move in moves:
                move.start()
            for move in moves:
                move.wait()

    grid_spec = pltpu.PrefetchScalarGridSpec(
        num_scalar_prefetch=1,
        grid=(picked,),
        in_specs=[chosen, cut]
        + [whole((rows, other))] * 2
        + anywhere(len(held) + len(needed)),
        out_specs=anywhere(4),
        scratch_shapes=[
            pltpu.VMEM((4, 2, unit // 2, other), BF16),
            pltpu.SemaphoreType.DMA((4,)),
        ],
    )
    place = jnp.concatenate([place, place[2:3] * 2 + place[1:2] // 2])
    return pl.pallas_call(
        kernel,
        grid_spec=grid_spec,
        out_shape=[jax.ShapeDtypeStruct(shape, BF16) for shape in shapes],
        input_output_aliases={5 + index: index for index in range(len(held))},
        compiler_params=params(),
        cost_estimate=takes(60),
        name="blame_halves",
    )(place, *lefts, *rights, *held, *needed)


def blame(left, right, *needed):
    rows, columns = left.shape
    if right.ndim == 3:
        steps, other = right.shape[0], right.shape[2]
        in_specs = [whole((rows, columns)), pl.BlockSpec((1, rows, other), lambda j: (j, 0, 0))]
        target, shape = pl.BlockSpec((columns, other), lambda j: (0, j)), (columns, steps * other)
    else:
        steps, other = 4, right.shape[1]
        in_specs = [pl.BlockSpec((rows, columns // steps), lambda j: (0, j)), whole((rows, other))]
        target, shape = pl.BlockSpec((columns // steps, other), lambda j: (j, 0)), (columns, other)

    def kernel(left, right, *refs):
        theirs = right[0] if len(right.shape) == 3 else right[...]
        refs[-1][...] = lax.dot_general(
            left[...], theirs, (((0,), (0,)), ((), ())), preferred_element_type=F32
        ).astype(BF16)

    return pl.pallas_call(
        kernel,
        grid=(steps,),
        in_specs=in_specs + anywhere(len(needed)),
        out_specs=target,
        out_shape=jax.ShapeDtypeStruct(shape, BF16),
        compiler_params=params(),
        cost_estimate=takes(60),
        name="blame",
    )(left, right, *needed)


def turn_kernel(nctx, count, parts, unit, place, *refs):
    arrived, own = refs[:parts], refs[parts : 2 * parts]
    mixed, cot, gain = refs[2 * parts : 2 * parts + 3]
    weight, refs = refs[2 * parts + 3], refs[2 * parts + 4 + count :]
    out, grad_mixed, grad_low, gain_grad, shift_grad, half = refs
    rows, depth = mixed.shape
    piece = out.shape[3]

    @pl.when(pl.program_id(0) == 0)
    def _():
        incoming = jnp.concatenate(
            [there[...].astype(F32) + here[...].astype(F32) for there, here in zip(arrived, own)]
        )
        values = mixed[...]
        values = values - jnp.mean(values, axis=1, keepdims=True)
        scaling = lax.rsqrt(jnp.mean(values * values, axis=1, keepdims=True) + EPSILON)
        normed = values * scaling
        shift_grad[...] = jnp.sum(incoming, axis=0, keepdims=True)
        gain_grad[...] = jnp.sum(incoming * normed, axis=0, keepdims=True)
        scaled = incoming * gain[...]
        grads = jnp.concatenate([cot[block] for block in range(cot.shape[0])], axis=1)
        total = grads.astype(F32) + scaling * (
            scaled
            - jnp.mean(scaled, axis=1, keepdims=True)
            - normed * jnp.mean(scaled * normed, axis=1, keepdims=True)
        )
        grad_mixed[...] = total
        grad_low[...] = total.astype(BF16)
        write_half(half, grad_low, 1 - lax.rem(place[1], 2), unit)

    product = dot(grad_low[...], weight[0])
    for c in range(nctx):
        out[c, 0] = product[:, c * piece : (c + 1) * piece].astype(BF16)


def turn(arrived, own, mixed, cot, gain, weight, place, nctx, tp, unit, *needed):
    rows, depth = mixed.shape
    parts = len(arrived)
    head_width = weight.shape[2]
    piece = head_width // nctx
    grid_spec = pltpu.PrefetchScalarGridSpec(
        num_scalar_prefetch=1,
        grid=(tp,),
        in_specs=[whole((rows // parts, depth))] * (2 * parts)
        + [whole((rows, depth))]
        + [
            pl.BlockSpec((tp, rows, depth // tp), lambda k, s: (0, s[0], 0)),
            whole((1, depth)),
            pl.BlockSpec((1, depth, head_width), lambda k, s: (k, 0, 0)),
        ]
        + anywhere(len(needed)),
        out_specs=[
            pl.BlockSpec((nctx, 1, rows, piece), lambda k, s: (0, k, 0, 0)),
            whole((rows, depth)),
            whole((rows, depth)),
            whole((1, depth)),
            whole((1, depth)),
            whole((rows, depth // 2)),
        ],
    )
    return pl.pallas_call(
        functools.partial(turn_kernel, nctx, len(needed), parts, unit),
        grid_spec=grid_spec,
        out_shape=[
            jax.ShapeDtypeStruct((nctx, tp, rows, piece), BF16),
            jax.ShapeDtypeStruct((rows, depth), F32),
            jax.ShapeDtypeStruct((rows, depth), BF16),
            jax.ShapeDtypeStruct((1, depth), F32),
            jax.ShapeDtypeStruct((1, depth), F32),
            jax.ShapeDtypeStruct((rows, depth // 2), BF16),
        ],
        compiler_params=params(),
        cost_estimate=takes(60),
        name="turn",
    )(place, *arrived, *own, mixed, cot, gain, weight, *needed)


def finish_kernel(nctx, tp, extra_count, place, *refs):
    pieces = refs[:nctx]
    cosine, sine_up, sine_down, full, extra, gain = refs[nctx : nctx + 6]
    weight, refs = refs[nctx + 6], refs[nctx + 7 + extra_count :]
    outs = refs[:tp]
    low, bias_grad, gain_grad, shift_grad, spare = refs[tp:]
    rows, wide = pieces[0].shape
    piece = wide // 3
    width = outs[0].shape[1]
    strip = spare.shape[0]
    extra_rows = extra.shape[0]

    @pl.when(pl.program_id(0) == 0)
    def _():
        bias_grad[...] = jnp.zeros_like(bias_grad)
        gain_grad[...] = jnp.zeros_like(gain_grad)
        shift_grad[...] = jnp.zeros_like(shift_grad)

    for step in range(nctx):
        source = jnp.bitwise_xor(place[1], step)
        for part in range(3):
            values = pieces[step][:, part * piece : (part + 1) * piece].astype(F32)
            if part < 2:
                values = (
                    values * cosine[...]
                    - pltpu.roll(values, piece - ROT // 2, 1) * sine_up[...]
                    - pltpu.roll(values, ROT // 2, 1) * sine_down[...]
                )
            columns = pl.ds(pl.multiple_of(source * wide + part * piece, piece), piece)
            bias_grad[:, columns] += jnp.sum(values, axis=0, keepdims=True)
            low[:, columns] = values.astype(BF16)

    incoming = dot_turned(low[...], weight[...])
    source = full[...].astype(F32)
    source = source - jnp.mean(source, axis=1, keepdims=True)
    scaling = lax.rsqrt(jnp.mean(source * source, axis=1, keepdims=True) + EPSILON)
    normed = source * scaling
    shift_grad[...] += jnp.sum(incoming, axis=0, keepdims=True)
    gain_grad[...] += jnp.sum(incoming * normed, axis=0, keepdims=True)
    scaled = incoming * gain[...]
    spare[...] = scaling * (
        scaled
        - jnp.mean(scaled, axis=1, keepdims=True)
        - normed * jnp.mean(scaled * normed, axis=1, keepdims=True)
    )
    first = pl.program_id(0) * strip
    wanted = place[0] * extra_rows

    if strip <= extra_rows:

        @pl.when((first >= wanted) & (first < wanted + extra_rows))
        def _():
            spare[...] += extra[pl.ds(pl.multiple_of(first - wanted, strip), strip), :]

    else:

        @pl.when((wanted >= first) & (wanted < first + strip))
        def _():
            spare[pl.ds(pl.multiple_of(wanted - first, extra_rows), extra_rows), :] += extra[...]

    for step, out in enumerate(outs):
        owner = lax.rem(place[0] - step + tp, tp)
        out[...] = spare[:, pl.ds(pl.multiple_of(owner * width, width), width)].astype(BF16)


def finish(pieces, place, tables, full, extra, gain, weight, tp, *needed):
    rows, wide = pieces[0].shape
    depth = full.shape[1]
    total = weight.shape[1]
    strip = 256
    steps = rows // strip
    width = depth // tp
    nctx = len(pieces)
    by_rows = lambda columns: pl.BlockSpec((strip, columns), lambda i, s: (i, 0))
    grid_spec = pltpu.PrefetchScalarGridSpec(
        num_scalar_prefetch=1,
        grid=(steps,),
        in_specs=[by_rows(wide)] * nctx
        + [by_rows(2 * HEAD_DIM)] * 3
        + [
            by_rows(depth),
            whole(extra.shape),
            whole((1, depth)),
        ]
        + [whole(weight.shape)]
        + anywhere(len(needed)),
        out_specs=[by_rows(width)] * tp
        + [
            by_rows(total),
            whole((1, total)),
            whole((1, depth)),
            whole((1, depth)),
        ],
        scratch_shapes=[pltpu.VMEM((strip, depth), F32)],
    )
    return pl.pallas_call(
        functools.partial(finish_kernel, nctx, tp, len(needed)),
        grid_spec=grid_spec,
        out_shape=[jax.ShapeDtypeStruct((rows, width), BF16)] * tp
        + [
            jax.ShapeDtypeStruct((rows, total), BF16),
            jax.ShapeDtypeStruct((1, total), F32),
            jax.ShapeDtypeStruct((1, depth), F32),
            jax.ShapeDtypeStruct((1, depth), F32),
        ],
        compiler_params=params(),
        cost_estimate=takes(70),
        name="finish",
    )(place, *pieces, *tables, full, extra, gain, weight, *needed)


def join(rings, place, unit):
    parts, tp = len(rings), len(rings[0])
    rows, width = rings[0][0].shape

    def kernel(place, *refs):
        for part in range(parts):
            for step in range(tp):
                owner = lax.rem(place[0] - step + tp, tp)
                refs[-2][owner, part * rows : (part + 1) * rows, :] = refs[part * tp + step][...]
        per, half = width // unit, 1 - lax.rem(place[1], 2)
        for block in range(tp * per // 2):
            index = 2 * block + half if unit % 128 == 0 else 0
            first = pl.multiple_of(lax.rem(index, per) * unit, unit)
            if unit % 128:
                first = 0
            refs[-1][:, block * unit : (block + 1) * unit] = refs[-2][
                lax.div(index, per), :, pl.ds(first, unit)
            ]

    grid_spec = pltpu.PrefetchScalarGridSpec(
        num_scalar_prefetch=1,
        grid=(1,),
        in_specs=[whole((rows, width))] * (parts * tp),
        out_specs=[whole((tp, parts * rows, width)), whole((parts * rows, tp * width // 2))],
    )
    return pl.pallas_call(
        kernel,
        grid_spec=grid_spec,
        out_shape=[
            jax.ShapeDtypeStruct((tp, parts * rows, width), BF16),
            jax.ShapeDtypeStruct((parts * rows, tp * width // 2), BF16),
        ],
        compiler_params=params(),
        cost_estimate=takes(10),
        name="join",
    )(place, *[block for blocks in rings for block in blocks])


def pack_kernel(gate, up, down, out):
    rows = gate.shape[0]
    out[:rows] = gate[...]
    out[rows : 2 * rows] = up[...]
    out[2 * rows :] = jnp.transpose(down[...])


def pack(gate, up, down):
    rows, columns = gate.shape
    return pl.pallas_call(
        pack_kernel,
        out_shape=jax.ShapeDtypeStruct((3 * rows, columns), BF16),
        compiler_params=params(),
        cost_estimate=takes(10),
        name="pack",
    )(gate, up, down)


def contract_rows(left, right):
    return lax.dot_general(left, right, (((0,), (0,)), ((), ())), preferred_element_type=F32)


def pick(stack, index):
    return lax.dynamic_index_in_dim(stack, index, 0, keepdims=False)


def shards(
    nfsdp,
    nctx,
    tp,
    inputs,
    cotangent,
    first_gain,
    first_bias,
    qkv_weight,
    qkv_bias,
    out_weight,
    second_gain,
    second_bias,
    gate_weight,
    up_weight,
    down_weight,
    lengths,
    fill_counts,
):
    data = ("fsdp", "ctx")
    ndata = nfsdp * nctx
    block_rows, width = inputs.shape
    depth = tp * width
    half_depth = depth // 2
    unit = depth // ndata
    tensor_index = lax.axis_index("tp").astype(jnp.int32)
    context_index = lax.axis_index("ctx").astype(jnp.int32)
    fsdp_index = lax.axis_index("fsdp").astype(jnp.int32)
    part_rows = block_rows // tp
    chunk_rows = block_rows // CHUNKS
    head_width = qkv_weight.shape[2]
    piece = head_width // nctx
    wide = 3 * piece

    square = nfsdp == 2 and nctx == 4 and unit % 128 == 0
    place = jnp.stack([tensor_index, context_index, fsdp_index])

    def shift(value, step):
        return lax.ppermute(value, "tp", [(i, (i + step) % tp) for i in range(tp)])

    def swap(value, step):
        return lax.ppermute(value, "ctx", [(i, i ^ step) for i in range(nctx)])

    core_index = context_index % 2
    groups = [list(range(0, ndata, 2)), list(range(1, ndata, 2))]
    def mate(value):
        return swap(value, 1)

    def send(here, near, far, *needed):
        far = swap(far, 2)
        return [here, swap(near, 1), far[0], swap(tie(far[1], *needed), 1)]

    def scatter_half(value, axis):
        return lax.psum_scatter(
            value, data, scatter_dimension=axis, tiled=True, axis_index_groups=groups
        )

    def scatter(value, axis):
        return lax.psum_scatter(value, data, scatter_dimension=axis, tiled=True)

    def cross(value):
        return lax.ppermute(value, "fsdp", [(i, i ^ 1) for i in range(nfsdp)])

    def square_once(parts):
        near, far, low, high = parts
        return total(near, cross(far)), total(low, swap(high, 2))

    def square_twice(first, second):
        first = first[0].astype(F32) + swap(first[1], 2).astype(F32)
        second = second[0].astype(F32) + cross(second[1]).astype(F32)
        return jnp.concatenate([first, second], axis=0)

    def total(left, right):
        return (left.astype(F32) + right.astype(F32)).astype(BF16)

    owners = [(tensor_index - step + tp) % tp for step in range(tp)]

    own_qkv = (
        qkv_weight.reshape(-1, 3, nctx, piece).transpose(0, 2, 1, 3).reshape(-1, 3 * head_width)
    )
    full_qkv = lax.all_gather(own_qkv, data, axis=0, tiled=True)
    own_feed = pack(gate_weight, up_weight, down_weight)
    feed_weights = lax.all_gather(own_feed, data, axis=0, tiled=True).reshape(ndata, 3 * unit, -1)

    validity, position, first_key, last_key = layout(lengths[0], fill_counts[0], block_rows)
    own_position = lax.dynamic_slice_in_dim(position, context_index * block_rows, block_rows, 0)
    tables = rotary_tables(own_position)
    bounds = jnp.stack([first_key, last_key])
    tile_first = first_key[::TILE_Q]
    tile_count = tile_first.shape[0]
    lows = jnp.where(validity[::TILE_Q], tile_first // TILE_K, tile_count * TILE_Q).astype(jnp.int32)
    key_block = jnp.arange(0, nctx * block_rows, TILE_K, dtype=jnp.int32) // block_rows
    ends = (
        key_block * block_rows
        + jnp.sum(
            jnp.where(
                key_block[:, None] == jnp.arange(nctx, dtype=jnp.int32)[None, :],
                fill_counts[0][None, :],
                0,
            ),
            axis=1,
        )
    ).astype(jnp.int32)

    flat_bias = qkv_bias.reshape(3, nctx, piece).transpose(1, 0, 2).reshape(1, -1)
    gain_one, bias_one = first_gain[None], first_bias[None]
    gain_two, bias_two = second_gain[None], second_bias[None]

    rings = [[inputs[c * chunk_rows : (c + 1) * chunk_rows]] for c in range(CHUNKS)]
    share = unit // CHUNKS
    for chunk in range(CHUNKS):
        carried = out_weight.T[chunk * share : (chunk + 1) * share]
        rings[chunk][0] = jnp.concatenate([rings[chunk][0], carried], axis=0)
    for chunk in range(CHUNKS):
        for _ in range(tp - 1):
            rings[chunk].append(shift(rings[chunk][-1], 1))
            if len(rings[chunk]) == 2:
                rings[chunk][-1] = tie(rings[chunk][-1], own_feed)
    all_low, full, low_half, *outgoing, stack = project(
        rings, place, gain_one, bias_one, full_qkv, flat_bias, tables, nctx, unit
    )
    full_out = lax.all_gather(stack, data, axis=1, tiled=True)

    cot = tie(cotangent, *[blocks[-1] for blocks in rings])
    cot_rings = [[cot[c * chunk_rows : (c + 1) * chunk_rows]] for c in range(CHUNKS)]
    for blocks in cot_rings:
        for _ in range(tp - 1):
            blocks.append(shift(blocks[-1], 1))
    pieces = send(*outgoing, *[blocks[max(tp - 2, 0)] for blocks in cot_rings])

    attended, outgoing, logs = attend(
        pieces,
        place[1:2],
        lows,
        ends,
        bounds,
        nctx,
        block_rows,
        feed_weights,
    )
    cot, cot_half = join(cot_rings, place, unit)
    arrived = lax.all_to_all(
        tie(outgoing, *[blocks[-1] for blocks in cot_rings]).reshape(nctx * tp, part_rows, piece),
        ("ctx", "tp"),
        split_axis=0,
        concat_axis=0,
        tiled=True,
    )
    returned, mixed, second_low = mix(
        arrived.reshape(nctx, tp, part_rows, piece),
        full_out,
        full,
        gain_two,
        bias_two,
        place,
        1,
    )

    arrived, held, partials, travelling = second_low, [], [], None
    for step in range(tp):
        coming = shift(arrived, 1) if step < tp - 1 else None
        needed = travelling if step == tp - 1 and step > 2 else []
        *held, first, second = feed(
            arrived, cot, mixed, feed_weights, step, tp, place, held, HALVES, *needed
        )
        partials.append([first, second])
        if step == 1 % tp:
            travelling = partials[step]
        elif step > 1:
            travelling = [
                total(shift(value, 1), kept) for value, kept in zip(travelling, partials[step])
            ]
        if step == 0 and coming is not None:
            coming = tie(coming, partials[0][0])
        arrived = coming
    all_second, all_gate, all_up, hidden, feedforward = held

    last = [shift(value, 1) for value in travelling]
    half_gate = blame(all_second, all_gate, *travelling)
    half_up = blame(all_second, all_up, *travelling)
    grad_heads, grad_mixed, mixed_low, gain_grad_two, shift_grad_two, mixed_half = turn(
        last,
        partials[0],
        mixed,
        cot,
        gain_two,
        full_out,
        place,
        nctx,
        tp,
        unit,
        half_gate,
        half_up,
    )
    grad_heads = lax.all_to_all(
        grad_heads.reshape(nctx * tp, part_rows, piece),
        ("ctx", "tp"),
        split_axis=0,
        concat_axis=0,
        tiled=True,
    ).reshape(nctx * block_rows, piece)

    total_gate = scatter(tie(half_gate, mixed_low), 0).astype(F32)
    total_up = scatter(tie(half_up, mixed_low), 0).astype(F32)
    half_out = blame(mixed_low, returned)
    total_out = scatter(tie(half_out, grad_heads), 0)

    feedforward = tie(feedforward, grad_heads)
    layer_out = [pick(feedforward, owners[1 % tp])]
    for step in range(1, tp):
        kept = pick(feedforward, owners[(step + 1) % tp])
        layer_out.append(total(shift(layer_out[-1], 1), kept))

    grad_pieces = attend_back(
        pieces, place[1:2], lows, ends, bounds, logs, grad_heads, attended, nctx, block_rows, half_out
    )
    arrived = send(*grad_pieces, *layer_out[max(tp - 2, 0) : tp - 1])
    layer_out = layer_out[-1]
    inner = hidden.shape[1]
    both = inner + 3 * head_width
    if square:
        parts = blame_halves(
            (cot, mate(cot_half)), (hidden, mate(hidden)), place, unit, arrived[2], total=both
        )
        half_down = parts[0]
    else:
        half_down = blame(hidden, cot)
        total_down = scatter(half_down, 1).astype(F32)
    low_halves = mate(low_half) if square else low_half
    needed = [layer_out, low_halves, half_down]
    *partial, all_grad, bias_grad, gain_grad, shift_grad = finish(
        arrived, place, tables, full, grad_mixed, gain_one, full_qkv, tp, *needed
    )
    if square:
        parts = blame_halves(
            (all_low, low_halves),
            (all_grad, mate(all_grad)),
            place,
            unit,
            held=parts,
            offset=inner,
            total=both,
        )
    else:
        parts = []
    def exchange(value, axis, steps, size):
        for step in steps:
            value = value + lax.ppermute(value, axis, [(i, i ^ step) for i in range(size)])
        return value

    def powers(first, size):
        return [1 << bit for bit in range(first, size.bit_length() - 1)]

    small = jnp.concatenate([gain_grad, shift_grad, gain_grad_two, shift_grad_two], axis=1)
    small = sum([shift(small, step) for step in range(1, tp)], small)
    small = jnp.concatenate([bias_grad, small], axis=1)
    travelling, ring_steps = partial[1 % tp], []
    once = square_once(parts) if square else ()
    needed = [[total_gate, total_up, small, *parts], [*once], []]
    for step in range(1, tp):
        travelling = add(
            shift(travelling, 1), partial[(step + 1) % tp], *(needed[step - 1] if step < 4 else [])
        )
        ring_steps.append(travelling)
        if step < 3:
            bits = powers(0, min(nctx, 2)) if step == 1 else powers(1, nctx)
            small = exchange(tie(small, travelling), "ctx", bits, nctx)
            needed[step].append(small)
    small = exchange(tie(small, travelling), "fsdp", powers(0, nfsdp), nfsdp)
    grad_inputs = travelling
    if square:
        totals = square_twice(*once)
        total_down, total_qkv = totals[:, :inner].T, totals[:, inner:]
    else:
        total_qkv = scatter(blame(all_low, all_grad), 0).astype(F32)

    total_qkv = (
        total_qkv
        .reshape(-1, nctx, 3, piece)
        .transpose(0, 2, 1, 3)
        .reshape(-1, 3, head_width)
    )

    out_parts = jnp.swapaxes(
        tie(total_out, *ring_steps[:1]).reshape(-1, tp, head_width), 0, 1
    )
    total_out = pick(out_parts, tensor_index).astype(F32)
    for step in range(1, tp):
        total_out = total_out + shift(pick(out_parts, (tensor_index + step) % tp), step).astype(F32)
    total_out = total_out.T

    bias_total, small = small[:, : 3 * head_width], small[:, 3 * head_width :]
    bias_total = bias_total.reshape(nctx, 3, piece).transpose(1, 0, 2).reshape(3, head_width)
    small = small.reshape(4, depth)
    return (
        layer_out,
        grad_inputs,
        small[0],
        small[1],
        total_qkv,
        bias_total,
        total_out,
        small[2],
        small[3],
        total_gate,
        total_up,
        total_down,
    )


def solution(mesh):
    data = ("fsdp", "ctx")
    by_rows = P(data, "tp")
    by_columns = P("tp", data)
    qkv = P(data, None, "tp")
    return jax.shard_map(
        functools.partial(shards, mesh.shape["fsdp"], mesh.shape["ctx"], mesh.shape["tp"]),
        mesh=mesh,
        in_specs=(
            by_rows,
            by_rows,
            P(),
            P(),
            qkv,
            P(None, "tp"),
            by_columns,
            P(),
            P(),
            by_rows,
            by_rows,
            by_columns,
            P("fsdp", None),
            P("fsdp", None),
        ),
        out_specs=(
            by_rows,
            by_rows,
            P(),
            P(),
            qkv,
            P(None, "tp"),
            by_columns,
            P(),
            P(),
            by_rows,
            by_rows,
            by_columns,
        ),
        check_vma=False,
    )
```

```python
import functools

import jax
import jax.numpy as jnp
from jax import lax
from jax.experimental import pallas as pl
from jax.experimental.pallas import tpu as pltpu
from jax.sharding import PartitionSpec as P

HEAD_DIM = 64
ROT = 16
EPSILON = 1e-05
NEGATIVE = -1e30
FLOOR = -1e20
VMEM_LIMIT = 56 * 1024 * 1024
TILE_Q = 512
TILE_K = 512
STRIP = 32
CHUNKS = 2
HALVES = 2

F32 = jnp.float32
BF16 = jnp.bfloat16


def layout(lengths, fill_counts, block_rows):
    blocks_count = fill_counts.shape[0]
    seq_count = lengths.shape[0]
    slot_index = jnp.arange(blocks_count * block_rows, dtype=jnp.int32)
    block_of = slot_index // block_rows
    within = slot_index - block_of * block_rows
    chooser = block_of[:, None] == jnp.arange(blocks_count, dtype=jnp.int32)[None, :]
    fill_here = jnp.sum(jnp.where(chooser, fill_counts[None, :], 0), axis=1)
    before = jnp.cumsum(fill_counts) - fill_counts
    before_here = jnp.sum(jnp.where(chooser, before[None, :], 0), axis=1)
    validity = within < fill_here
    used_index = before_here + within
    seq_ends = jnp.cumsum(lengths)
    sequence = jnp.sum((used_index[:, None] >= seq_ends[None, :]).astype(jnp.int32), axis=1)
    seq_starts = seq_ends - lengths
    picker = sequence[:, None] == jnp.arange(seq_count, dtype=jnp.int32)[None, :]
    start_here = jnp.sum(jnp.where(picker, seq_starts[None, :], 0), axis=1)
    after = before + fill_counts
    start_block = jnp.sum((seq_starts[:, None] >= after[None, :]).astype(jnp.int32), axis=1)
    start_block = jnp.minimum(start_block, blocks_count - 1)
    block_pick = start_block[:, None] == jnp.arange(blocks_count, dtype=jnp.int32)[None, :]
    start_before = jnp.sum(jnp.where(block_pick, before[None, :], 0), axis=1)
    start_slot = start_block * block_rows + seq_starts - start_before
    slot_here = jnp.sum(jnp.where(picker, start_slot[None, :], 0), axis=1)
    first_key = jnp.where(validity, slot_here, 0).astype(jnp.int32)
    last_key = jnp.where(validity, slot_index, -1).astype(jnp.int32)
    return (validity, used_index - start_here, first_key, last_key)


def rotary_tables(position):
    half = ROT // 2
    lane = jnp.arange(2 * HEAD_DIM, dtype=jnp.int32) % HEAD_DIM
    frequency = 10000.0 ** (-(2.0 * (lane % half).astype(F32)) / ROT)
    angles = position.astype(F32)[:, None] * frequency[None, :]
    cosine, sine = jnp.cos(angles), jnp.sin(angles)
    lane = lane[None, :]
    return (
        jnp.where(lane < ROT, cosine, 1.0),
        jnp.where(lane < half, -sine, 0.0),
        jnp.where((lane >= half) & (lane < ROT), sine, 0.0),
    )


def params(**extra):
    return pltpu.CompilerParams(vmem_limit_bytes=VMEM_LIMIT, **extra)


def takes(microseconds):
    return pl.CostEstimate(
        flops=int(microseconds * 1e8), bytes_accessed=0, transcendentals=0
    )


def whole(shape):
    return pl.BlockSpec(shape, lambda *_: (0,) * len(shape))


def anywhere(count):
    return [pl.BlockSpec(memory_space=pl.ANY)] * count


def write_half(out, values, half, unit):
    if unit % 128:
        out[...] = values[:, : out.shape[1]]
        return
    for block in range(out.shape[1] // unit):
        first = pl.multiple_of((2 * block + half) * unit, unit)
        out[:, block * unit : (block + 1) * unit] = values[:, pl.ds(first, unit)]


def dot(left, right):
    return jnp.dot(left, right, preferred_element_type=F32)


def dot_turned(left, right):
    return lax.dot_general(left, right, (((1,), (1,)), ((), ())), preferred_element_type=F32)


def tie(value, *needed):
    def kernel(*refs):
        del refs

    return pl.pallas_call(
        kernel,
        in_specs=anywhere(1 + len(needed)),
        out_specs=pl.BlockSpec(memory_space=pl.ANY),
        out_shape=jax.ShapeDtypeStruct(value.shape, value.dtype),
        input_output_aliases={0: 0},
        name="tie",
    )(value, *needed)


def add_kernel(left, right, *refs):
    refs[-1][...] = (left[...].astype(F32) + right[...].astype(F32)).astype(BF16)


def add(left, right, *needed):
    rows, columns = left.shape
    strip = min(rows, 512)
    block = pl.BlockSpec((strip, columns), lambda i: (i, 0))
    return pl.pallas_call(
        add_kernel,
        grid=(rows // strip,),
        in_specs=[block, block] + anywhere(len(needed)),
        out_specs=block,
        out_shape=jax.ShapeDtypeStruct(left.shape, BF16),
        compiler_params=params(),
        cost_estimate=takes(10),
        name="ring_add",
    )(left, right, *needed)


def project_kernel(tp, chunks, per, unit, place, *refs):
    rings, refs = refs[: tp * chunks], refs[tp * chunks :]
    gain, bias, weight, weight_bias, cosine, sine_up, sine_down = refs[:7]
    low, full, half, here, near, far, stack = refs[7:]
    outs = [here, near] + [far.at[way] for way in range(far.shape[0])]
    rows, width = low.shape[0] // chunks, rings[0].shape[1]
    depth = tp * width
    wide = here.shape[1]
    piece = wide // 3
    step = pl.program_id(0)

    @pl.when(pl.program_id(0) == 0)
    def _():
        strip = 128
        for start in range(0, rows * chunks, strip):
            chunk, first = start // rows, start % rows
            blocks = rings[chunk * tp : (chunk + 1) * tp]
            at = slice(start, start + strip)
            inner = slice(first, first + strip)
            parts = [block[inner, :].astype(F32) for block in blocks]
            centre = sum(jnp.sum(part, axis=1, keepdims=True) for part in parts) / depth
            parts = [part - centre for part in parts]
            spread = sum(jnp.sum(part * part, axis=1, keepdims=True) for part in parts) / depth
            scaling = lax.rsqrt(spread + EPSILON)
            for step in range(tp):
                owner = lax.rem(place[0] - step + tp, tp)
                columns = pl.ds(pl.multiple_of(owner * width, width), width)
                low[at, columns] = (
                    parts[step] * scaling * gain[:, columns] + bias[:, columns]
                ).astype(BF16)
                full[at, columns] = blocks[step][inner, :]
        write_half(half, low, 1 - lax.rem(place[1], 2), unit)
        share = rings[0].shape[0] - rows
        for chunk in range(chunks):
            for step in range(tp):
                owner = lax.rem(place[0] - step + tp, tp)
                stack[owner, chunk * share : (chunk + 1) * share, :] = rings[chunk * tp + step][
                    rows:, :
                ]

    product = dot(low[...], weight[...]) + weight_bias[...]
    groups = []
    for group in range(per):
        parts = []
        for part in range(3):
            first = (group * 3 + part) * piece
            values = product[:, first : first + piece]
            if part < 2:
                values = (
                    values * cosine[...]
                    + pltpu.roll(values, piece - ROT // 2, 1) * sine_up[...]
                    + pltpu.roll(values, ROT // 2, 1) * sine_down[...]
                )
            parts.append(values.astype(BF16))
        groups.append(parts)
    flip = lax.rem(place[1], per)
    for way, out in enumerate(outs):
        for group in range(per):

            @pl.when((step == way // per) & (jnp.bitwise_xor(group, flip) == way % per))
            def _():
                for part in range(3):
                    out[:, part * piece : (part + 1) * piece] = groups[group][part]


def project(rings, place, gain, bias, weight, weight_bias, tables, nctx, unit):
    chunks, tp = len(rings), len(rings[0])
    rows, width = tables[0].shape[0], rings[0][0].shape[1]
    depth = tp * width
    total = weight.shape[1]
    wide = total // nctx
    per = 2 if nctx % 2 == 0 else 1
    grid_spec = pltpu.PrefetchScalarGridSpec(
        num_scalar_prefetch=1,
        grid=(nctx // per,),
        in_specs=[whole(rings[0][0].shape)] * (tp * chunks)
        + [whole((1, depth))] * 2
        + [
            pl.BlockSpec((depth, per * wide), lambda i, s: (0, jnp.bitwise_xor(i, s[1] // per))),
            pl.BlockSpec((1, per * wide), lambda i, s: (0, jnp.bitwise_xor(i, s[1] // per))),
        ]
        + [whole((rows, 2 * HEAD_DIM))] * 3,
        out_specs=[whole((rows, depth))] * 2
        + [whole((rows, depth // 2))]
        + [whole((rows, wide))] * 2
        + [whole((nctx - 2, rows, wide)), whole((tp, unit, width))],
    )
    return pl.pallas_call(
        functools.partial(project_kernel, tp, chunks, per, unit),
        grid_spec=grid_spec,
        out_shape=[
            jax.ShapeDtypeStruct((rows, depth), BF16),
            jax.ShapeDtypeStruct((rows, depth), BF16),
            jax.ShapeDtypeStruct((rows, depth // 2), BF16),
        ]
        + [jax.ShapeDtypeStruct((rows, wide), BF16)] * 2
        + [
            jax.ShapeDtypeStruct((nctx - 2, rows, wide), BF16),
            jax.ShapeDtypeStruct((tp, unit, width), BF16),
        ],
        compiler_params=params(),
        cost_estimate=takes(60),
        name="project",
    )(
        place,
        *[block for blocks in rings for block in blocks],
        gain,
        bias,
        weight,
        weight_bias,
        *tables,
    )


def stack_heads(tile, heads):
    lane = lax.broadcasted_iota(jnp.int32, tile.shape, 1) // HEAD_DIM
    return jnp.concatenate(
        [jnp.where(lane == head, tile, jnp.zeros_like(tile)) for head in range(heads)], axis=0
    )


def load_pieces(place, pieces, nctx, held, block_rows):
    chunk_rows = pieces[0].shape[0]
    chunks = len(pieces) // nctx
    for chunk in range(chunks):
        for step in range(nctx):
            source = jnp.bitwise_xor(place, step)
            first = source * block_rows + chunk * chunk_rows
            held[pl.ds(pl.multiple_of(first, chunk_rows), chunk_rows), :] = pieces[
                chunk * nctx + step
            ][...]


def attend_kernel(nctx, heads, count, extra, block_rows, place, lows, ends, bounds, *refs):
    pieces = refs[:count]
    out, sent, logs, held, turned, total, high, sums, raw, chances = refs[count + extra :]
    tile_q, tile_k = out.shape[0], turned.shape[2]
    width = heads * HEAD_DIM
    index = pl.program_id(0)

    @pl.when(index == 0)
    def _():
        load_pieces(place[0], pieces, nctx, held, block_rows)
        for tile in range(turned.shape[0]):
            turned[tile] = jnp.transpose(held[tile * tile_k : (tile + 1) * tile_k, 2 * width :])

    query_rows = pl.ds(pl.multiple_of(index * tile_q, tile_q), tile_q)
    queries = stack_heads(held[query_rows, :width] * jnp.asarray(HEAD_DIM**-0.5, BF16), heads)
    total[...] = jnp.zeros_like(total)
    high[...] = jnp.full_like(high, FLOOR)
    sums[...] = jnp.zeros_like(sums)
    first_key, last_key = bounds[0:1, :], bounds[1:2, :]

    def one(tile, _):
        start = tile * tile_k
        keys = held[pl.ds(pl.multiple_of(start, tile_k), tile_k), width : 2 * width]
        last = jnp.minimum(last_key, ends[tile] - 1) - start
        first = first_key - start
        for head in range(heads):
            raw[head] = dot_turned(keys, queries[head * tile_q : (head + 1) * tile_q])
        for head in range(heads):
            peaks = jnp.broadcast_to(high[head], (8, tile_q))
            for begin in range(0, tile_k, STRIP):
                scores = raw[head, begin : begin + STRIP, :]
                row = lax.broadcasted_iota(jnp.int32, scores.shape, 0) + begin
                scores = jnp.where((row <= last) & (row >= first), scores, NEGATIVE)
                raw[head, begin : begin + STRIP, :] = scores
                for group in range(0, STRIP, 8):
                    peaks = jnp.maximum(peaks, scores[group : group + 8])
            highest = jnp.max(peaks, axis=0, keepdims=True)
            partial = jnp.zeros((8, tile_q), F32)
            for begin in range(0, tile_k, STRIP):
                raised = jnp.exp(raw[head, begin : begin + STRIP, :] - highest)
                chances[head, begin : begin + STRIP, :] = raised.astype(BF16)
                for group in range(0, STRIP, 8):
                    partial = partial + raised[group : group + 8]
            shrink = jnp.exp(high[head] - highest)
            sums[head] = sums[head] * shrink + jnp.sum(partial, axis=0, keepdims=True)
            values = turned[tile, head * HEAD_DIM : (head + 1) * HEAD_DIM, :]
            total[head] = total[head] * shrink + dot(values, chances[head])
            high[head] = highest
        return 0

    upper = (index * tile_q + tile_q - 1) // tile_k + 1
    lax.fori_loop(lows[index], upper, one, 0)
    results = []
    for head in range(heads):
        found = sums[head] > 0.0
        safe = jnp.where(found, sums[head], 1.0)
        results.append(total[head] * jnp.where(found, 1.0 / safe, 0.0))
        logs[head : head + 1, :] = jnp.where(found, high[head] + jnp.log(safe), 0.0)
    result = jnp.transpose(jnp.concatenate(results, axis=0)).astype(BF16)
    out[...] = result
    sent[...] = result


def attend(pieces, place, lows, ends, bounds, nctx, block_rows, *needed):
    total_rows = nctx * block_rows
    width = pieces[0].shape[1] // 3
    heads = width // HEAD_DIM
    steps = total_rows // TILE_Q
    grid_spec = pltpu.PrefetchScalarGridSpec(
        num_scalar_prefetch=3,
        grid=(steps,),
        in_specs=[pl.BlockSpec((2, TILE_Q), lambda i, *_: (0, i))]
        + [whole(piece.shape) for piece in pieces]
        + anywhere(len(needed)),
        out_specs=[
            pl.BlockSpec((TILE_Q, width), lambda i, *_: (i, 0)),
            pl.BlockSpec((TILE_Q, width), lambda i, *_: (i, 0)),
            pl.BlockSpec((heads, TILE_Q), lambda i, *_: (0, i)),
        ],
        scratch_shapes=[
            pltpu.VMEM((total_rows, 3 * width), BF16),
            pltpu.VMEM((total_rows // TILE_K, width, TILE_K), BF16),
            pltpu.VMEM((heads, HEAD_DIM, TILE_Q), F32),
            pltpu.VMEM((heads, 1, TILE_Q), F32),
            pltpu.VMEM((heads, 1, TILE_Q), F32),
            pltpu.VMEM((heads, TILE_K, TILE_Q), F32),
            pltpu.VMEM((heads, TILE_K, TILE_Q), BF16),
        ],
    )
    return pl.pallas_call(
        functools.partial(attend_kernel, nctx, heads, len(pieces), len(needed), block_rows),
        grid_spec=grid_spec,
        out_shape=[
            jax.ShapeDtypeStruct((total_rows, width), BF16),
            jax.ShapeDtypeStruct((total_rows, width), BF16),
            jax.ShapeDtypeStruct((heads, total_rows), F32),
        ],
        compiler_params=params(),
        cost_estimate=takes(200),
        name="attend",
    )(place, lows, ends, bounds, *pieces, *needed)


def attend_back_kernel(
    nctx, heads, count, extra, block_rows, place, lows, ends, bounds, logs, *refs
):
    pieces, refs = refs[:count], refs[count:]
    grad, attended, refs = refs[0], refs[1], refs[2 + extra :]
    here, near, far, refs = *refs[:3], refs[3:]
    held, turned, grad_keys, grad_values, grad_query, raw, raw_grad, chances, steps, merged = refs
    tile_q, tile_k = grad.shape[0], turned.shape[2]
    width = grad.shape[1]
    index = pl.program_id(0)
    scale = jnp.asarray(HEAD_DIM**-0.5, BF16)

    @pl.when(index == 0)
    def _():
        load_pieces(place[0], pieces, nctx, held, block_rows)
        for tile in range(turned.shape[0]):
            turned[tile] = jnp.transpose(
                held[tile * tile_k : (tile + 1) * tile_k, width : 2 * width]
            )
        grad_keys[...] = jnp.zeros_like(grad_keys)
        grad_values[...] = jnp.zeros_like(grad_values)

    query_rows = pl.ds(pl.multiple_of(index * tile_q, tile_q), tile_q)
    queries = stack_heads(held[query_rows, :width] * scale, heads)
    incoming = stack_heads(grad[...], heads)
    product = jnp.transpose(grad[...].astype(F32) * attended[...].astype(F32))
    centres = [
        jnp.sum(product[head * HEAD_DIM : (head + 1) * HEAD_DIM, :], axis=0, keepdims=True)
        for head in range(heads)
    ]
    first_key, last_key = bounds[0:1, :], bounds[1:2, :]
    grad_query[...] = jnp.zeros_like(grad_query)

    def one(tile, _):
        start = tile * tile_k
        key_rows = pl.ds(pl.multiple_of(start, tile_k), tile_k)
        last = jnp.minimum(last_key, ends[tile] - 1) - start
        first = first_key - start
        by_head = [slice(head * tile_q, (head + 1) * tile_q) for head in range(heads)]
        for head in range(heads):
            raw[head] = dot_turned(held[key_rows, width : 2 * width], queries[by_head[head]])
            raw_grad[head] = dot_turned(held[key_rows, 2 * width :], incoming[by_head[head]])
        for head in range(heads):
            for begin in range(0, tile_k, STRIP):
                at = slice(begin, begin + STRIP)
                row = lax.broadcasted_iota(jnp.int32, (STRIP, tile_q), 0) + begin
                allowed = (row <= last) & (row >= first)
                scores = raw[head, at, :] - logs[head : head + 1, :]
                chance = jnp.exp(jnp.where(allowed, scores, NEGATIVE))
                chances[head, at, :] = chance.astype(BF16)
                steps[head, at, :] = (chance * (raw_grad[head, at, :] - centres[head])).astype(BF16)
            grad_values[key_rows, :] += dot(chances[head], incoming[by_head[head]])
            grad_keys[key_rows, :] += dot(steps[head], queries[by_head[head]])
            keys = turned[tile, head * HEAD_DIM : (head + 1) * HEAD_DIM, :]
            grad_query[head] += dot(keys, steps[head])
        return 0

    upper = (index * tile_q + tile_q - 1) // tile_k + 1
    lax.fori_loop(lows[index], upper, one, 0)
    result = jnp.concatenate([grad_query[head] for head in range(heads)], axis=0)
    merged[query_rows, :width] = (jnp.transpose(result) * HEAD_DIM**-0.5).astype(BF16)

    @pl.when(index == pl.num_programs(0) - 1)
    def _():
        merged[:, width : 2 * width] = grad_keys[...].astype(BF16)
        merged[:, 2 * width :] = grad_values[...].astype(BF16)
        outs = [here, near] + [far.at[way] for way in range(nctx - 2)]
        for way, out in enumerate(outs):
            first = jnp.bitwise_xor(place[0], way) * block_rows
            out[...] = merged[pl.ds(pl.multiple_of(first, block_rows), block_rows), :]


def attend_back(pieces, place, lows, ends, bounds, logs, grad, attended, nctx, block_rows, *needed):
    total_rows, width = grad.shape
    heads = width // HEAD_DIM
    by_tile = pl.BlockSpec((TILE_Q, width), lambda i, *_: (i, 0))
    sent = (block_rows, 3 * width)
    sent = [sent, sent, (nctx - 2, *sent)]
    grid_spec = pltpu.PrefetchScalarGridSpec(
        num_scalar_prefetch=3,
        grid=(total_rows // TILE_Q,),
        in_specs=[
            pl.BlockSpec((2, TILE_Q), lambda i, *_: (0, i)),
            pl.BlockSpec((heads, TILE_Q), lambda i, *_: (0, i)),
        ]
        + [whole(piece.shape) for piece in pieces]
        + [by_tile] * 2
        + anywhere(len(needed)),
        out_specs=[whole(shape) for shape in sent],
        scratch_shapes=[
            pltpu.VMEM((total_rows, 3 * width), BF16),
            pltpu.VMEM((total_rows // TILE_K, width, TILE_K), BF16),
            pltpu.VMEM((total_rows, width), F32),
            pltpu.VMEM((total_rows, width), F32),
            pltpu.VMEM((heads, HEAD_DIM, TILE_Q), F32),
            pltpu.VMEM((heads, TILE_K, TILE_Q), F32),
            pltpu.VMEM((heads, TILE_K, TILE_Q), F32),
            pltpu.VMEM((heads, TILE_K, TILE_Q), BF16),
            pltpu.VMEM((heads, TILE_K, TILE_Q), BF16),
            pltpu.VMEM((total_rows, 3 * width), BF16),
        ],
    )
    return pl.pallas_call(
        functools.partial(
            attend_back_kernel, nctx, heads, len(pieces), len(needed), block_rows
        ),
        grid_spec=grid_spec,
        out_shape=[jax.ShapeDtypeStruct(shape, BF16) for shape in sent],
        compiler_params=params(),
        cost_estimate=takes(250),
        name="attend_back",
    )(place, lows, ends, bounds, logs, *pieces, grad, attended, *needed)


def mix_kernel(nctx, count, place, heads_in, weight, source, gain, bias, *refs):
    returned, mixed, *lows = refs[count:]
    rows, depth = mixed.shape
    step = pl.program_id(0)
    left = jnp.concatenate([heads_in[c, 0] for c in range(nctx)], axis=1)
    returned[...] = left

    @pl.when(step == 0)
    def _():
        mixed[...] = source[...].astype(F32)

    mixed[...] += dot_turned(left, weight[0])

    @pl.when(step == pl.num_programs(0) - 1)
    def _():
        values = mixed[...]
        values = values - jnp.mean(values, axis=1, keepdims=True)
        scaling = lax.rsqrt(jnp.mean(values * values, axis=1, keepdims=True) + EPSILON)
        values = (values * scaling * gain[...] + bias[...]).astype(BF16)
        part_rows = lows[0].shape[0]
        for part, low in enumerate(lows):
            low[...] = values[part * part_rows : (part + 1) * part_rows]


def mix(heads_in, weight, full, gain, bias, place, parts, *needed):
    nctx, tp, rows, piece = heads_in.shape
    depth = full.shape[1]
    head_width = nctx * piece
    grid_spec = pltpu.PrefetchScalarGridSpec(
        num_scalar_prefetch=1,
        grid=(tp,),
        in_specs=[
            pl.BlockSpec((nctx, 1, rows, piece), lambda k, s: (0, k, 0, 0)),
            pl.BlockSpec((1, depth, head_width), lambda k, s: (k, 0, 0)),
            pl.BlockSpec((rows, depth), lambda k, s: (s[0], 0)),
            whole((1, depth)),
            whole((1, depth)),
        ]
        + anywhere(len(needed)),
        out_specs=[
            pl.BlockSpec((rows, head_width), lambda k, s: (0, k)),
            whole((rows, depth)),
        ]
        + [whole((rows // parts, depth))] * parts,
    )
    return pl.pallas_call(
        functools.partial(mix_kernel, nctx, len(needed)),
        grid_spec=grid_spec,
        out_shape=[
            jax.ShapeDtypeStruct((rows, tp * head_width), BF16),
            jax.ShapeDtypeStruct((rows, depth), F32),
        ]
        + [jax.ShapeDtypeStruct((rows // parts, depth), BF16)] * parts,
        compiler_params=params(),
        cost_estimate=takes(50),
        name="mix",
    )(place, heads_in, weight, full, gain, bias, *needed)


def feed_kernel(cuts, parts, tp, first_one, place, low, cot, mixed, source, *refs):
    refs = refs[-(5 + parts + 4) :]
    kept, grad_gate, grad_up, hidden, out = refs[:5]
    partials, held, sems = refs[5 : 5 + parts], refs[-4:-1], refs[-1]
    unit = source.shape[1] // 3
    width = out.shape[2]

    def copies(index):
        first, size = cuts[index]
        at = pl.ds(first, size)
        return [
            pltpu.make_async_copy(
                source.at[:, pl.ds(which * unit, unit), at],
                held[which].at[:, :, at],
                sems.at[index * 3 + which],
            )
            for which in range(3)
        ]

    for index in range(len(cuts)):
        for copy in copies(index):
            copy.start()
    kept[...] = low[...]
    rows, depth = kept.shape[0] // parts, kept.shape[1]
    grads = jnp.concatenate([cot[block] for block in range(tp)], axis=1)
    for index, (first, size) in enumerate(cuts):
        for copy in copies(index):
            copy.wait()
        at = slice(first, first + size)
        gate_weight, up_weight, down_weight = [w[:, :, at].reshape(depth, size) for w in held]
        gate = dot(kept[...], gate_weight)
        up = dot(kept[...], up_weight)
        sigma = 1.0 / (1.0 + jnp.exp(-gate))
        active = gate * sigma
        hidden[:, at] = (active * up).astype(BF16)
        grad = dot(grads, down_weight)
        grad_gate[:, at] = (grad * up * sigma * (1.0 + gate * (1.0 - sigma))).astype(BF16)
        grad_up[:, at] = (grad * active).astype(BF16)
    gate_weight, up_weight, down_weight = [w[...].reshape(depth, w.shape[2]) for w in held]
    product = dot_turned(grad_gate[...], gate_weight) + dot_turned(grad_up[...], up_weight)
    for part in range(parts):
        partials[part][...] = product[part * rows : (part + 1) * rows].astype(BF16)
    values = dot_turned(hidden[...], down_weight)
    if first_one:
        values = values + mixed[...]
    for block in range(tp):
        out[block] = values[:, block * width : (block + 1) * width].astype(BF16)


def feed(low, cot, mixed, weights, step, tp, place, held, parts, *needed):
    rows, depth = low.shape
    part_rows = rows // parts
    blocks, triple, hidden = weights.shape
    cuts = []
    while sum(size for _, size in cuts) < hidden:
        first = sum(size for _, size in cuts)
        cuts.append((first, min(512, hidden - first)))
    by_owner = lambda columns: pl.BlockSpec(
        (rows, columns), lambda i, s: (lax.rem(s[0] - step + tp, tp), 0)
    )
    width = depth // tp
    blocks_of_owner = pl.BlockSpec(
        (tp, rows, width), lambda i, s: (0, lax.rem(s[0] - step + tp, tp), 0)
    )
    grid_spec = pltpu.PrefetchScalarGridSpec(
        num_scalar_prefetch=1,
        grid=(1,),
        in_specs=[whole((rows, depth)), blocks_of_owner, whole(mixed.shape)]
        + anywhere(1 + len(held) + len(needed)),
        out_specs=[by_owner(depth)]
        + [by_owner(hidden)] * 3
        + [blocks_of_owner]
        + [whole((part_rows, depth))] * parts,
        scratch_shapes=[pltpu.VMEM((blocks, triple // 3, hidden), BF16)] * 3
        + [pltpu.SemaphoreType.DMA((3 * len(cuts),))],
    )
    return pl.pallas_call(
        functools.partial(feed_kernel, tuple(cuts), parts, tp, step == 0),
        grid_spec=grid_spec,
        out_shape=[
            jax.ShapeDtypeStruct((tp * rows, columns), BF16)
            for columns in (depth, hidden, hidden, hidden)
        ]
        + [jax.ShapeDtypeStruct((tp, tp * rows, width), BF16)]
        + [jax.ShapeDtypeStruct((part_rows, depth), BF16)] * parts,
        input_output_aliases={5 + index: index for index in range(len(held))},
        compiler_params=params(),
        cost_estimate=takes(100),
        name="feed",
    )(place, low, cot, mixed, weights, *held, *needed)


def blame_halves(lefts, rights, place, unit, *needed, held=(), offset=0, total=None):
    rows, other = rights[0].shape
    picked = lefts[1].shape[1] // unit
    chosen = pl.BlockSpec((rows, unit), lambda j, s: (0, 2 * (j ^ s[3]) + s[1] % 2))
    if lefts[0].ndim == 3:
        per = lefts[0].shape[2] // unit
        chosen = pl.BlockSpec(
            (1, rows, unit),
            lambda j, s: (
                (2 * (j ^ s[3]) + s[1] % 2) // per,
                0,
                lax.rem(2 * (j ^ s[3]) + s[1] % 2, per),
            ),
        )
    cut = pl.BlockSpec((rows, unit), lambda j, s: (0, j ^ s[3]))
    shapes = [(2, unit // 2, total or other)] * 4

    def kernel(place, left_here, left_there, right_here, right_there, *refs):
        outs, spare, sems = refs[len(held) + len(needed) : -2], refs[-2], refs[-1]
        product = 0.0
        for left, right in ((left_here, right_here), (left_there, right_there)):
            ours = left[0] if len(left.shape) == 3 else left[...]
            product = product + lax.dot_general(
                ours, right[...], (((0,), (0,)), ((), ())), preferred_element_type=F32
            )
        product = product.astype(BF16)
        for j in range(picked):

            @pl.when(pl.program_id(0) == j)
            def _():
                first, second = spare.at[j // 2, j % 2], spare.at[2 + j % 2, j // 2]
                first[...], second[...] = product[: unit // 2], product[unit // 2 :]

        @pl.when(pl.program_id(0) == picked - 1)
        def _():
            moves = [
                pltpu.make_async_copy(
                    spare.at[index], out.at[:, :, pl.ds(offset, other)], sems.at[index]
                )
                for index, out in enumerate(outs)
            ]
            for move in moves:
                move.start()
            for move in moves:
                move.wait()

    grid_spec = pltpu.PrefetchScalarGridSpec(
        num_scalar_prefetch=1,
        grid=(picked,),
        in_specs=[chosen, cut]
        + [whole((rows, other))] * 2
        + anywhere(len(held) + len(needed)),
        out_specs=anywhere(4),
        scratch_shapes=[
            pltpu.VMEM((4, 2, unit // 2, other), BF16),
            pltpu.SemaphoreType.DMA((4,)),
        ],
    )
    place = jnp.concatenate([place, place[2:3] * 2 + place[1:2] // 2])
    return pl.pallas_call(
        kernel,
        grid_spec=grid_spec,
        out_shape=[jax.ShapeDtypeStruct(shape, BF16) for shape in shapes],
        input_output_aliases={5 + index: index for index in range(len(held))},
        compiler_params=params(),
        cost_estimate=takes(60),
        name="blame_halves",
    )(place, *lefts, *rights, *held, *needed)


def blame(left, right, *needed):
    rows, columns = left.shape
    if right.ndim == 3:
        steps, other = right.shape[0], right.shape[2]
        in_specs = [whole((rows, columns)), pl.BlockSpec((1, rows, other), lambda j: (j, 0, 0))]
        target, shape = pl.BlockSpec((columns, other), lambda j: (0, j)), (columns, steps * other)
    else:
        steps, other = 4, right.shape[1]
        in_specs = [pl.BlockSpec((rows, columns // steps), lambda j: (0, j)), whole((rows, other))]
        target, shape = pl.BlockSpec((columns // steps, other), lambda j: (j, 0)), (columns, other)

    def kernel(left, right, *refs):
        theirs = right[0] if len(right.shape) == 3 else right[...]
        refs[-1][...] = lax.dot_general(
            left[...], theirs, (((0,), (0,)), ((), ())), preferred_element_type=F32
        ).astype(BF16)

    return pl.pallas_call(
        kernel,
        grid=(steps,),
        in_specs=in_specs + anywhere(len(needed)),
        out_specs=target,
        out_shape=jax.ShapeDtypeStruct(shape, BF16),
        compiler_params=params(),
        cost_estimate=takes(60),
        name="blame",
    )(left, right, *needed)


def turn_kernel(nctx, count, parts, unit, place, *refs):
    arrived, own = refs[:parts], refs[parts : 2 * parts]
    mixed, cot, gain = refs[2 * parts : 2 * parts + 3]
    weight, refs = refs[2 * parts + 3], refs[2 * parts + 4 + count :]
    out, grad_mixed, grad_low, gain_grad, shift_grad, half = refs
    rows, depth = mixed.shape
    piece = out.shape[3]

    @pl.when(pl.program_id(0) == 0)
    def _():
        incoming = jnp.concatenate(
            [there[...].astype(F32) + here[...].astype(F32) for there, here in zip(arrived, own)]
        )
        values = mixed[...]
        values = values - jnp.mean(values, axis=1, keepdims=True)
        scaling = lax.rsqrt(jnp.mean(values * values, axis=1, keepdims=True) + EPSILON)
        normed = values * scaling
        shift_grad[...] = jnp.sum(incoming, axis=0, keepdims=True)
        gain_grad[...] = jnp.sum(incoming * normed, axis=0, keepdims=True)
        scaled = incoming * gain[...]
        grads = jnp.concatenate([cot[block] for block in range(cot.shape[0])], axis=1)
        total = grads.astype(F32) + scaling * (
            scaled
            - jnp.mean(scaled, axis=1, keepdims=True)
            - normed * jnp.mean(scaled * normed, axis=1, keepdims=True)
        )
        grad_mixed[...] = total
        grad_low[...] = total.astype(BF16)
        write_half(half, grad_low, 1 - lax.rem(place[1], 2), unit)

    product = dot(grad_low[...], weight[0])
    for c in range(nctx):
        out[c, 0] = product[:, c * piece : (c + 1) * piece].astype(BF16)


def turn(arrived, own, mixed, cot, gain, weight, place, nctx, tp, unit, *needed):
    rows, depth = mixed.shape
    parts = len(arrived)
    head_width = weight.shape[2]
    piece = head_width // nctx
    grid_spec = pltpu.PrefetchScalarGridSpec(
        num_scalar_prefetch=1,
        grid=(tp,),
        in_specs=[whole((rows // parts, depth))] * (2 * parts)
        + [whole((rows, depth))]
        + [
            pl.BlockSpec((tp, rows, depth // tp), lambda k, s: (0, s[0], 0)),
            whole((1, depth)),
            pl.BlockSpec((1, depth, head_width), lambda k, s: (k, 0, 0)),
        ]
        + anywhere(len(needed)),
        out_specs=[
            pl.BlockSpec((nctx, 1, rows, piece), lambda k, s: (0, k, 0, 0)),
            whole((rows, depth)),
            whole((rows, depth)),
            whole((1, depth)),
            whole((1, depth)),
            whole((rows, depth // 2)),
        ],
    )
    return pl.pallas_call(
        functools.partial(turn_kernel, nctx, len(needed), parts, unit),
        grid_spec=grid_spec,
        out_shape=[
            jax.ShapeDtypeStruct((nctx, tp, rows, piece), BF16),
            jax.ShapeDtypeStruct((rows, depth), F32),
            jax.ShapeDtypeStruct((rows, depth), BF16),
            jax.ShapeDtypeStruct((1, depth), F32),
            jax.ShapeDtypeStruct((1, depth), F32),
            jax.ShapeDtypeStruct((rows, depth // 2), BF16),
        ],
        compiler_params=params(),
        cost_estimate=takes(60),
        name="turn",
    )(place, *arrived, *own, mixed, cot, gain, weight, *needed)


def finish_kernel(nctx, tp, extra_count, place, *refs):
    pieces = refs[:nctx]
    cosine, sine_up, sine_down, full, extra, gain = refs[nctx : nctx + 6]
    weight, refs = refs[nctx + 6], refs[nctx + 7 + extra_count :]
    outs = refs[:tp]
    low, bias_grad, gain_grad, shift_grad, spare = refs[tp:]
    rows, wide = pieces[0].shape
    piece = wide // 3
    width = outs[0].shape[1]
    strip = spare.shape[0]
    extra_rows = extra.shape[0]

    @pl.when(pl.program_id(0) == 0)
    def _():
        bias_grad[...] = jnp.zeros_like(bias_grad)
        gain_grad[...] = jnp.zeros_like(gain_grad)
        shift_grad[...] = jnp.zeros_like(shift_grad)

    for step in range(nctx):
        source = jnp.bitwise_xor(place[1], step)
        for part in range(3):
            values = pieces[step][:, part * piece : (part + 1) * piece].astype(F32)
            if part < 2:
                values = (
                    values * cosine[...]
                    - pltpu.roll(values, piece - ROT // 2, 1) * sine_up[...]
                    - pltpu.roll(values, ROT // 2, 1) * sine_down[...]
                )
            columns = pl.ds(pl.multiple_of(source * wide + part * piece, piece), piece)
            bias_grad[:, columns] += jnp.sum(values, axis=0, keepdims=True)
            low[:, columns] = values.astype(BF16)

    incoming = dot_turned(low[...], weight[...])
    source = full[...].astype(F32)
    source = source - jnp.mean(source, axis=1, keepdims=True)
    scaling = lax.rsqrt(jnp.mean(source * source, axis=1, keepdims=True) + EPSILON)
    normed = source * scaling
    shift_grad[...] += jnp.sum(incoming, axis=0, keepdims=True)
    gain_grad[...] += jnp.sum(incoming * normed, axis=0, keepdims=True)
    scaled = incoming * gain[...]
    spare[...] = scaling * (
        scaled
        - jnp.mean(scaled, axis=1, keepdims=True)
        - normed * jnp.mean(scaled * normed, axis=1, keepdims=True)
    )
    first = pl.program_id(0) * strip
    wanted = place[0] * extra_rows

    if strip <= extra_rows:

        @pl.when((first >= wanted) & (first < wanted + extra_rows))
        def _():
            spare[...] += extra[pl.ds(pl.multiple_of(first - wanted, strip), strip), :]

    else:

        @pl.when((wanted >= first) & (wanted < first + strip))
        def _():
            spare[pl.ds(pl.multiple_of(wanted - first, extra_rows), extra_rows), :] += extra[...]

    for step, out in enumerate(outs):
        owner = lax.rem(place[0] - step + tp, tp)
        out[...] = spare[:, pl.ds(pl.multiple_of(owner * width, width), width)].astype(BF16)


def finish(pieces, place, tables, full, extra, gain, weight, tp, *needed):
    rows, wide = pieces[0].shape
    depth = full.shape[1]
    total = weight.shape[1]
    strip = 256
    steps = rows // strip
    width = depth // tp
    nctx = len(pieces)
    by_rows = lambda columns: pl.BlockSpec((strip, columns), lambda i, s: (i, 0))
    grid_spec = pltpu.PrefetchScalarGridSpec(
        num_scalar_prefetch=1,
        grid=(steps,),
        in_specs=[by_rows(wide)] * nctx
        + [by_rows(2 * HEAD_DIM)] * 3
        + [
            by_rows(depth),
            whole(extra.shape),
            whole((1, depth)),
        ]
        + [whole(weight.shape)]
        + anywhere(len(needed)),
        out_specs=[by_rows(width)] * tp
        + [
            by_rows(total),
            whole((1, total)),
            whole((1, depth)),
            whole((1, depth)),
        ],
        scratch_shapes=[pltpu.VMEM((strip, depth), F32)],
    )
    return pl.pallas_call(
        functools.partial(finish_kernel, nctx, tp, len(needed)),
        grid_spec=grid_spec,
        out_shape=[jax.ShapeDtypeStruct((rows, width), BF16)] * tp
        + [
            jax.ShapeDtypeStruct((rows, total), BF16),
            jax.ShapeDtypeStruct((1, total), F32),
            jax.ShapeDtypeStruct((1, depth), F32),
            jax.ShapeDtypeStruct((1, depth), F32),
        ],
        compiler_params=params(),
        cost_estimate=takes(70),
        name="finish",
    )(place, *pieces, *tables, full, extra, gain, weight, *needed)


def join(rings, place, unit):
    parts, tp = len(rings), len(rings[0])
    rows, width = rings[0][0].shape

    def kernel(place, *refs):
        for part in range(parts):
            for step in range(tp):
                owner = lax.rem(place[0] - step + tp, tp)
                refs[-2][owner, part * rows : (part + 1) * rows, :] = refs[part * tp + step][...]
        per, half = width // unit, 1 - lax.rem(place[1], 2)
        for block in range(tp * per // 2):
            index = 2 * block + half if unit % 128 == 0 else 0
            first = pl.multiple_of(lax.rem(index, per) * unit, unit)
            if unit % 128:
                first = 0
            refs[-1][:, block * unit : (block + 1) * unit] = refs[-2][
                lax.div(index, per), :, pl.ds(first, unit)
            ]

    grid_spec = pltpu.PrefetchScalarGridSpec(
        num_scalar_prefetch=1,
        grid=(1,),
        in_specs=[whole((rows, width))] * (parts * tp),
        out_specs=[whole((tp, parts * rows, width)), whole((parts * rows, tp * width // 2))],
    )
    return pl.pallas_call(
        kernel,
        grid_spec=grid_spec,
        out_shape=[
            jax.ShapeDtypeStruct((tp, parts * rows, width), BF16),
            jax.ShapeDtypeStruct((parts * rows, tp * width // 2), BF16),
        ],
        compiler_params=params(),
        cost_estimate=takes(10),
        name="join",
    )(place, *[block for blocks in rings for block in blocks])


def pack_kernel(gate, up, down, out):
    rows = gate.shape[0]
    out[:rows] = gate[...]
    out[rows : 2 * rows] = up[...]
    out[2 * rows :] = jnp.transpose(down[...])


def pack(gate, up, down):
    rows, columns = gate.shape
    return pl.pallas_call(
        pack_kernel,
        out_shape=jax.ShapeDtypeStruct((3 * rows, columns), BF16),
        compiler_params=params(),
        cost_estimate=takes(10),
        name="pack",
    )(gate, up, down)


def contract_rows(left, right):
    return lax.dot_general(left, right, (((0,), (0,)), ((), ())), preferred_element_type=F32)


def pick(stack, index):
    return lax.dynamic_index_in_dim(stack, index, 0, keepdims=False)


def shards(
    nfsdp,
    nctx,
    tp,
    inputs,
    cotangent,
    first_gain,
    first_bias,
    qkv_weight,
    qkv_bias,
    out_weight,
    second_gain,
    second_bias,
    gate_weight,
    up_weight,
    down_weight,
    lengths,
    fill_counts,
):
    data = ("fsdp", "ctx")
    ndata = nfsdp * nctx
    block_rows, width = inputs.shape
    depth = tp * width
    half_depth = depth // 2
    unit = depth // ndata
    tensor_index = lax.axis_index("tp").astype(jnp.int32)
    context_index = lax.axis_index("ctx").astype(jnp.int32)
    fsdp_index = lax.axis_index("fsdp").astype(jnp.int32)
    part_rows = block_rows // tp
    chunk_rows = block_rows // CHUNKS
    head_width = qkv_weight.shape[2]
    piece = head_width // nctx
    wide = 3 * piece

    square = nfsdp == 2 and nctx == 4 and unit % 128 == 0
    place = jnp.stack([tensor_index, context_index, fsdp_index])

    def shift(value, step):
        return lax.ppermute(value, "tp", [(i, (i + step) % tp) for i in range(tp)])

    def swap(value, step):
        return lax.ppermute(value, "ctx", [(i, i ^ step) for i in range(nctx)])

    core_index = context_index % 2
    groups = [list(range(0, ndata, 2)), list(range(1, ndata, 2))]
    def mate(value):
        return swap(value, 1)

    def send(here, near, far, *needed):
        far = swap(far, 2)
        return [here, swap(near, 1), far[0], swap(tie(far[1], *needed), 1)]

    def scatter_half(value, axis):
        return lax.psum_scatter(
            value, data, scatter_dimension=axis, tiled=True, axis_index_groups=groups
        )

    def scatter(value, axis):
        return lax.psum_scatter(value, data, scatter_dimension=axis, tiled=True)

    def cross(value):
        return lax.ppermute(value, "fsdp", [(i, i ^ 1) for i in range(nfsdp)])

    def square_once(parts):
        near, far, low, high = parts
        return total(near, cross(far)), total(low, swap(high, 2))

    def square_twice(first, second):
        first = first[0].astype(F32) + swap(first[1], 2).astype(F32)
        second = second[0].astype(F32) + cross(second[1]).astype(F32)
        return jnp.concatenate([first, second], axis=0)

    def total(left, right):
        return (left.astype(F32) + right.astype(F32)).astype(BF16)

    owners = [(tensor_index - step + tp) % tp for step in range(tp)]

    own_qkv = (
        qkv_weight.reshape(-1, 3, nctx, piece).transpose(0, 2, 1, 3).reshape(-1, 3 * head_width)
    )
    full_qkv = lax.all_gather(own_qkv, data, axis=0, tiled=True)
    own_feed = pack(gate_weight, up_weight, down_weight)
    feed_weights = lax.all_gather(own_feed, data, axis=0, tiled=True).reshape(ndata, 3 * unit, -1)

    validity, position, first_key, last_key = layout(lengths[0], fill_counts[0], block_rows)
    own_position = lax.dynamic_slice_in_dim(position, context_index * block_rows, block_rows, 0)
    tables = rotary_tables(own_position)
    bounds = jnp.stack([first_key, last_key])
    tile_first = first_key[::TILE_Q]
    tile_count = tile_first.shape[0]
    lows = jnp.where(validity[::TILE_Q], tile_first // TILE_K, tile_count * TILE_Q).astype(jnp.int32)
    key_block = jnp.arange(0, nctx * block_rows, TILE_K, dtype=jnp.int32) // block_rows
    ends = (
        key_block * block_rows
        + jnp.sum(
            jnp.where(
                key_block[:, None] == jnp.arange(nctx, dtype=jnp.int32)[None, :],
                fill_counts[0][None, :],
                0,
            ),
            axis=1,
        )
    ).astype(jnp.int32)

    flat_bias = qkv_bias.reshape(3, nctx, piece).transpose(1, 0, 2).reshape(1, -1)
    gain_one, bias_one = first_gain[None], first_bias[None]
    gain_two, bias_two = second_gain[None], second_bias[None]

    rings = [[inputs[c * chunk_rows : (c + 1) * chunk_rows]] for c in range(CHUNKS)]
    share = unit // CHUNKS
    for chunk in range(CHUNKS):
        carried = out_weight.T[chunk * share : (chunk + 1) * share]
        rings[chunk][0] = jnp.concatenate([rings[chunk][0], carried], axis=0)
    for chunk in range(CHUNKS):
        for _ in range(tp - 1):
            rings[chunk].append(shift(rings[chunk][-1], 1))
            if len(rings[chunk]) == 2:
                rings[chunk][-1] = tie(rings[chunk][-1], own_feed)
    all_low, full, low_half, *outgoing, stack = project(
        rings, place, gain_one, bias_one, full_qkv, flat_bias, tables, nctx, unit
    )
    full_out = lax.all_gather(stack, data, axis=1, tiled=True)

    cot = tie(cotangent, *[blocks[-1] for blocks in rings])
    cot_rings = [[cot[c * chunk_rows : (c + 1) * chunk_rows]] for c in range(CHUNKS)]
    for blocks in cot_rings:
        for _ in range(tp - 1):
            blocks.append(shift(blocks[-1], 1))
    pieces = send(*outgoing, *[blocks[max(tp - 2, 0)] for blocks in cot_rings])

    attended, outgoing, logs = attend(
        pieces,
        place[1:2],
        lows,
        ends,
        bounds,
        nctx,
        block_rows,
        feed_weights,
    )
    cot, cot_half = join(cot_rings, place, unit)
    arrived = lax.all_to_all(
        tie(outgoing, *[blocks[-1] for blocks in cot_rings]).reshape(nctx * tp, part_rows, piece),
        ("ctx", "tp"),
        split_axis=0,
        concat_axis=0,
        tiled=True,
    )
    returned, mixed, second_low = mix(
        arrived.reshape(nctx, tp, part_rows, piece),
        full_out,
        full,
        gain_two,
        bias_two,
        place,
        1,
    )

    arrived, held, partials, travelling = second_low, [], [], None
    for step in range(tp):
        coming = shift(arrived, 1) if step < tp - 1 else None
        needed = travelling if step == tp - 1 and step > 2 else []
        *held, first, second = feed(
            arrived, cot, mixed, feed_weights, step, tp, place, held, HALVES, *needed
        )
        partials.append([first, second])
        if step == 1 % tp:
            travelling = partials[step]
        elif step > 1:
            travelling = [
                total(shift(value, 1), kept) for value, kept in zip(travelling, partials[step])
            ]
        if step == 0 and coming is not None:
            coming = tie(coming, partials[0][0])
        arrived = coming
    all_second, all_gate, all_up, hidden, feedforward = held

    last = [shift(value, 1) for value in travelling]
    half_gate = blame(all_second, all_gate, *travelling)
    half_up = blame(all_second, all_up, *travelling)
    grad_heads, grad_mixed, mixed_low, gain_grad_two, shift_grad_two, mixed_half = turn(
        last,
        partials[0],
        mixed,
        cot,
        gain_two,
        full_out,
        place,
        nctx,
        tp,
        unit,
        half_gate,
        half_up,
    )
    grad_heads = lax.all_to_all(
        grad_heads.reshape(nctx * tp, part_rows, piece),
        ("ctx", "tp"),
        split_axis=0,
        concat_axis=0,
        tiled=True,
    ).reshape(nctx * block_rows, piece)

    total_gate = scatter(tie(half_gate, mixed_low), 0).astype(F32)
    total_up = scatter(tie(half_up, mixed_low), 0).astype(F32)
    half_out = blame(mixed_low, returned)
    total_out = scatter(tie(half_out, grad_heads), 0)

    feedforward = tie(feedforward, grad_heads)
    layer_out = [pick(feedforward, owners[1 % tp])]
    for step in range(1, tp):
        kept = pick(feedforward, owners[(step + 1) % tp])
        layer_out.append(total(shift(layer_out[-1], 1), kept))

    grad_pieces = attend_back(
        pieces, place[1:2], lows, ends, bounds, logs, grad_heads, attended, nctx, block_rows, half_out
    )
    arrived = send(*grad_pieces, *layer_out[max(tp - 2, 0) : tp - 1])
    layer_out = layer_out[-1]
    inner = hidden.shape[1]
    both = inner + 3 * head_width
    if square:
        parts = blame_halves(
            (cot, mate(cot_half)), (hidden, mate(hidden)), place, unit, arrived[2], total=both
        )
        half_down = parts[0]
    else:
        half_down = blame(hidden, cot)
        total_down = scatter(half_down, 1).astype(F32)
    low_halves = mate(low_half) if square else low_half
    needed = [layer_out, low_halves, half_down]
    *partial, all_grad, bias_grad, gain_grad, shift_grad = finish(
        arrived, place, tables, full, grad_mixed, gain_one, full_qkv, tp, *needed
    )
    if square:
        parts = blame_halves(
            (all_low, low_halves),
            (all_grad, mate(all_grad)),
            place,
            unit,
            held=parts,
            offset=inner,
            total=both,
        )
    else:
        parts = []
    def exchange(value, axis, steps, size):
        for step in steps:
            value = value + lax.ppermute(value, axis, [(i, i ^ step) for i in range(size)])
        return value

    def powers(first, size):
        return [1 << bit for bit in range(first, size.bit_length() - 1)]

    small = jnp.concatenate([gain_grad, shift_grad, gain_grad_two, shift_grad_two], axis=1)
    small = sum([shift(small, step) for step in range(1, tp)], small)
    small = jnp.concatenate([bias_grad, small], axis=1)
    travelling, ring_steps = partial[1 % tp], []
    once = square_once(parts) if square else ()
    needed = [[total_gate, total_up, small, *parts], [*once], []]
    for step in range(1, tp):
        travelling = add(
            shift(travelling, 1), partial[(step + 1) % tp], *(needed[step - 1] if step < 4 else [])
        )
        if step == 1:
            out_parts = jnp.swapaxes(
                tie(total_out, travelling).reshape(-1, tp, head_width), 0, 1
            )
            total_out = pick(out_parts, tensor_index).astype(F32)
            for ahead in range(1, tp):
                total_out = total_out + shift(pick(out_parts, (tensor_index + ahead) % tp), ahead).astype(F32)
            total_out = total_out.T
            needed[2].append(total_out)
        if step < 3:
            bits = powers(0, min(nctx, 2)) if step == 1 else powers(1, nctx)
            small = exchange(tie(small, travelling), "ctx", bits, nctx)
            needed[step].append(small)
    small = exchange(tie(small, travelling), "fsdp", powers(0, nfsdp), nfsdp)
    grad_inputs = travelling
    if square:
        totals = square_twice(*once)
        total_down, total_qkv = totals[:, :inner].T, totals[:, inner:]
    else:
        total_qkv = scatter(blame(all_low, all_grad), 0).astype(F32)

    total_qkv = (
        total_qkv
        .reshape(-1, nctx, 3, piece)
        .transpose(0, 2, 1, 3)
        .reshape(-1, 3, head_width)
    )


    bias_total, small = small[:, : 3 * head_width], small[:, 3 * head_width :]
    bias_total = bias_total.reshape(nctx, 3, piece).transpose(1, 0, 2).reshape(3, head_width)
    small = small.reshape(4, depth)
    return (
        layer_out,
        grad_inputs,
        small[0],
        small[1],
        total_qkv,
        bias_total,
        total_out,
        small[2],
        small[3],
        total_gate,
        total_up,
        total_down,
    )


def solution(mesh):
    data = ("fsdp", "ctx")
    by_rows = P(data, "tp")
    by_columns = P("tp", data)
    qkv = P(data, None, "tp")
    return jax.shard_map(
        functools.partial(shards, mesh.shape["fsdp"], mesh.shape["ctx"], mesh.shape["tp"]),
        mesh=mesh,
        in_specs=(
            by_rows,
            by_rows,
            P(),
            P(),
            qkv,
            P(None, "tp"),
            by_columns,
            P(),
            P(),
            by_rows,
            by_rows,
            by_columns,
            P("fsdp", None),
            P("fsdp", None),
        ),
        out_specs=(
            by_rows,
            by_rows,
            P(),
            P(),
            qkv,
            P(None, "tp"),
            by_columns,
            P(),
            P(),
            by_rows,
            by_rows,
            by_columns,
        ),
        check_vma=False,
    )
```

```python
import functools

import jax
import jax.numpy as jnp
from jax import lax
from jax.experimental import pallas as pl
from jax.experimental.pallas import tpu as pltpu
from jax.sharding import PartitionSpec as P

HEAD_DIM = 64
ROT = 16
EPSILON = 1e-05
NEGATIVE = -1e30
FLOOR = -1e20
VMEM_LIMIT = 56 * 1024 * 1024
TILE_Q = 512
TILE_K = 512
STRIP = 32
CHUNKS = 2
HALVES = 2

F32 = jnp.float32
BF16 = jnp.bfloat16


def layout(lengths, fill_counts, block_rows):
    blocks_count = fill_counts.shape[0]
    seq_count = lengths.shape[0]
    slot_index = jnp.arange(blocks_count * block_rows, dtype=jnp.int32)
    block_of = slot_index // block_rows
    within = slot_index - block_of * block_rows
    chooser = block_of[:, None] == jnp.arange(blocks_count, dtype=jnp.int32)[None, :]
    fill_here = jnp.sum(jnp.where(chooser, fill_counts[None, :], 0), axis=1)
    before = jnp.cumsum(fill_counts) - fill_counts
    before_here = jnp.sum(jnp.where(chooser, before[None, :], 0), axis=1)
    validity = within < fill_here
    used_index = before_here + within
    seq_ends = jnp.cumsum(lengths)
    sequence = jnp.sum((used_index[:, None] >= seq_ends[None, :]).astype(jnp.int32), axis=1)
    seq_starts = seq_ends - lengths
    picker = sequence[:, None] == jnp.arange(seq_count, dtype=jnp.int32)[None, :]
    start_here = jnp.sum(jnp.where(picker, seq_starts[None, :], 0), axis=1)
    after = before + fill_counts
    start_block = jnp.sum((seq_starts[:, None] >= after[None, :]).astype(jnp.int32), axis=1)
    start_block = jnp.minimum(start_block, blocks_count - 1)
    block_pick = start_block[:, None] == jnp.arange(blocks_count, dtype=jnp.int32)[None, :]
    start_before = jnp.sum(jnp.where(block_pick, before[None, :], 0), axis=1)
    start_slot = start_block * block_rows + seq_starts - start_before
    slot_here = jnp.sum(jnp.where(picker, start_slot[None, :], 0), axis=1)
    first_key = jnp.where(validity, slot_here, 0).astype(jnp.int32)
    last_key = jnp.where(validity, slot_index, -1).astype(jnp.int32)
    return (validity, used_index - start_here, first_key, last_key)


def rotary_tables(position):
    half = ROT // 2
    lane = jnp.arange(2 * HEAD_DIM, dtype=jnp.int32) % HEAD_DIM
    frequency = 10000.0 ** (-(2.0 * (lane % half).astype(F32)) / ROT)
    angles = position.astype(F32)[:, None] * frequency[None, :]
    cosine, sine = jnp.cos(angles), jnp.sin(angles)
    lane = lane[None, :]
    return (
        jnp.where(lane < ROT, cosine, 1.0),
        jnp.where(lane < half, -sine, 0.0),
        jnp.where((lane >= half) & (lane < ROT), sine, 0.0),
    )


def params(**extra):
    return pltpu.CompilerParams(vmem_limit_bytes=VMEM_LIMIT, **extra)


def takes(microseconds):
    return pl.CostEstimate(
        flops=int(microseconds * 1e8), bytes_accessed=0, transcendentals=0
    )


def whole(shape):
    return pl.BlockSpec(shape, lambda *_: (0,) * len(shape))


def anywhere(count):
    return [pl.BlockSpec(memory_space=pl.ANY)] * count


def write_half(out, values, half, unit):
    if unit % 128:
        out[...] = values[:, : out.shape[1]]
        return
    for block in range(out.shape[1] // unit):
        first = pl.multiple_of((2 * block + half) * unit, unit)
        out[:, block * unit : (block + 1) * unit] = values[:, pl.ds(first, unit)]


def dot(left, right):
    return jnp.dot(left, right, preferred_element_type=F32)


def dot_turned(left, right):
    return lax.dot_general(left, right, (((1,), (1,)), ((), ())), preferred_element_type=F32)


def tie(value, *needed):
    def kernel(*refs):
        del refs

    return pl.pallas_call(
        kernel,
        in_specs=anywhere(1 + len(needed)),
        out_specs=pl.BlockSpec(memory_space=pl.ANY),
        out_shape=jax.ShapeDtypeStruct(value.shape, value.dtype),
        input_output_aliases={0: 0},
        name="tie",
    )(value, *needed)


def add_kernel(left, right, *refs):
    refs[-1][...] = (left[...].astype(F32) + right[...].astype(F32)).astype(BF16)


def add(left, right, *needed):
    rows, columns = left.shape
    strip = min(rows, 512)
    block = pl.BlockSpec((strip, columns), lambda i: (i, 0))
    return pl.pallas_call(
        add_kernel,
        grid=(rows // strip,),
        in_specs=[block, block] + anywhere(len(needed)),
        out_specs=block,
        out_shape=jax.ShapeDtypeStruct(left.shape, BF16),
        compiler_params=params(),
        cost_estimate=takes(10),
        name="ring_add",
    )(left, right, *needed)


def project_kernel(tp, chunks, per, unit, place, *refs):
    rings, refs = refs[: tp * chunks], refs[tp * chunks :]
    gain, bias, weight, weight_bias, cosine, sine_up, sine_down = refs[:7]
    low, full, half, here, near, far, stack = refs[7:]
    outs = [here, near] + [far.at[way] for way in range(far.shape[0])]
    rows, width = low.shape[0] // chunks, rings[0].shape[1]
    depth = tp * width
    wide = here.shape[1]
    piece = wide // 3
    step = pl.program_id(0)

    @pl.when(pl.program_id(0) == 0)
    def _():
        strip = 128
        for start in range(0, rows * chunks, strip):
            chunk, first = start // rows, start % rows
            blocks = rings[chunk * tp : (chunk + 1) * tp]
            at = slice(start, start + strip)
            inner = slice(first, first + strip)
            parts = [block[inner, :].astype(F32) for block in blocks]
            centre = sum(jnp.sum(part, axis=1, keepdims=True) for part in parts) / depth
            parts = [part - centre for part in parts]
            spread = sum(jnp.sum(part * part, axis=1, keepdims=True) for part in parts) / depth
            scaling = lax.rsqrt(spread + EPSILON)
            for step in range(tp):
                owner = lax.rem(place[0] - step + tp, tp)
                columns = pl.ds(pl.multiple_of(owner * width, width), width)
                low[at, columns] = (
                    parts[step] * scaling * gain[:, columns] + bias[:, columns]
                ).astype(BF16)
                full[at, columns] = blocks[step][inner, :]
        write_half(half, low, 1 - lax.rem(place[1], 2), unit)
        share = rings[0].shape[0] - rows
        for chunk in range(chunks):
            for step in range(tp):
                owner = lax.rem(place[0] - step + tp, tp)
                stack[owner, chunk * share : (chunk + 1) * share, :] = rings[chunk * tp + step][
                    rows:, :
                ]

    product = dot(low[...], weight[...]) + weight_bias[...]
    groups = []
    for group in range(per):
        parts = []
        for part in range(3):
            first = (group * 3 + part) * piece
            values = product[:, first : first + piece]
            if part < 2:
                values = (
                    values * cosine[...]
                    + pltpu.roll(values, piece - ROT // 2, 1) * sine_up[...]
                    + pltpu.roll(values, ROT // 2, 1) * sine_down[...]
                )
            parts.append(values.astype(BF16))
        groups.append(parts)
    flip = lax.rem(place[1], per)
    for way, out in enumerate(outs):
        for group in range(per):

            @pl.when((step == way // per) & (jnp.bitwise_xor(group, flip) == way % per))
            def _():
                for part in range(3):
                    out[:, part * piece : (part + 1) * piece] = groups[group][part]


def project(rings, place, gain, bias, weight, weight_bias, tables, nctx, unit):
    chunks, tp = len(rings), len(rings[0])
    rows, width = tables[0].shape[0], rings[0][0].shape[1]
    depth = tp * width
    total = weight.shape[1]
    wide = total // nctx
    per = 2 if nctx % 2 == 0 else 1
    grid_spec = pltpu.PrefetchScalarGridSpec(
        num_scalar_prefetch=1,
        grid=(nctx // per,),
        in_specs=[whole(rings[0][0].shape)] * (tp * chunks)
        + [whole((1, depth))] * 2
        + [
            pl.BlockSpec((depth, per * wide), lambda i, s: (0, jnp.bitwise_xor(i, s[1] // per))),
            pl.BlockSpec((1, per * wide), lambda i, s: (0, jnp.bitwise_xor(i, s[1] // per))),
        ]
        + [whole((rows, 2 * HEAD_DIM))] * 3,
        out_specs=[whole((rows, depth))] * 2
        + [whole((rows, depth // 2))]
        + [whole((rows, wide))] * 2
        + [whole((nctx - 2, rows, wide)), whole((tp, unit, width))],
    )
    return pl.pallas_call(
        functools.partial(project_kernel, tp, chunks, per, unit),
        grid_spec=grid_spec,
        out_shape=[
            jax.ShapeDtypeStruct((rows, depth), BF16),
            jax.ShapeDtypeStruct((rows, depth), BF16),
            jax.ShapeDtypeStruct((rows, depth // 2), BF16),
        ]
        + [jax.ShapeDtypeStruct((rows, wide), BF16)] * 2
        + [
            jax.ShapeDtypeStruct((nctx - 2, rows, wide), BF16),
            jax.ShapeDtypeStruct((tp, unit, width), BF16),
        ],
        compiler_params=params(),
        cost_estimate=takes(60),
        name="project",
    )(
        place,
        *[block for blocks in rings for block in blocks],
        gain,
        bias,
        weight,
        weight_bias,
        *tables,
    )


def stack_heads(tile, heads):
    lane = lax.broadcasted_iota(jnp.int32, tile.shape, 1) // HEAD_DIM
    return jnp.concatenate(
        [jnp.where(lane == head, tile, jnp.zeros_like(tile)) for head in range(heads)], axis=0
    )


def load_pieces(place, pieces, nctx, held, block_rows):
    chunk_rows = pieces[0].shape[0]
    chunks = len(pieces) // nctx
    for chunk in range(chunks):
        for step in range(nctx):
            source = jnp.bitwise_xor(place, step)
            first = source * block_rows + chunk * chunk_rows
            held[pl.ds(pl.multiple_of(first, chunk_rows), chunk_rows), :] = pieces[
                chunk * nctx + step
            ][...]


def attend_kernel(nctx, heads, count, extra, block_rows, place, lows, ends, bounds, *refs):
    pieces = refs[:count]
    out, sent, logs, held, turned, total, high, sums, raw, chances = refs[count + extra :]
    tile_q, tile_k = out.shape[0], turned.shape[2]
    width = heads * HEAD_DIM
    index = pl.program_id(0)

    @pl.when(index == 0)
    def _():
        load_pieces(place[0], pieces, nctx, held, block_rows)
        for tile in range(turned.shape[0]):
            turned[tile] = jnp.transpose(held[tile * tile_k : (tile + 1) * tile_k, 2 * width :])

    query_rows = pl.ds(pl.multiple_of(index * tile_q, tile_q), tile_q)
    queries = stack_heads(held[query_rows, :width] * jnp.asarray(HEAD_DIM**-0.5, BF16), heads)
    total[...] = jnp.zeros_like(total)
    high[...] = jnp.full_like(high, FLOOR)
    sums[...] = jnp.zeros_like(sums)
    first_key, last_key = bounds[0:1, :], bounds[1:2, :]

    def one(tile, _):
        start = tile * tile_k
        keys = held[pl.ds(pl.multiple_of(start, tile_k), tile_k), width : 2 * width]
        last = jnp.minimum(last_key, ends[tile] - 1) - start
        first = first_key - start
        for head in range(heads):
            raw[head] = dot_turned(keys, queries[head * tile_q : (head + 1) * tile_q])
        for head in range(heads):
            peaks = jnp.broadcast_to(high[head], (8, tile_q))
            for begin in range(0, tile_k, STRIP):
                scores = raw[head, begin : begin + STRIP, :]
                row = lax.broadcasted_iota(jnp.int32, scores.shape, 0) + begin
                scores = jnp.where((row <= last) & (row >= first), scores, NEGATIVE)
                raw[head, begin : begin + STRIP, :] = scores
                for group in range(0, STRIP, 8):
                    peaks = jnp.maximum(peaks, scores[group : group + 8])
            highest = jnp.max(peaks, axis=0, keepdims=True)
            partial = jnp.zeros((8, tile_q), F32)
            for begin in range(0, tile_k, STRIP):
                raised = jnp.exp(raw[head, begin : begin + STRIP, :] - highest)
                chances[head, begin : begin + STRIP, :] = raised.astype(BF16)
                for group in range(0, STRIP, 8):
                    partial = partial + raised[group : group + 8]
            shrink = jnp.exp(high[head] - highest)
            sums[head] = sums[head] * shrink + jnp.sum(partial, axis=0, keepdims=True)
            values = turned[tile, head * HEAD_DIM : (head + 1) * HEAD_DIM, :]
            total[head] = total[head] * shrink + dot(values, chances[head])
            high[head] = highest
        return 0

    upper = (index * tile_q + tile_q - 1) // tile_k + 1
    lax.fori_loop(lows[index], upper, one, 0)
    results = []
    for head in range(heads):
        found = sums[head] > 0.0
        safe = jnp.where(found, sums[head], 1.0)
        results.append(total[head] * jnp.where(found, 1.0 / safe, 0.0))
        logs[head : head + 1, :] = jnp.where(found, high[head] + jnp.log(safe), 0.0)
    result = jnp.transpose(jnp.concatenate(results, axis=0)).astype(BF16)
    out[...] = result
    sent[...] = result


def attend(pieces, place, lows, ends, bounds, nctx, block_rows, *needed):
    total_rows = nctx * block_rows
    width = pieces[0].shape[1] // 3
    heads = width // HEAD_DIM
    steps = total_rows // TILE_Q
    grid_spec = pltpu.PrefetchScalarGridSpec(
        num_scalar_prefetch=3,
        grid=(steps,),
        in_specs=[pl.BlockSpec((2, TILE_Q), lambda i, *_: (0, i))]
        + [whole(piece.shape) for piece in pieces]
        + anywhere(len(needed)),
        out_specs=[
            pl.BlockSpec((TILE_Q, width), lambda i, *_: (i, 0)),
            pl.BlockSpec((TILE_Q, width), lambda i, *_: (i, 0)),
            pl.BlockSpec((heads, TILE_Q), lambda i, *_: (0, i)),
        ],
        scratch_shapes=[
            pltpu.VMEM((total_rows, 3 * width), BF16),
            pltpu.VMEM((total_rows // TILE_K, width, TILE_K), BF16),
            pltpu.VMEM((heads, HEAD_DIM, TILE_Q), F32),
            pltpu.VMEM((heads, 1, TILE_Q), F32),
            pltpu.VMEM((heads, 1, TILE_Q), F32),
            pltpu.VMEM((heads, TILE_K, TILE_Q), F32),
            pltpu.VMEM((heads, TILE_K, TILE_Q), BF16),
        ],
    )
    return pl.pallas_call(
        functools.partial(attend_kernel, nctx, heads, len(pieces), len(needed), block_rows),
        grid_spec=grid_spec,
        out_shape=[
            jax.ShapeDtypeStruct((total_rows, width), BF16),
            jax.ShapeDtypeStruct((total_rows, width), BF16),
            jax.ShapeDtypeStruct((heads, total_rows), F32),
        ],
        compiler_params=params(),
        cost_estimate=takes(200),
        name="attend",
    )(place, lows, ends, bounds, *pieces, *needed)


def attend_back_kernel(
    nctx, heads, count, extra, block_rows, place, lows, ends, bounds, logs, *refs
):
    pieces, refs = refs[:count], refs[count:]
    grad, attended, refs = refs[0], refs[1], refs[2 + extra :]
    here, near, far, refs = *refs[:3], refs[3:]
    held, turned, grad_keys, grad_values, grad_query, raw, raw_grad, chances, steps, merged = refs
    tile_q, tile_k = grad.shape[0], turned.shape[2]
    width = grad.shape[1]
    index = pl.program_id(0)
    scale = jnp.asarray(HEAD_DIM**-0.5, BF16)

    @pl.when(index == 0)
    def _():
        load_pieces(place[0], pieces, nctx, held, block_rows)
        for tile in range(turned.shape[0]):
            turned[tile] = jnp.transpose(
                held[tile * tile_k : (tile + 1) * tile_k, width : 2 * width]
            )
        grad_keys[...] = jnp.zeros_like(grad_keys)
        grad_values[...] = jnp.zeros_like(grad_values)

    query_rows = pl.ds(pl.multiple_of(index * tile_q, tile_q), tile_q)
    queries = stack_heads(held[query_rows, :width] * scale, heads)
    incoming = stack_heads(grad[...], heads)
    product = jnp.transpose(grad[...].astype(F32) * attended[...].astype(F32))
    centres = [
        jnp.sum(product[head * HEAD_DIM : (head + 1) * HEAD_DIM, :], axis=0, keepdims=True)
        for head in range(heads)
    ]
    first_key, last_key = bounds[0:1, :], bounds[1:2, :]
    grad_query[...] = jnp.zeros_like(grad_query)

    def one(tile, _):
        start = tile * tile_k
        key_rows = pl.ds(pl.multiple_of(start, tile_k), tile_k)
        last = jnp.minimum(last_key, ends[tile] - 1) - start
        first = first_key - start
        by_head = [slice(head * tile_q, (head + 1) * tile_q) for head in range(heads)]
        for head in range(heads):
            raw[head] = dot_turned(held[key_rows, width : 2 * width], queries[by_head[head]])
            raw_grad[head] = dot_turned(held[key_rows, 2 * width :], incoming[by_head[head]])
        for head in range(heads):
            for begin in range(0, tile_k, STRIP):
                at = slice(begin, begin + STRIP)
                row = lax.broadcasted_iota(jnp.int32, (STRIP, tile_q), 0) + begin
                allowed = (row <= last) & (row >= first)
                scores = raw[head, at, :] - logs[head : head + 1, :]
                chance = jnp.exp(jnp.where(allowed, scores, NEGATIVE))
                chances[head, at, :] = chance.astype(BF16)
                steps[head, at, :] = (chance * (raw_grad[head, at, :] - centres[head])).astype(BF16)
            grad_values[key_rows, :] += dot(chances[head], incoming[by_head[head]])
            grad_keys[key_rows, :] += dot(steps[head], queries[by_head[head]])
            keys = turned[tile, head * HEAD_DIM : (head + 1) * HEAD_DIM, :]
            grad_query[head] += dot(keys, steps[head])
        return 0

    upper = (index * tile_q + tile_q - 1) // tile_k + 1
    lax.fori_loop(lows[index], upper, one, 0)
    result = jnp.concatenate([grad_query[head] for head in range(heads)], axis=0)
    merged[query_rows, :width] = (jnp.transpose(result) * HEAD_DIM**-0.5).astype(BF16)

    @pl.when(index == pl.num_programs(0) - 1)
    def _():
        merged[:, width : 2 * width] = grad_keys[...].astype(BF16)
        merged[:, 2 * width :] = grad_values[...].astype(BF16)
        outs = [here, near] + [far.at[way] for way in range(nctx - 2)]
        for way, out in enumerate(outs):
            first = jnp.bitwise_xor(place[0], way) * block_rows
            out[...] = merged[pl.ds(pl.multiple_of(first, block_rows), block_rows), :]


def attend_back(pieces, place, lows, ends, bounds, logs, grad, attended, nctx, block_rows, *needed):
    total_rows, width = grad.shape
    heads = width // HEAD_DIM
    by_tile = pl.BlockSpec((TILE_Q, width), lambda i, *_: (i, 0))
    sent = (block_rows, 3 * width)
    sent = [sent, sent, (nctx - 2, *sent)]
    grid_spec = pltpu.PrefetchScalarGridSpec(
        num_scalar_prefetch=3,
        grid=(total_rows // TILE_Q,),
        in_specs=[
            pl.BlockSpec((2, TILE_Q), lambda i, *_: (0, i)),
            pl.BlockSpec((heads, TILE_Q), lambda i, *_: (0, i)),
        ]
        + [whole(piece.shape) for piece in pieces]
        + [by_tile] * 2
        + anywhere(len(needed)),
        out_specs=[whole(shape) for shape in sent],
        scratch_shapes=[
            pltpu.VMEM((total_rows, 3 * width), BF16),
            pltpu.VMEM((total_rows // TILE_K, width, TILE_K), BF16),
            pltpu.VMEM((total_rows, width), F32),
            pltpu.VMEM((total_rows, width), F32),
            pltpu.VMEM((heads, HEAD_DIM, TILE_Q), F32),
            pltpu.VMEM((heads, TILE_K, TILE_Q), F32),
            pltpu.VMEM((heads, TILE_K, TILE_Q), F32),
            pltpu.VMEM((heads, TILE_K, TILE_Q), BF16),
            pltpu.VMEM((heads, TILE_K, TILE_Q), BF16),
            pltpu.VMEM((total_rows, 3 * width), BF16),
        ],
    )
    return pl.pallas_call(
        functools.partial(
            attend_back_kernel, nctx, heads, len(pieces), len(needed), block_rows
        ),
        grid_spec=grid_spec,
        out_shape=[jax.ShapeDtypeStruct(shape, BF16) for shape in sent],
        compiler_params=params(),
        cost_estimate=takes(250),
        name="attend_back",
    )(place, lows, ends, bounds, logs, *pieces, grad, attended, *needed)


def mix_kernel(nctx, count, place, heads_in, weight, source, gain, bias, *refs):
    returned, mixed, *lows = refs[count:]
    rows, depth = mixed.shape
    step = pl.program_id(0)
    left = jnp.concatenate([heads_in[c, 0] for c in range(nctx)], axis=1)
    returned[...] = left

    @pl.when(step == 0)
    def _():
        mixed[...] = source[...].astype(F32)

    mixed[...] += dot_turned(left, weight[0])

    @pl.when(step == pl.num_programs(0) - 1)
    def _():
        values = mixed[...]
        values = values - jnp.mean(values, axis=1, keepdims=True)
        scaling = lax.rsqrt(jnp.mean(values * values, axis=1, keepdims=True) + EPSILON)
        values = (values * scaling * gain[...] + bias[...]).astype(BF16)
        part_rows = lows[0].shape[0]
        for part, low in enumerate(lows):
            low[...] = values[part * part_rows : (part + 1) * part_rows]


def mix(heads_in, weight, full, gain, bias, place, parts, *needed):
    nctx, tp, rows, piece = heads_in.shape
    depth = full.shape[1]
    head_width = nctx * piece
    grid_spec = pltpu.PrefetchScalarGridSpec(
        num_scalar_prefetch=1,
        grid=(tp,),
        in_specs=[
            pl.BlockSpec((nctx, 1, rows, piece), lambda k, s: (0, k, 0, 0)),
            pl.BlockSpec((1, depth, head_width), lambda k, s: (k, 0, 0)),
            pl.BlockSpec((rows, depth), lambda k, s: (s[0], 0)),
            whole((1, depth)),
            whole((1, depth)),
        ]
        + anywhere(len(needed)),
        out_specs=[
            pl.BlockSpec((rows, head_width), lambda k, s: (0, k)),
            whole((rows, depth)),
        ]
        + [whole((rows // parts, depth))] * parts,
    )
    return pl.pallas_call(
        functools.partial(mix_kernel, nctx, len(needed)),
        grid_spec=grid_spec,
        out_shape=[
            jax.ShapeDtypeStruct((rows, tp * head_width), BF16),
            jax.ShapeDtypeStruct((rows, depth), F32),
        ]
        + [jax.ShapeDtypeStruct((rows // parts, depth), BF16)] * parts,
        compiler_params=params(),
        cost_estimate=takes(50),
        name="mix",
    )(place, heads_in, weight, full, gain, bias, *needed)


def feed_kernel(cuts, parts, tp, first_one, place, low, cot, mixed, source, *refs):
    refs = refs[-(5 + parts + 4) :]
    kept, grad_gate, grad_up, hidden, out = refs[:5]
    partials, held, sems = refs[5 : 5 + parts], refs[-4:-1], refs[-1]
    unit = source.shape[1] // 3
    width = out.shape[2]

    def copies(index):
        first, size = cuts[index]
        at = pl.ds(first, size)
        return [
            pltpu.make_async_copy(
                source.at[:, pl.ds(which * unit, unit), at],
                held[which].at[:, :, at],
                sems.at[index * 3 + which],
            )
            for which in range(3)
        ]

    for index in range(len(cuts)):
        for copy in copies(index):
            copy.start()
    kept[...] = low[...]
    rows, depth = kept.shape[0] // parts, kept.shape[1]
    grads = jnp.concatenate([cot[block] for block in range(tp)], axis=1)
    for index, (first, size) in enumerate(cuts):
        for copy in copies(index):
            copy.wait()
        at = slice(first, first + size)
        gate_weight, up_weight, down_weight = [w[:, :, at].reshape(depth, size) for w in held]
        gate = dot(kept[...], gate_weight)
        up = dot(kept[...], up_weight)
        sigma = 1.0 / (1.0 + jnp.exp(-gate))
        active = gate * sigma
        hidden[:, at] = (active * up).astype(BF16)
        grad = dot(grads, down_weight)
        grad_gate[:, at] = (grad * up * sigma * (1.0 + gate * (1.0 - sigma))).astype(BF16)
        grad_up[:, at] = (grad * active).astype(BF16)
    gate_weight, up_weight, down_weight = [w[...].reshape(depth, w.shape[2]) for w in held]
    product = dot_turned(grad_gate[...], gate_weight) + dot_turned(grad_up[...], up_weight)
    for part in range(parts):
        partials[part][...] = product[part * rows : (part + 1) * rows].astype(BF16)
    values = dot_turned(hidden[...], down_weight)
    if first_one:
        values = values + mixed[...]
    for block in range(tp):
        out[block] = values[:, block * width : (block + 1) * width].astype(BF16)


def feed(low, cot, mixed, weights, step, tp, place, held, parts, *needed):
    rows, depth = low.shape
    part_rows = rows // parts
    blocks, triple, hidden = weights.shape
    cuts = []
    while sum(size for _, size in cuts) < hidden:
        first = sum(size for _, size in cuts)
        cuts.append((first, min(512, hidden - first)))
    by_owner = lambda columns: pl.BlockSpec(
        (rows, columns), lambda i, s: (lax.rem(s[0] - step + tp, tp), 0)
    )
    width = depth // tp
    blocks_of_owner = pl.BlockSpec(
        (tp, rows, width), lambda i, s: (0, lax.rem(s[0] - step + tp, tp), 0)
    )
    grid_spec = pltpu.PrefetchScalarGridSpec(
        num_scalar_prefetch=1,
        grid=(1,),
        in_specs=[whole((rows, depth)), blocks_of_owner, whole(mixed.shape)]
        + anywhere(1 + len(held) + len(needed)),
        out_specs=[by_owner(depth)]
        + [by_owner(hidden)] * 3
        + [blocks_of_owner]
        + [whole((part_rows, depth))] * parts,
        scratch_shapes=[pltpu.VMEM((blocks, triple // 3, hidden), BF16)] * 3
        + [pltpu.SemaphoreType.DMA((3 * len(cuts),))],
    )
    return pl.pallas_call(
        functools.partial(feed_kernel, tuple(cuts), parts, tp, step == 0),
        grid_spec=grid_spec,
        out_shape=[
            jax.ShapeDtypeStruct((tp * rows, columns), BF16)
            for columns in (depth, hidden, hidden, hidden)
        ]
        + [jax.ShapeDtypeStruct((tp, tp * rows, width), BF16)]
        + [jax.ShapeDtypeStruct((part_rows, depth), BF16)] * parts,
        input_output_aliases={5 + index: index for index in range(len(held))},
        compiler_params=params(),
        cost_estimate=takes(100),
        name="feed",
    )(place, low, cot, mixed, weights, *held, *needed)


def blame_halves(lefts, rights, place, unit, *needed, held=(), offset=0, total=None):
    rows, other = rights[0].shape
    picked = lefts[1].shape[1] // unit
    chosen = pl.BlockSpec((rows, unit), lambda j, s: (0, 2 * (j ^ s[3]) + s[1] % 2))
    if lefts[0].ndim == 3:
        per = lefts[0].shape[2] // unit
        chosen = pl.BlockSpec(
            (1, rows, unit),
            lambda j, s: (
                (2 * (j ^ s[3]) + s[1] % 2) // per,
                0,
                lax.rem(2 * (j ^ s[3]) + s[1] % 2, per),
            ),
        )
    cut = pl.BlockSpec((rows, unit), lambda j, s: (0, j ^ s[3]))
    shapes = [(2, unit // 2, total or other)] * 4

    def kernel(place, left_here, left_there, right_here, right_there, *refs):
        outs, spare, sems = refs[len(held) + len(needed) : -2], refs[-2], refs[-1]
        product = 0.0
        for left, right in ((left_here, right_here), (left_there, right_there)):
            ours = left[0] if len(left.shape) == 3 else left[...]
            product = product + lax.dot_general(
                ours, right[...], (((0,), (0,)), ((), ())), preferred_element_type=F32
            )
        product = product.astype(BF16)
        for j in range(picked):

            @pl.when(pl.program_id(0) == j)
            def _():
                first, second = spare.at[j // 2, j % 2], spare.at[2 + j % 2, j // 2]
                first[...], second[...] = product[: unit // 2], product[unit // 2 :]

        @pl.when(pl.program_id(0) == picked - 1)
        def _():
            moves = [
                pltpu.make_async_copy(
                    spare.at[index], out.at[:, :, pl.ds(offset, other)], sems.at[index]
                )
                for index, out in enumerate(outs)
            ]
            for move in moves:
                move.start()
            for move in moves:
                move.wait()

    grid_spec = pltpu.PrefetchScalarGridSpec(
        num_scalar_prefetch=1,
        grid=(picked,),
        in_specs=[chosen, cut]
        + [whole((rows, other))] * 2
        + anywhere(len(held) + len(needed)),
        out_specs=anywhere(4),
        scratch_shapes=[
            pltpu.VMEM((4, 2, unit // 2, other), BF16),
            pltpu.SemaphoreType.DMA((4,)),
        ],
    )
    place = jnp.concatenate([place, place[2:3] * 2 + place[1:2] // 2])
    return pl.pallas_call(
        kernel,
        grid_spec=grid_spec,
        out_shape=[jax.ShapeDtypeStruct(shape, BF16) for shape in shapes],
        input_output_aliases={5 + index: index for index in range(len(held))},
        compiler_params=params(),
        cost_estimate=takes(60),
        name="blame_halves",
    )(place, *lefts, *rights, *held, *needed)


def blame(left, right, *needed):
    rows, columns = left.shape
    if right.ndim == 3:
        steps, other = right.shape[0], right.shape[2]
        in_specs = [whole((rows, columns)), pl.BlockSpec((1, rows, other), lambda j: (j, 0, 0))]
        target, shape = pl.BlockSpec((columns, other), lambda j: (0, j)), (columns, steps * other)
    else:
        steps, other = 4, right.shape[1]
        in_specs = [pl.BlockSpec((rows, columns // steps), lambda j: (0, j)), whole((rows, other))]
        target, shape = pl.BlockSpec((columns // steps, other), lambda j: (j, 0)), (columns, other)

    def kernel(left, right, *refs):
        theirs = right[0] if len(right.shape) == 3 else right[...]
        refs[-1][...] = lax.dot_general(
            left[...], theirs, (((0,), (0,)), ((), ())), preferred_element_type=F32
        ).astype(BF16)

    return pl.pallas_call(
        kernel,
        grid=(steps,),
        in_specs=in_specs + anywhere(len(needed)),
        out_specs=target,
        out_shape=jax.ShapeDtypeStruct(shape, BF16),
        compiler_params=params(),
        cost_estimate=takes(60),
        name="blame",
    )(left, right, *needed)


def turn_kernel(nctx, count, parts, unit, place, *refs):
    arrived, own = refs[:parts], refs[parts : 2 * parts]
    mixed, cot, gain = refs[2 * parts : 2 * parts + 3]
    weight, refs = refs[2 * parts + 3], refs[2 * parts + 4 + count :]
    out, grad_mixed, grad_low, gain_grad, shift_grad, half = refs
    rows, depth = mixed.shape
    piece = out.shape[3]

    @pl.when(pl.program_id(0) == 0)
    def _():
        incoming = jnp.concatenate(
            [there[...].astype(F32) + here[...].astype(F32) for there, here in zip(arrived, own)]
        )
        values = mixed[...]
        values = values - jnp.mean(values, axis=1, keepdims=True)
        scaling = lax.rsqrt(jnp.mean(values * values, axis=1, keepdims=True) + EPSILON)
        normed = values * scaling
        shift_grad[...] = jnp.sum(incoming, axis=0, keepdims=True)
        gain_grad[...] = jnp.sum(incoming * normed, axis=0, keepdims=True)
        scaled = incoming * gain[...]
        grads = jnp.concatenate([cot[block] for block in range(cot.shape[0])], axis=1)
        total = grads.astype(F32) + scaling * (
            scaled
            - jnp.mean(scaled, axis=1, keepdims=True)
            - normed * jnp.mean(scaled * normed, axis=1, keepdims=True)
        )
        grad_mixed[...] = total
        grad_low[...] = total.astype(BF16)
        write_half(half, grad_low, 1 - lax.rem(place[1], 2), unit)

    product = dot(grad_low[...], weight[0])
    for c in range(nctx):
        out[c, 0] = product[:, c * piece : (c + 1) * piece].astype(BF16)


def turn(arrived, own, mixed, cot, gain, weight, place, nctx, tp, unit, *needed):
    rows, depth = mixed.shape
    parts = len(arrived)
    head_width = weight.shape[2]
    piece = head_width // nctx
    grid_spec = pltpu.PrefetchScalarGridSpec(
        num_scalar_prefetch=1,
        grid=(tp,),
        in_specs=[whole((rows // parts, depth))] * (2 * parts)
        + [whole((rows, depth))]
        + [
            pl.BlockSpec((tp, rows, depth // tp), lambda k, s: (0, s[0], 0)),
            whole((1, depth)),
            pl.BlockSpec((1, depth, head_width), lambda k, s: (k, 0, 0)),
        ]
        + anywhere(len(needed)),
        out_specs=[
            pl.BlockSpec((nctx, 1, rows, piece), lambda k, s: (0, k, 0, 0)),
            whole((rows, depth)),
            whole((rows, depth)),
            whole((1, depth)),
            whole((1, depth)),
            whole((rows, depth // 2)),
        ],
    )
    return pl.pallas_call(
        functools.partial(turn_kernel, nctx, len(needed), parts, unit),
        grid_spec=grid_spec,
        out_shape=[
            jax.ShapeDtypeStruct((nctx, tp, rows, piece), BF16),
            jax.ShapeDtypeStruct((rows, depth), F32),
            jax.ShapeDtypeStruct((rows, depth), BF16),
            jax.ShapeDtypeStruct((1, depth), F32),
            jax.ShapeDtypeStruct((1, depth), F32),
            jax.ShapeDtypeStruct((rows, depth // 2), BF16),
        ],
        compiler_params=params(),
        cost_estimate=takes(60),
        name="turn",
    )(place, *arrived, *own, mixed, cot, gain, weight, *needed)


def finish_kernel(nctx, tp, extra_count, place, *refs):
    pieces = refs[:nctx]
    cosine, sine_up, sine_down, full, extra, gain = refs[nctx : nctx + 6]
    weight, refs = refs[nctx + 6], refs[nctx + 7 + extra_count :]
    outs = refs[:tp]
    low, bias_grad, gain_grad, shift_grad, spare = refs[tp:]
    rows, wide = pieces[0].shape
    piece = wide // 3
    width = outs[0].shape[1]
    strip = spare.shape[0]
    extra_rows = extra.shape[0]

    @pl.when(pl.program_id(0) == 0)
    def _():
        bias_grad[...] = jnp.zeros_like(bias_grad)
        gain_grad[...] = jnp.zeros_like(gain_grad)
        shift_grad[...] = jnp.zeros_like(shift_grad)

    for step in range(nctx):
        source = jnp.bitwise_xor(place[1], step)
        for part in range(3):
            values = pieces[step][:, part * piece : (part + 1) * piece].astype(F32)
            if part < 2:
                values = (
                    values * cosine[...]
                    - pltpu.roll(values, piece - ROT // 2, 1) * sine_up[...]
                    - pltpu.roll(values, ROT // 2, 1) * sine_down[...]
                )
            columns = pl.ds(pl.multiple_of(source * wide + part * piece, piece), piece)
            bias_grad[:, columns] += jnp.sum(values, axis=0, keepdims=True)
            low[:, columns] = values.astype(BF16)

    incoming = dot_turned(low[...], weight[...])
    source = full[...].astype(F32)
    source = source - jnp.mean(source, axis=1, keepdims=True)
    scaling = lax.rsqrt(jnp.mean(source * source, axis=1, keepdims=True) + EPSILON)
    normed = source * scaling
    shift_grad[...] += jnp.sum(incoming, axis=0, keepdims=True)
    gain_grad[...] += jnp.sum(incoming * normed, axis=0, keepdims=True)
    scaled = incoming * gain[...]
    spare[...] = scaling * (
        scaled
        - jnp.mean(scaled, axis=1, keepdims=True)
        - normed * jnp.mean(scaled * normed, axis=1, keepdims=True)
    )
    first = pl.program_id(0) * strip
    wanted = place[0] * extra_rows

    if strip <= extra_rows:

        @pl.when((first >= wanted) & (first < wanted + extra_rows))
        def _():
            spare[...] += extra[pl.ds(pl.multiple_of(first - wanted, strip), strip), :]

    else:

        @pl.when((wanted >= first) & (wanted < first + strip))
        def _():
            spare[pl.ds(pl.multiple_of(wanted - first, extra_rows), extra_rows), :] += extra[...]

    for step, out in enumerate(outs):
        owner = lax.rem(place[0] - step + tp, tp)
        out[...] = spare[:, pl.ds(pl.multiple_of(owner * width, width), width)].astype(BF16)


def finish(pieces, place, tables, full, extra, gain, weight, tp, *needed):
    rows, wide = pieces[0].shape
    depth = full.shape[1]
    total = weight.shape[1]
    strip = 256
    steps = rows // strip
    width = depth // tp
    nctx = len(pieces)
    by_rows = lambda columns: pl.BlockSpec((strip, columns), lambda i, s: (i, 0))
    grid_spec = pltpu.PrefetchScalarGridSpec(
        num_scalar_prefetch=1,
        grid=(steps,),
        in_specs=[by_rows(wide)] * nctx
        + [by_rows(2 * HEAD_DIM)] * 3
        + [
            by_rows(depth),
            whole(extra.shape),
            whole((1, depth)),
        ]
        + [whole(weight.shape)]
        + anywhere(len(needed)),
        out_specs=[by_rows(width)] * tp
        + [
            by_rows(total),
            whole((1, total)),
            whole((1, depth)),
            whole((1, depth)),
        ],
        scratch_shapes=[pltpu.VMEM((strip, depth), F32)],
    )
    return pl.pallas_call(
        functools.partial(finish_kernel, nctx, tp, len(needed)),
        grid_spec=grid_spec,
        out_shape=[jax.ShapeDtypeStruct((rows, width), BF16)] * tp
        + [
            jax.ShapeDtypeStruct((rows, total), BF16),
            jax.ShapeDtypeStruct((1, total), F32),
            jax.ShapeDtypeStruct((1, depth), F32),
            jax.ShapeDtypeStruct((1, depth), F32),
        ],
        compiler_params=params(),
        cost_estimate=takes(70),
        name="finish",
    )(place, *pieces, *tables, full, extra, gain, weight, *needed)


def join(rings, place, unit):
    parts, tp = len(rings), len(rings[0])
    rows, width = rings[0][0].shape

    def kernel(place, *refs):
        for part in range(parts):
            for step in range(tp):
                owner = lax.rem(place[0] - step + tp, tp)
                refs[-2][owner, part * rows : (part + 1) * rows, :] = refs[part * tp + step][...]
        per, half = width // unit, 1 - lax.rem(place[1], 2)
        for block in range(tp * per // 2):
            index = 2 * block + half if unit % 128 == 0 else 0
            first = pl.multiple_of(lax.rem(index, per) * unit, unit)
            if unit % 128:
                first = 0
            refs[-1][:, block * unit : (block + 1) * unit] = refs[-2][
                lax.div(index, per), :, pl.ds(first, unit)
            ]

    grid_spec = pltpu.PrefetchScalarGridSpec(
        num_scalar_prefetch=1,
        grid=(1,),
        in_specs=[whole((rows, width))] * (parts * tp),
        out_specs=[whole((tp, parts * rows, width)), whole((parts * rows, tp * width // 2))],
    )
    return pl.pallas_call(
        kernel,
        grid_spec=grid_spec,
        out_shape=[
            jax.ShapeDtypeStruct((tp, parts * rows, width), BF16),
            jax.ShapeDtypeStruct((parts * rows, tp * width // 2), BF16),
        ],
        compiler_params=params(),
        cost_estimate=takes(10),
        name="join",
    )(place, *[block for blocks in rings for block in blocks])


def pack_kernel(gate, up, down, out):
    rows = gate.shape[0]
    out[:rows] = gate[...]
    out[rows : 2 * rows] = up[...]
    out[2 * rows :] = jnp.transpose(down[...])


def pack(gate, up, down):
    rows, columns = gate.shape
    return pl.pallas_call(
        pack_kernel,
        out_shape=jax.ShapeDtypeStruct((3 * rows, columns), BF16),
        compiler_params=params(),
        cost_estimate=takes(10),
        name="pack",
    )(gate, up, down)


def contract_rows(left, right):
    return lax.dot_general(left, right, (((0,), (0,)), ((), ())), preferred_element_type=F32)


def pick(stack, index):
    return lax.dynamic_index_in_dim(stack, index, 0, keepdims=False)


def shards(
    nfsdp,
    nctx,
    tp,
    inputs,
    cotangent,
    first_gain,
    first_bias,
    qkv_weight,
    qkv_bias,
    out_weight,
    second_gain,
    second_bias,
    gate_weight,
    up_weight,
    down_weight,
    lengths,
    fill_counts,
):
    data = ("fsdp", "ctx")
    ndata = nfsdp * nctx
    block_rows, width = inputs.shape
    depth = tp * width
    half_depth = depth // 2
    unit = depth // ndata
    tensor_index = lax.axis_index("tp").astype(jnp.int32)
    context_index = lax.axis_index("ctx").astype(jnp.int32)
    fsdp_index = lax.axis_index("fsdp").astype(jnp.int32)
    part_rows = block_rows // tp
    chunk_rows = block_rows // CHUNKS
    head_width = qkv_weight.shape[2]
    piece = head_width // nctx
    wide = 3 * piece

    square = nfsdp == 2 and nctx == 4 and unit % 128 == 0
    place = jnp.stack([tensor_index, context_index, fsdp_index])

    def shift(value, step):
        return lax.ppermute(value, "tp", [(i, (i + step) % tp) for i in range(tp)])

    def swap(value, step):
        return lax.ppermute(value, "ctx", [(i, i ^ step) for i in range(nctx)])

    core_index = context_index % 2
    groups = [list(range(0, ndata, 2)), list(range(1, ndata, 2))]
    def mate(value):
        return swap(value, 1)

    def send(here, near, far, *needed):
        far = swap(far, 2)
        return [here, swap(near, 1), far[0], swap(tie(far[1], *needed), 1)]

    def scatter_half(value, axis):
        return lax.psum_scatter(
            value, data, scatter_dimension=axis, tiled=True, axis_index_groups=groups
        )

    def scatter(value, axis):
        return lax.psum_scatter(value, data, scatter_dimension=axis, tiled=True)

    def cross(value):
        return lax.ppermute(value, "fsdp", [(i, i ^ 1) for i in range(nfsdp)])

    def square_once(parts):
        near, far, low, high = parts
        return total(near, cross(far)), total(low, swap(high, 2))

    def square_twice(first, second):
        first = first[0].astype(F32) + swap(first[1], 2).astype(F32)
        second = second[0].astype(F32) + cross(second[1]).astype(F32)
        return jnp.concatenate([first, second], axis=0)

    def total(left, right):
        return (left.astype(F32) + right.astype(F32)).astype(BF16)

    owners = [(tensor_index - step + tp) % tp for step in range(tp)]

    own_qkv = (
        qkv_weight.reshape(-1, 3, nctx, piece).transpose(0, 2, 1, 3).reshape(-1, 3 * head_width)
    )
    full_qkv = lax.all_gather(own_qkv, data, axis=0, tiled=True)
    own_feed = pack(gate_weight, up_weight, down_weight)
    feed_weights = lax.all_gather(own_feed, data, axis=0, tiled=True).reshape(ndata, 3 * unit, -1)

    validity, position, first_key, last_key = layout(lengths[0], fill_counts[0], block_rows)
    own_position = lax.dynamic_slice_in_dim(position, context_index * block_rows, block_rows, 0)
    tables = rotary_tables(own_position)
    bounds = jnp.stack([first_key, last_key])
    tile_first = first_key[::TILE_Q]
    tile_count = tile_first.shape[0]
    lows = jnp.where(validity[::TILE_Q], tile_first // TILE_K, tile_count * TILE_Q).astype(jnp.int32)
    key_block = jnp.arange(0, nctx * block_rows, TILE_K, dtype=jnp.int32) // block_rows
    ends = (
        key_block * block_rows
        + jnp.sum(
            jnp.where(
                key_block[:, None] == jnp.arange(nctx, dtype=jnp.int32)[None, :],
                fill_counts[0][None, :],
                0,
            ),
            axis=1,
        )
    ).astype(jnp.int32)

    flat_bias = qkv_bias.reshape(3, nctx, piece).transpose(1, 0, 2).reshape(1, -1)
    gain_one, bias_one = first_gain[None], first_bias[None]
    gain_two, bias_two = second_gain[None], second_bias[None]

    rings = [[inputs[c * chunk_rows : (c + 1) * chunk_rows]] for c in range(CHUNKS)]
    share = unit // CHUNKS
    for chunk in range(CHUNKS):
        carried = out_weight.T[chunk * share : (chunk + 1) * share]
        rings[chunk][0] = jnp.concatenate([rings[chunk][0], carried], axis=0)
    for chunk in range(CHUNKS):
        for _ in range(tp - 1):
            rings[chunk].append(shift(rings[chunk][-1], 1))
            if len(rings[chunk]) == 2:
                rings[chunk][-1] = tie(rings[chunk][-1], own_feed)
    all_low, full, low_half, *outgoing, stack = project(
        rings, place, gain_one, bias_one, full_qkv, flat_bias, tables, nctx, unit
    )
    full_out = lax.all_gather(stack, data, axis=1, tiled=True)

    cot = tie(cotangent, *[blocks[-1] for blocks in rings])
    cot_rings = [[cot[c * chunk_rows : (c + 1) * chunk_rows]] for c in range(CHUNKS)]
    for blocks in cot_rings:
        for _ in range(tp - 1):
            blocks.append(shift(blocks[-1], 1))
    pieces = send(*outgoing, *[blocks[max(tp - 2, 0)] for blocks in cot_rings])

    attended, outgoing, logs = attend(
        pieces,
        place[1:2],
        lows,
        ends,
        bounds,
        nctx,
        block_rows,
        feed_weights,
    )
    cot, cot_half = join(cot_rings, place, unit)
    arrived = lax.all_to_all(
        tie(outgoing, *[blocks[-1] for blocks in cot_rings]).reshape(nctx * tp, part_rows, piece),
        ("ctx", "tp"),
        split_axis=0,
        concat_axis=0,
        tiled=True,
    )
    returned, mixed, second_low = mix(
        arrived.reshape(nctx, tp, part_rows, piece),
        full_out,
        full,
        gain_two,
        bias_two,
        place,
        1,
    )

    arrived, held, partials, travelling = second_low, [], [], None
    for step in range(tp):
        coming = shift(arrived, 1) if step < tp - 1 else None
        needed = travelling if step == tp - 1 and step > 2 else []
        *held, first, second = feed(
            arrived, cot, mixed, feed_weights, step, tp, place, held, HALVES, *needed
        )
        partials.append([first, second])
        if step == 1 % tp:
            travelling = partials[step]
        elif step > 1:
            travelling = [
                total(shift(value, 1), kept) for value, kept in zip(travelling, partials[step])
            ]
        if step == 0 and coming is not None:
            coming = tie(coming, partials[0][0])
        arrived = coming
    all_second, all_gate, all_up, hidden, feedforward = held

    last = [shift(value, 1) for value in travelling]
    half_gate = blame(all_second, all_gate, *travelling)
    half_up = blame(all_second, all_up, *travelling)
    grad_heads, grad_mixed, mixed_low, gain_grad_two, shift_grad_two, mixed_half = turn(
        last,
        partials[0],
        mixed,
        cot,
        gain_two,
        full_out,
        place,
        nctx,
        tp,
        unit,
        half_gate,
        half_up,
    )
    grad_heads = lax.all_to_all(
        grad_heads.reshape(nctx * tp, part_rows, piece),
        ("ctx", "tp"),
        split_axis=0,
        concat_axis=0,
        tiled=True,
    ).reshape(nctx * block_rows, piece)

    total_gate = scatter(tie(half_gate, mixed_low), 0).astype(F32)
    half_out = blame(mixed_low, returned)
    total_out = scatter(tie(half_out, grad_heads), 0)
    total_up = scatter(tie(half_up, grad_heads), 0)

    feedforward = tie(feedforward, grad_heads)
    inner = hidden.shape[1]
    both = inner + 3 * head_width
    if square:
        parts = blame_halves(
            (cot, mate(cot_half)), (hidden, mate(hidden)), place, unit, total=both
        )
        half_down = parts[0]
    else:
        half_down = blame(hidden, cot)
        total_down = scatter(half_down, 1).astype(F32)
    layer_out = [pick(feedforward, owners[1 % tp])]
    for step in range(1, tp):
        kept = pick(feedforward, owners[(step + 1) % tp])
        if step == 2:
            layer_out.append(add(shift(layer_out[-1], 1), kept, half_down))
        else:
            layer_out.append(total(shift(layer_out[-1], 1), kept))

    grad_pieces = attend_back(
        pieces, place[1:2], lows, ends, bounds, logs, grad_heads, attended, nctx, block_rows, half_out
    )
    arrived = send(*grad_pieces, *layer_out[max(tp - 2, 0) : tp - 1])
    layer_out = layer_out[-1]
    low_halves = mate(low_half) if square else low_half
    needed = [layer_out, low_halves]
    *partial, all_grad, bias_grad, gain_grad, shift_grad = finish(
        arrived, place, tables, full, grad_mixed, gain_one, full_qkv, tp, *needed
    )
    if square:
        parts = blame_halves(
            (all_low, low_halves),
            (all_grad, mate(all_grad)),
            place,
            unit,
            held=parts,
            offset=inner,
            total=both,
        )
    else:
        parts = []
    def exchange(value, axis, steps, size):
        for step in steps:
            value = value + lax.ppermute(value, axis, [(i, i ^ step) for i in range(size)])
        return value

    def powers(first, size):
        return [1 << bit for bit in range(first, size.bit_length() - 1)]

    small = jnp.concatenate([gain_grad, shift_grad, gain_grad_two, shift_grad_two], axis=1)
    small = sum([shift(small, step) for step in range(1, tp)], small)
    small = jnp.concatenate([bias_grad, small], axis=1)
    travelling, ring_steps = partial[1 % tp], []
    once = square_once(parts) if square else ()
    needed = [[total_gate, total_out, small, *parts], [*once], []]
    for step in range(1, tp):
        travelling = add(
            shift(travelling, 1), partial[(step + 1) % tp], *(needed[step - 1] if step < 4 else [])
        )
        if step == 2:
            out_parts = jnp.swapaxes(
                tie(total_out, travelling).reshape(-1, tp, head_width), 0, 1
            )
            total_out = pick(out_parts, tensor_index).astype(F32)
            for ahead in range(1, tp):
                total_out = total_out + shift(pick(out_parts, (tensor_index + ahead) % tp), ahead).astype(F32)
            total_out = total_out.T
            total_up = tie(total_up, travelling).astype(F32)
            needed[2].extend([total_out, total_up])
        if step == 1:
            small = exchange(tie(small, travelling), "ctx", powers(0, nctx), nctx)
            needed[1].append(small)
        if step == 2:
            small = exchange(tie(small, travelling), "fsdp", powers(0, nfsdp), nfsdp)
            needed[2].append(small)
    grad_inputs = travelling
    if square:
        totals = square_twice(*once)
        total_down, total_qkv = totals[:, :inner].T, totals[:, inner:]
    else:
        total_qkv = scatter(blame(all_low, all_grad), 0).astype(F32)

    total_qkv = (
        total_qkv
        .reshape(-1, nctx, 3, piece)
        .transpose(0, 2, 1, 3)
        .reshape(-1, 3, head_width)
    )


    bias_total, small = small[:, : 3 * head_width], small[:, 3 * head_width :]
    bias_total = bias_total.reshape(nctx, 3, piece).transpose(1, 0, 2).reshape(3, head_width)
    small = small.reshape(4, depth)
    return (
        layer_out,
        grad_inputs,
        small[0],
        small[1],
        total_qkv,
        bias_total,
        total_out,
        small[2],
        small[3],
        total_gate,
        total_up,
        total_down,
    )


def solution(mesh):
    data = ("fsdp", "ctx")
    by_rows = P(data, "tp")
    by_columns = P("tp", data)
    qkv = P(data, None, "tp")
    return jax.shard_map(
        functools.partial(shards, mesh.shape["fsdp"], mesh.shape["ctx"], mesh.shape["tp"]),
        mesh=mesh,
        in_specs=(
            by_rows,
            by_rows,
            P(),
            P(),
            qkv,
            P(None, "tp"),
            by_columns,
            P(),
            P(),
            by_rows,
            by_rows,
            by_columns,
            P("fsdp", None),
            P("fsdp", None),
        ),
        out_specs=(
            by_rows,
            by_rows,
            P(),
            P(),
            qkv,
            P(None, "tp"),
            by_columns,
            P(),
            P(),
            by_rows,
            by_rows,
            by_columns,
        ),
        check_vma=False,
    )
```

```python
import functools

import jax
import jax.numpy as jnp
from jax import lax
from jax.experimental import pallas as pl
from jax.experimental.pallas import tpu as pltpu
from jax.sharding import PartitionSpec as P

HEAD_DIM = 64
ROT = 16
EPSILON = 1e-05
NEGATIVE = -1e30
FLOOR = -1e20
VMEM_LIMIT = 56 * 1024 * 1024
TILE_Q = 512
TILE_K = 512
STRIP = 32
CHUNKS = 2
HALVES = 2

F32 = jnp.float32
BF16 = jnp.bfloat16


def layout(lengths, fill_counts, block_rows):
    blocks_count = fill_counts.shape[0]
    seq_count = lengths.shape[0]
    slot_index = jnp.arange(blocks_count * block_rows, dtype=jnp.int32)
    block_of = slot_index // block_rows
    within = slot_index - block_of * block_rows
    chooser = block_of[:, None] == jnp.arange(blocks_count, dtype=jnp.int32)[None, :]
    fill_here = jnp.sum(jnp.where(chooser, fill_counts[None, :], 0), axis=1)
    before = jnp.cumsum(fill_counts) - fill_counts
    before_here = jnp.sum(jnp.where(chooser, before[None, :], 0), axis=1)
    validity = within < fill_here
    used_index = before_here + within
    seq_ends = jnp.cumsum(lengths)
    sequence = jnp.sum((used_index[:, None] >= seq_ends[None, :]).astype(jnp.int32), axis=1)
    seq_starts = seq_ends - lengths
    picker = sequence[:, None] == jnp.arange(seq_count, dtype=jnp.int32)[None, :]
    start_here = jnp.sum(jnp.where(picker, seq_starts[None, :], 0), axis=1)
    after = before + fill_counts
    start_block = jnp.sum((seq_starts[:, None] >= after[None, :]).astype(jnp.int32), axis=1)
    start_block = jnp.minimum(start_block, blocks_count - 1)
    block_pick = start_block[:, None] == jnp.arange(blocks_count, dtype=jnp.int32)[None, :]
    start_before = jnp.sum(jnp.where(block_pick, before[None, :], 0), axis=1)
    start_slot = start_block * block_rows + seq_starts - start_before
    slot_here = jnp.sum(jnp.where(picker, start_slot[None, :], 0), axis=1)
    first_key = jnp.where(validity, slot_here, 0).astype(jnp.int32)
    last_key = jnp.where(validity, slot_index, -1).astype(jnp.int32)
    return (validity, used_index - start_here, first_key, last_key)


def rotary_tables(position):
    half = ROT // 2
    lane = jnp.arange(2 * HEAD_DIM, dtype=jnp.int32) % HEAD_DIM
    frequency = 10000.0 ** (-(2.0 * (lane % half).astype(F32)) / ROT)
    angles = position.astype(F32)[:, None] * frequency[None, :]
    cosine, sine = jnp.cos(angles), jnp.sin(angles)
    lane = lane[None, :]
    return (
        jnp.where(lane < ROT, cosine, 1.0),
        jnp.where(lane < half, -sine, 0.0),
        jnp.where((lane >= half) & (lane < ROT), sine, 0.0),
    )


def params(**extra):
    return pltpu.CompilerParams(vmem_limit_bytes=VMEM_LIMIT, **extra)


def takes(microseconds):
    return pl.CostEstimate(
        flops=int(microseconds * 1e8), bytes_accessed=0, transcendentals=0
    )


def whole(shape):
    return pl.BlockSpec(shape, lambda *_: (0,) * len(shape))


def anywhere(count):
    return [pl.BlockSpec(memory_space=pl.ANY)] * count


def write_half(out, values, half, unit):
    if unit % 128:
        out[...] = values[:, : out.shape[1]]
        return
    for block in range(out.shape[1] // unit):
        first = pl.multiple_of((2 * block + half) * unit, unit)
        out[:, block * unit : (block + 1) * unit] = values[:, pl.ds(first, unit)]


def dot(left, right):
    return jnp.dot(left, right, preferred_element_type=F32)


def dot_turned(left, right):
    return lax.dot_general(left, right, (((1,), (1,)), ((), ())), preferred_element_type=F32)


def tie(value, *needed):
    def kernel(*refs):
        del refs

    return pl.pallas_call(
        kernel,
        in_specs=anywhere(1 + len(needed)),
        out_specs=pl.BlockSpec(memory_space=pl.ANY),
        out_shape=jax.ShapeDtypeStruct(value.shape, value.dtype),
        input_output_aliases={0: 0},
        name="tie",
    )(value, *needed)


def add_kernel(left, right, *refs):
    refs[-1][...] = (left[...].astype(F32) + right[...].astype(F32)).astype(BF16)


def add(left, right, *needed):
    rows, columns = left.shape
    strip = min(rows, 512)
    block = pl.BlockSpec((strip, columns), lambda i: (i, 0))
    return pl.pallas_call(
        add_kernel,
        grid=(rows // strip,),
        in_specs=[block, block] + anywhere(len(needed)),
        out_specs=block,
        out_shape=jax.ShapeDtypeStruct(left.shape, BF16),
        compiler_params=params(),
        cost_estimate=takes(10),
        name="ring_add",
    )(left, right, *needed)


def project_kernel(tp, chunks, per, unit, place, *refs):
    rings, refs = refs[: tp * chunks], refs[tp * chunks :]
    gain, bias, weight, weight_bias, cosine, sine_up, sine_down = refs[:7]
    low, full, half, here, near, far, stack = refs[7:]
    outs = [here, near] + [far.at[way] for way in range(far.shape[0])]
    rows, width = low.shape[0] // chunks, rings[0].shape[1]
    depth = tp * width
    wide = here.shape[1]
    piece = wide // 3
    step = pl.program_id(0)

    @pl.when(pl.program_id(0) == 0)
    def _():
        strip = 128
        for start in range(0, rows * chunks, strip):
            chunk, first = start // rows, start % rows
            blocks = rings[chunk * tp : (chunk + 1) * tp]
            at = slice(start, start + strip)
            inner = slice(first, first + strip)
            parts = [block[inner, :].astype(F32) for block in blocks]
            centre = sum(jnp.sum(part, axis=1, keepdims=True) for part in parts) / depth
            parts = [part - centre for part in parts]
            spread = sum(jnp.sum(part * part, axis=1, keepdims=True) for part in parts) / depth
            scaling = lax.rsqrt(spread + EPSILON)
            for step in range(tp):
                owner = lax.rem(place[0] - step + tp, tp)
                columns = pl.ds(pl.multiple_of(owner * width, width), width)
                low[at, columns] = (
                    parts[step] * scaling * gain[:, columns] + bias[:, columns]
                ).astype(BF16)
                full[at, columns] = blocks[step][inner, :]
        write_half(half, low, 1 - lax.rem(place[1], 2), unit)
        share = rings[0].shape[0] - rows
        for chunk in range(chunks):
            for step in range(tp):
                owner = lax.rem(place[0] - step + tp, tp)
                stack[owner, chunk * share : (chunk + 1) * share, :] = rings[chunk * tp + step][
                    rows:, :
                ]

    product = dot(low[...], weight[...]) + weight_bias[...]
    groups = []
    for group in range(per):
        parts = []
        for part in range(3):
            first = (group * 3 + part) * piece
            values = product[:, first : first + piece]
            if part < 2:
                values = (
                    values * cosine[...]
                    + pltpu.roll(values, piece - ROT // 2, 1) * sine_up[...]
                    + pltpu.roll(values, ROT // 2, 1) * sine_down[...]
                )
            parts.append(values.astype(BF16))
        groups.append(parts)
    flip = lax.rem(place[1], per)
    for way, out in enumerate(outs):
        for group in range(per):

            @pl.when((step == way // per) & (jnp.bitwise_xor(group, flip) == way % per))
            def _():
                for part in range(3):
                    out[:, part * piece : (part + 1) * piece] = groups[group][part]


def project(rings, place, gain, bias, weight, weight_bias, tables, nctx, unit):
    chunks, tp = len(rings), len(rings[0])
    rows, width = tables[0].shape[0], rings[0][0].shape[1]
    depth = tp * width
    total = weight.shape[1]
    wide = total // nctx
    per = 2 if nctx % 2 == 0 else 1
    grid_spec = pltpu.PrefetchScalarGridSpec(
        num_scalar_prefetch=1,
        grid=(nctx // per,),
        in_specs=[whole(rings[0][0].shape)] * (tp * chunks)
        + [whole((1, depth))] * 2
        + [
            pl.BlockSpec((depth, per * wide), lambda i, s: (0, jnp.bitwise_xor(i, s[1] // per))),
            pl.BlockSpec((1, per * wide), lambda i, s: (0, jnp.bitwise_xor(i, s[1] // per))),
        ]
        + [whole((rows, 2 * HEAD_DIM))] * 3,
        out_specs=[whole((rows, depth))] * 2
        + [whole((rows, depth // 2))]
        + [whole((rows, wide))] * 2
        + [whole((nctx - 2, rows, wide)), whole((tp, unit, width))],
    )
    return pl.pallas_call(
        functools.partial(project_kernel, tp, chunks, per, unit),
        grid_spec=grid_spec,
        out_shape=[
            jax.ShapeDtypeStruct((rows, depth), BF16),
            jax.ShapeDtypeStruct((rows, depth), BF16),
            jax.ShapeDtypeStruct((rows, depth // 2), BF16),
        ]
        + [jax.ShapeDtypeStruct((rows, wide), BF16)] * 2
        + [
            jax.ShapeDtypeStruct((nctx - 2, rows, wide), BF16),
            jax.ShapeDtypeStruct((tp, unit, width), BF16),
        ],
        compiler_params=params(),
        cost_estimate=takes(60),
        name="project",
    )(
        place,
        *[block for blocks in rings for block in blocks],
        gain,
        bias,
        weight,
        weight_bias,
        *tables,
    )


def stack_heads(tile, heads):
    lane = lax.broadcasted_iota(jnp.int32, tile.shape, 1) // HEAD_DIM
    return jnp.concatenate(
        [jnp.where(lane == head, tile, jnp.zeros_like(tile)) for head in range(heads)], axis=0
    )


def load_pieces(place, pieces, nctx, held, block_rows):
    chunk_rows = pieces[0].shape[0]
    chunks = len(pieces) // nctx
    for chunk in range(chunks):
        for step in range(nctx):
            source = jnp.bitwise_xor(place, step)
            first = source * block_rows + chunk * chunk_rows
            held[pl.ds(pl.multiple_of(first, chunk_rows), chunk_rows), :] = pieces[
                chunk * nctx + step
            ][...]


def attend_kernel(nctx, heads, count, extra, block_rows, place, lows, ends, bounds, *refs):
    pieces = refs[:count]
    out, sent, logs, held, turned, total, high, sums, raw, chances = refs[count + extra :]
    tile_q, tile_k = out.shape[0], turned.shape[2]
    width = heads * HEAD_DIM
    index = pl.program_id(0)

    @pl.when(index == 0)
    def _():
        load_pieces(place[0], pieces, nctx, held, block_rows)
        for tile in range(turned.shape[0]):
            turned[tile] = jnp.transpose(held[tile * tile_k : (tile + 1) * tile_k, 2 * width :])

    query_rows = pl.ds(pl.multiple_of(index * tile_q, tile_q), tile_q)
    queries = stack_heads(held[query_rows, :width] * jnp.asarray(HEAD_DIM**-0.5, BF16), heads)
    total[...] = jnp.zeros_like(total)
    high[...] = jnp.full_like(high, FLOOR)
    sums[...] = jnp.zeros_like(sums)
    first_key, last_key = bounds[0:1, :], bounds[1:2, :]

    def one(tile, _):
        start = tile * tile_k
        keys = held[pl.ds(pl.multiple_of(start, tile_k), tile_k), width : 2 * width]
        last = jnp.minimum(last_key, ends[tile] - 1) - start
        first = first_key - start
        for head in range(heads):
            raw[head] = dot_turned(keys, queries[head * tile_q : (head + 1) * tile_q])
        for head in range(heads):
            peaks = jnp.broadcast_to(high[head], (8, tile_q))
            for begin in range(0, tile_k, STRIP):
                scores = raw[head, begin : begin + STRIP, :]
                row = lax.broadcasted_iota(jnp.int32, scores.shape, 0) + begin
                scores = jnp.where((row <= last) & (row >= first), scores, NEGATIVE)
                raw[head, begin : begin + STRIP, :] = scores
                for group in range(0, STRIP, 8):
                    peaks = jnp.maximum(peaks, scores[group : group + 8])
            highest = jnp.max(peaks, axis=0, keepdims=True)
            partial = jnp.zeros((8, tile_q), F32)
            for begin in range(0, tile_k, STRIP):
                raised = jnp.exp(raw[head, begin : begin + STRIP, :] - highest)
                chances[head, begin : begin + STRIP, :] = raised.astype(BF16)
                for group in range(0, STRIP, 8):
                    partial = partial + raised[group : group + 8]
            shrink = jnp.exp(high[head] - highest)
            sums[head] = sums[head] * shrink + jnp.sum(partial, axis=0, keepdims=True)
            values = turned[tile, head * HEAD_DIM : (head + 1) * HEAD_DIM, :]
            total[head] = total[head] * shrink + dot(values, chances[head])
            high[head] = highest
        return 0

    upper = (index * tile_q + tile_q - 1) // tile_k + 1
    lax.fori_loop(lows[index], upper, one, 0)
    results = []
    for head in range(heads):
        found = sums[head] > 0.0
        safe = jnp.where(found, sums[head], 1.0)
        results.append(total[head] * jnp.where(found, 1.0 / safe, 0.0))
        logs[head : head + 1, :] = jnp.where(found, high[head] + jnp.log(safe), 0.0)
    result = jnp.transpose(jnp.concatenate(results, axis=0)).astype(BF16)
    out[...] = result
    sent[...] = result


def attend(pieces, place, lows, ends, bounds, nctx, block_rows, *needed):
    total_rows = nctx * block_rows
    width = pieces[0].shape[1] // 3
    heads = width // HEAD_DIM
    steps = total_rows // TILE_Q
    grid_spec = pltpu.PrefetchScalarGridSpec(
        num_scalar_prefetch=3,
        grid=(steps,),
        in_specs=[pl.BlockSpec((2, TILE_Q), lambda i, *_: (0, i))]
        + [whole(piece.shape) for piece in pieces]
        + anywhere(len(needed)),
        out_specs=[
            pl.BlockSpec((TILE_Q, width), lambda i, *_: (i, 0)),
            pl.BlockSpec((TILE_Q, width), lambda i, *_: (i, 0)),
            pl.BlockSpec((heads, TILE_Q), lambda i, *_: (0, i)),
        ],
        scratch_shapes=[
            pltpu.VMEM((total_rows, 3 * width), BF16),
            pltpu.VMEM((total_rows // TILE_K, width, TILE_K), BF16),
            pltpu.VMEM((heads, HEAD_DIM, TILE_Q), F32),
            pltpu.VMEM((heads, 1, TILE_Q), F32),
            pltpu.VMEM((heads, 1, TILE_Q), F32),
            pltpu.VMEM((heads, TILE_K, TILE_Q), F32),
            pltpu.VMEM((heads, TILE_K, TILE_Q), BF16),
        ],
    )
    return pl.pallas_call(
        functools.partial(attend_kernel, nctx, heads, len(pieces), len(needed), block_rows),
        grid_spec=grid_spec,
        out_shape=[
            jax.ShapeDtypeStruct((total_rows, width), BF16),
            jax.ShapeDtypeStruct((total_rows, width), BF16),
            jax.ShapeDtypeStruct((heads, total_rows), F32),
        ],
        compiler_params=params(),
        cost_estimate=takes(200),
        name="attend",
    )(place, lows, ends, bounds, *pieces, *needed)


def attend_back_kernel(
    nctx, heads, count, extra, block_rows, place, lows, ends, bounds, logs, *refs
):
    pieces, refs = refs[:count], refs[count:]
    grad, attended, refs = refs[0], refs[1], refs[2 + extra :]
    here, near, far, refs = *refs[:3], refs[3:]
    held, turned, grad_keys, grad_values, grad_query, raw, raw_grad, chances, steps, merged = refs
    tile_q, tile_k = grad.shape[0], turned.shape[2]
    width = grad.shape[1]
    index = pl.program_id(0)
    scale = jnp.asarray(HEAD_DIM**-0.5, BF16)

    @pl.when(index == 0)
    def _():
        load_pieces(place[0], pieces, nctx, held, block_rows)
        for tile in range(turned.shape[0]):
            turned[tile] = jnp.transpose(
                held[tile * tile_k : (tile + 1) * tile_k, width : 2 * width]
            )
        grad_keys[...] = jnp.zeros_like(grad_keys)
        grad_values[...] = jnp.zeros_like(grad_values)

    query_rows = pl.ds(pl.multiple_of(index * tile_q, tile_q), tile_q)
    queries = stack_heads(held[query_rows, :width] * scale, heads)
    incoming = stack_heads(grad[...], heads)
    product = jnp.transpose(grad[...].astype(F32) * attended[...].astype(F32))
    centres = [
        jnp.sum(product[head * HEAD_DIM : (head + 1) * HEAD_DIM, :], axis=0, keepdims=True)
        for head in range(heads)
    ]
    first_key, last_key = bounds[0:1, :], bounds[1:2, :]
    grad_query[...] = jnp.zeros_like(grad_query)

    def one(tile, _):
        start = tile * tile_k
        key_rows = pl.ds(pl.multiple_of(start, tile_k), tile_k)
        last = jnp.minimum(last_key, ends[tile] - 1) - start
        first = first_key - start
        by_head = [slice(head * tile_q, (head + 1) * tile_q) for head in range(heads)]
        for head in range(heads):
            raw[head] = dot_turned(held[key_rows, width : 2 * width], queries[by_head[head]])
            raw_grad[head] = dot_turned(held[key_rows, 2 * width :], incoming[by_head[head]])
        for head in range(heads):
            for begin in range(0, tile_k, STRIP):
                at = slice(begin, begin + STRIP)
                row = lax.broadcasted_iota(jnp.int32, (STRIP, tile_q), 0) + begin
                allowed = (row <= last) & (row >= first)
                scores = raw[head, at, :] - logs[head : head + 1, :]
                chance = jnp.exp(jnp.where(allowed, scores, NEGATIVE))
                chances[head, at, :] = chance.astype(BF16)
                steps[head, at, :] = (chance * (raw_grad[head, at, :] - centres[head])).astype(BF16)
            grad_values[key_rows, :] += dot(chances[head], incoming[by_head[head]])
            grad_keys[key_rows, :] += dot(steps[head], queries[by_head[head]])
            keys = turned[tile, head * HEAD_DIM : (head + 1) * HEAD_DIM, :]
            grad_query[head] += dot(keys, steps[head])
        return 0

    upper = (index * tile_q + tile_q - 1) // tile_k + 1
    lax.fori_loop(lows[index], upper, one, 0)
    result = jnp.concatenate([grad_query[head] for head in range(heads)], axis=0)
    merged[query_rows, :width] = (jnp.transpose(result) * HEAD_DIM**-0.5).astype(BF16)

    @pl.when(index == pl.num_programs(0) - 1)
    def _():
        merged[:, width : 2 * width] = grad_keys[...].astype(BF16)
        merged[:, 2 * width :] = grad_values[...].astype(BF16)
        outs = [here, near] + [far.at[way] for way in range(nctx - 2)]
        for way, out in enumerate(outs):
            first = jnp.bitwise_xor(place[0], way) * block_rows
            out[...] = merged[pl.ds(pl.multiple_of(first, block_rows), block_rows), :]


def attend_back(pieces, place, lows, ends, bounds, logs, grad, attended, nctx, block_rows, *needed):
    total_rows, width = grad.shape
    heads = width // HEAD_DIM
    by_tile = pl.BlockSpec((TILE_Q, width), lambda i, *_: (i, 0))
    sent = (block_rows, 3 * width)
    sent = [sent, sent, (nctx - 2, *sent)]
    grid_spec = pltpu.PrefetchScalarGridSpec(
        num_scalar_prefetch=3,
        grid=(total_rows // TILE_Q,),
        in_specs=[
            pl.BlockSpec((2, TILE_Q), lambda i, *_: (0, i)),
            pl.BlockSpec((heads, TILE_Q), lambda i, *_: (0, i)),
        ]
        + [whole(piece.shape) for piece in pieces]
        + [by_tile] * 2
        + anywhere(len(needed)),
        out_specs=[whole(shape) for shape in sent],
        scratch_shapes=[
            pltpu.VMEM((total_rows, 3 * width), BF16),
            pltpu.VMEM((total_rows // TILE_K, width, TILE_K), BF16),
            pltpu.VMEM((total_rows, width), F32),
            pltpu.VMEM((total_rows, width), F32),
            pltpu.VMEM((heads, HEAD_DIM, TILE_Q), F32),
            pltpu.VMEM((heads, TILE_K, TILE_Q), F32),
            pltpu.VMEM((heads, TILE_K, TILE_Q), F32),
            pltpu.VMEM((heads, TILE_K, TILE_Q), BF16),
            pltpu.VMEM((heads, TILE_K, TILE_Q), BF16),
            pltpu.VMEM((total_rows, 3 * width), BF16),
        ],
    )
    return pl.pallas_call(
        functools.partial(
            attend_back_kernel, nctx, heads, len(pieces), len(needed), block_rows
        ),
        grid_spec=grid_spec,
        out_shape=[jax.ShapeDtypeStruct(shape, BF16) for shape in sent],
        compiler_params=params(),
        cost_estimate=takes(250),
        name="attend_back",
    )(place, lows, ends, bounds, logs, *pieces, grad, attended, *needed)


def mix_kernel(nctx, count, place, heads_in, weight, source, gain, bias, *refs):
    returned, mixed, *lows = refs[count:]
    rows, depth = mixed.shape
    step = pl.program_id(0)
    left = jnp.concatenate([heads_in[c, 0] for c in range(nctx)], axis=1)
    returned[...] = left

    @pl.when(step == 0)
    def _():
        mixed[...] = source[...].astype(F32)

    mixed[...] += dot_turned(left, weight[0])

    @pl.when(step == pl.num_programs(0) - 1)
    def _():
        values = mixed[...]
        values = values - jnp.mean(values, axis=1, keepdims=True)
        scaling = lax.rsqrt(jnp.mean(values * values, axis=1, keepdims=True) + EPSILON)
        values = (values * scaling * gain[...] + bias[...]).astype(BF16)
        part_rows = lows[0].shape[0]
        for part, low in enumerate(lows):
            low[...] = values[part * part_rows : (part + 1) * part_rows]


def mix(heads_in, weight, full, gain, bias, place, parts, *needed):
    nctx, tp, rows, piece = heads_in.shape
    depth = full.shape[1]
    head_width = nctx * piece
    grid_spec = pltpu.PrefetchScalarGridSpec(
        num_scalar_prefetch=1,
        grid=(tp,),
        in_specs=[
            pl.BlockSpec((nctx, 1, rows, piece), lambda k, s: (0, k, 0, 0)),
            pl.BlockSpec((1, depth, head_width), lambda k, s: (k, 0, 0)),
            pl.BlockSpec((rows, depth), lambda k, s: (s[0], 0)),
            whole((1, depth)),
            whole((1, depth)),
        ]
        + anywhere(len(needed)),
        out_specs=[
            pl.BlockSpec((rows, head_width), lambda k, s: (0, k)),
            whole((rows, depth)),
        ]
        + [whole((rows // parts, depth))] * parts,
    )
    return pl.pallas_call(
        functools.partial(mix_kernel, nctx, len(needed)),
        grid_spec=grid_spec,
        out_shape=[
            jax.ShapeDtypeStruct((rows, tp * head_width), BF16),
            jax.ShapeDtypeStruct((rows, depth), F32),
        ]
        + [jax.ShapeDtypeStruct((rows // parts, depth), BF16)] * parts,
        compiler_params=params(),
        cost_estimate=takes(50),
        name="mix",
    )(place, heads_in, weight, full, gain, bias, *needed)


def feed_kernel(cuts, parts, tp, first_one, place, low, cot, mixed, source, *refs):
    refs = refs[-(5 + parts + 4) :]
    kept, grad_gate, grad_up, hidden, out = refs[:5]
    partials, held, sems = refs[5 : 5 + parts], refs[-4:-1], refs[-1]
    unit = source.shape[1] // 3
    width = out.shape[2]

    def copies(index):
        first, size = cuts[index]
        at = pl.ds(first, size)
        return [
            pltpu.make_async_copy(
                source.at[:, pl.ds(which * unit, unit), at],
                held[which].at[:, :, at],
                sems.at[index * 3 + which],
            )
            for which in range(3)
        ]

    for index in range(len(cuts)):
        for copy in copies(index):
            copy.start()
    kept[...] = low[...]
    rows, depth = kept.shape[0] // parts, kept.shape[1]
    grads = jnp.concatenate([cot[block] for block in range(tp)], axis=1)
    for index, (first, size) in enumerate(cuts):
        for copy in copies(index):
            copy.wait()
        at = slice(first, first + size)
        gate_weight, up_weight, down_weight = [w[:, :, at].reshape(depth, size) for w in held]
        gate = dot(kept[...], gate_weight)
        up = dot(kept[...], up_weight)
        sigma = 1.0 / (1.0 + jnp.exp(-gate))
        active = gate * sigma
        hidden[:, at] = (active * up).astype(BF16)
        grad = dot(grads, down_weight)
        grad_gate[:, at] = (grad * up * sigma * (1.0 + gate * (1.0 - sigma))).astype(BF16)
        grad_up[:, at] = (grad * active).astype(BF16)
    gate_weight, up_weight, down_weight = [w[...].reshape(depth, w.shape[2]) for w in held]
    product = dot_turned(grad_gate[...], gate_weight) + dot_turned(grad_up[...], up_weight)
    for part in range(parts):
        partials[part][...] = product[part * rows : (part + 1) * rows].astype(BF16)
    values = dot_turned(hidden[...], down_weight)
    if first_one:
        values = values + mixed[...]
    for block in range(tp):
        out[block] = values[:, block * width : (block + 1) * width].astype(BF16)


def feed(low, cot, mixed, weights, step, tp, place, held, parts, *needed):
    rows, depth = low.shape
    part_rows = rows // parts
    blocks, triple, hidden = weights.shape
    cuts = []
    while sum(size for _, size in cuts) < hidden:
        first = sum(size for _, size in cuts)
        cuts.append((first, min(512, hidden - first)))
    by_owner = lambda columns: pl.BlockSpec(
        (rows, columns), lambda i, s: (lax.rem(s[0] - step + tp, tp), 0)
    )
    width = depth // tp
    blocks_of_owner = pl.BlockSpec(
        (tp, rows, width), lambda i, s: (0, lax.rem(s[0] - step + tp, tp), 0)
    )
    grid_spec = pltpu.PrefetchScalarGridSpec(
        num_scalar_prefetch=1,
        grid=(1,),
        in_specs=[whole((rows, depth)), blocks_of_owner, whole(mixed.shape)]
        + anywhere(1 + len(held) + len(needed)),
        out_specs=[by_owner(depth)]
        + [by_owner(hidden)] * 3
        + [blocks_of_owner]
        + [whole((part_rows, depth))] * parts,
        scratch_shapes=[pltpu.VMEM((blocks, triple // 3, hidden), BF16)] * 3
        + [pltpu.SemaphoreType.DMA((3 * len(cuts),))],
    )
    return pl.pallas_call(
        functools.partial(feed_kernel, tuple(cuts), parts, tp, step == 0),
        grid_spec=grid_spec,
        out_shape=[
            jax.ShapeDtypeStruct((tp * rows, columns), BF16)
            for columns in (depth, hidden, hidden, hidden)
        ]
        + [jax.ShapeDtypeStruct((tp, tp * rows, width), BF16)]
        + [jax.ShapeDtypeStruct((part_rows, depth), BF16)] * parts,
        input_output_aliases={5 + index: index for index in range(len(held))},
        compiler_params=params(),
        cost_estimate=takes(100),
        name="feed",
    )(place, low, cot, mixed, weights, *held, *needed)


def blame_halves(lefts, rights, place, unit, *needed, held=(), offset=0, total=None):
    rows, other = rights[0].shape
    picked = lefts[1].shape[1] // unit
    chosen = pl.BlockSpec((rows, unit), lambda j, s: (0, 2 * (j ^ s[3]) + s[1] % 2))
    if lefts[0].ndim == 3:
        per = lefts[0].shape[2] // unit
        chosen = pl.BlockSpec(
            (1, rows, unit),
            lambda j, s: (
                (2 * (j ^ s[3]) + s[1] % 2) // per,
                0,
                lax.rem(2 * (j ^ s[3]) + s[1] % 2, per),
            ),
        )
    cut = pl.BlockSpec((rows, unit), lambda j, s: (0, j ^ s[3]))
    shapes = [(2, unit // 2, total or other)] * 4

    def kernel(place, left_here, left_there, right_here, right_there, *refs):
        outs, spare, sems = refs[len(held) + len(needed) : -2], refs[-2], refs[-1]
        product = 0.0
        for left, right in ((left_here, right_here), (left_there, right_there)):
            ours = left[0] if len(left.shape) == 3 else left[...]
            product = product + lax.dot_general(
                ours, right[...], (((0,), (0,)), ((), ())), preferred_element_type=F32
            )
        product = product.astype(BF16)
        for j in range(picked):

            @pl.when(pl.program_id(0) == j)
            def _():
                first, second = spare.at[j // 2, j % 2], spare.at[2 + j % 2, j // 2]
                first[...], second[...] = product[: unit // 2], product[unit // 2 :]

        @pl.when(pl.program_id(0) == picked - 1)
        def _():
            moves = [
                pltpu.make_async_copy(
                    spare.at[index], out.at[:, :, pl.ds(offset, other)], sems.at[index]
                )
                for index, out in enumerate(outs)
            ]
            for move in moves:
                move.start()
            for move in moves:
                move.wait()

    grid_spec = pltpu.PrefetchScalarGridSpec(
        num_scalar_prefetch=1,
        grid=(picked,),
        in_specs=[chosen, cut]
        + [whole((rows, other))] * 2
        + anywhere(len(held) + len(needed)),
        out_specs=anywhere(4),
        scratch_shapes=[
            pltpu.VMEM((4, 2, unit // 2, other), BF16),
            pltpu.SemaphoreType.DMA((4,)),
        ],
    )
    place = jnp.concatenate([place, place[2:3] * 2 + place[1:2] // 2])
    return pl.pallas_call(
        kernel,
        grid_spec=grid_spec,
        out_shape=[jax.ShapeDtypeStruct(shape, BF16) for shape in shapes],
        input_output_aliases={5 + index: index for index in range(len(held))},
        compiler_params=params(),
        cost_estimate=takes(60),
        name="blame_halves",
    )(place, *lefts, *rights, *held, *needed)


def blame(left, right, *needed):
    rows, columns = left.shape
    if right.ndim == 3:
        steps, other = right.shape[0], right.shape[2]
        in_specs = [whole((rows, columns)), pl.BlockSpec((1, rows, other), lambda j: (j, 0, 0))]
        target, shape = pl.BlockSpec((columns, other), lambda j: (0, j)), (columns, steps * other)
    else:
        steps, other = 4, right.shape[1]
        in_specs = [pl.BlockSpec((rows, columns // steps), lambda j: (0, j)), whole((rows, other))]
        target, shape = pl.BlockSpec((columns // steps, other), lambda j: (j, 0)), (columns, other)

    def kernel(left, right, *refs):
        theirs = right[0] if len(right.shape) == 3 else right[...]
        refs[-1][...] = lax.dot_general(
            left[...], theirs, (((0,), (0,)), ((), ())), preferred_element_type=F32
        ).astype(BF16)

    return pl.pallas_call(
        kernel,
        grid=(steps,),
        in_specs=in_specs + anywhere(len(needed)),
        out_specs=target,
        out_shape=jax.ShapeDtypeStruct(shape, BF16),
        compiler_params=params(),
        cost_estimate=takes(60),
        name="blame",
    )(left, right, *needed)


def turn_kernel(nctx, count, parts, unit, place, *refs):
    arrived, own = refs[:parts], refs[parts : 2 * parts]
    mixed, cot, gain = refs[2 * parts : 2 * parts + 3]
    weight, refs = refs[2 * parts + 3], refs[2 * parts + 4 + count :]
    out, grad_mixed, grad_low, gain_grad, shift_grad, half = refs
    rows, depth = mixed.shape
    piece = out.shape[3]

    @pl.when(pl.program_id(0) == 0)
    def _():
        incoming = jnp.concatenate(
            [there[...].astype(F32) + here[...].astype(F32) for there, here in zip(arrived, own)]
        )
        values = mixed[...]
        values = values - jnp.mean(values, axis=1, keepdims=True)
        scaling = lax.rsqrt(jnp.mean(values * values, axis=1, keepdims=True) + EPSILON)
        normed = values * scaling
        shift_grad[...] = jnp.sum(incoming, axis=0, keepdims=True)
        gain_grad[...] = jnp.sum(incoming * normed, axis=0, keepdims=True)
        scaled = incoming * gain[...]
        grads = jnp.concatenate([cot[block] for block in range(cot.shape[0])], axis=1)
        total = grads.astype(F32) + scaling * (
            scaled
            - jnp.mean(scaled, axis=1, keepdims=True)
            - normed * jnp.mean(scaled * normed, axis=1, keepdims=True)
        )
        grad_mixed[...] = total
        grad_low[...] = total.astype(BF16)
        write_half(half, grad_low, 1 - lax.rem(place[1], 2), unit)

    product = dot(grad_low[...], weight[0])
    for c in range(nctx):
        out[c, 0] = product[:, c * piece : (c + 1) * piece].astype(BF16)


def turn(arrived, own, mixed, cot, gain, weight, place, nctx, tp, unit, *needed):
    rows, depth = mixed.shape
    parts = len(arrived)
    head_width = weight.shape[2]
    piece = head_width // nctx
    grid_spec = pltpu.PrefetchScalarGridSpec(
        num_scalar_prefetch=1,
        grid=(tp,),
        in_specs=[whole((rows // parts, depth))] * (2 * parts)
        + [whole((rows, depth))]
        + [
            pl.BlockSpec((tp, rows, depth // tp), lambda k, s: (0, s[0], 0)),
            whole((1, depth)),
            pl.BlockSpec((1, depth, head_width), lambda k, s: (k, 0, 0)),
        ]
        + anywhere(len(needed)),
        out_specs=[
            pl.BlockSpec((nctx, 1, rows, piece), lambda k, s: (0, k, 0, 0)),
            whole((rows, depth)),
            whole((rows, depth)),
            whole((1, depth)),
            whole((1, depth)),
            whole((rows, depth // 2)),
        ],
    )
    return pl.pallas_call(
        functools.partial(turn_kernel, nctx, len(needed), parts, unit),
        grid_spec=grid_spec,
        out_shape=[
            jax.ShapeDtypeStruct((nctx, tp, rows, piece), BF16),
            jax.ShapeDtypeStruct((rows, depth), F32),
            jax.ShapeDtypeStruct((rows, depth), BF16),
            jax.ShapeDtypeStruct((1, depth), F32),
            jax.ShapeDtypeStruct((1, depth), F32),
            jax.ShapeDtypeStruct((rows, depth // 2), BF16),
        ],
        compiler_params=params(),
        cost_estimate=takes(60),
        name="turn",
    )(place, *arrived, *own, mixed, cot, gain, weight, *needed)


def finish_kernel(nctx, tp, extra_count, place, *refs):
    pieces = refs[:nctx]
    cosine, sine_up, sine_down, full, extra, gain = refs[nctx : nctx + 6]
    weight, refs = refs[nctx + 6], refs[nctx + 7 + extra_count :]
    outs = refs[:tp]
    low, bias_grad, gain_grad, shift_grad, spare = refs[tp:]
    rows, wide = pieces[0].shape
    piece = wide // 3
    width = outs[0].shape[1]
    strip = spare.shape[0]
    extra_rows = extra.shape[0]

    @pl.when(pl.program_id(0) == 0)
    def _():
        bias_grad[...] = jnp.zeros_like(bias_grad)
        gain_grad[...] = jnp.zeros_like(gain_grad)
        shift_grad[...] = jnp.zeros_like(shift_grad)

    for step in range(nctx):
        source = jnp.bitwise_xor(place[1], step)
        for part in range(3):
            values = pieces[step][:, part * piece : (part + 1) * piece].astype(F32)
            if part < 2:
                values = (
                    values * cosine[...]
                    - pltpu.roll(values, piece - ROT // 2, 1) * sine_up[...]
                    - pltpu.roll(values, ROT // 2, 1) * sine_down[...]
                )
            columns = pl.ds(pl.multiple_of(source * wide + part * piece, piece), piece)
            bias_grad[:, columns] += jnp.sum(values, axis=0, keepdims=True)
            low[:, columns] = values.astype(BF16)

    incoming = dot_turned(low[...], weight[...])
    source = full[...].astype(F32)
    source = source - jnp.mean(source, axis=1, keepdims=True)
    scaling = lax.rsqrt(jnp.mean(source * source, axis=1, keepdims=True) + EPSILON)
    normed = source * scaling
    shift_grad[...] += jnp.sum(incoming, axis=0, keepdims=True)
    gain_grad[...] += jnp.sum(incoming * normed, axis=0, keepdims=True)
    scaled = incoming * gain[...]
    spare[...] = scaling * (
        scaled
        - jnp.mean(scaled, axis=1, keepdims=True)
        - normed * jnp.mean(scaled * normed, axis=1, keepdims=True)
    )
    first = pl.program_id(0) * strip
    wanted = place[0] * extra_rows

    if strip <= extra_rows:

        @pl.when((first >= wanted) & (first < wanted + extra_rows))
        def _():
            spare[...] += extra[pl.ds(pl.multiple_of(first - wanted, strip), strip), :]

    else:

        @pl.when((wanted >= first) & (wanted < first + strip))
        def _():
            spare[pl.ds(pl.multiple_of(wanted - first, extra_rows), extra_rows), :] += extra[...]

    for step, out in enumerate(outs):
        owner = lax.rem(place[0] - step + tp, tp)
        out[...] = spare[:, pl.ds(pl.multiple_of(owner * width, width), width)].astype(BF16)


def finish(pieces, place, tables, full, extra, gain, weight, tp, *needed):
    rows, wide = pieces[0].shape
    depth = full.shape[1]
    total = weight.shape[1]
    strip = 256
    steps = rows // strip
    width = depth // tp
    nctx = len(pieces)
    by_rows = lambda columns: pl.BlockSpec((strip, columns), lambda i, s: (i, 0))
    grid_spec = pltpu.PrefetchScalarGridSpec(
        num_scalar_prefetch=1,
        grid=(steps,),
        in_specs=[by_rows(wide)] * nctx
        + [by_rows(2 * HEAD_DIM)] * 3
        + [
            by_rows(depth),
            whole(extra.shape),
            whole((1, depth)),
        ]
        + [whole(weight.shape)]
        + anywhere(len(needed)),
        out_specs=[by_rows(width)] * tp
        + [
            by_rows(total),
            whole((1, total)),
            whole((1, depth)),
            whole((1, depth)),
        ],
        scratch_shapes=[pltpu.VMEM((strip, depth), F32)],
    )
    return pl.pallas_call(
        functools.partial(finish_kernel, nctx, tp, len(needed)),
        grid_spec=grid_spec,
        out_shape=[jax.ShapeDtypeStruct((rows, width), BF16)] * tp
        + [
            jax.ShapeDtypeStruct((rows, total), BF16),
            jax.ShapeDtypeStruct((1, total), F32),
            jax.ShapeDtypeStruct((1, depth), F32),
            jax.ShapeDtypeStruct((1, depth), F32),
        ],
        compiler_params=params(),
        cost_estimate=takes(70),
        name="finish",
    )(place, *pieces, *tables, full, extra, gain, weight, *needed)


def join(rings, place, unit):
    parts, tp = len(rings), len(rings[0])
    rows, width = rings[0][0].shape

    def kernel(place, *refs):
        for part in range(parts):
            for step in range(tp):
                owner = lax.rem(place[0] - step + tp, tp)
                refs[-2][owner, part * rows : (part + 1) * rows, :] = refs[part * tp + step][...]
        per, half = width // unit, 1 - lax.rem(place[1], 2)
        for block in range(tp * per // 2):
            index = 2 * block + half if unit % 128 == 0 else 0
            first = pl.multiple_of(lax.rem(index, per) * unit, unit)
            if unit % 128:
                first = 0
            refs[-1][:, block * unit : (block + 1) * unit] = refs[-2][
                lax.div(index, per), :, pl.ds(first, unit)
            ]

    grid_spec = pltpu.PrefetchScalarGridSpec(
        num_scalar_prefetch=1,
        grid=(1,),
        in_specs=[whole((rows, width))] * (parts * tp),
        out_specs=[whole((tp, parts * rows, width)), whole((parts * rows, tp * width // 2))],
    )
    return pl.pallas_call(
        kernel,
        grid_spec=grid_spec,
        out_shape=[
            jax.ShapeDtypeStruct((tp, parts * rows, width), BF16),
            jax.ShapeDtypeStruct((parts * rows, tp * width // 2), BF16),
        ],
        compiler_params=params(),
        cost_estimate=takes(10),
        name="join",
    )(place, *[block for blocks in rings for block in blocks])


def pack_kernel(gate, up, down, out):
    rows = gate.shape[0]
    out[:rows] = gate[...]
    out[rows : 2 * rows] = up[...]
    out[2 * rows :] = jnp.transpose(down[...])


def pack(gate, up, down):
    rows, columns = gate.shape
    return pl.pallas_call(
        pack_kernel,
        out_shape=jax.ShapeDtypeStruct((3 * rows, columns), BF16),
        compiler_params=params(),
        cost_estimate=takes(10),
        name="pack",
    )(gate, up, down)


def contract_rows(left, right):
    return lax.dot_general(left, right, (((0,), (0,)), ((), ())), preferred_element_type=F32)


def pick(stack, index):
    return lax.dynamic_index_in_dim(stack, index, 0, keepdims=False)


def shards(
    nfsdp,
    nctx,
    tp,
    inputs,
    cotangent,
    first_gain,
    first_bias,
    qkv_weight,
    qkv_bias,
    out_weight,
    second_gain,
    second_bias,
    gate_weight,
    up_weight,
    down_weight,
    lengths,
    fill_counts,
):
    data = ("fsdp", "ctx")
    ndata = nfsdp * nctx
    block_rows, width = inputs.shape
    depth = tp * width
    half_depth = depth // 2
    unit = depth // ndata
    tensor_index = lax.axis_index("tp").astype(jnp.int32)
    context_index = lax.axis_index("ctx").astype(jnp.int32)
    fsdp_index = lax.axis_index("fsdp").astype(jnp.int32)
    part_rows = block_rows // tp
    chunk_rows = block_rows // CHUNKS
    head_width = qkv_weight.shape[2]
    piece = head_width // nctx
    wide = 3 * piece

    square = nfsdp == 2 and nctx == 4 and unit % 128 == 0
    place = jnp.stack([tensor_index, context_index, fsdp_index])

    def shift(value, step):
        return lax.ppermute(value, "tp", [(i, (i + step) % tp) for i in range(tp)])

    def swap(value, step):
        return lax.ppermute(value, "ctx", [(i, i ^ step) for i in range(nctx)])

    core_index = context_index % 2
    groups = [list(range(0, ndata, 2)), list(range(1, ndata, 2))]
    def mate(value):
        return swap(value, 1)

    def send(here, near, far, *needed):
        far = swap(far, 2)
        return [here, swap(near, 1), far[0], swap(tie(far[1], *needed), 1)]

    def scatter_half(value, axis):
        return lax.psum_scatter(
            value, data, scatter_dimension=axis, tiled=True, axis_index_groups=groups
        )

    def scatter(value, axis):
        return lax.psum_scatter(value, data, scatter_dimension=axis, tiled=True)

    def cross(value):
        return lax.ppermute(value, "fsdp", [(i, i ^ 1) for i in range(nfsdp)])

    def square_once(parts, last):
        near, far, low, high = parts
        far, high = cross(far), swap(high, 2)
        return total(tie(near, last), far), total(tie(low, last), high)

    def square_twice(first, second):
        first = first[0].astype(F32) + swap(first[1], 2).astype(F32)
        second = second[0].astype(F32) + cross(second[1]).astype(F32)
        return jnp.concatenate([first, second], axis=0)

    def total(left, right):
        return (left.astype(F32) + right.astype(F32)).astype(BF16)

    owners = [(tensor_index - step + tp) % tp for step in range(tp)]

    own_qkv = (
        qkv_weight.reshape(-1, 3, nctx, piece).transpose(0, 2, 1, 3).reshape(-1, 3 * head_width)
    )
    full_qkv = lax.all_gather(own_qkv, data, axis=0, tiled=True)
    own_feed = pack(gate_weight, up_weight, down_weight)
    feed_weights = lax.all_gather(own_feed, data, axis=0, tiled=True).reshape(ndata, 3 * unit, -1)

    validity, position, first_key, last_key = layout(lengths[0], fill_counts[0], block_rows)
    own_position = lax.dynamic_slice_in_dim(position, context_index * block_rows, block_rows, 0)
    tables = rotary_tables(own_position)
    bounds = jnp.stack([first_key, last_key])
    tile_first = first_key[::TILE_Q]
    tile_count = tile_first.shape[0]
    lows = jnp.where(validity[::TILE_Q], tile_first // TILE_K, tile_count * TILE_Q).astype(jnp.int32)
    key_block = jnp.arange(0, nctx * block_rows, TILE_K, dtype=jnp.int32) // block_rows
    ends = (
        key_block * block_rows
        + jnp.sum(
            jnp.where(
                key_block[:, None] == jnp.arange(nctx, dtype=jnp.int32)[None, :],
                fill_counts[0][None, :],
                0,
            ),
            axis=1,
        )
    ).astype(jnp.int32)

    flat_bias = qkv_bias.reshape(3, nctx, piece).transpose(1, 0, 2).reshape(1, -1)
    gain_one, bias_one = first_gain[None], first_bias[None]
    gain_two, bias_two = second_gain[None], second_bias[None]

    rings = [[inputs[c * chunk_rows : (c + 1) * chunk_rows]] for c in range(CHUNKS)]
    share = unit // CHUNKS
    for chunk in range(CHUNKS):
        carried = out_weight.T[chunk * share : (chunk + 1) * share]
        rings[chunk][0] = jnp.concatenate([rings[chunk][0], carried], axis=0)
    for chunk in range(CHUNKS):
        for _ in range(tp - 1):
            rings[chunk].append(shift(rings[chunk][-1], 1))
            if len(rings[chunk]) == 2:
                rings[chunk][-1] = tie(rings[chunk][-1], own_feed)
    all_low, full, low_half, *outgoing, stack = project(
        rings, place, gain_one, bias_one, full_qkv, flat_bias, tables, nctx, unit
    )
    full_out = lax.all_gather(stack, data, axis=1, tiled=True)

    cot = tie(cotangent, *[blocks[-1] for blocks in rings])
    cot_rings = [[cot[c * chunk_rows : (c + 1) * chunk_rows]] for c in range(CHUNKS)]
    for blocks in cot_rings:
        for _ in range(tp - 1):
            blocks.append(shift(blocks[-1], 1))
    pieces = send(*outgoing, *[blocks[max(tp - 2, 0)] for blocks in cot_rings])

    attended, outgoing, logs = attend(
        pieces,
        place[1:2],
        lows,
        ends,
        bounds,
        nctx,
        block_rows,
        feed_weights,
    )
    cot, cot_half = join(cot_rings, place, unit)
    arrived = lax.all_to_all(
        tie(outgoing, *[blocks[-1] for blocks in cot_rings]).reshape(nctx * tp, part_rows, piece),
        ("ctx", "tp"),
        split_axis=0,
        concat_axis=0,
        tiled=True,
    )
    returned, mixed, second_low = mix(
        arrived.reshape(nctx, tp, part_rows, piece),
        full_out,
        full,
        gain_two,
        bias_two,
        place,
        1,
    )

    arrived, held, partials, travelling = second_low, [], [], None
    for step in range(tp):
        coming = shift(arrived, 1) if step < tp - 1 else None
        needed = travelling if step == tp - 1 and step > 2 else []
        *held, first, second = feed(
            arrived, cot, mixed, feed_weights, step, tp, place, held, HALVES, *needed
        )
        partials.append([first, second])
        if step == 1 % tp:
            travelling = partials[step]
        elif step > 1:
            travelling = [
                total(shift(value, 1), kept) for value, kept in zip(travelling, partials[step])
            ]
        if step == 0 and coming is not None:
            coming = tie(coming, partials[0][0])
        arrived = coming
    all_second, all_gate, all_up, hidden, feedforward = held

    last = [shift(value, 1) for value in travelling]
    half_gate = blame(all_second, all_gate, *travelling)
    half_up = blame(all_second, all_up, *travelling)
    grad_heads, grad_mixed, mixed_low, gain_grad_two, shift_grad_two, mixed_half = turn(
        last,
        partials[0],
        mixed,
        cot,
        gain_two,
        full_out,
        place,
        nctx,
        tp,
        unit,
        half_gate,
        half_up,
    )
    grad_heads = lax.all_to_all(
        grad_heads.reshape(nctx * tp, part_rows, piece),
        ("ctx", "tp"),
        split_axis=0,
        concat_axis=0,
        tiled=True,
    ).reshape(nctx * block_rows, piece)

    total_gate = scatter(tie(half_gate, mixed_low), 0).astype(F32)
    half_out = blame(mixed_low, returned)
    total_out = scatter(tie(half_out, grad_heads), 0)
    total_up = scatter(tie(half_up, grad_heads), 0)

    feedforward = tie(feedforward, grad_heads)
    inner = hidden.shape[1]
    both = inner + 3 * head_width
    if square:
        parts = blame_halves(
            (cot, mate(cot_half)), (hidden, mate(hidden)), place, unit, total=both
        )
        half_down = parts[0]
    else:
        half_down = blame(hidden, cot)
        total_down = scatter(half_down, 1).astype(F32)
    layer_out = [pick(feedforward, owners[1 % tp])]
    for step in range(1, tp):
        kept = pick(feedforward, owners[(step + 1) % tp])
        if step == 2:
            layer_out.append(add(shift(layer_out[-1], 1), kept, half_down))
        else:
            layer_out.append(total(shift(layer_out[-1], 1), kept))

    grad_pieces = attend_back(
        pieces, place[1:2], lows, ends, bounds, logs, grad_heads, attended, nctx, block_rows, half_out
    )
    arrived = send(*grad_pieces, *layer_out[max(tp - 2, 0) : tp - 1])
    layer_out = layer_out[-1]
    low_halves = mate(low_half) if square else low_half
    needed = [layer_out, low_halves]
    *partial, all_grad, bias_grad, gain_grad, shift_grad = finish(
        arrived, place, tables, full, grad_mixed, gain_one, full_qkv, tp, *needed
    )
    if square:
        parts = blame_halves(
            (all_low, low_halves),
            (all_grad, mate(all_grad)),
            place,
            unit,
            held=parts,
            offset=inner,
            total=both,
        )
    else:
        parts = []
    def exchange(value, axis, steps, size):
        for step in steps:
            value = value + lax.ppermute(value, axis, [(i, i ^ step) for i in range(size)])
        return value

    def powers(first, size):
        return [1 << bit for bit in range(first, size.bit_length() - 1)]

    small = jnp.concatenate([gain_grad, shift_grad, gain_grad_two, shift_grad_two], axis=1)
    small = sum([shift(small, step) for step in range(1, tp)], small)
    small = jnp.concatenate([bias_grad, small], axis=1)
    travelling, ring_steps = partial[1 % tp], []
    needed = [[total_gate, total_out, small, *parts], [], []]
    for step in range(1, tp):
        travelling = add(
            shift(travelling, 1), partial[(step + 1) % tp], *(needed[step - 1] if step < 4 else [])
        )
        if step == 2:
            out_parts = jnp.swapaxes(
                tie(total_out, travelling).reshape(-1, tp, head_width), 0, 1
            )
            total_out = pick(out_parts, tensor_index).astype(F32)
            for ahead in range(1, tp):
                total_out = total_out + shift(pick(out_parts, (tensor_index + ahead) % tp), ahead).astype(F32)
            total_out = total_out.T
            total_up = tie(total_up, travelling).astype(F32)
            needed[2].extend([total_out, total_up])
        if step == 1:
            once = square_once(parts, travelling) if square else ()
            needed[1].extend(once)
            small = exchange(tie(small, travelling), "ctx", powers(0, nctx), nctx)
            needed[1].append(small)
        if step == 2:
            small = exchange(tie(small, travelling), "fsdp", powers(0, nfsdp), nfsdp)
            needed[2].append(small)
    grad_inputs = travelling
    if square:
        totals = square_twice(*once)
        total_down, total_qkv = totals[:, :inner].T, totals[:, inner:]
    else:
        total_qkv = scatter(blame(all_low, all_grad), 0).astype(F32)

    total_qkv = (
        total_qkv
        .reshape(-1, nctx, 3, piece)
        .transpose(0, 2, 1, 3)
        .reshape(-1, 3, head_width)
    )


    bias_total, small = small[:, : 3 * head_width], small[:, 3 * head_width :]
    bias_total = bias_total.reshape(nctx, 3, piece).transpose(1, 0, 2).reshape(3, head_width)
    small = small.reshape(4, depth)
    return (
        layer_out,
        grad_inputs,
        small[0],
        small[1],
        total_qkv,
        bias_total,
        total_out,
        small[2],
        small[3],
        total_gate,
        total_up,
        total_down,
    )


def solution(mesh):
    data = ("fsdp", "ctx")
    by_rows = P(data, "tp")
    by_columns = P("tp", data)
    qkv = P(data, None, "tp")
    return jax.shard_map(
        functools.partial(shards, mesh.shape["fsdp"], mesh.shape["ctx"], mesh.shape["tp"]),
        mesh=mesh,
        in_specs=(
            by_rows,
            by_rows,
            P(),
            P(),
            qkv,
            P(None, "tp"),
            by_columns,
            P(),
            P(),
            by_rows,
            by_rows,
            by_columns,
            P("fsdp", None),
            P("fsdp", None),
        ),
        out_specs=(
            by_rows,
            by_rows,
            P(),
            P(),
            qkv,
            P(None, "tp"),
            by_columns,
            P(),
            P(),
            by_rows,
            by_rows,
            by_columns,
        ),
        check_vma=False,
    )
```

```python
import functools

import jax
import jax.numpy as jnp
from jax import lax
from jax.experimental import pallas as pl
from jax.experimental.pallas import tpu as pltpu
from jax.sharding import PartitionSpec as P

HEAD_DIM = 64
ROT = 16
EPSILON = 1e-05
NEGATIVE = -1e30
FLOOR = -1e20
VMEM_LIMIT = 56 * 1024 * 1024
TILE_Q = 512
TILE_K = 512
STRIP = 32
CHUNKS = 2
HALVES = 2

F32 = jnp.float32
BF16 = jnp.bfloat16


def layout(lengths, fill_counts, block_rows):
    blocks_count = fill_counts.shape[0]
    seq_count = lengths.shape[0]
    slot_index = jnp.arange(blocks_count * block_rows, dtype=jnp.int32)
    block_of = slot_index // block_rows
    within = slot_index - block_of * block_rows
    chooser = block_of[:, None] == jnp.arange(blocks_count, dtype=jnp.int32)[None, :]
    fill_here = jnp.sum(jnp.where(chooser, fill_counts[None, :], 0), axis=1)
    before = jnp.cumsum(fill_counts) - fill_counts
    before_here = jnp.sum(jnp.where(chooser, before[None, :], 0), axis=1)
    validity = within < fill_here
    used_index = before_here + within
    seq_ends = jnp.cumsum(lengths)
    sequence = jnp.sum((used_index[:, None] >= seq_ends[None, :]).astype(jnp.int32), axis=1)
    seq_starts = seq_ends - lengths
    picker = sequence[:, None] == jnp.arange(seq_count, dtype=jnp.int32)[None, :]
    start_here = jnp.sum(jnp.where(picker, seq_starts[None, :], 0), axis=1)
    after = before + fill_counts
    start_block = jnp.sum((seq_starts[:, None] >= after[None, :]).astype(jnp.int32), axis=1)
    start_block = jnp.minimum(start_block, blocks_count - 1)
    block_pick = start_block[:, None] == jnp.arange(blocks_count, dtype=jnp.int32)[None, :]
    start_before = jnp.sum(jnp.where(block_pick, before[None, :], 0), axis=1)
    start_slot = start_block * block_rows + seq_starts - start_before
    slot_here = jnp.sum(jnp.where(picker, start_slot[None, :], 0), axis=1)
    first_key = jnp.where(validity, slot_here, 0).astype(jnp.int32)
    last_key = jnp.where(validity, slot_index, -1).astype(jnp.int32)
    return (validity, used_index - start_here, first_key, last_key)


def rotary_tables(position):
    half = ROT // 2
    lane = jnp.arange(2 * HEAD_DIM, dtype=jnp.int32) % HEAD_DIM
    frequency = 10000.0 ** (-(2.0 * (lane % half).astype(F32)) / ROT)
    angles = position.astype(F32)[:, None] * frequency[None, :]
    cosine, sine = jnp.cos(angles), jnp.sin(angles)
    lane = lane[None, :]
    return (
        jnp.where(lane < ROT, cosine, 1.0),
        jnp.where(lane < half, -sine, 0.0),
        jnp.where((lane >= half) & (lane < ROT), sine, 0.0),
    )


def params(**extra):
    return pltpu.CompilerParams(vmem_limit_bytes=VMEM_LIMIT, **extra)


def takes(microseconds):
    return pl.CostEstimate(
        flops=int(microseconds * 1e8), bytes_accessed=0, transcendentals=0
    )


def whole(shape):
    return pl.BlockSpec(shape, lambda *_: (0,) * len(shape))


def anywhere(count):
    return [pl.BlockSpec(memory_space=pl.ANY)] * count


def write_half(out, values, half, unit):
    if unit % 128:
        out[...] = values[:, : out.shape[1]]
        return
    for block in range(out.shape[1] // unit):
        first = pl.multiple_of((2 * block + half) * unit, unit)
        out[:, block * unit : (block + 1) * unit] = values[:, pl.ds(first, unit)]


def dot(left, right):
    return jnp.dot(left, right, preferred_element_type=F32)


def dot_turned(left, right):
    return lax.dot_general(left, right, (((1,), (1,)), ((), ())), preferred_element_type=F32)


def tie(value, *needed):
    def kernel(*refs):
        del refs

    return pl.pallas_call(
        kernel,
        in_specs=anywhere(1 + len(needed)),
        out_specs=pl.BlockSpec(memory_space=pl.ANY),
        out_shape=jax.ShapeDtypeStruct(value.shape, value.dtype),
        input_output_aliases={0: 0},
        name="tie",
    )(value, *needed)


def add_kernel(left, right, *refs):
    refs[-1][...] = (left[...].astype(F32) + right[...].astype(F32)).astype(BF16)


def add(left, right, *needed):
    rows, columns = left.shape
    strip = min(rows, 512)
    block = pl.BlockSpec((strip, columns), lambda i: (i, 0))
    return pl.pallas_call(
        add_kernel,
        grid=(rows // strip,),
        in_specs=[block, block] + anywhere(len(needed)),
        out_specs=block,
        out_shape=jax.ShapeDtypeStruct(left.shape, BF16),
        compiler_params=params(),
        cost_estimate=takes(10),
        name="ring_add",
    )(left, right, *needed)


def project_kernel(tp, chunks, per, unit, place, *refs):
    rings, refs = refs[: tp * chunks], refs[tp * chunks :]
    gain, bias, weight, weight_bias, cosine, sine_up, sine_down = refs[:7]
    low, full, half, here, near, far, stack = refs[7:]
    outs = [here, near] + [far.at[way] for way in range(far.shape[0])]
    rows, width = low.shape[0] // chunks, rings[0].shape[1]
    depth = tp * width
    wide = here.shape[1]
    piece = wide // 3
    step = pl.program_id(0)

    @pl.when(pl.program_id(0) == 0)
    def _():
        strip = 128
        for start in range(0, rows * chunks, strip):
            chunk, first = start // rows, start % rows
            blocks = rings[chunk * tp : (chunk + 1) * tp]
            at = slice(start, start + strip)
            inner = slice(first, first + strip)
            parts = [block[inner, :].astype(F32) for block in blocks]
            centre = sum(jnp.sum(part, axis=1, keepdims=True) for part in parts) / depth
            parts = [part - centre for part in parts]
            spread = sum(jnp.sum(part * part, axis=1, keepdims=True) for part in parts) / depth
            scaling = lax.rsqrt(spread + EPSILON)
            for step in range(tp):
                owner = lax.rem(place[0] - step + tp, tp)
                columns = pl.ds(pl.multiple_of(owner * width, width), width)
                low[at, columns] = (
                    parts[step] * scaling * gain[:, columns] + bias[:, columns]
                ).astype(BF16)
                full[at, columns] = blocks[step][inner, :]
        write_half(half, low, 1 - lax.rem(place[1], 2), unit)
        share = rings[0].shape[0] - rows
        for chunk in range(chunks):
            for step in range(tp):
                owner = lax.rem(place[0] - step + tp, tp)
                stack[owner, chunk * share : (chunk + 1) * share, :] = rings[chunk * tp + step][
                    rows:, :
                ]

    product = dot(low[...], weight[...]) + weight_bias[...]
    groups = []
    for group in range(per):
        parts = []
        for part in range(3):
            first = (group * 3 + part) * piece
            values = product[:, first : first + piece]
            if part < 2:
                values = (
                    values * cosine[...]
                    + pltpu.roll(values, piece - ROT // 2, 1) * sine_up[...]
                    + pltpu.roll(values, ROT // 2, 1) * sine_down[...]
                )
            parts.append(values.astype(BF16))
        groups.append(parts)
    flip = lax.rem(place[1], per)
    for way, out in enumerate(outs):
        for group in range(per):

            @pl.when((step == way // per) & (jnp.bitwise_xor(group, flip) == way % per))
            def _():
                for part in range(3):
                    out[:, part * piece : (part + 1) * piece] = groups[group][part]


def project(rings, place, gain, bias, weight, weight_bias, tables, nctx, unit):
    chunks, tp = len(rings), len(rings[0])
    rows, width = tables[0].shape[0], rings[0][0].shape[1]
    depth = tp * width
    total = weight.shape[1]
    wide = total // nctx
    per = 2 if nctx % 2 == 0 else 1
    grid_spec = pltpu.PrefetchScalarGridSpec(
        num_scalar_prefetch=1,
        grid=(nctx // per,),
        in_specs=[whole(rings[0][0].shape)] * (tp * chunks)
        + [whole((1, depth))] * 2
        + [
            pl.BlockSpec((depth, per * wide), lambda i, s: (0, jnp.bitwise_xor(i, s[1] // per))),
            pl.BlockSpec((1, per * wide), lambda i, s: (0, jnp.bitwise_xor(i, s[1] // per))),
        ]
        + [whole((rows, 2 * HEAD_DIM))] * 3,
        out_specs=[whole((rows, depth))] * 2
        + [whole((rows, depth // 2))]
        + [whole((rows, wide))] * 2
        + [whole((nctx - 2, rows, wide)), whole((tp, unit, width))],
    )
    return pl.pallas_call(
        functools.partial(project_kernel, tp, chunks, per, unit),
        grid_spec=grid_spec,
        out_shape=[
            jax.ShapeDtypeStruct((rows, depth), BF16),
            jax.ShapeDtypeStruct((rows, depth), BF16),
            jax.ShapeDtypeStruct((rows, depth // 2), BF16),
        ]
        + [jax.ShapeDtypeStruct((rows, wide), BF16)] * 2
        + [
            jax.ShapeDtypeStruct((nctx - 2, rows, wide), BF16),
            jax.ShapeDtypeStruct((tp, unit, width), BF16),
        ],
        compiler_params=params(),
        cost_estimate=takes(60),
        name="project",
    )(
        place,
        *[block for blocks in rings for block in blocks],
        gain,
        bias,
        weight,
        weight_bias,
        *tables,
    )


def stack_heads(tile, heads):
    lane = lax.broadcasted_iota(jnp.int32, tile.shape, 1) // HEAD_DIM
    return jnp.concatenate(
        [jnp.where(lane == head, tile, jnp.zeros_like(tile)) for head in range(heads)], axis=0
    )


def load_pieces(place, pieces, nctx, held, block_rows):
    chunk_rows = pieces[0].shape[0]
    chunks = len(pieces) // nctx
    for chunk in range(chunks):
        for step in range(nctx):
            source = jnp.bitwise_xor(place, step)
            first = source * block_rows + chunk * chunk_rows
            held[pl.ds(pl.multiple_of(first, chunk_rows), chunk_rows), :] = pieces[
                chunk * nctx + step
            ][...]


def attend_kernel(nctx, heads, count, extra, block_rows, place, lows, ends, bounds, *refs):
    pieces = refs[:count]
    out, sent, logs, held, turned, total, high, sums, raw, chances = refs[count + extra :]
    tile_q, tile_k = out.shape[0], turned.shape[2]
    width = heads * HEAD_DIM
    index = pl.program_id(0)

    @pl.when(index == 0)
    def _():
        load_pieces(place[0], pieces, nctx, held, block_rows)
        for tile in range(turned.shape[0]):
            turned[tile] = jnp.transpose(held[tile * tile_k : (tile + 1) * tile_k, 2 * width :])

    query_rows = pl.ds(pl.multiple_of(index * tile_q, tile_q), tile_q)
    queries = stack_heads(held[query_rows, :width] * jnp.asarray(HEAD_DIM**-0.5, BF16), heads)
    total[...] = jnp.zeros_like(total)
    high[...] = jnp.full_like(high, FLOOR)
    sums[...] = jnp.zeros_like(sums)
    first_key, last_key = bounds[0:1, :], bounds[1:2, :]

    def one(tile, _):
        start = tile * tile_k
        keys = held[pl.ds(pl.multiple_of(start, tile_k), tile_k), width : 2 * width]
        last = jnp.minimum(last_key, ends[tile] - 1) - start
        first = first_key - start
        for head in range(heads):
            raw[head] = dot_turned(keys, queries[head * tile_q : (head + 1) * tile_q])
        for head in range(heads):
            peaks = jnp.broadcast_to(high[head], (8, tile_q))
            for begin in range(0, tile_k, STRIP):
                scores = raw[head, begin : begin + STRIP, :]
                row = lax.broadcasted_iota(jnp.int32, scores.shape, 0) + begin
                scores = jnp.where((row <= last) & (row >= first), scores, NEGATIVE)
                raw[head, begin : begin + STRIP, :] = scores
                for group in range(0, STRIP, 8):
                    peaks = jnp.maximum(peaks, scores[group : group + 8])
            highest = jnp.max(peaks, axis=0, keepdims=True)
            partial = jnp.zeros((8, tile_q), F32)
            for begin in range(0, tile_k, STRIP):
                raised = jnp.exp(raw[head, begin : begin + STRIP, :] - highest)
                chances[head, begin : begin + STRIP, :] = raised.astype(BF16)
                for group in range(0, STRIP, 8):
                    partial = partial + raised[group : group + 8]
            shrink = jnp.exp(high[head] - highest)
            sums[head] = sums[head] * shrink + jnp.sum(partial, axis=0, keepdims=True)
            values = turned[tile, head * HEAD_DIM : (head + 1) * HEAD_DIM, :]
            total[head] = total[head] * shrink + dot(values, chances[head])
            high[head] = highest
        return 0

    upper = (index * tile_q + tile_q - 1) // tile_k + 1
    lax.fori_loop(lows[index], upper, one, 0)
    results = []
    for head in range(heads):
        found = sums[head] > 0.0
        safe = jnp.where(found, sums[head], 1.0)
        results.append(total[head] * jnp.where(found, 1.0 / safe, 0.0))
        logs[head : head + 1, :] = jnp.where(found, high[head] + jnp.log(safe), 0.0)
    result = jnp.transpose(jnp.concatenate(results, axis=0)).astype(BF16)
    out[...] = result
    sent[...] = result


def attend(pieces, place, lows, ends, bounds, nctx, block_rows, *needed):
    total_rows = nctx * block_rows
    width = pieces[0].shape[1] // 3
    heads = width // HEAD_DIM
    steps = total_rows // TILE_Q
    grid_spec = pltpu.PrefetchScalarGridSpec(
        num_scalar_prefetch=3,
        grid=(steps,),
        in_specs=[pl.BlockSpec((2, TILE_Q), lambda i, *_: (0, i))]
        + [whole(piece.shape) for piece in pieces]
        + anywhere(len(needed)),
        out_specs=[
            pl.BlockSpec((TILE_Q, width), lambda i, *_: (i, 0)),
            pl.BlockSpec((TILE_Q, width), lambda i, *_: (i, 0)),
            pl.BlockSpec((heads, TILE_Q), lambda i, *_: (0, i)),
        ],
        scratch_shapes=[
            pltpu.VMEM((total_rows, 3 * width), BF16),
            pltpu.VMEM((total_rows // TILE_K, width, TILE_K), BF16),
            pltpu.VMEM((heads, HEAD_DIM, TILE_Q), F32),
            pltpu.VMEM((heads, 1, TILE_Q), F32),
            pltpu.VMEM((heads, 1, TILE_Q), F32),
            pltpu.VMEM((heads, TILE_K, TILE_Q), F32),
            pltpu.VMEM((heads, TILE_K, TILE_Q), BF16),
        ],
    )
    return pl.pallas_call(
        functools.partial(attend_kernel, nctx, heads, len(pieces), len(needed), block_rows),
        grid_spec=grid_spec,
        out_shape=[
            jax.ShapeDtypeStruct((total_rows, width), BF16),
            jax.ShapeDtypeStruct((total_rows, width), BF16),
            jax.ShapeDtypeStruct((heads, total_rows), F32),
        ],
        compiler_params=params(),
        cost_estimate=takes(200),
        name="attend",
    )(place, lows, ends, bounds, *pieces, *needed)


def attend_back_kernel(
    nctx, heads, count, extra, block_rows, place, lows, ends, bounds, logs, *refs
):
    pieces, refs = refs[:count], refs[count:]
    grad, attended, refs = refs[0], refs[1], refs[2 + extra :]
    here, near, far, refs = *refs[:3], refs[3:]
    held, turned, grad_keys, grad_values, grad_query, raw, raw_grad, chances, steps, merged = refs
    tile_q, tile_k = grad.shape[0], turned.shape[2]
    width = grad.shape[1]
    index = pl.program_id(0)
    scale = jnp.asarray(HEAD_DIM**-0.5, BF16)

    @pl.when(index == 0)
    def _():
        load_pieces(place[0], pieces, nctx, held, block_rows)
        for tile in range(turned.shape[0]):
            turned[tile] = jnp.transpose(
                held[tile * tile_k : (tile + 1) * tile_k, width : 2 * width]
            )
        grad_keys[...] = jnp.zeros_like(grad_keys)
        grad_values[...] = jnp.zeros_like(grad_values)

    query_rows = pl.ds(pl.multiple_of(index * tile_q, tile_q), tile_q)
    queries = stack_heads(held[query_rows, :width] * scale, heads)
    incoming = stack_heads(grad[...], heads)
    product = jnp.transpose(grad[...].astype(F32) * attended[...].astype(F32))
    centres = [
        jnp.sum(product[head * HEAD_DIM : (head + 1) * HEAD_DIM, :], axis=0, keepdims=True)
        for head in range(heads)
    ]
    first_key, last_key = bounds[0:1, :], bounds[1:2, :]
    grad_query[...] = jnp.zeros_like(grad_query)

    def one(tile, _):
        start = tile * tile_k
        key_rows = pl.ds(pl.multiple_of(start, tile_k), tile_k)
        last = jnp.minimum(last_key, ends[tile] - 1) - start
        first = first_key - start
        by_head = [slice(head * tile_q, (head + 1) * tile_q) for head in range(heads)]
        for head in range(heads):
            raw[head] = dot_turned(held[key_rows, width : 2 * width], queries[by_head[head]])
            raw_grad[head] = dot_turned(held[key_rows, 2 * width :], incoming[by_head[head]])
        for head in range(heads):
            for begin in range(0, tile_k, STRIP):
                at = slice(begin, begin + STRIP)
                row = lax.broadcasted_iota(jnp.int32, (STRIP, tile_q), 0) + begin
                allowed = (row <= last) & (row >= first)
                scores = raw[head, at, :] - logs[head : head + 1, :]
                chance = jnp.exp(jnp.where(allowed, scores, NEGATIVE))
                chances[head, at, :] = chance.astype(BF16)
                steps[head, at, :] = (chance * (raw_grad[head, at, :] - centres[head])).astype(BF16)
            grad_values[key_rows, :] += dot(chances[head], incoming[by_head[head]])
            grad_keys[key_rows, :] += dot(steps[head], queries[by_head[head]])
            keys = turned[tile, head * HEAD_DIM : (head + 1) * HEAD_DIM, :]
            grad_query[head] += dot(keys, steps[head])
        return 0

    upper = (index * tile_q + tile_q - 1) // tile_k + 1
    lax.fori_loop(lows[index], upper, one, 0)
    result = jnp.concatenate([grad_query[head] for head in range(heads)], axis=0)
    merged[query_rows, :width] = (jnp.transpose(result) * HEAD_DIM**-0.5).astype(BF16)

    @pl.when(index == pl.num_programs(0) - 1)
    def _():
        merged[:, width : 2 * width] = grad_keys[...].astype(BF16)
        merged[:, 2 * width :] = grad_values[...].astype(BF16)
        outs = [here, near] + [far.at[way] for way in range(nctx - 2)]
        for way, out in enumerate(outs):
            first = jnp.bitwise_xor(place[0], way) * block_rows
            out[...] = merged[pl.ds(pl.multiple_of(first, block_rows), block_rows), :]


def attend_back(pieces, place, lows, ends, bounds, logs, grad, attended, nctx, block_rows, *needed):
    total_rows, width = grad.shape
    heads = width // HEAD_DIM
    by_tile = pl.BlockSpec((TILE_Q, width), lambda i, *_: (i, 0))
    sent = (block_rows, 3 * width)
    sent = [sent, sent, (nctx - 2, *sent)]
    grid_spec = pltpu.PrefetchScalarGridSpec(
        num_scalar_prefetch=3,
        grid=(total_rows // TILE_Q,),
        in_specs=[
            pl.BlockSpec((2, TILE_Q), lambda i, *_: (0, i)),
            pl.BlockSpec((heads, TILE_Q), lambda i, *_: (0, i)),
        ]
        + [whole(piece.shape) for piece in pieces]
        + [by_tile] * 2
        + anywhere(len(needed)),
        out_specs=[whole(shape) for shape in sent],
        scratch_shapes=[
            pltpu.VMEM((total_rows, 3 * width), BF16),
            pltpu.VMEM((total_rows // TILE_K, width, TILE_K), BF16),
            pltpu.VMEM((total_rows, width), F32),
            pltpu.VMEM((total_rows, width), F32),
            pltpu.VMEM((heads, HEAD_DIM, TILE_Q), F32),
            pltpu.VMEM((heads, TILE_K, TILE_Q), F32),
            pltpu.VMEM((heads, TILE_K, TILE_Q), F32),
            pltpu.VMEM((heads, TILE_K, TILE_Q), BF16),
            pltpu.VMEM((heads, TILE_K, TILE_Q), BF16),
            pltpu.VMEM((total_rows, 3 * width), BF16),
        ],
    )
    return pl.pallas_call(
        functools.partial(
            attend_back_kernel, nctx, heads, len(pieces), len(needed), block_rows
        ),
        grid_spec=grid_spec,
        out_shape=[jax.ShapeDtypeStruct(shape, BF16) for shape in sent],
        compiler_params=params(),
        cost_estimate=takes(250),
        name="attend_back",
    )(place, lows, ends, bounds, logs, *pieces, grad, attended, *needed)


def mix_kernel(nctx, count, place, heads_in, weight, source, gain, bias, *refs):
    returned, mixed, *lows = refs[count:]
    rows, depth = mixed.shape
    step = pl.program_id(0)
    left = jnp.concatenate([heads_in[c, 0] for c in range(nctx)], axis=1)
    returned[...] = left

    @pl.when(step == 0)
    def _():
        mixed[...] = source[...].astype(F32)

    mixed[...] += dot_turned(left, weight[0])

    @pl.when(step == pl.num_programs(0) - 1)
    def _():
        values = mixed[...]
        values = values - jnp.mean(values, axis=1, keepdims=True)
        scaling = lax.rsqrt(jnp.mean(values * values, axis=1, keepdims=True) + EPSILON)
        values = (values * scaling * gain[...] + bias[...]).astype(BF16)
        part_rows = lows[0].shape[0]
        for part, low in enumerate(lows):
            low[...] = values[part * part_rows : (part + 1) * part_rows]


def mix(heads_in, weight, full, gain, bias, place, parts, *needed):
    nctx, tp, rows, piece = heads_in.shape
    depth = full.shape[1]
    head_width = nctx * piece
    grid_spec = pltpu.PrefetchScalarGridSpec(
        num_scalar_prefetch=1,
        grid=(tp,),
        in_specs=[
            pl.BlockSpec((nctx, 1, rows, piece), lambda k, s: (0, k, 0, 0)),
            pl.BlockSpec((1, depth, head_width), lambda k, s: (k, 0, 0)),
            pl.BlockSpec((rows, depth), lambda k, s: (s[0], 0)),
            whole((1, depth)),
            whole((1, depth)),
        ]
        + anywhere(len(needed)),
        out_specs=[
            pl.BlockSpec((rows, head_width), lambda k, s: (0, k)),
            whole((rows, depth)),
        ]
        + [whole((rows // parts, depth))] * parts,
    )
    return pl.pallas_call(
        functools.partial(mix_kernel, nctx, len(needed)),
        grid_spec=grid_spec,
        out_shape=[
            jax.ShapeDtypeStruct((rows, tp * head_width), BF16),
            jax.ShapeDtypeStruct((rows, depth), F32),
        ]
        + [jax.ShapeDtypeStruct((rows // parts, depth), BF16)] * parts,
        compiler_params=params(),
        cost_estimate=takes(50),
        name="mix",
    )(place, heads_in, weight, full, gain, bias, *needed)


def feed_kernel(cuts, parts, tp, first_one, place, low, cot, mixed, source, *refs):
    refs = refs[-(5 + parts + 4) :]
    kept, grad_gate, grad_up, hidden, out = refs[:5]
    partials, held, sems = refs[5 : 5 + parts], refs[-4:-1], refs[-1]
    unit = source.shape[1] // 3
    width = out.shape[2]

    def copies(index):
        first, size = cuts[index]
        at = pl.ds(first, size)
        return [
            pltpu.make_async_copy(
                source.at[:, pl.ds(which * unit, unit), at],
                held[which].at[:, :, at],
                sems.at[index * 3 + which],
            )
            for which in range(3)
        ]

    for index in range(len(cuts)):
        for copy in copies(index):
            copy.start()
    kept[...] = low[...]
    rows, depth = kept.shape[0] // parts, kept.shape[1]
    grads = jnp.concatenate([cot[block] for block in range(tp)], axis=1)
    for index, (first, size) in enumerate(cuts):
        for copy in copies(index):
            copy.wait()
        at = slice(first, first + size)
        gate_weight, up_weight, down_weight = [w[:, :, at].reshape(depth, size) for w in held]
        gate = dot(kept[...], gate_weight)
        up = dot(kept[...], up_weight)
        sigma = 1.0 / (1.0 + jnp.exp(-gate))
        active = gate * sigma
        hidden[:, at] = (active * up).astype(BF16)
        grad = dot(grads, down_weight)
        grad_gate[:, at] = (grad * up * sigma * (1.0 + gate * (1.0 - sigma))).astype(BF16)
        grad_up[:, at] = (grad * active).astype(BF16)
    gate_weight, up_weight, down_weight = [w[...].reshape(depth, w.shape[2]) for w in held]
    product = dot_turned(grad_gate[...], gate_weight) + dot_turned(grad_up[...], up_weight)
    for part in range(parts):
        partials[part][...] = product[part * rows : (part + 1) * rows].astype(BF16)
    values = dot_turned(hidden[...], down_weight)
    if first_one:
        values = values + mixed[...]
    for block in range(tp):
        out[block] = values[:, block * width : (block + 1) * width].astype(BF16)


def feed(low, cot, mixed, weights, step, tp, place, held, parts, *needed):
    rows, depth = low.shape
    part_rows = rows // parts
    blocks, triple, hidden = weights.shape
    cuts = []
    while sum(size for _, size in cuts) < hidden:
        first = sum(size for _, size in cuts)
        cuts.append((first, min(512, hidden - first)))
    by_owner = lambda columns: pl.BlockSpec(
        (rows, columns), lambda i, s: (lax.rem(s[0] - step + tp, tp), 0)
    )
    width = depth // tp
    blocks_of_owner = pl.BlockSpec(
        (tp, rows, width), lambda i, s: (0, lax.rem(s[0] - step + tp, tp), 0)
    )
    grid_spec = pltpu.PrefetchScalarGridSpec(
        num_scalar_prefetch=1,
        grid=(1,),
        in_specs=[whole((rows, depth)), blocks_of_owner, whole(mixed.shape)]
        + anywhere(1 + len(held) + len(needed)),
        out_specs=[by_owner(depth)]
        + [by_owner(hidden)] * 3
        + [blocks_of_owner]
        + [whole((part_rows, depth))] * parts,
        scratch_shapes=[pltpu.VMEM((blocks, triple // 3, hidden), BF16)] * 3
        + [pltpu.SemaphoreType.DMA((3 * len(cuts),))],
    )
    return pl.pallas_call(
        functools.partial(feed_kernel, tuple(cuts), parts, tp, step == 0),
        grid_spec=grid_spec,
        out_shape=[
            jax.ShapeDtypeStruct((tp * rows, columns), BF16)
            for columns in (depth, hidden, hidden, hidden)
        ]
        + [jax.ShapeDtypeStruct((tp, tp * rows, width), BF16)]
        + [jax.ShapeDtypeStruct((part_rows, depth), BF16)] * parts,
        input_output_aliases={5 + index: index for index in range(len(held))},
        compiler_params=params(),
        cost_estimate=takes(100),
        name="feed",
    )(place, low, cot, mixed, weights, *held, *needed)


def blame_halves(lefts, rights, place, unit, *needed, held=(), offset=0, total=None):
    rows, other = rights[0].shape
    picked = lefts[1].shape[1] // unit
    chosen = pl.BlockSpec((rows, unit), lambda j, s: (0, 2 * (j ^ s[3]) + s[1] % 2))
    if lefts[0].ndim == 3:
        per = lefts[0].shape[2] // unit
        chosen = pl.BlockSpec(
            (1, rows, unit),
            lambda j, s: (
                (2 * (j ^ s[3]) + s[1] % 2) // per,
                0,
                lax.rem(2 * (j ^ s[3]) + s[1] % 2, per),
            ),
        )
    cut = pl.BlockSpec((rows, unit), lambda j, s: (0, j ^ s[3]))
    shapes = [(2, unit // 2, total or other)] * 4

    def kernel(place, left_here, left_there, right_here, right_there, *refs):
        outs, spare, sems = refs[len(held) + len(needed) : -2], refs[-2], refs[-1]
        product = 0.0
        for left, right in ((left_here, right_here), (left_there, right_there)):
            ours = left[0] if len(left.shape) == 3 else left[...]
            product = product + lax.dot_general(
                ours, right[...], (((0,), (0,)), ((), ())), preferred_element_type=F32
            )
        product = product.astype(BF16)
        for j in range(picked):

            @pl.when(pl.program_id(0) == j)
            def _():
                first, second = spare.at[j // 2, j % 2], spare.at[2 + j % 2, j // 2]
                first[...], second[...] = product[: unit // 2], product[unit // 2 :]

        @pl.when(pl.program_id(0) == picked - 1)
        def _():
            moves = [
                pltpu.make_async_copy(
                    spare.at[index], out.at[:, :, pl.ds(offset, other)], sems.at[index]
                )
                for index, out in enumerate(outs)
            ]
            for move in moves:
                move.start()
            for move in moves:
                move.wait()

    grid_spec = pltpu.PrefetchScalarGridSpec(
        num_scalar_prefetch=1,
        grid=(picked,),
        in_specs=[chosen, cut]
        + [whole((rows, other))] * 2
        + anywhere(len(held) + len(needed)),
        out_specs=anywhere(4),
        scratch_shapes=[
            pltpu.VMEM((4, 2, unit // 2, other), BF16),
            pltpu.SemaphoreType.DMA((4,)),
        ],
    )
    place = jnp.concatenate([place, place[2:3] * 2 + place[1:2] // 2])
    return pl.pallas_call(
        kernel,
        grid_spec=grid_spec,
        out_shape=[jax.ShapeDtypeStruct(shape, BF16) for shape in shapes],
        input_output_aliases={5 + index: index for index in range(len(held))},
        compiler_params=params(),
        cost_estimate=takes(60),
        name="blame_halves",
    )(place, *lefts, *rights, *held, *needed)


def blame(left, right, *needed):
    rows, columns = left.shape
    if right.ndim == 3:
        steps, other = right.shape[0], right.shape[2]
        in_specs = [whole((rows, columns)), pl.BlockSpec((1, rows, other), lambda j: (j, 0, 0))]
        target, shape = pl.BlockSpec((columns, other), lambda j: (0, j)), (columns, steps * other)
    else:
        steps, other = 4, right.shape[1]
        in_specs = [pl.BlockSpec((rows, columns // steps), lambda j: (0, j)), whole((rows, other))]
        target, shape = pl.BlockSpec((columns // steps, other), lambda j: (j, 0)), (columns, other)

    def kernel(left, right, *refs):
        theirs = right[0] if len(right.shape) == 3 else right[...]
        refs[-1][...] = lax.dot_general(
            left[...], theirs, (((0,), (0,)), ((), ())), preferred_element_type=F32
        ).astype(BF16)

    return pl.pallas_call(
        kernel,
        grid=(steps,),
        in_specs=in_specs + anywhere(len(needed)),
        out_specs=target,
        out_shape=jax.ShapeDtypeStruct(shape, BF16),
        compiler_params=params(),
        cost_estimate=takes(60),
        name="blame",
    )(left, right, *needed)


def turn_kernel(nctx, count, parts, unit, place, *refs):
    arrived, own = refs[:parts], refs[parts : 2 * parts]
    mixed, cot, gain = refs[2 * parts : 2 * parts + 3]
    weight, refs = refs[2 * parts + 3], refs[2 * parts + 4 + count :]
    out, grad_mixed, grad_low, gain_grad, shift_grad, half = refs
    rows, depth = mixed.shape
    piece = out.shape[3]

    @pl.when(pl.program_id(0) == 0)
    def _():
        incoming = jnp.concatenate(
            [there[...].astype(F32) + here[...].astype(F32) for there, here in zip(arrived, own)]
        )
        values = mixed[...]
        values = values - jnp.mean(values, axis=1, keepdims=True)
        scaling = lax.rsqrt(jnp.mean(values * values, axis=1, keepdims=True) + EPSILON)
        normed = values * scaling
        shift_grad[...] = jnp.sum(incoming, axis=0, keepdims=True)
        gain_grad[...] = jnp.sum(incoming * normed, axis=0, keepdims=True)
        scaled = incoming * gain[...]
        grads = jnp.concatenate([cot[block] for block in range(cot.shape[0])], axis=1)
        total = grads.astype(F32) + scaling * (
            scaled
            - jnp.mean(scaled, axis=1, keepdims=True)
            - normed * jnp.mean(scaled * normed, axis=1, keepdims=True)
        )
        grad_mixed[...] = total
        grad_low[...] = total.astype(BF16)
        write_half(half, grad_low, 1 - lax.rem(place[1], 2), unit)

    product = dot(grad_low[...], weight[0])
    for c in range(nctx):
        out[c, 0] = product[:, c * piece : (c + 1) * piece].astype(BF16)


def turn(arrived, own, mixed, cot, gain, weight, place, nctx, tp, unit, *needed):
    rows, depth = mixed.shape
    parts = len(arrived)
    head_width = weight.shape[2]
    piece = head_width // nctx
    grid_spec = pltpu.PrefetchScalarGridSpec(
        num_scalar_prefetch=1,
        grid=(tp,),
        in_specs=[whole((rows // parts, depth))] * (2 * parts)
        + [whole((rows, depth))]
        + [
            pl.BlockSpec((tp, rows, depth // tp), lambda k, s: (0, s[0], 0)),
            whole((1, depth)),
            pl.BlockSpec((1, depth, head_width), lambda k, s: (k, 0, 0)),
        ]
        + anywhere(len(needed)),
        out_specs=[
            pl.BlockSpec((nctx, 1, rows, piece), lambda k, s: (0, k, 0, 0)),
            whole((rows, depth)),
            whole((rows, depth)),
            whole((1, depth)),
            whole((1, depth)),
            whole((rows, depth // 2)),
        ],
    )
    return pl.pallas_call(
        functools.partial(turn_kernel, nctx, len(needed), parts, unit),
        grid_spec=grid_spec,
        out_shape=[
            jax.ShapeDtypeStruct((nctx, tp, rows, piece), BF16),
            jax.ShapeDtypeStruct((rows, depth), F32),
            jax.ShapeDtypeStruct((rows, depth), BF16),
            jax.ShapeDtypeStruct((1, depth), F32),
            jax.ShapeDtypeStruct((1, depth), F32),
            jax.ShapeDtypeStruct((rows, depth // 2), BF16),
        ],
        compiler_params=params(),
        cost_estimate=takes(60),
        name="turn",
    )(place, *arrived, *own, mixed, cot, gain, weight, *needed)


def finish_kernel(nctx, tp, extra_count, place, *refs):
    pieces = refs[:nctx]
    cosine, sine_up, sine_down, full, extra, gain = refs[nctx : nctx + 6]
    weight, refs = refs[nctx + 6], refs[nctx + 7 + extra_count :]
    outs = refs[:tp]
    low, bias_grad, gain_grad, shift_grad, spare = refs[tp:]
    rows, wide = pieces[0].shape
    piece = wide // 3
    width = outs[0].shape[1]
    strip = spare.shape[0]
    extra_rows = extra.shape[0]

    @pl.when(pl.program_id(0) == 0)
    def _():
        bias_grad[...] = jnp.zeros_like(bias_grad)
        gain_grad[...] = jnp.zeros_like(gain_grad)
        shift_grad[...] = jnp.zeros_like(shift_grad)

    for step in range(nctx):
        source = jnp.bitwise_xor(place[1], step)
        for part in range(3):
            values = pieces[step][:, part * piece : (part + 1) * piece].astype(F32)
            if part < 2:
                values = (
                    values * cosine[...]
                    - pltpu.roll(values, piece - ROT // 2, 1) * sine_up[...]
                    - pltpu.roll(values, ROT // 2, 1) * sine_down[...]
                )
            columns = pl.ds(pl.multiple_of(source * wide + part * piece, piece), piece)
            bias_grad[:, columns] += jnp.sum(values, axis=0, keepdims=True)
            low[:, columns] = values.astype(BF16)

    incoming = dot_turned(low[...], weight[...])
    source = full[...].astype(F32)
    source = source - jnp.mean(source, axis=1, keepdims=True)
    scaling = lax.rsqrt(jnp.mean(source * source, axis=1, keepdims=True) + EPSILON)
    normed = source * scaling
    shift_grad[...] += jnp.sum(incoming, axis=0, keepdims=True)
    gain_grad[...] += jnp.sum(incoming * normed, axis=0, keepdims=True)
    scaled = incoming * gain[...]
    spare[...] = scaling * (
        scaled
        - jnp.mean(scaled, axis=1, keepdims=True)
        - normed * jnp.mean(scaled * normed, axis=1, keepdims=True)
    )
    first = pl.program_id(0) * strip
    wanted = place[0] * extra_rows

    if strip <= extra_rows:

        @pl.when((first >= wanted) & (first < wanted + extra_rows))
        def _():
            spare[...] += extra[pl.ds(pl.multiple_of(first - wanted, strip), strip), :]

    else:

        @pl.when((wanted >= first) & (wanted < first + strip))
        def _():
            spare[pl.ds(pl.multiple_of(wanted - first, extra_rows), extra_rows), :] += extra[...]

    for step, out in enumerate(outs):
        owner = lax.rem(place[0] - step + tp, tp)
        out[...] = spare[:, pl.ds(pl.multiple_of(owner * width, width), width)].astype(BF16)


def finish(pieces, place, tables, full, extra, gain, weight, tp, *needed):
    rows, wide = pieces[0].shape
    depth = full.shape[1]
    total = weight.shape[1]
    strip = 256
    steps = rows // strip
    width = depth // tp
    nctx = len(pieces)
    by_rows = lambda columns: pl.BlockSpec((strip, columns), lambda i, s: (i, 0))
    grid_spec = pltpu.PrefetchScalarGridSpec(
        num_scalar_prefetch=1,
        grid=(steps,),
        in_specs=[by_rows(wide)] * nctx
        + [by_rows(2 * HEAD_DIM)] * 3
        + [
            by_rows(depth),
            whole(extra.shape),
            whole((1, depth)),
        ]
        + [whole(weight.shape)]
        + anywhere(len(needed)),
        out_specs=[by_rows(width)] * tp
        + [
            by_rows(total),
            whole((1, total)),
            whole((1, depth)),
            whole((1, depth)),
        ],
        scratch_shapes=[pltpu.VMEM((strip, depth), F32)],
    )
    return pl.pallas_call(
        functools.partial(finish_kernel, nctx, tp, len(needed)),
        grid_spec=grid_spec,
        out_shape=[jax.ShapeDtypeStruct((rows, width), BF16)] * tp
        + [
            jax.ShapeDtypeStruct((rows, total), BF16),
            jax.ShapeDtypeStruct((1, total), F32),
            jax.ShapeDtypeStruct((1, depth), F32),
            jax.ShapeDtypeStruct((1, depth), F32),
        ],
        compiler_params=params(),
        cost_estimate=takes(70),
        name="finish",
    )(place, *pieces, *tables, full, extra, gain, weight, *needed)


def join(rings, place, unit):
    parts, tp = len(rings), len(rings[0])
    rows, width = rings[0][0].shape

    def kernel(place, *refs):
        for part in range(parts):
            for step in range(tp):
                owner = lax.rem(place[0] - step + tp, tp)
                refs[-2][owner, part * rows : (part + 1) * rows, :] = refs[part * tp + step][...]
        per, half = width // unit, 1 - lax.rem(place[1], 2)
        for block in range(tp * per // 2):
            index = 2 * block + half if unit % 128 == 0 else 0
            first = pl.multiple_of(lax.rem(index, per) * unit, unit)
            if unit % 128:
                first = 0
            refs[-1][:, block * unit : (block + 1) * unit] = refs[-2][
                lax.div(index, per), :, pl.ds(first, unit)
            ]

    grid_spec = pltpu.PrefetchScalarGridSpec(
        num_scalar_prefetch=1,
        grid=(1,),
        in_specs=[whole((rows, width))] * (parts * tp),
        out_specs=[whole((tp, parts * rows, width)), whole((parts * rows, tp * width // 2))],
    )
    return pl.pallas_call(
        kernel,
        grid_spec=grid_spec,
        out_shape=[
            jax.ShapeDtypeStruct((tp, parts * rows, width), BF16),
            jax.ShapeDtypeStruct((parts * rows, tp * width // 2), BF16),
        ],
        compiler_params=params(),
        cost_estimate=takes(10),
        name="join",
    )(place, *[block for blocks in rings for block in blocks])


def pack_kernel(gate, up, down, out):
    rows = gate.shape[0]
    out[:rows] = gate[...]
    out[rows : 2 * rows] = up[...]
    out[2 * rows :] = jnp.transpose(down[...])


def pack(gate, up, down):
    rows, columns = gate.shape
    return pl.pallas_call(
        pack_kernel,
        out_shape=jax.ShapeDtypeStruct((3 * rows, columns), BF16),
        compiler_params=params(),
        cost_estimate=takes(10),
        name="pack",
    )(gate, up, down)


def contract_rows(left, right):
    return lax.dot_general(left, right, (((0,), (0,)), ((), ())), preferred_element_type=F32)


def pick(stack, index):
    return lax.dynamic_index_in_dim(stack, index, 0, keepdims=False)


def shards(
    nfsdp,
    nctx,
    tp,
    inputs,
    cotangent,
    first_gain,
    first_bias,
    qkv_weight,
    qkv_bias,
    out_weight,
    second_gain,
    second_bias,
    gate_weight,
    up_weight,
    down_weight,
    lengths,
    fill_counts,
):
    data = ("fsdp", "ctx")
    ndata = nfsdp * nctx
    block_rows, width = inputs.shape
    depth = tp * width
    half_depth = depth // 2
    unit = depth // ndata
    tensor_index = lax.axis_index("tp").astype(jnp.int32)
    context_index = lax.axis_index("ctx").astype(jnp.int32)
    fsdp_index = lax.axis_index("fsdp").astype(jnp.int32)
    part_rows = block_rows // tp
    chunk_rows = block_rows // CHUNKS
    head_width = qkv_weight.shape[2]
    piece = head_width // nctx
    wide = 3 * piece

    square = nfsdp == 2 and nctx == 4 and unit % 128 == 0
    place = jnp.stack([tensor_index, context_index, fsdp_index])

    def shift(value, step):
        return lax.ppermute(value, "tp", [(i, (i + step) % tp) for i in range(tp)])

    def swap(value, step):
        return lax.ppermute(value, "ctx", [(i, i ^ step) for i in range(nctx)])

    core_index = context_index % 2
    groups = [list(range(0, ndata, 2)), list(range(1, ndata, 2))]
    def mate(value):
        return swap(value, 1)

    def send(here, near, far, *needed):
        far = swap(far, 2)
        return [here, swap(near, 1), far[0], swap(tie(far[1], *needed), 1)]

    def scatter_half(value, axis):
        return lax.psum_scatter(
            value, data, scatter_dimension=axis, tiled=True, axis_index_groups=groups
        )

    def scatter(value, axis):
        return lax.psum_scatter(value, data, scatter_dimension=axis, tiled=True)

    def cross(value):
        return lax.ppermute(value, "fsdp", [(i, i ^ 1) for i in range(nfsdp)])

    def square_once(parts):
        near, far, low, high = parts
        return total(near, cross(far)), total(low, swap(high, 2))

    def square_twice(first, second):
        first = first[0].astype(F32) + swap(first[1], 2).astype(F32)
        second = second[0].astype(F32) + cross(second[1]).astype(F32)
        return jnp.concatenate([first, second], axis=0)

    def total(left, right):
        return (left.astype(F32) + right.astype(F32)).astype(BF16)

    owners = [(tensor_index - step + tp) % tp for step in range(tp)]

    own_qkv = (
        qkv_weight.reshape(-1, 3, nctx, piece).transpose(0, 2, 1, 3).reshape(-1, 3 * head_width)
    )
    full_qkv = lax.all_gather(own_qkv, data, axis=0, tiled=True)
    own_feed = pack(gate_weight, up_weight, down_weight)
    feed_weights = lax.all_gather(own_feed, data, axis=0, tiled=True).reshape(ndata, 3 * unit, -1)

    validity, position, first_key, last_key = layout(lengths[0], fill_counts[0], block_rows)
    own_position = lax.dynamic_slice_in_dim(position, context_index * block_rows, block_rows, 0)
    tables = rotary_tables(own_position)
    bounds = jnp.stack([first_key, last_key])
    tile_first = first_key[::TILE_Q]
    tile_count = tile_first.shape[0]
    lows = jnp.where(validity[::TILE_Q], tile_first // TILE_K, tile_count * TILE_Q).astype(jnp.int32)
    key_block = jnp.arange(0, nctx * block_rows, TILE_K, dtype=jnp.int32) // block_rows
    ends = (
        key_block * block_rows
        + jnp.sum(
            jnp.where(
                key_block[:, None] == jnp.arange(nctx, dtype=jnp.int32)[None, :],
                fill_counts[0][None, :],
                0,
            ),
            axis=1,
        )
    ).astype(jnp.int32)

    flat_bias = qkv_bias.reshape(3, nctx, piece).transpose(1, 0, 2).reshape(1, -1)
    gain_one, bias_one = first_gain[None], first_bias[None]
    gain_two, bias_two = second_gain[None], second_bias[None]

    rings = [[inputs[c * chunk_rows : (c + 1) * chunk_rows]] for c in range(CHUNKS)]
    share = unit // CHUNKS
    for chunk in range(CHUNKS):
        carried = out_weight.T[chunk * share : (chunk + 1) * share]
        rings[chunk][0] = jnp.concatenate([rings[chunk][0], carried], axis=0)
    for chunk in range(CHUNKS):
        for _ in range(tp - 1):
            rings[chunk].append(shift(rings[chunk][-1], 1))
            if len(rings[chunk]) == 2:
                rings[chunk][-1] = tie(rings[chunk][-1], own_feed)
    all_low, full, low_half, *outgoing, stack = project(
        rings, place, gain_one, bias_one, full_qkv, flat_bias, tables, nctx, unit
    )
    full_out = lax.all_gather(stack, data, axis=1, tiled=True)

    cot = tie(cotangent, *[blocks[-1] for blocks in rings])
    cot_rings = [[cot[c * chunk_rows : (c + 1) * chunk_rows]] for c in range(CHUNKS)]
    for blocks in cot_rings:
        for _ in range(tp - 1):
            blocks.append(shift(blocks[-1], 1))
    pieces = send(*outgoing, *[blocks[max(tp - 2, 0)] for blocks in cot_rings])

    attended, outgoing, logs = attend(
        pieces,
        place[1:2],
        lows,
        ends,
        bounds,
        nctx,
        block_rows,
        feed_weights,
    )
    cot, cot_half = join(cot_rings, place, unit)
    arrived = lax.all_to_all(
        tie(outgoing, *[blocks[-1] for blocks in cot_rings]).reshape(nctx * tp, part_rows, piece),
        ("ctx", "tp"),
        split_axis=0,
        concat_axis=0,
        tiled=True,
    )
    returned, mixed, second_low = mix(
        arrived.reshape(nctx, tp, part_rows, piece),
        full_out,
        full,
        gain_two,
        bias_two,
        place,
        1,
    )

    arrived, held, partials, travelling = second_low, [], [], None
    for step in range(tp):
        coming = shift(arrived, 1) if step < tp - 1 else None
        needed = travelling if step == tp - 1 and step > 2 else []
        *held, first, second = feed(
            arrived, cot, mixed, feed_weights, step, tp, place, held, HALVES, *needed
        )
        partials.append([first, second])
        if step == 1 % tp:
            travelling = partials[step]
        elif step > 1:
            travelling = [
                total(shift(value, 1), kept) for value, kept in zip(travelling, partials[step])
            ]
        if step == 0 and coming is not None:
            coming = tie(coming, partials[0][0])
        arrived = coming
    all_second, all_gate, all_up, hidden, feedforward = held

    last = [shift(value, 1) for value in travelling]
    half_gate = blame(all_second, all_gate, *travelling)
    half_up = blame(all_second, all_up, *travelling)
    grad_heads, grad_mixed, mixed_low, gain_grad_two, shift_grad_two, mixed_half = turn(
        last,
        partials[0],
        mixed,
        cot,
        gain_two,
        full_out,
        place,
        nctx,
        tp,
        unit,
        half_gate,
        half_up,
    )
    grad_heads = lax.all_to_all(
        grad_heads.reshape(nctx * tp, part_rows, piece),
        ("ctx", "tp"),
        split_axis=0,
        concat_axis=0,
        tiled=True,
    ).reshape(nctx * block_rows, piece)

    total_gate = scatter(tie(half_gate, mixed_low), 0).astype(F32)
    total_up = scatter(tie(half_up, mixed_low), 0).astype(F32)
    half_out = blame(mixed_low, returned)
    total_out = scatter(tie(half_out, grad_heads), 0)

    feedforward = tie(feedforward, grad_heads)
    inner = hidden.shape[1]
    both = inner + 3 * head_width
    if square:
        parts = blame_halves(
            (cot, mate(cot_half)), (hidden, mate(hidden)), place, unit, total=both
        )
        half_down = parts[0]
    else:
        half_down = blame(hidden, cot)
        total_down = scatter(half_down, 1).astype(F32)
    layer_out = [pick(feedforward, owners[1 % tp])]
    for step in range(1, tp):
        kept = pick(feedforward, owners[(step + 1) % tp])
        if step == 2:
            layer_out.append(add(shift(layer_out[-1], 1), kept, half_down))
        else:
            layer_out.append(total(shift(layer_out[-1], 1), kept))

    grad_pieces = attend_back(
        pieces, place[1:2], lows, ends, bounds, logs, grad_heads, attended, nctx, block_rows, half_out
    )
    arrived = send(*grad_pieces, *layer_out[max(tp - 2, 0) : tp - 1])
    layer_out = layer_out[-1]
    low_halves = mate(low_half) if square else low_half
    needed = [layer_out, low_halves]
    *partial, all_grad, bias_grad, gain_grad, shift_grad = finish(
        arrived, place, tables, full, grad_mixed, gain_one, full_qkv, tp, *needed
    )
    if square:
        parts = blame_halves(
            (all_low, low_halves),
            (all_grad, mate(all_grad)),
            place,
            unit,
            held=parts,
            offset=inner,
            total=both,
        )
    else:
        parts = []
    def exchange(value, axis, steps, size):
        for step in steps:
            value = value + lax.ppermute(value, axis, [(i, i ^ step) for i in range(size)])
        return value

    def powers(first, size):
        return [1 << bit for bit in range(first, size.bit_length() - 1)]

    small = jnp.concatenate([gain_grad, shift_grad, gain_grad_two, shift_grad_two], axis=1)
    small = sum([shift(small, step) for step in range(1, tp)], small)
    small = jnp.concatenate([bias_grad, small], axis=1)
    travelling, ring_steps = partial[1 % tp], []
    once = square_once(parts) if square else ()
    needed = [[total_gate, total_up, small, *parts], [*once], []]
    for step in range(1, tp):
        travelling = add(
            shift(travelling, 1), partial[(step + 1) % tp], *(needed[step - 1] if step < 4 else [])
        )
        if step == 1:
            out_parts = jnp.swapaxes(
                tie(total_out, travelling).reshape(-1, tp, head_width), 0, 1
            )
            total_out = pick(out_parts, tensor_index).astype(F32)
            for ahead in range(1, tp):
                total_out = total_out + shift(pick(out_parts, (tensor_index + ahead) % tp), ahead).astype(F32)
            total_out = total_out.T
            needed[2].append(total_out)
        if step < 3:
            bits = powers(0, min(nctx, 2)) if step == 1 else powers(1, nctx)
            small = exchange(tie(small, travelling), "ctx", bits, nctx)
            needed[step].append(small)
    small = exchange(tie(small, travelling), "fsdp", powers(0, nfsdp), nfsdp)
    grad_inputs = travelling
    if square:
        totals = square_twice(*once)
        total_down, total_qkv = totals[:, :inner].T, totals[:, inner:]
    else:
        total_qkv = scatter(blame(all_low, all_grad), 0).astype(F32)

    total_qkv = (
        total_qkv
        .reshape(-1, nctx, 3, piece)
        .transpose(0, 2, 1, 3)
        .reshape(-1, 3, head_width)
    )


    bias_total, small = small[:, : 3 * head_width], small[:, 3 * head_width :]
    bias_total = bias_total.reshape(nctx, 3, piece).transpose(1, 0, 2).reshape(3, head_width)
    small = small.reshape(4, depth)
    return (
        layer_out,
        grad_inputs,
        small[0],
        small[1],
        total_qkv,
        bias_total,
        total_out,
        small[2],
        small[3],
        total_gate,
        total_up,
        total_down,
    )


def solution(mesh):
    data = ("fsdp", "ctx")
    by_rows = P(data, "tp")
    by_columns = P("tp", data)
    qkv = P(data, None, "tp")
    return jax.shard_map(
        functools.partial(shards, mesh.shape["fsdp"], mesh.shape["ctx"], mesh.shape["tp"]),
        mesh=mesh,
        in_specs=(
            by_rows,
            by_rows,
            P(),
            P(),
            qkv,
            P(None, "tp"),
            by_columns,
            P(),
            P(),
            by_rows,
            by_rows,
            by_columns,
            P("fsdp", None),
            P("fsdp", None),
        ),
        out_specs=(
            by_rows,
            by_rows,
            P(),
            P(),
            qkv,
            P(None, "tp"),
            by_columns,
            P(),
            P(),
            by_rows,
            by_rows,
            by_columns,
        ),
        check_vma=False,
    )
```

```python
import functools

import jax
import jax.numpy as jnp
from jax import lax
from jax.experimental import pallas as pl
from jax.experimental.pallas import tpu as pltpu
from jax.sharding import PartitionSpec as P

HEAD_DIM = 64
ROT = 16
EPSILON = 1e-05
NEGATIVE = -1e30
FLOOR = -1e20
VMEM_LIMIT = 56 * 1024 * 1024
TILE_Q = 512
TILE_K = 512
STRIP = 32
CHUNKS = 2
HALVES = 2

F32 = jnp.float32
BF16 = jnp.bfloat16


def layout(lengths, fill_counts, block_rows):
    blocks_count = fill_counts.shape[0]
    seq_count = lengths.shape[0]
    slot_index = jnp.arange(blocks_count * block_rows, dtype=jnp.int32)
    block_of = slot_index // block_rows
    within = slot_index - block_of * block_rows
    chooser = block_of[:, None] == jnp.arange(blocks_count, dtype=jnp.int32)[None, :]
    fill_here = jnp.sum(jnp.where(chooser, fill_counts[None, :], 0), axis=1)
    before = jnp.cumsum(fill_counts) - fill_counts
    before_here = jnp.sum(jnp.where(chooser, before[None, :], 0), axis=1)
    validity = within < fill_here
    used_index = before_here + within
    seq_ends = jnp.cumsum(lengths)
    sequence = jnp.sum((used_index[:, None] >= seq_ends[None, :]).astype(jnp.int32), axis=1)
    seq_starts = seq_ends - lengths
    picker = sequence[:, None] == jnp.arange(seq_count, dtype=jnp.int32)[None, :]
    start_here = jnp.sum(jnp.where(picker, seq_starts[None, :], 0), axis=1)
    after = before + fill_counts
    start_block = jnp.sum((seq_starts[:, None] >= after[None, :]).astype(jnp.int32), axis=1)
    start_block = jnp.minimum(start_block, blocks_count - 1)
    block_pick = start_block[:, None] == jnp.arange(blocks_count, dtype=jnp.int32)[None, :]
    start_before = jnp.sum(jnp.where(block_pick, before[None, :], 0), axis=1)
    start_slot = start_block * block_rows + seq_starts - start_before
    slot_here = jnp.sum(jnp.where(picker, start_slot[None, :], 0), axis=1)
    first_key = jnp.where(validity, slot_here, 0).astype(jnp.int32)
    last_key = jnp.where(validity, slot_index, -1).astype(jnp.int32)
    return (validity, used_index - start_here, first_key, last_key)


def rotary_tables(position):
    half = ROT // 2
    lane = jnp.arange(2 * HEAD_DIM, dtype=jnp.int32) % HEAD_DIM
    frequency = 10000.0 ** (-(2.0 * (lane % half).astype(F32)) / ROT)
    angles = position.astype(F32)[:, None] * frequency[None, :]
    cosine, sine = jnp.cos(angles), jnp.sin(angles)
    lane = lane[None, :]
    return (
        jnp.where(lane < ROT, cosine, 1.0),
        jnp.where(lane < half, -sine, 0.0),
        jnp.where((lane >= half) & (lane < ROT), sine, 0.0),
    )


def params(**extra):
    return pltpu.CompilerParams(vmem_limit_bytes=VMEM_LIMIT, **extra)


def takes(microseconds):
    return pl.CostEstimate(
        flops=int(microseconds * 1e8), bytes_accessed=0, transcendentals=0
    )


def whole(shape):
    return pl.BlockSpec(shape, lambda *_: (0,) * len(shape))


def anywhere(count):
    return [pl.BlockSpec(memory_space=pl.ANY)] * count


def write_half(out, values, half, unit):
    if unit % 128:
        out[...] = values[:, : out.shape[1]]
        return
    for block in range(out.shape[1] // unit):
        first = pl.multiple_of((2 * block + half) * unit, unit)
        out[:, block * unit : (block + 1) * unit] = values[:, pl.ds(first, unit)]


def dot(left, right):
    return jnp.dot(left, right, preferred_element_type=F32)


def dot_turned(left, right):
    return lax.dot_general(left, right, (((1,), (1,)), ((), ())), preferred_element_type=F32)


def tie(value, *needed):
    def kernel(*refs):
        del refs

    return pl.pallas_call(
        kernel,
        in_specs=anywhere(1 + len(needed)),
        out_specs=pl.BlockSpec(memory_space=pl.ANY),
        out_shape=jax.ShapeDtypeStruct(value.shape, value.dtype),
        input_output_aliases={0: 0},
        name="tie",
    )(value, *needed)


def add_kernel(left, right, *refs):
    refs[-1][...] = (left[...].astype(F32) + right[...].astype(F32)).astype(BF16)


def add(left, right, *needed):
    rows, columns = left.shape
    strip = min(rows, 512)
    block = pl.BlockSpec((strip, columns), lambda i: (i, 0))
    return pl.pallas_call(
        add_kernel,
        grid=(rows // strip,),
        in_specs=[block, block] + anywhere(len(needed)),
        out_specs=block,
        out_shape=jax.ShapeDtypeStruct(left.shape, BF16),
        compiler_params=params(),
        cost_estimate=takes(10),
        name="ring_add",
    )(left, right, *needed)


def project_kernel(tp, chunks, per, unit, place, *refs):
    rings, refs = refs[: tp * chunks], refs[tp * chunks :]
    gain, bias, weight, weight_bias, cosine, sine_up, sine_down = refs[:7]
    low, full, half, here, near, far, stack = refs[7:]
    outs = [here, near] + [far.at[way] for way in range(far.shape[0])]
    rows, width = low.shape[0] // chunks, rings[0].shape[1]
    depth = tp * width
    wide = here.shape[1]
    piece = wide // 3
    step = pl.program_id(0)

    @pl.when(pl.program_id(0) == 0)
    def _():
        strip = 128
        for start in range(0, rows * chunks, strip):
            chunk, first = start // rows, start % rows
            blocks = rings[chunk * tp : (chunk + 1) * tp]
            at = slice(start, start + strip)
            inner = slice(first, first + strip)
            parts = [block[inner, :].astype(F32) for block in blocks]
            centre = sum(jnp.sum(part, axis=1, keepdims=True) for part in parts) / depth
            parts = [part - centre for part in parts]
            spread = sum(jnp.sum(part * part, axis=1, keepdims=True) for part in parts) / depth
            scaling = lax.rsqrt(spread + EPSILON)
            for step in range(tp):
                owner = lax.rem(place[0] - step + tp, tp)
                columns = pl.ds(pl.multiple_of(owner * width, width), width)
                low[at, columns] = (
                    parts[step] * scaling * gain[:, columns] + bias[:, columns]
                ).astype(BF16)
                full[at, columns] = blocks[step][inner, :]
        write_half(half, low, 1 - lax.rem(place[1], 2), unit)
        share = rings[0].shape[0] - rows
        for chunk in range(chunks):
            for step in range(tp):
                owner = lax.rem(place[0] - step + tp, tp)
                stack[owner, chunk * share : (chunk + 1) * share, :] = rings[chunk * tp + step][
                    rows:, :
                ]

    product = dot(low[...], weight[...]) + weight_bias[...]
    groups = []
    for group in range(per):
        parts = []
        for part in range(3):
            first = (group * 3 + part) * piece
            values = product[:, first : first + piece]
            if part < 2:
                values = (
                    values * cosine[...]
                    + pltpu.roll(values, piece - ROT // 2, 1) * sine_up[...]
                    + pltpu.roll(values, ROT // 2, 1) * sine_down[...]
                )
            parts.append(values.astype(BF16))
        groups.append(parts)
    flip = lax.rem(place[1], per)
    for way, out in enumerate(outs):
        for group in range(per):

            @pl.when((step == way // per) & (jnp.bitwise_xor(group, flip) == way % per))
            def _():
                for part in range(3):
                    out[:, part * piece : (part + 1) * piece] = groups[group][part]


def project(rings, place, gain, bias, weight, weight_bias, tables, nctx, unit):
    chunks, tp = len(rings), len(rings[0])
    rows, width = tables[0].shape[0], rings[0][0].shape[1]
    depth = tp * width
    total = weight.shape[1]
    wide = total // nctx
    per = 2 if nctx % 2 == 0 else 1
    grid_spec = pltpu.PrefetchScalarGridSpec(
        num_scalar_prefetch=1,
        grid=(nctx // per,),
        in_specs=[whole(rings[0][0].shape)] * (tp * chunks)
        + [whole((1, depth))] * 2
        + [
            pl.BlockSpec((depth, per * wide), lambda i, s: (0, jnp.bitwise_xor(i, s[1] // per))),
            pl.BlockSpec((1, per * wide), lambda i, s: (0, jnp.bitwise_xor(i, s[1] // per))),
        ]
        + [whole((rows, 2 * HEAD_DIM))] * 3,
        out_specs=[whole((rows, depth))] * 2
        + [whole((rows, depth // 2))]
        + [whole((rows, wide))] * 2
        + [whole((nctx - 2, rows, wide)), whole((tp, unit, width))],
    )
    return pl.pallas_call(
        functools.partial(project_kernel, tp, chunks, per, unit),
        grid_spec=grid_spec,
        out_shape=[
            jax.ShapeDtypeStruct((rows, depth), BF16),
            jax.ShapeDtypeStruct((rows, depth), BF16),
            jax.ShapeDtypeStruct((rows, depth // 2), BF16),
        ]
        + [jax.ShapeDtypeStruct((rows, wide), BF16)] * 2
        + [
            jax.ShapeDtypeStruct((nctx - 2, rows, wide), BF16),
            jax.ShapeDtypeStruct((tp, unit, width), BF16),
        ],
        compiler_params=params(),
        cost_estimate=takes(60),
        name="project",
    )(
        place,
        *[block for blocks in rings for block in blocks],
        gain,
        bias,
        weight,
        weight_bias,
        *tables,
    )


def stack_heads(tile, heads):
    lane = lax.broadcasted_iota(jnp.int32, tile.shape, 1) // HEAD_DIM
    return jnp.concatenate(
        [jnp.where(lane == head, tile, jnp.zeros_like(tile)) for head in range(heads)], axis=0
    )


def load_pieces(place, pieces, nctx, held, block_rows):
    chunk_rows = pieces[0].shape[0]
    chunks = len(pieces) // nctx
    for chunk in range(chunks):
        for step in range(nctx):
            source = jnp.bitwise_xor(place, step)
            first = source * block_rows + chunk * chunk_rows
            held[pl.ds(pl.multiple_of(first, chunk_rows), chunk_rows), :] = pieces[
                chunk * nctx + step
            ][...]


def attend_kernel(nctx, heads, count, extra, block_rows, place, lows, ends, bounds, *refs):
    pieces = refs[:count]
    out, sent, logs, held, turned, total, high, sums, raw, chances = refs[count + extra :]
    tile_q, tile_k = out.shape[0], turned.shape[2]
    width = heads * HEAD_DIM
    index = pl.program_id(0)

    @pl.when(index == 0)
    def _():
        load_pieces(place[0], pieces, nctx, held, block_rows)
        for tile in range(turned.shape[0]):
            turned[tile] = jnp.transpose(held[tile * tile_k : (tile + 1) * tile_k, 2 * width :])

    query_rows = pl.ds(pl.multiple_of(index * tile_q, tile_q), tile_q)
    queries = stack_heads(held[query_rows, :width] * jnp.asarray(HEAD_DIM**-0.5, BF16), heads)
    total[...] = jnp.zeros_like(total)
    high[...] = jnp.full_like(high, FLOOR)
    sums[...] = jnp.zeros_like(sums)
    first_key, last_key = bounds[0:1, :], bounds[1:2, :]

    def one(tile, _):
        start = tile * tile_k
        keys = held[pl.ds(pl.multiple_of(start, tile_k), tile_k), width : 2 * width]
        last = jnp.minimum(last_key, ends[tile] - 1) - start
        first = first_key - start
        for head in range(heads):
            raw[head] = dot_turned(keys, queries[head * tile_q : (head + 1) * tile_q])
        for head in range(heads):
            peaks = jnp.broadcast_to(high[head], (8, tile_q))
            for begin in range(0, tile_k, STRIP):
                scores = raw[head, begin : begin + STRIP, :]
                row = lax.broadcasted_iota(jnp.int32, scores.shape, 0) + begin
                scores = jnp.where((row <= last) & (row >= first), scores, NEGATIVE)
                raw[head, begin : begin + STRIP, :] = scores
                for group in range(0, STRIP, 8):
                    peaks = jnp.maximum(peaks, scores[group : group + 8])
            highest = jnp.max(peaks, axis=0, keepdims=True)
            partial = jnp.zeros((8, tile_q), F32)
            for begin in range(0, tile_k, STRIP):
                raised = jnp.exp(raw[head, begin : begin + STRIP, :] - highest)
                chances[head, begin : begin + STRIP, :] = raised.astype(BF16)
                for group in range(0, STRIP, 8):
                    partial = partial + raised[group : group + 8]
            shrink = jnp.exp(high[head] - highest)
            sums[head] = sums[head] * shrink + jnp.sum(partial, axis=0, keepdims=True)
            values = turned[tile, head * HEAD_DIM : (head + 1) * HEAD_DIM, :]
            total[head] = total[head] * shrink + dot(values, chances[head])
            high[head] = highest
        return 0

    upper = (index * tile_q + tile_q - 1) // tile_k + 1
    lax.fori_loop(lows[index], upper, one, 0)
    results = []
    for head in range(heads):
        found = sums[head] > 0.0
        safe = jnp.where(found, sums[head], 1.0)
        results.append(total[head] * jnp.where(found, 1.0 / safe, 0.0))
        logs[head : head + 1, :] = jnp.where(found, high[head] + jnp.log(safe), 0.0)
    result = jnp.transpose(jnp.concatenate(results, axis=0)).astype(BF16)
    out[...] = result
    sent[...] = result


def attend(pieces, place, lows, ends, bounds, nctx, block_rows, *needed):
    total_rows = nctx * block_rows
    width = pieces[0].shape[1] // 3
    heads = width // HEAD_DIM
    steps = total_rows // TILE_Q
    grid_spec = pltpu.PrefetchScalarGridSpec(
        num_scalar_prefetch=3,
        grid=(steps,),
        in_specs=[pl.BlockSpec((2, TILE_Q), lambda i, *_: (0, i))]
        + [whole(piece.shape) for piece in pieces]
        + anywhere(len(needed)),
        out_specs=[
            pl.BlockSpec((TILE_Q, width), lambda i, *_: (i, 0)),
            pl.BlockSpec((TILE_Q, width), lambda i, *_: (i, 0)),
            pl.BlockSpec((heads, TILE_Q), lambda i, *_: (0, i)),
        ],
        scratch_shapes=[
            pltpu.VMEM((total_rows, 3 * width), BF16),
            pltpu.VMEM((total_rows // TILE_K, width, TILE_K), BF16),
            pltpu.VMEM((heads, HEAD_DIM, TILE_Q), F32),
            pltpu.VMEM((heads, 1, TILE_Q), F32),
            pltpu.VMEM((heads, 1, TILE_Q), F32),
            pltpu.VMEM((heads, TILE_K, TILE_Q), F32),
            pltpu.VMEM((heads, TILE_K, TILE_Q), BF16),
        ],
    )
    return pl.pallas_call(
        functools.partial(attend_kernel, nctx, heads, len(pieces), len(needed), block_rows),
        grid_spec=grid_spec,
        out_shape=[
            jax.ShapeDtypeStruct((total_rows, width), BF16),
            jax.ShapeDtypeStruct((total_rows, width), BF16),
            jax.ShapeDtypeStruct((heads, total_rows), F32),
        ],
        compiler_params=params(),
        cost_estimate=takes(200),
        name="attend",
    )(place, lows, ends, bounds, *pieces, *needed)


def attend_back_kernel(
    nctx, heads, count, extra, block_rows, place, lows, ends, bounds, logs, *refs
):
    pieces, refs = refs[:count], refs[count:]
    grad, attended, refs = refs[0], refs[1], refs[2 + extra :]
    here, near, far, refs = *refs[:3], refs[3:]
    held, turned, grad_keys, grad_values, grad_query, raw, raw_grad, chances, steps, merged = refs
    tile_q, tile_k = grad.shape[0], turned.shape[2]
    width = grad.shape[1]
    index = pl.program_id(0)
    scale = jnp.asarray(HEAD_DIM**-0.5, BF16)

    @pl.when(index == 0)
    def _():
        load_pieces(place[0], pieces, nctx, held, block_rows)
        for tile in range(turned.shape[0]):
            turned[tile] = jnp.transpose(
                held[tile * tile_k : (tile + 1) * tile_k, width : 2 * width]
            )
        grad_keys[...] = jnp.zeros_like(grad_keys)
        grad_values[...] = jnp.zeros_like(grad_values)

    query_rows = pl.ds(pl.multiple_of(index * tile_q, tile_q), tile_q)
    queries = stack_heads(held[query_rows, :width] * scale, heads)
    incoming = stack_heads(grad[...], heads)
    product = jnp.transpose(grad[...].astype(F32) * attended[...].astype(F32))
    centres = [
        jnp.sum(product[head * HEAD_DIM : (head + 1) * HEAD_DIM, :], axis=0, keepdims=True)
        for head in range(heads)
    ]
    first_key, last_key = bounds[0:1, :], bounds[1:2, :]
    grad_query[...] = jnp.zeros_like(grad_query)

    def one(tile, _):
        start = tile * tile_k
        key_rows = pl.ds(pl.multiple_of(start, tile_k), tile_k)
        last = jnp.minimum(last_key, ends[tile] - 1) - start
        first = first_key - start
        by_head = [slice(head * tile_q, (head + 1) * tile_q) for head in range(heads)]
        for head in range(heads):
            raw[head] = dot_turned(held[key_rows, width : 2 * width], queries[by_head[head]])
            raw_grad[head] = dot_turned(held[key_rows, 2 * width :], incoming[by_head[head]])
        for head in range(heads):
            for begin in range(0, tile_k, STRIP):
                at = slice(begin, begin + STRIP)
                row = lax.broadcasted_iota(jnp.int32, (STRIP, tile_q), 0) + begin
                allowed = (row <= last) & (row >= first)
                scores = raw[head, at, :] - logs[head : head + 1, :]
                chance = jnp.exp(jnp.where(allowed, scores, NEGATIVE))
                chances[head, at, :] = chance.astype(BF16)
                steps[head, at, :] = (chance * (raw_grad[head, at, :] - centres[head])).astype(BF16)
            grad_values[key_rows, :] += dot(chances[head], incoming[by_head[head]])
            grad_keys[key_rows, :] += dot(steps[head], queries[by_head[head]])
            keys = turned[tile, head * HEAD_DIM : (head + 1) * HEAD_DIM, :]
            grad_query[head] += dot(keys, steps[head])
        return 0

    upper = (index * tile_q + tile_q - 1) // tile_k + 1
    lax.fori_loop(lows[index], upper, one, 0)
    result = jnp.concatenate([grad_query[head] for head in range(heads)], axis=0)
    merged[query_rows, :width] = (jnp.transpose(result) * HEAD_DIM**-0.5).astype(BF16)

    @pl.when(index == pl.num_programs(0) - 1)
    def _():
        merged[:, width : 2 * width] = grad_keys[...].astype(BF16)
        merged[:, 2 * width :] = grad_values[...].astype(BF16)
        outs = [here, near] + [far.at[way] for way in range(nctx - 2)]
        for way, out in enumerate(outs):
            first = jnp.bitwise_xor(place[0], way) * block_rows
            out[...] = merged[pl.ds(pl.multiple_of(first, block_rows), block_rows), :]


def attend_back(pieces, place, lows, ends, bounds, logs, grad, attended, nctx, block_rows, *needed):
    total_rows, width = grad.shape
    heads = width // HEAD_DIM
    by_tile = pl.BlockSpec((TILE_Q, width), lambda i, *_: (i, 0))
    sent = (block_rows, 3 * width)
    sent = [sent, sent, (nctx - 2, *sent)]
    grid_spec = pltpu.PrefetchScalarGridSpec(
        num_scalar_prefetch=3,
        grid=(total_rows // TILE_Q,),
        in_specs=[
            pl.BlockSpec((2, TILE_Q), lambda i, *_: (0, i)),
            pl.BlockSpec((heads, TILE_Q), lambda i, *_: (0, i)),
        ]
        + [whole(piece.shape) for piece in pieces]
        + [by_tile] * 2
        + anywhere(len(needed)),
        out_specs=[whole(shape) for shape in sent],
        scratch_shapes=[
            pltpu.VMEM((total_rows, 3 * width), BF16),
            pltpu.VMEM((total_rows // TILE_K, width, TILE_K), BF16),
            pltpu.VMEM((total_rows, width), F32),
            pltpu.VMEM((total_rows, width), F32),
            pltpu.VMEM((heads, HEAD_DIM, TILE_Q), F32),
            pltpu.VMEM((heads, TILE_K, TILE_Q), F32),
            pltpu.VMEM((heads, TILE_K, TILE_Q), F32),
            pltpu.VMEM((heads, TILE_K, TILE_Q), BF16),
            pltpu.VMEM((heads, TILE_K, TILE_Q), BF16),
            pltpu.VMEM((total_rows, 3 * width), BF16),
        ],
    )
    return pl.pallas_call(
        functools.partial(
            attend_back_kernel, nctx, heads, len(pieces), len(needed), block_rows
        ),
        grid_spec=grid_spec,
        out_shape=[jax.ShapeDtypeStruct(shape, BF16) for shape in sent],
        compiler_params=params(),
        cost_estimate=takes(250),
        name="attend_back",
    )(place, lows, ends, bounds, logs, *pieces, grad, attended, *needed)


def mix_kernel(nctx, count, place, heads_in, weight, source, gain, bias, *refs):
    returned, mixed, *lows = refs[count:]
    rows, depth = mixed.shape
    step = pl.program_id(0)
    left = jnp.concatenate([heads_in[c, 0] for c in range(nctx)], axis=1)
    returned[...] = left

    @pl.when(step == 0)
    def _():
        mixed[...] = source[...].astype(F32)

    mixed[...] += dot_turned(left, weight[0])

    @pl.when(step == pl.num_programs(0) - 1)
    def _():
        values = mixed[...]
        values = values - jnp.mean(values, axis=1, keepdims=True)
        scaling = lax.rsqrt(jnp.mean(values * values, axis=1, keepdims=True) + EPSILON)
        values = (values * scaling * gain[...] + bias[...]).astype(BF16)
        part_rows = lows[0].shape[0]
        for part, low in enumerate(lows):
            low[...] = values[part * part_rows : (part + 1) * part_rows]


def mix(heads_in, weight, full, gain, bias, place, parts, *needed):
    nctx, tp, rows, piece = heads_in.shape
    depth = full.shape[1]
    head_width = nctx * piece
    grid_spec = pltpu.PrefetchScalarGridSpec(
        num_scalar_prefetch=1,
        grid=(tp,),
        in_specs=[
            pl.BlockSpec((nctx, 1, rows, piece), lambda k, s: (0, k, 0, 0)),
            pl.BlockSpec((1, depth, head_width), lambda k, s: (k, 0, 0)),
            pl.BlockSpec((rows, depth), lambda k, s: (s[0], 0)),
            whole((1, depth)),
            whole((1, depth)),
        ]
        + anywhere(len(needed)),
        out_specs=[
            pl.BlockSpec((rows, head_width), lambda k, s: (0, k)),
            whole((rows, depth)),
        ]
        + [whole((rows // parts, depth))] * parts,
    )
    return pl.pallas_call(
        functools.partial(mix_kernel, nctx, len(needed)),
        grid_spec=grid_spec,
        out_shape=[
            jax.ShapeDtypeStruct((rows, tp * head_width), BF16),
            jax.ShapeDtypeStruct((rows, depth), F32),
        ]
        + [jax.ShapeDtypeStruct((rows // parts, depth), BF16)] * parts,
        compiler_params=params(),
        cost_estimate=takes(50),
        name="mix",
    )(place, heads_in, weight, full, gain, bias, *needed)


def feed_kernel(cuts, parts, tp, first_one, place, low, cot, mixed, source, *refs):
    refs = refs[-(5 + parts + 4) :]
    kept, grad_gate, grad_up, hidden, out = refs[:5]
    partials, held, sems = refs[5 : 5 + parts], refs[-4:-1], refs[-1]
    unit = source.shape[1] // 3
    width = out.shape[2]

    def copies(index):
        first, size = cuts[index]
        at = pl.ds(first, size)
        return [
            pltpu.make_async_copy(
                source.at[:, pl.ds(which * unit, unit), at],
                held[which].at[:, :, at],
                sems.at[index * 3 + which],
            )
            for which in range(3)
        ]

    for index in range(len(cuts)):
        for copy in copies(index):
            copy.start()
    kept[...] = low[...]
    rows, depth = kept.shape[0] // parts, kept.shape[1]
    grads = jnp.concatenate([cot[block] for block in range(tp)], axis=1)
    for index, (first, size) in enumerate(cuts):
        for copy in copies(index):
            copy.wait()
        at = slice(first, first + size)
        gate_weight, up_weight, down_weight = [w[:, :, at].reshape(depth, size) for w in held]
        gate = dot(kept[...], gate_weight)
        up = dot(kept[...], up_weight)
        sigma = 1.0 / (1.0 + jnp.exp(-gate))
        active = gate * sigma
        hidden[:, at] = (active * up).astype(BF16)
        grad = dot(grads, down_weight)
        grad_gate[:, at] = (grad * up * sigma * (1.0 + gate * (1.0 - sigma))).astype(BF16)
        grad_up[:, at] = (grad * active).astype(BF16)
    gate_weight, up_weight, down_weight = [w[...].reshape(depth, w.shape[2]) for w in held]
    product = dot_turned(grad_gate[...], gate_weight) + dot_turned(grad_up[...], up_weight)
    for part in range(parts):
        partials[part][...] = product[part * rows : (part + 1) * rows].astype(BF16)
    values = dot_turned(hidden[...], down_weight)
    if first_one:
        values = values + mixed[...]
    for block in range(tp):
        out[block] = values[:, block * width : (block + 1) * width].astype(BF16)


def feed(low, cot, mixed, weights, step, tp, place, held, parts, *needed):
    rows, depth = low.shape
    part_rows = rows // parts
    blocks, triple, hidden = weights.shape
    cuts = []
    while sum(size for _, size in cuts) < hidden:
        first = sum(size for _, size in cuts)
        cuts.append((first, min(512, hidden - first)))
    by_owner = lambda columns: pl.BlockSpec(
        (rows, columns), lambda i, s: (lax.rem(s[0] - step + tp, tp), 0)
    )
    width = depth // tp
    blocks_of_owner = pl.BlockSpec(
        (tp, rows, width), lambda i, s: (0, lax.rem(s[0] - step + tp, tp), 0)
    )
    grid_spec = pltpu.PrefetchScalarGridSpec(
        num_scalar_prefetch=1,
        grid=(1,),
        in_specs=[whole((rows, depth)), blocks_of_owner, whole(mixed.shape)]
        + anywhere(1 + len(held) + len(needed)),
        out_specs=[by_owner(depth)]
        + [by_owner(hidden)] * 3
        + [blocks_of_owner]
        + [whole((part_rows, depth))] * parts,
        scratch_shapes=[pltpu.VMEM((blocks, triple // 3, hidden), BF16)] * 3
        + [pltpu.SemaphoreType.DMA((3 * len(cuts),))],
    )
    return pl.pallas_call(
        functools.partial(feed_kernel, tuple(cuts), parts, tp, step == 0),
        grid_spec=grid_spec,
        out_shape=[
            jax.ShapeDtypeStruct((tp * rows, columns), BF16)
            for columns in (depth, hidden, hidden, hidden)
        ]
        + [jax.ShapeDtypeStruct((tp, tp * rows, width), BF16)]
        + [jax.ShapeDtypeStruct((part_rows, depth), BF16)] * parts,
        input_output_aliases={5 + index: index for index in range(len(held))},
        compiler_params=params(),
        cost_estimate=takes(100),
        name="feed",
    )(place, low, cot, mixed, weights, *held, *needed)


def blame_halves(lefts, rights, place, unit, *needed, held=(), offset=0, total=None):
    rows, other = rights[0].shape
    picked = lefts[1].shape[1] // unit
    chosen = pl.BlockSpec((rows, unit), lambda j, s: (0, 2 * (j ^ s[3]) + s[1] % 2))
    if lefts[0].ndim == 3:
        per = lefts[0].shape[2] // unit
        chosen = pl.BlockSpec(
            (1, rows, unit),
            lambda j, s: (
                (2 * (j ^ s[3]) + s[1] % 2) // per,
                0,
                lax.rem(2 * (j ^ s[3]) + s[1] % 2, per),
            ),
        )
    cut = pl.BlockSpec((rows, unit), lambda j, s: (0, j ^ s[3]))
    shapes = [(2, unit // 2, total or other)] * 4

    def kernel(place, left_here, left_there, right_here, right_there, *refs):
        outs, spare, sems = refs[len(held) + len(needed) : -2], refs[-2], refs[-1]
        product = 0.0
        for left, right in ((left_here, right_here), (left_there, right_there)):
            ours = left[0] if len(left.shape) == 3 else left[...]
            product = product + lax.dot_general(
                ours, right[...], (((0,), (0,)), ((), ())), preferred_element_type=F32
            )
        product = product.astype(BF16)
        for j in range(picked):

            @pl.when(pl.program_id(0) == j)
            def _():
                first, second = spare.at[j // 2, j % 2], spare.at[2 + j % 2, j // 2]
                first[...], second[...] = product[: unit // 2], product[unit // 2 :]

        @pl.when(pl.program_id(0) == picked - 1)
        def _():
            moves = [
                pltpu.make_async_copy(
                    spare.at[index], out.at[:, :, pl.ds(offset, other)], sems.at[index]
                )
                for index, out in enumerate(outs)
            ]
            for move in moves:
                move.start()
            for move in moves:
                move.wait()

    grid_spec = pltpu.PrefetchScalarGridSpec(
        num_scalar_prefetch=1,
        grid=(picked,),
        in_specs=[chosen, cut]
        + [whole((rows, other))] * 2
        + anywhere(len(held) + len(needed)),
        out_specs=anywhere(4),
        scratch_shapes=[
            pltpu.VMEM((4, 2, unit // 2, other), BF16),
            pltpu.SemaphoreType.DMA((4,)),
        ],
    )
    place = jnp.concatenate([place, place[2:3] * 2 + place[1:2] // 2])
    return pl.pallas_call(
        kernel,
        grid_spec=grid_spec,
        out_shape=[jax.ShapeDtypeStruct(shape, BF16) for shape in shapes],
        input_output_aliases={5 + index: index for index in range(len(held))},
        compiler_params=params(),
        cost_estimate=takes(60),
        name="blame_halves",
    )(place, *lefts, *rights, *held, *needed)


def blame(left, right, *needed):
    rows, columns = left.shape
    if right.ndim == 3:
        steps, other = right.shape[0], right.shape[2]
        in_specs = [whole((rows, columns)), pl.BlockSpec((1, rows, other), lambda j: (j, 0, 0))]
        target, shape = pl.BlockSpec((columns, other), lambda j: (0, j)), (columns, steps * other)
    else:
        steps, other = 4, right.shape[1]
        in_specs = [pl.BlockSpec((rows, columns // steps), lambda j: (0, j)), whole((rows, other))]
        target, shape = pl.BlockSpec((columns // steps, other), lambda j: (j, 0)), (columns, other)

    def kernel(left, right, *refs):
        theirs = right[0] if len(right.shape) == 3 else right[...]
        refs[-1][...] = lax.dot_general(
            left[...], theirs, (((0,), (0,)), ((), ())), preferred_element_type=F32
        ).astype(BF16)

    return pl.pallas_call(
        kernel,
        grid=(steps,),
        in_specs=in_specs + anywhere(len(needed)),
        out_specs=target,
        out_shape=jax.ShapeDtypeStruct(shape, BF16),
        compiler_params=params(),
        cost_estimate=takes(60),
        name="blame",
    )(left, right, *needed)


def turn_kernel(nctx, count, parts, unit, place, *refs):
    arrived, own = refs[:parts], refs[parts : 2 * parts]
    mixed, cot, gain = refs[2 * parts : 2 * parts + 3]
    weight, refs = refs[2 * parts + 3], refs[2 * parts + 4 + count :]
    out, grad_mixed, grad_low, gain_grad, shift_grad, half = refs
    rows, depth = mixed.shape
    piece = out.shape[3]

    @pl.when(pl.program_id(0) == 0)
    def _():
        incoming = jnp.concatenate(
            [there[...].astype(F32) + here[...].astype(F32) for there, here in zip(arrived, own)]
        )
        values = mixed[...]
        values = values - jnp.mean(values, axis=1, keepdims=True)
        scaling = lax.rsqrt(jnp.mean(values * values, axis=1, keepdims=True) + EPSILON)
        normed = values * scaling
        shift_grad[...] = jnp.sum(incoming, axis=0, keepdims=True)
        gain_grad[...] = jnp.sum(incoming * normed, axis=0, keepdims=True)
        scaled = incoming * gain[...]
        grads = jnp.concatenate([cot[block] for block in range(cot.shape[0])], axis=1)
        total = grads.astype(F32) + scaling * (
            scaled
            - jnp.mean(scaled, axis=1, keepdims=True)
            - normed * jnp.mean(scaled * normed, axis=1, keepdims=True)
        )
        grad_mixed[...] = total
        grad_low[...] = total.astype(BF16)
        write_half(half, grad_low, 1 - lax.rem(place[1], 2), unit)

    product = dot(grad_low[...], weight[0])
    for c in range(nctx):
        out[c, 0] = product[:, c * piece : (c + 1) * piece].astype(BF16)


def turn(arrived, own, mixed, cot, gain, weight, place, nctx, tp, unit, *needed):
    rows, depth = mixed.shape
    parts = len(arrived)
    head_width = weight.shape[2]
    piece = head_width // nctx
    grid_spec = pltpu.PrefetchScalarGridSpec(
        num_scalar_prefetch=1,
        grid=(tp,),
        in_specs=[whole((rows // parts, depth))] * (2 * parts)
        + [whole((rows, depth))]
        + [
            pl.BlockSpec((tp, rows, depth // tp), lambda k, s: (0, s[0], 0)),
            whole((1, depth)),
            pl.BlockSpec((1, depth, head_width), lambda k, s: (k, 0, 0)),
        ]
        + anywhere(len(needed)),
        out_specs=[
            pl.BlockSpec((nctx, 1, rows, piece), lambda k, s: (0, k, 0, 0)),
            whole((rows, depth)),
            whole((rows, depth)),
            whole((1, depth)),
            whole((1, depth)),
            whole((rows, depth // 2)),
        ],
    )
    return pl.pallas_call(
        functools.partial(turn_kernel, nctx, len(needed), parts, unit),
        grid_spec=grid_spec,
        out_shape=[
            jax.ShapeDtypeStruct((nctx, tp, rows, piece), BF16),
            jax.ShapeDtypeStruct((rows, depth), F32),
            jax.ShapeDtypeStruct((rows, depth), BF16),
            jax.ShapeDtypeStruct((1, depth), F32),
            jax.ShapeDtypeStruct((1, depth), F32),
            jax.ShapeDtypeStruct((rows, depth // 2), BF16),
        ],
        compiler_params=params(),
        cost_estimate=takes(60),
        name="turn",
    )(place, *arrived, *own, mixed, cot, gain, weight, *needed)


def finish_kernel(nctx, tp, extra_count, place, *refs):
    pieces = refs[:nctx]
    cosine, sine_up, sine_down, full, extra, gain = refs[nctx : nctx + 6]
    weight, refs = refs[nctx + 6], refs[nctx + 7 + extra_count :]
    outs = refs[:tp]
    low, bias_grad, gain_grad, shift_grad, spare = refs[tp:]
    rows, wide = pieces[0].shape
    piece = wide // 3
    width = outs[0].shape[1]
    strip = spare.shape[0]
    extra_rows = extra.shape[0]

    @pl.when(pl.program_id(0) == 0)
    def _():
        bias_grad[...] = jnp.zeros_like(bias_grad)
        gain_grad[...] = jnp.zeros_like(gain_grad)
        shift_grad[...] = jnp.zeros_like(shift_grad)

    for step in range(nctx):
        source = jnp.bitwise_xor(place[1], step)
        for part in range(3):
            values = pieces[step][:, part * piece : (part + 1) * piece].astype(F32)
            if part < 2:
                values = (
                    values * cosine[...]
                    - pltpu.roll(values, piece - ROT // 2, 1) * sine_up[...]
                    - pltpu.roll(values, ROT // 2, 1) * sine_down[...]
                )
            columns = pl.ds(pl.multiple_of(source * wide + part * piece, piece), piece)
            bias_grad[:, columns] += jnp.sum(values, axis=0, keepdims=True)
            low[:, columns] = values.astype(BF16)

    incoming = dot_turned(low[...], weight[...])
    source = full[...].astype(F32)
    source = source - jnp.mean(source, axis=1, keepdims=True)
    scaling = lax.rsqrt(jnp.mean(source * source, axis=1, keepdims=True) + EPSILON)
    normed = source * scaling
    shift_grad[...] += jnp.sum(incoming, axis=0, keepdims=True)
    gain_grad[...] += jnp.sum(incoming * normed, axis=0, keepdims=True)
    scaled = incoming * gain[...]
    spare[...] = scaling * (
        scaled
        - jnp.mean(scaled, axis=1, keepdims=True)
        - normed * jnp.mean(scaled * normed, axis=1, keepdims=True)
    )
    first = pl.program_id(0) * strip
    wanted = place[0] * extra_rows

    if strip <= extra_rows:

        @pl.when((first >= wanted) & (first < wanted + extra_rows))
        def _():
            spare[...] += extra[pl.ds(pl.multiple_of(first - wanted, strip), strip), :]

    else:

        @pl.when((wanted >= first) & (wanted < first + strip))
        def _():
            spare[pl.ds(pl.multiple_of(wanted - first, extra_rows), extra_rows), :] += extra[...]

    for step, out in enumerate(outs):
        owner = lax.rem(place[0] - step + tp, tp)
        out[...] = spare[:, pl.ds(pl.multiple_of(owner * width, width), width)].astype(BF16)


def finish(pieces, place, tables, full, extra, gain, weight, tp, *needed):
    rows, wide = pieces[0].shape
    depth = full.shape[1]
    total = weight.shape[1]
    strip = 256
    steps = rows // strip
    width = depth // tp
    nctx = len(pieces)
    by_rows = lambda columns: pl.BlockSpec((strip, columns), lambda i, s: (i, 0))
    grid_spec = pltpu.PrefetchScalarGridSpec(
        num_scalar_prefetch=1,
        grid=(steps,),
        in_specs=[by_rows(wide)] * nctx
        + [by_rows(2 * HEAD_DIM)] * 3
        + [
            by_rows(depth),
            whole(extra.shape),
            whole((1, depth)),
        ]
        + [whole(weight.shape)]
        + anywhere(len(needed)),
        out_specs=[by_rows(width)] * tp
        + [
            by_rows(total),
            whole((1, total)),
            whole((1, depth)),
            whole((1, depth)),
        ],
        scratch_shapes=[pltpu.VMEM((strip, depth), F32)],
    )
    return pl.pallas_call(
        functools.partial(finish_kernel, nctx, tp, len(needed)),
        grid_spec=grid_spec,
        out_shape=[jax.ShapeDtypeStruct((rows, width), BF16)] * tp
        + [
            jax.ShapeDtypeStruct((rows, total), BF16),
            jax.ShapeDtypeStruct((1, total), F32),
            jax.ShapeDtypeStruct((1, depth), F32),
            jax.ShapeDtypeStruct((1, depth), F32),
        ],
        compiler_params=params(),
        cost_estimate=takes(70),
        name="finish",
    )(place, *pieces, *tables, full, extra, gain, weight, *needed)


def join(rings, place, unit):
    parts, tp = len(rings), len(rings[0])
    rows, width = rings[0][0].shape

    def kernel(place, *refs):
        for part in range(parts):
            for step in range(tp):
                owner = lax.rem(place[0] - step + tp, tp)
                refs[-2][owner, part * rows : (part + 1) * rows, :] = refs[part * tp + step][...]
        per, half = width // unit, 1 - lax.rem(place[1], 2)
        for block in range(tp * per // 2):
            index = 2 * block + half if unit % 128 == 0 else 0
            first = pl.multiple_of(lax.rem(index, per) * unit, unit)
            if unit % 128:
                first = 0
            refs[-1][:, block * unit : (block + 1) * unit] = refs[-2][
                lax.div(index, per), :, pl.ds(first, unit)
            ]

    grid_spec = pltpu.PrefetchScalarGridSpec(
        num_scalar_prefetch=1,
        grid=(1,),
        in_specs=[whole((rows, width))] * (parts * tp),
        out_specs=[whole((tp, parts * rows, width)), whole((parts * rows, tp * width // 2))],
    )
    return pl.pallas_call(
        kernel,
        grid_spec=grid_spec,
        out_shape=[
            jax.ShapeDtypeStruct((tp, parts * rows, width), BF16),
            jax.ShapeDtypeStruct((parts * rows, tp * width // 2), BF16),
        ],
        compiler_params=params(),
        cost_estimate=takes(10),
        name="join",
    )(place, *[block for blocks in rings for block in blocks])


def pack_kernel(gate, up, down, out):
    rows = gate.shape[0]
    out[:rows] = gate[...]
    out[rows : 2 * rows] = up[...]
    out[2 * rows :] = jnp.transpose(down[...])


def pack(gate, up, down):
    rows, columns = gate.shape
    return pl.pallas_call(
        pack_kernel,
        out_shape=jax.ShapeDtypeStruct((3 * rows, columns), BF16),
        compiler_params=params(),
        cost_estimate=takes(10),
        name="pack",
    )(gate, up, down)


def contract_rows(left, right):
    return lax.dot_general(left, right, (((0,), (0,)), ((), ())), preferred_element_type=F32)


def pick(stack, index):
    return lax.dynamic_index_in_dim(stack, index, 0, keepdims=False)


def shards(
    nfsdp,
    nctx,
    tp,
    inputs,
    cotangent,
    first_gain,
    first_bias,
    qkv_weight,
    qkv_bias,
    out_weight,
    second_gain,
    second_bias,
    gate_weight,
    up_weight,
    down_weight,
    lengths,
    fill_counts,
):
    data = ("fsdp", "ctx")
    ndata = nfsdp * nctx
    block_rows, width = inputs.shape
    depth = tp * width
    half_depth = depth // 2
    unit = depth // ndata
    tensor_index = lax.axis_index("tp").astype(jnp.int32)
    context_index = lax.axis_index("ctx").astype(jnp.int32)
    fsdp_index = lax.axis_index("fsdp").astype(jnp.int32)
    part_rows = block_rows // tp
    chunk_rows = block_rows // CHUNKS
    head_width = qkv_weight.shape[2]
    piece = head_width // nctx
    wide = 3 * piece

    square = nfsdp == 2 and nctx == 4 and unit % 128 == 0
    place = jnp.stack([tensor_index, context_index, fsdp_index])

    def shift(value, step):
        return lax.ppermute(value, "tp", [(i, (i + step) % tp) for i in range(tp)])

    def swap(value, step):
        return lax.ppermute(value, "ctx", [(i, i ^ step) for i in range(nctx)])

    core_index = context_index % 2
    groups = [list(range(0, ndata, 2)), list(range(1, ndata, 2))]
    def mate(value):
        return swap(value, 1)

    def send(here, near, far, *needed):
        far = swap(far, 2)
        return [here, swap(near, 1), far[0], swap(tie(far[1], *needed), 1)]

    def scatter_half(value, axis):
        return lax.psum_scatter(
            value, data, scatter_dimension=axis, tiled=True, axis_index_groups=groups
        )

    def scatter(value, axis):
        return lax.psum_scatter(value, data, scatter_dimension=axis, tiled=True)

    def cross(value):
        return lax.ppermute(value, "fsdp", [(i, i ^ 1) for i in range(nfsdp)])

    def square_once(parts):
        near, far, low, high = parts
        return total(near, cross(far)), total(low, swap(high, 2))

    def square_twice(first, second):
        first = first[0].astype(F32) + swap(first[1], 2).astype(F32)
        second = second[0].astype(F32) + cross(second[1]).astype(F32)
        return jnp.concatenate([first, second], axis=0)

    def total(left, right):
        return (left.astype(F32) + right.astype(F32)).astype(BF16)

    owners = [(tensor_index - step + tp) % tp for step in range(tp)]

    own_qkv = (
        qkv_weight.reshape(-1, 3, nctx, piece).transpose(0, 2, 1, 3).reshape(-1, 3 * head_width)
    )
    full_qkv = lax.all_gather(own_qkv, data, axis=0, tiled=True)
    own_feed = pack(gate_weight, up_weight, down_weight)
    feed_weights = lax.all_gather(own_feed, data, axis=0, tiled=True).reshape(ndata, 3 * unit, -1)

    validity, position, first_key, last_key = layout(lengths[0], fill_counts[0], block_rows)
    own_position = lax.dynamic_slice_in_dim(position, context_index * block_rows, block_rows, 0)
    tables = rotary_tables(own_position)
    bounds = jnp.stack([first_key, last_key])
    tile_first = first_key[::TILE_Q]
    tile_count = tile_first.shape[0]
    lows = jnp.where(validity[::TILE_Q], tile_first // TILE_K, tile_count * TILE_Q).astype(jnp.int32)
    key_block = jnp.arange(0, nctx * block_rows, TILE_K, dtype=jnp.int32) // block_rows
    ends = (
        key_block * block_rows
        + jnp.sum(
            jnp.where(
                key_block[:, None] == jnp.arange(nctx, dtype=jnp.int32)[None, :],
                fill_counts[0][None, :],
                0,
            ),
            axis=1,
        )
    ).astype(jnp.int32)

    flat_bias = qkv_bias.reshape(3, nctx, piece).transpose(1, 0, 2).reshape(1, -1)
    gain_one, bias_one = first_gain[None], first_bias[None]
    gain_two, bias_two = second_gain[None], second_bias[None]

    rings = [[inputs[c * chunk_rows : (c + 1) * chunk_rows]] for c in range(CHUNKS)]
    share = unit // CHUNKS
    for chunk in range(CHUNKS):
        carried = out_weight.T[chunk * share : (chunk + 1) * share]
        rings[chunk][0] = jnp.concatenate([rings[chunk][0], carried], axis=0)
    for chunk in range(CHUNKS):
        for _ in range(tp - 1):
            rings[chunk].append(shift(rings[chunk][-1], 1))
            if len(rings[chunk]) == 2:
                rings[chunk][-1] = tie(rings[chunk][-1], own_feed)
    all_low, full, low_half, *outgoing, stack = project(
        rings, place, gain_one, bias_one, full_qkv, flat_bias, tables, nctx, unit
    )
    full_out = lax.all_gather(stack, data, axis=1, tiled=True)

    cot = tie(cotangent, *[blocks[-1] for blocks in rings])
    cot_rings = [[cot[c * chunk_rows : (c + 1) * chunk_rows]] for c in range(CHUNKS)]
    for blocks in cot_rings:
        for _ in range(tp - 1):
            blocks.append(shift(blocks[-1], 1))
    pieces = send(*outgoing, *[blocks[max(tp - 2, 0)] for blocks in cot_rings])

    attended, outgoing, logs = attend(
        pieces,
        place[1:2],
        lows,
        ends,
        bounds,
        nctx,
        block_rows,
        feed_weights,
    )
    cot, cot_half = join(cot_rings, place, unit)
    arrived = lax.all_to_all(
        tie(outgoing, *[blocks[-1] for blocks in cot_rings]).reshape(nctx * tp, part_rows, piece),
        ("ctx", "tp"),
        split_axis=0,
        concat_axis=0,
        tiled=True,
    )
    returned, mixed, second_low = mix(
        arrived.reshape(nctx, tp, part_rows, piece),
        full_out,
        full,
        gain_two,
        bias_two,
        place,
        1,
    )

    arrived, held, partials, travelling = second_low, [], [], None
    for step in range(tp):
        coming = shift(arrived, 1) if step < tp - 1 else None
        needed = travelling if step == tp - 1 and step > 2 else []
        *held, first, second = feed(
            arrived, cot, mixed, feed_weights, step, tp, place, held, HALVES, *needed
        )
        partials.append([first, second])
        if step == 1 % tp:
            travelling = partials[step]
        elif step > 1:
            travelling = [
                total(shift(value, 1), kept) for value, kept in zip(travelling, partials[step])
            ]
        if step == 0 and coming is not None:
            coming = tie(coming, partials[0][0])
        arrived = coming
    all_second, all_gate, all_up, hidden, feedforward = held

    last = [shift(value, 1) for value in travelling]
    half_gate = blame(all_second, all_gate, *travelling)
    half_up = blame(all_second, all_up, *travelling)
    grad_heads, grad_mixed, mixed_low, gain_grad_two, shift_grad_two, mixed_half = turn(
        last,
        partials[0],
        mixed,
        cot,
        gain_two,
        full_out,
        place,
        nctx,
        tp,
        unit,
        half_gate,
        half_up,
    )
    grad_heads = lax.all_to_all(
        grad_heads.reshape(nctx * tp, part_rows, piece),
        ("ctx", "tp"),
        split_axis=0,
        concat_axis=0,
        tiled=True,
    ).reshape(nctx * block_rows, piece)

    total_gate = scatter(tie(half_gate, mixed_low), 0).astype(F32)
    total_up = scatter(tie(half_up, mixed_low), 0).astype(F32)
    half_out = blame(mixed_low, returned)
    total_out = scatter(tie(half_out, grad_heads), 0)

    feedforward = tie(feedforward, grad_heads)
    inner = hidden.shape[1]
    both = inner + 3 * head_width
    if square:
        parts = blame_halves(
            (cot, mate(cot_half)), (hidden, mate(hidden)), place, unit, total=both
        )
        half_down = parts[0]
    else:
        half_down = blame(hidden, cot)
        total_down = scatter(half_down, 1).astype(F32)
    layer_out = [pick(feedforward, owners[1 % tp])]
    for step in range(1, tp):
        kept = pick(feedforward, owners[(step + 1) % tp])
        if step == 2:
            layer_out.append(add(shift(layer_out[-1], 1), kept, half_down))
        else:
            layer_out.append(total(shift(layer_out[-1], 1), kept))

    grad_pieces = attend_back(
        pieces, place[1:2], lows, ends, bounds, logs, grad_heads, attended, nctx, block_rows, half_out
    )
    arrived = send(*grad_pieces, *layer_out[max(tp - 2, 0) : tp - 1])
    layer_out = layer_out[-1]
    low_halves = mate(low_half) if square else low_half
    needed = [layer_out, low_halves]
    *partial, all_grad, bias_grad, gain_grad, shift_grad = finish(
        arrived, place, tables, full, grad_mixed, gain_one, full_qkv, tp, *needed
    )
    if square:
        parts = blame_halves(
            (all_low, low_halves),
            (all_grad, mate(all_grad)),
            place,
            unit,
            held=parts,
            offset=inner,
            total=both,
        )
    else:
        parts = []
    def exchange(value, axis, steps, size):
        for step in steps:
            value = value + lax.ppermute(value, axis, [(i, i ^ step) for i in range(size)])
        return value

    def powers(first, size):
        return [1 << bit for bit in range(first, size.bit_length() - 1)]

    small = jnp.concatenate([gain_grad, shift_grad, gain_grad_two, shift_grad_two], axis=1)
    small = sum([shift(small, step) for step in range(1, tp)], small)
    small = jnp.concatenate([bias_grad, small], axis=1)
    travelling, ring_steps = partial[1 % tp], []
    once = square_once(parts) if square else ()
    needed = [[total_gate, total_up, small, *parts], [], [*once]]
    for step in range(1, tp):
        travelling = add(
            shift(travelling, 1), partial[(step + 1) % tp], *(needed[step - 1] if step < 4 else [])
        )
        if step == 1:
            out_parts = jnp.swapaxes(
                tie(total_out, travelling).reshape(-1, tp, head_width), 0, 1
            )
            total_out = pick(out_parts, tensor_index).astype(F32)
            for ahead in range(1, tp):
                total_out = total_out + shift(pick(out_parts, (tensor_index + ahead) % tp), ahead).astype(F32)
            total_out = total_out.T
            needed[2].append(total_out)
        if step < 3:
            bits = powers(0, min(nctx, 2)) if step == 1 else powers(1, nctx)
            small = exchange(tie(small, travelling), "ctx", bits, nctx)
            needed[step].append(small)
    small = exchange(tie(small, travelling), "fsdp", powers(0, nfsdp), nfsdp)
    grad_inputs = travelling
    if square:
        totals = square_twice(*once)
        total_down, total_qkv = totals[:, :inner].T, totals[:, inner:]
    else:
        total_qkv = scatter(blame(all_low, all_grad), 0).astype(F32)

    total_qkv = (
        total_qkv
        .reshape(-1, nctx, 3, piece)
        .transpose(0, 2, 1, 3)
        .reshape(-1, 3, head_width)
    )


    bias_total, small = small[:, : 3 * head_width], small[:, 3 * head_width :]
    bias_total = bias_total.reshape(nctx, 3, piece).transpose(1, 0, 2).reshape(3, head_width)
    small = small.reshape(4, depth)
    return (
        layer_out,
        grad_inputs,
        small[0],
        small[1],
        total_qkv,
        bias_total,
        total_out,
        small[2],
        small[3],
        total_gate,
        total_up,
        total_down,
    )


def solution(mesh):
    data = ("fsdp", "ctx")
    by_rows = P(data, "tp")
    by_columns = P("tp", data)
    qkv = P(data, None, "tp")
    return jax.shard_map(
        functools.partial(shards, mesh.shape["fsdp"], mesh.shape["ctx"], mesh.shape["tp"]),
        mesh=mesh,
        in_specs=(
            by_rows,
            by_rows,
            P(),
            P(),
            qkv,
            P(None, "tp"),
            by_columns,
            P(),
            P(),
            by_rows,
            by_rows,
            by_columns,
            P("fsdp", None),
            P("fsdp", None),
        ),
        out_specs=(
            by_rows,
            by_rows,
            P(),
            P(),
            qkv,
            P(None, "tp"),
            by_columns,
            P(),
            P(),
            by_rows,
            by_rows,
            by_columns,
        ),
        check_vma=False,
    )
```

```python
import functools

import jax
import jax.numpy as jnp
from jax import lax
from jax.experimental import pallas as pl
from jax.experimental.pallas import tpu as pltpu
from jax.sharding import PartitionSpec as P

HEAD_DIM = 64
ROT = 16
EPSILON = 1e-05
NEGATIVE = -1e30
FLOOR = -1e20
VMEM_LIMIT = 56 * 1024 * 1024
TILE_Q = 512
TILE_K = 512
STRIP = 32
CHUNKS = 2
HALVES = 2

F32 = jnp.float32
BF16 = jnp.bfloat16


def layout(lengths, fill_counts, block_rows):
    blocks_count = fill_counts.shape[0]
    seq_count = lengths.shape[0]
    slot_index = jnp.arange(blocks_count * block_rows, dtype=jnp.int32)
    block_of = slot_index // block_rows
    within = slot_index - block_of * block_rows
    chooser = block_of[:, None] == jnp.arange(blocks_count, dtype=jnp.int32)[None, :]
    fill_here = jnp.sum(jnp.where(chooser, fill_counts[None, :], 0), axis=1)
    before = jnp.cumsum(fill_counts) - fill_counts
    before_here = jnp.sum(jnp.where(chooser, before[None, :], 0), axis=1)
    validity = within < fill_here
    used_index = before_here + within
    seq_ends = jnp.cumsum(lengths)
    sequence = jnp.sum((used_index[:, None] >= seq_ends[None, :]).astype(jnp.int32), axis=1)
    seq_starts = seq_ends - lengths
    picker = sequence[:, None] == jnp.arange(seq_count, dtype=jnp.int32)[None, :]
    start_here = jnp.sum(jnp.where(picker, seq_starts[None, :], 0), axis=1)
    after = before + fill_counts
    start_block = jnp.sum((seq_starts[:, None] >= after[None, :]).astype(jnp.int32), axis=1)
    start_block = jnp.minimum(start_block, blocks_count - 1)
    block_pick = start_block[:, None] == jnp.arange(blocks_count, dtype=jnp.int32)[None, :]
    start_before = jnp.sum(jnp.where(block_pick, before[None, :], 0), axis=1)
    start_slot = start_block * block_rows + seq_starts - start_before
    slot_here = jnp.sum(jnp.where(picker, start_slot[None, :], 0), axis=1)
    first_key = jnp.where(validity, slot_here, 0).astype(jnp.int32)
    last_key = jnp.where(validity, slot_index, -1).astype(jnp.int32)
    return (validity, used_index - start_here, first_key, last_key)


def rotary_tables(position):
    half = ROT // 2
    lane = jnp.arange(2 * HEAD_DIM, dtype=jnp.int32) % HEAD_DIM
    frequency = 10000.0 ** (-(2.0 * (lane % half).astype(F32)) / ROT)
    angles = position.astype(F32)[:, None] * frequency[None, :]
    cosine, sine = jnp.cos(angles), jnp.sin(angles)
    lane = lane[None, :]
    return (
        jnp.where(lane < ROT, cosine, 1.0),
        jnp.where(lane < half, -sine, 0.0),
        jnp.where((lane >= half) & (lane < ROT), sine, 0.0),
    )


def params(**extra):
    return pltpu.CompilerParams(vmem_limit_bytes=VMEM_LIMIT, **extra)


def takes(microseconds):
    return pl.CostEstimate(
        flops=int(microseconds * 1e8), bytes_accessed=0, transcendentals=0
    )


def whole(shape):
    return pl.BlockSpec(shape, lambda *_: (0,) * len(shape))


def anywhere(count):
    return [pl.BlockSpec(memory_space=pl.ANY)] * count


def write_half(out, values, half, unit):
    if unit % 128:
        out[...] = values[:, : out.shape[1]]
        return
    for block in range(out.shape[1] // unit):
        first = pl.multiple_of((2 * block + half) * unit, unit)
        out[:, block * unit : (block + 1) * unit] = values[:, pl.ds(first, unit)]


def dot(left, right):
    return jnp.dot(left, right, preferred_element_type=F32)


def dot_turned(left, right):
    return lax.dot_general(left, right, (((1,), (1,)), ((), ())), preferred_element_type=F32)


def tie(value, *needed):
    def kernel(*refs):
        del refs

    return pl.pallas_call(
        kernel,
        in_specs=anywhere(1 + len(needed)),
        out_specs=pl.BlockSpec(memory_space=pl.ANY),
        out_shape=jax.ShapeDtypeStruct(value.shape, value.dtype),
        input_output_aliases={0: 0},
        name="tie",
    )(value, *needed)


def add_kernel(left, right, *refs):
    refs[-1][...] = (left[...].astype(F32) + right[...].astype(F32)).astype(BF16)


def add(left, right, *needed):
    rows, columns = left.shape
    strip = min(rows, 512)
    block = pl.BlockSpec((strip, columns), lambda i: (i, 0))
    return pl.pallas_call(
        add_kernel,
        grid=(rows // strip,),
        in_specs=[block, block] + anywhere(len(needed)),
        out_specs=block,
        out_shape=jax.ShapeDtypeStruct(left.shape, BF16),
        compiler_params=params(),
        cost_estimate=takes(10),
        name="ring_add",
    )(left, right, *needed)


def project_kernel(tp, chunks, per, unit, place, *refs):
    rings, refs = refs[: tp * chunks], refs[tp * chunks :]
    gain, bias, weight, weight_bias, cosine, sine_up, sine_down = refs[:7]
    low, full, half, here, near, far, stack = refs[7:]
    outs = [here, near] + [far.at[way] for way in range(far.shape[0])]
    rows, width = low.shape[0] // chunks, rings[0].shape[1]
    depth = tp * width
    wide = here.shape[1]
    piece = wide // 3
    step = pl.program_id(0)

    @pl.when(pl.program_id(0) == 0)
    def _():
        strip = 128
        for start in range(0, rows * chunks, strip):
            chunk, first = start // rows, start % rows
            blocks = rings[chunk * tp : (chunk + 1) * tp]
            at = slice(start, start + strip)
            inner = slice(first, first + strip)
            parts = [block[inner, :].astype(F32) for block in blocks]
            centre = sum(jnp.sum(part, axis=1, keepdims=True) for part in parts) / depth
            parts = [part - centre for part in parts]
            spread = sum(jnp.sum(part * part, axis=1, keepdims=True) for part in parts) / depth
            scaling = lax.rsqrt(spread + EPSILON)
            for step in range(tp):
                owner = lax.rem(place[0] - step + tp, tp)
                columns = pl.ds(pl.multiple_of(owner * width, width), width)
                low[at, columns] = (
                    parts[step] * scaling * gain[:, columns] + bias[:, columns]
                ).astype(BF16)
                full[at, columns] = blocks[step][inner, :]
        write_half(half, low, 1 - lax.rem(place[1], 2), unit)
        share = rings[0].shape[0] - rows
        for chunk in range(chunks):
            for step in range(tp):
                owner = lax.rem(place[0] - step + tp, tp)
                stack[owner, chunk * share : (chunk + 1) * share, :] = rings[chunk * tp + step][
                    rows:, :
                ]

    product = dot(low[...], weight[...]) + weight_bias[...]
    groups = []
    for group in range(per):
        parts = []
        for part in range(3):
            first = (group * 3 + part) * piece
            values = product[:, first : first + piece]
            if part < 2:
                values = (
                    values * cosine[...]
                    + pltpu.roll(values, piece - ROT // 2, 1) * sine_up[...]
                    + pltpu.roll(values, ROT // 2, 1) * sine_down[...]
                )
            parts.append(values.astype(BF16))
        groups.append(parts)
    flip = lax.rem(place[1], per)
    for way, out in enumerate(outs):
        for group in range(per):

            @pl.when((step == way // per) & (jnp.bitwise_xor(group, flip) == way % per))
            def _():
                for part in range(3):
                    out[:, part * piece : (part + 1) * piece] = groups[group][part]


def project(rings, place, gain, bias, weight, weight_bias, tables, nctx, unit):
    chunks, tp = len(rings), len(rings[0])
    rows, width = tables[0].shape[0], rings[0][0].shape[1]
    depth = tp * width
    total = weight.shape[1]
    wide = total // nctx
    per = 2 if nctx % 2 == 0 else 1
    grid_spec = pltpu.PrefetchScalarGridSpec(
        num_scalar_prefetch=1,
        grid=(nctx // per,),
        in_specs=[whole(rings[0][0].shape)] * (tp * chunks)
        + [whole((1, depth))] * 2
        + [
            pl.BlockSpec((depth, per * wide), lambda i, s: (0, jnp.bitwise_xor(i, s[1] // per))),
            pl.BlockSpec((1, per * wide), lambda i, s: (0, jnp.bitwise_xor(i, s[1] // per))),
        ]
        + [whole((rows, 2 * HEAD_DIM))] * 3,
        out_specs=[whole((rows, depth))] * 2
        + [whole((rows, depth // 2))]
        + [whole((rows, wide))] * 2
        + [whole((nctx - 2, rows, wide)), whole((tp, unit, width))],
    )
    return pl.pallas_call(
        functools.partial(project_kernel, tp, chunks, per, unit),
        grid_spec=grid_spec,
        out_shape=[
            jax.ShapeDtypeStruct((rows, depth), BF16),
            jax.ShapeDtypeStruct((rows, depth), BF16),
            jax.ShapeDtypeStruct((rows, depth // 2), BF16),
        ]
        + [jax.ShapeDtypeStruct((rows, wide), BF16)] * 2
        + [
            jax.ShapeDtypeStruct((nctx - 2, rows, wide), BF16),
            jax.ShapeDtypeStruct((tp, unit, width), BF16),
        ],
        compiler_params=params(),
        cost_estimate=takes(60),
        name="project",
    )(
        place,
        *[block for blocks in rings for block in blocks],
        gain,
        bias,
        weight,
        weight_bias,
        *tables,
    )


def stack_heads(tile, heads):
    lane = lax.broadcasted_iota(jnp.int32, tile.shape, 1) // HEAD_DIM
    return jnp.concatenate(
        [jnp.where(lane == head, tile, jnp.zeros_like(tile)) for head in range(heads)], axis=0
    )


def load_pieces(place, pieces, nctx, held, block_rows):
    chunk_rows = pieces[0].shape[0]
    chunks = len(pieces) // nctx
    for chunk in range(chunks):
        for step in range(nctx):
            source = jnp.bitwise_xor(place, step)
            first = source * block_rows + chunk * chunk_rows
            held[pl.ds(pl.multiple_of(first, chunk_rows), chunk_rows), :] = pieces[
                chunk * nctx + step
            ][...]


def attend_kernel(nctx, heads, count, extra, block_rows, place, lows, ends, bounds, *refs):
    pieces = refs[:count]
    out, sent, logs, held, turned, total, high, sums, raw, chances = refs[count + extra :]
    tile_q, tile_k = out.shape[0], turned.shape[2]
    width = heads * HEAD_DIM
    index = pl.program_id(0)

    @pl.when(index == 0)
    def _():
        load_pieces(place[0], pieces, nctx, held, block_rows)
        for tile in range(turned.shape[0]):
            turned[tile] = jnp.transpose(held[tile * tile_k : (tile + 1) * tile_k, 2 * width :])

    query_rows = pl.ds(pl.multiple_of(index * tile_q, tile_q), tile_q)
    queries = stack_heads(held[query_rows, :width] * jnp.asarray(HEAD_DIM**-0.5, BF16), heads)
    total[...] = jnp.zeros_like(total)
    high[...] = jnp.full_like(high, FLOOR)
    sums[...] = jnp.zeros_like(sums)
    first_key, last_key = bounds[0:1, :], bounds[1:2, :]

    def one(tile, _):
        start = tile * tile_k
        keys = held[pl.ds(pl.multiple_of(start, tile_k), tile_k), width : 2 * width]
        last = jnp.minimum(last_key, ends[tile] - 1) - start
        first = first_key - start
        for head in range(heads):
            raw[head] = dot_turned(keys, queries[head * tile_q : (head + 1) * tile_q])
        for head in range(heads):
            peaks = jnp.broadcast_to(high[head], (8, tile_q))
            for begin in range(0, tile_k, STRIP):
                scores = raw[head, begin : begin + STRIP, :]
                row = lax.broadcasted_iota(jnp.int32, scores.shape, 0) + begin
                scores = jnp.where((row <= last) & (row >= first), scores, NEGATIVE)
                raw[head, begin : begin + STRIP, :] = scores
                for group in range(0, STRIP, 8):
                    peaks = jnp.maximum(peaks, scores[group : group + 8])
            highest = jnp.max(peaks, axis=0, keepdims=True)
            partial = jnp.zeros((8, tile_q), F32)
            for begin in range(0, tile_k, STRIP):
                raised = jnp.exp(raw[head, begin : begin + STRIP, :] - highest)
                chances[head, begin : begin + STRIP, :] = raised.astype(BF16)
                for group in range(0, STRIP, 8):
                    partial = partial + raised[group : group + 8]
            shrink = jnp.exp(high[head] - highest)
            sums[head] = sums[head] * shrink + jnp.sum(partial, axis=0, keepdims=True)
            values = turned[tile, head * HEAD_DIM : (head + 1) * HEAD_DIM, :]
            total[head] = total[head] * shrink + dot(values, chances[head])
            high[head] = highest
        return 0

    upper = (index * tile_q + tile_q - 1) // tile_k + 1
    lax.fori_loop(lows[index], upper, one, 0)
    results = []
    for head in range(heads):
        found = sums[head] > 0.0
        safe = jnp.where(found, sums[head], 1.0)
        results.append(total[head] * jnp.where(found, 1.0 / safe, 0.0))
        logs[head : head + 1, :] = jnp.where(found, high[head] + jnp.log(safe), 0.0)
    result = jnp.transpose(jnp.concatenate(results, axis=0)).astype(BF16)
    out[...] = result
    sent[...] = result


def attend(pieces, place, lows, ends, bounds, nctx, block_rows, *needed):
    total_rows = nctx * block_rows
    width = pieces[0].shape[1] // 3
    heads = width // HEAD_DIM
    steps = total_rows // TILE_Q
    grid_spec = pltpu.PrefetchScalarGridSpec(
        num_scalar_prefetch=3,
        grid=(steps,),
        in_specs=[pl.BlockSpec((2, TILE_Q), lambda i, *_: (0, i))]
        + [whole(piece.shape) for piece in pieces]
        + anywhere(len(needed)),
        out_specs=[
            pl.BlockSpec((TILE_Q, width), lambda i, *_: (i, 0)),
            pl.BlockSpec((TILE_Q, width), lambda i, *_: (i, 0)),
            pl.BlockSpec((heads, TILE_Q), lambda i, *_: (0, i)),
        ],
        scratch_shapes=[
            pltpu.VMEM((total_rows, 3 * width), BF16),
            pltpu.VMEM((total_rows // TILE_K, width, TILE_K), BF16),
            pltpu.VMEM((heads, HEAD_DIM, TILE_Q), F32),
            pltpu.VMEM((heads, 1, TILE_Q), F32),
            pltpu.VMEM((heads, 1, TILE_Q), F32),
            pltpu.VMEM((heads, TILE_K, TILE_Q), F32),
            pltpu.VMEM((heads, TILE_K, TILE_Q), BF16),
        ],
    )
    return pl.pallas_call(
        functools.partial(attend_kernel, nctx, heads, len(pieces), len(needed), block_rows),
        grid_spec=grid_spec,
        out_shape=[
            jax.ShapeDtypeStruct((total_rows, width), BF16),
            jax.ShapeDtypeStruct((total_rows, width), BF16),
            jax.ShapeDtypeStruct((heads, total_rows), F32),
        ],
        compiler_params=params(),
        cost_estimate=takes(200),
        name="attend",
    )(place, lows, ends, bounds, *pieces, *needed)


def attend_back_kernel(
    nctx, heads, count, extra, block_rows, place, lows, ends, bounds, logs, *refs
):
    pieces, refs = refs[:count], refs[count:]
    grad, attended, refs = refs[0], refs[1], refs[2 + extra :]
    here, near, far, refs = *refs[:3], refs[3:]
    held, turned, grad_keys, grad_values, grad_query, raw, raw_grad, chances, steps, merged = refs
    tile_q, tile_k = grad.shape[0], turned.shape[2]
    width = grad.shape[1]
    index = pl.program_id(0)
    scale = jnp.asarray(HEAD_DIM**-0.5, BF16)

    @pl.when(index == 0)
    def _():
        load_pieces(place[0], pieces, nctx, held, block_rows)
        for tile in range(turned.shape[0]):
            turned[tile] = jnp.transpose(
                held[tile * tile_k : (tile + 1) * tile_k, width : 2 * width]
            )
        grad_keys[...] = jnp.zeros_like(grad_keys)
        grad_values[...] = jnp.zeros_like(grad_values)

    query_rows = pl.ds(pl.multiple_of(index * tile_q, tile_q), tile_q)
    queries = stack_heads(held[query_rows, :width] * scale, heads)
    incoming = stack_heads(grad[...], heads)
    product = jnp.transpose(grad[...].astype(F32) * attended[...].astype(F32))
    centres = [
        jnp.sum(product[head * HEAD_DIM : (head + 1) * HEAD_DIM, :], axis=0, keepdims=True)
        for head in range(heads)
    ]
    first_key, last_key = bounds[0:1, :], bounds[1:2, :]
    grad_query[...] = jnp.zeros_like(grad_query)

    def one(tile, _):
        start = tile * tile_k
        key_rows = pl.ds(pl.multiple_of(start, tile_k), tile_k)
        last = jnp.minimum(last_key, ends[tile] - 1) - start
        first = first_key - start
        by_head = [slice(head * tile_q, (head + 1) * tile_q) for head in range(heads)]
        for head in range(heads):
            raw[head] = dot_turned(held[key_rows, width : 2 * width], queries[by_head[head]])
            raw_grad[head] = dot_turned(held[key_rows, 2 * width :], incoming[by_head[head]])
        for head in range(heads):
            for begin in range(0, tile_k, STRIP):
                at = slice(begin, begin + STRIP)
                row = lax.broadcasted_iota(jnp.int32, (STRIP, tile_q), 0) + begin
                allowed = (row <= last) & (row >= first)
                scores = raw[head, at, :] - logs[head : head + 1, :]
                chance = jnp.exp(jnp.where(allowed, scores, NEGATIVE))
                chances[head, at, :] = chance.astype(BF16)
                steps[head, at, :] = (chance * (raw_grad[head, at, :] - centres[head])).astype(BF16)
            grad_values[key_rows, :] += dot(chances[head], incoming[by_head[head]])
            grad_keys[key_rows, :] += dot(steps[head], queries[by_head[head]])
            keys = turned[tile, head * HEAD_DIM : (head + 1) * HEAD_DIM, :]
            grad_query[head] += dot(keys, steps[head])
        return 0

    upper = (index * tile_q + tile_q - 1) // tile_k + 1
    lax.fori_loop(lows[index], upper, one, 0)
    result = jnp.concatenate([grad_query[head] for head in range(heads)], axis=0)
    merged[query_rows, :width] = (jnp.transpose(result) * HEAD_DIM**-0.5).astype(BF16)

    @pl.when(index == pl.num_programs(0) - 1)
    def _():
        merged[:, width : 2 * width] = grad_keys[...].astype(BF16)
        merged[:, 2 * width :] = grad_values[...].astype(BF16)
        outs = [here, near] + [far.at[way] for way in range(nctx - 2)]
        for way, out in enumerate(outs):
            first = jnp.bitwise_xor(place[0], way) * block_rows
            out[...] = merged[pl.ds(pl.multiple_of(first, block_rows), block_rows), :]


def attend_back(pieces, place, lows, ends, bounds, logs, grad, attended, nctx, block_rows, *needed):
    total_rows, width = grad.shape
    heads = width // HEAD_DIM
    by_tile = pl.BlockSpec((TILE_Q, width), lambda i, *_: (i, 0))
    sent = (block_rows, 3 * width)
    sent = [sent, sent, (nctx - 2, *sent)]
    grid_spec = pltpu.PrefetchScalarGridSpec(
        num_scalar_prefetch=3,
        grid=(total_rows // TILE_Q,),
        in_specs=[
            pl.BlockSpec((2, TILE_Q), lambda i, *_: (0, i)),
            pl.BlockSpec((heads, TILE_Q), lambda i, *_: (0, i)),
        ]
        + [whole(piece.shape) for piece in pieces]
        + [by_tile] * 2
        + anywhere(len(needed)),
        out_specs=[whole(shape) for shape in sent],
        scratch_shapes=[
            pltpu.VMEM((total_rows, 3 * width), BF16),
            pltpu.VMEM((total_rows // TILE_K, width, TILE_K), BF16),
            pltpu.VMEM((total_rows, width), F32),
            pltpu.VMEM((total_rows, width), F32),
            pltpu.VMEM((heads, HEAD_DIM, TILE_Q), F32),
            pltpu.VMEM((heads, TILE_K, TILE_Q), F32),
            pltpu.VMEM((heads, TILE_K, TILE_Q), F32),
            pltpu.VMEM((heads, TILE_K, TILE_Q), BF16),
            pltpu.VMEM((heads, TILE_K, TILE_Q), BF16),
            pltpu.VMEM((total_rows, 3 * width), BF16),
        ],
    )
    return pl.pallas_call(
        functools.partial(
            attend_back_kernel, nctx, heads, len(pieces), len(needed), block_rows
        ),
        grid_spec=grid_spec,
        out_shape=[jax.ShapeDtypeStruct(shape, BF16) for shape in sent],
        compiler_params=params(),
        cost_estimate=takes(250),
        name="attend_back",
    )(place, lows, ends, bounds, logs, *pieces, grad, attended, *needed)


def mix_kernel(nctx, count, place, heads_in, weight, source, gain, bias, *refs):
    returned, mixed, *lows = refs[count:]
    rows, depth = mixed.shape
    step = pl.program_id(0)
    left = jnp.concatenate([heads_in[c, 0] for c in range(nctx)], axis=1)
    returned[...] = left

    @pl.when(step == 0)
    def _():
        mixed[...] = source[...].astype(F32)

    mixed[...] += dot_turned(left, weight[0])

    @pl.when(step == pl.num_programs(0) - 1)
    def _():
        values = mixed[...]
        values = values - jnp.mean(values, axis=1, keepdims=True)
        scaling = lax.rsqrt(jnp.mean(values * values, axis=1, keepdims=True) + EPSILON)
        values = (values * scaling * gain[...] + bias[...]).astype(BF16)
        part_rows = lows[0].shape[0]
        for part, low in enumerate(lows):
            low[...] = values[part * part_rows : (part + 1) * part_rows]


def mix(heads_in, weight, full, gain, bias, place, parts, *needed):
    nctx, tp, rows, piece = heads_in.shape
    depth = full.shape[1]
    head_width = nctx * piece
    grid_spec = pltpu.PrefetchScalarGridSpec(
        num_scalar_prefetch=1,
        grid=(tp,),
        in_specs=[
            pl.BlockSpec((nctx, 1, rows, piece), lambda k, s: (0, k, 0, 0)),
            pl.BlockSpec((1, depth, head_width), lambda k, s: (k, 0, 0)),
            pl.BlockSpec((rows, depth), lambda k, s: (s[0], 0)),
            whole((1, depth)),
            whole((1, depth)),
        ]
        + anywhere(len(needed)),
        out_specs=[
            pl.BlockSpec((rows, head_width), lambda k, s: (0, k)),
            whole((rows, depth)),
        ]
        + [whole((rows // parts, depth))] * parts,
    )
    return pl.pallas_call(
        functools.partial(mix_kernel, nctx, len(needed)),
        grid_spec=grid_spec,
        out_shape=[
            jax.ShapeDtypeStruct((rows, tp * head_width), BF16),
            jax.ShapeDtypeStruct((rows, depth), F32),
        ]
        + [jax.ShapeDtypeStruct((rows // parts, depth), BF16)] * parts,
        compiler_params=params(),
        cost_estimate=takes(50),
        name="mix",
    )(place, heads_in, weight, full, gain, bias, *needed)


def feed_kernel(cuts, parts, tp, first_one, place, low, cot, mixed, source, *refs):
    refs = refs[-(5 + parts + 4) :]
    kept, grad_gate, grad_up, hidden, out = refs[:5]
    partials, held, sems = refs[5 : 5 + parts], refs[-4:-1], refs[-1]
    unit = source.shape[1] // 3
    width = out.shape[2]

    def copies(index):
        first, size = cuts[index]
        at = pl.ds(first, size)
        return [
            pltpu.make_async_copy(
                source.at[:, pl.ds(which * unit, unit), at],
                held[which].at[:, :, at],
                sems.at[index * 3 + which],
            )
            for which in range(3)
        ]

    for index in range(len(cuts)):
        for copy in copies(index):
            copy.start()
    kept[...] = low[...]
    rows, depth = kept.shape[0] // parts, kept.shape[1]
    grads = jnp.concatenate([cot[block] for block in range(tp)], axis=1)
    for index, (first, size) in enumerate(cuts):
        for copy in copies(index):
            copy.wait()
        at = slice(first, first + size)
        gate_weight, up_weight, down_weight = [w[:, :, at].reshape(depth, size) for w in held]
        gate = dot(kept[...], gate_weight)
        up = dot(kept[...], up_weight)
        sigma = 1.0 / (1.0 + jnp.exp(-gate))
        active = gate * sigma
        hidden[:, at] = (active * up).astype(BF16)
        grad = dot(grads, down_weight)
        grad_gate[:, at] = (grad * up * sigma * (1.0 + gate * (1.0 - sigma))).astype(BF16)
        grad_up[:, at] = (grad * active).astype(BF16)
    gate_weight, up_weight, down_weight = [w[...].reshape(depth, w.shape[2]) for w in held]
    product = dot_turned(grad_gate[...], gate_weight) + dot_turned(grad_up[...], up_weight)
    for part in range(parts):
        partials[part][...] = product[part * rows : (part + 1) * rows].astype(BF16)
    values = dot_turned(hidden[...], down_weight)
    if first_one:
        values = values + mixed[...]
    for block in range(tp):
        out[block] = values[:, block * width : (block + 1) * width].astype(BF16)


def feed(low, cot, mixed, weights, step, tp, place, held, parts, *needed):
    rows, depth = low.shape
    part_rows = rows // parts
    blocks, triple, hidden = weights.shape
    cuts = []
    while sum(size for _, size in cuts) < hidden:
        first = sum(size for _, size in cuts)
        cuts.append((first, min(512, hidden - first)))
    by_owner = lambda columns: pl.BlockSpec(
        (rows, columns), lambda i, s: (lax.rem(s[0] - step + tp, tp), 0)
    )
    width = depth // tp
    blocks_of_owner = pl.BlockSpec(
        (tp, rows, width), lambda i, s: (0, lax.rem(s[0] - step + tp, tp), 0)
    )
    grid_spec = pltpu.PrefetchScalarGridSpec(
        num_scalar_prefetch=1,
        grid=(1,),
        in_specs=[whole((rows, depth)), blocks_of_owner, whole(mixed.shape)]
        + anywhere(1 + len(held) + len(needed)),
        out_specs=[by_owner(depth)]
        + [by_owner(hidden)] * 3
        + [blocks_of_owner]
        + [whole((part_rows, depth))] * parts,
        scratch_shapes=[pltpu.VMEM((blocks, triple // 3, hidden), BF16)] * 3
        + [pltpu.SemaphoreType.DMA((3 * len(cuts),))],
    )
    return pl.pallas_call(
        functools.partial(feed_kernel, tuple(cuts), parts, tp, step == 0),
        grid_spec=grid_spec,
        out_shape=[
            jax.ShapeDtypeStruct((tp * rows, columns), BF16)
            for columns in (depth, hidden, hidden, hidden)
        ]
        + [jax.ShapeDtypeStruct((tp, tp * rows, width), BF16)]
        + [jax.ShapeDtypeStruct((part_rows, depth), BF16)] * parts,
        input_output_aliases={5 + index: index for index in range(len(held))},
        compiler_params=params(),
        cost_estimate=takes(100),
        name="feed",
    )(place, low, cot, mixed, weights, *held, *needed)


def blame_halves(lefts, rights, place, unit, *needed, held=(), offset=0, total=None):
    rows, other = rights[0].shape
    picked = lefts[1].shape[1] // unit
    chosen = pl.BlockSpec((rows, unit), lambda j, s: (0, 2 * (j ^ s[3]) + s[1] % 2))
    if lefts[0].ndim == 3:
        per = lefts[0].shape[2] // unit
        chosen = pl.BlockSpec(
            (1, rows, unit),
            lambda j, s: (
                (2 * (j ^ s[3]) + s[1] % 2) // per,
                0,
                lax.rem(2 * (j ^ s[3]) + s[1] % 2, per),
            ),
        )
    cut = pl.BlockSpec((rows, unit), lambda j, s: (0, j ^ s[3]))
    shapes = [(2, unit // 2, total or other)] * 4

    def kernel(place, left_here, left_there, right_here, right_there, *refs):
        outs, spare, sems = refs[len(held) + len(needed) : -2], refs[-2], refs[-1]
        product = 0.0
        for left, right in ((left_here, right_here), (left_there, right_there)):
            ours = left[0] if len(left.shape) == 3 else left[...]
            product = product + lax.dot_general(
                ours, right[...], (((0,), (0,)), ((), ())), preferred_element_type=F32
            )
        product = product.astype(BF16)
        for j in range(picked):

            @pl.when(pl.program_id(0) == j)
            def _():
                first, second = spare.at[j // 2, j % 2], spare.at[2 + j % 2, j // 2]
                first[...], second[...] = product[: unit // 2], product[unit // 2 :]

        @pl.when(pl.program_id(0) == picked - 1)
        def _():
            moves = [
                pltpu.make_async_copy(
                    spare.at[index], out.at[:, :, pl.ds(offset, other)], sems.at[index]
                )
                for index, out in enumerate(outs)
            ]
            for move in moves:
                move.start()
            for move in moves:
                move.wait()

    grid_spec = pltpu.PrefetchScalarGridSpec(
        num_scalar_prefetch=1,
        grid=(picked,),
        in_specs=[chosen, cut]
        + [whole((rows, other))] * 2
        + anywhere(len(held) + len(needed)),
        out_specs=anywhere(4),
        scratch_shapes=[
            pltpu.VMEM((4, 2, unit // 2, other), BF16),
            pltpu.SemaphoreType.DMA((4,)),
        ],
    )
    place = jnp.concatenate([place, place[2:3] * 2 + place[1:2] // 2])
    return pl.pallas_call(
        kernel,
        grid_spec=grid_spec,
        out_shape=[jax.ShapeDtypeStruct(shape, BF16) for shape in shapes],
        input_output_aliases={5 + index: index for index in range(len(held))},
        compiler_params=params(),
        cost_estimate=takes(60),
        name="blame_halves",
    )(place, *lefts, *rights, *held, *needed)


def blame(left, right, *needed):
    rows, columns = left.shape
    if right.ndim == 3:
        steps, other = right.shape[0], right.shape[2]
        in_specs = [whole((rows, columns)), pl.BlockSpec((1, rows, other), lambda j: (j, 0, 0))]
        target, shape = pl.BlockSpec((columns, other), lambda j: (0, j)), (columns, steps * other)
    else:
        steps, other = 4, right.shape[1]
        in_specs = [pl.BlockSpec((rows, columns // steps), lambda j: (0, j)), whole((rows, other))]
        target, shape = pl.BlockSpec((columns // steps, other), lambda j: (j, 0)), (columns, other)

    def kernel(left, right, *refs):
        theirs = right[0] if len(right.shape) == 3 else right[...]
        refs[-1][...] = lax.dot_general(
            left[...], theirs, (((0,), (0,)), ((), ())), preferred_element_type=F32
        ).astype(BF16)

    return pl.pallas_call(
        kernel,
        grid=(steps,),
        in_specs=in_specs + anywhere(len(needed)),
        out_specs=target,
        out_shape=jax.ShapeDtypeStruct(shape, BF16),
        compiler_params=params(),
        cost_estimate=takes(60),
        name="blame",
    )(left, right, *needed)


def turn_kernel(nctx, count, parts, unit, place, *refs):
    arrived, own = refs[:parts], refs[parts : 2 * parts]
    mixed, cot, gain = refs[2 * parts : 2 * parts + 3]
    weight, refs = refs[2 * parts + 3], refs[2 * parts + 4 + count :]
    out, grad_mixed, grad_low, gain_grad, shift_grad, half = refs
    rows, depth = mixed.shape
    piece = out.shape[3]

    @pl.when(pl.program_id(0) == 0)
    def _():
        incoming = jnp.concatenate(
            [there[...].astype(F32) + here[...].astype(F32) for there, here in zip(arrived, own)]
        )
        values = mixed[...]
        values = values - jnp.mean(values, axis=1, keepdims=True)
        scaling = lax.rsqrt(jnp.mean(values * values, axis=1, keepdims=True) + EPSILON)
        normed = values * scaling
        shift_grad[...] = jnp.sum(incoming, axis=0, keepdims=True)
        gain_grad[...] = jnp.sum(incoming * normed, axis=0, keepdims=True)
        scaled = incoming * gain[...]
        grads = jnp.concatenate([cot[block] for block in range(cot.shape[0])], axis=1)
        total = grads.astype(F32) + scaling * (
            scaled
            - jnp.mean(scaled, axis=1, keepdims=True)
            - normed * jnp.mean(scaled * normed, axis=1, keepdims=True)
        )
        grad_mixed[...] = total
        grad_low[...] = total.astype(BF16)
        write_half(half, grad_low, 1 - lax.rem(place[1], 2), unit)

    product = dot(grad_low[...], weight[0])
    for c in range(nctx):
        out[c, 0] = product[:, c * piece : (c + 1) * piece].astype(BF16)


def turn(arrived, own, mixed, cot, gain, weight, place, nctx, tp, unit, *needed):
    rows, depth = mixed.shape
    parts = len(arrived)
    head_width = weight.shape[2]
    piece = head_width // nctx
    grid_spec = pltpu.PrefetchScalarGridSpec(
        num_scalar_prefetch=1,
        grid=(tp,),
        in_specs=[whole((rows // parts, depth))] * (2 * parts)
        + [whole((rows, depth))]
        + [
            pl.BlockSpec((tp, rows, depth // tp), lambda k, s: (0, s[0], 0)),
            whole((1, depth)),
            pl.BlockSpec((1, depth, head_width), lambda k, s: (k, 0, 0)),
        ]
        + anywhere(len(needed)),
        out_specs=[
            pl.BlockSpec((nctx, 1, rows, piece), lambda k, s: (0, k, 0, 0)),
            whole((rows, depth)),
            whole((rows, depth)),
            whole((1, depth)),
            whole((1, depth)),
            whole((rows, depth // 2)),
        ],
    )
    return pl.pallas_call(
        functools.partial(turn_kernel, nctx, len(needed), parts, unit),
        grid_spec=grid_spec,
        out_shape=[
            jax.ShapeDtypeStruct((nctx, tp, rows, piece), BF16),
            jax.ShapeDtypeStruct((rows, depth), F32),
            jax.ShapeDtypeStruct((rows, depth), BF16),
            jax.ShapeDtypeStruct((1, depth), F32),
            jax.ShapeDtypeStruct((1, depth), F32),
            jax.ShapeDtypeStruct((rows, depth // 2), BF16),
        ],
        compiler_params=params(),
        cost_estimate=takes(60),
        name="turn",
    )(place, *arrived, *own, mixed, cot, gain, weight, *needed)


def finish_kernel(nctx, tp, extra_count, place, *refs):
    pieces = refs[:nctx]
    cosine, sine_up, sine_down, full, extra, gain = refs[nctx : nctx + 6]
    weight, refs = refs[nctx + 6], refs[nctx + 7 + extra_count :]
    outs = refs[:tp]
    low, bias_grad, gain_grad, shift_grad, spare = refs[tp:]
    rows, wide = pieces[0].shape
    piece = wide // 3
    width = outs[0].shape[1]
    strip = spare.shape[0]
    extra_rows = extra.shape[0]

    @pl.when(pl.program_id(0) == 0)
    def _():
        bias_grad[...] = jnp.zeros_like(bias_grad)
        gain_grad[...] = jnp.zeros_like(gain_grad)
        shift_grad[...] = jnp.zeros_like(shift_grad)

    for step in range(nctx):
        source = jnp.bitwise_xor(place[1], step)
        for part in range(3):
            values = pieces[step][:, part * piece : (part + 1) * piece].astype(F32)
            if part < 2:
                values = (
                    values * cosine[...]
                    - pltpu.roll(values, piece - ROT // 2, 1) * sine_up[...]
                    - pltpu.roll(values, ROT // 2, 1) * sine_down[...]
                )
            columns = pl.ds(pl.multiple_of(source * wide + part * piece, piece), piece)
            bias_grad[:, columns] += jnp.sum(values, axis=0, keepdims=True)
            low[:, columns] = values.astype(BF16)

    incoming = dot_turned(low[...], weight[...])
    source = full[...].astype(F32)
    source = source - jnp.mean(source, axis=1, keepdims=True)
    scaling = lax.rsqrt(jnp.mean(source * source, axis=1, keepdims=True) + EPSILON)
    normed = source * scaling
    shift_grad[...] += jnp.sum(incoming, axis=0, keepdims=True)
    gain_grad[...] += jnp.sum(incoming * normed, axis=0, keepdims=True)
    scaled = incoming * gain[...]
    spare[...] = scaling * (
        scaled
        - jnp.mean(scaled, axis=1, keepdims=True)
        - normed * jnp.mean(scaled * normed, axis=1, keepdims=True)
    )
    first = pl.program_id(0) * strip
    wanted = place[0] * extra_rows

    if strip <= extra_rows:

        @pl.when((first >= wanted) & (first < wanted + extra_rows))
        def _():
            spare[...] += extra[pl.ds(pl.multiple_of(first - wanted, strip), strip), :]

    else:

        @pl.when((wanted >= first) & (wanted < first + strip))
        def _():
            spare[pl.ds(pl.multiple_of(wanted - first, extra_rows), extra_rows), :] += extra[...]

    for step, out in enumerate(outs):
        owner = lax.rem(place[0] - step + tp, tp)
        out[...] = spare[:, pl.ds(pl.multiple_of(owner * width, width), width)].astype(BF16)


def finish(pieces, place, tables, full, extra, gain, weight, tp, *needed):
    rows, wide = pieces[0].shape
    depth = full.shape[1]
    total = weight.shape[1]
    strip = 256
    steps = rows // strip
    width = depth // tp
    nctx = len(pieces)
    by_rows = lambda columns: pl.BlockSpec((strip, columns), lambda i, s: (i, 0))
    grid_spec = pltpu.PrefetchScalarGridSpec(
        num_scalar_prefetch=1,
        grid=(steps,),
        in_specs=[by_rows(wide)] * nctx
        + [by_rows(2 * HEAD_DIM)] * 3
        + [
            by_rows(depth),
            whole(extra.shape),
            whole((1, depth)),
        ]
        + [whole(weight.shape)]
        + anywhere(len(needed)),
        out_specs=[by_rows(width)] * tp
        + [
            by_rows(total),
            whole((1, total)),
            whole((1, depth)),
            whole((1, depth)),
        ],
        scratch_shapes=[pltpu.VMEM((strip, depth), F32)],
    )
    return pl.pallas_call(
        functools.partial(finish_kernel, nctx, tp, len(needed)),
        grid_spec=grid_spec,
        out_shape=[jax.ShapeDtypeStruct((rows, width), BF16)] * tp
        + [
            jax.ShapeDtypeStruct((rows, total), BF16),
            jax.ShapeDtypeStruct((1, total), F32),
            jax.ShapeDtypeStruct((1, depth), F32),
            jax.ShapeDtypeStruct((1, depth), F32),
        ],
        compiler_params=params(),
        cost_estimate=takes(70),
        name="finish",
    )(place, *pieces, *tables, full, extra, gain, weight, *needed)


def join(rings, place, unit):
    parts, tp = len(rings), len(rings[0])
    rows, width = rings[0][0].shape

    def kernel(place, *refs):
        for part in range(parts):
            for step in range(tp):
                owner = lax.rem(place[0] - step + tp, tp)
                refs[-2][owner, part * rows : (part + 1) * rows, :] = refs[part * tp + step][...]
        per, half = width // unit, 1 - lax.rem(place[1], 2)
        for block in range(tp * per // 2):
            index = 2 * block + half if unit % 128 == 0 else 0
            first = pl.multiple_of(lax.rem(index, per) * unit, unit)
            if unit % 128:
                first = 0
            refs[-1][:, block * unit : (block + 1) * unit] = refs[-2][
                lax.div(index, per), :, pl.ds(first, unit)
            ]

    grid_spec = pltpu.PrefetchScalarGridSpec(
        num_scalar_prefetch=1,
        grid=(1,),
        in_specs=[whole((rows, width))] * (parts * tp),
        out_specs=[whole((tp, parts * rows, width)), whole((parts * rows, tp * width // 2))],
    )
    return pl.pallas_call(
        kernel,
        grid_spec=grid_spec,
        out_shape=[
            jax.ShapeDtypeStruct((tp, parts * rows, width), BF16),
            jax.ShapeDtypeStruct((parts * rows, tp * width // 2), BF16),
        ],
        compiler_params=params(),
        cost_estimate=takes(10),
        name="join",
    )(place, *[block for blocks in rings for block in blocks])


def pack_kernel(gate, up, down, out):
    rows = gate.shape[0]
    out[:rows] = gate[...]
    out[rows : 2 * rows] = up[...]
    out[2 * rows :] = jnp.transpose(down[...])


def pack(gate, up, down):
    rows, columns = gate.shape
    return pl.pallas_call(
        pack_kernel,
        out_shape=jax.ShapeDtypeStruct((3 * rows, columns), BF16),
        compiler_params=params(),
        cost_estimate=takes(10),
        name="pack",
    )(gate, up, down)


def contract_rows(left, right):
    return lax.dot_general(left, right, (((0,), (0,)), ((), ())), preferred_element_type=F32)


def pick(stack, index):
    return lax.dynamic_index_in_dim(stack, index, 0, keepdims=False)


def shards(
    nfsdp,
    nctx,
    tp,
    inputs,
    cotangent,
    first_gain,
    first_bias,
    qkv_weight,
    qkv_bias,
    out_weight,
    second_gain,
    second_bias,
    gate_weight,
    up_weight,
    down_weight,
    lengths,
    fill_counts,
):
    data = ("fsdp", "ctx")
    ndata = nfsdp * nctx
    block_rows, width = inputs.shape
    depth = tp * width
    half_depth = depth // 2
    unit = depth // ndata
    tensor_index = lax.axis_index("tp").astype(jnp.int32)
    context_index = lax.axis_index("ctx").astype(jnp.int32)
    fsdp_index = lax.axis_index("fsdp").astype(jnp.int32)
    part_rows = block_rows // tp
    chunk_rows = block_rows // CHUNKS
    head_width = qkv_weight.shape[2]
    piece = head_width // nctx
    wide = 3 * piece

    square = nfsdp == 2 and nctx == 4 and unit % 128 == 0
    place = jnp.stack([tensor_index, context_index, fsdp_index])

    def shift(value, step):
        return lax.ppermute(value, "tp", [(i, (i + step) % tp) for i in range(tp)])

    def swap(value, step):
        return lax.ppermute(value, "ctx", [(i, i ^ step) for i in range(nctx)])

    core_index = context_index % 2
    groups = [list(range(0, ndata, 2)), list(range(1, ndata, 2))]
    def mate(value):
        return swap(value, 1)

    def send(here, near, far, *needed):
        far = swap(far, 2)
        return [here, swap(near, 1), far[0], swap(tie(far[1], *needed), 1)]

    def scatter_half(value, axis):
        return lax.psum_scatter(
            value, data, scatter_dimension=axis, tiled=True, axis_index_groups=groups
        )

    def scatter(value, axis):
        return lax.psum_scatter(value, data, scatter_dimension=axis, tiled=True)

    def cross(value):
        return lax.ppermute(value, "fsdp", [(i, i ^ 1) for i in range(nfsdp)])

    def square_once(parts, coming, last):
        return total(tie(parts[0], last), coming[0]), total(tie(parts[2], last), coming[1])

    def square_twice(first, second):
        first = first[0].astype(F32) + swap(first[1], 2).astype(F32)
        second = second[0].astype(F32) + cross(second[1]).astype(F32)
        return jnp.concatenate([first, second], axis=0)

    def total(left, right):
        return (left.astype(F32) + right.astype(F32)).astype(BF16)

    owners = [(tensor_index - step + tp) % tp for step in range(tp)]

    own_qkv = (
        qkv_weight.reshape(-1, 3, nctx, piece).transpose(0, 2, 1, 3).reshape(-1, 3 * head_width)
    )
    full_qkv = lax.all_gather(own_qkv, data, axis=0, tiled=True)
    own_feed = pack(gate_weight, up_weight, down_weight)
    feed_weights = lax.all_gather(own_feed, data, axis=0, tiled=True).reshape(ndata, 3 * unit, -1)

    validity, position, first_key, last_key = layout(lengths[0], fill_counts[0], block_rows)
    own_position = lax.dynamic_slice_in_dim(position, context_index * block_rows, block_rows, 0)
    tables = rotary_tables(own_position)
    bounds = jnp.stack([first_key, last_key])
    tile_first = first_key[::TILE_Q]
    tile_count = tile_first.shape[0]
    lows = jnp.where(validity[::TILE_Q], tile_first // TILE_K, tile_count * TILE_Q).astype(jnp.int32)
    key_block = jnp.arange(0, nctx * block_rows, TILE_K, dtype=jnp.int32) // block_rows
    ends = (
        key_block * block_rows
        + jnp.sum(
            jnp.where(
                key_block[:, None] == jnp.arange(nctx, dtype=jnp.int32)[None, :],
                fill_counts[0][None, :],
                0,
            ),
            axis=1,
        )
    ).astype(jnp.int32)

    flat_bias = qkv_bias.reshape(3, nctx, piece).transpose(1, 0, 2).reshape(1, -1)
    gain_one, bias_one = first_gain[None], first_bias[None]
    gain_two, bias_two = second_gain[None], second_bias[None]

    rings = [[inputs[c * chunk_rows : (c + 1) * chunk_rows]] for c in range(CHUNKS)]
    share = unit // CHUNKS
    for chunk in range(CHUNKS):
        carried = out_weight.T[chunk * share : (chunk + 1) * share]
        rings[chunk][0] = jnp.concatenate([rings[chunk][0], carried], axis=0)
    for chunk in range(CHUNKS):
        for _ in range(tp - 1):
            rings[chunk].append(shift(rings[chunk][-1], 1))
            if len(rings[chunk]) == 2:
                rings[chunk][-1] = tie(rings[chunk][-1], own_feed)
    all_low, full, low_half, *outgoing, stack = project(
        rings, place, gain_one, bias_one, full_qkv, flat_bias, tables, nctx, unit
    )
    full_out = lax.all_gather(stack, data, axis=1, tiled=True)

    cot = tie(cotangent, *[blocks[-1] for blocks in rings])
    cot_rings = [[cot[c * chunk_rows : (c + 1) * chunk_rows]] for c in range(CHUNKS)]
    for blocks in cot_rings:
        for _ in range(tp - 1):
            blocks.append(shift(blocks[-1], 1))
    pieces = send(*outgoing, *[blocks[max(tp - 2, 0)] for blocks in cot_rings])

    attended, outgoing, logs = attend(
        pieces,
        place[1:2],
        lows,
        ends,
        bounds,
        nctx,
        block_rows,
        feed_weights,
    )
    cot, cot_half = join(cot_rings, place, unit)
    arrived = lax.all_to_all(
        tie(outgoing, *[blocks[-1] for blocks in cot_rings]).reshape(nctx * tp, part_rows, piece),
        ("ctx", "tp"),
        split_axis=0,
        concat_axis=0,
        tiled=True,
    )
    returned, mixed, second_low = mix(
        arrived.reshape(nctx, tp, part_rows, piece),
        full_out,
        full,
        gain_two,
        bias_two,
        place,
        1,
    )

    arrived, held, partials, travelling = second_low, [], [], None
    for step in range(tp):
        coming = shift(arrived, 1) if step < tp - 1 else None
        needed = travelling if step == tp - 1 and step > 2 else []
        *held, first, second = feed(
            arrived, cot, mixed, feed_weights, step, tp, place, held, HALVES, *needed
        )
        partials.append([first, second])
        if step == 1 % tp:
            travelling = partials[step]
        elif step > 1:
            travelling = [
                total(shift(value, 1), kept) for value, kept in zip(travelling, partials[step])
            ]
        if step == 0 and coming is not None:
            coming = tie(coming, partials[0][0])
        arrived = coming
    all_second, all_gate, all_up, hidden, feedforward = held

    last = [shift(value, 1) for value in travelling]
    half_gate = blame(all_second, all_gate, *travelling)
    half_up = blame(all_second, all_up, *travelling)
    grad_heads, grad_mixed, mixed_low, gain_grad_two, shift_grad_two, mixed_half = turn(
        last,
        partials[0],
        mixed,
        cot,
        gain_two,
        full_out,
        place,
        nctx,
        tp,
        unit,
        half_gate,
        half_up,
    )
    grad_heads = lax.all_to_all(
        grad_heads.reshape(nctx * tp, part_rows, piece),
        ("ctx", "tp"),
        split_axis=0,
        concat_axis=0,
        tiled=True,
    ).reshape(nctx * block_rows, piece)

    total_gate = scatter(tie(half_gate, mixed_low), 0).astype(F32)
    total_up = scatter(tie(half_up, mixed_low), 0).astype(F32)
    half_out = blame(mixed_low, returned)
    total_out = scatter(tie(half_out, grad_heads), 0)

    feedforward = tie(feedforward, grad_heads)
    inner = hidden.shape[1]
    both = inner + 3 * head_width
    if square:
        parts = blame_halves(
            (cot, mate(cot_half)), (hidden, mate(hidden)), place, unit, total=both
        )
        half_down = parts[0]
    else:
        half_down = blame(hidden, cot)
        total_down = scatter(half_down, 1).astype(F32)
    layer_out = [pick(feedforward, owners[1 % tp])]
    for step in range(1, tp):
        kept = pick(feedforward, owners[(step + 1) % tp])
        if step == 2:
            layer_out.append(add(shift(layer_out[-1], 1), kept, half_down))
        else:
            layer_out.append(total(shift(layer_out[-1], 1), kept))

    grad_pieces = attend_back(
        pieces, place[1:2], lows, ends, bounds, logs, grad_heads, attended, nctx, block_rows, half_out
    )
    arrived = send(*grad_pieces, *layer_out[max(tp - 2, 0) : tp - 1])
    layer_out = layer_out[-1]
    low_halves = mate(low_half) if square else low_half
    needed = [layer_out, low_halves]
    *partial, all_grad, bias_grad, gain_grad, shift_grad = finish(
        arrived, place, tables, full, grad_mixed, gain_one, full_qkv, tp, *needed
    )
    if square:
        parts = blame_halves(
            (all_low, low_halves),
            (all_grad, mate(all_grad)),
            place,
            unit,
            held=parts,
            offset=inner,
            total=both,
        )
    else:
        parts = []
    def exchange(value, axis, steps, size):
        for step in steps:
            value = value + lax.ppermute(value, axis, [(i, i ^ step) for i in range(size)])
        return value

    def powers(first, size):
        return [1 << bit for bit in range(first, size.bit_length() - 1)]

    small = jnp.concatenate([gain_grad, shift_grad, gain_grad_two, shift_grad_two], axis=1)
    small = sum([shift(small, step) for step in range(1, tp)], small)
    small = jnp.concatenate([bias_grad, small], axis=1)
    travelling, ring_steps = partial[1 % tp], []
    coming = [cross(parts[1]), swap(parts[3], 2)] if square else []
    needed = [[total_gate, total_up, small, *parts], [], coming]
    for step in range(1, tp):
        travelling = add(
            shift(travelling, 1), partial[(step + 1) % tp], *(needed[step - 1] if step < 4 else [])
        )
        if step == 1:
            small = exchange(tie(small, travelling), "ctx", powers(0, min(nctx, 2)), nctx)
            needed[1].append(small)
    grad_inputs = travelling
    once = square_once(parts, coming, travelling) if square else ()
    small = exchange(tie(small, travelling), "ctx", powers(1, nctx), nctx)
    small = exchange(small, "fsdp", powers(0, nfsdp), nfsdp)

    out_parts = jnp.swapaxes(tie(total_out, travelling).reshape(-1, tp, head_width), 0, 1)
    total_out = pick(out_parts, tensor_index).astype(F32)
    for step in range(1, tp):
        total_out = total_out + shift(pick(out_parts, (tensor_index + step) % tp), step).astype(F32)
    total_out = total_out.T

    if square:
        totals = square_twice(*once)
        total_down, total_qkv = totals[:, :inner].T, totals[:, inner:]
    else:
        total_qkv = scatter(blame(all_low, all_grad), 0).astype(F32)

    total_qkv = (
        total_qkv
        .reshape(-1, nctx, 3, piece)
        .transpose(0, 2, 1, 3)
        .reshape(-1, 3, head_width)
    )


    bias_total, small = small[:, : 3 * head_width], small[:, 3 * head_width :]
    bias_total = bias_total.reshape(nctx, 3, piece).transpose(1, 0, 2).reshape(3, head_width)
    small = small.reshape(4, depth)
    return (
        layer_out,
        grad_inputs,
        small[0],
        small[1],
        total_qkv,
        bias_total,
        total_out,
        small[2],
        small[3],
        total_gate,
        total_up,
        total_down,
    )


def solution(mesh):
    data = ("fsdp", "ctx")
    by_rows = P(data, "tp")
    by_columns = P("tp", data)
    qkv = P(data, None, "tp")
    return jax.shard_map(
        functools.partial(shards, mesh.shape["fsdp"], mesh.shape["ctx"], mesh.shape["tp"]),
        mesh=mesh,
        in_specs=(
            by_rows,
            by_rows,
            P(),
            P(),
            qkv,
            P(None, "tp"),
            by_columns,
            P(),
            P(),
            by_rows,
            by_rows,
            by_columns,
            P("fsdp", None),
            P("fsdp", None),
        ),
        out_specs=(
            by_rows,
            by_rows,
            P(),
            P(),
            qkv,
            P(None, "tp"),
            by_columns,
            P(),
            P(),
            by_rows,
            by_rows,
            by_columns,
        ),
        check_vma=False,
    )
```
